32 devices in a mesh: group: 4 (over y, core), shard: 8 (over z, x).
Axes of the slice: x: 2, y: 2, z: 4, core: 2. Of those that a mesh axis runs over, the one named last changes fastest.
Arguments:
- tokens: float32 [8192, 2048], P(('group', 'shard')), may hold values from -6 to 6
- cotangent: float32 [8192, 2048], P(('group', 'shard')), may hold values from -6 to 6
- lengths: int32 [4, 3], P('group'), may hold values from 256 to 1024, as said below
- deal_slot: int32 [8192], P(('group', 'shard')), may hold values from 0 to 2047, as said below
- in_weight: float32 [2048, 8512], P('shard', 'group'), may hold values from -0.125 to 0.125
- out_weight: float32 [4096, 2048], P('shard', 'group'), may hold values from -0.09375 to 0.09375
- small_params: float32 [28096], replicated, may hold values from -12 to 3, as said below
- in_moment: float32 [2048, 8512], P('shard', 'group'), may hold values from -160 to 160
- out_moment: float32 [4096, 2048], P('shard', 'group'), may hold values from -448 to 448
- small_moment: float32 [28096], replicated, may hold values from -160 to 160
- in_average: float32 [2048, 8512], P('shard', 'group'), may hold values from -0.125 to 0.125
- out_average: float32 [4096, 2048], P('shard', 'group'), may hold values from -0.09375 to 0.09375
- small_average: float32 [28096], replicated, may hold values from -12 to 3, as said below
Outputs:
- block_out: float32 [8192, 2048], P(('group', 'shard'))
- input_grad: float32 [8192, 2048], P(('group', 'shard'))
- in_moment_new: float32 [2048, 8512], P('shard', 'group')
- in_weight_new: float32 [2048, 8512], P('shard', 'group')
- in_average_new: float32 [2048, 8512], P('shard', 'group')
- out_moment_new: float32 [4096, 2048], P('shard', 'group')
- out_weight_new: float32 [4096, 2048], P('shard', 'group')
- out_average_new: float32 [4096, 2048], P('shard', 'group')
- small_moment_new: float32 [28096], replicated
- small_params_new: float32 [28096], replicated
- small_average_new: float32 [28096], replicated
The draws below stay inside these ranges and needn't reach their ends.
Inputs may be any that keep to these rules, and one draw needn't show every extreme that they name: `lengths`: each group holds 3 sequences summing to 2048 tokens; the middle one has exactly 1024 tokens, the others 256 or more. `deal_slot`: within each group a permutation of the packed positions; the 256 tokens that one device holds go 32 apiece to each block of 256 packed positions of its group. `small_params`: the step biases lie between -12 and -2, the log decay rates between 0 and 2.8, gains between 0.5 and 1.5. `small_average`: laid out as small_params.
All inputs are finite; a program needn't handle non-finite values.
Results may differ from the reference program's by a relative error of at most 0.00075.
The reference program's roundings to bfloat16 on the way (of `in_low`, `normed` and `normed_out`) count: a program that leaves them out, or rounds other values in their place, can miss the bound.
Values may be sent and summed in bfloat16 or wider, within the bound.
A program may use at most 384 MiB of HBM per device.

```python
import functools
import jax
import jax.numpy as jnp
from jax import lax

D = 2048
HEADS = 64
HDIM = 64
STATE = 128
CONV = 4
BLOCK = 256
INNER = 4096
XBC = 4352
E = 8512
SMALL = 28096
TOK_DEV = 256
GT = 2048
GROUPS = 4
TOKENS = 8192
MAXLEN = 1024
MINLEN = 256


def small_pack(key, spread, dt_lowest, dt_highest):
    subkeys = jax.random.split(key, 7)
    conv_flat = jnp.clip(0.5 * jax.random.normal(subkeys[0], (CONV * XBC,), jnp.float32), -2.0, 2.0)
    conv_bias = jnp.clip(0.2 * jax.random.normal(subkeys[1], (XBC,), jnp.float32), -1.0, 1.0)
    dt_init = jnp.exp(jax.random.uniform(subkeys[2], (HEADS,), jnp.float32, jnp.log(dt_lowest), jnp.log(dt_highest)))
    dt_bias = jnp.log(jnp.expm1(dt_init))
    rate_log = jnp.log(jax.random.uniform(subkeys[3], (HEADS,), jnp.float32, 1.0, 16.0))
    skip_gain = jax.random.uniform(subkeys[4], (HEADS,), jnp.float32, 0.5, 1.5)
    norm_gain = jax.random.uniform(subkeys[5], (INNER,), jnp.float32, 1.0 - spread, 1.0 + spread)
    pre_gain = jax.random.uniform(subkeys[6], (D,), jnp.float32, 1.0 - spread, 1.0 + spread)
    return jnp.concatenate([conv_flat, conv_bias, dt_bias, rate_log, skip_gain, norm_gain, pre_gain]).astype(jnp.float32)


def draw_small_params(key, part):
    key = jax.random.fold_in(key, 11)
    return small_pack(key, 0.5, 0.0001, 0.1)


def draw_small_average(key, part):
    key = jax.random.fold_in(key, 12)
    return small_pack(key, 0.4, 0.0001, 0.1)


def draw_lengths(key, part):
    key = jax.random.fold_in(key, 21)
    leading = jax.random.randint(key, (GROUPS,), MINLEN, GT - MAXLEN - MINLEN + 1)
    middle = jnp.full((GROUPS,), MAXLEN, jnp.int32)
    return jnp.stack([leading, middle, GT - MAXLEN - leading], axis=1).astype(jnp.int32)


def permute_one(subkey):
    return jax.random.permutation(subkey, TOK_DEV)


def place_one(perm_row, value_row):
    return jnp.zeros((TOK_DEV,), jnp.int32).at[perm_row].set(value_row)


def draw_deal_slot(key, part):
    key = jax.random.fold_in(key, 31)
    shards = GT // TOK_DEV
    share = TOK_DEV // shards
    source_key, target_key = jax.random.split(key)
    source_perm = jax.vmap(permute_one)(jax.random.split(source_key, GROUPS * shards)).reshape(GROUPS, shards, TOK_DEV)
    target_perm = jax.vmap(permute_one)(jax.random.split(target_key, GROUPS * shards)).reshape(GROUPS, shards, TOK_DEV)
    ordinal = jnp.arange(TOK_DEV, dtype=jnp.int32)
    target = ordinal // share
    within = ordinal % share
    sources = jnp.arange(shards, dtype=jnp.int32)
    slot_in = sources[:, None] * share + within[None, :]
    chosen = target_perm[:, target[None, :], slot_in]
    slot_values = chosen + (target * TOK_DEV)[None, None, :]
    placed = jax.vmap(jax.vmap(place_one))(source_perm, slot_values)
    return placed.reshape(GROUPS * GT).astype(jnp.int32)


def steps_of(stream_key, shape, cuts, smallest, largest):
    factor_of = 1.0
    for axis_at, parts in cuts:
        draws = jax.random.uniform(jax.random.fold_in(jax.random.fold_in(stream_key, 6), axis_at), (parts,), jnp.float32, smallest / len(cuts), largest / len(cuts))
        factor_of = factor_of * jnp.repeat(jnp.exp(draws), shape[axis_at] // parts).reshape((-1,) + (1,) * (len(shape) - 1 - axis_at))
    return factor_of


def centred(own_key, dims, scale, limit, cuts=(), held_as=jnp.bfloat16):
    loudness = steps_of(own_key, dims, cuts, -0.22, 0.18) if cuts else 1.0
    drawn = jax.random.normal(own_key, dims, jnp.float32) * scale * loudness
    return jnp.minimum(jnp.maximum(drawn, -limit), limit).astype(held_as)


def setup_inputs(seed: int = 0) -> dict:
    streams_of = jax.random.split(jax.random.key(seed), 14)
    tokens = centred(streams_of[0], (TOKENS, D), 1.0, 6.0, ((0, 32),), jnp.float32)
    cotangent = centred(streams_of[1], (TOKENS, D), 1.0, 6.0, ((0, 32),), jnp.float32)
    lengths = draw_lengths(jax.random.fold_in(streams_of[13], 71), 0)
    deal_slot = draw_deal_slot(jax.random.fold_in(streams_of[13], 71), 0)
    in_weight = centred(streams_of[4], (D, E), D ** -0.5, 0.125, ((0, 8), (1, 4)), jnp.float32)
    out_weight = centred(streams_of[5], (INNER, D), INNER ** -0.5, 0.09375, ((0, 8), (1, 4)), jnp.float32)
    small_params = draw_small_params(jax.random.fold_in(streams_of[13], 71), 0)
    in_moment = centred(streams_of[7], (D, E), (0.3 * TOKENS ** 0.5), 160.0, ((0, 8), (1, 4)), jnp.float32)
    out_moment = centred(streams_of[8], (INNER, D), (0.8 * TOKENS ** 0.5), 448.0, ((0, 8), (1, 4)), jnp.float32)
    small_moment = centred(streams_of[9], (SMALL,), (0.3 * TOKENS ** 0.5), 160.0, (), jnp.float32)
    in_average = centred(streams_of[10], (D, E), D ** -0.5, 0.125, ((0, 8), (1, 4)), jnp.float32)
    out_average = centred(streams_of[11], (INNER, D), INNER ** -0.5, 0.09375, ((0, 8), (1, 4)), jnp.float32)
    small_average = draw_small_average(jax.random.fold_in(streams_of[13], 71), 0)
    return {"tokens": tokens, "cotangent": cotangent, "lengths": lengths, "deal_slot": deal_slot, "in_weight": in_weight, "out_weight": out_weight, "small_params": small_params, "in_moment": in_moment, "out_moment": out_moment, "small_moment": small_moment, "in_average": in_average, "out_average": out_average, "small_average": small_average}


eps_norm = 1e-05
momentum_decay = 0.9
weight_decay = 0.01
average_decay = 0.99
rate_in = 0.0001
rate_out = 3e-05
rate_small = 0.001

@jax.custom_vjp
def low(v):
    return lax.optimization_barrier(v.astype(jnp.bfloat16)).astype(jnp.float32)

@jax.custom_vjp
def low_back(v):
    return v

def low_keep(v):
    return (low(v), None)

def low_pass(kept, grad):
    return (grad,)

def back_keep(v):
    return (v, None)

def back_low(kept, grad):
    return (low(grad),)
low.defvjp(low_keep, low_pass)
low_back.defvjp(back_keep, back_low)

def unpack(packed_small):
    extents = [CONV * XBC, XBC, HEADS, HEADS, HEADS, INNER, D]
    pieces = []
    offset = 0
    for extent in extents:
        pieces.append(packed_small[offset:offset + extent])
        offset = offset + extent
    return pieces

def segment_of(positions, lengths_row):
    bounds = jnp.cumsum(lengths_row)[:-1]
    inside = lax.optimization_barrier(jnp.sum((positions[:, None] >= bounds[None, :]).astype(jnp.int32), axis=1))
    return jnp.where(positions < 0, -1, inside).astype(jnp.int32)

def convolve(conv_rows, edge_rows, seg_rows, seg_edge, conv_flat, conv_bias):
    extended = jnp.concatenate([edge_rows, conv_rows], axis=0)
    seg_ext = jnp.concatenate([seg_edge, seg_rows], axis=0)
    row_count = conv_rows.shape[0]
    conv_taps = conv_flat.reshape(CONV, XBC)
    conv_sum = jnp.zeros_like(conv_rows) + conv_bias[None, :]
    for tap_index in range(CONV):
        same_seq = (seg_ext[tap_index:tap_index + row_count] == seg_rows)[:, None]
        conv_sum = conv_sum + jnp.where(same_seq, extended[tap_index:tap_index + row_count] * conv_taps[tap_index][None, :], 0.0)
    return jax.nn.silu(conv_sum)

def block_step(carry, inputs):
    state_now, seg_prev, neg_rate = carry
    values, b_blk, c_blk, dt_blk, seg_blk = inputs
    log_decay = dt_blk * neg_rate[None, :]
    cumulative = jnp.cumsum(log_decay, axis=0)
    places = jnp.arange(seg_blk.shape[0])
    allowed = (seg_blk[:, None] == seg_blk[None, :]) & (places[:, None] >= places[None, :])
    spread = jnp.minimum(cumulative[:, None, :] - cumulative[None, :, :], 0.0)
    decay_mat = jnp.where(allowed[:, :, None], jnp.exp(spread), 0.0)
    scores = jnp.dot(c_blk, b_blk.T, precision=lax.Precision.HIGHEST)
    mixing = decay_mat * scores[:, :, None] * dt_blk[None, :, :]
    output = jnp.einsum('tsh,shp->thp', mixing, values, precision=lax.Precision.HIGHEST)
    carried = jnp.where((seg_blk == seg_prev)[:, None], jnp.exp(cumulative), 0.0)
    output = output + carried[:, :, None] * jnp.einsum('tn,hpn->thp', c_blk, state_now, precision=lax.Precision.HIGHEST)
    seg_last = seg_blk[-1]
    tail_weight = jnp.where((seg_blk == seg_last)[:, None], jnp.exp(cumulative[-1][None, :] - cumulative), 0.0) * dt_blk
    fresh_state = jnp.einsum('sh,shp,sn->hpn', tail_weight, values, b_blk, precision=lax.Precision.HIGHEST)
    keep_old = jnp.where(seg_last == seg_prev, jnp.exp(cumulative[-1]), 0.0)
    new_state = keep_old[:, None, None] * state_now + fresh_state
    return ((new_state, seg_last, neg_rate), output)

def mixer(packed_x, segments, in_low, out_low, packed_small):
    conv_flat, conv_bias, dt_bias, rate_log, skip_gain, norm_gain, pre_gain = unpack(packed_small)
    group_len = packed_x.shape[0]
    normed = packed_x * lax.rsqrt(lax.optimization_barrier(jnp.mean(packed_x * packed_x, axis=1, keepdims=True)) + eps_norm) * pre_gain[None, :]
    projected = low_back(jnp.dot(low(normed), in_low, precision=lax.Precision.HIGHEST))
    gate_part = projected[:, :INNER]
    conv_in = projected[:, INNER:INNER + XBC]
    dt_raw = projected[:, INNER + XBC:]
    edge_rows = jnp.zeros((CONV - 1, XBC), conv_in.dtype)
    seg_edge = jnp.full((CONV - 1,), -1, jnp.int32)
    conv_out = convolve(conv_in, edge_rows, segments, seg_edge, conv_flat, conv_bias)
    values = conv_out[:, :INNER].reshape(group_len, HEADS, HDIM)
    b_rows = conv_out[:, INNER:INNER + STATE]
    c_rows = conv_out[:, INNER + STATE:]
    dt_vals = jax.nn.softplus(dt_raw + dt_bias[None, :])
    neg_rate = -jnp.exp(rate_log)
    block_count = group_len // BLOCK
    start_carry = (jnp.zeros((HEADS, HDIM, STATE), packed_x.dtype), jnp.array(-1, jnp.int32), neg_rate)
    final_carry, ssd_out = lax.scan(jax.checkpoint(block_step), start_carry, (values.reshape(block_count, BLOCK, HEADS, HDIM), b_rows.reshape(block_count, BLOCK, STATE), c_rows.reshape(block_count, BLOCK, STATE), dt_vals.reshape(block_count, BLOCK, HEADS), segments.reshape(block_count, BLOCK)))
    mixed_rows = ssd_out.reshape(group_len, HEADS, HDIM) + skip_gain[None, :, None] * values
    gated_rows = mixed_rows.reshape(group_len, INNER) * jax.nn.silu(gate_part)
    normed_out = gated_rows * lax.rsqrt(lax.optimization_barrier(jnp.mean(gated_rows * gated_rows, axis=1, keepdims=True)) + eps_norm) * norm_gain[None, :]
    branch = low_back(jnp.dot(low(normed_out), out_low, precision=lax.Precision.HIGHEST))
    return packed_x + branch

def nesterov(weight, gradient, moment, average, step_rate):
    decayed = gradient + weight_decay * weight
    new_moment = momentum_decay * moment + decayed
    new_weight = weight - step_rate * (decayed + momentum_decay * new_moment)
    new_average = average_decay * average + (1.0 - average_decay) * new_weight
    return (new_moment, new_weight, new_average)

def pack_rows(row_block, slot_row):
    return jnp.zeros_like(row_block).at[slot_row].set(row_block)

def take_rows(row_block, slot_row):
    return row_block[slot_row]

def reference(tokens, cotangent, lengths, deal_slot, in_weight, out_weight, small_params, in_moment, out_moment, small_moment, in_average, out_average, small_average):
    positions = jnp.arange(GT, dtype=jnp.int32)
    segments = jax.vmap(functools.partial(segment_of, positions))(lengths)
    slot_rows = deal_slot.reshape(GROUPS, GT)
    packed_x = jax.vmap(pack_rows)(tokens.reshape(GROUPS, GT, D), slot_rows)
    packed_cot = jax.vmap(pack_rows)(cotangent.reshape(GROUPS, GT, D), slot_rows)

    def forward(packed_all, in_full, out_full, small_full):
        in_low = low(in_full)
        out_low = low(out_full)

        def one_group(pair):
            return mixer(pair[0], pair[1], in_low, out_low, small_full)
        return lax.map(jax.checkpoint(one_group), (packed_all, segments))
    block_packed, pullback = jax.vjp(forward, packed_x, in_weight, out_weight, small_params)
    grad_packed, grad_in, grad_out, grad_small = pullback(packed_cot)
    block_out = jax.vmap(take_rows)(block_packed, slot_rows).reshape(TOKENS, D)
    input_grad = jax.vmap(take_rows)(grad_packed, slot_rows).reshape(TOKENS, D)
    in_new = nesterov(in_weight, grad_in, in_moment, in_average, rate_in)
    out_new = nesterov(out_weight, grad_out, out_moment, out_average, rate_out)
    small_new = nesterov(small_params, grad_small, small_moment, small_average, rate_small)
    return (block_out, input_grad, in_new[0], in_new[1], in_new[2], out_new[0], out_new[1], out_new[2], small_new[0], small_new[1], small_new[2])
```

```python
import functools

import jax
import jax.numpy as jnp
from jax import lax
from jax.sharding import PartitionSpec as P

D = 2048
HEADS = 64
HDIM = 64
STATE = 128
CONV = 4
BLOCK = 256
INNER = 4096
XBC = 4352
SHARED = 2 * STATE


eps_norm = 1e-05
momentum_decay = 0.9
weight_decay = 0.01
average_decay = 0.99
rate_in = 0.0001
rate_out = 3e-05
rate_small = 0.001


def unpack(packed_small):
    extents = [CONV * XBC, XBC, HEADS, HEADS, HEADS, INNER, D]
    pieces = []
    offset = 0
    for extent in extents:
        pieces.append(packed_small[offset : offset + extent])
        offset = offset + extent
    return pieces


def segment_of(positions, lengths_row):
    bounds = jnp.cumsum(lengths_row)[:-1]
    inside = jnp.sum((positions[:, None] >= bounds[None, :]).astype(jnp.int32), axis=1)
    return jnp.where(positions < 0, -1, inside)


def convolve(conv_rows, seg_rows, conv_taps, conv_bias):
    row_count, width = conv_rows.shape
    extended = jnp.concatenate([jnp.zeros((CONV - 1, width), conv_rows.dtype), conv_rows], axis=0)
    seg_ext = jnp.concatenate([jnp.full((CONV - 1,), -1, jnp.int32), seg_rows], axis=0)
    conv_sum = jnp.zeros_like(conv_rows) + conv_bias[None, :]
    for tap_index in range(CONV):
        same_seq = (seg_ext[tap_index : tap_index + row_count] == seg_rows)[:, None]
        conv_sum = conv_sum + jnp.where(
            same_seq,
            extended[tap_index : tap_index + row_count] * conv_taps[tap_index][None, :],
            0.0,
        )
    return jax.nn.silu(conv_sum)


def block_step(carry, inputs):
    state_now, seg_prev, neg_rate = carry
    values, b_blk, c_blk, dt_blk, seg_blk = inputs
    log_decay = dt_blk * neg_rate[None, :]
    cumulative = jnp.cumsum(log_decay, axis=0)
    places = jnp.arange(seg_blk.shape[0])
    allowed = (seg_blk[:, None] == seg_blk[None, :]) & (places[:, None] >= places[None, :])
    spread = jnp.minimum(cumulative[:, None, :] - cumulative[None, :, :], 0.0)
    decay_mat = jnp.where(allowed[:, :, None], jnp.exp(spread), 0.0)
    scores = jnp.dot(c_blk, b_blk.T, precision=lax.Precision.HIGHEST)
    mixing = decay_mat * scores[:, :, None] * dt_blk[None, :, :]
    output = jnp.einsum("tsh,shp->thp", mixing, values, precision=lax.Precision.HIGHEST)
    carried = jnp.where((seg_blk == seg_prev)[:, None], jnp.exp(cumulative), 0.0)
    output = output + carried[:, :, None] * jnp.einsum(
        "tn,hpn->thp", c_blk, state_now, precision=lax.Precision.HIGHEST
    )
    seg_last = seg_blk[-1]
    tail_weight = (
        jnp.where(
            (seg_blk == seg_last)[:, None], jnp.exp(cumulative[-1][None, :] - cumulative), 0.0
        )
        * dt_blk
    )
    fresh_state = jnp.einsum(
        "sh,shp,sn->hpn", tail_weight, values, b_blk, precision=lax.Precision.HIGHEST
    )
    keep_old = jnp.where(seg_last == seg_prev, jnp.exp(cumulative[-1]), 0.0)
    new_state = keep_old[:, None, None] * state_now + fresh_state
    return ((new_state, seg_last, neg_rate), output)


def recursion(values, b_rows, c_rows, dt_raw, dt_bias, rate_log, seg_rows):
    row_count, heads = dt_raw.shape
    dt_vals = jax.nn.softplus(dt_raw + dt_bias[None, :])
    neg_rate = -jnp.exp(rate_log)
    blocks = row_count // BLOCK
    start = (jnp.zeros((heads, HDIM, STATE), jnp.float32), jnp.array(-1, jnp.int32), neg_rate)
    _, out = lax.scan(
        jax.checkpoint(block_step),
        start,
        (
            values.reshape(blocks, BLOCK, heads, HDIM),
            b_rows.reshape(blocks, BLOCK, STATE),
            c_rows.reshape(blocks, BLOCK, STATE),
            dt_vals.reshape(blocks, BLOCK, heads),
            seg_rows.reshape(blocks, BLOCK),
        ),
    )
    return out.reshape(row_count, heads * HDIM)


def silu_grad(value):
    sig = jax.nn.sigmoid(value)
    return sig * (1.0 + value * (1.0 - sig))


def nesterov(weight, gradient, moment, average, step_rate):
    decayed = gradient + weight_decay * weight
    new_moment = momentum_decay * moment + decayed
    new_weight = weight - step_rate * (decayed + momentum_decay * new_moment)
    new_average = average_decay * average + (1.0 - average_decay) * new_weight
    return (new_moment, new_weight, new_average)


def dot32(a, b, contract=((1,), (0,))):
    return lax.dot_general(a, b, (contract, ((), ())), preferred_element_type=jnp.float32)


def own_slice(value, index, width, axis):
    return lax.dynamic_slice_in_dim(value, index * width, width, axis)


def local(
    tokens,
    cotangent,
    lengths,
    deal_slot,
    in_weight,
    out_weight,
    small_params,
    in_moment,
    out_moment,
    small_moment,
    in_average,
    out_average,
    small_average,
):
    shards, groups = lax.axis_size("shard"), lax.axis_size("group")
    shard, group = lax.axis_index("shard"), lax.axis_index("group")
    rows, width = tokens.shape
    per = rows // shards
    total = rows * shards
    blocks = total // BLOCK
    heads = HEADS // shards
    inner = INNER // shards
    shared = SHARED // shards
    conv_flat, conv_bias, dt_bias, rate_log, skip_gain, norm_gain, pre_gain = unpack(small_params)
    taps = conv_flat.reshape(CONV, XBC)

    rank = jnp.sum((deal_slot[None, :] < deal_slot[:, None]).astype(jnp.int32), axis=1)
    sort_mat = (rank[None, :] == jnp.arange(rows)[:, None]).astype(jnp.bfloat16)
    sorted_slot = jnp.sum(jnp.where(sort_mat > 0, deal_slot[None, :], 0), axis=1)
    r_in = lax.rsqrt(jnp.mean(tokens * tokens, axis=1, keepdims=True) + eps_norm)
    normed_low = (tokens * r_in * pre_gain[None, :]).astype(jnp.bfloat16)
    x_sorted = dot32(sort_mat, normed_low).astype(jnp.bfloat16)
    c_sorted = dot32(sort_mat, cotangent.astype(jnp.bfloat16)).astype(jnp.bfloat16)
    x_all = lax.all_gather(x_sorted, "shard")
    c_all = lax.all_gather(c_sorted, "shard")
    slot_all = lax.all_gather(sorted_slot, "shard")

    slot_blk = slot_all.reshape(shards, blocks, per).transpose(1, 0, 2).reshape(blocks, BLOCK)
    slot_blk = slot_blk - jnp.arange(blocks, dtype=jnp.int32)[:, None] * BLOCK
    place = (slot_blk[:, None, :] == jnp.arange(BLOCK)[None, :, None]).astype(jnp.bfloat16)

    def to_packed(value):
        value = value.reshape(shards, blocks, per, -1).transpose(1, 0, 2, 3)
        value = value.reshape(blocks, BLOCK, -1)
        value = jnp.einsum("bps,bsd->bpd", place, value, preferred_element_type=jnp.float32)
        return value.astype(jnp.bfloat16).reshape(total, -1)

    def to_sorted(value):
        value = jnp.einsum(
            "bps,bpd->bsd", place, value.reshape(blocks, BLOCK, -1), preferred_element_type=jnp.float32
        )
        value = value.astype(jnp.bfloat16).reshape(blocks, shards, per, -1).transpose(1, 0, 2, 3)
        return value.reshape(total, -1)

    normed = to_packed(x_all)
    cot_low = to_packed(c_all)
    seg_rows = segment_of(jnp.arange(total, dtype=jnp.int32), lengths[0])

    part = in_weight.shape[0] // groups
    pieces = in_weight.astype(jnp.bfloat16).reshape(groups, part, -1)
    pieces = lax.all_to_all(pieces, "group", 0, 0)
    pieces = pieces.transpose(1, 0, 2).reshape(part, -1)

    def cut(lo, each):
        return pieces[:, lo : lo + each * shards].reshape(part, shards, each).transpose(1, 0, 2)

    spread = jnp.broadcast_to(pieces[None, :, 2 * INNER : 2 * INNER + SHARED], (shards, part, SHARED))
    send = jnp.concatenate(
        [cut(0, inner), cut(INNER, inner), spread, cut(2 * INNER + SHARED, heads)], axis=2
    )
    got = lax.all_to_all(send, "shard", 0, 0)
    got = lax.all_gather(got, "group")
    in_low = got.transpose(1, 0, 2, 3).reshape(width, -1)
    out_low = lax.all_gather(out_weight.astype(jnp.bfloat16), "group", axis=1, tiled=True)
    out_full = lax.all_gather(out_low, "shard", axis=0, tiled=True)

    projected = dot32(normed, in_low)
    gate_part = projected[:, :inner]
    conv_v = projected[:, inner : 2 * inner]
    conv_bc = projected[:, 2 * inner : 2 * inner + SHARED]
    dt_raw = projected[:, 2 * inner + SHARED :]
    taps_v = own_slice(taps[:, :INNER], shard, inner, 1)
    bias_v = own_slice(conv_bias[:INNER], shard, inner, 0)
    bc_out = convolve(conv_bc, seg_rows, taps[:, INNER:], conv_bias[INNER:])
    values, pull_v = jax.vjp(
        lambda c, t, b: convolve(c, seg_rows, t, b), conv_v, taps_v, bias_v
    )
    ssd, pull_ssd = jax.vjp(
        functools.partial(recursion, seg_rows=seg_rows),
        values,
        bc_out[:, :STATE],
        bc_out[:, STATE:],
        dt_raw,
        own_slice(dt_bias, shard, heads, 0),
        own_slice(rate_log, shard, heads, 0),
    )
    skip_own = own_slice(skip_gain, shard, heads, 0)
    skip_wide = jnp.repeat(skip_own, HDIM)
    gain_own = own_slice(norm_gain, shard, inner, 0)
    mixed = ssd + skip_wide[None, :] * values
    gate_act = jax.nn.silu(gate_part)
    gated = mixed * gate_act
    d_out = dot32(cot_low, out_low, ((1,), (1,)))
    sums = jnp.stack(
        [jnp.sum(gated * gated, axis=1), jnp.sum(gated * gain_own[None, :] * d_out, axis=1)]
    )
    sums = lax.psum(sums, "shard") / INNER
    r_out = lax.rsqrt(sums[0] + eps_norm)[:, None]
    normed_out = (gated * r_out * gain_own[None, :]).astype(jnp.bfloat16)
    grad_out_part = dot32(normed_out, cot_low, ((0,), (0,)))
    grad_out = lax.psum_scatter(grad_out_part, "group", scatter_dimension=1, tiled=True)

    home = lax.all_to_all(to_sorted(normed_out).reshape(shards, rows, inner), "shard", 0, 0)
    home = home.transpose(1, 0, 2).reshape(rows, INNER)
    home = dot32(sort_mat, home, ((0,), (0,))).astype(jnp.bfloat16)
    block_out = tokens + dot32(home, out_full)

    d_gated = r_out * (gain_own[None, :] * d_out - gated * (r_out * r_out) * sums[1][:, None])
    grad_norm = jnp.sum(gated * r_out * d_out, axis=0)
    d_mixed = d_gated * gate_act
    d_gate = d_gated * mixed * silu_grad(gate_part)
    grad_skip = jnp.sum(jnp.sum(d_mixed * values, axis=0).reshape(heads, HDIM), axis=1)
    d_values, d_b, d_c, d_dtraw, grad_dtb, grad_rate = pull_ssd(d_mixed)
    d_values = d_values + skip_wide[None, :] * d_mixed
    d_conv_v, grad_taps_v, grad_bias_v = pull_v(d_values)
    d_bc = jnp.concatenate([d_b, d_c], axis=1)
    d_bc = lax.psum_scatter(d_bc.T, "shard", scatter_dimension=0, tiled=True).T
    _, pull_bc = jax.vjp(
        lambda c, t, b: convolve(c, seg_rows, t, b),
        own_slice(conv_bc, shard, shared, 1),
        own_slice(taps[:, INNER:], shard, shared, 1),
        own_slice(conv_bias[INNER:], shard, shared, 0),
    )
    d_conv_bc, grad_taps_bc, grad_bias_bc = pull_bc(d_bc)
    d_project = jnp.concatenate([d_gate, d_conv_v, d_conv_bc, d_dtraw], axis=1).astype(jnp.bfloat16)
    in_own = jnp.concatenate(
        [
            in_low[:, : 2 * inner],
            own_slice(in_low[:, 2 * inner : 2 * inner + SHARED], shard, shared, 1),
            in_low[:, 2 * inner + SHARED :],
        ],
        axis=1,
    )
    d_normed = dot32(to_sorted(d_project), in_own, ((1,), (1,)))
    d_normed = lax.psum_scatter(d_normed, "shard", scatter_dimension=0, tiled=True)
    d_normed = jnp.dot(
        sort_mat.T.astype(jnp.float32), d_normed, precision=lax.Precision.HIGHEST
    )
    d_scaled = pre_gain[None, :] * d_normed
    inside = jnp.mean(tokens * d_scaled, axis=1, keepdims=True)
    input_grad = cotangent + r_in * (d_scaled - tokens * (r_in * r_in) * inside)
    grad_pre = jnp.sum(tokens * r_in * d_normed, axis=0)

    grad_in = dot32(normed, d_project, ((0,), (0,)))
    grad_in = grad_in.reshape(shards, groups, part, -1)
    grad_in = lax.psum_scatter(grad_in, "group", scatter_dimension=1)
    grad_in = lax.all_to_all(grad_in, "shard", 0, 0)

    def join(lo, each):
        return grad_in[:, :, lo : lo + each].transpose(1, 0, 2).reshape(part, shards * each)

    grad_in = jnp.concatenate(
        [
            join(0, inner),
            join(inner, inner),
            join(2 * inner, shared),
            join(2 * inner + shared, heads),
        ],
        axis=1,
    )
    grad_in = grad_in.reshape(part, groups, -1).transpose(1, 0, 2)
    grad_in = lax.all_to_all(grad_in, "group", 0, 0).reshape(in_weight.shape)

    mine = [
        grad_taps_v.reshape(-1),
        grad_taps_bc.reshape(-1),
        grad_bias_v,
        grad_bias_bc,
        grad_dtb,
        grad_rate,
        grad_skip,
        grad_norm,
    ]
    extents = [piece.shape[0] for piece in mine]
    mine = lax.all_gather(lax.psum(jnp.concatenate(mine), "group"), "shard")
    found, offset = [], 0
    for extent in extents:
        found.append(mine[:, offset : offset + extent])
        offset = offset + extent

    def taps_of(piece):
        return piece.reshape(shards, CONV, -1).transpose(1, 0, 2).reshape(CONV, -1)

    grad_taps = jnp.concatenate([taps_of(found[0]), taps_of(found[1])], axis=1).reshape(-1)
    grad_small = jnp.concatenate(
        [grad_taps] + [piece.reshape(-1) for piece in found[2:]]
        + [lax.psum(grad_pre, ("group", "shard"))]
    )
    in_new = nesterov(in_weight, grad_in, in_moment, in_average, rate_in)
    out_new = nesterov(out_weight, grad_out, out_moment, out_average, rate_out)
    small_new = nesterov(small_params, grad_small, small_moment, small_average, rate_small)
    return (block_out, input_grad) + in_new + out_new + small_new


def solution(mesh):
    rows = P(("group", "shard"), None)
    tile = P("shard", "group")
    return jax.shard_map(
        local,
        mesh=mesh,
        in_specs=(
            rows,
            rows,
            P("group", None),
            P(("group", "shard")),
            tile,
            tile,
            P(),
            tile,
            tile,
            P(),
            tile,
            tile,
            P(),
        ),
        out_specs=(rows, rows, tile, tile, tile, tile, tile, tile, P(), P(), P()),
        check_vma=False,
    )
```

```python
import functools

import jax
import jax.numpy as jnp
from jax import lax
from jax.experimental import pallas as pl
from jax.experimental.pallas import tpu as pltpu
from jax.sharding import PartitionSpec as P

D = 2048
HEADS = 64
HDIM = 64
STATE = 128
CONV = 4
BLOCK = 256
INNER = 4096
XBC = 4352
SHARED = 2 * STATE
TAIL = 8


eps_norm = 1e-05
momentum_decay = 0.9
weight_decay = 0.01
average_decay = 0.99
rate_in = 0.0001
rate_out = 3e-05
rate_small = 0.001


def unpack(packed_small):
    extents = [CONV * XBC, XBC, HEADS, HEADS, HEADS, INNER, D]
    pieces = []
    offset = 0
    for extent in extents:
        pieces.append(packed_small[offset : offset + extent])
        offset = offset + extent
    return pieces


def segment_of(positions, lengths_row):
    bounds = jnp.cumsum(lengths_row)[:-1]
    inside = jnp.sum((positions[:, None] >= bounds[None, :]).astype(jnp.int32), axis=1)
    return jnp.where(positions < 0, -1, inside)


def convolve(conv_rows, seg_rows, conv_taps, conv_bias):
    row_count, width = conv_rows.shape
    extended = jnp.concatenate([jnp.zeros((CONV - 1, width), conv_rows.dtype), conv_rows], axis=0)
    seg_ext = jnp.concatenate([jnp.full((CONV - 1,), -1, jnp.int32), seg_rows], axis=0)
    conv_sum = jnp.zeros_like(conv_rows) + conv_bias[None, :]
    for tap_index in range(CONV):
        same_seq = (seg_ext[tap_index : tap_index + row_count] == seg_rows)[:, None]
        conv_sum = conv_sum + jnp.where(
            same_seq,
            extended[tap_index : tap_index + row_count] * conv_taps[tap_index][None, :],
            0.0,
        )
    return jax.nn.silu(conv_sum)


def split(value):
    high = value.astype(jnp.bfloat16)
    return high, (value - high.astype(jnp.float32)).astype(jnp.bfloat16)


def dots(a, b, contract):
    return lax.dot_general(a, b, (contract, ((), ())), preferred_element_type=jnp.float32)


def dot3(a, b, contract=((1,), (0,))):
    a = a if isinstance(a, tuple) else split(a)
    b = b if isinstance(b, tuple) else split(b)
    return dots(a[0], b[0], contract) + (dots(a[0], b[1], contract) + dots(a[1], b[0], contract))


NT = ((1,), (1,))


def head_sums(value, marks):
    high = value.astype(jnp.bfloat16)
    rest = value - high.astype(jnp.float32)
    mid = rest.astype(jnp.bfloat16)
    low = (rest - mid.astype(jnp.float32)).astype(jnp.bfloat16)
    return dots(marks, high, NT) + (dots(marks, mid, NT) + dots(marks, low, NT))


def widen(columns, heads):
    rows = columns.shape[0]
    low_half = lax.broadcasted_iota(jnp.int32, (rows, 2 * HDIM), 1) < HDIM
    return jnp.concatenate(
        [
            jnp.where(low_half, columns[:, h : h + 1], columns[:, h + 1 : h + 2])
            for h in range(0, heads, 2)
        ],
        axis=1,
    )


def running_sum(value, reverse=False):
    lane = lax.broadcasted_iota(jnp.int32, value.shape, 1)
    count = value.shape[1]
    step = 1
    while step < count:
        if reverse:
            value = value + jnp.where(lane < count - step, pltpu.roll(value, count - step, 1), 0.0)
        else:
            value = value + jnp.where(lane >= step, pltpu.roll(value, step, 1), 0.0)
        step *= 2
    return value


def sequence_of(positions, bounds):
    inside = jnp.where(positions >= bounds[0], 1, 0) + jnp.where(positions >= bounds[1], 1, 0)
    return jnp.where(positions < 0, -1, inside)


def block_facts(block, bounds, dt_t, rate):
    start = block * BLOCK
    seg_col = sequence_of(start + lax.broadcasted_iota(jnp.int32, (BLOCK, 1), 0), bounds)
    seg_row = sequence_of(start + lax.broadcasted_iota(jnp.int32, (1, BLOCK), 1), bounds)
    before = sequence_of(start - 1 + lax.broadcasted_iota(jnp.int32, (1, 1), 1), bounds)
    last = sequence_of(start + BLOCK - 1 + lax.broadcasted_iota(jnp.int32, (1, 1), 1), bounds)
    run_t = running_sum(dt_t * rate)
    run = run_t.T
    final = run[BLOCK - 1 :, :]
    carried = jnp.where(seg_col == before, jnp.exp(run), 0.0)
    tail = jnp.where(seg_col == last, jnp.exp(final - run), 0.0)
    keep = jnp.where(last == before, jnp.exp(final), 0.0)
    return seg_col, seg_row, run_t, run, carried, tail, keep


def forward_kernel(
    heads, bounds, gate, conv_v, conv_bc, dt_t, d_out, taps, bias, rate, skip, gain,
    pre_out, mixed_out, state_out, sums_out, ext, state,
):
    block = pl.program_id(0)
    inner = heads * HDIM

    @pl.when(block == 0)
    def _():
        ext[:TAIL, :] = jnp.zeros((TAIL, ext.shape[1]), jnp.float32)
        state[...] = jnp.zeros_like(state)

    bounds = (bounds[0], bounds[1])
    seg_col, seg_row, run_t, run, carried, tail, keep = block_facts(block, bounds, dt_t[...], rate[...])
    ext[TAIL:, :inner] = conv_v[...]
    ext[TAIL:, inner:] = conv_bc[...]
    place = block * BLOCK + lax.broadcasted_iota(jnp.int32, (BLOCK, 1), 0)
    pre = bias[...] + taps[CONV - 1 : CONV, :] * ext[TAIL:, :]
    for back in range(1, CONV):
        same = sequence_of(place - back, bounds) == seg_col
        moved = ext[TAIL - back : TAIL - back + BLOCK, :]
        pre = pre + jnp.where(same, moved, 0.0) * taps[CONV - 1 - back : CONV - back, :]
    ext[:TAIL, :] = ext[BLOCK:, :]
    pre_out[...] = pre
    conv = pre / (1.0 + jnp.exp(-pre))
    values, b_rows, c_rows = conv[:, :inner], conv[:, inner : inner + STATE], conv[:, inner + STATE :]
    dt = dt_t[...].T
    fed = values * widen(dt, heads)
    rows = lax.broadcasted_iota(jnp.int32, (BLOCK, BLOCK), 0)
    cols = lax.broadcasted_iota(jnp.int32, (BLOCK, BLOCK), 1)
    allowed = (seg_col == seg_row) & (rows >= cols)
    b_parts, c_parts = split(b_rows), split(c_rows)
    scores = jnp.where(allowed, dot3(c_parts, b_parts, NT), 0.0)
    old = state[...]
    state_out[0] = old
    output = widen(carried, heads) * dot3(c_parts, old)
    low_half = lax.broadcasted_iota(jnp.int32, (BLOCK, 2 * HDIM), 1) < HDIM
    inside = []
    for h in range(0, heads, 2):
        pair = split(fed[:, h * HDIM : (h + 2) * HDIM])
        found = []
        for k in (h, h + 1):
            mixing = jnp.exp(jnp.minimum(run[:, k : k + 1] - run_t[k : k + 1, :], 0.0)) * scores
            found.append(dot3(mixing, pair))
        inside.append(jnp.where(low_half, found[0], found[1]))
    mixed = output + jnp.concatenate(inside, axis=1) + skip[...] * values
    mixed_out[...] = mixed
    state[...] = widen(keep, heads) * old + dot3(b_rows.T, widen(tail, heads) * fed)
    gated = mixed * (gate[...] / (1.0 + jnp.exp(-gate[...])))
    sums_out[:, 0:1] = jnp.sum(gated * gated, axis=1, keepdims=True)
    sums_out[:, 1:2] = jnp.sum(gated * gain[...] * d_out[...], axis=1, keepdims=True)


def backward_kernel(
    heads, blocks, bounds, pre, mixed, gate, d_out, conv_v, sums, state_in, dt_t, taps, rate, skip, gain, marks,
    d_cols, d_bc, d_dt, grads, grad_rate, ext, carry,
):
    step = pl.program_id(0)
    block = blocks - 1 - step
    inner = heads * HDIM

    @pl.when(step == 0)
    def _():
        ext[BLOCK:, :] = jnp.zeros((TAIL, ext.shape[1]), jnp.float32)
        carry[...] = jnp.zeros_like(carry)
        grads[...] = jnp.zeros_like(grads)
        grad_rate[...] = jnp.zeros_like(grad_rate)

    bounds = (bounds[0], bounds[1])
    seg_col, seg_row, run_t, run, carried, tail, keep = block_facts(block, bounds, dt_t[...], rate[...])
    r_out = lax.rsqrt(sums[:, 0:1] + 1e-05)
    inside = sums[:, 1:2]
    gate_now = gate[...]
    gate_sig = 1.0 / (1.0 + jnp.exp(-gate_now))
    act = gate_now * gate_sig
    mixed_now = mixed[...]
    gated = mixed_now * act
    d_out_now = d_out[...]
    d_gated = r_out * (gain[...] * d_out_now - gated * (r_out * r_out) * inside)
    dy = d_gated * act
    d_cols[:, :inner] = (d_gated * mixed_now * (gate_sig * (1.0 + gate_now * (1.0 - gate_sig)))).astype(jnp.bfloat16)
    grads[5:6, :] += jnp.sum(gated * r_out * d_out_now, axis=0, keepdims=True)
    pre_now = pre[...]
    sig = 1.0 / (1.0 + jnp.exp(-pre_now))
    conv = pre_now * sig
    values, b_rows, c_rows = conv[:, :inner], conv[:, inner : inner + STATE], conv[:, inner + STATE :]
    grads[6:7, :] += jnp.sum(dy * values, axis=0, keepdims=True)
    dt_wide = widen(dt_t[...].T, heads)
    fed = values * dt_wide
    old, after = state_in[0], carry[...]
    b_parts, c_parts, old_parts, after_parts = split(b_rows), split(c_rows), split(old), split(after)
    carried_wide, tail_wide, keep_wide = widen(carried, heads), widen(tail, heads), widen(keep, heads)
    rows = lax.broadcasted_iota(jnp.int32, (BLOCK, BLOCK), 0)
    cols = lax.broadcasted_iota(jnp.int32, (BLOCK, BLOCK), 1)
    allowed = (seg_col == seg_row) & (cols >= rows)
    scores_t = jnp.where(allowed, dot3(b_parts, c_parts, NT), 0.0)
    low_half = lax.broadcasted_iota(jnp.int32, (BLOCK, 2 * HDIM), 1) < HDIM
    d_scores_t = jnp.zeros((BLOCK, BLOCK), jnp.float32)
    d_fed, row_terms, col_terms = [], [], []
    for h in range(0, heads, 2):
        fed_pair = fed[:, h * HDIM : (h + 2) * HDIM]
        dy_pair = split(dy[:, h * HDIM : (h + 2) * HDIM])
        found = []
        for k in (h, h + 1):
            own = low_half if k == h else jnp.logical_not(low_half)
            d_mixing = dot3(jnp.where(own, fed_pair, 0.0), dy_pair, NT)
            decay = jnp.exp(jnp.minimum(run_t[k : k + 1, :] - run[:, k : k + 1], 0.0))
            mixing = decay * scores_t
            d_scores_t = d_scores_t + decay * d_mixing
            flow = mixing * d_mixing
            row_terms.append(jnp.sum(flow, axis=0, keepdims=True))
            col_terms.append(jnp.sum(flow, axis=1, keepdims=True))
            found.append(dot3(mixing, dy_pair))
        d_fed.append(jnp.where(low_half, found[0], found[1]))
    d_scores_t = split(jnp.where(allowed, d_scores_t, 0.0))
    fed_tail = fed * tail_wide
    dy_carried = dy * carried_wide
    d_fed_out = tail_wide * dot3(b_parts, after_parts)
    d_fed = jnp.concatenate(d_fed, axis=1) + d_fed_out
    dy_parts, tail_parts = split(dy_carried), split(fed_tail)
    d_bc[:, :STATE] = dot3(d_scores_t, c_parts) + dot3(tail_parts, after_parts, NT)
    d_bc[:, STATE:] = dot3(d_scores_t, b_parts, ((0,), (0,))) + dot3(dy_parts, old_parts, NT)
    head_count = dt_t.shape[0]
    pad = [jnp.zeros((1, BLOCK), jnp.float32)] * (head_count - heads)
    pad_col = [jnp.zeros((BLOCK, 1), jnp.float32)] * (head_count - heads)
    d_run = jnp.concatenate(row_terms + pad, axis=0) - jnp.concatenate(col_terms + pad_col, axis=1).T
    d_run = d_run + head_sums(dy_carried * dot3(c_parts, old_parts), marks[...])
    leaving = head_sums(fed * d_fed_out, marks[...])
    kept = jnp.sum(old * after, axis=0, keepdims=True) * keep_wide
    kept = jnp.sum(marks[...].astype(jnp.float32) * kept, axis=1, keepdims=True)
    at_end = lax.broadcasted_iota(jnp.int32, (head_count, BLOCK), 1) == BLOCK - 1
    total = jnp.sum(leaving, axis=1, keepdims=True) + kept
    d_run = d_run - leaving + jnp.where(at_end, total, 0.0)
    d_log = running_sum(d_run, reverse=True)
    d_dt[...] = d_log * rate[...] + head_sums(values * d_fed, marks[...])
    grad_rate[...] += d_log * (dt_t[...] * rate[...])
    carry[...] = keep_wide * after + dot3(c_rows.T, dy_parts)
    pre_v, sig_v = pre_now[:, :inner], sig[:, :inner]
    d_values = dt_wide * d_fed + skip[...] * dy
    d_pre = d_values * (sig_v * (1.0 + pre_v * (1.0 - sig_v)))
    ext[:BLOCK, :] = d_pre
    place = block * BLOCK + lax.broadcasted_iota(jnp.int32, (BLOCK, 1), 0)
    conv_in = conv_v[...]
    d_conv = taps[CONV - 1 : CONV, :] * d_pre
    grads[CONV - 1 : CONV, :] += jnp.sum(conv_in * d_pre, axis=0, keepdims=True)
    grads[CONV : CONV + 1, :] += jnp.sum(d_pre, axis=0, keepdims=True)
    for ahead in range(1, CONV):
        same = sequence_of(place + ahead, bounds) == seg_col
        moved = jnp.where(same, ext[ahead : ahead + BLOCK, :], 0.0)
        d_conv = d_conv + taps[CONV - 1 - ahead : CONV - ahead, :] * moved
        grads[CONV - 1 - ahead : CONV - ahead, :] += jnp.sum(conv_in * moved, axis=0, keepdims=True)
    ext[BLOCK:, :] = ext[:TAIL, :]
    d_cols[:, inner:] = d_conv.astype(jnp.bfloat16)


def whole(shape):
    return pl.BlockSpec(shape, lambda *_: (0,) * len(shape))


def mixer_forward(bounds, projected, dt_t, d_out, taps, bias, rate, skip, gain):
    total, inner = d_out.shape
    heads, blocks, padded = inner // HDIM, total // BLOCK, dt_t.shape[0]

    def block_of(width, column):
        return pl.BlockSpec((BLOCK, width), lambda i, _: (i, column))

    return pl.pallas_call(
        functools.partial(forward_kernel, heads),
        grid_spec=pltpu.PrefetchScalarGridSpec(
            num_scalar_prefetch=1,
            grid=(blocks,),
            in_specs=[
                block_of(inner, 0),
                block_of(inner, 1),
                block_of(SHARED, 2 * inner // SHARED),
                pl.BlockSpec((padded, BLOCK), lambda i, _: (0, i)),
                block_of(inner, 0),
                whole(taps.shape),
                whole(bias.shape),
                whole(rate.shape),
                whole(skip.shape),
                whole(gain.shape),
            ],
            out_specs=[
                block_of(inner + SHARED, 0),
                block_of(inner, 0),
                pl.BlockSpec((1, STATE, inner), lambda i, _: (i, 0, 0)),
                block_of(2, 0),
            ],
            scratch_shapes=[
                pltpu.VMEM((BLOCK + TAIL, inner + SHARED), jnp.float32),
                pltpu.VMEM((STATE, inner), jnp.float32),
            ],
        ),
        out_shape=[
            jax.ShapeDtypeStruct((total, inner + SHARED), jnp.float32),
            jax.ShapeDtypeStruct((total, inner), jnp.float32),
            jax.ShapeDtypeStruct((blocks, STATE, inner), jnp.float32),
            jax.ShapeDtypeStruct((total, 2), jnp.float32),
        ],
        compiler_params=pltpu.CompilerParams(vmem_limit_bytes=48 * 1024 * 1024),
        name="mixer_forward",
    )(bounds, projected, projected, projected, dt_t, d_out, taps, bias, rate, skip, gain)


def mixer_backward(bounds, pre, mixed, projected, d_out, sums, states, dt_t, taps, rate, skip, gain):
    total, inner = d_out.shape
    heads, blocks, padded = inner // HDIM, total // BLOCK, dt_t.shape[0]
    marks = (jnp.arange(padded)[:, None] == jnp.arange(inner)[None, :] // HDIM).astype(jnp.bfloat16)

    def block_of(width, column):
        return pl.BlockSpec((BLOCK, width), lambda i, _: (blocks - 1 - i, column))

    return pl.pallas_call(
        functools.partial(backward_kernel, heads, blocks),
        grid_spec=pltpu.PrefetchScalarGridSpec(
            num_scalar_prefetch=1,
            grid=(blocks,),
            in_specs=[
                block_of(inner + SHARED, 0),
                block_of(inner, 0),
                block_of(inner, 0),
                block_of(inner, 0),
                block_of(inner, 1),
                block_of(2, 0),
                pl.BlockSpec((1, STATE, inner), lambda i, _: (blocks - 1 - i, 0, 0)),
                pl.BlockSpec((padded, BLOCK), lambda i, _: (0, blocks - 1 - i)),
                whole(taps.shape),
                whole(rate.shape),
                whole(skip.shape),
                whole(gain.shape),
                whole(marks.shape),
            ],
            out_specs=[
                block_of(2 * inner, 0),
                block_of(SHARED, 0),
                pl.BlockSpec((padded, BLOCK), lambda i, _: (0, blocks - 1 - i)),
                whole((8, inner)),
                whole((padded, BLOCK)),
            ],
            scratch_shapes=[
                pltpu.VMEM((BLOCK + TAIL, inner), jnp.float32),
                pltpu.VMEM((STATE, inner), jnp.float32),
            ],
        ),
        out_shape=[
            jax.ShapeDtypeStruct((total, 2 * inner), jnp.bfloat16),
            jax.ShapeDtypeStruct((total, SHARED), jnp.float32),
            jax.ShapeDtypeStruct((padded, total), jnp.float32),
            jax.ShapeDtypeStruct((8, inner), jnp.float32),
            jax.ShapeDtypeStruct((padded, BLOCK), jnp.float32),
        ],
        compiler_params=pltpu.CompilerParams(vmem_limit_bytes=48 * 1024 * 1024),
        name="mixer_backward",
    )(bounds, pre, mixed, projected, d_out, projected, sums, states, dt_t, taps, rate, skip, gain, marks)


def nesterov(weight, gradient, moment, average, step_rate):
    decayed = gradient + weight_decay * weight
    new_moment = momentum_decay * moment + decayed
    new_weight = weight - step_rate * (decayed + momentum_decay * new_moment)
    new_average = average_decay * average + (1.0 - average_decay) * new_weight
    return (new_moment, new_weight, new_average)


def dot32(a, b, contract=((1,), (0,))):
    return lax.dot_general(a, b, (contract, ((), ())), preferred_element_type=jnp.float32)


def own_slice(value, index, width, axis):
    return lax.dynamic_slice_in_dim(value, index * width, width, axis)


def local(
    tokens,
    cotangent,
    lengths,
    deal_slot,
    in_weight,
    out_weight,
    small_params,
    in_moment,
    out_moment,
    small_moment,
    in_average,
    out_average,
    small_average,
):
    shards, groups = lax.axis_size("shard"), lax.axis_size("group")
    shard, group = lax.axis_index("shard"), lax.axis_index("group")
    rows, width = tokens.shape
    per = rows // shards
    total = rows * shards
    blocks = total // BLOCK
    heads = HEADS // shards
    inner = INNER // shards
    shared = SHARED // shards
    conv_flat, conv_bias, dt_bias, rate_log, skip_gain, norm_gain, pre_gain = unpack(small_params)
    taps = conv_flat.reshape(CONV, XBC)

    rank = jnp.sum((deal_slot[None, :] < deal_slot[:, None]).astype(jnp.int32), axis=1)
    sort_mat = (rank[None, :] == jnp.arange(rows)[:, None]).astype(jnp.bfloat16)
    sorted_slot = jnp.sum(jnp.where(sort_mat > 0, deal_slot[None, :], 0), axis=1)
    r_in = lax.rsqrt(jnp.mean(tokens * tokens, axis=1, keepdims=True) + eps_norm)
    normed_low = (tokens * r_in * pre_gain[None, :]).astype(jnp.bfloat16)
    part = in_weight.shape[0] // groups
    normed_low = normed_low.reshape(rows, shards, groups, part).transpose(0, 2, 1, 3).reshape(rows, width)
    x_sorted = dot32(sort_mat, normed_low).astype(jnp.bfloat16)
    c_sorted = dot32(sort_mat, cotangent.astype(jnp.bfloat16)).astype(jnp.bfloat16)
    x_all = lax.all_gather(x_sorted, "shard")
    c_all = lax.all_gather(c_sorted, "shard")
    slot_all = lax.all_gather(sorted_slot, "shard")

    slot_blk = slot_all.reshape(shards, blocks, per).transpose(1, 0, 2).reshape(blocks, BLOCK)
    slot_blk = slot_blk - jnp.arange(blocks, dtype=jnp.int32)[:, None] * BLOCK
    place = (slot_blk[:, None, :] == jnp.arange(BLOCK)[None, :, None]).astype(jnp.bfloat16)

    def to_packed(value):
        value = value.reshape(shards, blocks, per, -1).transpose(1, 0, 2, 3)
        value = value.reshape(blocks, BLOCK, -1)
        value = jnp.einsum("bps,bsd->bpd", place, value, preferred_element_type=jnp.float32)
        return value.astype(jnp.bfloat16).reshape(total, -1)

    def to_sorted(value):
        value = jnp.einsum(
            "bps,bpd->bsd", place, value.reshape(blocks, BLOCK, -1), preferred_element_type=jnp.float32
        )
        value = value.astype(jnp.bfloat16).reshape(blocks, shards, per, -1).transpose(1, 0, 2, 3)
        return value.reshape(total, -1)

    normed = to_packed(x_all)
    cot_low = to_packed(c_all)
    seg_rows = segment_of(jnp.arange(total, dtype=jnp.int32), lengths[0])
    bounds = jnp.cumsum(lengths[0])[:-1].astype(jnp.int32)

    pieces = in_weight.astype(jnp.bfloat16).reshape(groups, part, -1)
    pieces = lax.all_to_all(pieces, "group", 0, 0)
    pieces = pieces.transpose(1, 0, 2).reshape(part, -1)

    def cut(lo, each):
        return pieces[:, lo : lo + each * shards].reshape(part, shards, each).transpose(1, 0, 2)

    spread = jnp.broadcast_to(pieces[None, :, 2 * INNER : 2 * INNER + SHARED], (shards, part, SHARED))
    send = jnp.concatenate(
        [cut(0, inner), cut(INNER, inner), spread, cut(2 * INNER + SHARED, heads)], axis=2
    )
    got = lax.all_to_all(send, "shard", 0, 0)
    got = lax.all_gather(got, "group")
    in_low = got.reshape(width, -1)
    out_low = lax.all_gather(out_weight.astype(jnp.bfloat16), "group", axis=1, tiled=True)
    out_full = lax.all_gather(out_low, "shard", axis=0, tiled=True)

    projected = dot32(normed, in_low)
    conv_bc = projected[:, 2 * inner : 2 * inner + SHARED]
    taps_v = own_slice(taps[:, :INNER], shard, inner, 1)
    taps_all = jnp.concatenate([taps_v, taps[:, INNER:]], axis=1)
    bias_all = jnp.concatenate([own_slice(conv_bias[:INNER], shard, inner, 0), conv_bias[INNER:]])[None, :]
    skip_wide = jnp.repeat(own_slice(skip_gain, shard, heads, 0), HDIM)[None, :]
    gain_own = own_slice(norm_gain, shard, inner, 0)[None, :]
    padding = max(TAIL - heads, 0)
    dt_bias_own = own_slice(dt_bias, shard, heads, 0)[:, None]
    dt_raw_t = projected[:, 2 * inner + SHARED :].T + dt_bias_own
    dt_t = jnp.pad(jax.nn.softplus(dt_raw_t), ((0, padding), (0, 0)))
    rate = jnp.pad(-jnp.exp(own_slice(rate_log, shard, heads, 0)), (0, padding))[:, None]
    d_out = dot32(cot_low, out_low, ((1,), (1,)))
    pre, mixed, states, sums = mixer_forward(
        bounds, projected, dt_t, d_out, taps_all, bias_all, rate, skip_wide, gain_own
    )
    sums = lax.psum(sums, "shard") / INNER
    r_out = lax.rsqrt(sums[:, 0:1] + eps_norm)
    normed_out = (mixed * jax.nn.silu(projected[:, :inner]) * r_out * gain_own).astype(jnp.bfloat16)
    grad_out_part = dot32(normed_out, cot_low, ((0,), (0,)))
    grad_out = lax.psum_scatter(grad_out_part, "group", scatter_dimension=1, tiled=True)

    home = lax.all_to_all(to_sorted(normed_out).reshape(shards, rows, inner), "shard", 0, 0)
    home = home.transpose(1, 0, 2).reshape(rows, INNER)
    home = dot32(sort_mat, home, ((0,), (0,))).astype(jnp.bfloat16)
    block_out = tokens + dot32(home, out_full)

    d_cols, d_bc, d_dt, grads, rate_terms = mixer_backward(
        bounds, pre, mixed, projected, d_out, sums, states, dt_t, taps_v, rate, skip_wide, gain_own
    )
    d_dtraw = d_dt[:heads] * jax.nn.sigmoid(dt_raw_t)
    grad_dtb = jnp.sum(d_dtraw, axis=1)
    grad_rate = jnp.sum(rate_terms[:heads], axis=1)
    grad_skip = jnp.sum(grads[6].reshape(heads, HDIM), axis=1)
    d_bc = lax.psum_scatter(d_bc.T, "shard", scatter_dimension=0, tiled=True).T
    _, pull_bc = jax.vjp(
        lambda c, t, b: convolve(c, seg_rows, t, b),
        own_slice(conv_bc, shard, shared, 1),
        own_slice(taps[:, INNER:], shard, shared, 1),
        own_slice(conv_bias[INNER:], shard, shared, 0),
    )
    d_conv_bc, grad_taps_bc, grad_bias_bc = pull_bc(d_bc)
    d_rest = jnp.concatenate([d_conv_bc, d_dtraw.T], axis=1).astype(jnp.bfloat16)
    d_project = jnp.concatenate([d_cols, d_rest], axis=1)
    in_own = jnp.concatenate(
        [
            in_low[:, : 2 * inner],
            own_slice(in_low[:, 2 * inner : 2 * inner + SHARED], shard, shared, 1),
            in_low[:, 2 * inner + SHARED :],
        ],
        axis=1,
    )
    d_normed = dot32(to_sorted(d_project), in_own, ((1,), (1,)))
    d_normed = lax.psum_scatter(d_normed, "shard", scatter_dimension=0, tiled=True)
    d_normed = jnp.dot(
        sort_mat.T.astype(jnp.float32), d_normed, precision=lax.Precision.HIGHEST
    )
    d_normed = d_normed.reshape(rows, groups, shards, part).transpose(0, 2, 1, 3).reshape(rows, width)
    d_scaled = pre_gain[None, :] * d_normed
    inside = jnp.mean(tokens * d_scaled, axis=1, keepdims=True)
    input_grad = cotangent + r_in * (d_scaled - tokens * (r_in * r_in) * inside)
    grad_pre = jnp.sum(tokens * r_in * d_normed, axis=0)

    grad_in = dot32(normed, d_project, ((0,), (0,)))
    grad_in = lax.psum_scatter(grad_in, "group", scatter_dimension=0, tiled=True)
    grad_in = lax.all_to_all(grad_in.reshape(shards, part, -1), "shard", 0, 0)

    def join(lo, each):
        return grad_in[:, :, lo : lo + each].transpose(1, 0, 2).reshape(part, shards * each)

    grad_in = jnp.concatenate(
        [
            join(0, inner),
            join(inner, inner),
            join(2 * inner, shared),
            join(2 * inner + shared, heads),
        ],
        axis=1,
    )
    grad_in = grad_in.reshape(part, groups, -1).transpose(1, 0, 2)
    grad_in = lax.all_to_all(grad_in, "group", 0, 0).reshape(in_weight.shape)

    mine = [
        grads[:CONV].reshape(-1),
        grad_taps_bc.reshape(-1),
        grads[4],
        grad_bias_bc,
        grad_dtb,
        grad_rate,
        grad_skip,
        grads[5],
    ]
    extents = [piece.shape[0] for piece in mine]
    mine = lax.all_gather(lax.psum(jnp.concatenate(mine), "group"), "shard")
    found, offset = [], 0
    for extent in extents:
        found.append(mine[:, offset : offset + extent])
        offset = offset + extent

    def taps_of(piece):
        return piece.reshape(shards, CONV, -1).transpose(1, 0, 2).reshape(CONV, -1)

    grad_taps = jnp.concatenate([taps_of(found[0]), taps_of(found[1])], axis=1).reshape(-1)
    grad_small = jnp.concatenate(
        [grad_taps] + [piece.reshape(-1) for piece in found[2:]]
        + [lax.psum(grad_pre, ("group", "shard"))]
    )
    in_new = nesterov(in_weight, grad_in, in_moment, in_average, rate_in)
    out_new = nesterov(out_weight, grad_out, out_moment, out_average, rate_out)
    small_new = nesterov(small_params, grad_small, small_moment, small_average, rate_small)
    return (block_out, input_grad) + in_new + out_new + small_new


def solution(mesh):
    rows = P(("group", "shard"), None)
    tile = P("shard", "group")
    return jax.shard_map(
        local,
        mesh=mesh,
        in_specs=(
            rows,
            rows,
            P("group", None),
            P(("group", "shard")),
            tile,
            tile,
            P(),
            tile,
            tile,
            P(),
            tile,
            tile,
            P(),
        ),
        out_specs=(rows, rows, tile, tile, tile, tile, tile, tile, P(), P(), P()),
        check_vma=False,
    )
```

```python
import functools

import jax
import jax.numpy as jnp
from jax import lax
from jax.experimental import pallas as pl
from jax.experimental.pallas import tpu as pltpu
from jax.sharding import PartitionSpec as P

D = 2048
HEADS = 64
HDIM = 64
STATE = 128
CONV = 4
BLOCK = 256
INNER = 4096
XBC = 4352
SHARED = 2 * STATE
TAIL = 8
MESH = pl.DeviceIdType.MESH


eps_norm = 1e-05
momentum_decay = 0.9
weight_decay = 0.01
average_decay = 0.99
rate_in = 0.0001
rate_out = 3e-05
rate_small = 0.001


def unpack(packed_small):
    extents = [CONV * XBC, XBC, HEADS, HEADS, HEADS, INNER, D]
    pieces = []
    offset = 0
    for extent in extents:
        pieces.append(packed_small[offset : offset + extent])
        offset = offset + extent
    return pieces


def segment_of(positions, lengths_row):
    bounds = jnp.cumsum(lengths_row)[:-1]
    inside = jnp.sum((positions[:, None] >= bounds[None, :]).astype(jnp.int32), axis=1)
    return jnp.where(positions < 0, -1, inside)


def convolve(conv_rows, seg_rows, conv_taps, conv_bias):
    row_count, width = conv_rows.shape
    extended = jnp.concatenate([jnp.zeros((CONV - 1, width), conv_rows.dtype), conv_rows], axis=0)
    seg_ext = jnp.concatenate([jnp.full((CONV - 1,), -1, jnp.int32), seg_rows], axis=0)
    conv_sum = jnp.zeros_like(conv_rows) + conv_bias[None, :]
    for tap_index in range(CONV):
        same_seq = (seg_ext[tap_index : tap_index + row_count] == seg_rows)[:, None]
        conv_sum = conv_sum + jnp.where(
            same_seq,
            extended[tap_index : tap_index + row_count] * conv_taps[tap_index][None, :],
            0.0,
        )
    return jax.nn.silu(conv_sum)


def split(value):
    high = value.astype(jnp.bfloat16)
    return high, (value - high.astype(jnp.float32)).astype(jnp.bfloat16)


def dots(a, b, contract):
    return lax.dot_general(a, b, (contract, ((), ())), preferred_element_type=jnp.float32)


def dot3(a, b, contract=((1,), (0,))):
    a = a if isinstance(a, tuple) else split(a)
    b = b if isinstance(b, tuple) else split(b)
    return dots(a[0], b[0], contract) + (dots(a[0], b[1], contract) + dots(a[1], b[0], contract))


NT = ((1,), (1,))


def head_sums(value, marks):
    high = value.astype(jnp.bfloat16)
    rest = value - high.astype(jnp.float32)
    mid = rest.astype(jnp.bfloat16)
    low = (rest - mid.astype(jnp.float32)).astype(jnp.bfloat16)
    return dots(marks, high, NT) + (dots(marks, mid, NT) + dots(marks, low, NT))


def widen(columns, heads):
    rows = columns.shape[0]
    low_half = lax.broadcasted_iota(jnp.int32, (rows, 2 * HDIM), 1) < HDIM
    return jnp.concatenate(
        [
            jnp.where(low_half, columns[:, h : h + 1], columns[:, h + 1 : h + 2])
            for h in range(0, heads, 2)
        ],
        axis=1,
    )


def running_sum(value, reverse=False):
    lane = lax.broadcasted_iota(jnp.int32, value.shape, 1)
    count = value.shape[1]
    step = 1
    while step < count:
        if reverse:
            value = value + jnp.where(lane < count - step, pltpu.roll(value, count - step, 1), 0.0)
        else:
            value = value + jnp.where(lane >= step, pltpu.roll(value, step, 1), 0.0)
        step *= 2
    return value


def sequence_of(positions, bounds):
    inside = jnp.where(positions >= bounds[0], 1, 0) + jnp.where(positions >= bounds[1], 1, 0)
    return jnp.where(positions < 0, -1, inside)


def block_facts(block, bounds, dt_t, rate):
    start = block * BLOCK
    seg_col = sequence_of(start + lax.broadcasted_iota(jnp.int32, (BLOCK, 1), 0), bounds)
    seg_row = sequence_of(start + lax.broadcasted_iota(jnp.int32, (1, BLOCK), 1), bounds)
    before = sequence_of(start - 1 + lax.broadcasted_iota(jnp.int32, (1, 1), 1), bounds)
    last = sequence_of(start + BLOCK - 1 + lax.broadcasted_iota(jnp.int32, (1, 1), 1), bounds)
    run_t = running_sum(dt_t * rate)
    run = run_t.T
    final = run[BLOCK - 1 :, :]
    carried = jnp.where(seg_col == before, jnp.exp(run), 0.0)
    tail = jnp.where(seg_col == last, jnp.exp(final - run), 0.0)
    keep = jnp.where(last == before, jnp.exp(final), 0.0)
    return seg_col, seg_row, run_t, run, carried, tail, keep


def forward_kernel(
    heads, bounds, gate, conv_v, conv_bc, dt_cols, d_out, taps, bias, rate, skip, gain,
    pre_out, mixed_out, state_out, sums_out, ext, state,
):
    block = pl.program_id(0)
    inner = heads * HDIM

    @pl.when(block == 0)
    def _():
        ext[:TAIL, :] = jnp.zeros((TAIL, ext.shape[1]), jnp.float32)
        state[...] = jnp.zeros_like(state)

    bounds = (bounds[0], bounds[1])
    dt = dt_cols[...]
    dt_t = dt.T[: rate.shape[0], :]
    seg_col, seg_row, run_t, run, carried, tail, keep = block_facts(block, bounds, dt_t, rate[...])
    ext[TAIL:, :inner] = conv_v[...]
    ext[TAIL:, inner:] = conv_bc[...]
    place = block * BLOCK + lax.broadcasted_iota(jnp.int32, (BLOCK, 1), 0)
    pre = bias[...] + taps[CONV - 1 : CONV, :] * ext[TAIL:, :]
    for back in range(1, CONV):
        same = sequence_of(place - back, bounds) == seg_col
        moved = ext[TAIL - back : TAIL - back + BLOCK, :]
        pre = pre + jnp.where(same, moved, 0.0) * taps[CONV - 1 - back : CONV - back, :]
    ext[:TAIL, :] = ext[BLOCK:, :]
    pre_out[...] = pre
    conv = pre / (1.0 + jnp.exp(-pre))
    values, b_rows, c_rows = conv[:, :inner], conv[:, inner : inner + STATE], conv[:, inner + STATE :]
    fed = values * widen(dt, heads)
    rows = lax.broadcasted_iota(jnp.int32, (BLOCK, BLOCK), 0)
    cols = lax.broadcasted_iota(jnp.int32, (BLOCK, BLOCK), 1)
    allowed = (seg_col == seg_row) & (rows >= cols)
    b_parts, c_parts = split(b_rows), split(c_rows)
    scores = jnp.where(allowed, dot3(c_parts, b_parts, NT), 0.0)
    old = state[...]
    state_out[0] = old
    output = widen(carried, heads) * dot3(c_parts, old)
    low_half = lax.broadcasted_iota(jnp.int32, (BLOCK, 2 * HDIM), 1) < HDIM
    inside = []
    for h in range(0, heads, 2):
        pair = split(fed[:, h * HDIM : (h + 2) * HDIM])
        found = []
        for k in (h, h + 1):
            mixing = jnp.exp(jnp.minimum(run[:, k : k + 1] - run_t[k : k + 1, :], 0.0)) * scores
            found.append(dot3(mixing, pair))
        inside.append(jnp.where(low_half, found[0], found[1]))
    mixed = output + jnp.concatenate(inside, axis=1) + skip[...] * values
    mixed_out[...] = mixed
    state[...] = widen(keep, heads) * old + dot3(b_rows.T, widen(tail, heads) * fed)
    gated = mixed * (gate[...] / (1.0 + jnp.exp(-gate[...])))
    sums_out[:, 0:1] = jnp.sum(gated * gated, axis=1, keepdims=True)
    sums_out[:, 1:2] = jnp.sum(gated * gain[...] * d_out[...], axis=1, keepdims=True)


def backward_kernel(
    heads, blocks, bounds, pre, mixed, gate, d_out, conv_v, sums, state_in, dt_cols, taps, rate, skip, gain, marks,
    d_cols, d_bc, d_dt, grads, grad_rate, ext, carry,
):
    step = pl.program_id(0)
    block = blocks - 1 - step
    inner = heads * HDIM

    @pl.when(step == 0)
    def _():
        ext[BLOCK:, :] = jnp.zeros((TAIL, ext.shape[1]), jnp.float32)
        carry[...] = jnp.zeros_like(carry)
        grads[...] = jnp.zeros_like(grads)
        grad_rate[...] = jnp.zeros_like(grad_rate)

    bounds = (bounds[0], bounds[1])
    dt = dt_cols[...]
    dt_t = dt.T[: rate.shape[0], :]
    seg_col, seg_row, run_t, run, carried, tail, keep = block_facts(block, bounds, dt_t, rate[...])
    r_out = lax.rsqrt(sums[:, 0:1] + 1e-05)
    inside = sums[:, 1:2]
    gate_now = gate[...]
    gate_sig = 1.0 / (1.0 + jnp.exp(-gate_now))
    act = gate_now * gate_sig
    mixed_now = mixed[...]
    gated = mixed_now * act
    d_out_now = d_out[...]
    d_gated = r_out * (gain[...] * d_out_now - gated * (r_out * r_out) * inside)
    dy = d_gated * act
    d_cols[:, :inner] = (d_gated * mixed_now * (gate_sig * (1.0 + gate_now * (1.0 - gate_sig)))).astype(jnp.bfloat16)
    grads[5:6, :] += jnp.sum(gated * r_out * d_out_now, axis=0, keepdims=True)
    pre_now = pre[...]
    sig = 1.0 / (1.0 + jnp.exp(-pre_now))
    conv = pre_now * sig
    values, b_rows, c_rows = conv[:, :inner], conv[:, inner : inner + STATE], conv[:, inner + STATE :]
    grads[6:7, :] += jnp.sum(dy * values, axis=0, keepdims=True)
    dt_wide = widen(dt, heads)
    fed = values * dt_wide
    old, after = state_in[0], carry[...]
    b_parts, c_parts, old_parts, after_parts = split(b_rows), split(c_rows), split(old), split(after)
    carried_wide, tail_wide, keep_wide = widen(carried, heads), widen(tail, heads), widen(keep, heads)
    rows = lax.broadcasted_iota(jnp.int32, (BLOCK, BLOCK), 0)
    cols = lax.broadcasted_iota(jnp.int32, (BLOCK, BLOCK), 1)
    allowed = (seg_col == seg_row) & (cols >= rows)
    scores_t = jnp.where(allowed, dot3(b_parts, c_parts, NT), 0.0)
    low_half = lax.broadcasted_iota(jnp.int32, (BLOCK, 2 * HDIM), 1) < HDIM
    d_scores_t = jnp.zeros((BLOCK, BLOCK), jnp.float32)
    d_fed, row_terms, col_terms = [], [], []
    for h in range(0, heads, 2):
        fed_pair = fed[:, h * HDIM : (h + 2) * HDIM]
        dy_pair = split(dy[:, h * HDIM : (h + 2) * HDIM])
        found = []
        for k in (h, h + 1):
            own = low_half if k == h else jnp.logical_not(low_half)
            d_mixing = dot3(jnp.where(own, fed_pair, 0.0), dy_pair, NT)
            decay = jnp.exp(jnp.minimum(run_t[k : k + 1, :] - run[:, k : k + 1], 0.0))
            mixing = decay * scores_t
            d_scores_t = d_scores_t + decay * d_mixing
            flow = mixing * d_mixing
            row_terms.append(jnp.sum(flow, axis=0, keepdims=True))
            col_terms.append(jnp.sum(flow, axis=1, keepdims=True))
            found.append(dot3(mixing, dy_pair))
        d_fed.append(jnp.where(low_half, found[0], found[1]))
    d_scores_t = split(jnp.where(allowed, d_scores_t, 0.0))
    fed_tail = fed * tail_wide
    dy_carried = dy * carried_wide
    d_fed_out = tail_wide * dot3(b_parts, after_parts)
    d_fed = jnp.concatenate(d_fed, axis=1) + d_fed_out
    dy_parts, tail_parts = split(dy_carried), split(fed_tail)
    d_bc[:, :STATE] = dot3(d_scores_t, c_parts) + dot3(tail_parts, after_parts, NT)
    d_bc[:, STATE:] = dot3(d_scores_t, b_parts, ((0,), (0,))) + dot3(dy_parts, old_parts, NT)
    head_count = dt_t.shape[0]
    pad = [jnp.zeros((1, BLOCK), jnp.float32)] * (head_count - heads)
    pad_col = [jnp.zeros((BLOCK, 1), jnp.float32)] * (head_count - heads)
    d_run = jnp.concatenate(row_terms + pad, axis=0) - jnp.concatenate(col_terms + pad_col, axis=1).T
    d_run = d_run + head_sums(dy_carried * dot3(c_parts, old_parts), marks[...])
    leaving = head_sums(fed * d_fed_out, marks[...])
    kept = jnp.sum(old * after, axis=0, keepdims=True) * keep_wide
    kept = jnp.sum(marks[...].astype(jnp.float32) * kept, axis=1, keepdims=True)
    at_end = lax.broadcasted_iota(jnp.int32, (head_count, BLOCK), 1) == BLOCK - 1
    total = jnp.sum(leaving, axis=1, keepdims=True) + kept
    d_run = d_run - leaving + jnp.where(at_end, total, 0.0)
    d_log = running_sum(d_run, reverse=True)
    d_dt[...] = d_log * rate[...] + head_sums(values * d_fed, marks[...])
    grad_rate[...] += d_log * (dt_t * rate[...])
    carry[...] = keep_wide * after + dot3(c_rows.T, dy_parts)
    pre_v, sig_v = pre_now[:, :inner], sig[:, :inner]
    d_values = dt_wide * d_fed + skip[...] * dy
    d_pre = d_values * (sig_v * (1.0 + pre_v * (1.0 - sig_v)))
    ext[:BLOCK, :] = d_pre
    place = block * BLOCK + lax.broadcasted_iota(jnp.int32, (BLOCK, 1), 0)
    conv_in = conv_v[...]
    d_conv = taps[CONV - 1 : CONV, :] * d_pre
    grads[CONV - 1 : CONV, :] += jnp.sum(conv_in * d_pre, axis=0, keepdims=True)
    grads[CONV : CONV + 1, :] += jnp.sum(d_pre, axis=0, keepdims=True)
    for ahead in range(1, CONV):
        same = sequence_of(place + ahead, bounds) == seg_col
        moved = jnp.where(same, ext[ahead : ahead + BLOCK, :], 0.0)
        d_conv = d_conv + taps[CONV - 1 - ahead : CONV - ahead, :] * moved
        grads[CONV - 1 - ahead : CONV - ahead, :] += jnp.sum(conv_in * moved, axis=0, keepdims=True)
    ext[BLOCK:, :] = ext[:TAIL, :]
    d_cols[:, inner:] = d_conv.astype(jnp.bfloat16)


def whole(shape):
    return pl.BlockSpec(shape, lambda *_: (0,) * len(shape))


def mixer_forward(bounds, projected, dt_cols, d_out, taps, bias, rate, skip, gain):
    total, inner = d_out.shape
    heads, blocks, padded = inner // HDIM, total // BLOCK, rate.shape[0]

    def block_of(width, column):
        return pl.BlockSpec((BLOCK, width), lambda i, _: (i, column))

    return pl.pallas_call(
        functools.partial(forward_kernel, heads),
        grid_spec=pltpu.PrefetchScalarGridSpec(
            num_scalar_prefetch=1,
            grid=(blocks,),
            in_specs=[
                block_of(inner, 0),
                block_of(inner, 1),
                block_of(SHARED, 2 * inner // SHARED),
                block_of(dt_cols.shape[1], 0),
                block_of(inner, 0),
                whole(taps.shape),
                whole(bias.shape),
                whole(rate.shape),
                whole(skip.shape),
                whole(gain.shape),
            ],
            out_specs=[
                block_of(inner + SHARED, 0),
                block_of(inner, 0),
                pl.BlockSpec((1, STATE, inner), lambda i, _: (i, 0, 0)),
                block_of(2, 0),
            ],
            scratch_shapes=[
                pltpu.VMEM((BLOCK + TAIL, inner + SHARED), jnp.float32),
                pltpu.VMEM((STATE, inner), jnp.float32),
            ],
        ),
        out_shape=[
            jax.ShapeDtypeStruct((total, inner + SHARED), jnp.float32),
            jax.ShapeDtypeStruct((total, inner), jnp.float32),
            jax.ShapeDtypeStruct((blocks, STATE, inner), jnp.float32),
            jax.ShapeDtypeStruct((total, 2), jnp.float32),
        ],
        compiler_params=pltpu.CompilerParams(vmem_limit_bytes=48 * 1024 * 1024),
        name="mixer_forward",
    )(bounds, projected, projected, projected, dt_cols, d_out, taps, bias, rate, skip, gain)


def mixer_backward(bounds, pre, mixed, projected, d_out, sums, states, dt_cols, taps, rate, skip, gain):
    total, inner = d_out.shape
    heads, blocks, padded = inner // HDIM, total // BLOCK, rate.shape[0]
    marks = (jnp.arange(padded)[:, None] == jnp.arange(inner)[None, :] // HDIM).astype(jnp.bfloat16)

    def block_of(width, column):
        return pl.BlockSpec((BLOCK, width), lambda i, _: (blocks - 1 - i, column))

    return pl.pallas_call(
        functools.partial(backward_kernel, heads, blocks),
        grid_spec=pltpu.PrefetchScalarGridSpec(
            num_scalar_prefetch=1,
            grid=(blocks,),
            in_specs=[
                block_of(inner + SHARED, 0),
                block_of(inner, 0),
                block_of(inner, 0),
                block_of(inner, 0),
                block_of(inner, 1),
                block_of(2, 0),
                pl.BlockSpec((1, STATE, inner), lambda i, _: (blocks - 1 - i, 0, 0)),
                block_of(dt_cols.shape[1], 0),
                whole(taps.shape),
                whole(rate.shape),
                whole(skip.shape),
                whole(gain.shape),
                whole(marks.shape),
            ],
            out_specs=[
                block_of(2 * inner, 0),
                block_of(SHARED, 0),
                pl.BlockSpec((padded, BLOCK), lambda i, _: (0, blocks - 1 - i)),
                whole((8, inner)),
                whole((padded, BLOCK)),
            ],
            scratch_shapes=[
                pltpu.VMEM((BLOCK + TAIL, inner), jnp.float32),
                pltpu.VMEM((STATE, inner), jnp.float32),
            ],
        ),
        out_shape=[
            jax.ShapeDtypeStruct((total, 2 * inner), jnp.bfloat16),
            jax.ShapeDtypeStruct((total, SHARED), jnp.float32),
            jax.ShapeDtypeStruct((padded, total), jnp.float32),
            jax.ShapeDtypeStruct((8, inner), jnp.float32),
            jax.ShapeDtypeStruct((padded, BLOCK), jnp.float32),
        ],
        compiler_params=pltpu.CompilerParams(vmem_limit_bytes=48 * 1024 * 1024),
        name="mixer_backward",
    )(bounds, pre, mixed, projected, d_out, projected, sums, states, dt_cols, taps, rate, skip, gain, marks)


def far_first(index, count):
    return jnp.where(index % 2 == 0, count - 1 - index // 2, index // 2)


def other_place(step, place, count):
    own = jnp.where(2 * place >= count, 2 * (count - 1 - place), 2 * place + 1)
    return far_first(jnp.where(step >= own, step + 1, step), count)


def barrier_with(peers):
    barrier = pltpu.get_barrier_semaphore()
    for peer in peers:
        pl.semaphore_signal(barrier, inc=1, device_id=peer, device_id_type=MESH)
    pl.semaphore_wait(barrier, len(peers))


def tail_kernel(
    shards, groups, columns,
    partial, weight_part, small, scaled_rows,
    rows_out, weight_out, small_out, gain_out,
    wide_in, wide_scale, line_in, line_scale, core_in, row_in, small_in, gain_in,
    held, coded, scales, line_coded, line_scales, got, got_scale, marks, total, other, send_rows, small_sum, gain_sum,
    load_sem, wide_send, wide_recv, line_send, line_recv, core_send, core_recv, row_send, row_recv,
    deal_send, deal_recv, small_send, small_recv, gain_send, gain_recv,
):
    shard, group = lax.axis_index("shard"), lax.axis_index("group")
    lines = shards // columns
    rows_y = groups // 2
    z, x = shard // columns, shard % columns
    y, core = group // 2, group % 2
    part = weight_out.shape[1]
    count = held.shape[0]

    def remote(src, dst, sends, recvs, **where):
        return pltpu.make_async_remote_copy(
            src_ref=src, dst_ref=dst, send_sem=sends, recv_sem=recvs, device_id=where, device_id_type=MESH
        )

    def load(src, dst):
        copy = pltpu.make_async_copy(src, dst, load_sem)
        copy.start()
        copy.wait()

    shard_peers = [(shard + step) % shards for step in range(1, shards)]
    group_peers = [(group + step) % groups for step in range(1, groups)]
    barrier_with([{"shard": peer} for peer in shard_peers] + [{"group": peer} for peer in group_peers])

    mate = y * 2 + 1 - core

    def core_copy(turn):
        return remote(weight_part.at[turn * 2 + 1 - core], core_in.at[turn], core_send.at[turn], core_recv.at[turn], group=mate)

    for turn in range(rows_y):
        core_copy(turn).start()

    def small_copy(step):
        return remote(small, small_in.at[step - 1], small_send.at[step - 1], small_recv.at[step - 1], group=(group + step) % groups)

    for step in range(1, groups):
        small_copy(step).start()

    def code(coded_to, scales_to):
        @pl.loop(0, count // 32)
        def _(turn):
            rows = pl.ds(pl.multiple_of(turn * 32, 32), 32)
            value = held[rows, :]
            most = jnp.maximum(jnp.max(jnp.abs(value), axis=1, keepdims=True), 1e-30)
            coded_to[rows, :] = jnp.round(value * (32767.0 / most)).astype(jnp.int32).astype(jnp.int16)
            marks[rows, :] = jnp.broadcast_to(most * (1.0 / 32767.0), (32, 128))

        scales_to[...] = marks[...].T[:8, :]

    def add(coded_from, scales_from):
        load(coded_from, got)
        load(scales_from, got_scale)
        marks[...] = jnp.broadcast_to(got_scale[0:1, :], (128, count)).T

        @pl.loop(0, count // 32)
        def _(turn):
            rows = pl.ds(pl.multiple_of(turn * 32, 32), 32)
            held[rows, :] += got[rows, :].astype(jnp.float32) * marks[rows, 0:1]

    def place_of(step):
        return other_place(step, z, lines) if step < lines - 1 else z

    def wide_copies(step, hop):
        at = (hop - 1) * lines + step
        peer = z * columns + (x + hop) % columns
        target = place_of(step)
        return (
            remote(coded.at[step], wide_in.at[hop - 1, target], wide_send.at[0, at], wide_recv.at[0, at], shard=peer),
            remote(scales.at[step], wide_scale.at[hop - 1, target], wide_send.at[1, at], wide_recv.at[1, at], shard=peer),
        )

    for hop in range(1, columns):
        for step in range(lines):
            if hop > 1:
                for copy in wide_copies(step, hop - 1):
                    copy.wait_send()
            load(partial.at[place_of(step) * columns + (x + hop) % columns], held)
            code(coded.at[step], scales.at[step])
            for copy in wide_copies(step, hop):
                copy.start()

    load(small, small_sum)
    for step in range(1, groups):
        small_copy(step).wait_recv()
        load(small_in.at[step - 1], other.at[: small.shape[0], :128])
        small_sum[...] += other[: small.shape[0], :128]

    def small_deal(step):
        return remote(small_sum, small_out.at[shard], small_send.at[groups + step], small_recv.at[groups + step], shard=(shard + step) % shards)

    for step in range(1, shards):
        small_deal(step).start()
    load(small_sum, small_out.at[shard])

    def row_copy(step):
        return remote(send_rows.at[step - 1], row_in.at[step - 1], row_send.at[step - 1], row_recv.at[step - 1], group=(y + step) % rows_y * 2 + core)

    def add_other():
        @pl.loop(0, total.shape[0] // part)
        def _(turn):
            rows = pl.ds(pl.multiple_of(turn * part, part), part)
            total[rows, :] += other[rows, :]

    def core_sum(turn):
        load(weight_part.at[turn * 2 + core], total)
        load(core_in.at[turn], other)
        add_other()

    for turn in range(rows_y):
        core_copy(turn).wait_recv()
    for step in range(1, rows_y):
        core_sum((y + step) % rows_y)
        load(total, send_rows.at[step - 1])
        row_copy(step).start()
    core_sum(y)

    def line_copies(step):
        target = place_of(step)
        way = jnp.where(target > z, 0, 1)
        peer = jnp.where(target > z, z + 1, z - 1) * columns + x
        return (
            remote(line_coded.at[step], line_in.at[way, target], line_send.at[0, step], line_recv.at[0, way, target], shard=peer),
            remote(line_scales.at[step], line_scale.at[way, target], line_send.at[1, step], line_recv.at[1, way, target], shard=peer),
        )

    def take(way, target):
        source = jnp.where(way == 0, z - 1, z + 1)
        peer = jnp.clip(source, 0, lines - 1) * columns + x
        remote(line_coded.at[0], line_in.at[way, target], line_send.at[0, 0], line_recv.at[0, way, target], shard=peer).wait_recv()
        remote(line_scales.at[0], line_scale.at[way, target], line_send.at[1, 0], line_recv.at[1, way, target], shard=peer).wait_recv()
        add(line_in.at[way, target], line_scale.at[way, target])

    def gather_wide(step):
        target = place_of(step)
        load(partial.at[target * columns + x], held)
        for hop in range(1, columns):
            for copy in wide_copies(step, hop):
                copy.wait_recv()
            add(wide_in.at[hop - 1, target], wide_scale.at[hop - 1, target])

    def deal_copy(step):
        peer = (shard + step) % shards
        rows = pl.ds(pl.multiple_of(peer * part, part), part)
        return remote(total.at[rows], weight_out.at[shard], deal_send.at[step], deal_recv.at[step], shard=peer)

    def deal():
        for step in range(1, rows_y):
            row_copy(step).wait_recv()
            load(row_in.at[step - 1], other)
            add_other()
        for step in range(1, shards):
            deal_copy(step).start()
        load(total.at[pl.ds(pl.multiple_of(shard * part, part), part)], weight_out.at[shard])

    for step in range(lines - 1):
        if step == lines - 2:
            deal()
        target = place_of(step)
        way = jnp.where(target > z, 0, 1)
        gather_wide(step)

        @pl.when(jnp.where(target > z, z > 0, z < lines - 1))
        def _():
            take(way, target)

        code(line_coded.at[step], line_scales.at[step])
        for copy in line_copies(step):
            copy.start()
    gather_wide(lines - 1)

    @pl.when(z > 0)
    def _():
        take(0, z)

    @pl.when(z < lines - 1)
    def _():
        take(1, z)

    rows_out[...] = held[...]
    gain_sum[...] = jnp.zeros_like(gain_sum)

    @pl.loop(0, count // 8)
    def _(turn):
        rows = pl.ds(pl.multiple_of(turn * 8, 8), 8)
        gain_sum[...] += held[rows, :] * scaled_rows[rows, :]

    def gain_copy(step):
        return remote(gain_sum, gain_in.at[step - 1], gain_send.at[step - 1], gain_recv.at[step - 1], shard=(shard + step) % shards)

    def gain_deal(step):
        at = shards - 1 + step - 1
        return remote(gain_out, gain_in.at[at], gain_send.at[at], gain_recv.at[at], group=(group + step) % groups)

    for step in range(1, shards):
        gain_copy(step).start()
    gain_out[...] = gain_sum[...]
    for step in range(1, shards):
        gain_copy(step).wait_recv()
        gain_out[...] += gain_in[step - 1]
    for step in range(1, groups):
        gain_deal(step).start()
    for step in range(1, groups):
        gain_deal(step).wait_recv()
    for step in range(1, groups):
        gain_deal(step).wait_send()
    for step in range(1, groups):
        gain_out[...] += gain_in[shards - 1 + step - 1]

    for step in range(1, shards):
        gain_copy(step).wait_send()
        small_deal(step).wait()
        deal_copy(step).wait()
    for step in range(1, groups):
        small_copy(step).wait_send()
    for step in range(1, rows_y):
        row_copy(step).wait_send()
    for turn in range(rows_y):
        core_copy(turn).wait_send()
    for step in range(lines):
        for copy in wide_copies(step, columns - 1) if columns > 1 else ():
            copy.wait_send()
    for step in range(lines - 1):
        for copy in line_copies(step):
            copy.wait_send()


def grid_columns(shards):
    columns = 1
    while 2 * (2 * columns) * (2 * columns) <= shards:
        columns *= 2
    return columns if shards % columns == 0 else 1


def tail_exchange(shards, groups, partial, weight_part, small, scaled_rows):
    columns = grid_columns(shards)
    lines, rows_y = shards // columns, groups // 2
    count, width = scaled_rows.shape
    weight_rows, weight_width = weight_part.shape[1:]
    part = weight_rows // shards
    small_shape = small.shape
    coded, scale = (count, width), (8, count)
    any_space, vmem = pl.BlockSpec(memory_space=pl.ANY), pl.BlockSpec(memory_space=pltpu.VMEM)
    f32, i16 = jnp.float32, jnp.int16
    slots = max(columns - 1, 1)
    dma = pltpu.SemaphoreType.DMA
    out = pl.pallas_call(
        functools.partial(tail_kernel, shards, groups, columns),
        in_specs=[any_space, any_space, any_space, vmem],
        out_specs=[vmem, any_space, any_space, vmem] + [any_space] * 7 + [vmem],
        out_shape=[
            jax.ShapeDtypeStruct((count, width), f32),
            jax.ShapeDtypeStruct((shards, part, weight_width), f32),
            jax.ShapeDtypeStruct((shards,) + small_shape, f32),
            jax.ShapeDtypeStruct((8, width), f32),
            jax.ShapeDtypeStruct((slots, lines) + coded, i16),
            jax.ShapeDtypeStruct((slots, lines) + scale, f32),
            jax.ShapeDtypeStruct((2, lines) + coded, i16),
            jax.ShapeDtypeStruct((2, lines) + scale, f32),
            jax.ShapeDtypeStruct((rows_y, weight_rows, weight_width), f32),
            jax.ShapeDtypeStruct((max(rows_y - 1, 1), weight_rows, weight_width), f32),
            jax.ShapeDtypeStruct((max(groups - 1, 1),) + small_shape, f32),
            jax.ShapeDtypeStruct((shards - 1 + groups - 1, 8, width), f32),
        ],
        scratch_shapes=[
            pltpu.VMEM((count, width), f32),
            pltpu.VMEM((lines,) + coded, i16),
            pltpu.VMEM((lines,) + scale, f32),
            pltpu.VMEM((lines,) + coded, i16),
            pltpu.VMEM((lines,) + scale, f32),
            pltpu.VMEM(coded, i16),
            pltpu.VMEM(scale, f32),
            pltpu.VMEM((count, 128), f32),
            pltpu.VMEM((weight_rows, weight_width), f32),
            pltpu.VMEM((weight_rows, weight_width), f32),
            pltpu.VMEM((max(rows_y - 1, 1), weight_rows, weight_width), f32),
            pltpu.VMEM(small_shape, f32),
            pltpu.VMEM((8, width), f32),
            dma,
            dma((2, slots * lines)),
            dma((2, slots * lines)),
            dma((2, lines)),
            dma((2, 2, lines)),
            dma((rows_y,)),
            dma((rows_y,)),
            dma((max(rows_y - 1, 1),)),
            dma((max(rows_y - 1, 1),)),
            dma((shards,)),
            dma((shards,)),
            dma((groups + shards,)),
            dma((groups + shards,)),
            dma((shards + groups,)),
            dma((shards + groups,)),
        ],
        compiler_params=pltpu.CompilerParams(
            collective_id=1, has_side_effects=True, vmem_limit_bytes=60 * 1024 * 1024
        ),
        name="tail_exchange",
    )(partial, weight_part, small, scaled_rows)
    return out[:4]


def nesterov(weight, gradient, moment, average, step_rate):
    decayed = gradient + weight_decay * weight
    new_moment = momentum_decay * moment + decayed
    new_weight = weight - step_rate * (decayed + momentum_decay * new_moment)
    new_average = average_decay * average + (1.0 - average_decay) * new_weight
    return (new_moment, new_weight, new_average)


def dot32(a, b, contract=((1,), (0,))):
    return lax.dot_general(a, b, (contract, ((), ())), preferred_element_type=jnp.float32)


def own_slice(value, index, width, axis):
    return lax.dynamic_slice_in_dim(value, index * width, width, axis)


def local(
    tokens,
    cotangent,
    lengths,
    deal_slot,
    in_weight,
    out_weight,
    small_params,
    in_moment,
    out_moment,
    small_moment,
    in_average,
    out_average,
    small_average,
):
    shards, groups = lax.axis_size("shard"), lax.axis_size("group")
    shard, group = lax.axis_index("shard"), lax.axis_index("group")
    rows, width = tokens.shape
    per = rows // shards
    total = rows * shards
    blocks = total // BLOCK
    heads = HEADS // shards
    inner = INNER // shards
    shared = SHARED // shards
    conv_flat, conv_bias, dt_bias, rate_log, skip_gain, norm_gain, pre_gain = unpack(small_params)
    taps = conv_flat.reshape(CONV, XBC)

    rank = jnp.sum((deal_slot[None, :] < deal_slot[:, None]).astype(jnp.int32), axis=1)
    sort_mat = (rank[None, :] == jnp.arange(rows)[:, None]).astype(jnp.bfloat16)
    sorted_slot = jnp.sum(jnp.where(sort_mat > 0, deal_slot[None, :], 0), axis=1)
    r_in = lax.rsqrt(jnp.mean(tokens * tokens, axis=1, keepdims=True) + eps_norm)
    normed_low = (tokens * r_in * pre_gain[None, :]).astype(jnp.bfloat16)
    part = in_weight.shape[0] // groups
    normed_low = normed_low.reshape(rows, shards, groups, part).transpose(0, 2, 1, 3).reshape(rows, width)
    x_sorted = dot32(sort_mat, normed_low).astype(jnp.bfloat16)
    c_sorted = dot32(sort_mat, cotangent.astype(jnp.bfloat16)).astype(jnp.bfloat16)
    x_all = lax.all_gather(x_sorted, "shard")
    c_all = lax.all_gather(c_sorted, "shard")
    slot_all = lax.all_gather(sorted_slot, "shard")

    slot_blk = slot_all.reshape(shards, blocks, per).transpose(1, 0, 2).reshape(blocks, BLOCK)
    slot_blk = slot_blk - jnp.arange(blocks, dtype=jnp.int32)[:, None] * BLOCK
    place = (slot_blk[:, None, :] == jnp.arange(BLOCK)[None, :, None]).astype(jnp.bfloat16)

    def to_packed(value):
        value = value.reshape(shards, blocks, per, -1).transpose(1, 0, 2, 3)
        value = value.reshape(blocks, BLOCK, -1)
        value = jnp.einsum("bps,bsd->bpd", place, value, preferred_element_type=jnp.float32)
        return value.astype(jnp.bfloat16).reshape(total, -1)

    def to_sorted(value):
        value = jnp.einsum(
            "bps,bpd->bsd", place, value.reshape(blocks, BLOCK, -1), preferred_element_type=jnp.float32
        )
        value = value.astype(jnp.bfloat16).reshape(blocks, shards, per, -1).transpose(1, 0, 2, 3)
        return value.reshape(total, -1)

    normed = to_packed(x_all)
    cot_low = to_packed(c_all)
    seg_rows = segment_of(jnp.arange(total, dtype=jnp.int32), lengths[0])
    bounds = jnp.cumsum(lengths[0])[:-1].astype(jnp.int32)

    pieces = in_weight.astype(jnp.bfloat16).reshape(groups, part, -1)
    pieces = lax.all_to_all(pieces, "group", 0, 0)
    pieces = pieces.transpose(1, 0, 2).reshape(part, -1)

    def cut(lo, each):
        return pieces[:, lo : lo + each * shards].reshape(part, shards, each).transpose(1, 0, 2)

    spread = jnp.broadcast_to(pieces[None, :, 2 * INNER : 2 * INNER + SHARED], (shards, part, SHARED))
    send = jnp.concatenate(
        [cut(0, inner), cut(INNER, inner), spread, cut(2 * INNER + SHARED, heads)], axis=2
    )
    got = lax.all_to_all(send, "shard", 0, 0)
    got = lax.all_gather(got, "group")
    in_low = got.reshape(width, -1)
    out_low = lax.all_gather(out_weight.astype(jnp.bfloat16), "group", axis=1, tiled=True)
    out_full = lax.all_gather(out_low, "shard", axis=0, tiled=True)

    projected = dot32(normed, jnp.pad(in_low, ((0, 0), (0, -in_low.shape[1] % 128))))
    conv_bc = projected[:, 2 * inner : 2 * inner + SHARED]
    taps_v = own_slice(taps[:, :INNER], shard, inner, 1)
    taps_all = jnp.concatenate([taps_v, taps[:, INNER:]], axis=1)
    bias_all = jnp.concatenate([own_slice(conv_bias[:INNER], shard, inner, 0), conv_bias[INNER:]])[None, :]
    skip_wide = jnp.repeat(own_slice(skip_gain, shard, heads, 0), HDIM)[None, :]
    gain_own = own_slice(norm_gain, shard, inner, 0)[None, :]
    padding = max(TAIL - heads, 0)
    dt_raw = projected[:, 2 * inner + SHARED :]
    dt_raw = dt_raw + jnp.pad(own_slice(dt_bias, shard, heads, 0), (0, dt_raw.shape[1] - heads))[None, :]
    dt_cols = jax.nn.softplus(dt_raw)
    rate = jnp.pad(-jnp.exp(own_slice(rate_log, shard, heads, 0)), (0, padding))[:, None]
    d_out = dot32(cot_low, out_low, ((1,), (1,)))
    pre, mixed, states, sums = mixer_forward(
        bounds, projected, dt_cols, d_out, taps_all, bias_all, rate, skip_wide, gain_own
    )
    sums = lax.psum(sums.T, "shard").T / INNER
    r_out = lax.rsqrt(sums[:, 0:1] + eps_norm)
    normed_out = (mixed * jax.nn.silu(projected[:, :inner]) * r_out * gain_own).astype(jnp.bfloat16)
    grad_out_part = dot32(normed_out, cot_low, ((0,), (0,)))
    grad_out = lax.psum_scatter(grad_out_part, "group", scatter_dimension=1, tiled=True)

    home = lax.all_to_all(to_sorted(normed_out).reshape(shards, rows, inner), "shard", 0, 0)
    home = home.transpose(1, 0, 2).reshape(rows, INNER)
    home = dot32(sort_mat, home, ((0,), (0,))).astype(jnp.bfloat16)
    block_out = tokens + dot32(home, out_full)

    d_cols, d_bc, d_dt, grads, rate_terms = mixer_backward(
        bounds, pre, mixed, projected, d_out, sums, states, dt_cols, taps_v, rate, skip_wide, gain_own
    )
    d_dtraw = d_dt[:heads].T * jax.nn.sigmoid(dt_raw[:, :heads])
    grad_dtb = jnp.sum(d_dtraw, axis=0)
    grad_rate = jnp.sum(rate_terms[:heads], axis=1)
    grad_skip = jnp.sum(grads[6].reshape(heads, HDIM), axis=1)
    d_bc = lax.psum_scatter(d_bc.T, "shard", scatter_dimension=0, tiled=True).T
    _, pull_bc = jax.vjp(
        lambda c, t, b: convolve(c, seg_rows, t, b),
        own_slice(conv_bc, shard, shared, 1),
        own_slice(taps[:, INNER:], shard, shared, 1),
        own_slice(conv_bias[INNER:], shard, shared, 0),
    )
    d_conv_bc, grad_taps_bc, grad_bias_bc = pull_bc(d_bc)
    d_rest = jnp.concatenate([d_conv_bc, d_dtraw], axis=1).astype(jnp.bfloat16)
    d_project = jnp.concatenate([d_cols, d_rest], axis=1)
    in_own = jnp.concatenate(
        [
            in_low[:, : 2 * inner],
            own_slice(in_low[:, 2 * inner : 2 * inner + SHARED], shard, shared, 1),
            in_low[:, 2 * inner + SHARED :],
        ],
        axis=1,
    )
    d_normed = dot32(to_sorted(d_project), in_own, ((1,), (1,)))
    grad_in = dot32(normed, d_project, ((0,), (0,)))
    mine = [
        grads[:CONV].reshape(-1),
        grad_taps_bc.reshape(-1),
        grads[4],
        grad_bias_bc,
        grad_dtb,
        grad_rate,
        grad_skip,
        grads[5],
    ]
    extents = [piece.shape[0] for piece in mine]
    mine = jnp.concatenate(mine)
    mine = jnp.pad(mine, (0, -mine.shape[0] % 1024)).reshape(-1, 128)
    x_scaled = (tokens * r_in).reshape(rows, shards, groups, part).transpose(0, 2, 1, 3).reshape(rows, width)
    x_scaled = jnp.dot(sort_mat.astype(jnp.float32), x_scaled, precision=lax.Precision.HIGHEST)
    d_normed, grad_in, small_all, gain_all = tail_exchange(
        shards,
        groups,
        d_normed.reshape(shards, rows, width),
        grad_in.reshape(groups, shards * part, -1),
        mine,
        x_scaled,
    )
    d_normed = jnp.dot(
        sort_mat.T.astype(jnp.float32), d_normed, precision=lax.Precision.HIGHEST
    )
    d_normed = d_normed.reshape(rows, groups, shards, part).transpose(0, 2, 1, 3).reshape(rows, width)
    d_scaled = pre_gain[None, :] * d_normed
    inside = jnp.mean(tokens * d_scaled, axis=1, keepdims=True)
    input_grad = cotangent + r_in * (d_scaled - tokens * (r_in * r_in) * inside)
    grad_pre = jnp.sum(gain_all, axis=0).reshape(groups, shards, part).transpose(1, 0, 2).reshape(width)


    def join(lo, each):
        return grad_in[:, :, lo : lo + each].transpose(1, 0, 2).reshape(part, shards * each)

    grad_in = jnp.concatenate(
        [
            join(0, inner),
            join(inner, inner),
            join(2 * inner, shared),
            join(2 * inner + shared, heads),
        ],
        axis=1,
    )
    grad_in = grad_in.reshape(part, groups, -1).transpose(1, 0, 2)
    grad_in = lax.all_to_all(grad_in, "group", 0, 0).reshape(in_weight.shape)

    mine = small_all.reshape(shards, -1)
    found, offset = [], 0
    for extent in extents:
        found.append(mine[:, offset : offset + extent])
        offset = offset + extent

    def taps_of(piece):
        return piece.reshape(shards, CONV, -1).transpose(1, 0, 2).reshape(CONV, -1)

    grad_taps = jnp.concatenate([taps_of(found[0]), taps_of(found[1])], axis=1).reshape(-1)
    grad_small = jnp.concatenate(
        [grad_taps] + [piece.reshape(-1) for piece in found[2:]]
        + [grad_pre]
    )
    in_new = nesterov(in_weight, grad_in, in_moment, in_average, rate_in)
    out_new = nesterov(out_weight, grad_out, out_moment, out_average, rate_out)
    small_new = nesterov(small_params, grad_small, small_moment, small_average, rate_small)
    return (block_out, input_grad) + in_new + out_new + small_new


def solution(mesh):
    rows = P(("group", "shard"), None)
    tile = P("shard", "group")
    return jax.shard_map(
        local,
        mesh=mesh,
        in_specs=(
            rows,
            rows,
            P("group", None),
            P(("group", "shard")),
            tile,
            tile,
            P(),
            tile,
            tile,
            P(),
            tile,
            tile,
            P(),
        ),
        out_specs=(rows, rows, tile, tile, tile, tile, tile, tile, P(), P(), P()),
        check_vma=False,
    )
```

```python
import functools

import jax
import jax.numpy as jnp
from jax import lax
from jax.experimental import pallas as pl
from jax.experimental.pallas import tpu as pltpu
from jax.sharding import PartitionSpec as P

D = 2048
HEADS = 64
HDIM = 64
STATE = 128
CONV = 4
BLOCK = 256
INNER = 4096
XBC = 4352
SHARED = 2 * STATE
TAIL = 8
MESH = pl.DeviceIdType.MESH


eps_norm = 1e-05
momentum_decay = 0.9
weight_decay = 0.01
average_decay = 0.99
rate_in = 0.0001
rate_out = 3e-05
rate_small = 0.001


def unpack(packed_small):
    extents = [CONV * XBC, XBC, HEADS, HEADS, HEADS, INNER, D]
    pieces = []
    offset = 0
    for extent in extents:
        pieces.append(packed_small[offset : offset + extent])
        offset = offset + extent
    return pieces


def segment_of(positions, lengths_row):
    bounds = jnp.cumsum(lengths_row)[:-1]
    inside = jnp.sum((positions[:, None] >= bounds[None, :]).astype(jnp.int32), axis=1)
    return jnp.where(positions < 0, -1, inside)


def convolve(conv_rows, seg_rows, conv_taps, conv_bias):
    row_count, width = conv_rows.shape
    extended = jnp.concatenate([jnp.zeros((CONV - 1, width), conv_rows.dtype), conv_rows], axis=0)
    seg_ext = jnp.concatenate([jnp.full((CONV - 1,), -1, jnp.int32), seg_rows], axis=0)
    conv_sum = jnp.zeros_like(conv_rows) + conv_bias[None, :]
    for tap_index in range(CONV):
        same_seq = (seg_ext[tap_index : tap_index + row_count] == seg_rows)[:, None]
        conv_sum = conv_sum + jnp.where(
            same_seq,
            extended[tap_index : tap_index + row_count] * conv_taps[tap_index][None, :],
            0.0,
        )
    return jax.nn.silu(conv_sum)


def split(value):
    high = value.astype(jnp.bfloat16)
    return high, (value - high.astype(jnp.float32)).astype(jnp.bfloat16)


def dots(a, b, contract):
    return lax.dot_general(a, b, (contract, ((), ())), preferred_element_type=jnp.float32)


def dot3(a, b, contract=((1,), (0,))):
    a = a if isinstance(a, tuple) else split(a)
    b = b if isinstance(b, tuple) else split(b)
    return dots(a[0], b[0], contract) + (dots(a[0], b[1], contract) + dots(a[1], b[0], contract))


NT = ((1,), (1,))


def head_sums(value, marks):
    high = value.astype(jnp.bfloat16)
    rest = value - high.astype(jnp.float32)
    mid = rest.astype(jnp.bfloat16)
    low = (rest - mid.astype(jnp.float32)).astype(jnp.bfloat16)
    return dots(marks, high, NT) + (dots(marks, mid, NT) + dots(marks, low, NT))


def widen(columns, heads):
    rows = columns.shape[0]
    low_half = lax.broadcasted_iota(jnp.int32, (rows, 2 * HDIM), 1) < HDIM
    return jnp.concatenate(
        [
            jnp.where(low_half, columns[:, h : h + 1], columns[:, h + 1 : h + 2])
            for h in range(0, heads, 2)
        ],
        axis=1,
    )


def running_sum(value, reverse=False):
    lane = lax.broadcasted_iota(jnp.int32, value.shape, 1)
    count = value.shape[1]
    step = 1
    while step < count:
        if reverse:
            value = value + jnp.where(lane < count - step, pltpu.roll(value, count - step, 1), 0.0)
        else:
            value = value + jnp.where(lane >= step, pltpu.roll(value, step, 1), 0.0)
        step *= 2
    return value


def sequence_of(positions, bounds):
    inside = jnp.where(positions >= bounds[0], 1, 0) + jnp.where(positions >= bounds[1], 1, 0)
    return jnp.where(positions < 0, -1, inside)


def block_facts(block, bounds, dt_t, rate):
    start = block * BLOCK
    seg_col = sequence_of(start + lax.broadcasted_iota(jnp.int32, (BLOCK, 1), 0), bounds)
    seg_row = sequence_of(start + lax.broadcasted_iota(jnp.int32, (1, BLOCK), 1), bounds)
    before = sequence_of(start - 1 + lax.broadcasted_iota(jnp.int32, (1, 1), 1), bounds)
    last = sequence_of(start + BLOCK - 1 + lax.broadcasted_iota(jnp.int32, (1, 1), 1), bounds)
    run_t = running_sum(dt_t * rate)
    run = run_t.T
    final = run[BLOCK - 1 :, :]
    carried = jnp.where(seg_col == before, jnp.exp(run), 0.0)
    tail = jnp.where(seg_col == last, jnp.exp(final - run), 0.0)
    keep = jnp.where(last == before, jnp.exp(final), 0.0)
    return seg_col, seg_row, run_t, run, carried, tail, keep


def barrier_with(peers):
    barrier = pltpu.get_barrier_semaphore()
    for peer in peers:
        pl.semaphore_signal(barrier, inc=1, device_id=peer, device_id_type=MESH)
    pl.semaphore_wait(barrier, len(peers))


def remote(src, dst, sends, recvs, **where):
    return pltpu.make_async_remote_copy(
        src_ref=src, dst_ref=dst, send_sem=sends, recv_sem=recvs, device_id=where, device_id_type=MESH
    )


def forward_kernel(
    heads, shards, bounds, gate, conv_v, conv_bc, dt_cols, d_out, taps, bias, rate, skip, gain,
    pre_out, mixed_out, state_out, sums_out, ext, state, own_sums, sums_in, sums_send, sums_recv,
):
    block = pl.program_id(0)
    inner = heads * HDIM
    shard = lax.axis_index("shard")

    @pl.when(block == 0)
    def _():
        barrier_with([{"shard": (shard + step) % shards} for step in range(1, shards)])
        ext[:TAIL, :] = jnp.zeros((TAIL, ext.shape[1]), jnp.float32)
        state[...] = jnp.zeros_like(state)

    bounds = (bounds[0], bounds[1])
    dt = dt_cols[...]
    dt_t = dt.T[: rate.shape[0], :]
    seg_col, seg_row, run_t, run, carried, tail, keep = block_facts(block, bounds, dt_t, rate[...])
    ext[TAIL:, :inner] = conv_v[...]
    ext[TAIL:, inner:] = conv_bc[...]
    place = block * BLOCK + lax.broadcasted_iota(jnp.int32, (BLOCK, 1), 0)
    pre = bias[...] + taps[CONV - 1 : CONV, :] * ext[TAIL:, :]
    for back in range(1, CONV):
        same = sequence_of(place - back, bounds) == seg_col
        moved = ext[TAIL - back : TAIL - back + BLOCK, :]
        pre = pre + jnp.where(same, moved, 0.0) * taps[CONV - 1 - back : CONV - back, :]
    ext[:TAIL, :] = ext[BLOCK:, :]
    pre_out[...] = pre
    conv = pre / (1.0 + jnp.exp(-pre))
    values, b_rows, c_rows = conv[:, :inner], conv[:, inner : inner + STATE], conv[:, inner + STATE :]
    fed = values * widen(dt, heads)
    rows = lax.broadcasted_iota(jnp.int32, (BLOCK, BLOCK), 0)
    cols = lax.broadcasted_iota(jnp.int32, (BLOCK, BLOCK), 1)
    allowed = (seg_col == seg_row) & (rows >= cols)
    b_parts, c_parts = split(b_rows), split(c_rows)
    scores = jnp.where(allowed, dot3(c_parts, b_parts, NT), 0.0)
    old = state[...]
    state_out[0] = old
    output = widen(carried, heads) * dot3(c_parts, old)
    low_half = lax.broadcasted_iota(jnp.int32, (BLOCK, 2 * HDIM), 1) < HDIM
    inside = []
    for h in range(0, heads, 2):
        pair = split(fed[:, h * HDIM : (h + 2) * HDIM])
        found = []
        for k in (h, h + 1):
            mixing = jnp.exp(jnp.minimum(run[:, k : k + 1] - run_t[k : k + 1, :], 0.0)) * scores
            found.append(dot3(mixing, pair))
        inside.append(jnp.where(low_half, found[0], found[1]))
    mixed = output + jnp.concatenate(inside, axis=1) + skip[...] * values
    mixed_out[...] = mixed
    state[...] = widen(keep, heads) * old + dot3(b_rows.T, widen(tail, heads) * fed)
    gated = mixed * (gate[...] / (1.0 + jnp.exp(-gate[...])))
    squares = jnp.sum(gated * gated, axis=1, keepdims=True)
    products = jnp.sum(gated * gain[...] * d_out[...], axis=1, keepdims=True)
    lane = lax.broadcasted_iota(jnp.int32, (BLOCK, 128), 1)
    both = jnp.where(lane == 0, squares, jnp.where(lane == 1, products, 0.0))
    here = pl.ds(pl.multiple_of(block * BLOCK, BLOCK), BLOCK)
    own_sums[:, here] = both.T[:8, :]

    def push(step, at):
        return remote(
            own_sums.at[:, at], sums_in.at[step - 1, :, at], sums_send.at[step], sums_recv.at[step],
            shard=(shard + step) % shards,
        )

    for step in range(1, shards):
        push(step, here).start()

    @pl.when(block == pl.num_programs(0) - 1)
    def _():
        everything = pl.ds(0, own_sums.shape[1])
        for step in range(1, shards):
            push(step, everything).wait()
        found = own_sums[...]
        for step in range(1, shards):
            found = found + sums_in[step - 1]
        sums_out[...] = found * (1.0 / INNER)


def backward_kernel(
    heads, blocks, shards, bounds, pre, mixed, gate, d_out, conv_v, sums, state_in, dt_cols, taps, rate, skip, gain, marks,
    d_cols, d_bc, d_dt, grads, grad_rate, ext, carry, bc_rows, bc_in, bc_send, bc_recv,
):
    step = pl.program_id(0)
    block = blocks - 1 - step
    inner = heads * HDIM
    shard = lax.axis_index("shard")
    shared = SHARED // shards

    @pl.when(step == 0)
    def _():
        barrier_with([{"shard": (shard + turn) % shards} for turn in range(1, shards)])
        ext[BLOCK:, :] = jnp.zeros((TAIL, ext.shape[1]), jnp.float32)
        carry[...] = jnp.zeros_like(carry)
        grads[...] = jnp.zeros_like(grads)
        grad_rate[...] = jnp.zeros_like(grad_rate)

    bounds = (bounds[0], bounds[1])
    dt = dt_cols[...]
    dt_t = dt.T[: rate.shape[0], :]
    seg_col, seg_row, run_t, run, carried, tail, keep = block_facts(block, bounds, dt_t, rate[...])
    sums_cols = sums[...].T
    r_out = lax.rsqrt(sums_cols[:, 0:1] + 1e-05)
    inside = sums_cols[:, 1:2]
    gate_now = gate[...]
    gate_sig = 1.0 / (1.0 + jnp.exp(-gate_now))
    act = gate_now * gate_sig
    mixed_now = mixed[...]
    gated = mixed_now * act
    d_out_now = d_out[...]
    d_gated = r_out * (gain[...] * d_out_now - gated * (r_out * r_out) * inside)
    dy = d_gated * act
    d_cols[:, :inner] = (d_gated * mixed_now * (gate_sig * (1.0 + gate_now * (1.0 - gate_sig)))).astype(jnp.bfloat16)
    grads[5:6, :] += jnp.sum(gated * r_out * d_out_now, axis=0, keepdims=True)
    pre_now = pre[...]
    sig = 1.0 / (1.0 + jnp.exp(-pre_now))
    conv = pre_now * sig
    values, b_rows, c_rows = conv[:, :inner], conv[:, inner : inner + STATE], conv[:, inner + STATE :]
    grads[6:7, :] += jnp.sum(dy * values, axis=0, keepdims=True)
    dt_wide = widen(dt, heads)
    fed = values * dt_wide
    old, after = state_in[0], carry[...]
    b_parts, c_parts, old_parts, after_parts = split(b_rows), split(c_rows), split(old), split(after)
    carried_wide, tail_wide, keep_wide = widen(carried, heads), widen(tail, heads), widen(keep, heads)
    rows = lax.broadcasted_iota(jnp.int32, (BLOCK, BLOCK), 0)
    cols = lax.broadcasted_iota(jnp.int32, (BLOCK, BLOCK), 1)
    allowed = (seg_col == seg_row) & (cols >= rows)
    scores_t = jnp.where(allowed, dot3(b_parts, c_parts, NT), 0.0)
    low_half = lax.broadcasted_iota(jnp.int32, (BLOCK, 2 * HDIM), 1) < HDIM
    d_scores_t = jnp.zeros((BLOCK, BLOCK), jnp.float32)
    d_fed, row_terms, col_terms = [], [], []
    for h in range(0, heads, 2):
        fed_pair = fed[:, h * HDIM : (h + 2) * HDIM]
        dy_pair = split(dy[:, h * HDIM : (h + 2) * HDIM])
        found = []
        for k in (h, h + 1):
            own = low_half if k == h else jnp.logical_not(low_half)
            d_mixing = dot3(jnp.where(own, fed_pair, 0.0), dy_pair, NT)
            decay = jnp.exp(jnp.minimum(run_t[k : k + 1, :] - run[:, k : k + 1], 0.0))
            mixing = decay * scores_t
            d_scores_t = d_scores_t + decay * d_mixing
            flow = mixing * d_mixing
            row_terms.append(jnp.sum(flow, axis=0, keepdims=True))
            col_terms.append(jnp.sum(flow, axis=1, keepdims=True))
            found.append(dot3(mixing, dy_pair))
        d_fed.append(jnp.where(low_half, found[0], found[1]))
    d_scores_t = split(jnp.where(allowed, d_scores_t, 0.0))
    fed_tail = fed * tail_wide
    dy_carried = dy * carried_wide
    d_fed_out = tail_wide * dot3(b_parts, after_parts)
    d_fed = jnp.concatenate(d_fed, axis=1) + d_fed_out
    dy_parts, tail_parts = split(dy_carried), split(fed_tail)
    here = pl.ds(pl.multiple_of(block * BLOCK, BLOCK), BLOCK)
    bc_rows[:STATE, here] = (dot3(d_scores_t, c_parts) + dot3(tail_parts, after_parts, NT)).T
    bc_rows[STATE:, here] = (dot3(d_scores_t, b_parts, ((0,), (0,))) + dot3(dy_parts, old_parts, NT)).T

    def push(turn, at):
        peer = (shard + turn) % shards
        rows_at = pl.ds(pl.multiple_of(peer * shared, shared), shared)
        return remote(
            bc_rows.at[rows_at, at], bc_in.at[turn - 1, :, at], bc_send.at[turn], bc_recv.at[turn], shard=peer
        )

    for turn in range(1, shards):
        push(turn, here).start()
    head_count = dt_t.shape[0]
    pad = [jnp.zeros((1, BLOCK), jnp.float32)] * (head_count - heads)
    pad_col = [jnp.zeros((BLOCK, 1), jnp.float32)] * (head_count - heads)
    d_run = jnp.concatenate(row_terms + pad, axis=0) - jnp.concatenate(col_terms + pad_col, axis=1).T
    d_run = d_run + head_sums(dy_carried * dot3(c_parts, old_parts), marks[...])
    leaving = head_sums(fed * d_fed_out, marks[...])
    kept = jnp.sum(old * after, axis=0, keepdims=True) * keep_wide
    kept = jnp.sum(marks[...].astype(jnp.float32) * kept, axis=1, keepdims=True)
    at_end = lax.broadcasted_iota(jnp.int32, (head_count, BLOCK), 1) == BLOCK - 1
    total = jnp.sum(leaving, axis=1, keepdims=True) + kept
    d_run = d_run - leaving + jnp.where(at_end, total, 0.0)
    d_log = running_sum(d_run, reverse=True)
    d_dt[...] = d_log * rate[...] + head_sums(values * d_fed, marks[...])
    grad_rate[...] += d_log * (dt_t * rate[...])
    carry[...] = keep_wide * after + dot3(c_rows.T, dy_parts)
    pre_v, sig_v = pre_now[:, :inner], sig[:, :inner]
    d_values = dt_wide * d_fed + skip[...] * dy
    d_pre = d_values * (sig_v * (1.0 + pre_v * (1.0 - sig_v)))
    ext[:BLOCK, :] = d_pre
    place = block * BLOCK + lax.broadcasted_iota(jnp.int32, (BLOCK, 1), 0)
    conv_in = conv_v[...]
    d_conv = taps[CONV - 1 : CONV, :] * d_pre
    grads[CONV - 1 : CONV, :] += jnp.sum(conv_in * d_pre, axis=0, keepdims=True)
    grads[CONV : CONV + 1, :] += jnp.sum(d_pre, axis=0, keepdims=True)
    for ahead in range(1, CONV):
        same = sequence_of(place + ahead, bounds) == seg_col
        moved = jnp.where(same, ext[ahead : ahead + BLOCK, :], 0.0)
        d_conv = d_conv + taps[CONV - 1 - ahead : CONV - ahead, :] * moved
        grads[CONV - 1 - ahead : CONV - ahead, :] += jnp.sum(conv_in * moved, axis=0, keepdims=True)
    ext[BLOCK:, :] = ext[:TAIL, :]
    d_cols[:, inner:] = d_conv.astype(jnp.bfloat16)

    @pl.when(step == blocks - 1)
    def _():
        everything = pl.ds(0, bc_rows.shape[1])
        for turn in range(1, shards):
            push(turn, everything).wait()
        found = bc_rows[pl.ds(pl.multiple_of(shard * shared, shared), shared), :]
        for turn in range(1, shards):
            found = found + bc_in[turn - 1]
        d_bc[...] = found


def whole(shape):
    return pl.BlockSpec(shape, lambda *_: (0,) * len(shape))


def mixer_forward(shards, bounds, projected, dt_cols, d_out, taps, bias, rate, skip, gain):
    total, inner = d_out.shape
    heads, blocks, padded = inner // HDIM, total // BLOCK, rate.shape[0]

    def block_of(width, column):
        return pl.BlockSpec((BLOCK, width), lambda i: (i, column))

    return pl.pallas_call(
        functools.partial(forward_kernel, heads, shards),
        grid_spec=pltpu.PrefetchScalarGridSpec(
            num_scalar_prefetch=0,
            grid=(blocks,),
            in_specs=[
                pl.BlockSpec(memory_space=pltpu.SMEM),
                block_of(inner, 0),
                block_of(inner, 1),
                block_of(SHARED, 2 * inner // SHARED),
                block_of(dt_cols.shape[1], 0),
                block_of(inner, 0),
                whole(taps.shape),
                whole(bias.shape),
                whole(rate.shape),
                whole(skip.shape),
                whole(gain.shape),
            ],
            out_specs=[
                block_of(inner + SHARED, 0),
                block_of(inner, 0),
                pl.BlockSpec((1, STATE, inner), lambda i: (i, 0, 0)),
                whole((8, total)),
            ],
            scratch_shapes=[
                pltpu.VMEM((BLOCK + TAIL, inner + SHARED), jnp.float32),
                pltpu.VMEM((STATE, inner), jnp.float32),
                pltpu.VMEM((8, total), jnp.float32),
                pltpu.VMEM((shards - 1, 8, total), jnp.float32),
                pltpu.SemaphoreType.DMA((shards,)),
                pltpu.SemaphoreType.DMA((shards,)),
            ],
        ),
        out_shape=[
            jax.ShapeDtypeStruct((total, inner + SHARED), jnp.float32),
            jax.ShapeDtypeStruct((total, inner), jnp.float32),
            jax.ShapeDtypeStruct((blocks, STATE, inner), jnp.float32),
            jax.ShapeDtypeStruct((8, total), jnp.float32),
        ],
        compiler_params=pltpu.CompilerParams(
            collective_id=2, has_side_effects=True, vmem_limit_bytes=56 * 1024 * 1024
        ),
        name="mixer_forward",
    )(bounds, projected, projected, projected, dt_cols, d_out, taps, bias, rate, skip, gain)


def mixer_backward(shards, bounds, pre, mixed, projected, d_out, sums, states, dt_cols, taps, rate, skip, gain):
    total, inner = d_out.shape
    heads, blocks, padded = inner // HDIM, total // BLOCK, rate.shape[0]
    shared = SHARED // shards
    marks = (jnp.arange(padded)[:, None] == jnp.arange(inner)[None, :] // HDIM).astype(jnp.bfloat16)

    def block_of(width, column):
        return pl.BlockSpec((BLOCK, width), lambda i: (blocks - 1 - i, column))

    return pl.pallas_call(
        functools.partial(backward_kernel, heads, blocks, shards),
        grid_spec=pltpu.PrefetchScalarGridSpec(
            num_scalar_prefetch=0,
            grid=(blocks,),
            in_specs=[
                pl.BlockSpec(memory_space=pltpu.SMEM),
                block_of(inner + SHARED, 0),
                block_of(inner, 0),
                block_of(inner, 0),
                block_of(inner, 0),
                block_of(inner, 1),
                pl.BlockSpec((8, BLOCK), lambda i: (0, blocks - 1 - i)),
                pl.BlockSpec((1, STATE, inner), lambda i: (blocks - 1 - i, 0, 0)),
                block_of(dt_cols.shape[1], 0),
                whole(taps.shape),
                whole(rate.shape),
                whole(skip.shape),
                whole(gain.shape),
                whole(marks.shape),
            ],
            out_specs=[
                block_of(2 * inner, 0),
                whole((shared, total)),
                pl.BlockSpec((padded, BLOCK), lambda i: (0, blocks - 1 - i)),
                whole((8, inner)),
                whole((padded, BLOCK)),
            ],
            scratch_shapes=[
                pltpu.VMEM((BLOCK + TAIL, inner), jnp.float32),
                pltpu.VMEM((STATE, inner), jnp.float32),
                pltpu.VMEM((SHARED, total), jnp.float32),
                pltpu.VMEM((shards - 1, shared, total), jnp.float32),
                pltpu.SemaphoreType.DMA((shards,)),
                pltpu.SemaphoreType.DMA((shards,)),
            ],
        ),
        out_shape=[
            jax.ShapeDtypeStruct((total, 2 * inner), jnp.bfloat16),
            jax.ShapeDtypeStruct((shared, total), jnp.float32),
            jax.ShapeDtypeStruct((padded, total), jnp.float32),
            jax.ShapeDtypeStruct((8, inner), jnp.float32),
            jax.ShapeDtypeStruct((padded, BLOCK), jnp.float32),
        ],
        compiler_params=pltpu.CompilerParams(
            collective_id=3, has_side_effects=True, vmem_limit_bytes=56 * 1024 * 1024
        ),
        name="mixer_backward",
    )(bounds, pre, mixed, projected, d_out, projected, sums, states, dt_cols, taps, rate, skip, gain, marks)


def other_place(step, place, count):
    upwards = count - 1 - place
    low = jnp.where(step < upwards, count - 1 - step, step - upwards)
    high = jnp.where(step < place, step, count - 1 - (step - place))
    return jnp.where(2 * place < count, low, high)


def tail_kernel(
    shards, groups, columns, near,
    partial, weight_part, small, scaled_rows,
    rows_out, weight_out, small_out, gain_out, core_in, row_in, small_in, gain_in,
    wide_in, wide_scale, line_in, line_scale,
    held, coded, scales, line_coded, line_scales, got, got_scale, marks, total, other, send_rows, small_sum, gain_sum,
    load_sem, wide_send, wide_recv, line_send, line_recv, core_send, core_recv, row_send, row_recv,
    deal_send, deal_recv, small_send, small_recv, gain_send, gain_recv,
):
    shard, group = lax.axis_index("shard"), lax.axis_index("group")
    lines = shards // columns
    rows_y = groups // 2
    z, x = shard // columns, shard % columns
    y, core = group // 2, group % 2
    part = weight_out.shape[1]
    count = held.shape[0]

    def load(src, dst):
        copy = pltpu.make_async_copy(src, dst, load_sem)
        copy.start()
        copy.wait()

    shard_peers = [(shard + step) % shards for step in range(1, shards)]
    group_peers = [(group + step) % groups for step in range(1, groups)]
    barrier_with([{"shard": peer} for peer in shard_peers] + [{"group": peer} for peer in group_peers])

    mate = y * 2 + 1 - core

    def core_copy(turn):
        return remote(weight_part.at[turn * 2 + 1 - core], core_in.at[turn], core_send.at[turn], core_recv.at[turn], group=mate)

    for turn in range(rows_y):
        core_copy(turn).start()

    def small_copy(step):
        return remote(small, small_in.at[step - 1], small_send.at[step - 1], small_recv.at[step - 1], group=(group + step) % groups)

    for step in range(1, groups):
        small_copy(step).start()

    def code(coded_to, scales_to):
        @pl.loop(0, count // 32, unroll=2)
        def _(turn):
            rows = pl.ds(pl.multiple_of(turn * 32, 32), 32)
            value = held[rows, :]
            most = jnp.maximum(jnp.max(jnp.abs(value), axis=1, keepdims=True), 1e-30)
            coded_to[rows, :] = jnp.round(value * (32767.0 / most)).astype(jnp.int32).astype(jnp.int16)
            marks[rows, :] = jnp.broadcast_to(most * (1.0 / 32767.0), (32, 128))

        scales_to[...] = marks[...].T[:8, :]

    def add(coded_from, scales_from):
        if not near:
            load(coded_from, got)
            load(scales_from, got_scale)
            coded_from, scales_from = got, got_scale
        marks[...] = jnp.broadcast_to(scales_from[0:1, :], (128, count)).T

        @pl.loop(0, count // 32, unroll=2)
        def _(turn):
            rows = pl.ds(pl.multiple_of(turn * 32, 32), 32)
            held[rows, :] += coded_from[rows, :].astype(jnp.float32) * marks[rows, 0:1]

    def place_of(step):
        return other_place(step, z, lines) if step < lines - 1 else z

    def wide_copies(step, hop):
        at = (hop - 1) * lines + step
        peer = z * columns + (x + hop) % columns
        target = place_of(step)
        return (
            remote(coded.at[step], wide_in.at[hop - 1, target], wide_send.at[0, at], wide_recv.at[0, at], shard=peer),
            remote(scales.at[step], wide_scale.at[hop - 1, target], wide_send.at[1, at], wide_recv.at[1, at], shard=peer),
        )

    for hop in range(1, columns):
        for step in range(lines):
            if hop > 1:
                for copy in wide_copies(step, hop - 1):
                    copy.wait_send()
            load(partial.at[place_of(step) * columns + (x + hop) % columns], held)
            code(coded.at[step], scales.at[step])
            for copy in wide_copies(step, hop):
                copy.start()

    load(small, small_sum)
    for step in range(1, groups):
        small_copy(step).wait_recv()
        load(small_in.at[step - 1], other.at[: small.shape[0], :128])
        small_sum[...] += other[: small.shape[0], :128]

    def small_deal(step):
        return remote(small_sum, small_out.at[shard], small_send.at[groups + step], small_recv.at[groups + step], shard=(shard + step) % shards)

    for step in range(1, shards):
        small_deal(step).start()
    load(small_sum, small_out.at[shard])

    def row_copy(step):
        return remote(send_rows.at[step - 1], row_in.at[step - 1], row_send.at[step - 1], row_recv.at[step - 1], group=(y + step) % rows_y * 2 + core)

    def add_other():
        @pl.loop(0, total.shape[0] // part)
        def _(turn):
            rows = pl.ds(pl.multiple_of(turn * part, part), part)
            total[rows, :] += other[rows, :]

    def core_sum(turn):
        load(weight_part.at[turn * 2 + core], total)
        load(core_in.at[turn], other)
        add_other()

    for turn in range(rows_y):
        core_copy(turn).wait_recv()
    for step in range(1, rows_y):
        core_sum((y + step) % rows_y)
        load(total, send_rows.at[step - 1])
        row_copy(step).start()
    core_sum(y)

    def line_copies(step):
        target = place_of(step)
        way = jnp.where(target > z, 0, 1)
        peer = jnp.where(target > z, z + 1, z - 1) * columns + x
        return (
            remote(line_coded.at[step], line_in.at[way, target], line_send.at[0, step], line_recv.at[0, way, target], shard=peer),
            remote(line_scales.at[step], line_scale.at[way, target], line_send.at[1, step], line_recv.at[1, way, target], shard=peer),
        )

    def take(way, target):
        source = jnp.where(way == 0, z - 1, z + 1)
        peer = jnp.clip(source, 0, lines - 1) * columns + x
        remote(line_coded.at[0], line_in.at[way, target], line_send.at[0, 0], line_recv.at[0, way, target], shard=peer).wait_recv()
        remote(line_scales.at[0], line_scale.at[way, target], line_send.at[1, 0], line_recv.at[1, way, target], shard=peer).wait_recv()
        add(line_in.at[way, target], line_scale.at[way, target])

    def gather_wide(step):
        target = place_of(step)
        load(partial.at[target * columns + x], held)
        for hop in range(1, columns):
            for copy in wide_copies(step, hop):
                copy.wait_recv()
            add(wide_in.at[hop - 1, target], wide_scale.at[hop - 1, target])

    def deal_copy(step):
        peer = (shard + step) % shards
        rows = pl.ds(pl.multiple_of(peer * part, part), part)
        return remote(total.at[rows], weight_out.at[shard], deal_send.at[step], deal_recv.at[step], shard=peer)

    def deal():
        for step in range(1, rows_y):
            row_copy(step).wait_recv()
            load(row_in.at[step - 1], other)
            add_other()
        for step in range(1, shards):
            deal_copy(step).start()
        load(total.at[pl.ds(pl.multiple_of(shard * part, part), part)], weight_out.at[shard])

    for step in range(lines - 1):
        if step == lines - 2:
            deal()
        target = place_of(step)
        way = jnp.where(target > z, 0, 1)
        gather_wide(step)

        @pl.when(jnp.where(target > z, z > 0, z < lines - 1))
        def _():
            take(way, target)

        code(line_coded.at[step], line_scales.at[step])
        for copy in line_copies(step):
            copy.start()
    gather_wide(lines - 1)

    @pl.when(z > 0)
    def _():
        take(0, z)

    @pl.when(z < lines - 1)
    def _():
        take(1, z)

    rows_out[...] = held[...]
    gain_sum[...] = jnp.zeros_like(gain_sum)

    @pl.loop(0, count // 8)
    def _(turn):
        rows = pl.ds(pl.multiple_of(turn * 8, 8), 8)
        gain_sum[...] += held[rows, :] * scaled_rows[rows, :]

    def gain_copy(step):
        return remote(gain_sum, gain_in.at[step - 1], gain_send.at[step - 1], gain_recv.at[step - 1], shard=(shard + step) % shards)

    def gain_deal(step):
        at = shards - 1 + step - 1
        return remote(gain_out, gain_in.at[at], gain_send.at[at], gain_recv.at[at], group=(group + step) % groups)

    for step in range(1, shards):
        gain_copy(step).start()
    gain_out[...] = gain_sum[...]
    for step in range(1, shards):
        gain_copy(step).wait_recv()
        gain_out[...] += gain_in[step - 1]
    for step in range(1, groups):
        gain_deal(step).start()
    for step in range(1, groups):
        gain_deal(step).wait_recv()
    for step in range(1, groups):
        gain_deal(step).wait_send()
    for step in range(1, groups):
        gain_out[...] += gain_in[shards - 1 + step - 1]

    for step in range(1, shards):
        gain_copy(step).wait_send()
        small_deal(step).wait()
        deal_copy(step).wait()
    for step in range(1, groups):
        small_copy(step).wait_send()
    for step in range(1, rows_y):
        row_copy(step).wait_send()
    for turn in range(rows_y):
        core_copy(turn).wait_send()
    for step in range(lines):
        for copy in wide_copies(step, columns - 1) if columns > 1 else ():
            copy.wait_send()
    for step in range(lines - 1):
        for copy in line_copies(step):
            copy.wait_send()


def grid_columns(shards):
    columns = 1
    while 2 * (2 * columns) * (2 * columns) <= shards:
        columns *= 2
    return columns if shards % columns == 0 else 1


def tail_exchange(shards, groups, partial, weight_part, small, scaled_rows):
    columns = grid_columns(shards)
    lines, rows_y = shards // columns, groups // 2
    count, width = scaled_rows.shape
    weight_rows, weight_width = weight_part.shape[1:]
    part = weight_rows // shards
    small_shape = small.shape
    coded, scale = (count, width), (8, count)
    any_space, vmem = pl.BlockSpec(memory_space=pl.ANY), pl.BlockSpec(memory_space=pltpu.VMEM)
    f32, i16 = jnp.float32, jnp.int16
    slots = max(columns - 1, 1)
    dma = pltpu.SemaphoreType.DMA
    landing = [
        ((slots, lines) + coded, i16),
        ((slots, lines) + scale, f32),
        ((2, lines) + coded, i16),
        ((2, lines) + scale, f32),
    ]
    near = shards * count * width <= 1 << 22
    out = pl.pallas_call(
        functools.partial(tail_kernel, shards, groups, columns, near),
        in_specs=[any_space, any_space, any_space, vmem],
        out_specs=[vmem, any_space, any_space, vmem] + [any_space] * 3 + [vmem] + ([] if near else [any_space] * 4),
        out_shape=[
            jax.ShapeDtypeStruct((count, width), f32),
            jax.ShapeDtypeStruct((shards, part, weight_width), f32),
            jax.ShapeDtypeStruct((shards,) + small_shape, f32),
            jax.ShapeDtypeStruct((8, width), f32),
            jax.ShapeDtypeStruct((rows_y, weight_rows, weight_width), f32),
            jax.ShapeDtypeStruct((max(rows_y - 1, 1), weight_rows, weight_width), f32),
            jax.ShapeDtypeStruct((max(groups - 1, 1),) + small_shape, f32),
            jax.ShapeDtypeStruct((shards - 1 + groups - 1, 8, width), f32),
        ]
        + ([] if near else [jax.ShapeDtypeStruct(*each) for each in landing]),
        scratch_shapes=([pltpu.VMEM(*each) for each in landing] if near else [])
        + [
            pltpu.VMEM((count, width), f32),
            pltpu.VMEM((lines,) + coded, i16),
            pltpu.VMEM((lines,) + scale, f32),
            pltpu.VMEM((lines,) + coded, i16),
            pltpu.VMEM((lines,) + scale, f32),
            pltpu.VMEM((16, 128) if near else coded, i16),
            pltpu.VMEM((8, 128) if near else scale, f32),
            pltpu.VMEM((count, 128), f32),
            pltpu.VMEM((weight_rows, weight_width), f32),
            pltpu.VMEM((weight_rows, weight_width), f32),
            pltpu.VMEM((max(rows_y - 1, 1), weight_rows, weight_width), f32),
            pltpu.VMEM(small_shape, f32),
            pltpu.VMEM((8, width), f32),
            dma,
            dma((2, slots * lines)),
            dma((2, slots * lines)),
            dma((2, lines)),
            dma((2, 2, lines)),
            dma((rows_y,)),
            dma((rows_y,)),
            dma((max(rows_y - 1, 1),)),
            dma((max(rows_y - 1, 1),)),
            dma((shards,)),
            dma((shards,)),
            dma((groups + shards,)),
            dma((groups + shards,)),
            dma((shards + groups,)),
            dma((shards + groups,)),
        ],
        compiler_params=pltpu.CompilerParams(
            collective_id=1, has_side_effects=True, vmem_limit_bytes=60 * 1024 * 1024
        ),
        name="tail_exchange",
    )(partial, weight_part, small, scaled_rows)
    return out[:4]


def nesterov(weight, gradient, moment, average, step_rate):
    decayed = gradient + weight_decay * weight
    new_moment = momentum_decay * moment + decayed
    new_weight = weight - step_rate * (decayed + momentum_decay * new_moment)
    new_average = average_decay * average + (1.0 - average_decay) * new_weight
    return (new_moment, new_weight, new_average)


def dot32(a, b, contract=((1,), (0,))):
    return lax.dot_general(a, b, (contract, ((), ())), preferred_element_type=jnp.float32)


def own_slice(value, index, width, axis):
    return lax.dynamic_slice_in_dim(value, index * width, width, axis)


def local(
    tokens,
    cotangent,
    lengths,
    deal_slot,
    in_weight,
    out_weight,
    small_params,
    in_moment,
    out_moment,
    small_moment,
    in_average,
    out_average,
    small_average,
):
    shards, groups = lax.axis_size("shard"), lax.axis_size("group")
    shard, group = lax.axis_index("shard"), lax.axis_index("group")
    rows, width = tokens.shape
    per = rows // shards
    total = rows * shards
    blocks = total // BLOCK
    heads = HEADS // shards
    inner = INNER // shards
    shared = SHARED // shards
    conv_flat, conv_bias, dt_bias, rate_log, skip_gain, norm_gain, pre_gain = unpack(small_params)
    taps = conv_flat.reshape(CONV, XBC)

    rank = jnp.sum((deal_slot[None, :] < deal_slot[:, None]).astype(jnp.int32), axis=1)
    sort_mat = (rank[None, :] == jnp.arange(rows)[:, None]).astype(jnp.bfloat16)
    sorted_slot = jnp.sum(jnp.where(sort_mat > 0, deal_slot[None, :], 0), axis=1)
    r_in = lax.rsqrt(jnp.mean(tokens * tokens, axis=1, keepdims=True) + eps_norm)
    normed_low = (tokens * r_in * pre_gain[None, :]).astype(jnp.bfloat16)
    part = in_weight.shape[0] // groups
    normed_low = normed_low.reshape(rows, shards, groups, part).transpose(0, 2, 1, 3).reshape(rows, width)
    x_sorted = dot32(sort_mat, normed_low).astype(jnp.bfloat16)
    c_sorted = dot32(sort_mat, cotangent.astype(jnp.bfloat16)).astype(jnp.bfloat16)
    x_all = lax.all_gather(x_sorted, "shard")
    c_all = lax.all_gather(c_sorted, "shard")
    slot_all = lax.all_gather(sorted_slot, "shard")

    slot_blk = slot_all.reshape(shards, blocks, per).transpose(1, 0, 2).reshape(blocks, BLOCK)
    slot_blk = slot_blk - jnp.arange(blocks, dtype=jnp.int32)[:, None] * BLOCK
    place = (slot_blk[:, None, :] == jnp.arange(BLOCK)[None, :, None]).astype(jnp.bfloat16)

    def to_packed(value):
        value = value.reshape(shards, blocks, per, -1).transpose(1, 0, 2, 3)
        value = value.reshape(blocks, BLOCK, -1)
        value = jnp.einsum("bps,bsd->bpd", place, value, preferred_element_type=jnp.float32)
        return value.astype(jnp.bfloat16).reshape(total, -1)

    def to_sorted(value):
        value = jnp.einsum(
            "bps,bpd->bsd", place, value.reshape(blocks, BLOCK, -1), preferred_element_type=jnp.float32
        )
        value = value.astype(jnp.bfloat16).reshape(blocks, shards, per, -1).transpose(1, 0, 2, 3)
        return value.reshape(total, -1)

    normed = to_packed(x_all)
    cot_low = to_packed(c_all)
    seg_rows = segment_of(jnp.arange(total, dtype=jnp.int32), lengths[0])
    bounds = jnp.cumsum(lengths[0])[:-1].astype(jnp.int32)

    pieces = in_weight.astype(jnp.bfloat16).reshape(groups, part, -1)
    pieces = lax.all_to_all(pieces, "group", 0, 0)
    pieces = pieces.transpose(1, 0, 2).reshape(part, -1)

    def cut(lo, each):
        return pieces[:, lo : lo + each * shards].reshape(part, shards, each).transpose(1, 0, 2)

    spread = jnp.broadcast_to(pieces[None, :, 2 * INNER : 2 * INNER + SHARED], (shards, part, SHARED))
    send = jnp.concatenate(
        [cut(0, inner), cut(INNER, inner), spread, cut(2 * INNER + SHARED, heads)], axis=2
    )
    got = lax.all_to_all(send, "shard", 0, 0)
    got = lax.all_gather(got, "group")
    in_low = got.reshape(width, -1)
    out_low = lax.all_gather(out_weight.astype(jnp.bfloat16), "group", axis=1, tiled=True)
    out_full = lax.all_gather(out_weight.astype(jnp.bfloat16), "shard", axis=0, tiled=True)
    out_full = lax.all_gather(out_full, "group", axis=1, tiled=True)

    projected = dot32(normed, jnp.pad(in_low, ((0, 0), (0, -in_low.shape[1] % 128))))
    conv_bc = projected[:, 2 * inner : 2 * inner + SHARED]
    taps_v = own_slice(taps[:, :INNER], shard, inner, 1)
    taps_all = jnp.concatenate([taps_v, taps[:, INNER:]], axis=1)
    bias_all = jnp.concatenate([own_slice(conv_bias[:INNER], shard, inner, 0), conv_bias[INNER:]])[None, :]
    skip_wide = jnp.repeat(own_slice(skip_gain, shard, heads, 0), HDIM)[None, :]
    gain_own = own_slice(norm_gain, shard, inner, 0)[None, :]
    padding = max(TAIL - heads, 0)
    dt_raw = projected[:, 2 * inner + SHARED :]
    dt_raw = dt_raw + jnp.pad(own_slice(dt_bias, shard, heads, 0), (0, dt_raw.shape[1] - heads))[None, :]
    dt_cols = jax.nn.softplus(dt_raw)
    rate = jnp.pad(-jnp.exp(own_slice(rate_log, shard, heads, 0)), (0, padding))[:, None]
    d_out = dot32(cot_low, out_low, ((1,), (1,)))
    pre, mixed, states, sums = mixer_forward(
        shards, bounds, projected, dt_cols, d_out, taps_all, bias_all, rate, skip_wide, gain_own
    )
    r_out = lax.rsqrt(sums[0][:, None] + eps_norm)
    normed_out = (mixed * jax.nn.silu(projected[:, :inner]) * r_out * gain_own).astype(jnp.bfloat16)
    grad_out_part = dot32(normed_out, cot_low, ((0,), (0,)))
    grad_out = lax.psum_scatter(grad_out_part, "group", scatter_dimension=1, tiled=True)

    home = lax.all_to_all(to_sorted(normed_out).reshape(shards, rows, inner), "shard", 0, 0)
    home = home.transpose(1, 0, 2).reshape(rows, INNER)
    home = dot32(sort_mat, home, ((0,), (0,))).astype(jnp.bfloat16)
    block_out = tokens + dot32(home, out_full)

    d_cols, d_bc, d_dt, grads, rate_terms = mixer_backward(
        shards, bounds, pre, mixed, projected, d_out, sums, states, dt_cols, taps_v, rate, skip_wide, gain_own
    )
    d_dtraw = d_dt[:heads].T * jax.nn.sigmoid(dt_raw[:, :heads])
    grad_dtb = jnp.sum(d_dtraw, axis=0)
    grad_rate = jnp.sum(rate_terms[:heads], axis=1)
    grad_skip = jnp.sum(grads[6].reshape(heads, HDIM), axis=1)
    d_bc = d_bc.T
    _, pull_bc = jax.vjp(
        lambda c, t, b: convolve(c, seg_rows, t, b),
        own_slice(conv_bc, shard, shared, 1),
        own_slice(taps[:, INNER:], shard, shared, 1),
        own_slice(conv_bias[INNER:], shard, shared, 0),
    )
    d_conv_bc, grad_taps_bc, grad_bias_bc = pull_bc(d_bc)
    d_rest = jnp.concatenate([d_conv_bc, d_dtraw], axis=1).astype(jnp.bfloat16)
    d_project = jnp.concatenate([d_cols, d_rest], axis=1)
    in_own = jnp.concatenate(
        [
            in_low[:, : 2 * inner],
            own_slice(in_low[:, 2 * inner : 2 * inner + SHARED], shard, shared, 1),
            in_low[:, 2 * inner + SHARED :],
        ],
        axis=1,
    )
    d_normed = dot32(to_sorted(d_project), in_own, ((1,), (1,)))
    grad_in = dot32(normed, d_project, ((0,), (0,)))
    mine = [
        grads[:CONV].reshape(-1),
        grad_taps_bc.reshape(-1),
        grads[4],
        grad_bias_bc,
        grad_dtb,
        grad_rate,
        grad_skip,
        grads[5],
    ]
    extents = [piece.shape[0] for piece in mine]
    mine = jnp.concatenate(mine)
    mine = jnp.pad(mine, (0, -mine.shape[0] % 1024)).reshape(-1, 128)
    x_scaled = (tokens * r_in).reshape(rows, shards, groups, part).transpose(0, 2, 1, 3).reshape(rows, width)
    x_scaled = jnp.dot(sort_mat.astype(jnp.float32), x_scaled, precision=lax.Precision.HIGHEST)
    d_normed, grad_in, small_all, gain_all = tail_exchange(
        shards,
        groups,
        d_normed.reshape(shards, rows, width),
        grad_in.reshape(groups, shards * part, -1),
        mine,
        x_scaled,
    )
    d_normed = jnp.dot(
        sort_mat.T.astype(jnp.float32), d_normed, precision=lax.Precision.HIGHEST
    )
    d_normed = d_normed.reshape(rows, groups, shards, part).transpose(0, 2, 1, 3).reshape(rows, width)
    d_scaled = pre_gain[None, :] * d_normed
    inside = jnp.mean(tokens * d_scaled, axis=1, keepdims=True)
    input_grad = cotangent + r_in * (d_scaled - tokens * (r_in * r_in) * inside)
    grad_pre = jnp.sum(gain_all, axis=0).reshape(groups, shards, part).transpose(1, 0, 2).reshape(width)


    def join(lo, each):
        return grad_in[:, :, lo : lo + each].transpose(1, 0, 2).reshape(part, shards * each)

    grad_in = jnp.concatenate(
        [
            join(0, inner),
            join(inner, inner),
            join(2 * inner, shared),
            join(2 * inner + shared, heads),
        ],
        axis=1,
    )
    grad_in = grad_in.reshape(part, groups, -1).transpose(1, 0, 2)
    grad_in = lax.all_to_all(grad_in, "group", 0, 0).reshape(in_weight.shape)

    mine = small_all.reshape(shards, -1)
    found, offset = [], 0
    for extent in extents:
        found.append(mine[:, offset : offset + extent])
        offset = offset + extent

    def taps_of(piece):
        return piece.reshape(shards, CONV, -1).transpose(1, 0, 2).reshape(CONV, -1)

    grad_taps = jnp.concatenate([taps_of(found[0]), taps_of(found[1])], axis=1).reshape(-1)
    grad_small = jnp.concatenate(
        [grad_taps] + [piece.reshape(-1) for piece in found[2:]]
        + [grad_pre]
    )
    in_new = nesterov(in_weight, grad_in, in_moment, in_average, rate_in)
    out_new = nesterov(out_weight, grad_out, out_moment, out_average, rate_out)
    small_new = nesterov(small_params, grad_small, small_moment, small_average, rate_small)
    return (block_out, input_grad) + in_new + out_new + small_new


def solution(mesh):
    rows = P(("group", "shard"), None)
    tile = P("shard", "group")
    return jax.shard_map(
        local,
        mesh=mesh,
        in_specs=(
            rows,
            rows,
            P("group", None),
            P(("group", "shard")),
            tile,
            tile,
            P(),
            tile,
            tile,
            P(),
            tile,
            tile,
            P(),
        ),
        out_specs=(rows, rows, tile, tile, tile, tile, tile, tile, P(), P(), P()),
        check_vma=False,
    )
```

```python
import functools

import jax
import jax.numpy as jnp
from jax import lax
from jax.experimental import pallas as pl
from jax.experimental.pallas import tpu as pltpu
from jax.sharding import PartitionSpec as P

D = 2048
HEADS = 64
HDIM = 64
STATE = 128
CONV = 4
BLOCK = 256
INNER = 4096
XBC = 4352
SHARED = 2 * STATE
TAIL = 8
CHUNK = 16
MESH = pl.DeviceIdType.MESH


eps_norm = 1e-05
momentum_decay = 0.9
weight_decay = 0.01
average_decay = 0.99
rate_in = 0.0001
rate_out = 3e-05
rate_small = 0.001


def unpack(packed_small):
    extents = [CONV * XBC, XBC, HEADS, HEADS, HEADS, INNER, D]
    pieces = []
    offset = 0
    for extent in extents:
        pieces.append(packed_small[offset : offset + extent])
        offset = offset + extent
    return pieces


def segment_of(positions, lengths_row):
    bounds = jnp.cumsum(lengths_row)[:-1]
    inside = jnp.sum((positions[:, None] >= bounds[None, :]).astype(jnp.int32), axis=1)
    return jnp.where(positions < 0, -1, inside)


def convolve(conv_rows, seg_rows, conv_taps, conv_bias):
    row_count, width = conv_rows.shape
    extended = jnp.concatenate([jnp.zeros((CONV - 1, width), conv_rows.dtype), conv_rows], axis=0)
    seg_ext = jnp.concatenate([jnp.full((CONV - 1,), -1, jnp.int32), seg_rows], axis=0)
    conv_sum = jnp.zeros_like(conv_rows) + conv_bias[None, :]
    for tap_index in range(CONV):
        same_seq = (seg_ext[tap_index : tap_index + row_count] == seg_rows)[:, None]
        conv_sum = conv_sum + jnp.where(
            same_seq,
            extended[tap_index : tap_index + row_count] * conv_taps[tap_index][None, :],
            0.0,
        )
    return jax.nn.silu(conv_sum)


def split(value):
    high = value.astype(jnp.bfloat16)
    return high, (value - high.astype(jnp.float32)).astype(jnp.bfloat16)


def dots(a, b, contract):
    return lax.dot_general(a, b, (contract, ((), ())), preferred_element_type=jnp.float32)


def dot3(a, b, contract=((1,), (0,))):
    a = a if isinstance(a, tuple) else split(a)
    b = b if isinstance(b, tuple) else split(b)
    return dots(a[0], b[0], contract) + (dots(a[0], b[1], contract) + dots(a[1], b[0], contract))


NT = ((1,), (1,))


def head_sums(value, marks):
    high = value.astype(jnp.bfloat16)
    rest = value - high.astype(jnp.float32)
    mid = rest.astype(jnp.bfloat16)
    low = (rest - mid.astype(jnp.float32)).astype(jnp.bfloat16)
    return dots(marks, high, NT) + (dots(marks, mid, NT) + dots(marks, low, NT))


def widen(columns, heads):
    rows = columns.shape[0]
    low_half = lax.broadcasted_iota(jnp.int32, (rows, 2 * HDIM), 1) < HDIM
    return jnp.concatenate(
        [
            jnp.where(low_half, columns[:, h : h + 1], columns[:, h + 1 : h + 2])
            for h in range(0, heads, 2)
        ],
        axis=1,
    )


def running_sum(value, reverse=False):
    lane = lax.broadcasted_iota(jnp.int32, value.shape, 1)
    count = value.shape[1]
    step = 1
    while step < count:
        if reverse:
            value = value + jnp.where(lane < count - step, pltpu.roll(value, count - step, 1), 0.0)
        else:
            value = value + jnp.where(lane >= step, pltpu.roll(value, step, 1), 0.0)
        step *= 2
    return value


def sequence_of(positions, bounds):
    inside = jnp.where(positions >= bounds[0], 1, 0) + jnp.where(positions >= bounds[1], 1, 0)
    return jnp.where(positions < 0, -1, inside)


def block_facts(block, bounds, dt_t, rate):
    start = block * BLOCK
    seg_col = sequence_of(start + lax.broadcasted_iota(jnp.int32, (BLOCK, 1), 0), bounds)
    seg_row = sequence_of(start + lax.broadcasted_iota(jnp.int32, (1, BLOCK), 1), bounds)
    before = sequence_of(start - 1 + lax.broadcasted_iota(jnp.int32, (1, 1), 1), bounds)
    last = sequence_of(start + BLOCK - 1 + lax.broadcasted_iota(jnp.int32, (1, 1), 1), bounds)
    run_t = running_sum(dt_t * rate)
    run = run_t.T
    final = run[BLOCK - 1 :, :]
    carried = jnp.where(seg_col == before, jnp.exp(run), 0.0)
    tail = jnp.where(seg_col == last, jnp.exp(final - run), 0.0)
    keep = jnp.where(last == before, jnp.exp(final), 0.0)
    return seg_col, seg_row, run_t, run, carried, tail, keep


def barrier_with(peers):
    barrier = pltpu.get_barrier_semaphore()
    for peer in peers:
        pl.semaphore_signal(barrier, inc=1, device_id=peer, device_id_type=MESH)
    pl.semaphore_wait(barrier, len(peers))


def remote(src, dst, sends, recvs, **where):
    return pltpu.make_async_remote_copy(
        src_ref=src, dst_ref=dst, send_sem=sends, recv_sem=recvs, device_id=where, device_id_type=MESH
    )


def forward_kernel(
    heads, shards, bounds, gate, conv_v, conv_bc, dt_cols, d_out, taps, bias, rate, skip, gain,
    pre_out, mixed_out, state_out, sums_out, ext, state, own_sums, sums_in, sums_send, sums_recv,
):
    block = pl.program_id(0)
    inner = heads * HDIM
    shard = lax.axis_index("shard")

    @pl.when(block == 0)
    def _():
        barrier_with([{"shard": (shard + step) % shards} for step in range(1, shards)])
        ext[:TAIL, :] = jnp.zeros((TAIL, ext.shape[1]), jnp.float32)
        state[...] = jnp.zeros_like(state)

    bounds = (bounds[0], bounds[1])
    dt = dt_cols[...]
    dt_t = dt.T[: rate.shape[0], :]
    seg_col, seg_row, run_t, run, carried, tail, keep = block_facts(block, bounds, dt_t, rate[...])
    ext[TAIL:, :inner] = conv_v[...]
    ext[TAIL:, inner:] = conv_bc[...]
    place = block * BLOCK + lax.broadcasted_iota(jnp.int32, (BLOCK, 1), 0)
    pre = bias[...] + taps[CONV - 1 : CONV, :] * ext[TAIL:, :]
    for back in range(1, CONV):
        same = sequence_of(place - back, bounds) == seg_col
        moved = ext[TAIL - back : TAIL - back + BLOCK, :]
        pre = pre + jnp.where(same, moved, 0.0) * taps[CONV - 1 - back : CONV - back, :]
    ext[:TAIL, :] = ext[BLOCK:, :]
    pre_out[...] = pre
    conv = pre / (1.0 + jnp.exp(-pre))
    values, b_rows, c_rows = conv[:, :inner], conv[:, inner : inner + STATE], conv[:, inner + STATE :]
    fed = values * widen(dt, heads)
    rows = lax.broadcasted_iota(jnp.int32, (BLOCK, BLOCK), 0)
    cols = lax.broadcasted_iota(jnp.int32, (BLOCK, BLOCK), 1)
    allowed = (seg_col == seg_row) & (rows >= cols)
    b_parts, c_parts = split(b_rows), split(c_rows)
    scores = jnp.where(allowed, dot3(c_parts, b_parts, NT), 0.0)
    old = state[...]
    state_out[0] = old
    output = widen(carried, heads) * dot3(c_parts, old)
    low_half = lax.broadcasted_iota(jnp.int32, (BLOCK, 2 * HDIM), 1) < HDIM
    inside = []
    for h in range(0, heads, 2):
        pair = split(fed[:, h * HDIM : (h + 2) * HDIM])
        found = []
        for k in (h, h + 1):
            mixing = jnp.exp(jnp.minimum(run[:, k : k + 1] - run_t[k : k + 1, :], 0.0)) * scores
            found.append(dot3(mixing, pair))
        inside.append(jnp.where(low_half, found[0], found[1]))
    mixed = output + jnp.concatenate(inside, axis=1) + skip[...] * values
    mixed_out[...] = mixed
    state[...] = widen(keep, heads) * old + dot3(b_rows.T, widen(tail, heads) * fed)
    gated = mixed * (gate[...] / (1.0 + jnp.exp(-gate[...])))
    squares = jnp.sum(gated * gated, axis=1, keepdims=True)
    products = jnp.sum(gated * gain[...] * d_out[...], axis=1, keepdims=True)
    lane = lax.broadcasted_iota(jnp.int32, (BLOCK, 128), 1)
    both = jnp.where(lane == 0, squares, jnp.where(lane == 1, products, 0.0))
    here = pl.ds(pl.multiple_of(block * BLOCK, BLOCK), BLOCK)
    own_sums[:, here] = both.T[:8, :]

    def push(step, at):
        return remote(
            own_sums.at[:, at], sums_in.at[step - 1, :, at], sums_send.at[step], sums_recv.at[step],
            shard=(shard + step) % shards,
        )

    for step in range(1, shards):
        push(step, here).start()

    @pl.when(block == pl.num_programs(0) - 1)
    def _():
        everything = pl.ds(0, own_sums.shape[1])
        for step in range(1, shards):
            push(step, everything).wait()
        found = own_sums[...]
        for step in range(1, shards):
            found = found + sums_in[step - 1]
        sums_out[...] = found * (1.0 / INNER)


def backward_kernel(
    heads, blocks, shards, bounds, pre, mixed, gate, d_out, conv_v, sums, state_in, dt_cols, taps, rate, skip, gain, marks,
    d_cols, d_bc, d_dt, grads, grad_rate, ext, carry, bc_rows, bc_in, bc_send, bc_recv,
):
    step = pl.program_id(0)
    block = blocks - 1 - step
    inner = heads * HDIM
    shard = lax.axis_index("shard")
    shared = SHARED // shards

    @pl.when(step == 0)
    def _():
        barrier_with([{"shard": (shard + turn) % shards} for turn in range(1, shards)])
        ext[BLOCK:, :] = jnp.zeros((TAIL, ext.shape[1]), jnp.float32)
        carry[...] = jnp.zeros_like(carry)
        grads[...] = jnp.zeros_like(grads)
        grad_rate[...] = jnp.zeros_like(grad_rate)

    bounds = (bounds[0], bounds[1])
    dt = dt_cols[...]
    dt_t = dt.T[: rate.shape[0], :]
    seg_col, seg_row, run_t, run, carried, tail, keep = block_facts(block, bounds, dt_t, rate[...])
    sums_cols = sums[...].T
    r_out = lax.rsqrt(sums_cols[:, 0:1] + 1e-05)
    inside = sums_cols[:, 1:2]
    gate_now = gate[...]
    gate_sig = 1.0 / (1.0 + jnp.exp(-gate_now))
    act = gate_now * gate_sig
    mixed_now = mixed[...]
    gated = mixed_now * act
    d_out_now = d_out[...]
    d_gated = r_out * (gain[...] * d_out_now - gated * (r_out * r_out) * inside)
    dy = d_gated * act
    d_cols[:, :inner] = (d_gated * mixed_now * (gate_sig * (1.0 + gate_now * (1.0 - gate_sig)))).astype(jnp.bfloat16)
    grads[5:6, :] += jnp.sum(gated * r_out * d_out_now, axis=0, keepdims=True)
    pre_now = pre[...]
    sig = 1.0 / (1.0 + jnp.exp(-pre_now))
    conv = pre_now * sig
    values, b_rows, c_rows = conv[:, :inner], conv[:, inner : inner + STATE], conv[:, inner + STATE :]
    grads[6:7, :] += jnp.sum(dy * values, axis=0, keepdims=True)
    dt_wide = widen(dt, heads)
    fed = values * dt_wide
    old, after = state_in[0], carry[...]
    b_parts, c_parts, old_parts, after_parts = split(b_rows), split(c_rows), split(old), split(after)
    carried_wide, tail_wide, keep_wide = widen(carried, heads), widen(tail, heads), widen(keep, heads)
    rows = lax.broadcasted_iota(jnp.int32, (BLOCK, BLOCK), 0)
    cols = lax.broadcasted_iota(jnp.int32, (BLOCK, BLOCK), 1)
    allowed = (seg_col == seg_row) & (cols >= rows)
    scores_t = jnp.where(allowed, dot3(b_parts, c_parts, NT), 0.0)
    low_half = lax.broadcasted_iota(jnp.int32, (BLOCK, 2 * HDIM), 1) < HDIM
    d_scores_t = jnp.zeros((BLOCK, BLOCK), jnp.float32)
    d_fed, row_terms, col_terms = [], [], []
    for h in range(0, heads, 2):
        fed_pair = fed[:, h * HDIM : (h + 2) * HDIM]
        dy_pair = split(dy[:, h * HDIM : (h + 2) * HDIM])
        found = []
        for k in (h, h + 1):
            own = low_half if k == h else jnp.logical_not(low_half)
            d_mixing = dot3(jnp.where(own, fed_pair, 0.0), dy_pair, NT)
            decay = jnp.exp(jnp.minimum(run_t[k : k + 1, :] - run[:, k : k + 1], 0.0))
            mixing = decay * scores_t
            d_scores_t = d_scores_t + decay * d_mixing
            flow = mixing * d_mixing
            row_terms.append(jnp.sum(flow, axis=0, keepdims=True))
            col_terms.append(jnp.sum(flow, axis=1, keepdims=True))
            found.append(dot3(mixing, dy_pair))
        d_fed.append(jnp.where(low_half, found[0], found[1]))
    d_scores_t = split(jnp.where(allowed, d_scores_t, 0.0))
    fed_tail = fed * tail_wide
    dy_carried = dy * carried_wide
    d_fed_out = tail_wide * dot3(b_parts, after_parts)
    d_fed = jnp.concatenate(d_fed, axis=1) + d_fed_out
    dy_parts, tail_parts = split(dy_carried), split(fed_tail)
    here = pl.ds(pl.multiple_of(block * BLOCK, BLOCK), BLOCK)
    bc_rows[:STATE, here] = (dot3(d_scores_t, c_parts) + dot3(tail_parts, after_parts, NT)).T
    bc_rows[STATE:, here] = (dot3(d_scores_t, b_parts, ((0,), (0,))) + dot3(dy_parts, old_parts, NT)).T

    def push(turn, at):
        peer = (shard + turn) % shards
        rows_at = pl.ds(pl.multiple_of(peer * shared, shared), shared)
        return remote(
            bc_rows.at[rows_at, at], bc_in.at[turn - 1, :, at], bc_send.at[turn], bc_recv.at[turn], shard=peer
        )

    for turn in range(1, shards):
        push(turn, here).start()
    head_count = dt_t.shape[0]
    pad = [jnp.zeros((1, BLOCK), jnp.float32)] * (head_count - heads)
    pad_col = [jnp.zeros((BLOCK, 1), jnp.float32)] * (head_count - heads)
    d_run = jnp.concatenate(row_terms + pad, axis=0) - jnp.concatenate(col_terms + pad_col, axis=1).T
    d_run = d_run + head_sums(dy_carried * dot3(c_parts, old_parts), marks[...])
    leaving = head_sums(fed * d_fed_out, marks[...])
    kept = jnp.sum(old * after, axis=0, keepdims=True) * keep_wide
    kept = jnp.sum(marks[...].astype(jnp.float32) * kept, axis=1, keepdims=True)
    at_end = lax.broadcasted_iota(jnp.int32, (head_count, BLOCK), 1) == BLOCK - 1
    total = jnp.sum(leaving, axis=1, keepdims=True) + kept
    d_run = d_run - leaving + jnp.where(at_end, total, 0.0)
    d_log = running_sum(d_run, reverse=True)
    d_dt[...] = d_log * rate[...] + head_sums(values * d_fed, marks[...])
    grad_rate[...] += d_log * (dt_t * rate[...])
    carry[...] = keep_wide * after + dot3(c_rows.T, dy_parts)
    pre_v, sig_v = pre_now[:, :inner], sig[:, :inner]
    d_values = dt_wide * d_fed + skip[...] * dy
    d_pre = d_values * (sig_v * (1.0 + pre_v * (1.0 - sig_v)))
    ext[:BLOCK, :] = d_pre
    place = block * BLOCK + lax.broadcasted_iota(jnp.int32, (BLOCK, 1), 0)
    conv_in = conv_v[...]
    d_conv = taps[CONV - 1 : CONV, :] * d_pre
    grads[CONV - 1 : CONV, :] += jnp.sum(conv_in * d_pre, axis=0, keepdims=True)
    grads[CONV : CONV + 1, :] += jnp.sum(d_pre, axis=0, keepdims=True)
    for ahead in range(1, CONV):
        same = sequence_of(place + ahead, bounds) == seg_col
        moved = jnp.where(same, ext[ahead : ahead + BLOCK, :], 0.0)
        d_conv = d_conv + taps[CONV - 1 - ahead : CONV - ahead, :] * moved
        grads[CONV - 1 - ahead : CONV - ahead, :] += jnp.sum(conv_in * moved, axis=0, keepdims=True)
    ext[BLOCK:, :] = ext[:TAIL, :]
    d_cols[:, inner:] = d_conv.astype(jnp.bfloat16)

    @pl.when(step == blocks - 1)
    def _():
        everything = pl.ds(0, bc_rows.shape[1])
        for turn in range(1, shards):
            push(turn, everything).wait()
        found = bc_rows[pl.ds(pl.multiple_of(shard * shared, shared), shared), :]
        for turn in range(1, shards):
            found = found + bc_in[turn - 1]
        d_bc[...] = found


def whole(shape):
    return pl.BlockSpec(shape, lambda *_: (0,) * len(shape))


def mixer_forward(shards, bounds, projected, dt_cols, d_out, taps, bias, rate, skip, gain):
    total, inner = d_out.shape
    heads, blocks, padded = inner // HDIM, total // BLOCK, rate.shape[0]

    def block_of(width, column):
        return pl.BlockSpec((BLOCK, width), lambda i: (i, column))

    return pl.pallas_call(
        functools.partial(forward_kernel, heads, shards),
        grid_spec=pltpu.PrefetchScalarGridSpec(
            num_scalar_prefetch=0,
            grid=(blocks,),
            in_specs=[
                pl.BlockSpec(memory_space=pltpu.SMEM),
                block_of(inner, 0),
                block_of(inner, 1),
                block_of(SHARED, 2 * inner // SHARED),
                block_of(dt_cols.shape[1], 0),
                block_of(inner, 0),
                whole(taps.shape),
                whole(bias.shape),
                whole(rate.shape),
                whole(skip.shape),
                whole(gain.shape),
            ],
            out_specs=[
                block_of(inner + SHARED, 0),
                block_of(inner, 0),
                pl.BlockSpec((1, STATE, inner), lambda i: (i, 0, 0)),
                whole((8, total)),
            ],
            scratch_shapes=[
                pltpu.VMEM((BLOCK + TAIL, inner + SHARED), jnp.float32),
                pltpu.VMEM((STATE, inner), jnp.float32),
                pltpu.VMEM((8, total), jnp.float32),
                pltpu.VMEM((shards - 1, 8, total), jnp.float32),
                pltpu.SemaphoreType.DMA((shards,)),
                pltpu.SemaphoreType.DMA((shards,)),
            ],
        ),
        out_shape=[
            jax.ShapeDtypeStruct((total, inner + SHARED), jnp.float32),
            jax.ShapeDtypeStruct((total, inner), jnp.float32),
            jax.ShapeDtypeStruct((blocks, STATE, inner), jnp.float32),
            jax.ShapeDtypeStruct((8, total), jnp.float32),
        ],
        compiler_params=pltpu.CompilerParams(
            collective_id=2, has_side_effects=True, vmem_limit_bytes=56 * 1024 * 1024
        ),
        cost_estimate=pl.CostEstimate(flops=0, bytes_accessed=100_000_000, transcendentals=0),
        name="mixer_forward",
    )(bounds, projected, projected, projected, dt_cols, d_out, taps, bias, rate, skip, gain)


def mixer_backward(shards, bounds, pre, mixed, projected, d_out, sums, states, dt_cols, taps, rate, skip, gain):
    total, inner = d_out.shape
    heads, blocks, padded = inner // HDIM, total // BLOCK, rate.shape[0]
    shared = SHARED // shards
    marks = (jnp.arange(padded)[:, None] == jnp.arange(inner)[None, :] // HDIM).astype(jnp.bfloat16)

    def block_of(width, column):
        return pl.BlockSpec((BLOCK, width), lambda i: (blocks - 1 - i, column))

    return pl.pallas_call(
        functools.partial(backward_kernel, heads, blocks, shards),
        grid_spec=pltpu.PrefetchScalarGridSpec(
            num_scalar_prefetch=0,
            grid=(blocks,),
            in_specs=[
                pl.BlockSpec(memory_space=pltpu.SMEM),
                block_of(inner + SHARED, 0),
                block_of(inner, 0),
                block_of(inner, 0),
                block_of(inner, 0),
                block_of(inner, 1),
                pl.BlockSpec((8, BLOCK), lambda i: (0, blocks - 1 - i)),
                pl.BlockSpec((1, STATE, inner), lambda i: (blocks - 1 - i, 0, 0)),
                block_of(dt_cols.shape[1], 0),
                whole(taps.shape),
                whole(rate.shape),
                whole(skip.shape),
                whole(gain.shape),
                whole(marks.shape),
            ],
            out_specs=[
                block_of(2 * inner, 0),
                whole((shared, total)),
                pl.BlockSpec((padded, BLOCK), lambda i: (0, blocks - 1 - i)),
                whole((8, inner)),
                whole((padded, BLOCK)),
            ],
            scratch_shapes=[
                pltpu.VMEM((BLOCK + TAIL, inner), jnp.float32),
                pltpu.VMEM((STATE, inner), jnp.float32),
                pltpu.VMEM((SHARED, total), jnp.float32),
                pltpu.VMEM((shards - 1, shared, total), jnp.float32),
                pltpu.SemaphoreType.DMA((shards,)),
                pltpu.SemaphoreType.DMA((shards,)),
            ],
        ),
        out_shape=[
            jax.ShapeDtypeStruct((total, 2 * inner), jnp.bfloat16),
            jax.ShapeDtypeStruct((shared, total), jnp.float32),
            jax.ShapeDtypeStruct((padded, total), jnp.float32),
            jax.ShapeDtypeStruct((8, inner), jnp.float32),
            jax.ShapeDtypeStruct((padded, BLOCK), jnp.float32),
        ],
        compiler_params=pltpu.CompilerParams(
            collective_id=3, has_side_effects=True, vmem_limit_bytes=56 * 1024 * 1024
        ),
        cost_estimate=pl.CostEstimate(flops=0, bytes_accessed=180_000_000, transcendentals=0),
        name="mixer_backward",
    )(bounds, pre, mixed, projected, d_out, projected, sums, states, dt_cols, taps, rate, skip, gain, marks)


def piece_rows(shards, groups):
    chunks = (2 * INNER // shards + SHARED // shards) // CHUNK
    return -(-chunks // groups) * CHUNK


def grid_columns(shards):
    columns = 1
    while 2 * (2 * columns) * (2 * columns) <= shards:
        columns *= 2
    return columns if shards % columns == 0 else 1


def column_runs(shards, groups):
    inner, width = INNER // shards, (2 * INNER + SHARED + HEADS) // groups
    kept = 2 * inner + SHARED + HEADS
    quarter = kept // groups
    spans = []
    for shard in range(shards):
        spans.append((inner * shard, shard, 0, inner))
        spans.append((INNER + inner * shard, shard, inner, inner))
    spans.append((2 * INNER, None, 2 * inner, SHARED + HEADS))
    runs = []
    for column, shard, row, length in spans:
        while length > 0:
            step = min(length, width - column % width, quarter - row % quarter)
            runs.append((column // width, column % width, shard, row, step))
            column, row, length = column + step, row + step, length - step
    return runs


def front_kernel(
    shards, groups, columns,
    rows_own, weight_own, out_own, slot_own,
    rows_all, weight_all, out_all, slot_all,
    local_sem, rows_send, rows_recv, run_send, run_recv, share_send, share_recv, out_send, out_recv, slot_send, slot_recv,
):
    shard, group = lax.axis_index("shard"), lax.axis_index("group")
    lines, rows_y = shards // columns, groups // 2
    z, x = shard // columns, shard % columns
    y, core = group // 2, group % 2
    mate = y * 2 + 1 - core
    quarter = weight_all.shape[0] // groups
    depth = weight_own.shape[1]
    out_width = out_own.shape[1]
    everyone = []
    for step in range(1, shards * groups):
        other_shard = (shard + step % shards) % shards
        other_group = (group + step // shards) % groups
        everyone.append({"shard": other_shard, "group": other_group})
    barrier_with(everyone)

    def line_copy(source, way):
        at = source * columns + x
        peer = jnp.clip(z + 1 - 2 * way, 0, lines - 1) * columns + x
        return remote(rows_all.at[:, at], rows_all.at[:, at], rows_send.at[way, source], rows_recv.at[at], shard=peer)

    def wide_copy(source, hop):
        at = source * columns + x
        peer = z * columns + (x + hop) % columns
        return remote(rows_all.at[:, at], rows_all.at[:, at], rows_send.at[1 + hop, source], rows_recv.at[at], shard=peer)

    def pass_on(source, ways):
        for way in ways:
            @pl.when(z < lines - 1 if way == 0 else z > 0)
            def _():
                line_copy(source, way).start()

        for hop in range(1, columns):
            wide_copy(source, hop).start()

    own = pltpu.make_async_copy(rows_own, rows_all.at[:, shard], local_sem.at[0])
    own.start()
    own.wait()
    pass_on(z, (0, 1))

    def slot_copy(step):
        return remote(slot_own, slot_all.at[shard], slot_send.at[step], slot_recv.at[step], shard=(shard + step) % shards)

    for step in range(1, shards):
        slot_copy(step).start()
    slot_here = pltpu.make_async_copy(slot_own, slot_all.at[shard], local_sem.at[1])
    slot_here.start()

    runs = column_runs(shards, groups)
    lanes = pl.ds(pl.multiple_of(shard * depth, depth), depth)
    jobs = {owner: [] for owner in range(groups)}
    for owner, column, target, row, length in runs:
        for to in range(shards) if target is None else (target,):
            jobs[owner].append((column, to, row, length))

    def run_copy(number, column, to, row, length):
        return remote(
            weight_own.at[pl.ds(column, length)], weight_all.at[pl.ds(row, length), lanes],
            run_send.at[number], run_recv, shard=to, group=row // quarter,
        )

    def each_run(act):
        for owner in range(groups):
            @pl.when(group == owner)
            def _():
                for number, (column, to, row, length) in enumerate(jobs[owner]):
                    if row // quarter == owner:
                        here = shard == to
                        act(number, column, to, row, length, here)
                    else:
                        act(number, column, to, row, length, None)

    def start_run(number, column, to, row, length, here):
        if here is None:
            run_copy(number, column, to, row, length).start()
            return

        @pl.when(here)
        def _():
            pltpu.make_async_copy(weight_own.at[pl.ds(column, length)], weight_all.at[pl.ds(row, length), lanes], run_recv).start()

        @pl.when(jnp.logical_not(here))
        def _():
            run_copy(number, column, to, row, length).start()

    def end_run(number, column, to, row, length, here):
        if here is None:
            run_copy(number, column, to, row, length).wait_send()
            return

        @pl.when(jnp.logical_not(here))
        def _():
            run_copy(number, column, to, row, length).wait_send()

    each_run(start_run)

    def own_part(ref, part):
        if ref is out_all:
            return ref.at[:, pl.ds(pl.multiple_of(part * out_width, out_width), out_width)]
        return ref.at[pl.ds(pl.multiple_of(part * quarter, quarter), quarter)]

    def share(ref, part, sends, recvs, number, peer):
        return remote(own_part(ref, part), own_part(ref, part), sends.at[number], recvs.at[part], group=peer)

    def share_start(ref, sends, recvs):
        share(ref, group, sends, recvs, 0, mate).start()
        for step in range(1, rows_y):
            share(ref, group, sends, recvs, step, (y + step) % rows_y * 2 + core).start()

    def share_pass(ref, sends, recvs):
        for step in range(1, rows_y):
            part = (y + step) % rows_y * 2 + core
            share(ref, part, sends, recvs, step, part).wait_recv()
            share(ref, part, sends, recvs, rows_y - 1 + step, mate).start()

    def share_end(ref, sends, recvs):
        for turn in range(rows_y):
            part = turn * 2 + 1 - core
            share(ref, part, sends, recvs, 0, mate).wait_recv()
        for number in range(2 * rows_y - 1):
            share(ref, group, sends, recvs, number, mate).wait_send()

    out_here = pltpu.make_async_copy(out_own, own_part(out_all, group), local_sem.at[2])
    out_here.start()
    out_here.wait()
    share_start(out_all, out_send, out_recv)

    for step in range(1, lines):
        @pl.when(z - step >= 0)
        def _():
            line_copy(z - step, 0).wait_recv()
            pass_on(z - step, (0,))

        @pl.when(z + step < lines)
        def _():
            line_copy(z + step, 1).wait_recv()
            pass_on(z + step, (1,))

        if step == 1:
            share_pass(out_all, out_send, out_recv)
            kept = own_part(weight_all, group)
            pltpu.make_async_copy(kept, kept, run_recv).wait()
            share_start(weight_all, share_send, share_recv)
    share_pass(weight_all, share_send, share_recv)

    for step in range(1, columns):
        for source in range(lines):
            at = source * columns + (x + step) % columns
            remote(rows_all.at[:, at], rows_all.at[:, at], rows_send.at[1 + step, source], rows_recv.at[at], shard=z * columns + (x + step) % columns).wait_recv()
    share_end(out_all, out_send, out_recv)
    share_end(weight_all, share_send, share_recv)
    each_run(end_run)
    for step in range(1, shards):
        slot_copy(step).wait()
    slot_here.wait()
    for source in range(lines):
        for hop in range(1, columns):
            wide_copy(source, hop).wait_send()

        @pl.when((z < lines - 1) & (source <= z))
        def _():
            line_copy(source, 0).wait_send()

        @pl.when((z > 0) & (source >= z))
        def _():
            line_copy(source, 1).wait_send()


def front_exchange(shards, groups, rows_own, weight_own, out_own, slot_own):
    columns = grid_columns(shards)
    lines, rows_y = shards // columns, groups // 2
    blocks, per, width = rows_own.shape
    kept = 2 * INNER // shards + SHARED + HEADS
    any_space = pl.BlockSpec(memory_space=pl.ANY)
    dma = pltpu.SemaphoreType.DMA
    counts = {}
    for owner, _, target, _, _ in column_runs(shards, groups):
        counts[owner] = counts.get(owner, 0) + (shards if target is None else 1)
    return pl.pallas_call(
        functools.partial(front_kernel, shards, groups, columns),
        in_specs=[any_space] * 4,
        out_specs=[any_space] * 4,
        out_shape=[
            jax.ShapeDtypeStruct((blocks, shards, per, width), jnp.bfloat16),
            jax.ShapeDtypeStruct((kept, width), jnp.bfloat16),
            jax.ShapeDtypeStruct((out_own.shape[0], out_own.shape[1] * groups), jnp.bfloat16),
            jax.ShapeDtypeStruct((shards,) + slot_own.shape, slot_own.dtype),
        ],
        scratch_shapes=[
            dma((3,)),
            dma((1 + columns, lines)),
            dma((shards,)),
            dma((max(counts.values()),)),
            dma,
            dma((2 * rows_y - 1,)),
            dma((groups,)),
            dma((2 * rows_y - 1,)),
            dma((groups,)),
            dma((shards,)),
            dma((shards,)),
        ],
        compiler_params=pltpu.CompilerParams(collective_id=4, has_side_effects=True),
        cost_estimate=pl.CostEstimate(flops=0, bytes_accessed=300_000_000, transcendentals=0),
        name="front_exchange",
    )(rows_own, weight_own, out_own, slot_own)


def place_of_rows(slots):
    count = slots.shape[1]
    return (lax.broadcasted_iota(jnp.int32, (BLOCK, count), 0) == slots).astype(jnp.bfloat16)


def pack_kernel(slots, rows, weight, packed, product):
    value = rows[...].reshape(BLOCK, rows.shape[-1])
    value = dots(place_of_rows(slots[0]), value, ((1,), (0,))).astype(jnp.bfloat16)
    packed[...] = value
    product[...] = dots(value, weight[...], NT)


def pack_and_project(slots, rows, weight):
    blocks, width = slots.shape[0], rows.shape[-1]
    if rows.shape[0] == blocks and rows.ndim == 3:
        block_rows = pl.BlockSpec((1,) + rows.shape[1:], lambda i: (i, 0, 0))
    else:
        block_rows = pl.BlockSpec((rows.shape[0], 1) + rows.shape[2:], lambda i: (0, i, 0, 0))
    return pl.pallas_call(
        pack_kernel,
        grid=(blocks,),
        in_specs=[pl.BlockSpec((1, 1, BLOCK), lambda i: (i, 0, 0)), block_rows, whole(weight.shape)],
        out_specs=[
            pl.BlockSpec((BLOCK, width), lambda i: (i, 0)),
            pl.BlockSpec((BLOCK, weight.shape[0]), lambda i: (i, 0)),
        ],
        out_shape=[
            jax.ShapeDtypeStruct((blocks * BLOCK, width), jnp.bfloat16),
            jax.ShapeDtypeStruct((blocks * BLOCK, weight.shape[0]), jnp.float32),
        ],
        compiler_params=pltpu.CompilerParams(vmem_limit_bytes=48 * 1024 * 1024),
        cost_estimate=pl.CostEstimate(
            flops=2 * blocks * BLOCK * width * (weight.shape[0] + BLOCK),
            bytes_accessed=blocks * BLOCK * (width * 4 + weight.shape[0] * 4),
            transcendentals=0,
        ),
        name="pack_and_project",
    )(slots, rows, weight)


def unpack_kernel(slots, d_cols, d_rest, normed, weight, weight_rest, partial, grad):
    place = place_of_rows(slots[0])
    cols, rest = d_cols[...], d_rest[...]
    main = cols.shape[1]
    sorted_cols = dots(place, cols, ((0,), (0,))).astype(jnp.bfloat16)
    sorted_rest = dots(place, rest, ((0,), (0,))).astype(jnp.bfloat16)
    found = dots(sorted_cols, weight[...], ((1,), (0,))) + dots(sorted_rest, weight_rest[...], ((1,), (0,)))
    partial[...] = found.reshape(partial.shape)

    @pl.when(pl.program_id(0) == 0)
    def _():
        grad[...] = jnp.zeros_like(grad)

    grad[:main, :] += dots(cols, normed[...], ((0,), (0,)))
    grad[main:, :] += dots(rest, normed[...], ((0,), (0,)))


def project_back(slots, d_cols, d_rest, normed, weight, weight_rest, shards):
    blocks, width = slots.shape[0], normed.shape[1]
    per, main, rest = BLOCK // shards, d_cols.shape[1], d_rest.shape[1]

    def block_of(columns):
        return pl.BlockSpec((BLOCK, columns), lambda i: (i, 0))

    return pl.pallas_call(
        unpack_kernel,
        grid=(blocks,),
        in_specs=[
            pl.BlockSpec((1, 1, BLOCK), lambda i: (i, 0, 0)),
            block_of(main),
            block_of(rest),
            block_of(width),
            pl.BlockSpec((main, width), lambda i: (0, 0)),
            whole(weight_rest.shape),
        ],
        out_specs=[
            pl.BlockSpec((shards, 1, per, width), lambda i: (0, i, 0, 0)),
            whole((main + rest, width)),
        ],
        out_shape=[
            jax.ShapeDtypeStruct((shards, blocks, per, width), jnp.float32),
            jax.ShapeDtypeStruct((main + rest, width), jnp.float32),
        ],
        compiler_params=pltpu.CompilerParams(vmem_limit_bytes=60 * 1024 * 1024),
        name="project_back",
    )(slots, d_cols, d_rest, normed, weight, weight_rest)


def other_place(step, place, count):
    upwards = count - 1 - place
    low = jnp.where(step < upwards, count - 1 - step, step - upwards)
    high = jnp.where(step < place, step, count - 1 - (step - place))
    return jnp.where(2 * place < count, low, high)


def tail_kernel(
    shards, groups, columns, near, direct,
    partial, weight_part, small, scaled_rows,
    rows_out, weight_out, small_out, gain_out, core_in, row_in, small_in, gain_in,
    wide_in, wide_scale, line_in, line_scale,
    held, coded, scales, line_coded, line_scales, got, got_scale, marks, total, other, send_rows, small_sum, small_got,
    gain_sum,
    load_sem, wide_send, wide_recv, line_send, line_recv, core_send, core_recv, row_send, row_recv,
    deal_send, deal_recv, small_send, small_recv, gain_send, gain_recv,
):
    shard, group = lax.axis_index("shard"), lax.axis_index("group")
    lines = shards // columns
    rows_y = groups // 2
    z, x = shard // columns, shard % columns
    y, core = group // 2, group % 2
    count = held.shape[0]
    owned, depth = weight_out.shape
    piece, chunk = total.shape[0], CHUNK
    inner, shared = INNER // shards, SHARED // shards

    def load(src, dst):
        copy = pltpu.make_async_copy(src, dst, load_sem)
        copy.start()
        copy.wait()

    shard_peers = [(shard + step) % shards for step in range(1, shards)]
    group_peers = [(group + step) % groups for step in range(1, groups)]
    if direct:
        barrier_with(
            [
                {"shard": (shard + step % shards) % shards, "group": (group + step // shards) % groups}
                for step in range(1, shards * groups)
            ]
        )
    else:
        barrier_with([{"shard": peer} for peer in shard_peers] + [{"group": peer} for peer in group_peers])

    mate = y * 2 + 1 - core

    def core_copy(turn):
        return remote(piece_of(turn * 2 + 1 - core), core_in.at[turn], core_send.at[turn], core_recv.at[turn], group=mate)

    def piece_of(owner):
        return weight_part.at[pl.ds(pl.multiple_of(owner * piece, piece), piece)]

    for turn in range(rows_y if direct else 0):
        core_copy(turn).start()

    def small_copy(step):
        return remote(small, small_in.at[step - 1], small_send.at[step - 1], small_recv.at[step - 1], group=(group + step) % groups)

    for step in range(1, groups):
        small_copy(step).start()

    def code(coded_to, scales_to):
        @pl.loop(0, count // 32, unroll=2)
        def _(turn):
            rows = pl.ds(pl.multiple_of(turn * 32, 32), 32)
            value = held[rows, :]
            most = jnp.maximum(jnp.max(jnp.abs(value), axis=1, keepdims=True), 1e-30)
            coded_to[rows, :] = jnp.round(value * (32767.0 / most)).astype(jnp.int32).astype(jnp.int16)
            marks[rows, :] = jnp.broadcast_to(most * (1.0 / 32767.0), (32, 128))

        scales_to[...] = marks[...].T[:8, :]

    def add(coded_from, scales_from):
        if not near:
            load(coded_from, got)
            load(scales_from, got_scale)
            coded_from, scales_from = got, got_scale
        marks[...] = jnp.broadcast_to(scales_from[0:1, :], (128, count)).T

        @pl.loop(0, count // 32, unroll=2)
        def _(turn):
            rows = pl.ds(pl.multiple_of(turn * 32, 32), 32)
            held[rows, :] += coded_from[rows, :].astype(jnp.float32) * marks[rows, 0:1]

    def place_of(step):
        return other_place(step, z, lines) if step < lines - 1 else z

    def wide_copies(step, hop):
        at = (hop - 1) * lines + step
        peer = z * columns + (x + hop) % columns
        target = place_of(step)
        return (
            remote(coded.at[step], wide_in.at[hop - 1, target], wide_send.at[0, at], wide_recv.at[0, at], shard=peer),
            remote(scales.at[step], wide_scale.at[hop - 1, target], wide_send.at[1, at], wide_recv.at[1, at], shard=peer),
        )

    for hop in range(1, columns):
        for step in range(lines):
            if hop > 1:
                for copy in wide_copies(step, hop - 1):
                    copy.wait_send()
            load(partial.at[place_of(step) * columns + (x + hop) % columns], held)
            code(coded.at[step], scales.at[step])
            for copy in wide_copies(step, hop):
                copy.start()

    load(small, small_sum)
    for step in range(1, groups):
        small_copy(step).wait_recv()
        load(small_in.at[step - 1], small_got)
        small_sum[...] += small_got[...]

    def small_deal(step):
        return remote(small_sum, small_out.at[shard], small_send.at[groups + step], small_recv.at[groups + step], shard=(shard + step) % shards)

    for step in range(1, shards):
        small_deal(step).start()
    load(small_sum, small_out.at[shard])

    def row_copy(step):
        return remote(send_rows.at[step - 1], row_in.at[step - 1], row_send.at[step - 1], row_recv.at[step - 1], group=(y + step) % rows_y * 2 + core)

    def add_other():
        @pl.loop(0, piece // chunk)
        def _(turn):
            rows = pl.ds(pl.multiple_of(turn * chunk, chunk), chunk)
            total[rows, :] += other[rows, :]

    def core_sum(turn):
        load(piece_of(turn * 2 + core), total)
        load(core_in.at[turn], other)
        add_other()

    if direct:
        for turn in range(rows_y):
            core_copy(turn).wait_recv()
        for step in range(1, rows_y):
            core_sum((y + step) % rows_y)
            load(total, send_rows.at[step - 1])
            row_copy(step).start()
        core_sum(y)

    def line_copies(step):
        target = place_of(step)
        way = jnp.where(target > z, 0, 1)
        peer = jnp.where(target > z, z + 1, z - 1) * columns + x
        return (
            remote(line_coded.at[step], line_in.at[way, target], line_send.at[0, step], line_recv.at[0, way, target], shard=peer),
            remote(line_scales.at[step], line_scale.at[way, target], line_send.at[1, step], line_recv.at[1, way, target], shard=peer),
        )

    def take(way, target):
        source = jnp.where(way == 0, z - 1, z + 1)
        peer = jnp.clip(source, 0, lines - 1) * columns + x
        remote(line_coded.at[0], line_in.at[way, target], line_send.at[0, 0], line_recv.at[0, way, target], shard=peer).wait_recv()
        remote(line_scales.at[0], line_scale.at[way, target], line_send.at[1, 0], line_recv.at[1, way, target], shard=peer).wait_recv()
        add(line_in.at[way, target], line_scale.at[way, target])

    def gather_wide(step):
        target = place_of(step)
        load(partial.at[target * columns + x], held)
        for hop in range(1, columns):
            for copy in wide_copies(step, hop):
                copy.wait_recv()
            add(wide_in.at[hop - 1, target], wide_scale.at[hop - 1, target])

    def deal_copy(turn, step):
        first = group * piece + turn * chunk
        column = jnp.where(
            first < inner,
            inner * shard + first,
            jnp.where(first < 2 * inner, INNER + inner * shard + first - inner, 2 * INNER + shared * shard + first - 2 * inner),
        )
        owner = jnp.minimum(column // owned, groups - 1)
        peer = (shard + step) % shards
        source = total.at[
            pl.ds(pl.multiple_of(turn * chunk, chunk), chunk), pl.ds(pl.multiple_of(peer * depth, depth), depth)
        ]
        target = weight_out.at[pl.ds(pl.multiple_of(column - owner * owned, chunk), chunk)]
        real = first < 2 * inner + shared
        here = real & (owner == group) if step == 0 else None
        away = real & (owner != group) if step == 0 else real

        def near_copy():
            return pltpu.make_async_copy(source, target, deal_recv)

        def far():
            return remote(source, target, deal_send.at[turn, step], deal_recv, shard=peer, group=owner)

        return here, near_copy, away, far

    def deal():
        for step in range(1, rows_y):
            row_copy(step).wait_recv()
            load(row_in.at[step - 1], other)
            add_other()

        @pl.loop(0, piece // chunk)
        def _(turn):
            for step in range(shards):
                here, near_copy, away, far = deal_copy(turn, step)
                if here is not None:
                    pl.when(here)(lambda: near_copy().start())
                pl.when(away)(lambda: far().start())

    def deal_end():
        @pl.when(group == groups - 1)
        def _():
            most = weight_out.at[pl.ds(0, owned - HEADS)]
            pltpu.make_async_copy(most, most, deal_recv).wait()

        @pl.when(group < groups - 1)
        def _():
            pltpu.make_async_copy(weight_out, weight_out, deal_recv).wait()

        @pl.loop(0, piece // chunk)
        def _(turn):
            for step in range(shards):
                _, _, away, far = deal_copy(turn, step)
                pl.when(away)(lambda: far().wait_send())

    for step in range(lines - 1):
        if direct and step == lines - 2:
            deal()
        target = place_of(step)
        way = jnp.where(target > z, 0, 1)
        gather_wide(step)

        @pl.when(jnp.where(target > z, z > 0, z < lines - 1))
        def _():
            take(way, target)

        code(line_coded.at[step], line_scales.at[step])
        for copy in line_copies(step):
            copy.start()
    gather_wide(lines - 1)

    @pl.when(z > 0)
    def _():
        take(0, z)

    @pl.when(z < lines - 1)
    def _():
        take(1, z)

    rows_out[...] = held[...]
    gain_sum[...] = jnp.zeros_like(gain_sum)

    @pl.loop(0, count // 8)
    def _(turn):
        rows = pl.ds(pl.multiple_of(turn * 8, 8), 8)
        gain_sum[...] += held[rows, :] * scaled_rows[rows, :]

    def gain_copy(step):
        return remote(gain_sum, gain_in.at[step - 1], gain_send.at[step - 1], gain_recv.at[step - 1], shard=(shard + step) % shards)

    def gain_deal(step):
        at = shards - 1 + step - 1
        return remote(gain_out, gain_in.at[at], gain_send.at[at], gain_recv.at[at], group=(group + step) % groups)

    for step in range(1, shards):
        gain_copy(step).start()
    gain_out[...] = gain_sum[...]
    for step in range(1, shards):
        gain_copy(step).wait_recv()
        gain_out[...] += gain_in[step - 1]
    for step in range(1, groups):
        gain_deal(step).start()
    for step in range(1, groups):
        gain_deal(step).wait_recv()
    for step in range(1, groups):
        gain_deal(step).wait_send()
    for step in range(1, groups):
        gain_out[...] += gain_in[shards - 1 + step - 1]

    for step in range(1, shards):
        gain_copy(step).wait_send()
        small_deal(step).wait()
    for step in range(1, groups):
        small_copy(step).wait_send()
    if direct:
        deal_end()
        for step in range(1, rows_y):
            row_copy(step).wait_send()
        for turn in range(rows_y):
            core_copy(turn).wait_send()
    for step in range(lines):
        for copy in wide_copies(step, columns - 1) if columns > 1 else ():
            copy.wait_send()
    for step in range(lines - 1):
        for copy in line_copies(step):
            copy.wait_send()


def tail_exchange(shards, groups, partial, weight_part, small, scaled_rows, owned, depth, direct):
    columns = grid_columns(shards)
    lines, rows_y = shards // columns, groups // 2
    count, width = scaled_rows.shape
    piece = piece_rows(shards, groups) if direct else CHUNK
    small_shape = small.shape
    coded, scale = (count, width), (8, count)
    any_space, vmem = pl.BlockSpec(memory_space=pl.ANY), pl.BlockSpec(memory_space=pltpu.VMEM)
    f32, i16 = jnp.float32, jnp.int16
    slots = max(columns - 1, 1)
    dma = pltpu.SemaphoreType.DMA
    landing = [
        ((slots, lines) + coded, i16),
        ((slots, lines) + scale, f32),
        ((2, lines) + coded, i16),
        ((2, lines) + scale, f32),
    ]
    near = shards * count * width <= 1 << 22
    out = pl.pallas_call(
        functools.partial(tail_kernel, shards, groups, columns, near, direct),
        in_specs=[any_space, any_space, any_space, vmem],
        out_specs=[vmem, any_space, any_space, vmem] + [any_space] * 3 + [vmem] + ([] if near else [any_space] * 4),
        out_shape=[
            jax.ShapeDtypeStruct((count, width), f32),
            jax.ShapeDtypeStruct((owned, depth), f32),
            jax.ShapeDtypeStruct((shards,) + small_shape, f32),
            jax.ShapeDtypeStruct((8, width), f32),
            jax.ShapeDtypeStruct((rows_y, piece, width), f32),
            jax.ShapeDtypeStruct((max(rows_y - 1, 1), piece, width), f32),
            jax.ShapeDtypeStruct((max(groups - 1, 1),) + small_shape, f32),
            jax.ShapeDtypeStruct((shards - 1 + groups - 1, 8, width), f32),
        ]
        + ([] if near else [jax.ShapeDtypeStruct(*each) for each in landing]),
        scratch_shapes=([pltpu.VMEM(*each) for each in landing] if near else [])
        + [
            pltpu.VMEM((count, width), f32),
            pltpu.VMEM((lines,) + coded, i16),
            pltpu.VMEM((lines,) + scale, f32),
            pltpu.VMEM((lines,) + coded, i16),
            pltpu.VMEM((lines,) + scale, f32),
            pltpu.VMEM((16, 128) if near else coded, i16),
            pltpu.VMEM((8, 128) if near else scale, f32),
            pltpu.VMEM((count, 128), f32),
            pltpu.VMEM((piece, width), f32),
            pltpu.VMEM((piece, width), f32),
            pltpu.VMEM((max(rows_y - 1, 1), piece, width), f32),
            pltpu.VMEM(small_shape, f32),
            pltpu.VMEM(small_shape, f32),
            pltpu.VMEM((8, width), f32),
            dma,
            dma((2, slots * lines)),
            dma((2, slots * lines)),
            dma((2, lines)),
            dma((2, 2, lines)),
            dma((rows_y,)),
            dma((rows_y,)),
            dma((max(rows_y - 1, 1),)),
            dma((max(rows_y - 1, 1),)),
            dma((piece // CHUNK, shards)),
            dma,
            dma((groups + shards,)),
            dma((groups + shards,)),
            dma((shards + groups,)),
            dma((shards + groups,)),
        ],
        compiler_params=pltpu.CompilerParams(
            collective_id=1, has_side_effects=True, vmem_limit_bytes=60 * 1024 * 1024
        ),
        cost_estimate=pl.CostEstimate(flops=0, bytes_accessed=400_000_000, transcendentals=0),
        name="tail_exchange",
    )(partial, weight_part, small, scaled_rows)
    return out[:4]


def nesterov(weight, gradient, moment, average, step_rate):
    decayed = gradient + weight_decay * weight
    new_moment = momentum_decay * moment + decayed
    new_weight = weight - step_rate * (decayed + momentum_decay * new_moment)
    new_average = average_decay * average + (1.0 - average_decay) * new_weight
    return (new_moment, new_weight, new_average)


def dot32(a, b, contract=((1,), (0,))):
    return lax.dot_general(a, b, (contract, ((), ())), preferred_element_type=jnp.float32)


def own_slice(value, index, width, axis):
    return lax.dynamic_slice_in_dim(value, index * width, width, axis)


def local(
    tokens,
    cotangent,
    lengths,
    deal_slot,
    in_weight,
    out_weight,
    small_params,
    in_moment,
    out_moment,
    small_moment,
    in_average,
    out_average,
    small_average,
):
    shards, groups = lax.axis_size("shard"), lax.axis_size("group")
    shard, group = lax.axis_index("shard"), lax.axis_index("group")
    rows, width = tokens.shape
    per = rows // shards
    total = rows * shards
    blocks = total // BLOCK
    heads = HEADS // shards
    inner = INNER // shards
    shared = SHARED // shards
    conv_flat, conv_bias, dt_bias, rate_log, skip_gain, norm_gain, pre_gain = unpack(small_params)
    taps = conv_flat.reshape(CONV, XBC)

    cols, depth, sends = in_weight.shape[1], in_weight.shape[0], out_weight.shape[1]
    direct = cols % CHUNK == 0 and depth % 128 == 0 and sends % 128 == 0 and per % CHUNK == 0
    direct = direct and (2 * inner + SHARED + HEADS) % (groups * CHUNK) == 0 and shared % CHUNK == 0
    bounds = jnp.cumsum(lengths[0])[:-1].astype(jnp.int32)
    seg_rows = segment_of(jnp.arange(total, dtype=jnp.int32), lengths[0])

    rank = jnp.sum((deal_slot[None, :] < deal_slot[:, None]).astype(jnp.int32), axis=1)
    sort_mat = (rank[None, :] == jnp.arange(rows)[:, None]).astype(jnp.bfloat16)
    sorted_slot = jnp.sum(jnp.where(sort_mat > 0, deal_slot[None, :], 0), axis=1)
    r_in = lax.rsqrt(jnp.mean(tokens * tokens, axis=1, keepdims=True) + eps_norm)
    normed_low = (tokens * r_in * pre_gain[None, :]).astype(jnp.bfloat16)
    x_sorted = dot32(sort_mat, normed_low).astype(jnp.bfloat16).reshape(blocks, per, width)
    c_sorted = dot32(sort_mat, cotangent.astype(jnp.bfloat16)).astype(jnp.bfloat16)
    c_all = lax.all_gather(c_sorted, "shard").reshape(shards, blocks, per, width)
    in_turned = in_weight.astype(jnp.bfloat16).T
    out_cast = out_weight.astype(jnp.bfloat16)

    if direct:
        slot_own = jnp.pad(sorted_slot, (0, 1024 - rows)).reshape(8, 128)
        x_all, in_low, out_low, slot_all = front_exchange(shards, groups, x_sorted, in_turned, out_cast, slot_own)
        x_all = x_all.reshape(blocks, BLOCK, width)
        slot_all = slot_all.reshape(shards, -1)[:, :rows]
    else:
        x_all = lax.all_gather(x_sorted, "shard").transpose(1, 0, 2, 3).reshape(blocks, BLOCK, width)
        c_all = c_all.transpose(1, 0, 2, 3).reshape(blocks, BLOCK, width)
        slot_all = lax.all_gather(sorted_slot, "shard")
        part = depth // groups
        pieces = lax.all_to_all(in_turned.reshape(cols, groups, part), "group", 1, 0)
        pieces = pieces.reshape(groups * cols, part)

        def cut(lo, each):
            return pieces[lo : lo + each * shards].reshape(shards, each, part)

        spread = jnp.broadcast_to(pieces[None, 2 * INNER :], (shards, SHARED + HEADS, part))
        got = jnp.concatenate([cut(0, inner), cut(INNER, inner), spread], axis=1)
        got = lax.all_gather(lax.all_to_all(got, "shard", 0, 0), "group")
        in_low = got.transpose(2, 1, 0, 3).reshape(-1, width)
        out_low = lax.all_gather(out_cast, "group", axis=1, tiled=True)
    out_full = lax.all_gather(out_cast, "shard", axis=0, tiled=True)
    out_full = lax.all_gather(out_full, "group", axis=1, tiled=True)
    slot_blk = slot_all.reshape(shards, blocks, per).transpose(1, 0, 2).reshape(blocks, 1, BLOCK)
    slot_blk = slot_blk - jnp.arange(blocks, dtype=jnp.int32)[:, None, None] * BLOCK

    def to_sorted(value):
        place = (slot_blk == jnp.arange(BLOCK)[None, :, None]).astype(jnp.bfloat16)
        value = value.reshape(blocks, BLOCK, -1)
        value = jnp.einsum("bps,bpd->bsd", place, value, preferred_element_type=jnp.float32)
        value = value.astype(jnp.bfloat16).reshape(blocks, shards, per, -1).transpose(1, 0, 2, 3)
        return value.reshape(total, -1)

    normed, projected = pack_and_project(slot_blk, x_all, in_low)
    conv_bc = projected[:, 2 * inner : 2 * inner + SHARED]
    taps_v = own_slice(taps[:, :INNER], shard, inner, 1)
    taps_all = jnp.concatenate([taps_v, taps[:, INNER:]], axis=1)
    bias_all = jnp.concatenate([own_slice(conv_bias[:INNER], shard, inner, 0), conv_bias[INNER:]])[None, :]
    skip_wide = jnp.repeat(own_slice(skip_gain, shard, heads, 0), HDIM)[None, :]
    gain_own = own_slice(norm_gain, shard, inner, 0)[None, :]
    padding = max(TAIL - heads, 0)
    dt_raw = projected[:, 2 * inner + SHARED :] + dt_bias[None, :]
    dt_raw = jnp.pad(own_slice(dt_raw, shard, heads, 1), ((0, 0), (0, 128 - heads)))
    dt_cols = jax.nn.softplus(dt_raw)
    rate = jnp.pad(-jnp.exp(own_slice(rate_log, shard, heads, 0)), (0, padding))[:, None]
    cot_low, d_out = pack_and_project(slot_blk, c_all, out_low)
    pre, mixed, states, sums = mixer_forward(
        shards, bounds, projected, dt_cols, d_out, taps_all, bias_all, rate, skip_wide, gain_own
    )
    r_out = lax.rsqrt(sums[0][:, None] + eps_norm)
    normed_out = (mixed * jax.nn.silu(projected[:, :inner]) * r_out * gain_own).astype(jnp.bfloat16)
    grad_out = dot32(normed_out, cot_low, ((0,), (0,)))
    grad_out = lax.psum_scatter(grad_out, "group", scatter_dimension=1, tiled=True)

    home = lax.all_to_all(to_sorted(normed_out).reshape(shards, rows, inner), "shard", 0, 0)
    home = home.transpose(1, 0, 2).reshape(rows, INNER)
    home = dot32(sort_mat, home, ((0,), (0,))).astype(jnp.bfloat16)
    block_out = tokens + dot32(home, out_full)

    d_cols, d_bc, d_dt, grads, rate_terms = mixer_backward(
        shards, bounds, pre, mixed, projected, d_out, sums, states, dt_cols, taps_v, rate, skip_wide, gain_own
    )
    d_dtraw = d_dt[:heads].T * jax.nn.sigmoid(dt_raw[:, :heads])
    grad_dtb = jnp.sum(d_dtraw, axis=0)
    grad_rate = jnp.sum(rate_terms[:heads], axis=1)
    grad_skip = jnp.sum(grads[6].reshape(heads, HDIM), axis=1)
    _, pull_bc = jax.vjp(
        lambda c, t, b: convolve(c, seg_rows, t, b),
        own_slice(conv_bc, shard, shared, 1),
        own_slice(taps[:, INNER:], shard, shared, 1),
        own_slice(conv_bias[INNER:], shard, shared, 0),
    )
    d_conv_bc, grad_taps_bc, grad_bias_bc = pull_bc(d_bc.T)
    rest = 128 - shared - heads
    d_rest = jnp.concatenate([d_conv_bc, d_dtraw, jnp.zeros((total, rest), jnp.float32)], axis=1)
    in_rest = jnp.concatenate(
        [
            own_slice(in_low[2 * inner : 2 * inner + SHARED], shard, shared, 0),
            own_slice(in_low[2 * inner + SHARED :], shard, heads, 0),
            jnp.zeros((rest, width), jnp.bfloat16),
        ]
    )
    partial, weight_part = project_back(
        slot_blk, d_cols, d_rest.astype(jnp.bfloat16), normed, in_low, in_rest, shards
    )
    dt_part = weight_part[2 * inner + shared : 2 * inner + shared + heads]

    mine = [
        grads[:CONV].reshape(-1),
        grad_taps_bc.reshape(-1),
        grads[4],
        grad_bias_bc,
        grad_dtb,
        grad_rate,
        grad_skip,
        grads[5],
    ]
    if direct:
        mine.append(dt_part.reshape(-1))
    extents = [piece.shape[0] for piece in mine]
    mine = jnp.concatenate(mine)
    mine = jnp.pad(mine, (0, -mine.shape[0] % 1024)).reshape(-1, 128)
    x_scaled = jnp.dot(sort_mat.astype(jnp.float32), tokens * r_in, precision=lax.Precision.HIGHEST)
    d_normed, grad_in, small_all, gain_all = tail_exchange(
        shards, groups, partial.reshape(shards, rows, width), weight_part, mine, x_scaled, cols, depth, direct
    )
    d_normed = jnp.dot(sort_mat.T.astype(jnp.float32), d_normed, precision=lax.Precision.HIGHEST)
    d_scaled = pre_gain[None, :] * d_normed
    inside = jnp.mean(tokens * d_scaled, axis=1, keepdims=True)
    input_grad = cotangent + r_in * (d_scaled - tokens * (r_in * r_in) * inside)
    grad_pre = jnp.sum(gain_all, axis=0)

    mine = small_all.reshape(shards, -1)
    found, offset = [], 0
    for extent in extents:
        found.append(mine[:, offset : offset + extent])
        offset = offset + extent
    if direct:
        dt_part = own_slice(found.pop().reshape(HEADS, width), shard, depth, 1)
        last = jnp.concatenate([grad_in[: cols - HEADS], dt_part])
        grad_in = jnp.where(group == groups - 1, last, grad_in)
    else:
        used = 2 * inner + shared + heads
        grad_in = weight_part[:used].reshape(used, shards, groups, part).transpose(2, 1, 0, 3)
        grad_in = lax.psum_scatter(grad_in, "group", scatter_dimension=0)
        grad_in = lax.all_to_all(grad_in, "shard", 0, 0)

        def join(lo, each):
            return grad_in[:, lo : lo + each].reshape(shards * each, part)

        grad_in = jnp.concatenate(
            [
                join(0, inner),
                join(inner, inner),
                join(2 * inner, shared),
                join(2 * inner + shared, heads),
            ]
        )
        grad_in = lax.all_to_all(grad_in.reshape(groups, cols, part), "group", 0, 0)
        grad_in = grad_in.transpose(1, 0, 2).reshape(cols, depth)

    def taps_of(piece):
        return piece.reshape(shards, CONV, -1).transpose(1, 0, 2).reshape(CONV, -1)

    grad_taps = jnp.concatenate([taps_of(found[0]), taps_of(found[1])], axis=1).reshape(-1)
    grad_small = jnp.concatenate([grad_taps] + [piece.reshape(-1) for piece in found[2:]] + [grad_pre])
    in_new = nesterov(in_weight.T, grad_in, in_moment.T, in_average.T, rate_in)
    in_new = tuple(value.T for value in in_new)
    out_new = nesterov(out_weight, grad_out, out_moment, out_average, rate_out)
    small_new = nesterov(small_params, grad_small, small_moment, small_average, rate_small)
    return (block_out, input_grad) + in_new + out_new + small_new


def solution(mesh):
    rows = P(("group", "shard"), None)
    tile = P("shard", "group")
    return jax.shard_map(
        local,
        mesh=mesh,
        in_specs=(
            rows,
            rows,
            P("group", None),
            P(("group", "shard")),
            tile,
            tile,
            P(),
            tile,
            tile,
            P(),
            tile,
            tile,
            P(),
        ),
        out_specs=(rows, rows, tile, tile, tile, tile, tile, tile, P(), P(), P()),
        check_vma=False,
    )
```

```python
import functools

import jax
import jax.numpy as jnp
from jax import lax
from jax.experimental import pallas as pl
from jax.experimental.pallas import tpu as pltpu
from jax.sharding import PartitionSpec as P

D = 2048
HEADS = 64
HDIM = 64
STATE = 128
CONV = 4
BLOCK = 256
INNER = 4096
XBC = 4352
SHARED = 2 * STATE
TAIL = 8
CHUNK = 16
MESH = pl.DeviceIdType.MESH


eps_norm = 1e-05
momentum_decay = 0.9
weight_decay = 0.01
average_decay = 0.99
rate_in = 0.0001
rate_out = 3e-05
rate_small = 0.001


def unpack(packed_small):
    extents = [CONV * XBC, XBC, HEADS, HEADS, HEADS, INNER, D]
    pieces = []
    offset = 0
    for extent in extents:
        pieces.append(packed_small[offset : offset + extent])
        offset = offset + extent
    return pieces


def segment_of(positions, lengths_row):
    bounds = jnp.cumsum(lengths_row)[:-1]
    inside = jnp.sum((positions[:, None] >= bounds[None, :]).astype(jnp.int32), axis=1)
    return jnp.where(positions < 0, -1, inside)


def convolve(conv_rows, seg_rows, conv_taps, conv_bias):
    row_count, width = conv_rows.shape
    extended = jnp.concatenate([jnp.zeros((CONV - 1, width), conv_rows.dtype), conv_rows], axis=0)
    seg_ext = jnp.concatenate([jnp.full((CONV - 1,), -1, jnp.int32), seg_rows], axis=0)
    conv_sum = jnp.zeros_like(conv_rows) + conv_bias[None, :]
    for tap_index in range(CONV):
        same_seq = (seg_ext[tap_index : tap_index + row_count] == seg_rows)[:, None]
        conv_sum = conv_sum + jnp.where(
            same_seq,
            extended[tap_index : tap_index + row_count] * conv_taps[tap_index][None, :],
            0.0,
        )
    return jax.nn.silu(conv_sum)


def split(value):
    high = value.astype(jnp.bfloat16)
    return high, (value - high.astype(jnp.float32)).astype(jnp.bfloat16)


def dots(a, b, contract):
    return lax.dot_general(a, b, (contract, ((), ())), preferred_element_type=jnp.float32)


def dot3(a, b, contract=((1,), (0,))):
    a = a if isinstance(a, tuple) else split(a)
    b = b if isinstance(b, tuple) else split(b)
    return dots(a[0], b[0], contract) + (dots(a[0], b[1], contract) + dots(a[1], b[0], contract))


NT = ((1,), (1,))


def head_sums(value, marks):
    high = value.astype(jnp.bfloat16)
    rest = value - high.astype(jnp.float32)
    mid = rest.astype(jnp.bfloat16)
    low = (rest - mid.astype(jnp.float32)).astype(jnp.bfloat16)
    return dots(marks, high, NT) + (dots(marks, mid, NT) + dots(marks, low, NT))


def widen(columns, heads):
    rows = columns.shape[0]
    low_half = lax.broadcasted_iota(jnp.int32, (rows, 2 * HDIM), 1) < HDIM
    return jnp.concatenate(
        [
            jnp.where(low_half, columns[:, h : h + 1], columns[:, h + 1 : h + 2])
            for h in range(0, heads, 2)
        ],
        axis=1,
    )


def running_sum(value, reverse=False):
    lane = lax.broadcasted_iota(jnp.int32, value.shape, 1)
    count = value.shape[1]
    step = 1
    while step < count:
        if reverse:
            value = value + jnp.where(lane < count - step, pltpu.roll(value, count - step, 1), 0.0)
        else:
            value = value + jnp.where(lane >= step, pltpu.roll(value, step, 1), 0.0)
        step *= 2
    return value


def sequence_of(positions, bounds):
    inside = jnp.where(positions >= bounds[0], 1, 0) + jnp.where(positions >= bounds[1], 1, 0)
    return jnp.where(positions < 0, -1, inside)


def block_facts(block, bounds, dt_t, rate):
    start = block * BLOCK
    seg_col = sequence_of(start + lax.broadcasted_iota(jnp.int32, (BLOCK, 1), 0), bounds)
    seg_row = sequence_of(start + lax.broadcasted_iota(jnp.int32, (1, BLOCK), 1), bounds)
    before = sequence_of(start - 1 + lax.broadcasted_iota(jnp.int32, (1, 1), 1), bounds)
    last = sequence_of(start + BLOCK - 1 + lax.broadcasted_iota(jnp.int32, (1, 1), 1), bounds)
    run_t = running_sum(dt_t * rate)
    run = run_t.T
    final = run[BLOCK - 1 :, :]
    carried = jnp.where(seg_col == before, jnp.exp(run), 0.0)
    tail = jnp.where(seg_col == last, jnp.exp(final - run), 0.0)
    keep = jnp.where(last == before, jnp.exp(final), 0.0)
    return seg_col, seg_row, run_t, run, carried, tail, keep


def barrier_with(peers):
    barrier = pltpu.get_barrier_semaphore()
    for peer in peers:
        pl.semaphore_signal(barrier, inc=1, device_id=peer, device_id_type=MESH)
    pl.semaphore_wait(barrier, len(peers))


def remote(src, dst, sends, recvs, **where):
    return pltpu.make_async_remote_copy(
        src_ref=src, dst_ref=dst, send_sem=sends, recv_sem=recvs, device_id=where, device_id_type=MESH
    )


def place_of_rows(slots):
    count = slots.shape[1]
    return (lax.broadcasted_iota(jnp.int32, (BLOCK, count), 0) == slots).astype(jnp.bfloat16)


def grid_columns(shards):
    columns = 1
    while 2 * (2 * columns) * (2 * columns) <= shards:
        columns *= 2
    return columns if shards % columns == 0 else 1


def whole(shape):
    return pl.BlockSpec(shape, lambda *_: (0,) * len(shape))


def row_gather(shards, columns, own, gathered, local_sem, sends, recvs):
    shard = lax.axis_index("shard")
    lines = shards // columns
    z, x = shard // columns, shard % columns

    def line_copy(source, way):
        at = source * columns + x
        peer = jnp.clip(z + 1 - 2 * way, 0, lines - 1) * columns + x
        return remote(gathered.at[:, at], gathered.at[:, at], sends.at[way, source], recvs.at[at], shard=peer)

    def wide_copy(source, hop):
        at = source * columns + x
        peer = z * columns + (x + hop) % columns
        return remote(gathered.at[:, at], gathered.at[:, at], sends.at[1 + hop, source], recvs.at[at], shard=peer)

    def pass_on(source, ways):
        for way in ways:
            @pl.when(z < lines - 1 if way == 0 else z > 0)
            def _():
                line_copy(source, way).start()

        for hop in range(1, columns):
            wide_copy(source, hop).start()

    def begin():
        copy = pltpu.make_async_copy(own, gathered.at[:, shard], local_sem)
        copy.start()
        copy.wait()
        pass_on(z, (0, 1))

    def hop(step):
        @pl.when(z - step >= 0)
        def _():
            line_copy(z - step, 0).wait_recv()
            pass_on(z - step, (0,))

        @pl.when(z + step < lines)
        def _():
            line_copy(z + step, 1).wait_recv()
            pass_on(z + step, (1,))

    def end():
        for step in range(1, columns):
            peer = z * columns + (x + step) % columns
            for source in range(lines):
                at = source * columns + (x + step) % columns
                remote(gathered.at[:, at], gathered.at[:, at], sends.at[1 + step, source], recvs.at[at], shard=peer).wait_recv()
        for source in range(lines):
            for step in range(1, columns):
                wide_copy(source, step).wait_send()

            @pl.when((z < lines - 1) & (source <= z))
            def _():
                line_copy(source, 0).wait_send()

            @pl.when((z > 0) & (source >= z))
            def _():
                line_copy(source, 1).wait_send()

    return begin, hop, end


def softplus(value):
    small = jnp.exp(-jnp.abs(value))
    ratio = small / (2.0 + small)
    square = ratio * ratio
    series = jnp.full_like(value, 1.0 / 15.0)
    for power in (13, 11, 9, 7, 5, 3, 1):
        series = series * square + 1.0 / power
    return jnp.maximum(value, 0.0) + 2.0 * ratio * series


def pick_columns(value, marks):
    high = value.astype(jnp.bfloat16)
    rest = value - high.astype(jnp.float32)
    mid = rest.astype(jnp.bfloat16)
    low = (rest - mid.astype(jnp.float32)).astype(jnp.bfloat16)
    plain = ((1,), (0,))
    return dots(high, marks, plain) + (dots(mid, marks, plain) + dots(low, marks, plain))


def forward_kernel(
    heads, shards, columns, bounds, slots, rows_in, weight, taps, bias, dt_bias, rate, skip, cot_own,
    packed, product, pre_out, mixed_out, state_out, dt_out, raw_out, cot_all,
    ext, state, local_sem, cot_send, cot_recv,
):
    block = pl.program_id(0)
    blocks = cot_own.shape[0]
    inner = heads * HDIM
    shard = lax.axis_index("shard")
    begin, hop, end = row_gather(shards, columns, cot_own, cot_all, local_sem, cot_send, cot_recv)
    hops = range(1, shards // columns)

    @pl.when(block == 0)
    def _():
        barrier_with([{"shard": (shard + step) % shards} for step in range(1, shards)])
        begin()
        ext[:TAIL, :] = jnp.zeros((TAIL, ext.shape[1]), jnp.float32)
        state[...] = jnp.zeros_like(state)

    for step in hops:
        if (7 * step + 1) // 2 < blocks:
            pl.when(block == (7 * step + 1) // 2)(functools.partial(hop, step))

    normed = dots(place_of_rows(slots[0]), rows_in[0], ((1,), (0,))).astype(jnp.bfloat16)
    packed[...] = normed
    product[...] = dots(normed, weight[...], NT)
    head = lax.broadcasted_iota(jnp.int32, (HEADS, 128), 0)
    lane = lax.broadcasted_iota(jnp.int32, (HEADS, 128), 1)
    marks = ((head == shard * heads + lane) & (lane < heads)).astype(jnp.bfloat16)
    raw = pick_columns(product[:, 2 * inner + SHARED :] + dt_bias[...], marks)
    raw_out[...] = raw
    dt = softplus(raw)
    dt_out[...] = dt

    bounds = (bounds[0], bounds[1])
    dt_t = dt.T[: rate.shape[0], :]
    seg_col, seg_row, run_t, run, carried, tail, keep = block_facts(block, bounds, dt_t, rate[...])
    ext[TAIL:, :] = product[:, inner : 2 * inner + SHARED]
    place = block * BLOCK + lax.broadcasted_iota(jnp.int32, (BLOCK, 1), 0)
    pre = bias[...] + taps[CONV - 1 : CONV, :] * ext[TAIL:, :]
    for back in range(1, CONV):
        same = sequence_of(place - back, bounds) == seg_col
        moved = ext[TAIL - back : TAIL - back + BLOCK, :]
        pre = pre + jnp.where(same, moved, 0.0) * taps[CONV - 1 - back : CONV - back, :]
    ext[:TAIL, :] = ext[BLOCK:, :]
    pre_out[...] = pre
    conv = pre / (1.0 + jnp.exp(-pre))
    values, b_rows, c_rows = conv[:, :inner], conv[:, inner : inner + STATE], conv[:, inner + STATE :]
    fed = values * widen(dt, heads)
    rows = lax.broadcasted_iota(jnp.int32, (BLOCK, BLOCK), 0)
    cols = lax.broadcasted_iota(jnp.int32, (BLOCK, BLOCK), 1)
    allowed = (seg_col == seg_row) & (rows >= cols)
    b_parts, c_parts = split(b_rows), split(c_rows)
    scores = jnp.where(allowed, dot3(c_parts, b_parts, NT), 0.0)
    old = state[...]
    state_out[0] = old
    output = widen(carried, heads) * dot3(c_parts, old)
    low_half = lax.broadcasted_iota(jnp.int32, (BLOCK, 2 * HDIM), 1) < HDIM
    inside = []
    for h in range(0, heads, 2):
        pair = split(fed[:, h * HDIM : (h + 2) * HDIM])
        found = []
        for k in (h, h + 1):
            mixing = jnp.exp(jnp.minimum(run[:, k : k + 1] - run_t[k : k + 1, :], 0.0)) * scores
            found.append(dot3(mixing, pair))
        inside.append(jnp.where(low_half, found[0], found[1]))
    mixed = output + jnp.concatenate(inside, axis=1) + skip[...] * values
    mixed_out[...] = mixed
    state[...] = widen(keep, heads) * old + dot3(b_rows.T, widen(tail, heads) * fed)

    @pl.when(block == blocks - 1)
    def _():
        for step in hops:
            if (7 * step + 1) // 2 >= blocks:
                hop(step)
        end()


def cotangent_kernel(
    shards, slots, rows_in, weight, mixed, gate, gain,
    packed, product, sums_out, own_sums, sums_in, sums_send, sums_recv,
):
    block = pl.program_id(0)
    shard = lax.axis_index("shard")

    @pl.when(block == 0)
    def _():
        barrier_with([{"shard": (shard + step) % shards} for step in range(1, shards)])

    cot = dots(place_of_rows(slots[0]), rows_in[0], ((1,), (0,))).astype(jnp.bfloat16)
    packed[...] = cot
    d_out = dots(cot, weight[...], NT)
    product[...] = d_out
    gate_now = gate[...]
    gated = mixed[...] * (gate_now / (1.0 + jnp.exp(-gate_now)))
    squares = jnp.sum(gated * gated, axis=1, keepdims=True)
    products = jnp.sum(gated * gain[...] * d_out, axis=1, keepdims=True)
    lane = lax.broadcasted_iota(jnp.int32, (BLOCK, 128), 1)
    both = jnp.where(lane == 0, squares, jnp.where(lane == 1, products, 0.0))
    here = pl.ds(pl.multiple_of(block * BLOCK, BLOCK), BLOCK)
    own_sums[:, here] = both.T[:8, :]

    def push(step, at):
        return remote(
            own_sums.at[:, at], sums_in.at[step - 1, :, at], sums_send.at[step], sums_recv.at[step],
            shard=(shard + step) % shards,
        )

    for step in range(1, shards):
        push(step, here).start()

    @pl.when(block == pl.num_programs(0) - 1)
    def _():
        everything = pl.ds(0, own_sums.shape[1])
        for step in range(1, shards):
            push(step, everything).wait()
        found = own_sums[...]
        for step in range(1, shards):
            found = found + sums_in[step - 1]
        sums_out[...] = found * (1.0 / INNER)


def backward_kernel(
    heads, blocks, shards, bounds, slots, pre, mixed, gate, d_out, conv_v, sums, state_in, dt_cols, cot,
    taps, rate, skip, gain, marks,
    d_cols, d_bc, d_dt, grads, grad_rate, grad_out, home,
    ext, carry, bc_rows, bc_in, no_rows, bc_send, bc_recv, no_send, no_recv, local_sem,
):
    step = pl.program_id(0)
    block = blocks - 1 - step
    inner = heads * HDIM
    shard = lax.axis_index("shard")
    shared = SHARED // shards

    @pl.when(step == 0)
    def _():
        barrier_with([{"shard": (shard + turn) % shards} for turn in range(1, shards)])
        ext[BLOCK:, :] = jnp.zeros((TAIL, ext.shape[1]), jnp.float32)
        carry[...] = jnp.zeros_like(carry)
        grads[...] = jnp.zeros_like(grads)
        grad_rate[...] = jnp.zeros_like(grad_rate)
        grad_out[...] = jnp.zeros_like(grad_out)

    bounds = (bounds[0], bounds[1])
    dt = dt_cols[...]
    dt_t = dt.T[: rate.shape[0], :]
    seg_col, seg_row, run_t, run, carried, tail, keep = block_facts(block, bounds, dt_t, rate[...])
    sums_cols = sums[...].T
    r_out = lax.rsqrt(sums_cols[:, 0:1] + 1e-05)
    inside = sums_cols[:, 1:2]
    gate_now = gate[...]
    gate_sig = 1.0 / (1.0 + jnp.exp(-gate_now))
    act = gate_now * gate_sig
    mixed_now = mixed[...]
    gated = mixed_now * act
    d_out_now = d_out[...]
    normed_out = (gated * r_out * gain[...]).astype(jnp.bfloat16)
    to_home = dots(place_of_rows(slots[0]), normed_out, ((0,), (0,)))
    per = BLOCK // shards
    if per % 16 == 0:
        no_rows[block] = to_home.astype(jnp.bfloat16).reshape(shards, per, inner)
    else:
        for turn in range(shards):
            no_rows[block, turn] = to_home[turn * per : (turn + 1) * per].astype(jnp.bfloat16)

    def push_home(turn, at):
        peer = (shard + turn) % shards
        return remote(
            no_rows.at[at, peer], home.at[shard, at], no_send.at[turn], no_recv.at[turn], shard=peer
        )

    for turn in range(1, shards):
        push_home(turn, pl.ds(block, 1)).start()
    grad_out[...] += dots(normed_out, cot[...], ((0,), (0,)))
    d_gated = r_out * (gain[...] * d_out_now - gated * (r_out * r_out) * inside)
    dy = d_gated * act
    d_cols[:, :inner] = (d_gated * mixed_now * (gate_sig * (1.0 + gate_now * (1.0 - gate_sig)))).astype(jnp.bfloat16)
    grads[5:6, :] += jnp.sum(gated * r_out * d_out_now, axis=0, keepdims=True)
    pre_now = pre[...]
    sig = 1.0 / (1.0 + jnp.exp(-pre_now))
    conv = pre_now * sig
    values, b_rows, c_rows = conv[:, :inner], conv[:, inner : inner + STATE], conv[:, inner + STATE :]
    grads[6:7, :] += jnp.sum(dy * values, axis=0, keepdims=True)
    dt_wide = widen(dt, heads)
    fed = values * dt_wide
    old, after = state_in[0], carry[...]
    b_parts, c_parts, old_parts, after_parts = split(b_rows), split(c_rows), split(old), split(after)
    carried_wide, tail_wide, keep_wide = widen(carried, heads), widen(tail, heads), widen(keep, heads)
    rows = lax.broadcasted_iota(jnp.int32, (BLOCK, BLOCK), 0)
    cols = lax.broadcasted_iota(jnp.int32, (BLOCK, BLOCK), 1)
    allowed = (seg_col == seg_row) & (cols >= rows)
    scores_t = jnp.where(allowed, dot3(b_parts, c_parts, NT), 0.0)
    low_half = lax.broadcasted_iota(jnp.int32, (BLOCK, 2 * HDIM), 1) < HDIM
    d_scores_t = jnp.zeros((BLOCK, BLOCK), jnp.float32)
    d_fed, row_terms, col_terms = [], [], []
    for h in range(0, heads, 2):
        fed_pair = fed[:, h * HDIM : (h + 2) * HDIM]
        dy_pair = split(dy[:, h * HDIM : (h + 2) * HDIM])
        found = []
        for k in (h, h + 1):
            own = low_half if k == h else jnp.logical_not(low_half)
            d_mixing = dot3(jnp.where(own, fed_pair, 0.0), dy_pair, NT)
            decay = jnp.exp(jnp.minimum(run_t[k : k + 1, :] - run[:, k : k + 1], 0.0))
            mixing = decay * scores_t
            d_scores_t = d_scores_t + decay * d_mixing
            flow = mixing * d_mixing
            row_terms.append(jnp.sum(flow, axis=0, keepdims=True))
            col_terms.append(jnp.sum(flow, axis=1, keepdims=True))
            found.append(dot3(mixing, dy_pair))
        d_fed.append(jnp.where(low_half, found[0], found[1]))
    d_scores_t = split(jnp.where(allowed, d_scores_t, 0.0))
    fed_tail = fed * tail_wide
    dy_carried = dy * carried_wide
    d_fed_out = tail_wide * dot3(b_parts, after_parts)
    d_fed = jnp.concatenate(d_fed, axis=1) + d_fed_out
    dy_parts, tail_parts = split(dy_carried), split(fed_tail)
    here = pl.ds(pl.multiple_of(block * BLOCK, BLOCK), BLOCK)
    bc_rows[:STATE, here] = (dot3(d_scores_t, c_parts) + dot3(tail_parts, after_parts, NT)).T
    bc_rows[STATE:, here] = (dot3(d_scores_t, b_parts, ((0,), (0,))) + dot3(dy_parts, old_parts, NT)).T

    def push(turn, at):
        peer = (shard + turn) % shards
        rows_at = pl.ds(pl.multiple_of(peer * shared, shared), shared)
        return remote(
            bc_rows.at[rows_at, at], bc_in.at[turn - 1, :, at], bc_send.at[turn], bc_recv.at[turn], shard=peer
        )

    for turn in range(1, shards):
        push(turn, here).start()
    head_count = dt_t.shape[0]
    pad = [jnp.zeros((1, BLOCK), jnp.float32)] * (head_count - heads)
    pad_col = [jnp.zeros((BLOCK, 1), jnp.float32)] * (head_count - heads)
    d_run = jnp.concatenate(row_terms + pad, axis=0) - jnp.concatenate(col_terms + pad_col, axis=1).T
    d_run = d_run + head_sums(dy_carried * dot3(c_parts, old_parts), marks[...])
    leaving = head_sums(fed * d_fed_out, marks[...])
    kept = jnp.sum(old * after, axis=0, keepdims=True) * keep_wide
    kept = jnp.sum(marks[...].astype(jnp.float32) * kept, axis=1, keepdims=True)
    at_end = lax.broadcasted_iota(jnp.int32, (head_count, BLOCK), 1) == BLOCK - 1
    total = jnp.sum(leaving, axis=1, keepdims=True) + kept
    d_run = d_run - leaving + jnp.where(at_end, total, 0.0)
    d_log = running_sum(d_run, reverse=True)
    d_dt[...] = d_log * rate[...] + head_sums(values * d_fed, marks[...])
    grad_rate[...] += d_log * (dt_t * rate[...])
    carry[...] = keep_wide * after + dot3(c_rows.T, dy_parts)
    pre_v, sig_v = pre_now[:, :inner], sig[:, :inner]
    d_values = dt_wide * d_fed + skip[...] * dy
    d_pre = d_values * (sig_v * (1.0 + pre_v * (1.0 - sig_v)))
    ext[:BLOCK, :] = d_pre
    place = block * BLOCK + lax.broadcasted_iota(jnp.int32, (BLOCK, 1), 0)
    conv_in = conv_v[...]
    d_conv = taps[CONV - 1 : CONV, :] * d_pre
    grads[CONV - 1 : CONV, :] += jnp.sum(conv_in * d_pre, axis=0, keepdims=True)
    grads[CONV : CONV + 1, :] += jnp.sum(d_pre, axis=0, keepdims=True)
    for ahead in range(1, CONV):
        same = sequence_of(place + ahead, bounds) == seg_col
        moved = jnp.where(same, ext[ahead : ahead + BLOCK, :], 0.0)
        d_conv = d_conv + taps[CONV - 1 - ahead : CONV - ahead, :] * moved
        grads[CONV - 1 - ahead : CONV - ahead, :] += jnp.sum(conv_in * moved, axis=0, keepdims=True)
    ext[BLOCK:, :] = ext[:TAIL, :]
    d_cols[:, inner:] = d_conv.astype(jnp.bfloat16)

    @pl.when(step == blocks - 1)
    def _():
        everything = pl.ds(0, bc_rows.shape[1])
        own = pltpu.make_async_copy(no_rows.at[:, shard], home.at[shard], local_sem)
        own.start()
        for turn in range(1, shards):
            push(turn, everything).wait()
            push_home(turn, pl.ds(0, blocks)).wait()
        own.wait()
        found = bc_rows[pl.ds(pl.multiple_of(shard * shared, shared), shared), :]
        for turn in range(1, shards):
            found = found + bc_in[turn - 1]
        d_bc[...] = found


def mixer_forward(shards, bounds, slots, rows_in, weight, taps, bias, dt_bias, rate, skip, cot_own):
    blocks, _, width = rows_in.shape
    columns = grid_columns(shards)
    total, inner, kept = blocks * BLOCK, INNER // shards, weight.shape[0]
    heads = inner // HDIM
    f32, bf16, any_space = jnp.float32, jnp.bfloat16, pl.BlockSpec(memory_space=pl.ANY)

    def block_of(lanes):
        return pl.BlockSpec((BLOCK, lanes), lambda i: (i, 0))

    return pl.pallas_call(
        functools.partial(forward_kernel, heads, shards, columns),
        grid=(blocks,),
        in_specs=[
            pl.BlockSpec(memory_space=pltpu.SMEM),
            pl.BlockSpec((1, 1, BLOCK), lambda i: (i, 0, 0)),
            pl.BlockSpec((1, BLOCK, width), lambda i: (i, 0, 0)),
            whole(weight.shape),
            whole(taps.shape),
            whole(bias.shape),
            whole(dt_bias.shape),
            whole(rate.shape),
            whole(skip.shape),
            any_space,
        ],
        out_specs=[
            block_of(width),
            block_of(kept),
            block_of(inner + SHARED),
            block_of(inner),
            pl.BlockSpec((1, STATE, inner), lambda i: (i, 0, 0)),
            block_of(128),
            block_of(128),
            any_space,
        ],
        out_shape=[
            jax.ShapeDtypeStruct((total, width), bf16),
            jax.ShapeDtypeStruct((total, kept), f32),
            jax.ShapeDtypeStruct((total, inner + SHARED), f32),
            jax.ShapeDtypeStruct((total, inner), f32),
            jax.ShapeDtypeStruct((blocks, STATE, inner), f32),
            jax.ShapeDtypeStruct((total, 128), f32),
            jax.ShapeDtypeStruct((total, 128), f32),
            jax.ShapeDtypeStruct((cot_own.shape[0], shards) + cot_own.shape[1:], bf16),
        ],
        scratch_shapes=[
            pltpu.VMEM((BLOCK + TAIL, inner + SHARED), f32),
            pltpu.VMEM((STATE, inner), f32),
            pltpu.SemaphoreType.DMA,
            pltpu.SemaphoreType.DMA((1 + columns, shards // columns)),
            pltpu.SemaphoreType.DMA((shards,)),
        ],
        compiler_params=pltpu.CompilerParams(
            collective_id=2, has_side_effects=True, vmem_limit_bytes=56 * 1024 * 1024
        ),
        cost_estimate=pl.CostEstimate(flops=0, bytes_accessed=300_000_000, transcendentals=0),
        name="mixer_forward",
    )(bounds, slots, rows_in, weight, taps, bias, dt_bias, rate, skip, cot_own)


def pack_cotangent(shards, slots, rows_in, weight, mixed, projected, gain):
    blocks, _, width = rows_in.shape
    total, inner = mixed.shape

    def block_of(lanes):
        return pl.BlockSpec((BLOCK, lanes), lambda i: (i, 0))

    return pl.pallas_call(
        functools.partial(cotangent_kernel, shards),
        grid=(blocks,),
        in_specs=[
            pl.BlockSpec((1, 1, BLOCK), lambda i: (i, 0, 0)),
            pl.BlockSpec((1, BLOCK, width), lambda i: (i, 0, 0)),
            whole(weight.shape),
            block_of(inner),
            block_of(inner),
            whole(gain.shape),
        ],
        out_specs=[block_of(width), block_of(inner), whole((8, total))],
        out_shape=[
            jax.ShapeDtypeStruct((total, width), jnp.bfloat16),
            jax.ShapeDtypeStruct((total, inner), jnp.float32),
            jax.ShapeDtypeStruct((8, total), jnp.float32),
        ],
        scratch_shapes=[
            pltpu.VMEM((8, total), jnp.float32),
            pltpu.VMEM((shards - 1, 8, total), jnp.float32),
            pltpu.SemaphoreType.DMA((shards,)),
            pltpu.SemaphoreType.DMA((shards,)),
        ],
        compiler_params=pltpu.CompilerParams(
            collective_id=5, has_side_effects=True, vmem_limit_bytes=48 * 1024 * 1024
        ),
        cost_estimate=pl.CostEstimate(flops=0, bytes_accessed=60_000_000, transcendentals=0),
        name="pack_cotangent",
    )(slots, rows_in, weight, mixed, projected, gain)


def mixer_backward(
    shards, bounds, slots, pre, mixed, projected, d_out, sums, states, dt_cols, cot, taps, rate, skip, gain
):
    total, inner = d_out.shape
    heads, blocks, padded = inner // HDIM, total // BLOCK, rate.shape[0]
    shared = SHARED // shards
    marks = (jnp.arange(padded)[:, None] == jnp.arange(inner)[None, :] // HDIM).astype(jnp.bfloat16)

    def block_of(width, column):
        return pl.BlockSpec((BLOCK, width), lambda i: (blocks - 1 - i, column))

    return pl.pallas_call(
        functools.partial(backward_kernel, heads, blocks, shards),
        grid_spec=pltpu.PrefetchScalarGridSpec(
            num_scalar_prefetch=0,
            grid=(blocks,),
            in_specs=[
                pl.BlockSpec(memory_space=pltpu.SMEM),
                pl.BlockSpec((1, 1, BLOCK), lambda i: (blocks - 1 - i, 0, 0)),
                block_of(inner + SHARED, 0),
                block_of(inner, 0),
                block_of(inner, 0),
                block_of(inner, 0),
                block_of(inner, 1),
                pl.BlockSpec((8, BLOCK), lambda i: (0, blocks - 1 - i)),
                pl.BlockSpec((1, STATE, inner), lambda i: (blocks - 1 - i, 0, 0)),
                block_of(dt_cols.shape[1], 0),
                block_of(cot.shape[1], 0),
                whole(taps.shape),
                whole(rate.shape),
                whole(skip.shape),
                whole(gain.shape),
                whole(marks.shape),
            ],
            out_specs=[
                block_of(2 * inner, 0),
                whole((shared, total)),
                pl.BlockSpec((padded, BLOCK), lambda i: (0, blocks - 1 - i)),
                whole((8, inner)),
                whole((padded, BLOCK)),
                whole((inner, cot.shape[1])),
                pl.BlockSpec(memory_space=pl.ANY),
            ],
            scratch_shapes=[
                pltpu.VMEM((BLOCK + TAIL, inner), jnp.float32),
                pltpu.VMEM((STATE, inner), jnp.float32),
                pltpu.VMEM((SHARED, total), jnp.float32),
                pltpu.VMEM((shards - 1, shared, total), jnp.float32),
                pltpu.VMEM((blocks, shards, BLOCK // shards, inner), jnp.bfloat16),
                pltpu.SemaphoreType.DMA((shards,)),
                pltpu.SemaphoreType.DMA((shards,)),
                pltpu.SemaphoreType.DMA((shards,)),
                pltpu.SemaphoreType.DMA((shards,)),
                pltpu.SemaphoreType.DMA,
            ],
        ),
        out_shape=[
            jax.ShapeDtypeStruct((total, 2 * inner), jnp.bfloat16),
            jax.ShapeDtypeStruct((shared, total), jnp.float32),
            jax.ShapeDtypeStruct((padded, total), jnp.float32),
            jax.ShapeDtypeStruct((8, inner), jnp.float32),
            jax.ShapeDtypeStruct((padded, BLOCK), jnp.float32),
            jax.ShapeDtypeStruct((inner, cot.shape[1]), jnp.float32),
            jax.ShapeDtypeStruct((shards, blocks, BLOCK // shards, inner), jnp.bfloat16),
        ],
        compiler_params=pltpu.CompilerParams(
            collective_id=3, has_side_effects=True, vmem_limit_bytes=56 * 1024 * 1024
        ),
        cost_estimate=pl.CostEstimate(flops=0, bytes_accessed=200_000_000, transcendentals=0),
        name="mixer_backward",
    )(bounds, slots, pre, mixed, projected, d_out, projected, sums, states, dt_cols, cot, taps, rate, skip, gain, marks)


def piece_rows(shards, groups):
    chunks = (2 * INNER // shards + SHARED // shards) // CHUNK
    return -(-chunks // groups) * CHUNK


def column_runs(shards, groups):
    inner, width = INNER // shards, (2 * INNER + SHARED + HEADS) // groups
    kept = 2 * inner + SHARED + HEADS
    quarter = kept // groups
    spans = []
    for shard in range(shards):
        spans.append((inner * shard, shard, 0, inner))
        spans.append((INNER + inner * shard, shard, inner, inner))
    spans.append((2 * INNER, None, 2 * inner, SHARED + HEADS))
    runs = []
    for column, shard, row, length in spans:
        while length > 0:
            step = min(length, width - column % width, quarter - row % quarter)
            runs.append((column // width, column % width, shard, row, step))
            column, row, length = column + step, row + step, length - step
    return runs


def front_kernel(
    shards, groups, columns,
    rows_own, weight_own, out_own, slot_own,
    rows_all, weight_all, out_all, slot_all,
    local_sem, rows_send, rows_recv, run_send, run_recv, share_send, share_recv, out_send, out_recv, slot_send, slot_recv,
):
    shard, group = lax.axis_index("shard"), lax.axis_index("group")
    lines, rows_y = shards // columns, groups // 2
    y, core = group // 2, group % 2
    mate = y * 2 + 1 - core
    quarter = weight_all.shape[0] // groups
    depth = weight_own.shape[1]
    out_width = out_own.shape[1]
    everyone = []
    for step in range(1, shards * groups):
        other_shard = (shard + step % shards) % shards
        other_group = (group + step // shards) % groups
        everyone.append({"shard": other_shard, "group": other_group})
    barrier_with(everyone)

    begin, hop, end = row_gather(shards, columns, rows_own, rows_all, local_sem.at[0], rows_send, rows_recv)
    begin()

    def slot_copy(step):
        return remote(slot_own, slot_all.at[shard], slot_send.at[step], slot_recv.at[step], shard=(shard + step) % shards)

    for step in range(1, shards):
        slot_copy(step).start()
    slot_here = pltpu.make_async_copy(slot_own, slot_all.at[shard], local_sem.at[1])
    slot_here.start()

    runs = column_runs(shards, groups)
    lanes = pl.ds(pl.multiple_of(shard * depth, depth), depth)
    jobs = {owner: [] for owner in range(groups)}
    for owner, column, target, row, length in runs:
        for to in range(shards) if target is None else (target,):
            jobs[owner].append((column, to, row, length))

    def run_copy(number, column, to, row, length):
        return remote(
            weight_own.at[pl.ds(column, length)], weight_all.at[pl.ds(row, length), lanes],
            run_send.at[number], run_recv, shard=to, group=row // quarter,
        )

    def each_run(act):
        for owner in range(groups):
            @pl.when(group == owner)
            def _():
                for number, (column, to, row, length) in enumerate(jobs[owner]):
                    if row // quarter == owner:
                        here = shard == to
                        act(number, column, to, row, length, here)
                    else:
                        act(number, column, to, row, length, None)

    def start_run(number, column, to, row, length, here):
        if here is None:
            run_copy(number, column, to, row, length).start()
            return

        @pl.when(here)
        def _():
            pltpu.make_async_copy(weight_own.at[pl.ds(column, length)], weight_all.at[pl.ds(row, length), lanes], run_recv).start()

        @pl.when(jnp.logical_not(here))
        def _():
            run_copy(number, column, to, row, length).start()

    def end_run(number, column, to, row, length, here):
        if here is None:
            run_copy(number, column, to, row, length).wait_send()
            return

        @pl.when(jnp.logical_not(here))
        def _():
            run_copy(number, column, to, row, length).wait_send()

    each_run(start_run)

    def own_part(ref, part):
        if ref is out_all:
            return ref.at[:, pl.ds(pl.multiple_of(part * out_width, out_width), out_width)]
        return ref.at[pl.ds(pl.multiple_of(part * quarter, quarter), quarter)]

    def share(ref, part, sends, recvs, number, peer):
        return remote(own_part(ref, part), own_part(ref, part), sends.at[number], recvs.at[part], group=peer)

    def share_start(ref, sends, recvs):
        share(ref, group, sends, recvs, 0, mate).start()
        for step in range(1, rows_y):
            share(ref, group, sends, recvs, step, (y + step) % rows_y * 2 + core).start()

    def share_pass(ref, sends, recvs):
        for step in range(1, rows_y):
            part = (y + step) % rows_y * 2 + core
            share(ref, part, sends, recvs, step, part).wait_recv()
            share(ref, part, sends, recvs, rows_y - 1 + step, mate).start()

    def share_end(ref, sends, recvs):
        for turn in range(rows_y):
            part = turn * 2 + 1 - core
            share(ref, part, sends, recvs, 0, mate).wait_recv()
        for number in range(2 * rows_y - 1):
            share(ref, group, sends, recvs, number, mate).wait_send()

    out_here = pltpu.make_async_copy(out_own, own_part(out_all, group), local_sem.at[2])
    out_here.start()
    out_here.wait()
    share_start(out_all, out_send, out_recv)

    for step in range(1, lines):
        hop(step)
        if step == 1:
            share_pass(out_all, out_send, out_recv)
            kept = own_part(weight_all, group)
            pltpu.make_async_copy(kept, kept, run_recv).wait()
            share_start(weight_all, share_send, share_recv)
    share_pass(weight_all, share_send, share_recv)

    end()
    share_end(out_all, out_send, out_recv)
    share_end(weight_all, share_send, share_recv)
    each_run(end_run)
    for step in range(1, shards):
        slot_copy(step).wait()
    slot_here.wait()


def front_exchange(shards, groups, rows_own, weight_own, out_own, slot_own):
    columns = grid_columns(shards)
    lines, rows_y = shards // columns, groups // 2
    blocks, per, width = rows_own.shape
    kept = 2 * INNER // shards + SHARED + HEADS
    any_space = pl.BlockSpec(memory_space=pl.ANY)
    dma = pltpu.SemaphoreType.DMA
    counts = {}
    for owner, _, target, _, _ in column_runs(shards, groups):
        counts[owner] = counts.get(owner, 0) + (shards if target is None else 1)
    return pl.pallas_call(
        functools.partial(front_kernel, shards, groups, columns),
        in_specs=[any_space] * 4,
        out_specs=[any_space] * 4,
        out_shape=[
            jax.ShapeDtypeStruct((blocks, shards, per, width), jnp.bfloat16),
            jax.ShapeDtypeStruct((kept, width), jnp.bfloat16),
            jax.ShapeDtypeStruct((out_own.shape[0], out_own.shape[1] * groups), jnp.bfloat16),
            jax.ShapeDtypeStruct((shards,) + slot_own.shape, slot_own.dtype),
        ],
        scratch_shapes=[
            dma((3,)),
            dma((1 + columns, lines)),
            dma((shards,)),
            dma((max(counts.values()),)),
            dma,
            dma((2 * rows_y - 1,)),
            dma((groups,)),
            dma((2 * rows_y - 1,)),
            dma((groups,)),
            dma((shards,)),
            dma((shards,)),
        ],
        compiler_params=pltpu.CompilerParams(collective_id=4, has_side_effects=True),
        cost_estimate=pl.CostEstimate(flops=0, bytes_accessed=300_000_000, transcendentals=0),
        name="front_exchange",
    )(rows_own, weight_own, out_own, slot_own)


def unpack_kernel(slots, d_cols, d_rest, normed, weight, weight_rest, partial, grad):
    place = place_of_rows(slots[0])
    cols, rest = d_cols[...], d_rest[...]
    main = cols.shape[1]
    sorted_cols = dots(place, cols, ((0,), (0,))).astype(jnp.bfloat16)
    sorted_rest = dots(place, rest, ((0,), (0,))).astype(jnp.bfloat16)
    found = dots(sorted_cols, weight[...], ((1,), (0,))) + dots(sorted_rest, weight_rest[...], ((1,), (0,)))
    partial[...] = found.reshape(partial.shape)

    @pl.when(pl.program_id(0) == 0)
    def _():
        grad[...] = jnp.zeros_like(grad)

    grad[:main, :] += dots(cols, normed[...], ((0,), (0,)))
    grad[main:, :] += dots(rest, normed[...], ((0,), (0,)))


def project_back(slots, d_cols, d_rest, normed, weight, weight_rest, shards):
    blocks, width = slots.shape[0], normed.shape[1]
    per, main, rest = BLOCK // shards, d_cols.shape[1], d_rest.shape[1]

    def block_of(columns):
        return pl.BlockSpec((BLOCK, columns), lambda i: (i, 0))

    return pl.pallas_call(
        unpack_kernel,
        grid=(blocks,),
        in_specs=[
            pl.BlockSpec((1, 1, BLOCK), lambda i: (i, 0, 0)),
            block_of(main),
            block_of(rest),
            block_of(width),
            pl.BlockSpec((main, width), lambda i: (0, 0)),
            whole(weight_rest.shape),
        ],
        out_specs=[
            pl.BlockSpec((shards, 1, per, width), lambda i: (0, i, 0, 0)),
            whole((main + rest, width)),
        ],
        out_shape=[
            jax.ShapeDtypeStruct((shards, blocks, per, width), jnp.float32),
            jax.ShapeDtypeStruct((main + rest, width), jnp.float32),
        ],
        compiler_params=pltpu.CompilerParams(vmem_limit_bytes=60 * 1024 * 1024),
        name="project_back",
    )(slots, d_cols, d_rest, normed, weight, weight_rest)


def other_place(step, place, count):
    upwards = count - 1 - place
    low = jnp.where(step < upwards, count - 1 - step, step - upwards)
    high = jnp.where(step < place, step, count - 1 - (step - place))
    return jnp.where(2 * place < count, low, high)


def tail_kernel(
    shards, groups, columns, near, direct,
    partial, weight_part, small, scaled_rows,
    rows_out, weight_out, small_out, gain_out, core_in, row_in, small_in, gain_in,
    wide_in, wide_scale, line_in, line_scale,
    held, coded, scales, line_coded, line_scales, got, got_scale, marks, total, other, send_rows, small_sum, small_got,
    gain_sum,
    load_sem, wide_send, wide_recv, line_send, line_recv, core_send, core_recv, row_send, row_recv,
    deal_send, deal_recv, small_send, small_recv, gain_send, gain_recv,
):
    shard, group = lax.axis_index("shard"), lax.axis_index("group")
    lines = shards // columns
    rows_y = groups // 2
    z, x = shard // columns, shard % columns
    y, core = group // 2, group % 2
    count = held.shape[0]
    owned, depth = weight_out.shape
    piece, chunk = total.shape[0], CHUNK
    inner, shared = INNER // shards, SHARED // shards

    def load(src, dst):
        copy = pltpu.make_async_copy(src, dst, load_sem)
        copy.start()
        copy.wait()

    shard_peers = [(shard + step) % shards for step in range(1, shards)]
    group_peers = [(group + step) % groups for step in range(1, groups)]
    if direct:
        barrier_with(
            [
                {"shard": (shard + step % shards) % shards, "group": (group + step // shards) % groups}
                for step in range(1, shards * groups)
            ]
        )
    else:
        barrier_with([{"shard": peer} for peer in shard_peers] + [{"group": peer} for peer in group_peers])

    mate = y * 2 + 1 - core

    def core_copy(turn):
        return remote(piece_of(turn * 2 + 1 - core), core_in.at[turn], core_send.at[turn], core_recv.at[turn], group=mate)

    def piece_of(owner):
        return weight_part.at[pl.ds(pl.multiple_of(owner * piece, piece), piece)]

    for turn in range(rows_y if direct else 0):
        core_copy(turn).start()

    def small_copy(step):
        return remote(small, small_in.at[step - 1], small_send.at[step - 1], small_recv.at[step - 1], group=(group + step) % groups)

    for step in range(1, groups):
        small_copy(step).start()

    def code(coded_to, scales_to):
        @pl.loop(0, count // 32, unroll=2)
        def _(turn):
            rows = pl.ds(pl.multiple_of(turn * 32, 32), 32)
            value = held[rows, :]
            most = jnp.maximum(jnp.max(jnp.abs(value), axis=1, keepdims=True), 1e-30)
            coded_to[rows, :] = jnp.round(value * (32767.0 / most)).astype(jnp.int32).astype(jnp.int16)
            marks[rows, :] = jnp.broadcast_to(most * (1.0 / 32767.0), (32, 128))

        scales_to[...] = marks[...].T[:8, :]

    def add(coded_from, scales_from):
        if not near:
            load(coded_from, got)
            load(scales_from, got_scale)
            coded_from, scales_from = got, got_scale
        marks[...] = jnp.broadcast_to(scales_from[0:1, :], (128, count)).T

        @pl.loop(0, count // 32, unroll=2)
        def _(turn):
            rows = pl.ds(pl.multiple_of(turn * 32, 32), 32)
            held[rows, :] += coded_from[rows, :].astype(jnp.float32) * marks[rows, 0:1]

    def place_of(step):
        return other_place(step, z, lines) if step < lines - 1 else z

    def wide_copies(step, hop):
        at = (hop - 1) * lines + step
        peer = z * columns + (x + hop) % columns
        target = place_of(step)
        return (
            remote(coded.at[step], wide_in.at[hop - 1, target], wide_send.at[0, at], wide_recv.at[0, at], shard=peer),
            remote(scales.at[step], wide_scale.at[hop - 1, target], wide_send.at[1, at], wide_recv.at[1, at], shard=peer),
        )

    for hop in range(1, columns):
        for step in range(lines):
            if hop > 1:
                for copy in wide_copies(step, hop - 1):
                    copy.wait_send()
            load(partial.at[place_of(step) * columns + (x + hop) % columns], held)
            code(coded.at[step], scales.at[step])
            for copy in wide_copies(step, hop):
                copy.start()

    load(small, small_sum)
    for step in range(1, groups):
        small_copy(step).wait_recv()
        load(small_in.at[step - 1], small_got)
        small_sum[...] += small_got[...]

    def small_deal(step):
        return remote(small_sum, small_out.at[shard], small_send.at[groups + step], small_recv.at[groups + step], shard=(shard + step) % shards)

    for step in range(1, shards):
        small_deal(step).start()
    load(small_sum, small_out.at[shard])

    def row_copy(step):
        return remote(send_rows.at[step - 1], row_in.at[step - 1], row_send.at[step - 1], row_recv.at[step - 1], group=(y + step) % rows_y * 2 + core)

    def add_other():
        @pl.loop(0, piece // chunk)
        def _(turn):
            rows = pl.ds(pl.multiple_of(turn * chunk, chunk), chunk)
            total[rows, :] += other[rows, :]

    def core_sum(turn):
        load(piece_of(turn * 2 + core), total)
        load(core_in.at[turn], other)
        add_other()

    if direct:
        for turn in range(rows_y):
            core_copy(turn).wait_recv()
        for step in range(1, rows_y):
            core_sum((y + step) % rows_y)
            load(total, send_rows.at[step - 1])
            row_copy(step).start()
        core_sum(y)

    def line_copies(step):
        target = place_of(step)
        way = jnp.where(target > z, 0, 1)
        peer = jnp.where(target > z, z + 1, z - 1) * columns + x
        return (
            remote(line_coded.at[step], line_in.at[way, target], line_send.at[0, step], line_recv.at[0, way, target], shard=peer),
            remote(line_scales.at[step], line_scale.at[way, target], line_send.at[1, step], line_recv.at[1, way, target], shard=peer),
        )

    def take(way, target):
        source = jnp.where(way == 0, z - 1, z + 1)
        peer = jnp.clip(source, 0, lines - 1) * columns + x
        remote(line_coded.at[0], line_in.at[way, target], line_send.at[0, 0], line_recv.at[0, way, target], shard=peer).wait_recv()
        remote(line_scales.at[0], line_scale.at[way, target], line_send.at[1, 0], line_recv.at[1, way, target], shard=peer).wait_recv()
        add(line_in.at[way, target], line_scale.at[way, target])

    def gather_wide(step):
        target = place_of(step)
        load(partial.at[target * columns + x], held)
        for hop in range(1, columns):
            for copy in wide_copies(step, hop):
                copy.wait_recv()
            add(wide_in.at[hop - 1, target], wide_scale.at[hop - 1, target])

    def deal_copy(turn, step):
        first = group * piece + turn * chunk
        column = jnp.where(
            first < inner,
            inner * shard + first,
            jnp.where(first < 2 * inner, INNER + inner * shard + first - inner, 2 * INNER + shared * shard + first - 2 * inner),
        )
        owner = jnp.minimum(column // owned, groups - 1)
        peer = (shard + step) % shards
        source = total.at[
            pl.ds(pl.multiple_of(turn * chunk, chunk), chunk), pl.ds(pl.multiple_of(peer * depth, depth), depth)
        ]
        target = weight_out.at[pl.ds(pl.multiple_of(column - owner * owned, chunk), chunk)]
        real = first < 2 * inner + shared
        here = real & (owner == group) if step == 0 else None
        away = real & (owner != group) if step == 0 else real

        def near_copy():
            return pltpu.make_async_copy(source, target, deal_recv)

        def far():
            return remote(source, target, deal_send.at[turn, step], deal_recv, shard=peer, group=owner)

        return here, near_copy, away, far

    def deal():
        for step in range(1, rows_y):
            row_copy(step).wait_recv()
            load(row_in.at[step - 1], other)
            add_other()

        @pl.loop(0, piece // chunk)
        def _(turn):
            for step in range(shards):
                here, near_copy, away, far = deal_copy(turn, step)
                if here is not None:
                    pl.when(here)(lambda: near_copy().start())
                pl.when(away)(lambda: far().start())

    def deal_end():
        @pl.when(group == groups - 1)
        def _():
            most = weight_out.at[pl.ds(0, owned - HEADS)]
            pltpu.make_async_copy(most, most, deal_recv).wait()

        @pl.when(group < groups - 1)
        def _():
            pltpu.make_async_copy(weight_out, weight_out, deal_recv).wait()

        @pl.loop(0, piece // chunk)
        def _(turn):
            for step in range(shards):
                _, _, away, far = deal_copy(turn, step)
                pl.when(away)(lambda: far().wait_send())

    for step in range(lines - 1):
        if direct and step == lines - 2:
            deal()
        target = place_of(step)
        way = jnp.where(target > z, 0, 1)
        gather_wide(step)

        @pl.when(jnp.where(target > z, z > 0, z < lines - 1))
        def _():
            take(way, target)

        code(line_coded.at[step], line_scales.at[step])
        for copy in line_copies(step):
            copy.start()
    gather_wide(lines - 1)

    @pl.when(z > 0)
    def _():
        take(0, z)

    @pl.when(z < lines - 1)
    def _():
        take(1, z)

    rows_out[...] = held[...]
    gain_sum[...] = jnp.zeros_like(gain_sum)

    @pl.loop(0, count // 8)
    def _(turn):
        rows = pl.ds(pl.multiple_of(turn * 8, 8), 8)
        gain_sum[...] += held[rows, :] * scaled_rows[rows, :]

    def gain_copy(step):
        return remote(gain_sum, gain_in.at[step - 1], gain_send.at[step - 1], gain_recv.at[step - 1], shard=(shard + step) % shards)

    def gain_deal(step):
        at = shards - 1 + step - 1
        return remote(gain_out, gain_in.at[at], gain_send.at[at], gain_recv.at[at], group=(group + step) % groups)

    for step in range(1, shards):
        gain_copy(step).start()
    gain_out[...] = gain_sum[...]
    for step in range(1, shards):
        gain_copy(step).wait_recv()
        gain_out[...] += gain_in[step - 1]
    for step in range(1, groups):
        gain_deal(step).start()
    for step in range(1, groups):
        gain_deal(step).wait_recv()
    for step in range(1, groups):
        gain_deal(step).wait_send()
    for step in range(1, groups):
        gain_out[...] += gain_in[shards - 1 + step - 1]

    for step in range(1, shards):
        gain_copy(step).wait_send()
        small_deal(step).wait()
    for step in range(1, groups):
        small_copy(step).wait_send()
    if direct:
        deal_end()
        for step in range(1, rows_y):
            row_copy(step).wait_send()
        for turn in range(rows_y):
            core_copy(turn).wait_send()
    for step in range(lines):
        for copy in wide_copies(step, columns - 1) if columns > 1 else ():
            copy.wait_send()
    for step in range(lines - 1):
        for copy in line_copies(step):
            copy.wait_send()


def tail_exchange(shards, groups, partial, weight_part, small, scaled_rows, owned, depth, direct):
    columns = grid_columns(shards)
    lines, rows_y = shards // columns, groups // 2
    count, width = scaled_rows.shape
    piece = piece_rows(shards, groups) if direct else CHUNK
    small_shape = small.shape
    coded, scale = (count, width), (8, count)
    any_space, vmem = pl.BlockSpec(memory_space=pl.ANY), pl.BlockSpec(memory_space=pltpu.VMEM)
    f32, i16 = jnp.float32, jnp.int16
    slots = max(columns - 1, 1)
    dma = pltpu.SemaphoreType.DMA
    landing = [
        ((slots, lines) + coded, i16),
        ((slots, lines) + scale, f32),
        ((2, lines) + coded, i16),
        ((2, lines) + scale, f32),
    ]
    near = shards * count * width <= 1 << 22
    out = pl.pallas_call(
        functools.partial(tail_kernel, shards, groups, columns, near, direct),
        in_specs=[any_space, any_space, any_space, vmem],
        out_specs=[vmem, any_space, any_space, vmem] + [any_space] * 3 + [vmem] + ([] if near else [any_space] * 4),
        out_shape=[
            jax.ShapeDtypeStruct((count, width), f32),
            jax.ShapeDtypeStruct((owned, depth), f32),
            jax.ShapeDtypeStruct((shards,) + small_shape, f32),
            jax.ShapeDtypeStruct((8, width), f32),
            jax.ShapeDtypeStruct((rows_y, piece, width), f32),
            jax.ShapeDtypeStruct((max(rows_y - 1, 1), piece, width), f32),
            jax.ShapeDtypeStruct((max(groups - 1, 1),) + small_shape, f32),
            jax.ShapeDtypeStruct((shards - 1 + groups - 1, 8, width), f32),
        ]
        + ([] if near else [jax.ShapeDtypeStruct(*each) for each in landing]),
        scratch_shapes=([pltpu.VMEM(*each) for each in landing] if near else [])
        + [
            pltpu.VMEM((count, width), f32),
            pltpu.VMEM((lines,) + coded, i16),
            pltpu.VMEM((lines,) + scale, f32),
            pltpu.VMEM((lines,) + coded, i16),
            pltpu.VMEM((lines,) + scale, f32),
            pltpu.VMEM((16, 128) if near else coded, i16),
            pltpu.VMEM((8, 128) if near else scale, f32),
            pltpu.VMEM((count, 128), f32),
            pltpu.VMEM((piece, width), f32),
            pltpu.VMEM((piece, width), f32),
            pltpu.VMEM((max(rows_y - 1, 1), piece, width), f32),
            pltpu.VMEM(small_shape, f32),
            pltpu.VMEM(small_shape, f32),
            pltpu.VMEM((8, width), f32),
            dma,
            dma((2, slots * lines)),
            dma((2, slots * lines)),
            dma((2, lines)),
            dma((2, 2, lines)),
            dma((rows_y,)),
            dma((rows_y,)),
            dma((max(rows_y - 1, 1),)),
            dma((max(rows_y - 1, 1),)),
            dma((piece // CHUNK, shards)),
            dma,
            dma((groups + shards,)),
            dma((groups + shards,)),
            dma((shards + groups,)),
            dma((shards + groups,)),
        ],
        compiler_params=pltpu.CompilerParams(
            collective_id=1, has_side_effects=True, vmem_limit_bytes=60 * 1024 * 1024
        ),
        cost_estimate=pl.CostEstimate(flops=0, bytes_accessed=400_000_000, transcendentals=0),
        name="tail_exchange",
    )(partial, weight_part, small, scaled_rows)
    return out[:4]


def nesterov(weight, gradient, moment, average, step_rate):
    decayed = gradient + weight_decay * weight
    new_moment = momentum_decay * moment + decayed
    new_weight = weight - step_rate * (decayed + momentum_decay * new_moment)
    new_average = average_decay * average + (1.0 - average_decay) * new_weight
    return (new_moment, new_weight, new_average)


def dot32(a, b, contract=((1,), (0,))):
    return lax.dot_general(a, b, (contract, ((), ())), preferred_element_type=jnp.float32)


def own_slice(value, index, width, axis):
    return lax.dynamic_slice_in_dim(value, index * width, width, axis)


def local(
    tokens,
    cotangent,
    lengths,
    deal_slot,
    in_weight,
    out_weight,
    small_params,
    in_moment,
    out_moment,
    small_moment,
    in_average,
    out_average,
    small_average,
):
    shards, groups = lax.axis_size("shard"), lax.axis_size("group")
    shard, group = lax.axis_index("shard"), lax.axis_index("group")
    rows, width = tokens.shape
    per = rows // shards
    total = rows * shards
    blocks = total // BLOCK
    heads = HEADS // shards
    inner = INNER // shards
    shared = SHARED // shards
    conv_flat, conv_bias, dt_bias, rate_log, skip_gain, norm_gain, pre_gain = unpack(small_params)
    taps = conv_flat.reshape(CONV, XBC)

    cols, depth, sends = in_weight.shape[1], in_weight.shape[0], out_weight.shape[1]
    direct = cols % CHUNK == 0 and depth % 128 == 0 and sends % 128 == 0 and per % CHUNK == 0
    direct = direct and (2 * inner + SHARED + HEADS) % (groups * CHUNK) == 0 and shared % CHUNK == 0
    bounds = jnp.cumsum(lengths[0])[:-1].astype(jnp.int32)
    seg_rows = segment_of(jnp.arange(total, dtype=jnp.int32), lengths[0])

    rank = jnp.sum((deal_slot[None, :] < deal_slot[:, None]).astype(jnp.int32), axis=1)
    sort_mat = (rank[None, :] == jnp.arange(rows)[:, None]).astype(jnp.bfloat16)
    sorted_slot = jnp.sum(jnp.where(sort_mat > 0, deal_slot[None, :], 0), axis=1)
    r_in = lax.rsqrt(jnp.mean(tokens * tokens, axis=1, keepdims=True) + eps_norm)
    normed_low = (tokens * r_in * pre_gain[None, :]).astype(jnp.bfloat16)
    x_sorted = dot32(sort_mat, normed_low).astype(jnp.bfloat16).reshape(blocks, per, width)
    c_sorted = dot32(sort_mat, cotangent.astype(jnp.bfloat16)).astype(jnp.bfloat16).reshape(blocks, per, width)
    in_turned = in_weight.astype(jnp.bfloat16).T
    out_cast = out_weight.astype(jnp.bfloat16)

    if direct:
        slot_own = jnp.pad(sorted_slot, (0, 1024 - rows)).reshape(8, 128)
        x_all, in_low, out_low, slot_all = front_exchange(shards, groups, x_sorted, in_turned, out_cast, slot_own)
        x_all = x_all.reshape(blocks, BLOCK, width)
        slot_all = slot_all.reshape(shards, -1)[:, :rows]
    else:
        x_all = lax.all_gather(x_sorted, "shard").transpose(1, 0, 2, 3).reshape(blocks, BLOCK, width)
        slot_all = lax.all_gather(sorted_slot, "shard")
        part = depth // groups
        pieces = lax.all_to_all(in_turned.reshape(cols, groups, part), "group", 1, 0)
        pieces = pieces.reshape(groups * cols, part)

        def cut(lo, each):
            return pieces[lo : lo + each * shards].reshape(shards, each, part)

        spread = jnp.broadcast_to(pieces[None, 2 * INNER :], (shards, SHARED + HEADS, part))
        got = jnp.concatenate([cut(0, inner), cut(INNER, inner), spread], axis=1)
        got = lax.all_gather(lax.all_to_all(got, "shard", 0, 0), "group")
        in_low = got.transpose(2, 1, 0, 3).reshape(-1, width)
        out_low = lax.all_gather(out_cast, "group", axis=1, tiled=True)
    out_full = lax.all_gather(out_cast, "shard", axis=0, tiled=True)
    out_full = lax.all_gather(out_full, "group", axis=1, tiled=True)
    slot_blk = slot_all.reshape(shards, blocks, per).transpose(1, 0, 2).reshape(blocks, 1, BLOCK)
    slot_blk = slot_blk - jnp.arange(blocks, dtype=jnp.int32)[:, None, None] * BLOCK

    taps_v = own_slice(taps[:, :INNER], shard, inner, 1)
    taps_all = jnp.concatenate([taps_v, taps[:, INNER:]], axis=1)
    bias_all = jnp.concatenate([own_slice(conv_bias[:INNER], shard, inner, 0), conv_bias[INNER:]])[None, :]
    skip_wide = jnp.repeat(own_slice(skip_gain, shard, heads, 0), HDIM)[None, :]
    gain_own = own_slice(norm_gain, shard, inner, 0)[None, :]
    padding = max(TAIL - heads, 0)
    rate = jnp.pad(-jnp.exp(own_slice(rate_log, shard, heads, 0)), (0, padding))[:, None]
    normed, projected, pre, mixed, states, dt_cols, dt_raw, c_all = mixer_forward(
        shards, bounds, slot_blk, x_all, in_low, taps_all, bias_all, dt_bias[None, :], rate, skip_wide, c_sorted
    )
    conv_bc = projected[:, 2 * inner : 2 * inner + SHARED]
    cot_low, d_out, sums = pack_cotangent(
        shards, slot_blk, c_all.reshape(blocks, BLOCK, width), out_low, mixed, projected, gain_own
    )

    d_cols, d_bc, d_dt, grads, rate_terms, grad_out, home = mixer_backward(
        shards, bounds, slot_blk, pre, mixed, projected, d_out, sums, states, dt_cols, cot_low,
        taps_v, rate, skip_wide, gain_own,
    )
    grad_out = lax.psum_scatter(grad_out, "group", scatter_dimension=1, tiled=True)

    home = home.reshape(shards, rows, inner).transpose(1, 0, 2).reshape(rows, INNER)
    home = dot32(sort_mat, home, ((0,), (0,))).astype(jnp.bfloat16)
    block_out = tokens + dot32(home, out_full)
    d_dtraw = d_dt[:heads].T * jax.nn.sigmoid(dt_raw[:, :heads])
    grad_dtb = jnp.sum(d_dtraw, axis=0)
    grad_rate = jnp.sum(rate_terms[:heads], axis=1)
    grad_skip = jnp.sum(grads[6].reshape(heads, HDIM), axis=1)
    _, pull_bc = jax.vjp(
        lambda c, t, b: convolve(c, seg_rows, t, b),
        own_slice(conv_bc, shard, shared, 1),
        own_slice(taps[:, INNER:], shard, shared, 1),
        own_slice(conv_bias[INNER:], shard, shared, 0),
    )
    d_conv_bc, grad_taps_bc, grad_bias_bc = pull_bc(d_bc.T)
    rest = 128 - shared - heads
    d_rest = jnp.concatenate([d_conv_bc, d_dtraw, jnp.zeros((total, rest), jnp.float32)], axis=1)
    in_rest = jnp.concatenate(
        [
            own_slice(in_low[2 * inner : 2 * inner + SHARED], shard, shared, 0),
            own_slice(in_low[2 * inner + SHARED :], shard, heads, 0),
            jnp.zeros((rest, width), jnp.bfloat16),
        ]
    )
    partial, weight_part = project_back(
        slot_blk, d_cols, d_rest.astype(jnp.bfloat16), normed, in_low, in_rest, shards
    )
    dt_part = weight_part[2 * inner + shared : 2 * inner + shared + heads]

    mine = [
        grads[:CONV].reshape(-1),
        grad_taps_bc.reshape(-1),
        grads[4],
        grad_bias_bc,
        grad_dtb,
        grad_rate,
        grad_skip,
        grads[5],
    ]
    if direct:
        mine.append(dt_part.reshape(-1))
    extents = [piece.shape[0] for piece in mine]
    mine = jnp.concatenate(mine)
    mine = jnp.pad(mine, (0, -mine.shape[0] % 1024)).reshape(-1, 128)
    x_scaled = jnp.dot(sort_mat.astype(jnp.float32), tokens * r_in, precision=lax.Precision.HIGHEST)
    d_normed, grad_in, small_all, gain_all = tail_exchange(
        shards, groups, partial.reshape(shards, rows, width), weight_part, mine, x_scaled, cols, depth, direct
    )
    d_normed = jnp.dot(sort_mat.T.astype(jnp.float32), d_normed, precision=lax.Precision.HIGHEST)
    d_scaled = pre_gain[None, :] * d_normed
    inside = jnp.mean(tokens * d_scaled, axis=1, keepdims=True)
    input_grad = cotangent + r_in * (d_scaled - tokens * (r_in * r_in) * inside)
    grad_pre = jnp.sum(gain_all, axis=0)

    mine = small_all.reshape(shards, -1)
    found, offset = [], 0
    for extent in extents:
        found.append(mine[:, offset : offset + extent])
        offset = offset + extent
    if direct:
        dt_part = own_slice(found.pop().reshape(HEADS, width), shard, depth, 1)
        last = jnp.concatenate([grad_in[: cols - HEADS], dt_part])
        grad_in = jnp.where(group == groups - 1, last, grad_in)
    else:
        used = 2 * inner + shared + heads
        grad_in = weight_part[:used].reshape(used, shards, groups, part).transpose(2, 1, 0, 3)
        grad_in = lax.psum_scatter(grad_in, "group", scatter_dimension=0)
        grad_in = lax.all_to_all(grad_in, "shard", 0, 0)

        def join(lo, each):
            return grad_in[:, lo : lo + each].reshape(shards * each, part)

        grad_in = jnp.concatenate(
            [
                join(0, inner),
                join(inner, inner),
                join(2 * inner, shared),
                join(2 * inner + shared, heads),
            ]
        )
        grad_in = lax.all_to_all(grad_in.reshape(groups, cols, part), "group", 0, 0)
        grad_in = grad_in.transpose(1, 0, 2).reshape(cols, depth)

    def taps_of(piece):
        return piece.reshape(shards, CONV, -1).transpose(1, 0, 2).reshape(CONV, -1)

    grad_taps = jnp.concatenate([taps_of(found[0]), taps_of(found[1])], axis=1).reshape(-1)
    grad_small = jnp.concatenate([grad_taps] + [piece.reshape(-1) for piece in found[2:]] + [grad_pre])
    in_new = nesterov(in_weight.T, grad_in, in_moment.T, in_average.T, rate_in)
    in_new = tuple(value.T for value in in_new)
    out_new = nesterov(out_weight, grad_out, out_moment, out_average, rate_out)
    small_new = nesterov(small_params, grad_small, small_moment, small_average, rate_small)
    return (block_out, input_grad) + in_new + out_new + small_new


def solution(mesh):
    rows = P(("group", "shard"), None)
    tile = P("shard", "group")
    return jax.shard_map(
        local,
        mesh=mesh,
        in_specs=(
            rows,
            rows,
            P("group", None),
            P(("group", "shard")),
            tile,
            tile,
            P(),
            tile,
            tile,
            P(),
            tile,
            tile,
            P(),
        ),
        out_specs=(rows, rows, tile, tile, tile, tile, tile, tile, P(), P(), P()),
        check_vma=False,
    )
```

```python
import functools

import jax
import jax.numpy as jnp
from jax import lax
from jax.experimental import pallas as pl
from jax.experimental.pallas import tpu as pltpu
from jax.sharding import PartitionSpec as P

D = 2048
HEADS = 64
HDIM = 64
STATE = 128
CONV = 4
BLOCK = 256
INNER = 4096
XBC = 4352
SHARED = 2 * STATE
TAIL = 8
CHUNK = 16
MESH = pl.DeviceIdType.MESH


eps_norm = 1e-05
momentum_decay = 0.9
weight_decay = 0.01
average_decay = 0.99
rate_in = 0.0001
rate_out = 3e-05
rate_small = 0.001


def unpack(packed_small):
    extents = [CONV * XBC, XBC, HEADS, HEADS, HEADS, INNER, D]
    pieces = []
    offset = 0
    for extent in extents:
        pieces.append(packed_small[offset : offset + extent])
        offset = offset + extent
    return pieces


def segment_of(positions, lengths_row):
    bounds = jnp.cumsum(lengths_row)[:-1]
    inside = jnp.sum((positions[:, None] >= bounds[None, :]).astype(jnp.int32), axis=1)
    return jnp.where(positions < 0, -1, inside)


def convolve(conv_rows, seg_rows, conv_taps, conv_bias):
    row_count, width = conv_rows.shape
    extended = jnp.concatenate([jnp.zeros((CONV - 1, width), conv_rows.dtype), conv_rows], axis=0)
    seg_ext = jnp.concatenate([jnp.full((CONV - 1,), -1, jnp.int32), seg_rows], axis=0)
    conv_sum = jnp.zeros_like(conv_rows) + conv_bias[None, :]
    for tap_index in range(CONV):
        same_seq = (seg_ext[tap_index : tap_index + row_count] == seg_rows)[:, None]
        conv_sum = conv_sum + jnp.where(
            same_seq,
            extended[tap_index : tap_index + row_count] * conv_taps[tap_index][None, :],
            0.0,
        )
    return jax.nn.silu(conv_sum)


def split(value):
    high = value.astype(jnp.bfloat16)
    return high, (value - high.astype(jnp.float32)).astype(jnp.bfloat16)


def dots(a, b, contract):
    return lax.dot_general(a, b, (contract, ((), ())), preferred_element_type=jnp.float32)


def dot3(a, b, contract=((1,), (0,))):
    a = a if isinstance(a, tuple) else split(a)
    b = b if isinstance(b, tuple) else split(b)
    return dots(a[0], b[0], contract) + (dots(a[0], b[1], contract) + dots(a[1], b[0], contract))


NT = ((1,), (1,))


def head_sums(value, marks):
    high = value.astype(jnp.bfloat16)
    rest = value - high.astype(jnp.float32)
    mid = rest.astype(jnp.bfloat16)
    low = (rest - mid.astype(jnp.float32)).astype(jnp.bfloat16)
    return dots(marks, high, NT) + (dots(marks, mid, NT) + dots(marks, low, NT))


def widen(columns, heads):
    rows = columns.shape[0]
    low_half = lax.broadcasted_iota(jnp.int32, (rows, 2 * HDIM), 1) < HDIM
    return jnp.concatenate(
        [
            jnp.where(low_half, columns[:, h : h + 1], columns[:, h + 1 : h + 2])
            for h in range(0, heads, 2)
        ],
        axis=1,
    )


def running_sum(value, reverse=False):
    lane = lax.broadcasted_iota(jnp.int32, value.shape, 1)
    count = value.shape[1]
    step = 1
    while step < count:
        if reverse:
            value = value + jnp.where(lane < count - step, pltpu.roll(value, count - step, 1), 0.0)
        else:
            value = value + jnp.where(lane >= step, pltpu.roll(value, step, 1), 0.0)
        step *= 2
    return value


def sequence_of(positions, bounds):
    inside = jnp.where(positions >= bounds[0], 1, 0) + jnp.where(positions >= bounds[1], 1, 0)
    return jnp.where(positions < 0, -1, inside)


def block_facts(block, bounds, dt_t, rate):
    start = block * BLOCK
    seg_col = sequence_of(start + lax.broadcasted_iota(jnp.int32, (BLOCK, 1), 0), bounds)
    seg_row = sequence_of(start + lax.broadcasted_iota(jnp.int32, (1, BLOCK), 1), bounds)
    before = sequence_of(start - 1 + lax.broadcasted_iota(jnp.int32, (1, 1), 1), bounds)
    last = sequence_of(start + BLOCK - 1 + lax.broadcasted_iota(jnp.int32, (1, 1), 1), bounds)
    run_t = running_sum(dt_t * rate)
    run = run_t.T
    final = run[BLOCK - 1 :, :]
    carried = jnp.where(seg_col == before, jnp.exp(run), 0.0)
    tail = jnp.where(seg_col == last, jnp.exp(final - run), 0.0)
    keep = jnp.where(last == before, jnp.exp(final), 0.0)
    return seg_col, seg_row, run_t, run, carried, tail, keep


def barrier_with(peers):
    barrier = pltpu.get_barrier_semaphore()
    for peer in peers:
        pl.semaphore_signal(barrier, inc=1, device_id=peer, device_id_type=MESH)
    pl.semaphore_wait(barrier, len(peers))


def remote(src, dst, sends, recvs, **where):
    return pltpu.make_async_remote_copy(
        src_ref=src, dst_ref=dst, send_sem=sends, recv_sem=recvs, device_id=where, device_id_type=MESH
    )


def place_of_rows(slots):
    count = slots.shape[1]
    return (lax.broadcasted_iota(jnp.int32, (BLOCK, count), 0) == slots).astype(jnp.bfloat16)


def grid_columns(shards):
    columns = 1
    while 2 * (2 * columns) * (2 * columns) <= shards:
        columns *= 2
    return columns if shards % columns == 0 else 1


def whole(shape):
    return pl.BlockSpec(shape, lambda *_: (0,) * len(shape))


def row_gather(shards, columns, own, gathered, local_sem, sends, recvs):
    shard = lax.axis_index("shard")
    lines = shards // columns
    z, x = shard // columns, shard % columns

    def line_copy(source, way, first=False):
        at = source * columns + x
        peer = jnp.clip(z + 1 - 2 * way, 0, lines - 1) * columns + x
        rows = own if first else gathered.at[:, at]
        return remote(rows, gathered.at[:, at], sends.at[way, source], recvs.at[at], shard=peer)

    def wide_copy(source, hop, first=False):
        at = source * columns + x
        peer = z * columns + (x + hop) % columns
        rows = own if first else gathered.at[:, at]
        return remote(rows, gathered.at[:, at], sends.at[1 + hop, source], recvs.at[at], shard=peer)

    def pass_on(source, ways, first=False):
        for way in ways:
            @pl.when(z < lines - 1 if way == 0 else z > 0)
            def _():
                line_copy(source, way, first).start()

        for hop in range(1, columns):
            wide_copy(source, hop, first).start()

    here = pltpu.make_async_copy(own, gathered.at[:, shard], local_sem)

    def begin():
        pass_on(z, (0, 1), True)
        here.start()

    def hop(step):
        @pl.when(z - step >= 0)
        def _():
            line_copy(z - step, 0).wait_recv()
            pass_on(z - step, (0,))

        @pl.when(z + step < lines)
        def _():
            line_copy(z + step, 1).wait_recv()
            pass_on(z + step, (1,))

    def end():
        here.wait()
        for step in range(1, columns):
            peer = z * columns + (x + step) % columns
            for source in range(lines):
                at = source * columns + (x + step) % columns
                remote(gathered.at[:, at], gathered.at[:, at], sends.at[1 + step, source], recvs.at[at], shard=peer).wait_recv()
        for source in range(lines):
            for step in range(1, columns):
                wide_copy(source, step).wait_send()

            @pl.when((z < lines - 1) & (source <= z))
            def _():
                line_copy(source, 0).wait_send()

            @pl.when((z > 0) & (source >= z))
            def _():
                line_copy(source, 1).wait_send()

    return begin, hop, end


def softplus(value):
    small = jnp.exp(-jnp.abs(value))
    ratio = small / (2.0 + small)
    square = ratio * ratio
    series = jnp.full_like(value, 1.0 / 15.0)
    for power in (13, 11, 9, 7, 5, 3, 1):
        series = series * square + 1.0 / power
    return jnp.maximum(value, 0.0) + 2.0 * ratio * series


def pick_columns(value, marks):
    high = value.astype(jnp.bfloat16)
    rest = value - high.astype(jnp.float32)
    mid = rest.astype(jnp.bfloat16)
    low = (rest - mid.astype(jnp.float32)).astype(jnp.bfloat16)
    plain = ((1,), (0,))
    return dots(high, marks, plain) + (dots(mid, marks, plain) + dots(low, marks, plain))


def forward_kernel(
    heads, shards, columns, bounds, slots, rows_in, weight, taps, bias, dt_bias, rate, skip, cot_own,
    packed, product, pre_out, mixed_out, state_out, dt_out, raw_out, cot_all,
    ext, state, local_sem, cot_send, cot_recv,
):
    block = pl.program_id(0)
    blocks = cot_own.shape[0]
    inner = heads * HDIM
    shard = lax.axis_index("shard")
    begin, hop, end = row_gather(shards, columns, cot_own, cot_all, local_sem, cot_send, cot_recv)
    hops = range(1, shards // columns)

    @pl.when(block == 0)
    def _():
        barrier_with([{"shard": (shard + step) % shards} for step in range(1, shards)])
        begin()
        ext[:TAIL, :] = jnp.zeros((TAIL, ext.shape[1]), jnp.float32)
        state[...] = jnp.zeros_like(state)

    for step in hops:
        if (7 * step + 1) // 2 < blocks:
            pl.when(block == (7 * step + 1) // 2)(functools.partial(hop, step))

    normed = dots(place_of_rows(slots[0]), rows_in[0], ((1,), (0,))).astype(jnp.bfloat16)
    packed[...] = normed
    product[...] = dots(normed, weight[...], NT)
    head = lax.broadcasted_iota(jnp.int32, (HEADS, 128), 0)
    lane = lax.broadcasted_iota(jnp.int32, (HEADS, 128), 1)
    marks = ((head == shard * heads + lane) & (lane < heads)).astype(jnp.bfloat16)
    raw = pick_columns(product[:, 2 * inner + SHARED :] + dt_bias[...], marks)
    raw_out[...] = raw
    dt = softplus(raw)
    dt_out[...] = dt

    bounds = (bounds[0], bounds[1])
    dt_t = dt.T[: rate.shape[0], :]
    seg_col, seg_row, run_t, run, carried, tail, keep = block_facts(block, bounds, dt_t, rate[...])
    ext[TAIL:, :] = product[:, inner : 2 * inner + SHARED]
    place = block * BLOCK + lax.broadcasted_iota(jnp.int32, (BLOCK, 1), 0)
    pre = bias[...] + taps[CONV - 1 : CONV, :] * ext[TAIL:, :]
    for back in range(1, CONV):
        same = sequence_of(place - back, bounds) == seg_col
        moved = ext[TAIL - back : TAIL - back + BLOCK, :]
        pre = pre + jnp.where(same, moved, 0.0) * taps[CONV - 1 - back : CONV - back, :]
    ext[:TAIL, :] = ext[BLOCK:, :]
    pre_out[...] = pre
    conv = pre / (1.0 + jnp.exp(-pre))
    values, b_rows, c_rows = conv[:, :inner], conv[:, inner : inner + STATE], conv[:, inner + STATE :]
    fed = values * widen(dt, heads)
    rows = lax.broadcasted_iota(jnp.int32, (BLOCK, BLOCK), 0)
    cols = lax.broadcasted_iota(jnp.int32, (BLOCK, BLOCK), 1)
    allowed = (seg_col == seg_row) & (rows >= cols)
    b_parts, c_parts = split(b_rows), split(c_rows)
    scores = jnp.where(allowed, dot3(c_parts, b_parts, NT), 0.0)
    old = state[...]
    state_out[0] = old
    output = widen(carried, heads) * dot3(c_parts, old)
    low_half = lax.broadcasted_iota(jnp.int32, (BLOCK, 2 * HDIM), 1) < HDIM
    inside = []
    for h in range(0, heads, 2):
        pair = split(fed[:, h * HDIM : (h + 2) * HDIM])
        found = []
        for k in (h, h + 1):
            mixing = jnp.exp(jnp.minimum(run[:, k : k + 1] - run_t[k : k + 1, :], 0.0)) * scores
            found.append(dot3(mixing, pair))
        inside.append(jnp.where(low_half, found[0], found[1]))
    mixed = output + jnp.concatenate(inside, axis=1) + skip[...] * values
    mixed_out[...] = mixed
    state[...] = widen(keep, heads) * old + dot3(b_rows.T, widen(tail, heads) * fed)

    @pl.when(block == blocks - 1)
    def _():
        for step in hops:
            if (7 * step + 1) // 2 >= blocks:
                hop(step)
        end()


def cotangent_kernel(
    shards, slots, rows_in, weight, mixed, gate, gain,
    packed, product, sums_out, own_sums, sums_in, sums_send, sums_recv,
):
    block = pl.program_id(0)
    shard = lax.axis_index("shard")

    @pl.when(block == 0)
    def _():
        barrier_with([{"shard": (shard + step) % shards} for step in range(1, shards)])

    cot = dots(place_of_rows(slots[0]), rows_in[0], ((1,), (0,))).astype(jnp.bfloat16)
    packed[...] = cot
    d_out = dots(cot, weight[...], NT)
    product[...] = d_out
    gate_now = gate[...]
    gated = mixed[...] * (gate_now / (1.0 + jnp.exp(-gate_now)))
    squares = jnp.sum(gated * gated, axis=1, keepdims=True)
    products = jnp.sum(gated * gain[...] * d_out, axis=1, keepdims=True)
    lane = lax.broadcasted_iota(jnp.int32, (BLOCK, 128), 1)
    both = jnp.where(lane == 0, squares, jnp.where(lane == 1, products, 0.0))
    here = pl.ds(pl.multiple_of(block * BLOCK, BLOCK), BLOCK)
    own_sums[:, here] = both.T[:8, :]

    def push(step, at):
        return remote(
            own_sums.at[:, at], sums_in.at[step - 1, :, at], sums_send.at[step], sums_recv.at[step],
            shard=(shard + step) % shards,
        )

    for step in range(1, shards):
        push(step, here).start()

    @pl.when(block == pl.num_programs(0) - 1)
    def _():
        everything = pl.ds(0, own_sums.shape[1])
        for step in range(1, shards):
            push(step, everything).wait()
        found = own_sums[...]
        for step in range(1, shards):
            found = found + sums_in[step - 1]
        sums_out[...] = found * (1.0 / INNER)


def backward_kernel(
    heads, blocks, shards, bounds, slots, pre, mixed, gate, d_out, conv_v, sums, state_in, dt_cols, cot,
    taps, rate, skip, gain, marks,
    d_cols, d_bc, d_dt, grads, grad_rate, grad_out, no_rows, home,
    ext, carry, bc_rows, bc_in, late_rows, bc_send, bc_recv, home_send, home_recv, local_sem,
):
    step = pl.program_id(0)
    block = blocks - 1 - step
    inner = heads * HDIM
    shard = lax.axis_index("shard")
    shared = SHARED // shards

    @pl.when(step == 0)
    def _():
        barrier_with([{"shard": (shard + turn) % shards} for turn in range(1, shards)])
        ext[BLOCK:, :] = jnp.zeros((TAIL, ext.shape[1]), jnp.float32)
        carry[...] = jnp.zeros_like(carry)
        grads[...] = jnp.zeros_like(grads)
        grad_rate[...] = jnp.zeros_like(grad_rate)
        grad_out[...] = jnp.zeros_like(grad_out)

    bounds = (bounds[0], bounds[1])
    dt = dt_cols[...]
    dt_t = dt.T[: rate.shape[0], :]
    seg_col, seg_row, run_t, run, carried, tail, keep = block_facts(block, bounds, dt_t, rate[...])
    sums_cols = sums[...].T
    r_out = lax.rsqrt(sums_cols[:, 0:1] + 1e-05)
    inside = sums_cols[:, 1:2]
    gate_now = gate[...]
    gate_sig = 1.0 / (1.0 + jnp.exp(-gate_now))
    act = gate_now * gate_sig
    mixed_now = mixed[...]
    gated = mixed_now * act
    d_out_now = d_out[...]
    normed_out = (gated * r_out * gain[...]).astype(jnp.bfloat16)
    to_home = dots(place_of_rows(slots[0]), normed_out, ((0,), (0,)))
    per = BLOCK // shards
    if per % 16 == 0:
        no_rows[0] = to_home.astype(jnp.bfloat16).reshape(shards, per, inner)
    else:
        for turn in range(shards):
            no_rows[0, turn] = to_home[turn * per : (turn + 1) * per].astype(jnp.bfloat16)
    half = home.shape[1]

    def push_home(turn, at):
        peer = (shard + turn) % shards
        return remote(late_rows.at[at, peer], home.at[shard, at], home_send.at[turn], home_recv.at[turn], shard=peer)

    @pl.when(step < blocks - half)
    def _():
        late_rows[block - half] = no_rows[0]
        for turn in range(1, shards):
            push_home(turn, pl.ds(block - half, 1)).start()
    grad_out[...] += dots(normed_out, cot[...], ((0,), (0,)))
    d_gated = r_out * (gain[...] * d_out_now - gated * (r_out * r_out) * inside)
    dy = d_gated * act
    d_cols[:, :inner] = (d_gated * mixed_now * (gate_sig * (1.0 + gate_now * (1.0 - gate_sig)))).astype(jnp.bfloat16)
    grads[5:6, :] += jnp.sum(gated * r_out * d_out_now, axis=0, keepdims=True)
    pre_now = pre[...]
    sig = 1.0 / (1.0 + jnp.exp(-pre_now))
    conv = pre_now * sig
    values, b_rows, c_rows = conv[:, :inner], conv[:, inner : inner + STATE], conv[:, inner + STATE :]
    grads[6:7, :] += jnp.sum(dy * values, axis=0, keepdims=True)
    dt_wide = widen(dt, heads)
    fed = values * dt_wide
    old, after = state_in[0], carry[...]
    b_parts, c_parts, old_parts, after_parts = split(b_rows), split(c_rows), split(old), split(after)
    carried_wide, tail_wide, keep_wide = widen(carried, heads), widen(tail, heads), widen(keep, heads)
    rows = lax.broadcasted_iota(jnp.int32, (BLOCK, BLOCK), 0)
    cols = lax.broadcasted_iota(jnp.int32, (BLOCK, BLOCK), 1)
    allowed = (seg_col == seg_row) & (cols >= rows)
    scores_t = jnp.where(allowed, dot3(b_parts, c_parts, NT), 0.0)
    low_half = lax.broadcasted_iota(jnp.int32, (BLOCK, 2 * HDIM), 1) < HDIM
    d_scores_t = jnp.zeros((BLOCK, BLOCK), jnp.float32)
    d_fed, row_terms, col_terms = [], [], []
    for h in range(0, heads, 2):
        fed_pair = fed[:, h * HDIM : (h + 2) * HDIM]
        dy_pair = split(dy[:, h * HDIM : (h + 2) * HDIM])
        found = []
        for k in (h, h + 1):
            own = low_half if k == h else jnp.logical_not(low_half)
            d_mixing = dot3(jnp.where(own, fed_pair, 0.0), dy_pair, NT)
            decay = jnp.exp(jnp.minimum(run_t[k : k + 1, :] - run[:, k : k + 1], 0.0))
            mixing = decay * scores_t
            d_scores_t = d_scores_t + decay * d_mixing
            flow = mixing * d_mixing
            row_terms.append(jnp.sum(flow, axis=0, keepdims=True))
            col_terms.append(jnp.sum(flow, axis=1, keepdims=True))
            found.append(dot3(mixing, dy_pair))
        d_fed.append(jnp.where(low_half, found[0], found[1]))
    d_scores_t = split(jnp.where(allowed, d_scores_t, 0.0))
    fed_tail = fed * tail_wide
    dy_carried = dy * carried_wide
    d_fed_out = tail_wide * dot3(b_parts, after_parts)
    d_fed = jnp.concatenate(d_fed, axis=1) + d_fed_out
    dy_parts, tail_parts = split(dy_carried), split(fed_tail)
    here = pl.ds(pl.multiple_of(block * BLOCK, BLOCK), BLOCK)
    bc_rows[:STATE, here] = (dot3(d_scores_t, c_parts) + dot3(tail_parts, after_parts, NT)).T
    bc_rows[STATE:, here] = (dot3(d_scores_t, b_parts, ((0,), (0,))) + dot3(dy_parts, old_parts, NT)).T

    def push(turn, at):
        peer = (shard + turn) % shards
        rows_at = pl.ds(pl.multiple_of(peer * shared, shared), shared)
        return remote(
            bc_rows.at[rows_at, at], bc_in.at[turn - 1, :, at], bc_send.at[turn], bc_recv.at[turn], shard=peer
        )

    for turn in range(1, shards):
        push(turn, here).start()
    head_count = dt_t.shape[0]
    pad = [jnp.zeros((1, BLOCK), jnp.float32)] * (head_count - heads)
    pad_col = [jnp.zeros((BLOCK, 1), jnp.float32)] * (head_count - heads)
    d_run = jnp.concatenate(row_terms + pad, axis=0) - jnp.concatenate(col_terms + pad_col, axis=1).T
    d_run = d_run + head_sums(dy_carried * dot3(c_parts, old_parts), marks[...])
    leaving = head_sums(fed * d_fed_out, marks[...])
    kept = jnp.sum(old * after, axis=0, keepdims=True) * keep_wide
    kept = jnp.sum(marks[...].astype(jnp.float32) * kept, axis=1, keepdims=True)
    at_end = lax.broadcasted_iota(jnp.int32, (head_count, BLOCK), 1) == BLOCK - 1
    total = jnp.sum(leaving, axis=1, keepdims=True) + kept
    d_run = d_run - leaving + jnp.where(at_end, total, 0.0)
    d_log = running_sum(d_run, reverse=True)
    d_dt[...] = d_log * rate[...] + head_sums(values * d_fed, marks[...])
    grad_rate[...] += d_log * (dt_t * rate[...])
    carry[...] = keep_wide * after + dot3(c_rows.T, dy_parts)
    pre_v, sig_v = pre_now[:, :inner], sig[:, :inner]
    d_values = dt_wide * d_fed + skip[...] * dy
    d_pre = d_values * (sig_v * (1.0 + pre_v * (1.0 - sig_v)))
    ext[:BLOCK, :] = d_pre
    place = block * BLOCK + lax.broadcasted_iota(jnp.int32, (BLOCK, 1), 0)
    conv_in = conv_v[...]
    d_conv = taps[CONV - 1 : CONV, :] * d_pre
    grads[CONV - 1 : CONV, :] += jnp.sum(conv_in * d_pre, axis=0, keepdims=True)
    grads[CONV : CONV + 1, :] += jnp.sum(d_pre, axis=0, keepdims=True)
    for ahead in range(1, CONV):
        same = sequence_of(place + ahead, bounds) == seg_col
        moved = jnp.where(same, ext[ahead : ahead + BLOCK, :], 0.0)
        d_conv = d_conv + taps[CONV - 1 - ahead : CONV - ahead, :] * moved
        grads[CONV - 1 - ahead : CONV - ahead, :] += jnp.sum(conv_in * moved, axis=0, keepdims=True)
    ext[BLOCK:, :] = ext[:TAIL, :]
    d_cols[:, inner:] = d_conv.astype(jnp.bfloat16)

    @pl.when(step == blocks - 1)
    def _():
        everything = pl.ds(0, bc_rows.shape[1])
        here = pltpu.make_async_copy(late_rows.at[:, shard], home.at[shard], local_sem)
        here.start()
        for turn in range(1, shards):
            push(turn, everything).wait()
            push_home(turn, pl.ds(0, half)).wait()
        here.wait()
        found = bc_rows[pl.ds(pl.multiple_of(shard * shared, shared), shared), :]
        for turn in range(1, shards):
            found = found + bc_in[turn - 1]
        d_bc[...] = found


def mixer_forward(shards, bounds, slots, rows_in, weight, taps, bias, dt_bias, rate, skip, cot_own):
    blocks, _, width = rows_in.shape
    columns = grid_columns(shards)
    total, inner, kept = blocks * BLOCK, INNER // shards, weight.shape[0]
    heads = inner // HDIM
    f32, bf16, any_space = jnp.float32, jnp.bfloat16, pl.BlockSpec(memory_space=pl.ANY)

    def block_of(lanes):
        return pl.BlockSpec((BLOCK, lanes), lambda i: (i, 0))

    return pl.pallas_call(
        functools.partial(forward_kernel, heads, shards, columns),
        grid=(blocks,),
        in_specs=[
            pl.BlockSpec(memory_space=pltpu.SMEM),
            pl.BlockSpec((1, 1, BLOCK), lambda i: (i, 0, 0)),
            pl.BlockSpec((1, BLOCK, width), lambda i: (i, 0, 0)),
            whole(weight.shape),
            whole(taps.shape),
            whole(bias.shape),
            whole(dt_bias.shape),
            whole(rate.shape),
            whole(skip.shape),
            any_space,
        ],
        out_specs=[
            block_of(width),
            block_of(kept),
            block_of(inner + SHARED),
            block_of(inner),
            pl.BlockSpec((1, STATE, inner), lambda i: (i, 0, 0)),
            block_of(128),
            block_of(128),
            any_space,
        ],
        out_shape=[
            jax.ShapeDtypeStruct((total, width), bf16),
            jax.ShapeDtypeStruct((total, kept), f32),
            jax.ShapeDtypeStruct((total, inner + SHARED), f32),
            jax.ShapeDtypeStruct((total, inner), f32),
            jax.ShapeDtypeStruct((blocks, STATE, inner), f32),
            jax.ShapeDtypeStruct((total, 128), f32),
            jax.ShapeDtypeStruct((total, 128), f32),
            jax.ShapeDtypeStruct((cot_own.shape[0], shards) + cot_own.shape[1:], bf16),
        ],
        scratch_shapes=[
            pltpu.VMEM((BLOCK + TAIL, inner + SHARED), f32),
            pltpu.VMEM((STATE, inner), f32),
            pltpu.SemaphoreType.DMA,
            pltpu.SemaphoreType.DMA((1 + columns, shards // columns)),
            pltpu.SemaphoreType.DMA((shards,)),
        ],
        compiler_params=pltpu.CompilerParams(
            collective_id=2, has_side_effects=True, vmem_limit_bytes=56 * 1024 * 1024
        ),
        cost_estimate=pl.CostEstimate(flops=0, bytes_accessed=300_000_000, transcendentals=0),
        name="mixer_forward",
    )(bounds, slots, rows_in, weight, taps, bias, dt_bias, rate, skip, cot_own)


def pack_cotangent(shards, slots, rows_in, weight, mixed, projected, gain):
    blocks, _, width = rows_in.shape
    total, inner = mixed.shape

    def block_of(lanes):
        return pl.BlockSpec((BLOCK, lanes), lambda i: (i, 0))

    return pl.pallas_call(
        functools.partial(cotangent_kernel, shards),
        grid=(blocks,),
        in_specs=[
            pl.BlockSpec((1, 1, BLOCK), lambda i: (i, 0, 0)),
            pl.BlockSpec((1, BLOCK, width), lambda i: (i, 0, 0)),
            whole(weight.shape),
            block_of(inner),
            block_of(inner),
            whole(gain.shape),
        ],
        out_specs=[block_of(width), block_of(inner), whole((8, total))],
        out_shape=[
            jax.ShapeDtypeStruct((total, width), jnp.bfloat16),
            jax.ShapeDtypeStruct((total, inner), jnp.float32),
            jax.ShapeDtypeStruct((8, total), jnp.float32),
        ],
        scratch_shapes=[
            pltpu.VMEM((8, total), jnp.float32),
            pltpu.VMEM((shards - 1, 8, total), jnp.float32),
            pltpu.SemaphoreType.DMA((shards,)),
            pltpu.SemaphoreType.DMA((shards,)),
        ],
        compiler_params=pltpu.CompilerParams(
            collective_id=5, has_side_effects=True, vmem_limit_bytes=48 * 1024 * 1024
        ),
        cost_estimate=pl.CostEstimate(flops=0, bytes_accessed=60_000_000, transcendentals=0),
        name="pack_cotangent",
    )(slots, rows_in, weight, mixed, projected, gain)


def mixer_backward(
    shards, bounds, slots, pre, mixed, projected, d_out, sums, states, dt_cols, cot, taps, rate, skip, gain
):
    total, inner = d_out.shape
    heads, blocks, padded = inner // HDIM, total // BLOCK, rate.shape[0]
    shared = SHARED // shards
    marks = (jnp.arange(padded)[:, None] == jnp.arange(inner)[None, :] // HDIM).astype(jnp.bfloat16)

    def block_of(width, column):
        return pl.BlockSpec((BLOCK, width), lambda i: (blocks - 1 - i, column))

    return pl.pallas_call(
        functools.partial(backward_kernel, heads, blocks, shards),
        grid_spec=pltpu.PrefetchScalarGridSpec(
            num_scalar_prefetch=0,
            grid=(blocks,),
            in_specs=[
                pl.BlockSpec(memory_space=pltpu.SMEM),
                pl.BlockSpec((1, 1, BLOCK), lambda i: (blocks - 1 - i, 0, 0)),
                block_of(inner + SHARED, 0),
                block_of(inner, 0),
                block_of(inner, 0),
                block_of(inner, 0),
                block_of(inner, 1),
                pl.BlockSpec((8, BLOCK), lambda i: (0, blocks - 1 - i)),
                pl.BlockSpec((1, STATE, inner), lambda i: (blocks - 1 - i, 0, 0)),
                block_of(dt_cols.shape[1], 0),
                block_of(cot.shape[1], 0),
                whole(taps.shape),
                whole(rate.shape),
                whole(skip.shape),
                whole(gain.shape),
                whole(marks.shape),
            ],
            out_specs=[
                block_of(2 * inner, 0),
                whole((shared, total)),
                pl.BlockSpec((padded, BLOCK), lambda i: (0, blocks - 1 - i)),
                whole((8, inner)),
                whole((padded, BLOCK)),
                whole((inner, cot.shape[1])),
                pl.BlockSpec((1, shards, BLOCK // shards, inner), lambda i: (blocks - 1 - i, 0, 0, 0)),
                pl.BlockSpec(memory_space=pl.ANY),
            ],
            scratch_shapes=[
                pltpu.VMEM((BLOCK + TAIL, inner), jnp.float32),
                pltpu.VMEM((STATE, inner), jnp.float32),
                pltpu.VMEM((SHARED, total), jnp.float32),
                pltpu.VMEM((shards - 1, shared, total), jnp.float32),
                pltpu.VMEM((blocks // 2, shards, BLOCK // shards, inner), jnp.bfloat16),
                pltpu.SemaphoreType.DMA((shards,)),
                pltpu.SemaphoreType.DMA((shards,)),
                pltpu.SemaphoreType.DMA((shards,)),
                pltpu.SemaphoreType.DMA((shards,)),
                pltpu.SemaphoreType.DMA,
            ],
        ),
        out_shape=[
            jax.ShapeDtypeStruct((total, 2 * inner), jnp.bfloat16),
            jax.ShapeDtypeStruct((shared, total), jnp.float32),
            jax.ShapeDtypeStruct((padded, total), jnp.float32),
            jax.ShapeDtypeStruct((8, inner), jnp.float32),
            jax.ShapeDtypeStruct((padded, BLOCK), jnp.float32),
            jax.ShapeDtypeStruct((inner, cot.shape[1]), jnp.float32),
            jax.ShapeDtypeStruct((blocks, shards, BLOCK // shards, inner), jnp.bfloat16),
            jax.ShapeDtypeStruct((shards, blocks // 2, BLOCK // shards, inner), jnp.bfloat16),
        ],
        compiler_params=pltpu.CompilerParams(
            collective_id=3, has_side_effects=True, vmem_limit_bytes=56 * 1024 * 1024
        ),
        cost_estimate=pl.CostEstimate(flops=0, bytes_accessed=200_000_000, transcendentals=0),
        name="mixer_backward",
    )(bounds, slots, pre, mixed, projected, d_out, projected, sums, states, dt_cols, cot, taps, rate, skip, gain, marks)


def piece_rows(shards, groups):
    chunks = (2 * INNER // shards + SHARED // shards) // CHUNK
    return -(-chunks // groups) * CHUNK


def column_runs(shards, groups):
    inner, width = INNER // shards, (2 * INNER + SHARED + HEADS) // groups
    kept = 2 * inner + SHARED + HEADS
    quarter = kept // groups
    spans = []
    for shard in range(shards):
        spans.append((inner * shard, shard, 0, inner))
        spans.append((INNER + inner * shard, shard, inner, inner))
    spans.append((2 * INNER, None, 2 * inner, SHARED + HEADS))
    runs = []
    for column, shard, row, length in spans:
        while length > 0:
            step = min(length, width - column % width, quarter - row % quarter)
            runs.append((column // width, column % width, shard, row, step))
            column, row, length = column + step, row + step, length - step
    return runs


def front_kernel(
    shards, groups, columns,
    rows_own, weight_own, out_own, slot_own,
    rows_all, weight_all, out_all, slot_all,
    local_sem, rows_send, rows_recv, run_send, run_recv, share_send, share_recv, out_send, out_recv, slot_send, slot_recv,
):
    shard, group = lax.axis_index("shard"), lax.axis_index("group")
    lines, rows_y = shards // columns, groups // 2
    y, core = group // 2, group % 2
    mate = y * 2 + 1 - core
    quarter = weight_all.shape[0] // groups
    depth = weight_own.shape[1]
    out_width = out_own.shape[1]
    everyone = []
    for step in range(1, shards * groups):
        other_shard = (shard + step % shards) % shards
        other_group = (group + step // shards) % groups
        everyone.append({"shard": other_shard, "group": other_group})
    barrier_with(everyone)

    begin, hop, end = row_gather(shards, columns, rows_own, rows_all, local_sem.at[0], rows_send, rows_recv)
    begin()

    def slot_copy(step):
        return remote(slot_own, slot_all.at[shard], slot_send.at[step], slot_recv.at[step], shard=(shard + step) % shards)

    for step in range(1, shards):
        slot_copy(step).start()
    slot_here = pltpu.make_async_copy(slot_own, slot_all.at[shard], local_sem.at[1])
    slot_here.start()

    runs = column_runs(shards, groups)
    lanes = pl.ds(pl.multiple_of(shard * depth, depth), depth)
    jobs = {owner: [] for owner in range(groups)}
    for owner, column, target, row, length in runs:
        for to in range(shards) if target is None else (target,):
            jobs[owner].append((column, to, row, length))

    def run_copy(number, column, to, row, length):
        return remote(
            weight_own.at[pl.ds(column, length)], weight_all.at[pl.ds(row, length), lanes],
            run_send.at[number], run_recv, shard=to, group=row // quarter,
        )

    def each_run(act):
        for owner in range(groups):
            @pl.when(group == owner)
            def _():
                for number, (column, to, row, length) in enumerate(jobs[owner]):
                    if row // quarter == owner:
                        here = shard == to
                        act(number, column, to, row, length, here)
                    else:
                        act(number, column, to, row, length, None)

    def start_run(number, column, to, row, length, here):
        if here is None:
            run_copy(number, column, to, row, length).start()
            return

        @pl.when(here)
        def _():
            pltpu.make_async_copy(weight_own.at[pl.ds(column, length)], weight_all.at[pl.ds(row, length), lanes], run_recv).start()

        @pl.when(jnp.logical_not(here))
        def _():
            run_copy(number, column, to, row, length).start()

    def end_run(number, column, to, row, length, here):
        if here is None:
            run_copy(number, column, to, row, length).wait_send()
            return

        @pl.when(jnp.logical_not(here))
        def _():
            run_copy(number, column, to, row, length).wait_send()

    each_run(start_run)

    def own_part(ref, part):
        if ref is out_all:
            return ref.at[:, pl.ds(pl.multiple_of(part * out_width, out_width), out_width)]
        return ref.at[pl.ds(pl.multiple_of(part * quarter, quarter), quarter)]

    def share(ref, part, sends, recvs, number, peer, first=None):
        source = own_part(ref, part) if first is None else first
        return remote(source, own_part(ref, part), sends.at[number], recvs.at[part], group=peer)

    def share_start(ref, sends, recvs, first=None):
        share(ref, group, sends, recvs, 0, mate, first).start()
        for step in range(1, rows_y):
            share(ref, group, sends, recvs, step, (y + step) % rows_y * 2 + core, first).start()

    def share_pass(ref, sends, recvs):
        for step in range(1, rows_y):
            part = (y + step) % rows_y * 2 + core
            share(ref, part, sends, recvs, step, part).wait_recv()
            share(ref, part, sends, recvs, rows_y - 1 + step, mate).start()

    def share_end(ref, sends, recvs):
        for turn in range(rows_y):
            part = turn * 2 + 1 - core
            share(ref, part, sends, recvs, 0, mate).wait_recv()
        for number in range(2 * rows_y - 1):
            share(ref, group, sends, recvs, number, mate).wait_send()

    out_here = pltpu.make_async_copy(out_own, own_part(out_all, group), local_sem.at[2])
    out_here.start()
    share_start(out_all, out_send, out_recv, out_own)

    for step in range(1, lines):
        hop(step)
        if step == 1:
            share_pass(out_all, out_send, out_recv)
            kept = own_part(weight_all, group)
            pltpu.make_async_copy(kept, kept, run_recv).wait()
            share_start(weight_all, share_send, share_recv)
    share_pass(weight_all, share_send, share_recv)

    end()
    out_here.wait()
    share_end(out_all, out_send, out_recv)
    share_end(weight_all, share_send, share_recv)
    each_run(end_run)
    for step in range(1, shards):
        slot_copy(step).wait()
    slot_here.wait()


def front_exchange(shards, groups, rows_own, weight_own, out_own, slot_own):
    columns = grid_columns(shards)
    lines, rows_y = shards // columns, groups // 2
    blocks, per, width = rows_own.shape
    kept = 2 * INNER // shards + SHARED + HEADS
    any_space = pl.BlockSpec(memory_space=pl.ANY)
    dma = pltpu.SemaphoreType.DMA
    counts = {}
    for owner, _, target, _, _ in column_runs(shards, groups):
        counts[owner] = counts.get(owner, 0) + (shards if target is None else 1)
    return pl.pallas_call(
        functools.partial(front_kernel, shards, groups, columns),
        in_specs=[any_space] * 4,
        out_specs=[any_space] * 4,
        out_shape=[
            jax.ShapeDtypeStruct((blocks, shards, per, width), jnp.bfloat16),
            jax.ShapeDtypeStruct((kept, width), jnp.bfloat16),
            jax.ShapeDtypeStruct((out_own.shape[0], out_own.shape[1] * groups), jnp.bfloat16),
            jax.ShapeDtypeStruct((shards,) + slot_own.shape, slot_own.dtype),
        ],
        scratch_shapes=[
            dma((3,)),
            dma((1 + columns, lines)),
            dma((shards,)),
            dma((max(counts.values()),)),
            dma,
            dma((2 * rows_y - 1,)),
            dma((groups,)),
            dma((2 * rows_y - 1,)),
            dma((groups,)),
            dma((shards,)),
            dma((shards,)),
        ],
        compiler_params=pltpu.CompilerParams(collective_id=4, has_side_effects=True),
        cost_estimate=pl.CostEstimate(flops=0, bytes_accessed=300_000_000, transcendentals=0),
        name="front_exchange",
    )(rows_own, weight_own, out_own, slot_own)


def unpack_kernel(
    shards, slots, d_cols, d_rest, normed, weight, weight_rest, no_rows,
    partial, grad, home, moved_cols, moved_rest, local_sem, home_send, home_recv,
):
    step = pl.program_id(0)
    shard = lax.axis_index("shard")
    main = d_cols.shape[1]
    per = BLOCK // shards

    def push(turn):
        peer = (shard + turn) % shards
        return remote(no_rows.at[first, peer], home.at[shard], home_send.at[turn], home_recv.at[turn], shard=peer)

    first = pl.ds(0, home.shape[1])
    here = pltpu.make_async_copy(no_rows.at[first, shard], home.at[shard], local_sem)

    @pl.when(step == 0)
    def _():
        barrier_with([{"shard": (shard + turn) % shards} for turn in range(1, shards)])
        for turn in range(1, shards):
            push(turn).start()
        here.start()
        grad[...] = jnp.zeros_like(grad)

    several = d_cols.shape[0] // BLOCK
    for turn in range(several):
        rows = pl.ds(turn * BLOCK, BLOCK)
        place = place_of_rows(slots[turn])
        moved_cols[rows, :] = dots(place, d_cols[rows, :], ((0,), (0,))).astype(jnp.bfloat16)
        moved_rest[rows, :] = dots(place, d_rest[rows, :], ((0,), (0,))).astype(jnp.bfloat16)
    tile = 512
    for lane in range(0, weight.shape[1], tile):
        lanes = pl.ds(lane, tile)
        found = dots(moved_cols[...], weight[:, lanes], ((1,), (0,)))
        found = found + dots(moved_rest[...], weight_rest[:, lanes], ((1,), (0,)))
        for turn in range(several):
            rows = found[turn * BLOCK : (turn + 1) * BLOCK]
            partial[:, turn, :, lanes] = rows.reshape(shards, per, tile)
    grad[:main, :] += dots(d_cols[...], normed[...], ((0,), (0,)))
    grad[main:, :] += dots(d_rest[...], normed[...], ((0,), (0,)))

    @pl.when(step == pl.num_programs(0) - 1)
    def _():
        for turn in range(1, shards):
            push(turn).wait()
        here.wait()


def project_back(slots, d_cols, d_rest, normed, weight, weight_rest, no_rows, shards):
    blocks, width = slots.shape[0], normed.shape[1]
    per, main, rest = BLOCK // shards, d_cols.shape[1], d_rest.shape[1]
    several = 2
    any_space = pl.BlockSpec(memory_space=pl.ANY)

    def block_of(columns):
        return pl.BlockSpec((several * BLOCK, columns), lambda i: (i, 0))

    return pl.pallas_call(
        functools.partial(unpack_kernel, shards),
        grid=(blocks // several,),
        in_specs=[
            pl.BlockSpec((several, 1, BLOCK), lambda i: (i, 0, 0)),
            block_of(main),
            block_of(rest),
            block_of(width),
            pl.BlockSpec((main, width), lambda i: (0, 0)),
            whole(weight_rest.shape),
            any_space,
        ],
        out_specs=[
            pl.BlockSpec((shards, several, per, width), lambda i: (0, i, 0, 0)),
            whole((main + rest, width)),
            any_space,
        ],
        out_shape=[
            jax.ShapeDtypeStruct((shards, blocks, per, width), jnp.float32),
            jax.ShapeDtypeStruct((main + rest, width), jnp.float32),
            jax.ShapeDtypeStruct((shards, blocks // 2) + no_rows.shape[2:], jnp.bfloat16),
        ],
        scratch_shapes=[
            pltpu.VMEM((several * BLOCK, main), jnp.bfloat16),
            pltpu.VMEM((several * BLOCK, rest), jnp.bfloat16),
            pltpu.SemaphoreType.DMA,
            pltpu.SemaphoreType.DMA((shards,)),
            pltpu.SemaphoreType.DMA((shards,)),
        ],
        compiler_params=pltpu.CompilerParams(
            collective_id=6, has_side_effects=True, vmem_limit_bytes=60 * 1024 * 1024
        ),
        cost_estimate=pl.CostEstimate(flops=0, bytes_accessed=90_000_000, transcendentals=0),
        name="project_back",
    )(slots, d_cols, d_rest, normed, weight, weight_rest, no_rows)


def other_place(step, place, count):
    upwards = count - 1 - place
    low = jnp.where(step < upwards, count - 1 - step, step - upwards)
    high = jnp.where(step < place, step, count - 1 - (step - place))
    return jnp.where(2 * place < count, low, high)


def tail_kernel(
    shards, groups, columns, near, direct,
    partial, weight_part, small, scaled_rows,
    rows_out, weight_out, mark_out, small_out, gain_out, core_in, row_in, row_scale_in, small_in, gain_in,
    wide_in, wide_scale, line_in, line_scale,
    held, coded, scales, line_coded, line_scales, got, got_scale, marks, total, other, send_rows, send_scales, row_got, row_scale_got, deal_rows, deal_scales, small_sum, small_got,
    gain_sum,
    load_sem, wide_send, wide_recv, line_send, line_recv, core_send, core_recv, row_send, row_recv,
    deal_send, deal_recv, mark_send, mark_recv, small_send, small_recv, gain_send, gain_recv,
):
    shard, group = lax.axis_index("shard"), lax.axis_index("group")
    lines = shards // columns
    rows_y = groups // 2
    z, x = shard // columns, shard % columns
    y, core = group // 2, group % 2
    count = held.shape[0]
    owned, depth = weight_out.shape
    piece, chunk = total.shape[0], CHUNK
    inner, shared = INNER // shards, SHARED // shards

    def load(src, dst):
        copy = pltpu.make_async_copy(src, dst, load_sem)
        copy.start()
        copy.wait()

    shard_peers = [(shard + step) % shards for step in range(1, shards)]
    group_peers = [(group + step) % groups for step in range(1, groups)]
    if direct:
        barrier_with(
            [
                {"shard": (shard + step % shards) % shards, "group": (group + step // shards) % groups}
                for step in range(1, shards * groups)
            ]
        )
    else:
        barrier_with([{"shard": peer} for peer in shard_peers] + [{"group": peer} for peer in group_peers])

    mate = y * 2 + 1 - core

    def core_copy(turn):
        return remote(piece_of(turn * 2 + 1 - core), core_in.at[turn], core_send.at[turn], core_recv.at[turn], group=mate)

    def piece_of(owner):
        return weight_part.at[pl.ds(pl.multiple_of(owner * piece, piece), piece)]

    for turn in range(rows_y if direct else 0):
        core_copy(turn).start()

    def small_copy(step):
        return remote(small, small_in.at[step - 1], small_send.at[step - 1], small_recv.at[step - 1], group=(group + step) % groups)

    for step in range(1, groups):
        small_copy(step).start()

    def code(coded_to, scales_to, values=held, lot=32):
        @pl.loop(0, values.shape[0] // lot, unroll=2)
        def _(turn):
            rows = pl.ds(pl.multiple_of(turn * lot, lot), lot)
            value = values[rows, :]
            most = jnp.maximum(jnp.max(jnp.abs(value), axis=1, keepdims=True), 1e-30)
            coded_to[rows, :] = jnp.round(value * (32767.0 / most)).astype(jnp.int32).astype(jnp.int16)
            marks[rows, :] = jnp.broadcast_to(most * (1.0 / 32767.0), (lot, 128))

        scales_to[...] = marks[: scales_to.shape[1], :].T[:8, :]

    def add(coded_from, scales_from):
        if not near:
            load(coded_from, got)
            load(scales_from, got_scale)
            coded_from, scales_from = got, got_scale
        marks[:count, :] = jnp.broadcast_to(scales_from[0:1, :], (128, count)).T

        @pl.loop(0, count // 32, unroll=2)
        def _(turn):
            rows = pl.ds(pl.multiple_of(turn * 32, 32), 32)
            held[rows, :] += coded_from[rows, :].astype(jnp.float32) * marks[rows, 0:1]

    def place_of(step):
        return other_place(step, z, lines) if step < lines - 1 else z

    def wide_copies(step, hop):
        at = (hop - 1) * lines + step
        peer = z * columns + (x + hop) % columns
        target = place_of(step)
        return (
            remote(coded.at[step], wide_in.at[hop - 1, target], wide_send.at[0, at], wide_recv.at[0, at], shard=peer),
            remote(scales.at[step], wide_scale.at[hop - 1, target], wide_send.at[1, at], wide_recv.at[1, at], shard=peer),
        )

    def send_wide(hop, steps):
        for step in steps:
            if hop > 1:
                for copy in wide_copies(step, hop - 1):
                    copy.wait_send()
            load(partial.at[place_of(step) * columns + (x + hop) % columns], held)
            code(coded.at[step], scales.at[step])
            for copy in wide_copies(step, hop):
                copy.start()

    def row_copies(step):
        peer = (y + step) % rows_y * 2 + core
        return (
            remote(send_rows.at[step - 1], row_in.at[step - 1], row_send.at[0, step - 1], row_recv.at[0, step - 1], group=peer),
            remote(send_scales.at[step - 1], row_scale_in.at[step - 1], row_send.at[1, step - 1], row_recv.at[1, step - 1], group=peer),
        )

    def core_sum(turn):
        load(piece_of(turn * 2 + core), total)
        load(core_in.at[turn], other)

        @pl.loop(0, piece // chunk)
        def _(turn):
            rows = pl.ds(pl.multiple_of(turn * chunk, chunk), chunk)
            total[rows, :] += other[rows, :]

    if columns > 1:
        send_wide(1, range(0, 1))
    if direct:
        for turn in range(rows_y):
            core_copy(turn).wait_recv()
        for step in range(1, rows_y):
            core_sum((y + step) % rows_y)
            code(send_rows.at[step - 1], send_scales.at[step - 1], total, chunk)
            for copy in row_copies(step):
                copy.start()
        core_sum(y)
    if columns > 1:
        send_wide(1, range(1, lines))
    for hop in range(2, columns):
        send_wide(hop, range(lines))

    load(small, small_sum)
    for step in range(1, groups):
        small_copy(step).wait_recv()
        load(small_in.at[step - 1], small_got)
        small_sum[...] += small_got[...]

    def small_deal(step):
        return remote(small_sum, small_out.at[shard], small_send.at[groups + step], small_recv.at[groups + step], shard=(shard + step) % shards)

    for step in range(1, shards):
        small_deal(step).start()
    load(small_sum, small_out.at[shard])

    def line_copies(step):
        target = place_of(step)
        way = jnp.where(target > z, 0, 1)
        peer = jnp.where(target > z, z + 1, z - 1) * columns + x
        return (
            remote(line_coded.at[step], line_in.at[way, target], line_send.at[0, step], line_recv.at[0, way, target], shard=peer),
            remote(line_scales.at[step], line_scale.at[way, target], line_send.at[1, step], line_recv.at[1, way, target], shard=peer),
        )

    def take(way, target):
        source = jnp.where(way == 0, z - 1, z + 1)
        peer = jnp.clip(source, 0, lines - 1) * columns + x
        remote(line_coded.at[0], line_in.at[way, target], line_send.at[0, 0], line_recv.at[0, way, target], shard=peer).wait_recv()
        remote(line_scales.at[0], line_scale.at[way, target], line_send.at[1, 0], line_recv.at[1, way, target], shard=peer).wait_recv()
        add(line_in.at[way, target], line_scale.at[way, target])

    def gather_wide(step):
        target = place_of(step)
        load(partial.at[target * columns + x], held)
        for hop in range(1, columns):
            for copy in wide_copies(step, hop):
                copy.wait_recv()
            add(wide_in.at[hop - 1, target], wide_scale.at[hop - 1, target])

    def deal_copy(turn, step):
        first = group * piece + turn * chunk
        column = jnp.where(
            first < inner,
            inner * shard + first,
            jnp.where(first < 2 * inner, INNER + inner * shard + first - inner, 2 * INNER + shared * shard + first - 2 * inner),
        )
        owner = jnp.minimum(column // owned, groups - 1)
        peer = (shard + step) % shards
        source = deal_rows.at[
            pl.ds(pl.multiple_of(turn * chunk, chunk), chunk), pl.ds(pl.multiple_of(peer * depth, depth), depth)
        ]
        target = weight_out.at[pl.ds(pl.multiple_of(column - owner * owned, chunk), chunk)]
        real = first < 2 * inner + shared
        here = real & (owner == group) if step == 0 else None
        away = real & (owner != group) if step == 0 else real

        def near_copy():
            return pltpu.make_async_copy(source, target, deal_recv)

        def far():
            return remote(source, target, deal_send.at[turn, step], deal_recv, shard=peer, group=owner)

        return here, near_copy, away, far

    def deal():
        for step in range(1, rows_y):
            for copy in row_copies(step):
                copy.wait_recv()
            load(row_in.at[step - 1], row_got)
            load(row_scale_in.at[step - 1], row_scale_got)
            marks[: row_scale_got.shape[1], :] = jnp.broadcast_to(row_scale_got[0:1, :], (128, row_scale_got.shape[1])).T

            @pl.loop(0, piece // chunk)
            def _(turn):
                rows = pl.ds(pl.multiple_of(turn * chunk, chunk), chunk)
                total[rows, :] += row_got[rows, :].astype(jnp.float32) * marks[rows, 0:1]

        code(deal_rows, deal_scales, total, chunk)

        @pl.loop(0, piece // chunk)
        def _(turn):
            for step in range(shards):
                here, near_copy, away, far = deal_copy(turn, step)
                if here is not None:
                    pl.when(here)(lambda: near_copy().start())
                pl.when(away)(lambda: far().start())

        load(deal_scales, mark_out.at[shard, group])
        for step in range(1, shards * groups):
            mark_copy(step).start()

    def mark_copy(step):
        where = {"shard": (shard + step % shards) % shards, "group": (group + step // shards) % groups}
        return remote(deal_scales, mark_out.at[shard, group], mark_send.at[step], mark_recv.at[step], **where)

    def deal_end():
        for step in range(1, shards * groups):
            mark_copy(step).wait()

        @pl.when(group == groups - 1)
        def _():
            most = weight_out.at[pl.ds(0, owned - HEADS)]
            pltpu.make_async_copy(most, most, deal_recv).wait()

        @pl.when(group < groups - 1)
        def _():
            pltpu.make_async_copy(weight_out, weight_out, deal_recv).wait()

        @pl.loop(0, piece // chunk)
        def _(turn):
            for step in range(shards):
                _, _, away, far = deal_copy(turn, step)
                pl.when(away)(lambda: far().wait_send())

    for step in range(lines - 1):
        if direct and step == min(1, lines - 2):
            deal()
        target = place_of(step)
        way = jnp.where(target > z, 0, 1)
        gather_wide(step)

        @pl.when(jnp.where(target > z, z > 0, z < lines - 1))
        def _():
            take(way, target)

        code(line_coded.at[step], line_scales.at[step])
        for copy in line_copies(step):
            copy.start()
    gather_wide(lines - 1)

    @pl.when(z > 0)
    def _():
        take(0, z)

    @pl.when(z < lines - 1)
    def _():
        take(1, z)

    rows_out[...] = held[...]
    gain_sum[...] = jnp.zeros_like(gain_sum)

    @pl.loop(0, count // 8)
    def _(turn):
        rows = pl.ds(pl.multiple_of(turn * 8, 8), 8)
        gain_sum[...] += held[rows, :] * scaled_rows[rows, :]

    def gain_copy(step):
        return remote(gain_sum, gain_in.at[step - 1], gain_send.at[step - 1], gain_recv.at[step - 1], shard=(shard + step) % shards)

    def gain_deal(step):
        at = shards - 1 + step - 1
        return remote(gain_out, gain_in.at[at], gain_send.at[at], gain_recv.at[at], group=(group + step) % groups)

    for step in range(1, shards):
        gain_copy(step).start()
    gain_out[...] = gain_sum[...]
    for step in range(1, shards):
        gain_copy(step).wait_recv()
        gain_out[...] += gain_in[step - 1]
    for step in range(1, groups):
        gain_deal(step).start()
    for step in range(1, groups):
        gain_deal(step).wait_recv()
    for step in range(1, groups):
        gain_deal(step).wait_send()
    for step in range(1, groups):
        gain_out[...] += gain_in[shards - 1 + step - 1]

    for step in range(1, shards):
        gain_copy(step).wait_send()
        small_deal(step).wait()
    for step in range(1, groups):
        small_copy(step).wait_send()
    if direct:
        deal_end()
        for step in range(1, rows_y):
            for copy in row_copies(step):
                copy.wait_send()
        for turn in range(rows_y):
            core_copy(turn).wait_send()
    for step in range(lines):
        for copy in wide_copies(step, columns - 1) if columns > 1 else ():
            copy.wait_send()
    for step in range(lines - 1):
        for copy in line_copies(step):
            copy.wait_send()


def tail_exchange(shards, groups, partial, weight_part, small, scaled_rows, owned, depth, direct):
    columns = grid_columns(shards)
    lines, rows_y = shards // columns, groups // 2
    count, width = scaled_rows.shape
    piece = piece_rows(shards, groups) if direct else CHUNK
    padded = -(-piece // 128) * 128
    small_shape = small.shape
    coded, scale = (count, width), (8, count)
    any_space, vmem = pl.BlockSpec(memory_space=pl.ANY), pl.BlockSpec(memory_space=pltpu.VMEM)
    f32, i16 = jnp.float32, jnp.int16
    slots = max(columns - 1, 1)
    dma = pltpu.SemaphoreType.DMA
    landing = [
        ((slots, lines) + coded, i16),
        ((slots, lines) + scale, f32),
        ((2, lines) + coded, i16),
        ((2, lines) + scale, f32),
    ]
    near = shards * count * width <= 1 << 22
    out = pl.pallas_call(
        functools.partial(tail_kernel, shards, groups, columns, near, direct),
        in_specs=[any_space, any_space, any_space, vmem],
        out_specs=[vmem, any_space, any_space, any_space, vmem] + [any_space] * 4 + [vmem] + ([] if near else [any_space] * 4),
        out_shape=[
            jax.ShapeDtypeStruct((count, width), f32),
            jax.ShapeDtypeStruct((owned, depth), i16),
            jax.ShapeDtypeStruct((shards, groups, 8, padded), f32),
            jax.ShapeDtypeStruct((shards,) + small_shape, f32),
            jax.ShapeDtypeStruct((8, width), f32),
            jax.ShapeDtypeStruct((rows_y, piece, width), f32),
            jax.ShapeDtypeStruct((max(rows_y - 1, 1), piece, width), i16),
            jax.ShapeDtypeStruct((max(rows_y - 1, 1), 8, padded), f32),
            jax.ShapeDtypeStruct((max(groups - 1, 1),) + small_shape, f32),
            jax.ShapeDtypeStruct((shards - 1 + groups - 1, 8, width), f32),
        ]
        + ([] if near else [jax.ShapeDtypeStruct(*each) for each in landing]),
        scratch_shapes=([pltpu.VMEM(*each) for each in landing] if near else [])
        + [
            pltpu.VMEM((count, width), f32),
            pltpu.VMEM((lines,) + coded, i16),
            pltpu.VMEM((lines,) + scale, f32),
            pltpu.VMEM((lines,) + coded, i16),
            pltpu.VMEM((lines,) + scale, f32),
            pltpu.VMEM((16, 128) if near else coded, i16),
            pltpu.VMEM((8, 128) if near else scale, f32),
            pltpu.VMEM((max(count, padded), 128), f32),
            pltpu.VMEM((piece, width), f32),
            pltpu.VMEM((piece, width), f32),
            pltpu.VMEM((max(rows_y - 1, 1), piece, width), i16),
            pltpu.VMEM((max(rows_y - 1, 1), 8, padded), f32),
            pltpu.VMEM((piece, width), i16),
            pltpu.VMEM((8, padded), f32),
            pltpu.VMEM((piece, width), i16),
            pltpu.VMEM((8, padded), f32),
            pltpu.VMEM(small_shape, f32),
            pltpu.VMEM(small_shape, f32),
            pltpu.VMEM((8, width), f32),
            dma,
            dma((2, slots * lines)),
            dma((2, slots * lines)),
            dma((2, lines)),
            dma((2, 2, lines)),
            dma((rows_y,)),
            dma((rows_y,)),
            dma((2, max(rows_y - 1, 1))),
            dma((2, max(rows_y - 1, 1))),
            dma((piece // CHUNK, shards)),
            dma,
            dma((shards * groups,)),
            dma((shards * groups,)),
            dma((groups + shards,)),
            dma((groups + shards,)),
            dma((shards + groups,)),
            dma((shards + groups,)),
        ],
        compiler_params=pltpu.CompilerParams(
            collective_id=1, has_side_effects=True, vmem_limit_bytes=60 * 1024 * 1024
        ),
        cost_estimate=pl.CostEstimate(flops=0, bytes_accessed=400_000_000, transcendentals=0),
        name="tail_exchange",
    )(partial, weight_part, small, scaled_rows)
    return out[:5]


def nesterov(weight, gradient, moment, average, step_rate):
    decayed = gradient + weight_decay * weight
    new_moment = momentum_decay * moment + decayed
    new_weight = weight - step_rate * (decayed + momentum_decay * new_moment)
    new_average = average_decay * average + (1.0 - average_decay) * new_weight
    return (new_moment, new_weight, new_average)


def dot32(a, b, contract=((1,), (0,))):
    return lax.dot_general(a, b, (contract, ((), ())), preferred_element_type=jnp.float32)


def own_slice(value, index, width, axis):
    return lax.dynamic_slice_in_dim(value, index * width, width, axis)


def local(
    tokens,
    cotangent,
    lengths,
    deal_slot,
    in_weight,
    out_weight,
    small_params,
    in_moment,
    out_moment,
    small_moment,
    in_average,
    out_average,
    small_average,
):
    shards, groups = lax.axis_size("shard"), lax.axis_size("group")
    shard, group = lax.axis_index("shard"), lax.axis_index("group")
    rows, width = tokens.shape
    per = rows // shards
    total = rows * shards
    blocks = total // BLOCK
    heads = HEADS // shards
    inner = INNER // shards
    shared = SHARED // shards
    conv_flat, conv_bias, dt_bias, rate_log, skip_gain, norm_gain, pre_gain = unpack(small_params)
    taps = conv_flat.reshape(CONV, XBC)

    cols, depth, sends = in_weight.shape[1], in_weight.shape[0], out_weight.shape[1]
    direct = cols % CHUNK == 0 and depth % 128 == 0 and sends % 128 == 0 and per % CHUNK == 0
    direct = direct and (2 * inner + SHARED + HEADS) % (groups * CHUNK) == 0 and shared % CHUNK == 0
    bounds = jnp.cumsum(lengths[0])[:-1].astype(jnp.int32)
    seg_rows = segment_of(jnp.arange(total, dtype=jnp.int32), lengths[0])

    rank = jnp.sum((deal_slot[None, :] < deal_slot[:, None]).astype(jnp.int32), axis=1)
    sort_mat = (rank[None, :] == jnp.arange(rows)[:, None]).astype(jnp.bfloat16)
    sorted_slot = jnp.sum(jnp.where(sort_mat > 0, deal_slot[None, :], 0), axis=1)
    r_in = lax.rsqrt(jnp.mean(tokens * tokens, axis=1, keepdims=True) + eps_norm)
    normed_low = (tokens * r_in * pre_gain[None, :]).astype(jnp.bfloat16)
    x_sorted = dot32(sort_mat, normed_low).astype(jnp.bfloat16).reshape(blocks, per, width)
    c_sorted = dot32(sort_mat, cotangent.astype(jnp.bfloat16)).astype(jnp.bfloat16).reshape(blocks, per, width)
    in_turned = in_weight.astype(jnp.bfloat16).T
    out_cast = out_weight.astype(jnp.bfloat16)

    if direct:
        slot_own = jnp.pad(sorted_slot, (0, 1024 - rows)).reshape(8, 128)
        x_all, in_low, out_low, slot_all = front_exchange(shards, groups, x_sorted, in_turned, out_cast, slot_own)
        x_all = x_all.reshape(blocks, BLOCK, width)
        slot_all = slot_all.reshape(shards, -1)[:, :rows]
    else:
        x_all = lax.all_gather(x_sorted, "shard").transpose(1, 0, 2, 3).reshape(blocks, BLOCK, width)
        slot_all = lax.all_gather(sorted_slot, "shard")
        part = depth // groups
        pieces = lax.all_to_all(in_turned.reshape(cols, groups, part), "group", 1, 0)
        pieces = pieces.reshape(groups * cols, part)

        def cut(lo, each):
            return pieces[lo : lo + each * shards].reshape(shards, each, part)

        spread = jnp.broadcast_to(pieces[None, 2 * INNER :], (shards, SHARED + HEADS, part))
        got = jnp.concatenate([cut(0, inner), cut(INNER, inner), spread], axis=1)
        got = lax.all_gather(lax.all_to_all(got, "shard", 0, 0), "group")
        in_low = got.transpose(2, 1, 0, 3).reshape(-1, width)
        out_low = lax.all_gather(out_cast, "group", axis=1, tiled=True)
    slot_blk = slot_all.reshape(shards, blocks, per).transpose(1, 0, 2).reshape(blocks, 1, BLOCK)
    slot_blk = slot_blk - jnp.arange(blocks, dtype=jnp.int32)[:, None, None] * BLOCK

    taps_v = own_slice(taps[:, :INNER], shard, inner, 1)
    taps_all = jnp.concatenate([taps_v, taps[:, INNER:]], axis=1)
    bias_all = jnp.concatenate([own_slice(conv_bias[:INNER], shard, inner, 0), conv_bias[INNER:]])[None, :]
    skip_wide = jnp.repeat(own_slice(skip_gain, shard, heads, 0), HDIM)[None, :]
    gain_own = own_slice(norm_gain, shard, inner, 0)[None, :]
    padding = max(TAIL - heads, 0)
    rate = jnp.pad(-jnp.exp(own_slice(rate_log, shard, heads, 0)), (0, padding))[:, None]
    normed, projected, pre, mixed, states, dt_cols, dt_raw, c_all = mixer_forward(
        shards, bounds, slot_blk, x_all, in_low, taps_all, bias_all, dt_bias[None, :], rate, skip_wide, c_sorted
    )
    out_late, mixed = lax.optimization_barrier((out_cast, mixed))
    out_full = lax.all_gather(out_late, "shard", axis=0, tiled=True)
    out_full = lax.all_gather(out_full, "group", axis=1, tiled=True)
    conv_bc = projected[:, 2 * inner : 2 * inner + SHARED]
    cot_low, d_out, sums = pack_cotangent(
        shards, slot_blk, c_all.reshape(blocks, BLOCK, width), out_low, mixed, projected, gain_own
    )

    d_cols, d_bc, d_dt, grads, rate_terms, grad_out, no_rows, home_late = mixer_backward(
        shards, bounds, slot_blk, pre, mixed, projected, d_out, sums, states, dt_cols, cot_low,
        taps_v, rate, skip_wide, gain_own,
    )
    grad_out = lax.psum_scatter(grad_out, "group", scatter_dimension=1, tiled=True)

    d_dtraw = d_dt[:heads].T * jax.nn.sigmoid(dt_raw[:, :heads])
    grad_dtb = jnp.sum(d_dtraw, axis=0)
    grad_rate = jnp.sum(rate_terms[:heads], axis=1)
    grad_skip = jnp.sum(grads[6].reshape(heads, HDIM), axis=1)
    _, pull_bc = jax.vjp(
        lambda c, t, b: convolve(c, seg_rows, t, b),
        own_slice(conv_bc, shard, shared, 1),
        own_slice(taps[:, INNER:], shard, shared, 1),
        own_slice(conv_bias[INNER:], shard, shared, 0),
    )
    d_conv_bc, grad_taps_bc, grad_bias_bc = pull_bc(d_bc.T)
    rest = 128 - shared - heads
    d_rest = jnp.concatenate([d_conv_bc, d_dtraw, jnp.zeros((total, rest), jnp.float32)], axis=1)
    in_rest = jnp.concatenate(
        [
            own_slice(in_low[2 * inner : 2 * inner + SHARED], shard, shared, 0),
            own_slice(in_low[2 * inner + SHARED :], shard, heads, 0),
            jnp.zeros((rest, width), jnp.bfloat16),
        ]
    )
    partial, weight_part, home = project_back(
        slot_blk, d_cols, d_rest.astype(jnp.bfloat16), normed, in_low, in_rest, no_rows, shards
    )

    home = jnp.concatenate([home, home_late], axis=1)
    home = home.reshape(shards, rows, inner).transpose(1, 0, 2).reshape(rows, INNER)
    home = dot32(sort_mat, home, ((0,), (0,))).astype(jnp.bfloat16)
    block_out = tokens + dot32(home, out_full)
    dt_part = weight_part[2 * inner + shared : 2 * inner + shared + heads]

    mine = [
        grads[:CONV].reshape(-1),
        grad_taps_bc.reshape(-1),
        grads[4],
        grad_bias_bc,
        grad_dtb,
        grad_rate,
        grad_skip,
        grads[5],
    ]
    if direct:
        mine.append(dt_part.reshape(-1))
    extents = [piece.shape[0] for piece in mine]
    mine = jnp.concatenate(mine)
    mine = jnp.pad(mine, (0, -mine.shape[0] % 1024)).reshape(-1, 128)
    x_scaled = jnp.dot(sort_mat.astype(jnp.float32), tokens * r_in, precision=lax.Precision.HIGHEST)
    d_normed, grad_in, grad_marks, small_all, gain_all = tail_exchange(
        shards, groups, partial.reshape(shards, rows, width), weight_part, mine, x_scaled, cols, depth, direct
    )
    d_normed = jnp.dot(sort_mat.T.astype(jnp.float32), d_normed, precision=lax.Precision.HIGHEST)
    d_scaled = pre_gain[None, :] * d_normed
    inside = jnp.mean(tokens * d_scaled, axis=1, keepdims=True)
    input_grad = cotangent + r_in * (d_scaled - tokens * (r_in * r_in) * inside)
    grad_pre = jnp.sum(gain_all, axis=0)

    mine = small_all.reshape(shards, -1)
    found, offset = [], 0
    for extent in extents:
        found.append(mine[:, offset : offset + extent])
        offset = offset + extent
    if direct:
        dt_part = own_slice(found.pop().reshape(HEADS, width), shard, depth, 1)
        steps = grad_marks[:, :, 0, : piece_rows(shards, groups)].reshape(shards, -1)
        steps = jnp.concatenate(
            [
                steps[:, :inner].reshape(-1),
                steps[:, inner : 2 * inner].reshape(-1),
                steps[:, 2 * inner : 2 * inner + shared].reshape(-1),
                jnp.zeros((HEADS,), jnp.float32),
            ]
        )
        grad_in = grad_in.astype(jnp.float32) * own_slice(steps, group, cols, 0)[:, None]
        last = jnp.concatenate([grad_in[: cols - HEADS], dt_part])
        grad_in = jnp.where(group == groups - 1, last, grad_in)
    else:
        used = 2 * inner + shared + heads
        grad_in = weight_part[:used].reshape(used, shards, groups, part).transpose(2, 1, 0, 3)
        grad_in = lax.psum_scatter(grad_in, "group", scatter_dimension=0)
        grad_in = lax.all_to_all(grad_in, "shard", 0, 0)

        def join(lo, each):
            return grad_in[:, lo : lo + each].reshape(shards * each, part)

        grad_in = jnp.concatenate(
            [
                join(0, inner),
                join(inner, inner),
                join(2 * inner, shared),
                join(2 * inner + shared, heads),
            ]
        )
        grad_in = lax.all_to_all(grad_in.reshape(groups, cols, part), "group", 0, 0)
        grad_in = grad_in.transpose(1, 0, 2).reshape(cols, depth)

    def taps_of(piece):
        return piece.reshape(shards, CONV, -1).transpose(1, 0, 2).reshape(CONV, -1)

    grad_taps = jnp.concatenate([taps_of(found[0]), taps_of(found[1])], axis=1).reshape(-1)
    grad_small = jnp.concatenate([grad_taps] + [piece.reshape(-1) for piece in found[2:]] + [grad_pre])
    in_new = nesterov(in_weight.T, grad_in, in_moment.T, in_average.T, rate_in)
    in_new = tuple(value.T for value in in_new)
    out_new = nesterov(out_weight, grad_out, out_moment, out_average, rate_out)
    small_new = nesterov(small_params, grad_small, small_moment, small_average, rate_small)
    return (block_out, input_grad) + in_new + out_new + small_new


def solution(mesh):
    rows = P(("group", "shard"), None)
    tile = P("shard", "group")
    return jax.shard_map(
        local,
        mesh=mesh,
        in_specs=(
            rows,
            rows,
            P("group", None),
            P(("group", "shard")),
            tile,
            tile,
            P(),
            tile,
            tile,
            P(),
            tile,
            tile,
            P(),
        ),
        out_specs=(rows, rows, tile, tile, tile, tile, tile, tile, P(), P(), P()),
        check_vma=False,
    )
```

```python
import functools

import jax
import jax.numpy as jnp
from jax import lax
from jax.experimental import pallas as pl
from jax.experimental.pallas import tpu as pltpu
from jax.sharding import PartitionSpec as P

D = 2048
HEADS = 64
HDIM = 64
STATE = 128
CONV = 4
BLOCK = 256
INNER = 4096
XBC = 4352
SHARED = 2 * STATE
TAIL = 8
CHUNK = 16
MESH = pl.DeviceIdType.MESH


eps_norm = 1e-05
momentum_decay = 0.9
weight_decay = 0.01
average_decay = 0.99
rate_in = 0.0001
rate_out = 3e-05
rate_small = 0.001


def unpack(packed_small):
    extents = [CONV * XBC, XBC, HEADS, HEADS, HEADS, INNER, D]
    pieces = []
    offset = 0
    for extent in extents:
        pieces.append(packed_small[offset : offset + extent])
        offset = offset + extent
    return pieces


def segment_of(positions, lengths_row):
    bounds = jnp.cumsum(lengths_row)[:-1]
    inside = jnp.sum((positions[:, None] >= bounds[None, :]).astype(jnp.int32), axis=1)
    return jnp.where(positions < 0, -1, inside)


def convolve(conv_rows, seg_rows, conv_taps, conv_bias):
    row_count, width = conv_rows.shape
    extended = jnp.concatenate([jnp.zeros((CONV - 1, width), conv_rows.dtype), conv_rows], axis=0)
    seg_ext = jnp.concatenate([jnp.full((CONV - 1,), -1, jnp.int32), seg_rows], axis=0)
    conv_sum = jnp.zeros_like(conv_rows) + conv_bias[None, :]
    for tap_index in range(CONV):
        same_seq = (seg_ext[tap_index : tap_index + row_count] == seg_rows)[:, None]
        conv_sum = conv_sum + jnp.where(
            same_seq,
            extended[tap_index : tap_index + row_count] * conv_taps[tap_index][None, :],
            0.0,
        )
    return jax.nn.silu(conv_sum)


def split(value):
    high = value.astype(jnp.bfloat16)
    return high, (value - high.astype(jnp.float32)).astype(jnp.bfloat16)


def dots(a, b, contract):
    return lax.dot_general(a, b, (contract, ((), ())), preferred_element_type=jnp.float32)


def dot3(a, b, contract=((1,), (0,))):
    a = a if isinstance(a, tuple) else split(a)
    b = b if isinstance(b, tuple) else split(b)
    return dots(a[0], b[0], contract) + (dots(a[0], b[1], contract) + dots(a[1], b[0], contract))


NT = ((1,), (1,))


def dot_wide(a, wide):
    high, low = split(a)
    lanes = wide.shape[1] // 2
    plain = ((1,), (0,))
    first = dots(high, wide, plain)
    return first[:, :lanes] + (first[:, lanes:] + dots(low, wide[:, :lanes], plain))


def beside(first, second, own):
    moved = pltpu.roll(second.astype(jnp.float32), HDIM, 1).astype(jnp.bfloat16)
    return jnp.where(own, first, moved)


def head_sums(value, marks):
    high = value.astype(jnp.bfloat16)
    rest = value - high.astype(jnp.float32)
    mid = rest.astype(jnp.bfloat16)
    low = (rest - mid.astype(jnp.float32)).astype(jnp.bfloat16)
    return dots(marks, high, NT) + (dots(marks, mid, NT) + dots(marks, low, NT))


def widen(columns, heads):
    rows = columns.shape[0]
    low_half = lax.broadcasted_iota(jnp.int32, (rows, 2 * HDIM), 1) < HDIM
    return jnp.concatenate(
        [
            jnp.where(low_half, columns[:, h : h + 1], columns[:, h + 1 : h + 2])
            for h in range(0, heads, 2)
        ],
        axis=1,
    )


def running_sum(value, reverse=False):
    lane = lax.broadcasted_iota(jnp.int32, value.shape, 1)
    count = value.shape[1]
    step = 1
    while step < count:
        if reverse:
            value = value + jnp.where(lane < count - step, pltpu.roll(value, count - step, 1), 0.0)
        else:
            value = value + jnp.where(lane >= step, pltpu.roll(value, step, 1), 0.0)
        step *= 2
    return value


def sequence_of(positions, bounds):
    inside = jnp.where(positions >= bounds[0], 1, 0) + jnp.where(positions >= bounds[1], 1, 0)
    return jnp.where(positions < 0, -1, inside)


def block_facts(block, bounds, dt_t, rate):
    start = block * BLOCK
    seg_col = sequence_of(start + lax.broadcasted_iota(jnp.int32, (BLOCK, 1), 0), bounds)
    seg_row = sequence_of(start + lax.broadcasted_iota(jnp.int32, (1, BLOCK), 1), bounds)
    before = sequence_of(start - 1 + lax.broadcasted_iota(jnp.int32, (1, 1), 1), bounds)
    last = sequence_of(start + BLOCK - 1 + lax.broadcasted_iota(jnp.int32, (1, 1), 1), bounds)
    run_t = running_sum(dt_t * rate)
    run = run_t.T
    final = run[BLOCK - 1 :, :]
    carried = jnp.where(seg_col == before, jnp.exp(run), 0.0)
    tail = jnp.where(seg_col == last, jnp.exp(final - run), 0.0)
    keep = jnp.where(last == before, jnp.exp(final), 0.0)
    return seg_col, seg_row, run_t, run, carried, tail, keep


def barrier_with(peers):
    barrier = pltpu.get_barrier_semaphore()
    for peer in peers:
        pl.semaphore_signal(barrier, inc=1, device_id=peer, device_id_type=MESH)
    pl.semaphore_wait(barrier, len(peers))


def remote(src, dst, sends, recvs, **where):
    return pltpu.make_async_remote_copy(
        src_ref=src, dst_ref=dst, send_sem=sends, recv_sem=recvs, device_id=where, device_id_type=MESH
    )


def place_of_rows(slots):
    count = slots.shape[1]
    return (lax.broadcasted_iota(jnp.int32, (BLOCK, count), 0) == slots).astype(jnp.bfloat16)


def grid_columns(shards):
    columns = 1
    while 2 * (2 * columns) * (2 * columns) <= shards:
        columns *= 2
    return columns if shards % columns == 0 else 1


def whole(shape):
    return pl.BlockSpec(shape, lambda *_: (0,) * len(shape))


def row_gather(shards, columns, own, gathered, local_sem, sends, recvs):
    shard = lax.axis_index("shard")
    lines = shards // columns
    z, x = shard // columns, shard % columns

    def line_copy(source, way, first=False):
        at = source * columns + x
        peer = jnp.clip(z + 1 - 2 * way, 0, lines - 1) * columns + x
        rows = own if first else gathered.at[:, at]
        return remote(rows, gathered.at[:, at], sends.at[way, source], recvs.at[at], shard=peer)

    def wide_copy(source, hop, first=False):
        at = source * columns + x
        peer = z * columns + (x + hop) % columns
        rows = own if first else gathered.at[:, at]
        return remote(rows, gathered.at[:, at], sends.at[1 + hop, source], recvs.at[at], shard=peer)

    def pass_on(source, ways, first=False):
        for way in ways:
            @pl.when(z < lines - 1 if way == 0 else z > 0)
            def _():
                line_copy(source, way, first).start()

        for hop in range(1, columns):
            wide_copy(source, hop, first).start()

    here = pltpu.make_async_copy(own, gathered.at[:, shard], local_sem)

    def begin():
        pass_on(z, (0, 1), True)
        here.start()

    def hop(step):
        @pl.when(z - step >= 0)
        def _():
            line_copy(z - step, 0).wait_recv()
            pass_on(z - step, (0,))

        @pl.when(z + step < lines)
        def _():
            line_copy(z + step, 1).wait_recv()
            pass_on(z + step, (1,))

    def end():
        here.wait()
        for step in range(1, columns):
            peer = z * columns + (x + step) % columns
            for source in range(lines):
                at = source * columns + (x + step) % columns
                remote(gathered.at[:, at], gathered.at[:, at], sends.at[1 + step, source], recvs.at[at], shard=peer).wait_recv()
        for source in range(lines):
            for step in range(1, columns):
                wide_copy(source, step).wait_send()

            @pl.when((z < lines - 1) & (source <= z))
            def _():
                line_copy(source, 0).wait_send()

            @pl.when((z > 0) & (source >= z))
            def _():
                line_copy(source, 1).wait_send()

    return begin, hop, end


def gather_semaphores(shards, columns):
    dma = pltpu.SemaphoreType.DMA
    return [
        dma,
        dma((1 + columns, shards // columns)),
        dma((shards,)),
    ]


def softplus(value):
    small = jnp.exp(-jnp.abs(value))
    ratio = small / (2.0 + small)
    square = ratio * ratio
    series = jnp.full_like(value, 1.0 / 15.0)
    for power in (13, 11, 9, 7, 5, 3, 1):
        series = series * square + 1.0 / power
    return jnp.maximum(value, 0.0) + 2.0 * ratio * series


def pick_columns(value, marks):
    high = value.astype(jnp.bfloat16)
    rest = value - high.astype(jnp.float32)
    mid = rest.astype(jnp.bfloat16)
    low = (rest - mid.astype(jnp.float32)).astype(jnp.bfloat16)
    plain = ((1,), (0,))
    return dots(high, marks, plain) + (dots(mid, marks, plain) + dots(low, marks, plain))


def forward_kernel(
    heads, shards, columns, bounds, slots, rows_in, weight, taps, bias, dt_bias, rate, skip, cot_own,
    packed, product, pre_out, mixed_out, state_out, dt_out, raw_out, cot_all,
    ext, state, *gather_sems,
):
    block = pl.program_id(0)
    blocks = cot_own.shape[0]
    inner = heads * HDIM
    shard = lax.axis_index("shard")
    begin, hop, end = row_gather(shards, columns, cot_own, cot_all, *gather_sems)
    hops = range(1, shards // columns)

    @pl.when(block == 0)
    def _():
        barrier_with([{"shard": (shard + step) % shards} for step in range(1, shards)])
        begin()
        ext[:TAIL, :] = jnp.zeros((TAIL, ext.shape[1]), jnp.float32)
        state[...] = jnp.zeros_like(state)

    for step in hops:
        if (7 * step + 1) // 2 < blocks:
            pl.when(block == (7 * step + 1) // 2)(functools.partial(hop, step))

    normed = dots(place_of_rows(slots[0]), rows_in[0], ((1,), (0,))).astype(jnp.bfloat16)
    packed[...] = normed
    product[...] = dots(normed, weight[...], NT)
    head = lax.broadcasted_iota(jnp.int32, (HEADS, 128), 0)
    lane = lax.broadcasted_iota(jnp.int32, (HEADS, 128), 1)
    marks = ((head == shard * heads + lane) & (lane < heads)).astype(jnp.bfloat16)
    raw = pick_columns(product[:, 2 * inner + SHARED :] + dt_bias[...], marks)
    raw_out[...] = raw
    dt = softplus(raw)
    dt_out[...] = dt

    bounds = (bounds[0], bounds[1])
    dt_t = dt.T[: rate.shape[0], :]
    seg_col, seg_row, run_t, run, carried, tail, keep = block_facts(block, bounds, dt_t, rate[...])
    ext[TAIL:, :] = product[:, inner : 2 * inner + SHARED]
    place = block * BLOCK + lax.broadcasted_iota(jnp.int32, (BLOCK, 1), 0)
    pre = bias[...] + taps[CONV - 1 : CONV, :] * ext[TAIL:, :]
    for back in range(1, CONV):
        same = sequence_of(place - back, bounds) == seg_col
        moved = ext[TAIL - back : TAIL - back + BLOCK, :]
        pre = pre + jnp.where(same, moved, 0.0) * taps[CONV - 1 - back : CONV - back, :]
    ext[:TAIL, :] = ext[BLOCK:, :]
    pre_out[...] = pre
    conv = pre / (1.0 + jnp.exp(-pre))
    values, b_rows, c_rows = conv[:, :inner], conv[:, inner : inner + STATE], conv[:, inner + STATE :]
    fed = values * widen(dt, heads)
    rows = lax.broadcasted_iota(jnp.int32, (BLOCK, BLOCK), 0)
    cols = lax.broadcasted_iota(jnp.int32, (BLOCK, BLOCK), 1)
    allowed = (seg_col == seg_row) & (rows >= cols)
    b_parts, c_parts = split(b_rows), split(c_rows)
    scores = jnp.where(allowed, dot3(c_parts, b_parts, NT), 0.0)
    old = state[...]
    state_out[0] = old
    output = widen(carried, heads) * dot3(c_parts, old)
    low_half = lax.broadcasted_iota(jnp.int32, (BLOCK, 2 * HDIM), 1) < HDIM
    inside = []
    for h in range(0, heads, 2):
        pair = jnp.concatenate(split(fed[:, h * HDIM : (h + 2) * HDIM]), axis=1)
        found = []
        for k in (h, h + 1):
            mixing = jnp.exp(jnp.minimum(run[:, k : k + 1] - run_t[k : k + 1, :], 0.0)) * scores
            found.append(dot_wide(mixing, pair))
        inside.append(jnp.where(low_half, found[0], found[1]))
    mixed = output + jnp.concatenate(inside, axis=1) + skip[...] * values
    mixed_out[...] = mixed
    state[...] = widen(keep, heads) * old + dot3(b_rows.T, widen(tail, heads) * fed)

    @pl.when(block == blocks - 1)
    def _():
        for step in hops:
            if (7 * step + 1) // 2 >= blocks:
                hop(step)
        end()


def cotangent_kernel(
    shards, slots, rows_in, weight, mixed, gate, gain,
    packed, product, sums_out, own_sums, sums_in, sums_send, sums_recv,
):
    block = pl.program_id(0)
    shard = lax.axis_index("shard")

    @pl.when(block == 0)
    def _():
        barrier_with([{"shard": (shard + step) % shards} for step in range(1, shards)])

    cot = dots(place_of_rows(slots[0]), rows_in[0], ((1,), (0,))).astype(jnp.bfloat16)
    packed[...] = cot
    d_out = dots(cot, weight[...], NT)
    product[...] = d_out
    gate_now = gate[...]
    gated = mixed[...] * (gate_now / (1.0 + jnp.exp(-gate_now)))
    squares = jnp.sum(gated * gated, axis=1, keepdims=True)
    products = jnp.sum(gated * gain[...] * d_out, axis=1, keepdims=True)
    lane = lax.broadcasted_iota(jnp.int32, (BLOCK, 128), 1)
    both = jnp.where(lane == 0, squares, jnp.where(lane == 1, products, 0.0))
    here = pl.ds(pl.multiple_of(block * BLOCK, BLOCK), BLOCK)
    own_sums[:, here] = both.T[:8, :]

    def push(step, at):
        return remote(
            own_sums.at[:, at], sums_in.at[step - 1, :, at], sums_send.at[step], sums_recv.at[step],
            shard=(shard + step) % shards,
        )

    for step in range(1, shards):
        push(step, here).start()

    @pl.when(block == pl.num_programs(0) - 1)
    def _():
        everything = pl.ds(0, own_sums.shape[1])
        for step in range(1, shards):
            push(step, everything).wait()
        found = own_sums[...]
        for step in range(1, shards):
            found = found + sums_in[step - 1]
        sums_out[...] = found * (1.0 / INNER)


def backward_kernel(
    heads, blocks, shards, columns, bounds, slots, pre, mixed, gate, d_out, conv_v, sums, state_in, dt_cols, cot,
    taps, rate, skip, gain, marks, out_own,
    d_cols, d_bc, d_dt, grads, grad_rate, grad_out, no_rows, home, out_all,
    ext, carry, bc_rows, bc_wide, bc_sum, bc_in, late_rows, wide_send, wide_recv, bc_send, bc_recv, home_send, home_recv, local_sem, *gather_sems,
):
    step = pl.program_id(0)
    block = blocks - 1 - step
    inner = heads * HDIM
    shard = lax.axis_index("shard")
    shared = SHARED // shards
    lines = shards // columns
    z, x = shard // columns, shard % columns
    begin, hop, end = row_gather(shards, columns, out_own, out_all, *gather_sems)
    hops = range(1, shards // columns)

    @pl.when(step == 0)
    def _():
        barrier_with([{"shard": (shard + turn) % shards} for turn in range(1, shards)])
        begin()
        ext[BLOCK:, :] = jnp.zeros((TAIL, ext.shape[1]), jnp.float32)
        carry[...] = jnp.zeros_like(carry)
        grads[...] = jnp.zeros_like(grads)
        grad_rate[...] = jnp.zeros_like(grad_rate)
        grad_out[...] = jnp.zeros_like(grad_out)

    for turn in hops:
        if 2 * turn < blocks:
            pl.when(step == 2 * turn)(functools.partial(hop, turn))

    bounds = (bounds[0], bounds[1])
    dt = dt_cols[...]
    dt_t = dt.T[: rate.shape[0], :]
    seg_col, seg_row, run_t, run, carried, tail, keep = block_facts(block, bounds, dt_t, rate[...])
    sums_cols = sums[...].T
    r_out = lax.rsqrt(sums_cols[:, 0:1] + 1e-05)
    inside = sums_cols[:, 1:2]
    gate_now = gate[...]
    gate_sig = 1.0 / (1.0 + jnp.exp(-gate_now))
    act = gate_now * gate_sig
    mixed_now = mixed[...]
    gated = mixed_now * act
    d_out_now = d_out[...]
    normed_out = (gated * r_out * gain[...]).astype(jnp.bfloat16)
    to_home = dots(place_of_rows(slots[0]), normed_out, ((0,), (0,)))
    per = BLOCK // shards
    if per % 16 == 0:
        no_rows[0] = to_home.astype(jnp.bfloat16).reshape(shards, per, inner)
    else:
        for turn in range(shards):
            no_rows[0, turn] = to_home[turn * per : (turn + 1) * per].astype(jnp.bfloat16)
    half = home.shape[1]

    def push_home(turn, at):
        peer = (shard + turn) % shards
        return remote(late_rows.at[at, peer], home.at[shard, at], home_send.at[turn], home_recv.at[turn], shard=peer)

    @pl.when(step < blocks - half)
    def _():
        late_rows[block - half] = no_rows[0]
        for turn in range(1, shards):
            push_home(turn, pl.ds(block - half, 1)).start()
    grad_out[...] += dots(normed_out, cot[...], ((0,), (0,)))
    d_gated = r_out * (gain[...] * d_out_now - gated * (r_out * r_out) * inside)
    dy = d_gated * act
    d_cols[:, :inner] = (d_gated * mixed_now * (gate_sig * (1.0 + gate_now * (1.0 - gate_sig)))).astype(jnp.bfloat16)
    grads[5:6, :] += jnp.sum(gated * r_out * d_out_now, axis=0, keepdims=True)
    pre_now = pre[...]
    sig = 1.0 / (1.0 + jnp.exp(-pre_now))
    conv = pre_now * sig
    values, b_rows, c_rows = conv[:, :inner], conv[:, inner : inner + STATE], conv[:, inner + STATE :]
    grads[6:7, :] += jnp.sum(dy * values, axis=0, keepdims=True)
    dt_wide = widen(dt, heads)
    fed = values * dt_wide
    old, after = state_in[0], carry[...]
    b_parts, c_parts, old_parts, after_parts = split(b_rows), split(c_rows), split(old), split(after)
    carried_wide, tail_wide, keep_wide = widen(carried, heads), widen(tail, heads), widen(keep, heads)
    rows = lax.broadcasted_iota(jnp.int32, (BLOCK, BLOCK), 0)
    cols = lax.broadcasted_iota(jnp.int32, (BLOCK, BLOCK), 1)
    allowed = (seg_col == seg_row) & (cols >= rows)
    scores_t = jnp.where(allowed, dot3(b_parts, c_parts, NT), 0.0)
    low_half = lax.broadcasted_iota(jnp.int32, (BLOCK, 2 * HDIM), 1) < HDIM
    d_scores_t = jnp.zeros((BLOCK, BLOCK), jnp.float32)
    d_fed, row_terms, col_terms = [], [], []
    for h in range(0, heads, 2):
        fed_pair = fed[:, h * HDIM : (h + 2) * HDIM]
        fed_high, fed_low = split(fed_pair)
        dy_high, dy_low = split(dy[:, h * HDIM : (h + 2) * HDIM])
        dy_wide = jnp.concatenate([dy_high, dy_low], axis=1)
        found = []
        for k in (h, h + 1):
            own = low_half if k == h else jnp.logical_not(low_half)
            left = jnp.concatenate(
                [beside(fed_high, fed_low, own), jnp.where(own, fed_high, 0.0).astype(jnp.bfloat16)], axis=1
            )
            right = jnp.concatenate([beside(dy_high, dy_high, own), dy_low], axis=1)
            d_mixing = dots(left, right, NT)
            decay = jnp.exp(jnp.minimum(run_t[k : k + 1, :] - run[:, k : k + 1], 0.0))
            mixing = decay * scores_t
            d_scores_t = d_scores_t + decay * d_mixing
            flow = mixing * d_mixing
            row_terms.append(jnp.sum(flow, axis=0, keepdims=True))
            col_terms.append(jnp.sum(flow, axis=1, keepdims=True))
            found.append(dot_wide(mixing, dy_wide))
        d_fed.append(jnp.where(low_half, found[0], found[1]))
    d_scores_t = split(jnp.where(allowed, d_scores_t, 0.0))
    fed_tail = fed * tail_wide
    dy_carried = dy * carried_wide
    d_fed_out = tail_wide * dot3(b_parts, after_parts)
    d_fed = jnp.concatenate(d_fed, axis=1) + d_fed_out
    dy_parts, tail_parts = split(dy_carried), split(fed_tail)
    here = pl.ds(pl.multiple_of(block * BLOCK, BLOCK), BLOCK)
    bc_now = jnp.concatenate(
        [
            (dot3(d_scores_t, c_parts) + dot3(tail_parts, after_parts, NT)).T,
            (dot3(d_scores_t, b_parts, ((0,), (0,))) + dot3(dy_parts, old_parts, NT)).T,
        ],
        axis=0,
    )
    bc_rows[:, :, :, here] = bc_now.reshape(lines, columns, shared, BLOCK)

    def at_step(turn):
        return pl.ds(pl.multiple_of((blocks - 1 - turn) * BLOCK, BLOCK), BLOCK)

    def push_wide(turn, hop):
        to = (x + hop) % columns
        return remote(
            bc_rows.at[:, to, :, at_step(turn)], bc_wide.at[hop - 1, :, :, at_step(turn)],
            wide_send.at[hop - 1, turn], wide_recv.at[hop - 1, turn], shard=z * columns + to,
        )

    def push_line(hop, at):
        to = (z + hop) % lines
        return remote(bc_sum.at[to, :, at], bc_in.at[hop - 1, :, at], bc_send.at[hop], bc_recv.at[hop], shard=to * columns + x)

    def add_wide(turn):
        found = bc_rows[:, x, :, at_step(turn)]
        for hop in range(1, columns):
            push_wide(turn, hop).wait_recv()
            found = found + bc_wide[hop - 1, :, :, at_step(turn)]
        bc_sum[:, :, at_step(turn)] = found
        for hop in range(1, lines):
            push_line(hop, at_step(turn)).start()

    for hop_x in range(1, columns):
        push_wide(step, hop_x).start()

    lag = min(3, blocks - 1)

    @pl.when(step >= lag)
    def _():
        add_wide(step - lag)

    head_count = dt_t.shape[0]
    pad = [jnp.zeros((1, BLOCK), jnp.float32)] * (head_count - heads)
    pad_col = [jnp.zeros((BLOCK, 1), jnp.float32)] * (head_count - heads)
    d_run = jnp.concatenate(row_terms + pad, axis=0) - jnp.concatenate(col_terms + pad_col, axis=1).T
    d_run = d_run + head_sums(dy_carried * dot3(c_parts, old_parts), marks[...])
    leaving = head_sums(fed * d_fed_out, marks[...])
    kept = jnp.sum(old * after, axis=0, keepdims=True) * keep_wide
    kept = jnp.sum(marks[...].astype(jnp.float32) * kept, axis=1, keepdims=True)
    at_end = lax.broadcasted_iota(jnp.int32, (head_count, BLOCK), 1) == BLOCK - 1
    total = jnp.sum(leaving, axis=1, keepdims=True) + kept
    d_run = d_run - leaving + jnp.where(at_end, total, 0.0)
    d_log = running_sum(d_run, reverse=True)
    d_dt[...] = d_log * rate[...] + head_sums(values * d_fed, marks[...])
    grad_rate[...] += d_log * (dt_t * rate[...])
    carry[...] = keep_wide * after + dot3(c_rows.T, dy_parts)
    pre_v, sig_v = pre_now[:, :inner], sig[:, :inner]
    d_values = dt_wide * d_fed + skip[...] * dy
    d_pre = d_values * (sig_v * (1.0 + pre_v * (1.0 - sig_v)))
    ext[:BLOCK, :] = d_pre
    place = block * BLOCK + lax.broadcasted_iota(jnp.int32, (BLOCK, 1), 0)
    conv_in = conv_v[...]
    d_conv = taps[CONV - 1 : CONV, :] * d_pre
    grads[CONV - 1 : CONV, :] += jnp.sum(conv_in * d_pre, axis=0, keepdims=True)
    grads[CONV : CONV + 1, :] += jnp.sum(d_pre, axis=0, keepdims=True)
    for ahead in range(1, CONV):
        same = sequence_of(place + ahead, bounds) == seg_col
        moved = jnp.where(same, ext[ahead : ahead + BLOCK, :], 0.0)
        d_conv = d_conv + taps[CONV - 1 - ahead : CONV - ahead, :] * moved
        grads[CONV - 1 - ahead : CONV - ahead, :] += jnp.sum(conv_in * moved, axis=0, keepdims=True)
    ext[BLOCK:, :] = ext[:TAIL, :]
    d_cols[:, inner:] = d_conv.astype(jnp.bfloat16)

    @pl.when(step == blocks - 1)
    def _():
        everything = pl.ds(0, bc_sum.shape[2])
        for turn in range(blocks - lag, blocks):
            add_wide(turn)
        for turn in hops:
            if 2 * turn >= blocks:
                hop(turn)
        end()
        here = pltpu.make_async_copy(late_rows.at[:, shard], home.at[shard], local_sem)
        here.start()
        for turn in range(1, lines):
            push_line(turn, everything).wait()
        found = bc_sum[z]
        for turn in range(1, lines):
            found = found + bc_in[turn - 1]
        d_bc[...] = found
        for turn in range(1, shards):
            push_home(turn, pl.ds(0, half)).wait()
        here.wait()
        for turn in range(blocks):
            for hop_x in range(1, columns):
                push_wide(turn, hop_x).wait_send()


def mixer_forward(shards, bounds, slots, rows_in, weight, taps, bias, dt_bias, rate, skip, cot_own):
    blocks, _, width = rows_in.shape
    columns = grid_columns(shards)
    total, inner, kept = blocks * BLOCK, INNER // shards, weight.shape[0]
    heads = inner // HDIM
    f32, bf16, any_space = jnp.float32, jnp.bfloat16, pl.BlockSpec(memory_space=pl.ANY)

    def block_of(lanes):
        return pl.BlockSpec((BLOCK, lanes), lambda i: (i, 0))

    return pl.pallas_call(
        functools.partial(forward_kernel, heads, shards, columns),
        grid=(blocks,),
        in_specs=[
            pl.BlockSpec(memory_space=pltpu.SMEM),
            pl.BlockSpec((1, 1, BLOCK), lambda i: (i, 0, 0)),
            pl.BlockSpec((1, BLOCK, width), lambda i: (i, 0, 0)),
            whole(weight.shape),
            whole(taps.shape),
            whole(bias.shape),
            whole(dt_bias.shape),
            whole(rate.shape),
            whole(skip.shape),
            any_space,
        ],
        out_specs=[
            block_of(width),
            block_of(kept),
            block_of(inner + SHARED),
            block_of(inner),
            pl.BlockSpec((1, STATE, inner), lambda i: (i, 0, 0)),
            block_of(128),
            block_of(128),
            any_space,
        ],
        out_shape=[
            jax.ShapeDtypeStruct((total, width), bf16),
            jax.ShapeDtypeStruct((total, kept), f32),
            jax.ShapeDtypeStruct((total, inner + SHARED), f32),
            jax.ShapeDtypeStruct((total, inner), f32),
            jax.ShapeDtypeStruct((blocks, STATE, inner), f32),
            jax.ShapeDtypeStruct((total, 128), f32),
            jax.ShapeDtypeStruct((total, 128), f32),
            jax.ShapeDtypeStruct((cot_own.shape[0], shards) + cot_own.shape[1:], bf16),
        ],
        scratch_shapes=[
            pltpu.VMEM((BLOCK + TAIL, inner + SHARED), f32),
            pltpu.VMEM((STATE, inner), f32),
            *gather_semaphores(shards, columns),
        ],
        compiler_params=pltpu.CompilerParams(
            collective_id=2, has_side_effects=True, vmem_limit_bytes=56 * 1024 * 1024
        ),
        cost_estimate=pl.CostEstimate(flops=0, bytes_accessed=300_000_000, transcendentals=0),
        name="mixer_forward",
    )(bounds, slots, rows_in, weight, taps, bias, dt_bias, rate, skip, cot_own)


def pack_cotangent(shards, slots, rows_in, weight, mixed, projected, gain):
    blocks, _, width = rows_in.shape
    total, inner = mixed.shape

    def block_of(lanes):
        return pl.BlockSpec((BLOCK, lanes), lambda i: (i, 0))

    return pl.pallas_call(
        functools.partial(cotangent_kernel, shards),
        grid=(blocks,),
        in_specs=[
            pl.BlockSpec((1, 1, BLOCK), lambda i: (i, 0, 0)),
            pl.BlockSpec((1, BLOCK, width), lambda i: (i, 0, 0)),
            whole(weight.shape),
            block_of(inner),
            block_of(inner),
            whole(gain.shape),
        ],
        out_specs=[block_of(width), block_of(inner), whole((8, total))],
        out_shape=[
            jax.ShapeDtypeStruct((total, width), jnp.bfloat16),
            jax.ShapeDtypeStruct((total, inner), jnp.float32),
            jax.ShapeDtypeStruct((8, total), jnp.float32),
        ],
        scratch_shapes=[
            pltpu.VMEM((8, total), jnp.float32),
            pltpu.VMEM((shards - 1, 8, total), jnp.float32),
            pltpu.SemaphoreType.DMA((shards,)),
            pltpu.SemaphoreType.DMA((shards,)),
        ],
        compiler_params=pltpu.CompilerParams(
            collective_id=5, has_side_effects=True, vmem_limit_bytes=48 * 1024 * 1024
        ),
        cost_estimate=pl.CostEstimate(flops=0, bytes_accessed=60_000_000, transcendentals=0),
        name="pack_cotangent",
    )(slots, rows_in, weight, mixed, projected, gain)


def mixer_backward(
    shards, bounds, slots, pre, mixed, projected, d_out, sums, states, dt_cols, cot, taps, rate, skip, gain, out_own
):
    total, inner = d_out.shape
    heads, blocks, padded = inner // HDIM, total // BLOCK, rate.shape[0]
    shared = SHARED // shards
    columns = grid_columns(shards)
    marks = (jnp.arange(padded)[:, None] == jnp.arange(inner)[None, :] // HDIM).astype(jnp.bfloat16)

    def block_of(width, column):
        return pl.BlockSpec((BLOCK, width), lambda i: (blocks - 1 - i, column))

    return pl.pallas_call(
        functools.partial(backward_kernel, heads, blocks, shards, columns),
        grid_spec=pltpu.PrefetchScalarGridSpec(
            num_scalar_prefetch=0,
            grid=(blocks,),
            in_specs=[
                pl.BlockSpec(memory_space=pltpu.SMEM),
                pl.BlockSpec((1, 1, BLOCK), lambda i: (blocks - 1 - i, 0, 0)),
                block_of(inner + SHARED, 0),
                block_of(inner, 0),
                block_of(inner, 0),
                block_of(inner, 0),
                block_of(inner, 1),
                pl.BlockSpec((8, BLOCK), lambda i: (0, blocks - 1 - i)),
                pl.BlockSpec((1, STATE, inner), lambda i: (blocks - 1 - i, 0, 0)),
                block_of(dt_cols.shape[1], 0),
                block_of(cot.shape[1], 0),
                whole(taps.shape),
                whole(rate.shape),
                whole(skip.shape),
                whole(gain.shape),
                whole(marks.shape),
                pl.BlockSpec(memory_space=pl.ANY),
            ],
            out_specs=[
                block_of(2 * inner, 0),
                whole((shared, total)),
                pl.BlockSpec((padded, BLOCK), lambda i: (0, blocks - 1 - i)),
                whole((8, inner)),
                whole((padded, BLOCK)),
                whole((inner, cot.shape[1])),
                pl.BlockSpec((1, shards, BLOCK // shards, inner), lambda i: (blocks - 1 - i, 0, 0, 0)),
                pl.BlockSpec(memory_space=pl.ANY),
                pl.BlockSpec(memory_space=pl.ANY),
            ],
            scratch_shapes=[
                pltpu.VMEM((BLOCK + TAIL, inner), jnp.float32),
                pltpu.VMEM((STATE, inner), jnp.float32),
                pltpu.VMEM((shards // columns, columns, shared, total), jnp.float32),
                pltpu.VMEM((max(columns - 1, 1), shards // columns, shared, total), jnp.float32),
                pltpu.VMEM((shards // columns, shared, total), jnp.float32),
                pltpu.VMEM((shards // columns - 1, shared, total), jnp.float32),
                pltpu.VMEM((blocks // 2, shards, BLOCK // shards, inner), jnp.bfloat16),
                pltpu.SemaphoreType.DMA((max(columns - 1, 1), blocks)),
                pltpu.SemaphoreType.DMA((max(columns - 1, 1), blocks)),
                pltpu.SemaphoreType.DMA((shards,)),
                pltpu.SemaphoreType.DMA((shards,)),
                pltpu.SemaphoreType.DMA((shards,)),
                pltpu.SemaphoreType.DMA((shards,)),
                pltpu.SemaphoreType.DMA,
                *gather_semaphores(shards, columns),
            ],
        ),
        out_shape=[
            jax.ShapeDtypeStruct((total, 2 * inner), jnp.bfloat16),
            jax.ShapeDtypeStruct((shared, total), jnp.float32),
            jax.ShapeDtypeStruct((padded, total), jnp.float32),
            jax.ShapeDtypeStruct((8, inner), jnp.float32),
            jax.ShapeDtypeStruct((padded, BLOCK), jnp.float32),
            jax.ShapeDtypeStruct((inner, cot.shape[1]), jnp.float32),
            jax.ShapeDtypeStruct((blocks, shards, BLOCK // shards, inner), jnp.bfloat16),
            jax.ShapeDtypeStruct((shards, blocks // 2, BLOCK // shards, inner), jnp.bfloat16),
            jax.ShapeDtypeStruct((out_own.shape[0], shards) + out_own.shape[1:], jnp.bfloat16),
        ],
        compiler_params=pltpu.CompilerParams(
            collective_id=3, has_side_effects=True, vmem_limit_bytes=56 * 1024 * 1024
        ),
        cost_estimate=pl.CostEstimate(flops=0, bytes_accessed=200_000_000, transcendentals=0),
        name="mixer_backward",
    )(bounds, slots, pre, mixed, projected, d_out, projected, sums, states, dt_cols, cot, taps, rate, skip, gain, marks, out_own)


def piece_rows(shards, groups):
    chunks = (2 * INNER // shards + SHARED // shards) // CHUNK
    return -(-chunks // groups) * CHUNK


def column_runs(shards, groups):
    inner, width = INNER // shards, (2 * INNER + SHARED + HEADS) // groups
    kept = 2 * inner + SHARED + HEADS
    quarter = kept // groups
    spans = []
    for shard in range(shards):
        spans.append((inner * shard, shard, 0, inner))
        spans.append((INNER + inner * shard, shard, inner, inner))
    spans.append((2 * INNER, None, 2 * inner, SHARED + HEADS))
    runs = []
    for column, shard, row, length in spans:
        while length > 0:
            step = min(length, width - column % width, quarter - row % quarter)
            runs.append((column // width, column % width, shard, row, step))
            column, row, length = column + step, row + step, length - step
    return runs


def front_kernel(
    shards, groups, columns,
    rows_in, gain, cot_in, weight_in, out_in, slot_row, slot_col,
    rows_all, weight_all, out_all, slot_all, cot_own, out_cast,
    rows_own, weight_own, out_own, slot_own,
    run_send, run_recv, share_send, share_recv, out_send, out_recv, slot_send, slot_recv, local_sem, *gather_sems,
):
    shard, group = lax.axis_index("shard"), lax.axis_index("group")
    lines, rows_y = shards // columns, groups // 2
    y, core = group // 2, group % 2
    mate = y * 2 + 1 - core
    quarter = weight_all.shape[0] // groups
    depth = weight_own.shape[1]
    out_width = out_own.shape[1]
    everyone = []
    for step in range(1, shards * groups):
        other_shard = (shard + step % shards) % shards
        other_group = (group + step // shards) % groups
        everyone.append({"shard": other_shard, "group": other_group})
    barrier_with(everyone)

    count = rows_in.shape[0]
    below = (slot_col[...] < slot_row[...]).astype(jnp.int32).astype(jnp.float32)
    rank = jnp.sum(below, axis=0, keepdims=True).astype(jnp.int32)
    sort = (lax.broadcasted_iota(jnp.int32, (count, count), 0) == rank).astype(jnp.bfloat16)
    value = rows_in[...]
    scale = lax.rsqrt(jnp.sum(value * value, axis=1, keepdims=True) * (1.0 / value.shape[1]) + 1e-05)
    value = (value * scale * gain[...]).astype(jnp.bfloat16)
    rows_own[...] = dots(sort, value, ((1,), (0,))).astype(jnp.bfloat16).reshape(rows_own.shape)
    begin, hop, end = row_gather(shards, columns, rows_own, rows_all, *gather_sems)
    begin()
    slots = slot_row[...]
    high = slots // 256
    both = jnp.where(lax.broadcasted_iota(jnp.int32, (8, count), 0) == 0, high, slots - 256 * high)
    both = dots(both.astype(jnp.float32).astype(jnp.bfloat16), sort, NT)
    slot_own[...] = jnp.broadcast_to(256.0 * both[0:1, :] + both[1:2, :], (8, count)).astype(jnp.int32)
    out_own[...] = out_in[...].astype(jnp.bfloat16)
    weight_own[...] = weight_in[...].astype(jnp.bfloat16)

    def slot_copy(step):
        return remote(slot_own, slot_all.at[shard], slot_send.at[step], slot_recv.at[step], shard=(shard + step) % shards)

    for step in range(1, shards):
        slot_copy(step).start()
    slot_here = pltpu.make_async_copy(slot_own, slot_all.at[shard], local_sem.at[0])
    slot_here.start()

    runs = column_runs(shards, groups)
    lanes = pl.ds(pl.multiple_of(shard * depth, depth), depth)
    jobs = {owner: [] for owner in range(groups)}
    for owner, column, target, row, length in runs:
        for to in range(shards) if target is None else (target,):
            jobs[owner].append((column, to, row, length))

    def run_copy(number, column, to, row, length):
        return remote(
            weight_own.at[pl.ds(column, length)], weight_all.at[pl.ds(row, length), lanes],
            run_send.at[number], run_recv, shard=to, group=row // quarter,
        )

    def each_run(act):
        for owner in range(groups):
            @pl.when(group == owner)
            def _():
                for number, (column, to, row, length) in enumerate(jobs[owner]):
                    if row // quarter == owner:
                        here = shard == to
                        act(number, column, to, row, length, here)
                    else:
                        act(number, column, to, row, length, None)

    def start_run(number, column, to, row, length, here):
        if here is None:
            run_copy(number, column, to, row, length).start()
            return

        @pl.when(here)
        def _():
            pltpu.make_async_copy(weight_own.at[pl.ds(column, length)], weight_all.at[pl.ds(row, length), lanes], run_recv).start()

        @pl.when(jnp.logical_not(here))
        def _():
            run_copy(number, column, to, row, length).start()

    def end_run(number, column, to, row, length, here):
        if here is None:
            run_copy(number, column, to, row, length).wait_send()
            return

        @pl.when(jnp.logical_not(here))
        def _():
            run_copy(number, column, to, row, length).wait_send()

    each_run(start_run)

    def own_part(ref, part):
        if ref is out_all:
            return ref.at[:, pl.ds(pl.multiple_of(part * out_width, out_width), out_width)]
        return ref.at[pl.ds(pl.multiple_of(part * quarter, quarter), quarter)]

    def share(ref, part, sends, recvs, number, peer, first=None):
        source = own_part(ref, part) if first is None else first
        return remote(source, own_part(ref, part), sends.at[number], recvs.at[part], group=peer)

    def share_start(ref, sends, recvs, first=None):
        share(ref, group, sends, recvs, 0, mate, first).start()
        for step in range(1, rows_y):
            share(ref, group, sends, recvs, step, (y + step) % rows_y * 2 + core, first).start()

    def share_pass(ref, sends, recvs):
        for step in range(1, rows_y):
            part = (y + step) % rows_y * 2 + core
            share(ref, part, sends, recvs, step, part).wait_recv()
            share(ref, part, sends, recvs, rows_y - 1 + step, mate).start()

    def share_end(ref, sends, recvs):
        for turn in range(rows_y):
            part = turn * 2 + 1 - core
            share(ref, part, sends, recvs, 0, mate).wait_recv()
        for number in range(2 * rows_y - 1):
            share(ref, group, sends, recvs, number, mate).wait_send()

    out_here = pltpu.make_async_copy(out_own, own_part(out_all, group), local_sem.at[1])
    out_here.start()
    share_start(out_all, out_send, out_recv, out_own)
    out_cast[...] = out_own[...]
    cot_own[...] = (
        dots(sort, cot_in[...].astype(jnp.bfloat16), ((1,), (0,))).astype(jnp.bfloat16).reshape(cot_own.shape)
    )

    for step in range(1, lines):
        hop(step)
        if step == 1:
            share_pass(out_all, out_send, out_recv)
            kept = own_part(weight_all, group)
            pltpu.make_async_copy(kept, kept, run_recv).wait()
            share_start(weight_all, share_send, share_recv)
    share_pass(weight_all, share_send, share_recv)

    end()
    out_here.wait()
    share_end(out_all, out_send, out_recv)
    share_end(weight_all, share_send, share_recv)
    each_run(end_run)
    for step in range(1, shards):
        slot_copy(step).wait()
    slot_here.wait()


def front_exchange(shards, groups, rows_in, gain, cot_in, weight_in, out_in, slots):
    columns = grid_columns(shards)
    rows_y = groups // 2
    count, width = rows_in.shape
    blocks, per = shards * count // BLOCK, BLOCK // shards
    kept = 2 * INNER // shards + SHARED + HEADS
    any_space, vmem = pl.BlockSpec(memory_space=pl.ANY), pl.BlockSpec(memory_space=pltpu.VMEM)
    dma, bf16 = pltpu.SemaphoreType.DMA, jnp.bfloat16
    counts = {}
    for owner, _, target, _, _ in column_runs(shards, groups):
        counts[owner] = counts.get(owner, 0) + (shards if target is None else 1)
    return pl.pallas_call(
        functools.partial(front_kernel, shards, groups, columns),
        in_specs=[vmem] * 7,
        out_specs=[any_space] * 4 + [vmem] * 2,
        out_shape=[
            jax.ShapeDtypeStruct((blocks, shards, per, width), bf16),
            jax.ShapeDtypeStruct((kept, width), bf16),
            jax.ShapeDtypeStruct((out_in.shape[0], out_in.shape[1] * groups), bf16),
            jax.ShapeDtypeStruct((shards, 8, count), jnp.int32),
            jax.ShapeDtypeStruct((blocks, per, width), bf16),
            jax.ShapeDtypeStruct(out_in.shape, bf16),
        ],
        scratch_shapes=[
            pltpu.VMEM((blocks, per, width), bf16),
            pltpu.VMEM(weight_in.shape, bf16),
            pltpu.VMEM(out_in.shape, bf16),
            pltpu.VMEM((8, count), jnp.int32),
            dma((max(counts.values()),)),
            dma,
            dma((2 * rows_y - 1,)),
            dma((groups,)),
            dma((2 * rows_y - 1,)),
            dma((groups,)),
            dma((shards,)),
            dma((shards,)),
            dma((2,)),
            *gather_semaphores(shards, columns),
        ],
        compiler_params=pltpu.CompilerParams(
            collective_id=4, has_side_effects=True, vmem_limit_bytes=48 * 1024 * 1024
        ),
        cost_estimate=pl.CostEstimate(flops=0, bytes_accessed=300_000_000, transcendentals=0),
        name="front_exchange",
    )(rows_in, gain[None, :], cot_in, weight_in, out_in, slots[None, :], slots[:, None])


def unpack_kernel(
    shards, slots, d_cols, d_rest, normed, weight, weight_rest, no_rows,
    partial, grad, home, moved_cols, moved_rest, local_sem, home_send, home_recv,
):
    step = pl.program_id(0)
    shard = lax.axis_index("shard")
    main = d_cols.shape[1]
    per = BLOCK // shards

    def push(turn):
        peer = (shard + turn) % shards
        return remote(no_rows.at[first, peer], home.at[shard], home_send.at[turn], home_recv.at[turn], shard=peer)

    first = pl.ds(0, home.shape[1])
    here = pltpu.make_async_copy(no_rows.at[first, shard], home.at[shard], local_sem)

    @pl.when(step == 0)
    def _():
        barrier_with([{"shard": (shard + turn) % shards} for turn in range(1, shards)])
        for turn in range(1, shards):
            push(turn).start()
        here.start()
        grad[...] = jnp.zeros_like(grad)

    several = d_cols.shape[0] // BLOCK
    for turn in range(several):
        rows = pl.ds(turn * BLOCK, BLOCK)
        place = place_of_rows(slots[turn])
        moved_cols[rows, :] = dots(place, d_cols[rows, :], ((0,), (0,))).astype(jnp.bfloat16)
        moved_rest[rows, :] = dots(place, d_rest[rows, :], ((0,), (0,))).astype(jnp.bfloat16)
    tile = 512
    for lane in range(0, weight.shape[1], tile):
        lanes = pl.ds(lane, tile)
        found = dots(moved_cols[...], weight[:, lanes], ((1,), (0,)))
        found = found + dots(moved_rest[...], weight_rest[:, lanes], ((1,), (0,)))
        for turn in range(several):
            rows = found[turn * BLOCK : (turn + 1) * BLOCK]
            partial[:, turn, :, lanes] = rows.reshape(shards, per, tile)
    grad[:main, :] += dots(d_cols[...], normed[...], ((0,), (0,)))
    grad[main:, :] += dots(d_rest[...], normed[...], ((0,), (0,)))

    @pl.when(step == pl.num_programs(0) - 1)
    def _():
        for turn in range(1, shards):
            push(turn).wait()
        here.wait()


def project_back(slots, d_cols, d_rest, normed, weight, weight_rest, no_rows, shards):
    blocks, width = slots.shape[0], normed.shape[1]
    per, main, rest = BLOCK // shards, d_cols.shape[1], d_rest.shape[1]
    several = 2
    any_space = pl.BlockSpec(memory_space=pl.ANY)

    def block_of(columns):
        return pl.BlockSpec((several * BLOCK, columns), lambda i: (i, 0))

    return pl.pallas_call(
        functools.partial(unpack_kernel, shards),
        grid=(blocks // several,),
        in_specs=[
            pl.BlockSpec((several, 1, BLOCK), lambda i: (i, 0, 0)),
            block_of(main),
            block_of(rest),
            block_of(width),
            pl.BlockSpec((main, width), lambda i: (0, 0)),
            whole(weight_rest.shape),
            any_space,
        ],
        out_specs=[
            pl.BlockSpec((shards, several, per, width), lambda i: (0, i, 0, 0)),
            whole((main + rest, width)),
            any_space,
        ],
        out_shape=[
            jax.ShapeDtypeStruct((shards, blocks, per, width), jnp.float32),
            jax.ShapeDtypeStruct((main + rest, width), jnp.float32),
            jax.ShapeDtypeStruct((shards, blocks // 2) + no_rows.shape[2:], jnp.bfloat16),
        ],
        scratch_shapes=[
            pltpu.VMEM((several * BLOCK, main), jnp.bfloat16),
            pltpu.VMEM((several * BLOCK, rest), jnp.bfloat16),
            pltpu.SemaphoreType.DMA,
            pltpu.SemaphoreType.DMA((shards,)),
            pltpu.SemaphoreType.DMA((shards,)),
        ],
        compiler_params=pltpu.CompilerParams(
            collective_id=6, has_side_effects=True, vmem_limit_bytes=60 * 1024 * 1024
        ),
        cost_estimate=pl.CostEstimate(flops=0, bytes_accessed=90_000_000, transcendentals=0),
        name="project_back",
    )(slots, d_cols, d_rest, normed, weight, weight_rest, no_rows)


def other_place(step, place, count):
    upwards = count - 1 - place
    low = jnp.where(step < upwards, count - 1 - step, step - upwards)
    high = jnp.where(step < place, step, count - 1 - (step - place))
    return jnp.where(2 * place < count, low, high)


def tail_kernel(
    shards, groups, columns, near, direct,
    partial, weight_part, small, scaled_rows,
    rows_out, weight_out, mark_out, small_out, gain_out, core_in, row_in, row_scale_in, small_in, gain_in,
    wide_in, wide_scale, line_in, line_scale,
    held, coded, scales, line_coded, line_scales, got, got_scale, marks, total, other, send_rows, send_scales, row_got, row_scale_got, deal_rows, deal_scales, small_sum, small_got,
    gain_sum, gain_part,
    load_sem, wide_send, wide_recv, line_send, line_recv, core_send, core_recv, row_send, row_recv,
    deal_send, deal_recv, mark_send, mark_recv, small_send, small_recv, gain_send, gain_recv,
):
    shard, group = lax.axis_index("shard"), lax.axis_index("group")
    lines = shards // columns
    rows_y = groups // 2
    z, x = shard // columns, shard % columns
    y, core = group // 2, group % 2
    count = held.shape[0]
    owned, depth = weight_out.shape
    piece, chunk = total.shape[0], CHUNK
    inner, shared = INNER // shards, SHARED // shards

    def load(src, dst):
        copy = pltpu.make_async_copy(src, dst, load_sem)
        copy.start()
        copy.wait()

    shard_peers = [(shard + step) % shards for step in range(1, shards)]
    group_peers = [(group + step) % groups for step in range(1, groups)]
    if direct:
        barrier_with(
            [
                {"shard": (shard + step % shards) % shards, "group": (group + step // shards) % groups}
                for step in range(1, shards * groups)
            ]
        )
    else:
        barrier_with([{"shard": peer} for peer in shard_peers] + [{"group": peer} for peer in group_peers])

    mate = y * 2 + 1 - core

    def core_copy(turn):
        return remote(piece_of(turn * 2 + 1 - core), core_in.at[turn], core_send.at[turn], core_recv.at[turn], group=mate)

    def piece_of(owner):
        return weight_part.at[pl.ds(pl.multiple_of(owner * piece, piece), piece)]

    for turn in range(rows_y if direct else 0):
        core_copy(turn).start()

    def small_copy(step):
        return remote(small, small_in.at[step - 1], small_send.at[step - 1], small_recv.at[step - 1], group=(group + step) % groups)

    for step in range(1, groups):
        small_copy(step).start()

    def code(coded_to, scales_to, values=held, lot=32):
        @pl.loop(0, values.shape[0] // lot, unroll=2)
        def _(turn):
            rows = pl.ds(pl.multiple_of(turn * lot, lot), lot)
            value = values[rows, :]
            most = jnp.maximum(jnp.max(jnp.abs(value), axis=1, keepdims=True), 1e-30)
            coded_to[rows, :] = jnp.round(value * (32767.0 / most)).astype(jnp.int32).astype(jnp.int16)
            marks[rows, :] = jnp.broadcast_to(most * (1.0 / 32767.0), (lot, 128))

        scales_to[...] = marks[: scales_to.shape[1], :].T[:8, :]

    def add(coded_from, scales_from):
        if not near:
            load(coded_from, got)
            load(scales_from, got_scale)
            coded_from, scales_from = got, got_scale
        marks[:count, :] = jnp.broadcast_to(scales_from[0:1, :], (128, count)).T

        @pl.loop(0, count // 32, unroll=2)
        def _(turn):
            rows = pl.ds(pl.multiple_of(turn * 32, 32), 32)
            held[rows, :] += coded_from[rows, :].astype(jnp.float32) * marks[rows, 0:1]

    def place_of(step):
        return other_place(step, z, lines) if step < lines - 1 else z

    def wide_copies(step, hop):
        at = (hop - 1) * lines + step
        peer = z * columns + (x + hop) % columns
        target = place_of(step)
        return (
            remote(coded.at[step], wide_in.at[hop - 1, target], wide_send.at[0, at], wide_recv.at[0, at], shard=peer),
            remote(scales.at[step], wide_scale.at[hop - 1, target], wide_send.at[1, at], wide_recv.at[1, at], shard=peer),
        )

    def send_wide(hop, steps):
        for step in steps:
            if hop > 1:
                for copy in wide_copies(step, hop - 1):
                    copy.wait_send()
            load(partial.at[place_of(step) * columns + (x + hop) % columns], held)
            code(coded.at[step], scales.at[step])
            for copy in wide_copies(step, hop):
                copy.start()

    def row_copies(step):
        peer = (y + step) % rows_y * 2 + core
        return (
            remote(send_rows.at[step - 1], row_in.at[step - 1], row_send.at[0, step - 1], row_recv.at[0, step - 1], group=peer),
            remote(send_scales.at[step - 1], row_scale_in.at[step - 1], row_send.at[1, step - 1], row_recv.at[1, step - 1], group=peer),
        )

    def core_sum(turn):
        load(piece_of(turn * 2 + core), total)
        load(core_in.at[turn], other)

        @pl.loop(0, piece // chunk)
        def _(turn):
            rows = pl.ds(pl.multiple_of(turn * chunk, chunk), chunk)
            total[rows, :] += other[rows, :]

    if columns > 1:
        send_wide(1, range(0, 1))
    if direct:
        for turn in range(rows_y):
            core_copy(turn).wait_recv()
        for step in range(1, rows_y):
            core_sum((y + step) % rows_y)
            code(send_rows.at[step - 1], send_scales.at[step - 1], total, chunk)
            for copy in row_copies(step):
                copy.start()
        core_sum(y)
    if columns > 1:
        send_wide(1, range(1, lines))
    for hop in range(2, columns):
        send_wide(hop, range(lines))

    load(small, small_sum)
    for step in range(1, groups):
        small_copy(step).wait_recv()
        load(small_in.at[step - 1], small_got)
        small_sum[...] += small_got[...]

    def small_deal(step):
        return remote(small_sum, small_out.at[shard], small_send.at[groups + step], small_recv.at[groups + step], shard=(shard + step) % shards)

    for step in range(1, shards):
        small_deal(step).start()
    load(small_sum, small_out.at[shard])

    def line_copies(step):
        target = place_of(step)
        way = jnp.where(target > z, 0, 1)
        peer = jnp.where(target > z, z + 1, z - 1) * columns + x
        return (
            remote(line_coded.at[step], line_in.at[way, target], line_send.at[0, step], line_recv.at[0, way, target], shard=peer),
            remote(line_scales.at[step], line_scale.at[way, target], line_send.at[1, step], line_recv.at[1, way, target], shard=peer),
        )

    def take(way, target):
        source = jnp.where(way == 0, z - 1, z + 1)
        peer = jnp.clip(source, 0, lines - 1) * columns + x
        remote(line_coded.at[0], line_in.at[way, target], line_send.at[0, 0], line_recv.at[0, way, target], shard=peer).wait_recv()
        remote(line_scales.at[0], line_scale.at[way, target], line_send.at[1, 0], line_recv.at[1, way, target], shard=peer).wait_recv()
        add(line_in.at[way, target], line_scale.at[way, target])

    def gather_wide(step):
        target = place_of(step)
        load(partial.at[target * columns + x], held)
        for hop in range(1, columns):
            for copy in wide_copies(step, hop):
                copy.wait_recv()
            add(wide_in.at[hop - 1, target], wide_scale.at[hop - 1, target])

    def deal_copy(turn, step):
        first = group * piece + turn * chunk
        column = jnp.where(
            first < inner,
            inner * shard + first,
            jnp.where(first < 2 * inner, INNER + inner * shard + first - inner, 2 * INNER + shared * shard + first - 2 * inner),
        )
        owner = jnp.minimum(column // owned, groups - 1)
        peer = (shard + step) % shards
        source = deal_rows.at[
            pl.ds(pl.multiple_of(turn * chunk, chunk), chunk), pl.ds(pl.multiple_of(peer * depth, depth), depth)
        ]
        target = weight_out.at[pl.ds(pl.multiple_of(column - owner * owned, chunk), chunk)]
        real = first < 2 * inner + shared
        here = real & (owner == group) if step == 0 else None
        away = real & (owner != group) if step == 0 else real

        def near_copy():
            return pltpu.make_async_copy(source, target, deal_recv)

        def far():
            return remote(source, target, deal_send.at[turn, step], deal_recv, shard=peer, group=owner)

        return here, near_copy, away, far

    def deal():
        for step in range(1, rows_y):
            for copy in row_copies(step):
                copy.wait_recv()
            load(row_in.at[step - 1], row_got)
            load(row_scale_in.at[step - 1], row_scale_got)
            marks[: row_scale_got.shape[1], :] = jnp.broadcast_to(row_scale_got[0:1, :], (128, row_scale_got.shape[1])).T

            @pl.loop(0, piece // chunk)
            def _(turn):
                rows = pl.ds(pl.multiple_of(turn * chunk, chunk), chunk)
                total[rows, :] += row_got[rows, :].astype(jnp.float32) * marks[rows, 0:1]

        code(deal_rows, deal_scales, total, chunk)
        load(deal_scales, mark_out.at[shard, group])
        for step in range(1, groups):
            mark_copy(step).start()

    def deal_some(part, parts):
        chunks = piece // chunk

        @pl.loop(part * chunks // parts, (part + 1) * chunks // parts)
        def _(turn):
            for step in range(shards):
                here, near_copy, away, far = deal_copy(turn, step)
                if here is not None:
                    pl.when(here)(lambda: near_copy().start())
                pl.when(away)(lambda: far().start())

    def mark_copy(step):
        to = (group + step) % groups
        return remote(deal_scales, mark_out.at[shard, group], mark_send.at[step], mark_recv.at[step], group=to)

    def mark_spread(step):
        to, at = (shard + step) % shards, groups + step
        return remote(mark_out.at[shard], mark_out.at[shard], mark_send.at[at], mark_recv.at[at], shard=to)

    def mark_pass():
        for step in range(1, groups):
            mark_copy(step).wait_recv()
        for step in range(1, shards):
            mark_spread(step).start()

    def deal_end():
        for step in range(1, groups):
            mark_copy(step).wait_send()
        for step in range(1, shards):
            mark_spread(step).wait()

        @pl.when(group == groups - 1)
        def _():
            most = weight_out.at[pl.ds(0, owned - HEADS)]
            pltpu.make_async_copy(most, most, deal_recv).wait()

        @pl.when(group < groups - 1)
        def _():
            pltpu.make_async_copy(weight_out, weight_out, deal_recv).wait()

        @pl.loop(0, piece // chunk)
        def _(turn):
            for step in range(shards):
                _, _, away, far = deal_copy(turn, step)
                pl.when(away)(lambda: far().wait_send())

    for step in range(lines - 1):
        if direct and step == min(1, lines - 2):
            deal()
        target = place_of(step)
        way = jnp.where(target > z, 0, 1)
        gather_wide(step)

        @pl.when(jnp.where(target > z, z > 0, z < lines - 1))
        def _():
            take(way, target)

        code(line_coded.at[step], line_scales.at[step])
        for copy in line_copies(step):
            copy.start()
        if direct and step >= min(1, lines - 2):
            deal_some(step - min(1, lines - 2), lines - 1 - min(1, lines - 2))
    if direct:
        mark_pass()
    gather_wide(lines - 1)

    @pl.when(z > 0)
    def _():
        take(0, z)

    @pl.when(z < lines - 1)
    def _():
        take(1, z)

    rows_out[...] = held[...]
    gain_sum[...] = jnp.zeros_like(gain_sum)

    @pl.loop(0, count // 8)
    def _(turn):
        rows = pl.ds(pl.multiple_of(turn * 8, 8), 8)
        gain_sum[...] += held[rows, :] * scaled_rows[rows, :]

    def gain_copy(step):
        return remote(gain_part, gain_in.at[step - 1], gain_send.at[step - 1], gain_recv.at[step - 1], shard=(shard + step) % shards)

    def gain_deal(step):
        at = shards - 1 + step - 1
        return remote(gain_out, gain_in.at[at], gain_send.at[at], gain_recv.at[at], group=(group + step) % groups)

    lanes = gain_out.shape[1]
    products = jnp.sum(gain_sum[...], axis=0, keepdims=True)
    gain_part[...] = jnp.concatenate([products[:, row * lanes : (row + 1) * lanes] for row in range(8)], axis=0)
    for step in range(1, shards):
        gain_copy(step).start()
    gain_out[...] = gain_part[...]
    for step in range(1, shards):
        gain_copy(step).wait_recv()
        gain_out[...] += gain_in[step - 1]
    for step in range(1, groups):
        gain_deal(step).start()
    for step in range(1, groups):
        gain_deal(step).wait_recv()
    for step in range(1, groups):
        gain_deal(step).wait_send()
    for step in range(1, groups):
        gain_out[...] += gain_in[shards - 1 + step - 1]

    for step in range(1, shards):
        gain_copy(step).wait_send()
        small_deal(step).wait()
    for step in range(1, groups):
        small_copy(step).wait_send()
    if direct:
        deal_end()
        for step in range(1, rows_y):
            for copy in row_copies(step):
                copy.wait_send()
        for turn in range(rows_y):
            core_copy(turn).wait_send()
    for step in range(lines):
        for copy in wide_copies(step, columns - 1) if columns > 1 else ():
            copy.wait_send()
    for step in range(lines - 1):
        for copy in line_copies(step):
            copy.wait_send()


def tail_exchange(shards, groups, partial, weight_part, small, scaled_rows, owned, depth, direct):
    columns = grid_columns(shards)
    lines, rows_y = shards // columns, groups // 2
    count, width = scaled_rows.shape
    piece = piece_rows(shards, groups) if direct else CHUNK
    padded = -(-piece // 128) * 128
    small_shape = small.shape
    coded, scale = (count, width), (8, count)
    any_space, vmem = pl.BlockSpec(memory_space=pl.ANY), pl.BlockSpec(memory_space=pltpu.VMEM)
    f32, i16 = jnp.float32, jnp.int16
    slots = max(columns - 1, 1)
    dma = pltpu.SemaphoreType.DMA
    landing = [
        ((slots, lines) + coded, i16),
        ((slots, lines) + scale, f32),
        ((2, lines) + coded, i16),
        ((2, lines) + scale, f32),
    ]
    near = shards * count * width <= 1 << 22
    out = pl.pallas_call(
        functools.partial(tail_kernel, shards, groups, columns, near, direct),
        in_specs=[any_space, any_space, any_space, vmem],
        out_specs=[vmem, any_space, any_space, any_space, vmem] + [any_space] * 4 + [vmem] + ([] if near else [any_space] * 4),
        out_shape=[
            jax.ShapeDtypeStruct((count, width), f32),
            jax.ShapeDtypeStruct((owned, depth), i16),
            jax.ShapeDtypeStruct((shards, groups, 8, padded), f32),
            jax.ShapeDtypeStruct((shards,) + small_shape, f32),
            jax.ShapeDtypeStruct((8, width // 8), f32),
            jax.ShapeDtypeStruct((rows_y, piece, width), f32),
            jax.ShapeDtypeStruct((max(rows_y - 1, 1), piece, width), i16),
            jax.ShapeDtypeStruct((max(rows_y - 1, 1), 8, padded), f32),
            jax.ShapeDtypeStruct((max(groups - 1, 1),) + small_shape, f32),
            jax.ShapeDtypeStruct((shards - 1 + groups - 1, 8, width // 8), f32),
        ]
        + ([] if near else [jax.ShapeDtypeStruct(*each) for each in landing]),
        scratch_shapes=([pltpu.VMEM(*each) for each in landing] if near else [])
        + [
            pltpu.VMEM((count, width), f32),
            pltpu.VMEM((lines,) + coded, i16),
            pltpu.VMEM((lines,) + scale, f32),
            pltpu.VMEM((lines,) + coded, i16),
            pltpu.VMEM((lines,) + scale, f32),
            pltpu.VMEM((16, 128) if near else coded, i16),
            pltpu.VMEM((8, 128) if near else scale, f32),
            pltpu.VMEM((max(count, padded), 128), f32),
            pltpu.VMEM((piece, width), f32),
            pltpu.VMEM((piece, width), f32),
            pltpu.VMEM((max(rows_y - 1, 1), piece, width), i16),
            pltpu.VMEM((max(rows_y - 1, 1), 8, padded), f32),
            pltpu.VMEM((piece, width), i16),
            pltpu.VMEM((8, padded), f32),
            pltpu.VMEM((piece, width), i16),
            pltpu.VMEM((8, padded), f32),
            pltpu.VMEM(small_shape, f32),
            pltpu.VMEM(small_shape, f32),
            pltpu.VMEM((8, width), f32),
            pltpu.VMEM((8, width // 8), f32),
            dma,
            dma((2, slots * lines)),
            dma((2, slots * lines)),
            dma((2, lines)),
            dma((2, 2, lines)),
            dma((rows_y,)),
            dma((rows_y,)),
            dma((2, max(rows_y - 1, 1))),
            dma((2, max(rows_y - 1, 1))),
            dma((piece // CHUNK, shards)),
            dma,
            dma((shards + groups,)),
            dma((shards + groups,)),
            dma((groups + shards,)),
            dma((groups + shards,)),
            dma((shards + groups,)),
            dma((shards + groups,)),
        ],
        compiler_params=pltpu.CompilerParams(
            collective_id=1, has_side_effects=True, vmem_limit_bytes=60 * 1024 * 1024
        ),
        cost_estimate=pl.CostEstimate(flops=0, bytes_accessed=400_000_000, transcendentals=0),
        name="tail_exchange",
    )(partial, weight_part, small, scaled_rows)
    return out[:5]


def nesterov(weight, gradient, moment, average, step_rate):
    decayed = gradient + weight_decay * weight
    new_moment = momentum_decay * moment + decayed
    new_weight = weight - step_rate * (decayed + momentum_decay * new_moment)
    new_average = average_decay * average + (1.0 - average_decay) * new_weight
    return (new_moment, new_weight, new_average)


def dot32(a, b, contract=((1,), (0,))):
    return lax.dot_general(a, b, (contract, ((), ())), preferred_element_type=jnp.float32)


def own_slice(value, index, width, axis):
    return lax.dynamic_slice_in_dim(value, index * width, width, axis)


def local(
    tokens,
    cotangent,
    lengths,
    deal_slot,
    in_weight,
    out_weight,
    small_params,
    in_moment,
    out_moment,
    small_moment,
    in_average,
    out_average,
    small_average,
):
    shards, groups = lax.axis_size("shard"), lax.axis_size("group")
    shard, group = lax.axis_index("shard"), lax.axis_index("group")
    rows, width = tokens.shape
    per = rows // shards
    total = rows * shards
    blocks = total // BLOCK
    heads = HEADS // shards
    inner = INNER // shards
    shared = SHARED // shards
    conv_flat, conv_bias, dt_bias, rate_log, skip_gain, norm_gain, pre_gain = unpack(small_params)
    taps = conv_flat.reshape(CONV, XBC)

    cols, depth, sends = in_weight.shape[1], in_weight.shape[0], out_weight.shape[1]
    direct = cols % CHUNK == 0 and depth % 128 == 0 and sends % 128 == 0 and per % CHUNK == 0
    direct = direct and (2 * inner + SHARED + HEADS) % (groups * CHUNK) == 0 and shared % CHUNK == 0
    bounds = jnp.cumsum(lengths[0])[:-1].astype(jnp.int32)
    seg_rows = segment_of(jnp.arange(total, dtype=jnp.int32), lengths[0])

    rank = jnp.sum((deal_slot[None, :] < deal_slot[:, None]).astype(jnp.int32), axis=1)
    sort_mat = (rank[None, :] == jnp.arange(rows)[:, None]).astype(jnp.bfloat16)
    r_in = lax.rsqrt(jnp.mean(tokens * tokens, axis=1, keepdims=True) + eps_norm)
    in_turned = in_weight.T

    if direct:
        x_all, in_low, out_low, slot_all, c_sorted, out_cast = front_exchange(
            shards, groups, tokens, pre_gain, cotangent, in_turned, out_weight, deal_slot
        )
        x_all = x_all.reshape(blocks, BLOCK, width)
        slot_all = slot_all[:, 0, :]
    else:
        sorted_slot = jnp.sum(jnp.where(sort_mat > 0, deal_slot[None, :], 0), axis=1)
        normed_low = (tokens * r_in * pre_gain[None, :]).astype(jnp.bfloat16)
        x_sorted = dot32(sort_mat, normed_low).astype(jnp.bfloat16).reshape(blocks, per, width)
        c_sorted = dot32(sort_mat, cotangent.astype(jnp.bfloat16)).astype(jnp.bfloat16)
        c_sorted = c_sorted.reshape(blocks, per, width)
        in_turned = in_turned.astype(jnp.bfloat16)
        out_cast = out_weight.astype(jnp.bfloat16)
        x_all = lax.all_gather(x_sorted, "shard").transpose(1, 0, 2, 3).reshape(blocks, BLOCK, width)
        slot_all = lax.all_gather(sorted_slot, "shard")
        part = depth // groups
        pieces = lax.all_to_all(in_turned.reshape(cols, groups, part), "group", 1, 0)
        pieces = pieces.reshape(groups * cols, part)

        def cut(lo, each):
            return pieces[lo : lo + each * shards].reshape(shards, each, part)

        spread = jnp.broadcast_to(pieces[None, 2 * INNER :], (shards, SHARED + HEADS, part))
        got = jnp.concatenate([cut(0, inner), cut(INNER, inner), spread], axis=1)
        got = lax.all_gather(lax.all_to_all(got, "shard", 0, 0), "group")
        in_low = got.transpose(2, 1, 0, 3).reshape(-1, width)
        out_low = lax.all_gather(out_cast, "group", axis=1, tiled=True)
    slot_blk = slot_all.reshape(shards, blocks, per).transpose(1, 0, 2).reshape(blocks, 1, BLOCK)
    slot_blk = slot_blk - jnp.arange(blocks, dtype=jnp.int32)[:, None, None] * BLOCK

    taps_v = own_slice(taps[:, :INNER], shard, inner, 1)
    taps_all = jnp.concatenate([taps_v, taps[:, INNER:]], axis=1)
    bias_all = jnp.concatenate([own_slice(conv_bias[:INNER], shard, inner, 0), conv_bias[INNER:]])[None, :]
    skip_wide = jnp.repeat(own_slice(skip_gain, shard, heads, 0), HDIM)[None, :]
    gain_own = own_slice(norm_gain, shard, inner, 0)[None, :]
    padding = max(TAIL - heads, 0)
    rate = jnp.pad(-jnp.exp(own_slice(rate_log, shard, heads, 0)), (0, padding))[:, None]
    normed, projected, pre, mixed, states, dt_cols, dt_raw, c_all = mixer_forward(
        shards, bounds, slot_blk, x_all, in_low, taps_all, bias_all, dt_bias[None, :], rate, skip_wide, c_sorted
    )
    conv_bc = projected[:, 2 * inner : 2 * inner + SHARED]
    cot_low, d_out, sums = pack_cotangent(
        shards, slot_blk, c_all.reshape(blocks, BLOCK, width), out_low, mixed, projected, gain_own
    )

    d_cols, d_bc, d_dt, grads, rate_terms, grad_out, no_rows, home_late, out_full = mixer_backward(
        shards, bounds, slot_blk, pre, mixed, projected, d_out, sums, states, dt_cols, cot_low,
        taps_v, rate, skip_wide, gain_own, out_cast[None],
    )
    out_full = lax.all_gather(out_full.reshape(INNER, -1), "group", axis=1, tiled=True)
    grad_out = lax.psum_scatter(grad_out, "group", scatter_dimension=1, tiled=True)

    d_dtraw = d_dt[:heads].T * jax.nn.sigmoid(dt_raw[:, :heads])
    grad_dtb = jnp.sum(d_dtraw, axis=0)
    grad_rate = jnp.sum(rate_terms[:heads], axis=1)
    grad_skip = jnp.sum(grads[6].reshape(heads, HDIM), axis=1)
    _, pull_bc = jax.vjp(
        lambda c, t, b: convolve(c, seg_rows, t, b),
        own_slice(conv_bc, shard, shared, 1),
        own_slice(taps[:, INNER:], shard, shared, 1),
        own_slice(conv_bias[INNER:], shard, shared, 0),
    )
    d_conv_bc, grad_taps_bc, grad_bias_bc = pull_bc(d_bc.T)
    rest = 128 - shared - heads
    d_rest = jnp.concatenate([d_conv_bc, d_dtraw, jnp.zeros((total, rest), jnp.float32)], axis=1)
    in_rest = jnp.concatenate(
        [
            own_slice(in_low[2 * inner : 2 * inner + SHARED], shard, shared, 0),
            own_slice(in_low[2 * inner + SHARED :], shard, heads, 0),
            jnp.zeros((rest, width), jnp.bfloat16),
        ]
    )
    partial, weight_part, home = project_back(
        slot_blk, d_cols, d_rest.astype(jnp.bfloat16), normed, in_low, in_rest, no_rows, shards
    )

    home = jnp.concatenate([home, home_late], axis=1)
    home = home.reshape(shards, rows, inner).transpose(1, 0, 2).reshape(rows, INNER)
    home = dot32(sort_mat, home, ((0,), (0,))).astype(jnp.bfloat16)
    block_out = tokens + dot32(home, out_full)
    dt_part = weight_part[2 * inner + shared : 2 * inner + shared + heads]

    mine = [
        grads[:CONV].reshape(-1),
        grad_taps_bc.reshape(-1),
        grads[4],
        grad_bias_bc,
        grad_dtb,
        grad_rate,
        grad_skip,
        grads[5],
    ]
    if direct:
        mine.append(dt_part.reshape(-1))
    extents = [piece.shape[0] for piece in mine]
    mine = jnp.concatenate(mine)
    mine = jnp.pad(mine, (0, -mine.shape[0] % 1024)).reshape(-1, 128)
    x_scaled = jnp.dot(sort_mat.astype(jnp.float32), tokens * r_in, precision=lax.Precision.HIGHEST)
    d_normed, grad_in, grad_marks, small_all, gain_all = tail_exchange(
        shards, groups, partial.reshape(shards, rows, width), weight_part, mine, x_scaled, cols, depth, direct
    )
    d_normed = jnp.dot(sort_mat.T.astype(jnp.float32), d_normed, precision=lax.Precision.HIGHEST)
    d_scaled = pre_gain[None, :] * d_normed
    inside = jnp.mean(tokens * d_scaled, axis=1, keepdims=True)
    input_grad = cotangent + r_in * (d_scaled - tokens * (r_in * r_in) * inside)
    grad_pre = gain_all.reshape(width)

    mine = small_all.reshape(shards, -1)
    found, offset = [], 0
    for extent in extents:
        found.append(mine[:, offset : offset + extent])
        offset = offset + extent
    if direct:
        dt_part = own_slice(found.pop().reshape(HEADS, width), shard, depth, 1)
        steps = grad_marks[:, :, 0, : piece_rows(shards, groups)].reshape(shards, -1)
        steps = jnp.concatenate(
            [
                steps[:, :inner].reshape(-1),
                steps[:, inner : 2 * inner].reshape(-1),
                steps[:, 2 * inner : 2 * inner + shared].reshape(-1),
                jnp.zeros((HEADS,), jnp.float32),
            ]
        )
        grad_in = grad_in.astype(jnp.float32) * own_slice(steps, group, cols, 0)[:, None]
        last = jnp.concatenate([grad_in[: cols - HEADS], dt_part])
        grad_in = jnp.where(group == groups - 1, last, grad_in)
    else:
        used = 2 * inner + shared + heads
        grad_in = weight_part[:used].reshape(used, shards, groups, part).transpose(2, 1, 0, 3)
        grad_in = lax.psum_scatter(grad_in, "group", scatter_dimension=0)
        grad_in = lax.all_to_all(grad_in, "shard", 0, 0)

        def join(lo, each):
            return grad_in[:, lo : lo + each].reshape(shards * each, part)

        grad_in = jnp.concatenate(
            [
                join(0, inner),
                join(inner, inner),
                join(2 * inner, shared),
                join(2 * inner + shared, heads),
            ]
        )
        grad_in = lax.all_to_all(grad_in.reshape(groups, cols, part), "group", 0, 0)
        grad_in = grad_in.transpose(1, 0, 2).reshape(cols, depth)

    def taps_of(piece):
        return piece.reshape(shards, CONV, -1).transpose(1, 0, 2).reshape(CONV, -1)

    grad_taps = jnp.concatenate([taps_of(found[0]), taps_of(found[1])], axis=1).reshape(-1)
    grad_small = jnp.concatenate([grad_taps] + [piece.reshape(-1) for piece in found[2:]] + [grad_pre])
    in_new = nesterov(in_weight.T, grad_in, in_moment.T, in_average.T, rate_in)
    in_new = tuple(value.T for value in in_new)
    out_new = nesterov(out_weight, grad_out, out_moment, out_average, rate_out)
    small_new = nesterov(small_params, grad_small, small_moment, small_average, rate_small)
    return (block_out, input_grad) + in_new + out_new + small_new


def solution(mesh):
    rows = P(("group", "shard"), None)
    tile = P("shard", "group")
    return jax.shard_map(
        local,
        mesh=mesh,
        in_specs=(
            rows,
            rows,
            P("group", None),
            P(("group", "shard")),
            tile,
            tile,
            P(),
            tile,
            tile,
            P(),
            tile,
            tile,
            P(),
        ),
        out_specs=(rows, rows, tile, tile, tile, tile, tile, tile, P(), P(), P()),
        check_vma=False,
    )
```

```python
import functools

import jax
import jax.numpy as jnp
from jax import lax
from jax.experimental import pallas as pl
from jax.experimental.pallas import tpu as pltpu
from jax.sharding import PartitionSpec as P

D = 2048
HEADS = 64
HDIM = 64
STATE = 128
CONV = 4
BLOCK = 256
INNER = 4096
XBC = 4352
SHARED = 2 * STATE
TAIL = 8
CHUNK = 16
MESH = pl.DeviceIdType.MESH


eps_norm = 1e-05
momentum_decay = 0.9
weight_decay = 0.01
average_decay = 0.99
rate_in = 0.0001
rate_out = 3e-05
rate_small = 0.001


def unpack(packed_small):
    extents = [CONV * XBC, XBC, HEADS, HEADS, HEADS, INNER, D]
    pieces = []
    offset = 0
    for extent in extents:
        pieces.append(packed_small[offset : offset + extent])
        offset = offset + extent
    return pieces


def segment_of(positions, lengths_row):
    bounds = jnp.cumsum(lengths_row)[:-1]
    inside = jnp.sum((positions[:, None] >= bounds[None, :]).astype(jnp.int32), axis=1)
    return jnp.where(positions < 0, -1, inside)


def convolve(conv_rows, seg_rows, conv_taps, conv_bias):
    row_count, width = conv_rows.shape
    extended = jnp.concatenate([jnp.zeros((CONV - 1, width), conv_rows.dtype), conv_rows], axis=0)
    seg_ext = jnp.concatenate([jnp.full((CONV - 1,), -1, jnp.int32), seg_rows], axis=0)
    conv_sum = jnp.zeros_like(conv_rows) + conv_bias[None, :]
    for tap_index in range(CONV):
        same_seq = (seg_ext[tap_index : tap_index + row_count] == seg_rows)[:, None]
        conv_sum = conv_sum + jnp.where(
            same_seq,
            extended[tap_index : tap_index + row_count] * conv_taps[tap_index][None, :],
            0.0,
        )
    return jax.nn.silu(conv_sum)


def split(value):
    high = value.astype(jnp.bfloat16)
    return high, (value - high.astype(jnp.float32)).astype(jnp.bfloat16)


def dots(a, b, contract):
    return lax.dot_general(a, b, (contract, ((), ())), preferred_element_type=jnp.float32)


def dot3(a, b, contract=((1,), (0,))):
    a = a if isinstance(a, tuple) else split(a)
    b = b if isinstance(b, tuple) else split(b)
    return dots(a[0], b[0], contract) + (dots(a[0], b[1], contract) + dots(a[1], b[0], contract))


NT = ((1,), (1,))


def dot_wide(a, wide):
    high, low = split(a)
    lanes = wide.shape[1] // 2
    plain = ((1,), (0,))
    first = dots(high, wide, plain)
    return first[:, :lanes] + (first[:, lanes:] + dots(low, wide[:, :lanes], plain))


def beside(first, second, own):
    moved = pltpu.roll(second.astype(jnp.float32), HDIM, 1).astype(jnp.bfloat16)
    return jnp.where(own, first, moved)


def head_sums(value, marks):
    high = value.astype(jnp.bfloat16)
    rest = value - high.astype(jnp.float32)
    mid = rest.astype(jnp.bfloat16)
    low = (rest - mid.astype(jnp.float32)).astype(jnp.bfloat16)
    return dots(marks, high, NT) + (dots(marks, mid, NT) + dots(marks, low, NT))


def widen(columns, heads):
    rows = columns.shape[0]
    low_half = lax.broadcasted_iota(jnp.int32, (rows, 2 * HDIM), 1) < HDIM
    return jnp.concatenate(
        [
            jnp.where(low_half, columns[:, h : h + 1], columns[:, h + 1 : h + 2])
            for h in range(0, heads, 2)
        ],
        axis=1,
    )


def running_sum(value, reverse=False):
    lane = lax.broadcasted_iota(jnp.int32, value.shape, 1)
    count = value.shape[1]
    step = 1
    while step < count:
        if reverse:
            value = value + jnp.where(lane < count - step, pltpu.roll(value, count - step, 1), 0.0)
        else:
            value = value + jnp.where(lane >= step, pltpu.roll(value, step, 1), 0.0)
        step *= 2
    return value


def sequence_of(positions, bounds):
    inside = jnp.where(positions >= bounds[0], 1, 0) + jnp.where(positions >= bounds[1], 1, 0)
    return jnp.where(positions < 0, -1, inside)


def block_facts(block, bounds, dt_t, rate):
    start = block * BLOCK
    seg_col = sequence_of(start + lax.broadcasted_iota(jnp.int32, (BLOCK, 1), 0), bounds)
    seg_row = sequence_of(start + lax.broadcasted_iota(jnp.int32, (1, BLOCK), 1), bounds)
    before = sequence_of(start - 1 + lax.broadcasted_iota(jnp.int32, (1, 1), 1), bounds)
    last = sequence_of(start + BLOCK - 1 + lax.broadcasted_iota(jnp.int32, (1, 1), 1), bounds)
    run_t = running_sum(dt_t * rate)
    run = run_t.T
    final = run[BLOCK - 1 :, :]
    carried = jnp.where(seg_col == before, jnp.exp(run), 0.0)
    tail = jnp.where(seg_col == last, jnp.exp(final - run), 0.0)
    keep = jnp.where(last == before, jnp.exp(final), 0.0)
    return seg_col, seg_row, run_t, run, carried, tail, keep


def barrier_with(peers):
    barrier = pltpu.get_barrier_semaphore()
    for peer in peers:
        pl.semaphore_signal(barrier, inc=1, device_id=peer, device_id_type=MESH)
    pl.semaphore_wait(barrier, len(peers))


def remote(src, dst, sends, recvs, **where):
    return pltpu.make_async_remote_copy(
        src_ref=src, dst_ref=dst, send_sem=sends, recv_sem=recvs, device_id=where, device_id_type=MESH
    )


def place_of_rows(slots):
    count = slots.shape[1]
    return (lax.broadcasted_iota(jnp.int32, (BLOCK, count), 0) == slots).astype(jnp.bfloat16)


def grid_columns(shards):
    columns = 1
    while 2 * (2 * columns) * (2 * columns) <= shards:
        columns *= 2
    return columns if shards % columns == 0 else 1


def whole(shape):
    return pl.BlockSpec(shape, lambda *_: (0,) * len(shape))


def row_gather(shards, columns, own, gathered, local_sem, sends, recvs):
    shard = lax.axis_index("shard")
    lines = shards // columns
    z, x = shard // columns, shard % columns

    def line_copy(source, way, first=False):
        at = source * columns + x
        peer = jnp.clip(z + 1 - 2 * way, 0, lines - 1) * columns + x
        rows = own if first else gathered.at[:, at]
        return remote(rows, gathered.at[:, at], sends.at[way, source], recvs.at[at], shard=peer)

    def wide_copy(source, hop, first=False):
        at = source * columns + x
        peer = z * columns + (x + hop) % columns
        rows = own if first else gathered.at[:, at]
        return remote(rows, gathered.at[:, at], sends.at[1 + hop, source], recvs.at[at], shard=peer)

    def pass_on(source, ways, first=False):
        for way in ways:
            @pl.when(z < lines - 1 if way == 0 else z > 0)
            def _():
                line_copy(source, way, first).start()

        for hop in range(1, columns):
            wide_copy(source, hop, first).start()

    here = pltpu.make_async_copy(own, gathered.at[:, shard], local_sem)

    def begin():
        pass_on(z, (0, 1), True)
        here.start()

    def hop(step):
        @pl.when(z - step >= 0)
        def _():
            line_copy(z - step, 0).wait_recv()
            pass_on(z - step, (0,))

        @pl.when(z + step < lines)
        def _():
            line_copy(z + step, 1).wait_recv()
            pass_on(z + step, (1,))

    def end():
        here.wait()
        for step in range(1, columns):
            peer = z * columns + (x + step) % columns
            for source in range(lines):
                at = source * columns + (x + step) % columns
                remote(gathered.at[:, at], gathered.at[:, at], sends.at[1 + step, source], recvs.at[at], shard=peer).wait_recv()
        for source in range(lines):
            for step in range(1, columns):
                wide_copy(source, step).wait_send()

            @pl.when((z < lines - 1) & (source <= z))
            def _():
                line_copy(source, 0).wait_send()

            @pl.when((z > 0) & (source >= z))
            def _():
                line_copy(source, 1).wait_send()

    return begin, hop, end


def gather_semaphores(shards, columns):
    dma = pltpu.SemaphoreType.DMA
    return [
        dma,
        dma((1 + columns, shards // columns)),
        dma((shards,)),
    ]


def softplus(value):
    small = jnp.exp(-jnp.abs(value))
    ratio = small / (2.0 + small)
    square = ratio * ratio
    series = jnp.full_like(value, 1.0 / 15.0)
    for power in (13, 11, 9, 7, 5, 3, 1):
        series = series * square + 1.0 / power
    return jnp.maximum(value, 0.0) + 2.0 * ratio * series


def pick_columns(value, marks):
    high = value.astype(jnp.bfloat16)
    rest = value - high.astype(jnp.float32)
    mid = rest.astype(jnp.bfloat16)
    low = (rest - mid.astype(jnp.float32)).astype(jnp.bfloat16)
    plain = ((1,), (0,))
    return dots(high, marks, plain) + (dots(mid, marks, plain) + dots(low, marks, plain))


def forward_kernel(
    heads, shards, columns, bounds, slots, rows_in, weight, taps, bias, dt_bias, rate, skip, cot_own,
    packed, product, pre_out, mixed_out, state_out, dt_out, raw_out, cot_all,
    ext, state, *gather_sems,
):
    block = pl.program_id(0)
    blocks = cot_own.shape[0]
    inner = heads * HDIM
    shard = lax.axis_index("shard")
    begin, hop, end = row_gather(shards, columns, cot_own, cot_all, *gather_sems)
    hops = range(1, shards // columns)

    @pl.when(block == 0)
    def _():
        barrier_with([{"shard": (shard + step) % shards} for step in range(1, shards)])
        begin()
        ext[:TAIL, :] = jnp.zeros((TAIL, ext.shape[1]), jnp.float32)
        state[...] = jnp.zeros_like(state)

    for step in hops:
        if (7 * step + 1) // 2 < blocks:
            pl.when(block == (7 * step + 1) // 2)(functools.partial(hop, step))

    normed = dots(place_of_rows(slots[0]), rows_in[0], ((1,), (0,))).astype(jnp.bfloat16)
    packed[...] = normed
    product[...] = dots(normed, weight[...], NT)
    head = lax.broadcasted_iota(jnp.int32, (HEADS, 128), 0)
    lane = lax.broadcasted_iota(jnp.int32, (HEADS, 128), 1)
    marks = ((head == shard * heads + lane) & (lane < heads)).astype(jnp.bfloat16)
    raw = pick_columns(product[:, 2 * inner + SHARED :] + dt_bias[...], marks)
    raw_out[...] = raw
    dt = softplus(raw)
    dt_out[...] = dt

    bounds = (bounds[0], bounds[1])
    dt_t = dt.T[: rate.shape[0], :]
    seg_col, seg_row, run_t, run, carried, tail, keep = block_facts(block, bounds, dt_t, rate[...])
    ext[TAIL:, :] = product[:, inner : 2 * inner + SHARED]
    place = block * BLOCK + lax.broadcasted_iota(jnp.int32, (BLOCK, 1), 0)
    pre = bias[...] + taps[CONV - 1 : CONV, :] * ext[TAIL:, :]
    for back in range(1, CONV):
        same = sequence_of(place - back, bounds) == seg_col
        moved = ext[TAIL - back : TAIL - back + BLOCK, :]
        pre = pre + jnp.where(same, moved, 0.0) * taps[CONV - 1 - back : CONV - back, :]
    ext[:TAIL, :] = ext[BLOCK:, :]
    pre_out[...] = pre
    conv = pre / (1.0 + jnp.exp(-pre))
    values, b_rows, c_rows = conv[:, :inner], conv[:, inner : inner + STATE], conv[:, inner + STATE :]
    fed = values * widen(dt, heads)
    rows = lax.broadcasted_iota(jnp.int32, (BLOCK, BLOCK), 0)
    cols = lax.broadcasted_iota(jnp.int32, (BLOCK, BLOCK), 1)
    allowed = (seg_col == seg_row) & (rows >= cols)
    b_parts, c_parts = split(b_rows), split(c_rows)
    scores = jnp.where(allowed, dot3(c_parts, b_parts, NT), 0.0)
    old = state[...]
    state_out[0] = old
    output = widen(carried, heads) * dot3(c_parts, old)
    low_half = lax.broadcasted_iota(jnp.int32, (BLOCK, 2 * HDIM), 1) < HDIM
    inside = []
    for h in range(0, heads, 2):
        pair = jnp.concatenate(split(fed[:, h * HDIM : (h + 2) * HDIM]), axis=1)
        found = []
        for k in (h, h + 1):
            mixing = jnp.exp(jnp.minimum(run[:, k : k + 1] - run_t[k : k + 1, :], 0.0)) * scores
            found.append(dot_wide(mixing, pair))
        inside.append(jnp.where(low_half, found[0], found[1]))
    mixed = output + jnp.concatenate(inside, axis=1) + skip[...] * values
    mixed_out[...] = mixed
    state[...] = widen(keep, heads) * old + dot3(b_rows.T, widen(tail, heads) * fed)

    @pl.when(block == blocks - 1)
    def _():
        for step in hops:
            if (7 * step + 1) // 2 >= blocks:
                hop(step)
        end()


def cotangent_kernel(
    shards, slots, rows_in, weight, mixed, gate, gain,
    packed, product, sums_out, own_sums, sums_in, sums_send, sums_recv,
):
    block = pl.program_id(0)
    shard = lax.axis_index("shard")

    @pl.when(block == 0)
    def _():
        barrier_with([{"shard": (shard + step) % shards} for step in range(1, shards)])

    cot = dots(place_of_rows(slots[0]), rows_in[0], ((1,), (0,))).astype(jnp.bfloat16)
    packed[...] = cot
    d_out = dots(cot, weight[...], NT)
    product[...] = d_out
    gate_now = gate[...]
    gated = mixed[...] * (gate_now / (1.0 + jnp.exp(-gate_now)))
    squares = jnp.sum(gated * gated, axis=1, keepdims=True)
    products = jnp.sum(gated * gain[...] * d_out, axis=1, keepdims=True)
    lane = lax.broadcasted_iota(jnp.int32, (BLOCK, 128), 1)
    both = jnp.where(lane == 0, squares, jnp.where(lane == 1, products, 0.0))
    here = pl.ds(pl.multiple_of(block * BLOCK, BLOCK), BLOCK)
    own_sums[:, here] = both.T[:8, :]

    def push(step, at):
        return remote(
            own_sums.at[:, at], sums_in.at[step - 1, :, at], sums_send.at[step], sums_recv.at[step],
            shard=(shard + step) % shards,
        )

    for step in range(1, shards):
        push(step, here).start()

    @pl.when(block == pl.num_programs(0) - 1)
    def _():
        everything = pl.ds(0, own_sums.shape[1])
        for step in range(1, shards):
            push(step, everything).wait()
        found = own_sums[...]
        for step in range(1, shards):
            found = found + sums_in[step - 1]
        sums_out[...] = found * (1.0 / INNER)


def backward_kernel(
    heads, blocks, shards, columns, bounds, slots, pre, mixed, gate, d_out, conv_v, sums, state_in, dt_cols, cot,
    taps, rate, skip, gain, marks, out_own,
    d_cols, d_bc, d_dt, grads, grad_rate, grad_out, no_rows, home, out_all,
    ext, carry, bc_rows, bc_wide, bc_sum, bc_in, late_rows, wide_send, wide_recv, bc_send, bc_recv, home_send, home_recv, local_sem, *gather_sems,
):
    step = pl.program_id(0)
    block = blocks - 1 - step
    inner = heads * HDIM
    shard = lax.axis_index("shard")
    shared = SHARED // shards
    lines = shards // columns
    z, x = shard // columns, shard % columns
    begin, hop, end = row_gather(shards, columns, out_own, out_all, *gather_sems)
    hops = range(1, shards // columns)

    @pl.when(step == 0)
    def _():
        barrier_with([{"shard": (shard + turn) % shards} for turn in range(1, shards)])
        begin()
        ext[BLOCK:, :] = jnp.zeros((TAIL, ext.shape[1]), jnp.float32)
        carry[...] = jnp.zeros_like(carry)
        grads[...] = jnp.zeros_like(grads)
        grad_rate[...] = jnp.zeros_like(grad_rate)
        grad_out[...] = jnp.zeros_like(grad_out)

    for turn in hops:
        if 2 * turn < blocks:
            pl.when(step == 2 * turn)(functools.partial(hop, turn))

    bounds = (bounds[0], bounds[1])
    dt = dt_cols[...]
    dt_t = dt.T[: rate.shape[0], :]
    seg_col, seg_row, run_t, run, carried, tail, keep = block_facts(block, bounds, dt_t, rate[...])
    sums_cols = sums[...].T
    r_out = lax.rsqrt(sums_cols[:, 0:1] + 1e-05)
    inside = sums_cols[:, 1:2]
    gate_now = gate[...]
    gate_sig = 1.0 / (1.0 + jnp.exp(-gate_now))
    act = gate_now * gate_sig
    mixed_now = mixed[...]
    gated = mixed_now * act
    d_out_now = d_out[...]
    normed_out = (gated * r_out * gain[...]).astype(jnp.bfloat16)
    to_home = dots(place_of_rows(slots[0]), normed_out, ((0,), (0,)))
    per = BLOCK // shards
    if per % 16 == 0:
        no_rows[0] = to_home.astype(jnp.bfloat16).reshape(shards, per, inner)
    else:
        for turn in range(shards):
            no_rows[0, turn] = to_home[turn * per : (turn + 1) * per].astype(jnp.bfloat16)
    half = home.shape[1]

    def push_home(turn, at):
        peer = (shard + turn) % shards
        return remote(late_rows.at[at, peer], home.at[shard, at], home_send.at[turn], home_recv.at[turn], shard=peer)

    @pl.when(step < blocks - half)
    def _():
        late_rows[block - half] = no_rows[0]
        for turn in range(1, shards):
            push_home(turn, pl.ds(block - half, 1)).start()
    grad_out[...] += dots(normed_out, cot[...], ((0,), (0,)))
    d_gated = r_out * (gain[...] * d_out_now - gated * (r_out * r_out) * inside)
    dy = d_gated * act
    d_cols[:, :inner] = (d_gated * mixed_now * (gate_sig * (1.0 + gate_now * (1.0 - gate_sig)))).astype(jnp.bfloat16)
    grads[5:6, :] += jnp.sum(gated * r_out * d_out_now, axis=0, keepdims=True)
    pre_now = pre[...]
    sig = 1.0 / (1.0 + jnp.exp(-pre_now))
    conv = pre_now * sig
    values, b_rows, c_rows = conv[:, :inner], conv[:, inner : inner + STATE], conv[:, inner + STATE :]
    grads[6:7, :] += jnp.sum(dy * values, axis=0, keepdims=True)
    dt_wide = widen(dt, heads)
    fed = values * dt_wide
    old, after = state_in[0], carry[...]
    b_parts, c_parts, old_parts, after_parts = split(b_rows), split(c_rows), split(old), split(after)
    carried_wide, tail_wide, keep_wide = widen(carried, heads), widen(tail, heads), widen(keep, heads)
    rows = lax.broadcasted_iota(jnp.int32, (BLOCK, BLOCK), 0)
    cols = lax.broadcasted_iota(jnp.int32, (BLOCK, BLOCK), 1)
    allowed = (seg_col == seg_row) & (cols >= rows)
    scores_t = jnp.where(allowed, dot3(b_parts, c_parts, NT), 0.0)
    low_half = lax.broadcasted_iota(jnp.int32, (BLOCK, 2 * HDIM), 1) < HDIM
    d_scores_t = jnp.zeros((BLOCK, BLOCK), jnp.float32)
    d_fed, row_terms, col_terms = [], [], []
    for h in range(0, heads, 2):
        fed_pair = fed[:, h * HDIM : (h + 2) * HDIM]
        fed_high, fed_low = split(fed_pair)
        dy_high, dy_low = split(dy[:, h * HDIM : (h + 2) * HDIM])
        dy_wide = jnp.concatenate([dy_high, dy_low], axis=1)
        found = []
        for k in (h, h + 1):
            own = low_half if k == h else jnp.logical_not(low_half)
            left = jnp.concatenate(
                [beside(fed_high, fed_low, own), jnp.where(own, fed_high, 0.0).astype(jnp.bfloat16)], axis=1
            )
            right = jnp.concatenate([beside(dy_high, dy_high, own), dy_low], axis=1)
            d_mixing = dots(left, right, NT)
            decay = jnp.exp(jnp.minimum(run_t[k : k + 1, :] - run[:, k : k + 1], 0.0))
            mixing = decay * scores_t
            d_scores_t = d_scores_t + decay * d_mixing
            flow = mixing * d_mixing
            row_terms.append(jnp.sum(flow, axis=0, keepdims=True))
            col_terms.append(jnp.sum(flow, axis=1, keepdims=True))
            found.append(dot_wide(mixing, dy_wide))
        d_fed.append(jnp.where(low_half, found[0], found[1]))
    d_scores_t = split(jnp.where(allowed, d_scores_t, 0.0))
    fed_tail = fed * tail_wide
    dy_carried = dy * carried_wide
    d_fed_out = tail_wide * dot3(b_parts, after_parts)
    d_fed = jnp.concatenate(d_fed, axis=1) + d_fed_out
    dy_parts, tail_parts = split(dy_carried), split(fed_tail)
    here = pl.ds(pl.multiple_of(block * BLOCK, BLOCK), BLOCK)
    bc_now = jnp.concatenate(
        [
            (dot3(d_scores_t, c_parts) + dot3(tail_parts, after_parts, NT)).T,
            (dot3(d_scores_t, b_parts, ((0,), (0,))) + dot3(dy_parts, old_parts, NT)).T,
        ],
        axis=0,
    )
    bc_rows[:, :, :, here] = bc_now.reshape(lines, columns, shared, BLOCK)

    def at_step(turn):
        return pl.ds(pl.multiple_of((blocks - 1 - turn) * BLOCK, BLOCK), BLOCK)

    def push_wide(turn, hop):
        to = (x + hop) % columns
        return remote(
            bc_rows.at[:, to, :, at_step(turn)], bc_wide.at[hop - 1, :, :, at_step(turn)],
            wide_send.at[hop - 1, turn], wide_recv.at[hop - 1, turn], shard=z * columns + to,
        )

    def push_line(hop, at):
        to = (z + hop) % lines
        return remote(bc_sum.at[to, :, at], bc_in.at[hop - 1, :, at], bc_send.at[hop], bc_recv.at[hop], shard=to * columns + x)

    def add_wide(turn):
        found = bc_rows[:, x, :, at_step(turn)]
        for hop in range(1, columns):
            push_wide(turn, hop).wait_recv()
            found = found + bc_wide[hop - 1, :, :, at_step(turn)]
        bc_sum[:, :, at_step(turn)] = found
        for hop in range(1, lines):
            push_line(hop, at_step(turn)).start()

    for hop_x in range(1, columns):
        push_wide(step, hop_x).start()

    lag = min(3, blocks - 1)

    @pl.when(step >= lag)
    def _():
        add_wide(step - lag)

    head_count = dt_t.shape[0]
    pad = [jnp.zeros((1, BLOCK), jnp.float32)] * (head_count - heads)
    pad_col = [jnp.zeros((BLOCK, 1), jnp.float32)] * (head_count - heads)
    d_run = jnp.concatenate(row_terms + pad, axis=0) - jnp.concatenate(col_terms + pad_col, axis=1).T
    d_run = d_run + head_sums(dy_carried * dot3(c_parts, old_parts), marks[...])
    leaving = head_sums(fed * d_fed_out, marks[...])
    kept = jnp.sum(old * after, axis=0, keepdims=True) * keep_wide
    kept = jnp.sum(marks[...].astype(jnp.float32) * kept, axis=1, keepdims=True)
    at_end = lax.broadcasted_iota(jnp.int32, (head_count, BLOCK), 1) == BLOCK - 1
    total = jnp.sum(leaving, axis=1, keepdims=True) + kept
    d_run = d_run - leaving + jnp.where(at_end, total, 0.0)
    d_log = running_sum(d_run, reverse=True)
    d_dt[...] = d_log * rate[...] + head_sums(values * d_fed, marks[...])
    grad_rate[...] += d_log * (dt_t * rate[...])
    carry[...] = keep_wide * after + dot3(c_rows.T, dy_parts)
    pre_v, sig_v = pre_now[:, :inner], sig[:, :inner]
    d_values = dt_wide * d_fed + skip[...] * dy
    d_pre = d_values * (sig_v * (1.0 + pre_v * (1.0 - sig_v)))
    ext[:BLOCK, :] = d_pre
    place = block * BLOCK + lax.broadcasted_iota(jnp.int32, (BLOCK, 1), 0)
    conv_in = conv_v[...]
    d_conv = taps[CONV - 1 : CONV, :] * d_pre
    grads[CONV - 1 : CONV, :] += jnp.sum(conv_in * d_pre, axis=0, keepdims=True)
    grads[CONV : CONV + 1, :] += jnp.sum(d_pre, axis=0, keepdims=True)
    for ahead in range(1, CONV):
        same = sequence_of(place + ahead, bounds) == seg_col
        moved = jnp.where(same, ext[ahead : ahead + BLOCK, :], 0.0)
        d_conv = d_conv + taps[CONV - 1 - ahead : CONV - ahead, :] * moved
        grads[CONV - 1 - ahead : CONV - ahead, :] += jnp.sum(conv_in * moved, axis=0, keepdims=True)
    ext[BLOCK:, :] = ext[:TAIL, :]
    d_cols[:, inner:] = d_conv.astype(jnp.bfloat16)

    @pl.when(step == blocks - 1)
    def _():
        everything = pl.ds(0, bc_sum.shape[2])
        for turn in range(blocks - lag, blocks):
            add_wide(turn)
        for turn in hops:
            if 2 * turn >= blocks:
                hop(turn)
        end()
        here = pltpu.make_async_copy(late_rows.at[:, shard], home.at[shard], local_sem)
        here.start()
        for turn in range(1, lines):
            push_line(turn, everything).wait()
        found = bc_sum[z]
        for turn in range(1, lines):
            found = found + bc_in[turn - 1]
        d_bc[...] = found
        for turn in range(1, shards):
            push_home(turn, pl.ds(0, half)).wait()
        here.wait()
        for turn in range(blocks):
            for hop_x in range(1, columns):
                push_wide(turn, hop_x).wait_send()


def mixer_forward(shards, bounds, slots, rows_in, weight, taps, bias, dt_bias, rate, skip, cot_own):
    blocks, _, width = rows_in.shape
    columns = grid_columns(shards)
    total, inner, kept = blocks * BLOCK, INNER // shards, weight.shape[0]
    heads = inner // HDIM
    f32, bf16, any_space = jnp.float32, jnp.bfloat16, pl.BlockSpec(memory_space=pl.ANY)

    def block_of(lanes):
        return pl.BlockSpec((BLOCK, lanes), lambda i: (i, 0))

    return pl.pallas_call(
        functools.partial(forward_kernel, heads, shards, columns),
        grid=(blocks,),
        in_specs=[
            pl.BlockSpec(memory_space=pltpu.SMEM),
            pl.BlockSpec((1, 1, BLOCK), lambda i: (i, 0, 0)),
            pl.BlockSpec((1, BLOCK, width), lambda i: (i, 0, 0)),
            whole(weight.shape),
            whole(taps.shape),
            whole(bias.shape),
            whole(dt_bias.shape),
            whole(rate.shape),
            whole(skip.shape),
            any_space,
        ],
        out_specs=[
            block_of(width),
            block_of(kept),
            block_of(inner + SHARED),
            block_of(inner),
            pl.BlockSpec((1, STATE, inner), lambda i: (i, 0, 0)),
            block_of(128),
            block_of(128),
            any_space,
        ],
        out_shape=[
            jax.ShapeDtypeStruct((total, width), bf16),
            jax.ShapeDtypeStruct((total, kept), f32),
            jax.ShapeDtypeStruct((total, inner + SHARED), f32),
            jax.ShapeDtypeStruct((total, inner), f32),
            jax.ShapeDtypeStruct((blocks, STATE, inner), f32),
            jax.ShapeDtypeStruct((total, 128), f32),
            jax.ShapeDtypeStruct((total, 128), f32),
            jax.ShapeDtypeStruct((cot_own.shape[0], shards) + cot_own.shape[1:], bf16),
        ],
        scratch_shapes=[
            pltpu.VMEM((BLOCK + TAIL, inner + SHARED), f32),
            pltpu.VMEM((STATE, inner), f32),
            *gather_semaphores(shards, columns),
        ],
        compiler_params=pltpu.CompilerParams(
            collective_id=2, has_side_effects=True, vmem_limit_bytes=56 * 1024 * 1024
        ),
        cost_estimate=pl.CostEstimate(flops=0, bytes_accessed=300_000_000, transcendentals=0),
        name="mixer_forward",
    )(bounds, slots, rows_in, weight, taps, bias, dt_bias, rate, skip, cot_own)


def pack_cotangent(shards, slots, rows_in, weight, mixed, projected, gain):
    blocks, _, width = rows_in.shape
    total, inner = mixed.shape

    def block_of(lanes):
        return pl.BlockSpec((BLOCK, lanes), lambda i: (i, 0))

    return pl.pallas_call(
        functools.partial(cotangent_kernel, shards),
        grid=(blocks,),
        in_specs=[
            pl.BlockSpec((1, 1, BLOCK), lambda i: (i, 0, 0)),
            pl.BlockSpec((1, BLOCK, width), lambda i: (i, 0, 0)),
            whole(weight.shape),
            block_of(inner),
            block_of(inner),
            whole(gain.shape),
        ],
        out_specs=[block_of(width), block_of(inner), whole((8, total))],
        out_shape=[
            jax.ShapeDtypeStruct((total, width), jnp.bfloat16),
            jax.ShapeDtypeStruct((total, inner), jnp.float32),
            jax.ShapeDtypeStruct((8, total), jnp.float32),
        ],
        scratch_shapes=[
            pltpu.VMEM((8, total), jnp.float32),
            pltpu.VMEM((shards - 1, 8, total), jnp.float32),
            pltpu.SemaphoreType.DMA((shards,)),
            pltpu.SemaphoreType.DMA((shards,)),
        ],
        compiler_params=pltpu.CompilerParams(
            collective_id=5, has_side_effects=True, vmem_limit_bytes=48 * 1024 * 1024
        ),
        cost_estimate=pl.CostEstimate(flops=0, bytes_accessed=60_000_000, transcendentals=0),
        name="pack_cotangent",
    )(slots, rows_in, weight, mixed, projected, gain)


def mixer_backward(
    shards, bounds, slots, pre, mixed, projected, d_out, sums, states, dt_cols, cot, taps, rate, skip, gain, out_own
):
    total, inner = d_out.shape
    heads, blocks, padded = inner // HDIM, total // BLOCK, rate.shape[0]
    shared = SHARED // shards
    columns = grid_columns(shards)
    marks = (jnp.arange(padded)[:, None] == jnp.arange(inner)[None, :] // HDIM).astype(jnp.bfloat16)

    def block_of(width, column):
        return pl.BlockSpec((BLOCK, width), lambda i: (blocks - 1 - i, column))

    return pl.pallas_call(
        functools.partial(backward_kernel, heads, blocks, shards, columns),
        grid_spec=pltpu.PrefetchScalarGridSpec(
            num_scalar_prefetch=0,
            grid=(blocks,),
            in_specs=[
                pl.BlockSpec(memory_space=pltpu.SMEM),
                pl.BlockSpec((1, 1, BLOCK), lambda i: (blocks - 1 - i, 0, 0)),
                block_of(inner + SHARED, 0),
                block_of(inner, 0),
                block_of(inner, 0),
                block_of(inner, 0),
                block_of(inner, 1),
                pl.BlockSpec((8, BLOCK), lambda i: (0, blocks - 1 - i)),
                pl.BlockSpec((1, STATE, inner), lambda i: (blocks - 1 - i, 0, 0)),
                block_of(dt_cols.shape[1], 0),
                block_of(cot.shape[1], 0),
                whole(taps.shape),
                whole(rate.shape),
                whole(skip.shape),
                whole(gain.shape),
                whole(marks.shape),
                pl.BlockSpec(memory_space=pl.ANY),
            ],
            out_specs=[
                block_of(2 * inner, 0),
                whole((shared, total)),
                pl.BlockSpec((padded, BLOCK), lambda i: (0, blocks - 1 - i)),
                whole((8, inner)),
                whole((padded, BLOCK)),
                whole((inner, cot.shape[1])),
                pl.BlockSpec((1, shards, BLOCK // shards, inner), lambda i: (blocks - 1 - i, 0, 0, 0)),
                pl.BlockSpec(memory_space=pl.ANY),
                pl.BlockSpec(memory_space=pl.ANY),
            ],
            scratch_shapes=[
                pltpu.VMEM((BLOCK + TAIL, inner), jnp.float32),
                pltpu.VMEM((STATE, inner), jnp.float32),
                pltpu.VMEM((shards // columns, columns, shared, total), jnp.float32),
                pltpu.VMEM((max(columns - 1, 1), shards // columns, shared, total), jnp.float32),
                pltpu.VMEM((shards // columns, shared, total), jnp.float32),
                pltpu.VMEM((shards // columns - 1, shared, total), jnp.float32),
                pltpu.VMEM((blocks // 2, shards, BLOCK // shards, inner), jnp.bfloat16),
                pltpu.SemaphoreType.DMA((max(columns - 1, 1), blocks)),
                pltpu.SemaphoreType.DMA((max(columns - 1, 1), blocks)),
                pltpu.SemaphoreType.DMA((shards,)),
                pltpu.SemaphoreType.DMA((shards,)),
                pltpu.SemaphoreType.DMA((shards,)),
                pltpu.SemaphoreType.DMA((shards,)),
                pltpu.SemaphoreType.DMA,
                *gather_semaphores(shards, columns),
            ],
        ),
        out_shape=[
            jax.ShapeDtypeStruct((total, 2 * inner), jnp.bfloat16),
            jax.ShapeDtypeStruct((shared, total), jnp.float32),
            jax.ShapeDtypeStruct((padded, total), jnp.float32),
            jax.ShapeDtypeStruct((8, inner), jnp.float32),
            jax.ShapeDtypeStruct((padded, BLOCK), jnp.float32),
            jax.ShapeDtypeStruct((inner, cot.shape[1]), jnp.float32),
            jax.ShapeDtypeStruct((blocks, shards, BLOCK // shards, inner), jnp.bfloat16),
            jax.ShapeDtypeStruct((shards, blocks // 2, BLOCK // shards, inner), jnp.bfloat16),
            jax.ShapeDtypeStruct((out_own.shape[0], shards) + out_own.shape[1:], jnp.bfloat16),
        ],
        compiler_params=pltpu.CompilerParams(
            collective_id=3, has_side_effects=True, vmem_limit_bytes=56 * 1024 * 1024
        ),
        cost_estimate=pl.CostEstimate(flops=0, bytes_accessed=200_000_000, transcendentals=0),
        name="mixer_backward",
    )(bounds, slots, pre, mixed, projected, d_out, projected, sums, states, dt_cols, cot, taps, rate, skip, gain, marks, out_own)


def piece_rows(shards, groups):
    chunks = (2 * INNER // shards + SHARED // shards) // CHUNK
    return -(-chunks // groups) * CHUNK


def column_runs(shards, groups):
    inner, width = INNER // shards, (2 * INNER + SHARED + HEADS) // groups
    kept = 2 * inner + SHARED + HEADS
    quarter = kept // groups
    spans = []
    for shard in range(shards):
        spans.append((inner * shard, shard, 0, inner))
        spans.append((INNER + inner * shard, shard, inner, inner))
    spans.append((2 * INNER, None, 2 * inner, SHARED + HEADS))
    runs = []
    for column, shard, row, length in spans:
        while length > 0:
            step = min(length, width - column % width, quarter - row % quarter)
            runs.append((column // width, column % width, shard, row, step))
            column, row, length = column + step, row + step, length - step
    return runs


def front_kernel(
    shards, groups, columns,
    rows_in, gain, cot_in, weight_in, out_in, slot_row, slot_col,
    rows_all, weight_all, out_all, slot_all, cot_own, out_cast,
    rows_own, weight_own, out_own, slot_own,
    run_send, run_recv, share_send, share_recv, out_send, out_recv, slot_send, slot_recv, local_sem, *gather_sems,
):
    shard, group = lax.axis_index("shard"), lax.axis_index("group")
    lines, rows_y = shards // columns, groups // 2
    y, core = group // 2, group % 2
    mate = y * 2 + 1 - core
    quarter = weight_all.shape[0] // groups
    depth = weight_own.shape[1]
    out_width = out_own.shape[1]
    everyone = []
    for step in range(1, shards * groups):
        other_shard = (shard + step % shards) % shards
        other_group = (group + step // shards) % groups
        everyone.append({"shard": other_shard, "group": other_group})
    barrier_with(everyone)

    count = rows_in.shape[0]
    below = (slot_col[...] < slot_row[...]).astype(jnp.int32).astype(jnp.float32)
    rank = jnp.sum(below, axis=0, keepdims=True).astype(jnp.int32)
    sort = (lax.broadcasted_iota(jnp.int32, (count, count), 0) == rank).astype(jnp.bfloat16)
    value = rows_in[...]
    scale = lax.rsqrt(jnp.sum(value * value, axis=1, keepdims=True) * (1.0 / value.shape[1]) + 1e-05)
    value = (value * scale * gain[...]).astype(jnp.bfloat16)
    rows_own[...] = dots(sort, value, ((1,), (0,))).astype(jnp.bfloat16).reshape(rows_own.shape)
    begin, hop, end = row_gather(shards, columns, rows_own, rows_all, *gather_sems)
    begin()
    slots = slot_row[...]
    high = slots // 256
    both = jnp.where(lax.broadcasted_iota(jnp.int32, (8, count), 0) == 0, high, slots - 256 * high)
    both = dots(both.astype(jnp.float32).astype(jnp.bfloat16), sort, NT)
    slot_own[...] = jnp.broadcast_to(256.0 * both[0:1, :] + both[1:2, :], (8, count)).astype(jnp.int32)
    out_own[...] = out_in[...].astype(jnp.bfloat16)
    weight_own[...] = weight_in[...].astype(jnp.bfloat16)

    def slot_copy(step):
        return remote(slot_own, slot_all.at[shard], slot_send.at[step], slot_recv.at[step], shard=(shard + step) % shards)

    for step in range(1, shards):
        slot_copy(step).start()
    slot_here = pltpu.make_async_copy(slot_own, slot_all.at[shard], local_sem.at[0])
    slot_here.start()

    runs = column_runs(shards, groups)
    lanes = pl.ds(pl.multiple_of(shard * depth, depth), depth)
    jobs = {owner: [] for owner in range(groups)}
    for owner, column, target, row, length in runs:
        for to in range(shards) if target is None else (target,):
            jobs[owner].append((column, to, row, length))

    def run_copy(number, column, to, row, length):
        return remote(
            weight_own.at[pl.ds(column, length)], weight_all.at[pl.ds(row, length), lanes],
            run_send.at[number], run_recv, shard=to, group=row // quarter,
        )

    def each_run(act):
        for owner in range(groups):
            @pl.when(group == owner)
            def _():
                for number, (column, to, row, length) in enumerate(jobs[owner]):
                    if row // quarter == owner:
                        here = shard == to
                        act(number, column, to, row, length, here)
                    else:
                        act(number, column, to, row, length, None)

    def start_run(number, column, to, row, length, here):
        if here is None:
            run_copy(number, column, to, row, length).start()
            return

        @pl.when(here)
        def _():
            pltpu.make_async_copy(weight_own.at[pl.ds(column, length)], weight_all.at[pl.ds(row, length), lanes], run_recv).start()

        @pl.when(jnp.logical_not(here))
        def _():
            run_copy(number, column, to, row, length).start()

    def end_run(number, column, to, row, length, here):
        if here is None:
            run_copy(number, column, to, row, length).wait_send()
            return

        @pl.when(jnp.logical_not(here))
        def _():
            run_copy(number, column, to, row, length).wait_send()

    each_run(start_run)

    def own_part(ref, part):
        if ref is out_all:
            return ref.at[:, pl.ds(pl.multiple_of(part * out_width, out_width), out_width)]
        return ref.at[pl.ds(pl.multiple_of(part * quarter, quarter), quarter)]

    def share(ref, part, sends, recvs, number, peer, first=None):
        source = own_part(ref, part) if first is None else first
        return remote(source, own_part(ref, part), sends.at[number], recvs.at[part], group=peer)

    def share_start(ref, sends, recvs, first=None):
        share(ref, group, sends, recvs, 0, mate, first).start()
        for step in range(1, rows_y):
            share(ref, group, sends, recvs, step, (y + step) % rows_y * 2 + core, first).start()

    def share_pass(ref, sends, recvs):
        for step in range(1, rows_y):
            part = (y + step) % rows_y * 2 + core
            share(ref, part, sends, recvs, step, part).wait_recv()
            share(ref, part, sends, recvs, rows_y - 1 + step, mate).start()

    def share_end(ref, sends, recvs):
        for turn in range(rows_y):
            part = turn * 2 + 1 - core
            share(ref, part, sends, recvs, 0, mate).wait_recv()
        for number in range(2 * rows_y - 1):
            share(ref, group, sends, recvs, number, mate).wait_send()

    out_here = pltpu.make_async_copy(out_own, own_part(out_all, group), local_sem.at[1])
    out_here.start()
    share_start(out_all, out_send, out_recv, out_own)
    out_cast[...] = out_own[...]
    cot_own[...] = (
        dots(sort, cot_in[...].astype(jnp.bfloat16), ((1,), (0,))).astype(jnp.bfloat16).reshape(cot_own.shape)
    )

    for step in range(1, lines):
        hop(step)
        if step == 1:
            share_pass(out_all, out_send, out_recv)
            kept = own_part(weight_all, group)
            pltpu.make_async_copy(kept, kept, run_recv).wait()
            share_start(weight_all, share_send, share_recv)
    share_pass(weight_all, share_send, share_recv)

    end()
    out_here.wait()
    share_end(out_all, out_send, out_recv)
    share_end(weight_all, share_send, share_recv)
    each_run(end_run)
    for step in range(1, shards):
        slot_copy(step).wait()
    slot_here.wait()


def front_exchange(shards, groups, rows_in, gain, cot_in, weight_in, out_in, slots):
    columns = grid_columns(shards)
    rows_y = groups // 2
    count, width = rows_in.shape
    blocks, per = shards * count // BLOCK, BLOCK // shards
    kept = 2 * INNER // shards + SHARED + HEADS
    any_space, vmem = pl.BlockSpec(memory_space=pl.ANY), pl.BlockSpec(memory_space=pltpu.VMEM)
    dma, bf16 = pltpu.SemaphoreType.DMA, jnp.bfloat16
    counts = {}
    for owner, _, target, _, _ in column_runs(shards, groups):
        counts[owner] = counts.get(owner, 0) + (shards if target is None else 1)
    return pl.pallas_call(
        functools.partial(front_kernel, shards, groups, columns),
        in_specs=[vmem] * 7,
        out_specs=[any_space] * 4 + [vmem] * 2,
        out_shape=[
            jax.ShapeDtypeStruct((blocks, shards, per, width), bf16),
            jax.ShapeDtypeStruct((kept, width), bf16),
            jax.ShapeDtypeStruct((out_in.shape[0], out_in.shape[1] * groups), bf16),
            jax.ShapeDtypeStruct((shards, 8, count), jnp.int32),
            jax.ShapeDtypeStruct((blocks, per, width), bf16),
            jax.ShapeDtypeStruct(out_in.shape, bf16),
        ],
        scratch_shapes=[
            pltpu.VMEM((blocks, per, width), bf16),
            pltpu.VMEM(weight_in.shape, bf16),
            pltpu.VMEM(out_in.shape, bf16),
            pltpu.VMEM((8, count), jnp.int32),
            dma((max(counts.values()),)),
            dma,
            dma((2 * rows_y - 1,)),
            dma((groups,)),
            dma((2 * rows_y - 1,)),
            dma((groups,)),
            dma((shards,)),
            dma((shards,)),
            dma((2,)),
            *gather_semaphores(shards, columns),
        ],
        compiler_params=pltpu.CompilerParams(
            collective_id=4, has_side_effects=True, vmem_limit_bytes=48 * 1024 * 1024
        ),
        cost_estimate=pl.CostEstimate(flops=0, bytes_accessed=300_000_000, transcendentals=0),
        name="front_exchange",
    )(rows_in, gain[None, :], cot_in, weight_in, out_in, slots[None, :], slots[:, None])


def unpack_kernel(
    shards, slots, d_cols, d_rest, normed, weight, weight_rest, no_rows,
    partial, grad, home, moved_cols, moved_rest, local_sem, home_send, home_recv,
):
    step = pl.program_id(0)
    shard = lax.axis_index("shard")
    main = d_cols.shape[1]
    per = BLOCK // shards

    def push(turn):
        peer = (shard + turn) % shards
        return remote(no_rows.at[first, peer], home.at[shard], home_send.at[turn], home_recv.at[turn], shard=peer)

    first = pl.ds(0, home.shape[1])
    here = pltpu.make_async_copy(no_rows.at[first, shard], home.at[shard], local_sem)

    @pl.when(step == 0)
    def _():
        barrier_with([{"shard": (shard + turn) % shards} for turn in range(1, shards)])
        for turn in range(1, shards):
            push(turn).start()
        here.start()
        grad[...] = jnp.zeros_like(grad)

    several = d_cols.shape[0] // BLOCK
    for turn in range(several):
        rows = pl.ds(turn * BLOCK, BLOCK)
        place = place_of_rows(slots[turn])
        moved_cols[rows, :] = dots(place, d_cols[rows, :], ((0,), (0,))).astype(jnp.bfloat16)
        moved_rest[rows, :] = dots(place, d_rest[rows, :], ((0,), (0,))).astype(jnp.bfloat16)
    tile = 512
    for lane in range(0, weight.shape[1], tile):
        lanes = pl.ds(lane, tile)
        found = dots(moved_cols[...], weight[:, lanes], ((1,), (0,)))
        found = found + dots(moved_rest[...], weight_rest[:, lanes], ((1,), (0,)))
        for turn in range(several):
            rows = found[turn * BLOCK : (turn + 1) * BLOCK]
            partial[:, turn, :, lanes] = rows.reshape(shards, per, tile)
    grad[:main, :] += dots(d_cols[...], normed[...], ((0,), (0,)))
    grad[main:, :] += dots(d_rest[...], normed[...], ((0,), (0,)))

    @pl.when(step == pl.num_programs(0) - 1)
    def _():
        for turn in range(1, shards):
            push(turn).wait()
        here.wait()


def project_back(slots, d_cols, d_rest, normed, weight, weight_rest, no_rows, shards):
    blocks, width = slots.shape[0], normed.shape[1]
    per, main, rest = BLOCK // shards, d_cols.shape[1], d_rest.shape[1]
    several = 2
    any_space = pl.BlockSpec(memory_space=pl.ANY)

    def block_of(columns):
        return pl.BlockSpec((several * BLOCK, columns), lambda i: (i, 0))

    return pl.pallas_call(
        functools.partial(unpack_kernel, shards),
        grid=(blocks // several,),
        in_specs=[
            pl.BlockSpec((several, 1, BLOCK), lambda i: (i, 0, 0)),
            block_of(main),
            block_of(rest),
            block_of(width),
            pl.BlockSpec((main, width), lambda i: (0, 0)),
            whole(weight_rest.shape),
            any_space,
        ],
        out_specs=[
            pl.BlockSpec((shards, several, per, width), lambda i: (0, i, 0, 0)),
            whole((main + rest, width)),
            any_space,
        ],
        out_shape=[
            jax.ShapeDtypeStruct((shards, blocks, per, width), jnp.float32),
            jax.ShapeDtypeStruct((main + rest, width), jnp.float32),
            jax.ShapeDtypeStruct((shards, blocks // 2) + no_rows.shape[2:], jnp.bfloat16),
        ],
        scratch_shapes=[
            pltpu.VMEM((several * BLOCK, main), jnp.bfloat16),
            pltpu.VMEM((several * BLOCK, rest), jnp.bfloat16),
            pltpu.SemaphoreType.DMA,
            pltpu.SemaphoreType.DMA((shards,)),
            pltpu.SemaphoreType.DMA((shards,)),
        ],
        compiler_params=pltpu.CompilerParams(
            collective_id=6, has_side_effects=True, vmem_limit_bytes=60 * 1024 * 1024
        ),
        cost_estimate=pl.CostEstimate(flops=0, bytes_accessed=90_000_000, transcendentals=0),
        name="project_back",
    )(slots, d_cols, d_rest, normed, weight, weight_rest, no_rows)


def other_place(step, place, count):
    upwards = count - 1 - place
    low = jnp.where(step < upwards, count - 1 - step, step - upwards)
    high = jnp.where(step < place, step, count - 1 - (step - place))
    return jnp.where(2 * place < count, low, high)


def tail_kernel(
    shards, groups, columns, near, direct,
    partial, weight_part, small, scaled_rows,
    rows_out, weight_out, mark_out, small_out, gain_out, core_in, row_in, row_scale_in, small_in, gain_in,
    wide_in, wide_scale, line_in, line_scale,
    held, coded, scales, line_coded, line_scales, got, got_scale, marks, total, other, send_rows, send_scales, row_got, row_scale_got, deal_rows, deal_scales, small_sum, small_got,
    gain_sum, gain_part,
    load_sem, wide_send, wide_recv, line_send, line_recv, core_send, core_recv, row_send, row_recv,
    deal_send, deal_recv, mark_send, mark_recv, small_send, small_recv, gain_send, gain_recv,
):
    shard, group = lax.axis_index("shard"), lax.axis_index("group")
    lines = shards // columns
    rows_y = groups // 2
    z, x = shard // columns, shard % columns
    y, core = group // 2, group % 2
    count = held.shape[0]
    owned, depth = weight_out.shape
    piece, chunk = total.shape[0], CHUNK
    inner, shared = INNER // shards, SHARED // shards

    def load(src, dst):
        copy = pltpu.make_async_copy(src, dst, load_sem)
        copy.start()
        copy.wait()

    shard_peers = [(shard + step) % shards for step in range(1, shards)]
    group_peers = [(group + step) % groups for step in range(1, groups)]
    if direct:
        barrier_with(
            [
                {"shard": (shard + step % shards) % shards, "group": (group + step // shards) % groups}
                for step in range(1, shards * groups)
            ]
        )
    else:
        barrier_with([{"shard": peer} for peer in shard_peers] + [{"group": peer} for peer in group_peers])

    mate = y * 2 + 1 - core

    def core_copy(turn):
        return remote(piece_of(turn * 2 + 1 - core), core_in.at[turn], core_send.at[turn], core_recv.at[turn], group=mate)

    def piece_of(owner):
        return weight_part.at[pl.ds(pl.multiple_of(owner * piece, piece), piece)]

    for turn in range(rows_y if direct else 0):
        core_copy(turn).start()

    def small_copy(step):
        return remote(small, small_in.at[step - 1], small_send.at[step - 1], small_recv.at[step - 1], group=(group + step) % groups)

    for step in range(1, groups):
        small_copy(step).start()

    def code(coded_to, scales_to, values=held, lot=32):
        @pl.loop(0, values.shape[0] // lot, unroll=2)
        def _(turn):
            rows = pl.ds(pl.multiple_of(turn * lot, lot), lot)
            value = values[rows, :]
            most = jnp.maximum(jnp.max(jnp.abs(value), axis=1, keepdims=True), 1e-30)
            coded_to[rows, :] = jnp.round(value * (32767.0 / most)).astype(jnp.int32).astype(jnp.int16)
            marks[rows, :] = jnp.broadcast_to(most * (1.0 / 32767.0), (lot, 128))

        scales_to[...] = marks[: scales_to.shape[1], :].T[:8, :]

    def add(coded_from, scales_from):
        if not near:
            load(coded_from, got)
            load(scales_from, got_scale)
            coded_from, scales_from = got, got_scale
        marks[:count, :] = jnp.broadcast_to(scales_from[0:1, :], (128, count)).T

        @pl.loop(0, count // 32, unroll=2)
        def _(turn):
            rows = pl.ds(pl.multiple_of(turn * 32, 32), 32)
            held[rows, :] += coded_from[rows, :].astype(jnp.float32) * marks[rows, 0:1]

    def place_of(step):
        return other_place(step, z, lines) if step < lines - 1 else z

    def wide_copies(step, hop):
        at = (hop - 1) * lines + step
        peer = z * columns + (x + hop) % columns
        target = place_of(step)
        return (
            remote(coded.at[step], wide_in.at[hop - 1, target], wide_send.at[0, at], wide_recv.at[0, at], shard=peer),
            remote(scales.at[step], wide_scale.at[hop - 1, target], wide_send.at[1, at], wide_recv.at[1, at], shard=peer),
        )

    def send_wide(hop, steps):
        for step in steps:
            if hop > 1:
                for copy in wide_copies(step, hop - 1):
                    copy.wait_send()
            load(partial.at[place_of(step) * columns + (x + hop) % columns], held)
            code(coded.at[step], scales.at[step])
            for copy in wide_copies(step, hop):
                copy.start()

    def row_copies(step):
        peer = (y + step) % rows_y * 2 + core
        return (
            remote(send_rows.at[step - 1], row_in.at[step - 1], row_send.at[0, step - 1], row_recv.at[0, step - 1], group=peer),
            remote(send_scales.at[step - 1], row_scale_in.at[step - 1], row_send.at[1, step - 1], row_recv.at[1, step - 1], group=peer),
        )

    def core_sum(turn):
        load(piece_of(turn * 2 + core), total)
        load(core_in.at[turn], other)

        @pl.loop(0, piece // chunk)
        def _(turn):
            rows = pl.ds(pl.multiple_of(turn * chunk, chunk), chunk)
            total[rows, :] += other[rows, :]

    if columns > 1:
        send_wide(1, range(0, 1))
    if direct:
        for turn in range(rows_y):
            core_copy(turn).wait_recv()
        for step in range(1, rows_y):
            core_sum((y + step) % rows_y)
            code(send_rows.at[step - 1], send_scales.at[step - 1], total, chunk)
            for copy in row_copies(step):
                copy.start()
        core_sum(y)
    if columns > 1:
        send_wide(1, range(1, lines))
    for hop in range(2, columns):
        send_wide(hop, range(lines))

    load(small, small_sum)
    for step in range(1, groups):
        small_copy(step).wait_recv()
        load(small_in.at[step - 1], small_got)
        small_sum[...] += small_got[...]

    def small_deal(step):
        return remote(small_sum, small_out.at[shard], small_send.at[groups + step], small_recv.at[groups + step], shard=(shard + step) % shards)

    for step in range(1, shards):
        small_deal(step).start()
    load(small_sum, small_out.at[shard])

    def line_copies(step):
        target = place_of(step)
        way = jnp.where(target > z, 0, 1)
        peer = jnp.where(target > z, z + 1, z - 1) * columns + x
        return (
            remote(line_coded.at[step], line_in.at[way, target], line_send.at[0, step], line_recv.at[0, way, target], shard=peer),
            remote(line_scales.at[step], line_scale.at[way, target], line_send.at[1, step], line_recv.at[1, way, target], shard=peer),
        )

    def take(way, target):
        source = jnp.where(way == 0, z - 1, z + 1)
        peer = jnp.clip(source, 0, lines - 1) * columns + x
        remote(line_coded.at[0], line_in.at[way, target], line_send.at[0, 0], line_recv.at[0, way, target], shard=peer).wait_recv()
        remote(line_scales.at[0], line_scale.at[way, target], line_send.at[1, 0], line_recv.at[1, way, target], shard=peer).wait_recv()
        add(line_in.at[way, target], line_scale.at[way, target])

    def gather_wide(step):
        target = place_of(step)
        load(partial.at[target * columns + x], held)
        for hop in range(1, columns):
            for copy in wide_copies(step, hop):
                copy.wait_recv()
            add(wide_in.at[hop - 1, target], wide_scale.at[hop - 1, target])

    def deal_copy(turn, step):
        first = group * piece + turn * chunk
        column = jnp.where(
            first < inner,
            inner * shard + first,
            jnp.where(first < 2 * inner, INNER + inner * shard + first - inner, 2 * INNER + shared * shard + first - 2 * inner),
        )
        owner = jnp.minimum(column // owned, groups - 1)
        peer = (shard + step) % shards
        source = deal_rows.at[
            pl.ds(pl.multiple_of(turn * chunk, chunk), chunk), pl.ds(pl.multiple_of(peer * depth, depth), depth)
        ]
        target = weight_out.at[pl.ds(pl.multiple_of(column - owner * owned, chunk), chunk)]
        real = first < 2 * inner + shared
        here = real & (owner == group) if step == 0 else None
        away = real & (owner != group) if step == 0 else real

        def near_copy():
            return pltpu.make_async_copy(source, target, deal_recv)

        def far():
            return remote(source, target, deal_send.at[turn, step], deal_recv, shard=peer, group=owner)

        return here, near_copy, away, far

    def deal():
        for step in range(1, rows_y):
            for copy in row_copies(step):
                copy.wait_recv()
            load(row_in.at[step - 1], row_got)
            load(row_scale_in.at[step - 1], row_scale_got)
            marks[: row_scale_got.shape[1], :] = jnp.broadcast_to(row_scale_got[0:1, :], (128, row_scale_got.shape[1])).T

            @pl.loop(0, piece // chunk)
            def _(turn):
                rows = pl.ds(pl.multiple_of(turn * chunk, chunk), chunk)
                total[rows, :] += row_got[rows, :].astype(jnp.float32) * marks[rows, 0:1]

        code(deal_rows, deal_scales, total, chunk)
        load(deal_scales, mark_out.at[shard, group])
        for step in range(1, groups):
            mark_copy(step).start()

    def deal_some(part, parts):
        chunks = piece // chunk

        @pl.loop(part * chunks // parts, (part + 1) * chunks // parts)
        def _(turn):
            for step in range(shards):
                here, near_copy, away, far = deal_copy(turn, step)
                if here is not None:
                    pl.when(here)(lambda: near_copy().start())
                pl.when(away)(lambda: far().start())

    def mark_copy(step):
        to = (group + step) % groups
        return remote(deal_scales, mark_out.at[shard, group], mark_send.at[step], mark_recv.at[step], group=to)

    def mark_spread(step):
        to, at = (shard + step) % shards, groups + step
        return remote(mark_out.at[shard], mark_out.at[shard], mark_send.at[at], mark_recv.at[at], shard=to)

    def mark_pass():
        for step in range(1, groups):
            mark_copy(step).wait_recv()
        for step in range(1, shards):
            mark_spread(step).start()

    def deal_end():
        for step in range(1, groups):
            mark_copy(step).wait_send()
        for step in range(1, shards):
            mark_spread(step).wait()

        @pl.when(group == groups - 1)
        def _():
            most = weight_out.at[pl.ds(0, owned - HEADS)]
            pltpu.make_async_copy(most, most, deal_recv).wait()

        @pl.when(group < groups - 1)
        def _():
            pltpu.make_async_copy(weight_out, weight_out, deal_recv).wait()

        @pl.loop(0, piece // chunk)
        def _(turn):
            for step in range(shards):
                _, _, away, far = deal_copy(turn, step)
                pl.when(away)(lambda: far().wait_send())

    for step in range(lines - 1):
        if direct and step == min(1, lines - 2):
            deal()
        target = place_of(step)
        way = jnp.where(target > z, 0, 1)
        gather_wide(step)

        @pl.when(jnp.where(target > z, z > 0, z < lines - 1))
        def _():
            take(way, target)

        code(line_coded.at[step], line_scales.at[step])
        for copy in line_copies(step):
            copy.start()
        if direct and step >= min(1, lines - 2):
            deal_some(step - min(1, lines - 2), lines - 1 - min(1, lines - 2))
    if direct:
        mark_pass()
    gather_wide(lines - 1)

    @pl.when(z > 0)
    def _():
        take(0, z)

    @pl.when(z < lines - 1)
    def _():
        take(1, z)

    rows_out[...] = held[...]
    gain_sum[...] = jnp.zeros_like(gain_sum)

    @pl.loop(0, count // 8)
    def _(turn):
        rows = pl.ds(pl.multiple_of(turn * 8, 8), 8)
        gain_sum[...] += held[rows, :] * scaled_rows[rows, :]

    def gain_copy(step):
        return remote(gain_part, gain_in.at[step - 1], gain_send.at[step - 1], gain_recv.at[step - 1], shard=(shard + step) % shards)

    def gain_deal(step):
        at = shards - 1 + step - 1
        return remote(gain_out, gain_in.at[at], gain_send.at[at], gain_recv.at[at], group=(group + step) % groups)

    lanes = gain_out.shape[1]
    products = jnp.sum(gain_sum[...], axis=0, keepdims=True)
    gain_part[...] = jnp.concatenate([products[:, row * lanes : (row + 1) * lanes] for row in range(8)], axis=0)
    for step in range(1, shards):
        gain_copy(step).start()
    gain_out[...] = gain_part[...]
    for step in range(1, shards):
        gain_copy(step).wait_recv()
        gain_out[...] += gain_in[step - 1]
    for step in range(1, groups):
        gain_deal(step).start()
    for step in range(1, groups):
        gain_deal(step).wait_recv()
    for step in range(1, groups):
        gain_deal(step).wait_send()
    for step in range(1, groups):
        gain_out[...] += gain_in[shards - 1 + step - 1]

    for step in range(1, shards):
        gain_copy(step).wait_send()
        small_deal(step).wait()
    for step in range(1, groups):
        small_copy(step).wait_send()
    if direct:
        deal_end()
        for step in range(1, rows_y):
            for copy in row_copies(step):
                copy.wait_send()
        for turn in range(rows_y):
            core_copy(turn).wait_send()
    for step in range(lines):
        for copy in wide_copies(step, columns - 1) if columns > 1 else ():
            copy.wait_send()
    for step in range(lines - 1):
        for copy in line_copies(step):
            copy.wait_send()


def tail_exchange(shards, groups, partial, weight_part, small, scaled_rows, owned, depth, direct):
    columns = grid_columns(shards)
    lines, rows_y = shards // columns, groups // 2
    count, width = scaled_rows.shape
    piece = piece_rows(shards, groups) if direct else CHUNK
    padded = -(-piece // 128) * 128
    small_shape = small.shape
    coded, scale = (count, width), (8, count)
    any_space, vmem = pl.BlockSpec(memory_space=pl.ANY), pl.BlockSpec(memory_space=pltpu.VMEM)
    f32, i16 = jnp.float32, jnp.int16
    slots = max(columns - 1, 1)
    dma = pltpu.SemaphoreType.DMA
    landing = [
        ((slots, lines) + coded, i16),
        ((slots, lines) + scale, f32),
        ((2, lines) + coded, i16),
        ((2, lines) + scale, f32),
    ]
    near = shards * count * width <= 1 << 22
    out = pl.pallas_call(
        functools.partial(tail_kernel, shards, groups, columns, near, direct),
        in_specs=[any_space, any_space, any_space, vmem],
        out_specs=[vmem, any_space, any_space, any_space, vmem] + [any_space] * 4 + [vmem] + ([] if near else [any_space] * 4),
        out_shape=[
            jax.ShapeDtypeStruct((count, width), f32),
            jax.ShapeDtypeStruct((owned, depth), i16),
            jax.ShapeDtypeStruct((shards, groups, 8, padded), f32),
            jax.ShapeDtypeStruct((shards,) + small_shape, f32),
            jax.ShapeDtypeStruct((8, width // 8), f32),
            jax.ShapeDtypeStruct((rows_y, piece, width), f32),
            jax.ShapeDtypeStruct((max(rows_y - 1, 1), piece, width), i16),
            jax.ShapeDtypeStruct((max(rows_y - 1, 1), 8, padded), f32),
            jax.ShapeDtypeStruct((max(groups - 1, 1),) + small_shape, f32),
            jax.ShapeDtypeStruct((shards - 1 + groups - 1, 8, width // 8), f32),
        ]
        + ([] if near else [jax.ShapeDtypeStruct(*each) for each in landing]),
        scratch_shapes=([pltpu.VMEM(*each) for each in landing] if near else [])
        + [
            pltpu.VMEM((count, width), f32),
            pltpu.VMEM((lines,) + coded, i16),
            pltpu.VMEM((lines,) + scale, f32),
            pltpu.VMEM((lines,) + coded, i16),
            pltpu.VMEM((lines,) + scale, f32),
            pltpu.VMEM((16, 128) if near else coded, i16),
            pltpu.VMEM((8, 128) if near else scale, f32),
            pltpu.VMEM((max(count, padded), 128), f32),
            pltpu.VMEM((piece, width), f32),
            pltpu.VMEM((piece, width), f32),
            pltpu.VMEM((max(rows_y - 1, 1), piece, width), i16),
            pltpu.VMEM((max(rows_y - 1, 1), 8, padded), f32),
            pltpu.VMEM((piece, width), i16),
            pltpu.VMEM((8, padded), f32),
            pltpu.VMEM((piece, width), i16),
            pltpu.VMEM((8, padded), f32),
            pltpu.VMEM(small_shape, f32),
            pltpu.VMEM(small_shape, f32),
            pltpu.VMEM((8, width), f32),
            pltpu.VMEM((8, width // 8), f32),
            dma,
            dma((2, slots * lines)),
            dma((2, slots * lines)),
            dma((2, lines)),
            dma((2, 2, lines)),
            dma((rows_y,)),
            dma((rows_y,)),
            dma((2, max(rows_y - 1, 1))),
            dma((2, max(rows_y - 1, 1))),
            dma((piece // CHUNK, shards)),
            dma,
            dma((shards + groups,)),
            dma((shards + groups,)),
            dma((groups + shards,)),
            dma((groups + shards,)),
            dma((shards + groups,)),
            dma((shards + groups,)),
        ],
        compiler_params=pltpu.CompilerParams(
            collective_id=1, has_side_effects=True, vmem_limit_bytes=60 * 1024 * 1024
        ),
        cost_estimate=pl.CostEstimate(flops=0, bytes_accessed=400_000_000, transcendentals=0),
        name="tail_exchange",
    )(partial, weight_part, small, scaled_rows)
    return out[:5]


def finish_kernel(
    shards, groups, columns,
    slots, d_cols, d_rest, normed, weight, weight_rest, no_rows, out_part, small, scaled_rows,
    rows_out, weight_out, mark_out, small_out, dt_out, gain_out, home, out_full, weight_part,
    core_in, row_in, row_scale_in, small_in, dt_in, gain_in,
    wide_in, wide_scale, line_in, line_scale,
    held, coded, scales, line_coded, line_scales, marks, total, other, send_rows, send_scales, row_got, row_scale_got,
    deal_rows, deal_scales, small_sum, small_got, dt_sum, dt_got, gain_sum, gain_part,
    moved, moved_rest, turned, weight_all, lot, tile, made,
    load_sem, fetch_sem, lot_sem, tile_sem, made_sem, out_sem, out_send, out_recv, out_pass_send, home_sem, home_send, home_recv,
    wide_send, wide_recv, line_send, line_recv, core_send, core_recv, row_send, row_recv,
    deal_send, deal_recv, mark_send, mark_recv, small_send, small_recv, dt_send, dt_recv, gain_send, gain_recv,
):
    shard, group = lax.axis_index("shard"), lax.axis_index("group")
    lines = shards // columns
    rows_y = groups // 2
    z, x = shard // columns, shard % columns
    y, core = group // 2, group % 2
    count = held.shape[0]
    parts = count // scales.shape[2]
    span = count // parts
    owned, depth = weight_out.shape
    piece, chunk = total.shape[0], CHUNK
    inner, shared = INNER // shards, SHARED // shards

    def load(src, dst):
        copy = pltpu.make_async_copy(src, dst, load_sem)
        copy.start()
        copy.wait()

    blocks, main, width = slots.shape[0], d_cols.shape[1], held.shape[1]
    per = BLOCK // shards
    fetch_weight = pltpu.make_async_copy(weight.at[pl.ds(0, main)], weight_all, fetch_sem)
    fetch_weight.start()

    def fetch_lot(turn):
        rows = pl.ds(turn * BLOCK, BLOCK)
        return pltpu.make_async_copy(d_cols.at[rows], lot.at[turn % 2], lot_sem.at[turn % 2])

    tile_width = tile.shape[2]

    def fetch_tile(turn):
        lanes = pl.ds(turn * tile_width, tile_width)
        return pltpu.make_async_copy(normed.at[:, lanes], tile.at[turn % 2], tile_sem.at[turn % 2])

    fetch_lot(0).start()
    fetch_tile(0).start()
    barrier_with(
        [
            {"shard": (shard + step % shards) % shards, "group": (group + step // shards) % groups}
            for step in range(1, shards * groups)
        ]
    )

    def push_home(step):
        peer = (shard + step) % shards
        rows = no_rows.at[pl.ds(0, home.shape[1]), peer]
        return remote(rows, home.at[shard], home_send.at[step], home_recv.at[step], shard=peer)

    for step in range(1, shards):
        push_home(step).start()
    home_here = pltpu.make_async_copy(no_rows.at[pl.ds(0, home.shape[1]), shard], home.at[shard], home_sem)
    home_here.start()

    mate = y * 2 + 1 - core

    def core_copy(turn):
        return remote(piece_of(turn * 2 + 1 - core), core_in.at[turn], core_send.at[turn], core_recv.at[turn], group=mate)

    def piece_of(owner):
        return weight_part.at[pl.ds(pl.multiple_of(owner * piece, piece), piece)]

    out_lots, out_width = out_sem.shape[0], out_part.shape[1]
    out_rows = out_part.shape[0] // out_lots

    def out_place(part, turn):
        return out_full.at[pl.ds(turn * out_rows, out_rows), pl.ds(pl.multiple_of(part * out_width, out_width), out_width)]

    def out_here(turn):
        return pltpu.make_async_copy(out_part.at[pl.ds(turn * out_rows, out_rows)], out_place(group, turn), out_sem.at[turn])

    def out_copy(step, turn):
        peer = mate if step == 0 else (y + step) % rows_y * 2 + core
        rows = out_part.at[pl.ds(turn * out_rows, out_rows)]
        return remote(rows, out_place(group, turn), out_send.at[step, turn], out_recv.at[group, turn], group=peer)

    def out_pass(step, turn):
        part = (y + step) % rows_y * 2 + core
        return remote(
            out_place(part, turn), out_place(part, turn), out_pass_send.at[step, turn], out_recv.at[part, turn], group=mate
        )

    def out_from(part, turn):
        rows = out_part.at[pl.ds(turn * out_rows, out_rows)]
        return remote(rows, out_place(part, turn), out_send.at[0, turn], out_recv.at[part, turn], group=mate)

    def out_start(turns):
        for turn in turns:
            for step in range(1, rows_y):
                out_copy(step, turn).start()
            out_copy(0, turn).start()

    def out_forward(turns):
        for turn in turns:
            for step in range(1, rows_y):
                out_from((y + step) % rows_y * 2 + core, turn).wait_recv()
                out_pass(step, turn).start()

    def out_end():
        for turn in range(out_lots):
            for step in range(rows_y):
                out_copy(step, turn).wait_send()
                out_from(step * 2 + 1 - core, turn).wait_recv()
            for step in range(1, rows_y):
                out_pass(step, turn).wait_send()
            out_here(turn).wait()

    half = out_lots // 2
    out_start(range(half))
    for turn in range(out_lots):
        out_here(turn).start()

    for turn in range(blocks):
        fetch_lot(turn).wait()
        if turn + 1 < blocks:
            fetch_lot(turn + 1).start()
        rows = pl.ds(turn * BLOCK, BLOCK)
        place = place_of_rows(slots[turn])
        cols, rest = lot[turn % 2], d_rest[rows, :]
        moved[:, turn] = dots(place, cols, ((0,), (0,))).astype(jnp.bfloat16).reshape(shards, per, main)
        moved_rest[:, turn] = dots(place, rest, ((0,), (0,))).astype(jnp.bfloat16).reshape(shards, per, rest.shape[1])
        turned[:main, rows] = cols.T
        turned[main:, rows] = rest.T
    fetch_weight.wait()

    def fetch(owner):
        cols, rest = moved[owner].reshape(count, main), moved_rest[owner].reshape(count, d_rest.shape[1])
        step = min(512, width)
        for lane in range(0, width, step):
            lanes = pl.ds(lane, step)
            found = dots(cols, weight_all[:, lanes], ((1,), (0,)))
            held[:, lanes] = found + dots(rest, weight_rest[:, lanes], ((1,), (0,)))

    def small_copy(step):
        return remote(small, small_in.at[step - 1], small_send.at[step - 1], small_recv.at[step - 1], group=(group + step) % groups)

    for step in range(1, groups):
        small_copy(step).start()

    def piece_of_rows(half):
        return held.at[pl.ds(half * span, span)]

    def code(coded_to, scales_to, values, lot=32):
        @pl.loop(0, values.shape[0] // lot, unroll=2)
        def _(turn):
            rows = pl.ds(pl.multiple_of(turn * lot, lot), lot)
            value = values[rows, :]
            most = jnp.maximum(jnp.max(jnp.abs(value), axis=1, keepdims=True), 1e-30)
            coded_to[rows, :] = jnp.round(value * (32767.0 / most)).astype(jnp.int32).astype(jnp.int16)
            marks[rows, :] = jnp.broadcast_to(most * (1.0 / 32767.0), (lot, 128))

        scales_to[...] = marks[: scales_to.shape[1], :].T[:8, :]

    def add(sums, coded_from, scales_from):
        marks[:span, :] = jnp.broadcast_to(scales_from[0:1, :], (128, span)).T

        @pl.loop(0, span // 32, unroll=2)
        def _(turn):
            rows = pl.ds(pl.multiple_of(turn * 32, 32), 32)
            sums[rows, :] += coded_from[rows, :].astype(jnp.float32) * marks[rows, 0:1]

    def place_of(step):
        return other_place(step, z, lines) if step < lines - 1 else z

    def wide_copies(step, half, hop):
        own = step * parts + half
        at = (hop - 1) * lines * parts + own
        peer = z * columns + (x + hop) % columns
        spot = place_of(step) * parts + half
        return (
            remote(coded.at[own], wide_in.at[hop - 1, spot], wide_send.at[0, at], wide_recv.at[0, at], shard=peer),
            remote(scales.at[own], wide_scale.at[hop - 1, spot], wide_send.at[1, at], wide_recv.at[1, at], shard=peer),
        )

    def send_wide(hop, steps):
        for step in steps:
            fetch(place_of(step) * columns + (x + hop) % columns)
            for half in range(parts):
                if hop > 1:
                    for copy in wide_copies(step, half, hop - 1):
                        copy.wait_send()
                code(coded.at[step * parts + half], scales.at[step * parts + half], piece_of_rows(half))
                for copy in wide_copies(step, half, hop):
                    copy.start()

    def row_copies(step):
        peer = (y + step) % rows_y * 2 + core
        return (
            remote(send_rows.at[step - 1], row_in.at[step - 1], row_send.at[0, step - 1], row_recv.at[0, step - 1], group=peer),
            remote(send_scales.at[step - 1], row_scale_in.at[step - 1], row_send.at[1, step - 1], row_recv.at[1, step - 1], group=peer),
        )

    def core_sum(turn):
        load(piece_of(turn * 2 + core), total)
        load(core_in.at[turn], other)

        @pl.loop(0, piece // chunk)
        def _(turn):
            rows = pl.ds(pl.multiple_of(turn * chunk, chunk), chunk)
            total[rows, :] += other[rows, :]

    early = min(2, lines)
    if columns > 1:
        send_wide(1, range(early))

    def store_made(turn):
        lanes = pl.ds(turn * tile_width, tile_width)
        return pltpu.make_async_copy(made.at[turn % 2], weight_part.at[:, lanes], made_sem.at[turn % 2])

    tiles = width // tile_width
    for turn in range(tiles):
        fetch_tile(turn).wait()
        if turn + 1 < tiles:
            fetch_tile(turn + 1).start()
        if turn >= 2:
            store_made(turn - 2).wait()
        made[turn % 2] = dots(turned[...], tile[turn % 2], ((1,), (0,)))
        store_made(turn).start()
    for turn in range(max(0, tiles - 2), tiles):
        store_made(turn).wait()
    for turn in range(rows_y):
        core_copy(turn).start()

    dt_own = weight_part.at[pl.ds(main + shared, HEADS // shards)]

    def dt_copy(step):
        return remote(dt_own, dt_in.at[step - 1], dt_send.at[step], dt_recv.at[step], group=(group + step) % groups)

    def dt_deal(step):
        at = groups + step
        return remote(dt_sum, dt_out.at[shard], dt_send.at[at], dt_recv.at[at], shard=(shard + step) % shards)

    for step in range(1, groups):
        dt_copy(step).start()
    if columns > 1:
        send_wide(1, range(early, lines))
    for hop in range(2, columns):
        send_wide(hop, range(lines))
    for turn in range(rows_y):
        core_copy(turn).wait_recv()
    for step in range(1, rows_y):
        core_sum((y + step) % rows_y)
        code(send_rows.at[step - 1], send_scales.at[step - 1], total, chunk)
        for copy in row_copies(step):
            copy.start()
    out_start(range(half, out_lots))
    core_sum(y)

    load(small, small_sum)
    for step in range(1, groups):
        small_copy(step).wait_recv()
        load(small_in.at[step - 1], small_got)
        small_sum[...] += small_got[...]

    def small_deal(step):
        return remote(small_sum, small_out.at[shard], small_send.at[groups + step], small_recv.at[groups + step], shard=(shard + step) % shards)

    load(dt_own, dt_sum)
    for step in range(1, groups):
        dt_copy(step).wait_recv()
        load(dt_in.at[step - 1], dt_got)
        dt_sum[...] += dt_got[...]
    for step in range(1, shards):
        small_deal(step).start()
        dt_deal(step).start()
    load(small_sum, small_out.at[shard])
    load(dt_sum, dt_out.at[shard])

    def line_copies(step, half):
        target = place_of(step)
        own = step * parts + half
        peer = jnp.where(target > z, z + 1, z - 1) * columns + x
        spot = jnp.where(target == z - 1, lines, target) * parts + half
        return (
            remote(line_coded.at[own], line_in.at[spot], line_send.at[0, own], line_recv.at[0, spot], shard=peer),
            remote(line_scales.at[own], line_scale.at[spot], line_send.at[1, own], line_recv.at[1, spot], shard=peer),
        )

    def take(way, target, half):
        source = jnp.where(way == 0, z - 1, z + 1)
        peer = jnp.clip(source, 0, lines - 1) * columns + x
        spot = jnp.where((way == 1) & (target == z), lines, target) * parts + half
        remote(line_coded.at[0], line_in.at[spot], line_send.at[0, 0], line_recv.at[0, spot], shard=peer).wait_recv()
        remote(line_scales.at[0], line_scale.at[spot], line_send.at[1, 0], line_recv.at[1, spot], shard=peer).wait_recv()
        add(piece_of_rows(half), line_in.at[spot], line_scale.at[spot])

    def gather_wide(step, half):
        spot = place_of(step) * parts + half
        for hop in range(1, columns):
            for copy in wide_copies(step, half, hop):
                copy.wait_recv()
            add(piece_of_rows(half), wide_in.at[hop - 1, spot], wide_scale.at[hop - 1, spot])

    def deal_copy(turn, step):
        first = group * piece + turn * chunk
        column = jnp.where(
            first < inner,
            inner * shard + first,
            jnp.where(first < 2 * inner, INNER + inner * shard + first - inner, 2 * INNER + shared * shard + first - 2 * inner),
        )
        owner = jnp.minimum(column // owned, groups - 1)
        peer = (shard + step) % shards
        source = deal_rows.at[
            pl.ds(pl.multiple_of(turn * chunk, chunk), chunk), pl.ds(pl.multiple_of(peer * depth, depth), depth)
        ]
        target = weight_out.at[pl.ds(pl.multiple_of(column - owner * owned, chunk), chunk)]
        real = first < 2 * inner + shared
        here = real & (owner == group) if step == 0 else None
        away = real & (owner != group) if step == 0 else real

        def near_copy():
            return pltpu.make_async_copy(source, target, deal_recv)

        def far():
            return remote(source, target, deal_send.at[turn, step], deal_recv, shard=peer, group=owner)

        return here, near_copy, away, far

    def deal():
        for step in range(1, rows_y):
            for copy in row_copies(step):
                copy.wait_recv()
            load(row_in.at[step - 1], row_got)
            load(row_scale_in.at[step - 1], row_scale_got)
            marks[: row_scale_got.shape[1], :] = jnp.broadcast_to(row_scale_got[0:1, :], (128, row_scale_got.shape[1])).T

            @pl.loop(0, piece // chunk)
            def _(turn):
                rows = pl.ds(pl.multiple_of(turn * chunk, chunk), chunk)
                total[rows, :] += row_got[rows, :].astype(jnp.float32) * marks[rows, 0:1]

        code(deal_rows, deal_scales, total, chunk)
        load(deal_scales, mark_out.at[shard, group])
        for step in range(1, groups):
            mark_copy(step).start()

    def deal_some(part, parts):
        chunks = piece // chunk

        @pl.loop(part * chunks // parts, (part + 1) * chunks // parts)
        def _(turn):
            for step in range(shards):
                here, near_copy, away, far = deal_copy(turn, step)
                if here is not None:
                    pl.when(here)(lambda: near_copy().start())
                pl.when(away)(lambda: far().start())

    def mark_copy(step):
        to = (group + step) % groups
        return remote(deal_scales, mark_out.at[shard, group], mark_send.at[step], mark_recv.at[step], group=to)

    def mark_spread(step):
        to, at = (shard + step) % shards, groups + step
        return remote(mark_out.at[shard], mark_out.at[shard], mark_send.at[at], mark_recv.at[at], shard=to)

    def mark_pass():
        for step in range(1, groups):
            mark_copy(step).wait_recv()
        for step in range(1, shards):
            mark_spread(step).start()

    def deal_end():
        for step in range(1, groups):
            mark_copy(step).wait_send()
        for step in range(1, shards):
            mark_spread(step).wait()

        @pl.when(group == groups - 1)
        def _():
            most = weight_out.at[pl.ds(0, owned - HEADS)]
            pltpu.make_async_copy(most, most, deal_recv).wait()

        @pl.when(group < groups - 1)
        def _():
            pltpu.make_async_copy(weight_out, weight_out, deal_recv).wait()

        @pl.loop(0, piece // chunk)
        def _(turn):
            for step in range(shards):
                _, _, away, far = deal_copy(turn, step)
                pl.when(away)(lambda: far().wait_send())

    for step in range(lines - 1):
        if step == min(1, lines - 2):
            deal()
            out_forward(range(half))
        target = place_of(step)
        way = jnp.where(target > z, 0, 1)
        fetch(target * columns + x)
        for half in range(parts):
            gather_wide(step, half)

            @pl.when(jnp.where(target > z, z > 0, z < lines - 1))
            def _():
                take(way, target, half)

            code(line_coded.at[step * parts + half], line_scales.at[step * parts + half], piece_of_rows(half))
            for copy in line_copies(step, half):
                copy.start()
        if step >= min(1, lines - 2):
            deal_some(step - min(1, lines - 2), lines - 1 - min(1, lines - 2))
    mark_pass()
    fetch(z * columns + x)
    for half in range(parts):
        gather_wide(lines - 1, half)

        @pl.when(z > 0)
        def _():
            take(0, z, half)

        @pl.when(z < lines - 1)
        def _():
            take(1, z, half)

    rows_out[...] = held[...]
    gain_sum[...] = jnp.zeros_like(gain_sum)

    @pl.loop(0, count // 8)
    def _(turn):
        rows = pl.ds(pl.multiple_of(turn * 8, 8), 8)
        gain_sum[...] += held[rows, :] * scaled_rows[rows, :]

    def gain_copy(step):
        return remote(gain_part, gain_in.at[step - 1], gain_send.at[step - 1], gain_recv.at[step - 1], shard=(shard + step) % shards)

    def gain_deal(step):
        at = shards - 1 + step - 1
        return remote(gain_out, gain_in.at[at], gain_send.at[at], gain_recv.at[at], group=(group + step) % groups)

    lanes = gain_out.shape[1]
    products = jnp.sum(gain_sum[...], axis=0, keepdims=True)
    gain_part[...] = jnp.concatenate([products[:, row * lanes : (row + 1) * lanes] for row in range(8)], axis=0)
    for step in range(1, shards):
        gain_copy(step).start()
    gain_out[...] = gain_part[...]
    out_forward(range(half, out_lots))
    for step in range(1, shards):
        gain_copy(step).wait_recv()
        gain_out[...] += gain_in[step - 1]
    for step in range(1, groups):
        gain_deal(step).start()
    for step in range(1, groups):
        gain_deal(step).wait_recv()
    for step in range(1, groups):
        gain_deal(step).wait_send()
    for step in range(1, groups):
        gain_out[...] += gain_in[shards - 1 + step - 1]

    for step in range(1, shards):
        gain_copy(step).wait_send()
        small_deal(step).wait()
        dt_deal(step).wait()
        push_home(step).wait()
    home_here.wait()
    for step in range(1, groups):
        small_copy(step).wait_send()
        dt_copy(step).wait_send()
    deal_end()
    out_end()
    for step in range(1, rows_y):
        for copy in row_copies(step):
            copy.wait_send()
    for turn in range(rows_y):
        core_copy(turn).wait_send()
    for half in range(parts):
        for step in range(lines):
            for copy in wide_copies(step, half, columns - 1) if columns > 1 else ():
                copy.wait_send()
        for step in range(lines - 1):
            for copy in line_copies(step, half):
                copy.wait_send()


def finish_exchange(
    shards, groups, slots, d_cols, d_rest, normed, weight, weight_rest, no_rows, out_part, small, scaled_rows, owned, depth
):
    columns = grid_columns(shards)
    lines, rows_y = shards // columns, groups // 2
    count, width = scaled_rows.shape
    blocks, main, rest = slots.shape[0], d_cols.shape[1], d_rest.shape[1]
    total, per, heads = blocks * BLOCK, BLOCK // shards, HEADS // shards
    piece = piece_rows(shards, groups)
    padded = -(-piece // 128) * 128
    small_shape = small.shape
    parts = 2
    coded, scale = (count // parts, width), (8, count // parts)
    any_space, vmem = pl.BlockSpec(memory_space=pl.ANY), pl.BlockSpec(memory_space=pltpu.VMEM)
    f32, i16, bf16 = jnp.float32, jnp.int16, jnp.bfloat16
    hops, turns, others = max(columns - 1, 1), max(rows_y - 1, 1), max(groups - 1, 1)
    lots, tile = 4, 256
    dma = pltpu.SemaphoreType.DMA
    out = pl.pallas_call(
        functools.partial(finish_kernel, shards, groups, columns),
        in_specs=[vmem, any_space, vmem, any_space, any_space, vmem, any_space, any_space, any_space, vmem],
        out_specs=[vmem] + [any_space] * 4 + [vmem] + [any_space] * 8 + [vmem],
        out_shape=[
            jax.ShapeDtypeStruct((count, width), f32),
            jax.ShapeDtypeStruct((owned, depth), i16),
            jax.ShapeDtypeStruct((shards, groups, 8, padded), f32),
            jax.ShapeDtypeStruct((shards,) + small_shape, f32),
            jax.ShapeDtypeStruct((shards, heads, width), f32),
            jax.ShapeDtypeStruct((8, width // 8), f32),
            jax.ShapeDtypeStruct((shards, blocks // 2) + no_rows.shape[2:], bf16),
            jax.ShapeDtypeStruct((out_part.shape[0], out_part.shape[1] * groups), bf16),
            jax.ShapeDtypeStruct((main + rest, width), f32),
            jax.ShapeDtypeStruct((rows_y, piece, width), f32),
            jax.ShapeDtypeStruct((turns, piece, width), i16),
            jax.ShapeDtypeStruct((turns, 8, padded), f32),
            jax.ShapeDtypeStruct((others,) + small_shape, f32),
            jax.ShapeDtypeStruct((others, heads, width), f32),
            jax.ShapeDtypeStruct((shards - 1 + groups - 1, 8, width // 8), f32),
        ],
        scratch_shapes=[
            pltpu.VMEM((hops, lines * parts) + coded, i16),
            pltpu.VMEM((hops, lines * parts) + scale, f32),
            pltpu.VMEM(((lines + 1) * parts,) + coded, i16),
            pltpu.VMEM(((lines + 1) * parts,) + scale, f32),
            pltpu.VMEM((count, width), f32),
            pltpu.VMEM((lines * parts,) + coded, i16),
            pltpu.VMEM((lines * parts,) + scale, f32),
            pltpu.VMEM(((lines - 1) * parts,) + coded, i16),
            pltpu.VMEM(((lines - 1) * parts,) + scale, f32),
            pltpu.VMEM((max(count, padded), 128), f32),
            pltpu.VMEM((piece, width), f32),
            pltpu.VMEM((piece, width), f32),
            pltpu.VMEM((turns, piece, width), i16),
            pltpu.VMEM((turns, 8, padded), f32),
            pltpu.VMEM((piece, width), i16),
            pltpu.VMEM((8, padded), f32),
            pltpu.VMEM((piece, width), i16),
            pltpu.VMEM((8, padded), f32),
            pltpu.VMEM(small_shape, f32),
            pltpu.VMEM(small_shape, f32),
            pltpu.VMEM((heads, width), f32),
            pltpu.VMEM((heads, width), f32),
            pltpu.VMEM((8, width), f32),
            pltpu.VMEM((8, width // 8), f32),
            pltpu.VMEM((shards, blocks, per, main), bf16),
            pltpu.VMEM((shards, blocks, per, rest), bf16),
            pltpu.VMEM((main + rest, total), bf16),
            pltpu.VMEM((main, width), bf16),
            pltpu.VMEM((2, BLOCK, main), bf16),
            pltpu.VMEM((2, total, tile), bf16),
            pltpu.VMEM((2, main + rest, tile), f32),
            dma,
            dma,
            dma((2,)),
            dma((2,)),
            dma((2,)),
            dma((lots,)),
            dma((rows_y, lots)),
            dma((groups, lots)),
            dma((rows_y, lots)),
            dma,
            dma((shards,)),
            dma((shards,)),
            dma((2, hops * lines * parts)),
            dma((2, hops * lines * parts)),
            dma((2, lines * parts)),
            dma((2, (lines + 1) * parts)),
            dma((rows_y,)),
            dma((rows_y,)),
            dma((2, turns)),
            dma((2, turns)),
            dma((piece // CHUNK, shards)),
            dma,
            dma((shards + groups,)),
            dma((shards + groups,)),
            dma((groups + shards,)),
            dma((groups + shards,)),
            dma((groups + shards,)),
            dma((groups + shards,)),
            dma((shards + groups,)),
            dma((shards + groups,)),
        ],
        compiler_params=pltpu.CompilerParams(
            collective_id=7, has_side_effects=True, vmem_limit_bytes=62 * 1024 * 1024
        ),
        cost_estimate=pl.CostEstimate(flops=0, bytes_accessed=450_000_000, transcendentals=0),
        name="finish_exchange",
    )(slots, d_cols, d_rest, normed, weight, weight_rest, no_rows, out_part, small, scaled_rows)
    return out[:8]


def nesterov(weight, gradient, moment, average, step_rate):
    decayed = gradient + weight_decay * weight
    new_moment = momentum_decay * moment + decayed
    new_weight = weight - step_rate * (decayed + momentum_decay * new_moment)
    new_average = average_decay * average + (1.0 - average_decay) * new_weight
    return (new_moment, new_weight, new_average)


def dot32(a, b, contract=((1,), (0,))):
    return lax.dot_general(a, b, (contract, ((), ())), preferred_element_type=jnp.float32)


def own_slice(value, index, width, axis):
    return lax.dynamic_slice_in_dim(value, index * width, width, axis)


def local(
    tokens,
    cotangent,
    lengths,
    deal_slot,
    in_weight,
    out_weight,
    small_params,
    in_moment,
    out_moment,
    small_moment,
    in_average,
    out_average,
    small_average,
):
    shards, groups = lax.axis_size("shard"), lax.axis_size("group")
    shard, group = lax.axis_index("shard"), lax.axis_index("group")
    rows, width = tokens.shape
    per = rows // shards
    total = rows * shards
    blocks = total // BLOCK
    heads = HEADS // shards
    inner = INNER // shards
    shared = SHARED // shards
    conv_flat, conv_bias, dt_bias, rate_log, skip_gain, norm_gain, pre_gain = unpack(small_params)
    taps = conv_flat.reshape(CONV, XBC)

    cols, depth, sends = in_weight.shape[1], in_weight.shape[0], out_weight.shape[1]
    direct = cols % CHUNK == 0 and depth % 128 == 0 and sends % 128 == 0 and per % CHUNK == 0
    direct = direct and (2 * inner + SHARED + HEADS) % (groups * CHUNK) == 0 and shared % CHUNK == 0
    bounds = jnp.cumsum(lengths[0])[:-1].astype(jnp.int32)
    seg_rows = segment_of(jnp.arange(total, dtype=jnp.int32), lengths[0])

    rank = jnp.sum((deal_slot[None, :] < deal_slot[:, None]).astype(jnp.int32), axis=1)
    sort_mat = (rank[None, :] == jnp.arange(rows)[:, None]).astype(jnp.bfloat16)
    r_in = lax.rsqrt(jnp.mean(tokens * tokens, axis=1, keepdims=True) + eps_norm)
    in_turned = in_weight.T

    if direct:
        x_all, in_low, out_low, slot_all, c_sorted, out_cast = front_exchange(
            shards, groups, tokens, pre_gain, cotangent, in_turned, out_weight, deal_slot
        )
        x_all = x_all.reshape(blocks, BLOCK, width)
        slot_all = slot_all[:, 0, :]
    else:
        sorted_slot = jnp.sum(jnp.where(sort_mat > 0, deal_slot[None, :], 0), axis=1)
        normed_low = (tokens * r_in * pre_gain[None, :]).astype(jnp.bfloat16)
        x_sorted = dot32(sort_mat, normed_low).astype(jnp.bfloat16).reshape(blocks, per, width)
        c_sorted = dot32(sort_mat, cotangent.astype(jnp.bfloat16)).astype(jnp.bfloat16)
        c_sorted = c_sorted.reshape(blocks, per, width)
        in_turned = in_turned.astype(jnp.bfloat16)
        out_cast = out_weight.astype(jnp.bfloat16)
        x_all = lax.all_gather(x_sorted, "shard").transpose(1, 0, 2, 3).reshape(blocks, BLOCK, width)
        slot_all = lax.all_gather(sorted_slot, "shard")
        part = depth // groups
        pieces = lax.all_to_all(in_turned.reshape(cols, groups, part), "group", 1, 0)
        pieces = pieces.reshape(groups * cols, part)

        def cut(lo, each):
            return pieces[lo : lo + each * shards].reshape(shards, each, part)

        spread = jnp.broadcast_to(pieces[None, 2 * INNER :], (shards, SHARED + HEADS, part))
        got = jnp.concatenate([cut(0, inner), cut(INNER, inner), spread], axis=1)
        got = lax.all_gather(lax.all_to_all(got, "shard", 0, 0), "group")
        in_low = got.transpose(2, 1, 0, 3).reshape(-1, width)
        out_low = lax.all_gather(out_cast, "group", axis=1, tiled=True)
    slot_blk = slot_all.reshape(shards, blocks, per).transpose(1, 0, 2).reshape(blocks, 1, BLOCK)
    slot_blk = slot_blk - jnp.arange(blocks, dtype=jnp.int32)[:, None, None] * BLOCK

    taps_v = own_slice(taps[:, :INNER], shard, inner, 1)
    taps_all = jnp.concatenate([taps_v, taps[:, INNER:]], axis=1)
    bias_all = jnp.concatenate([own_slice(conv_bias[:INNER], shard, inner, 0), conv_bias[INNER:]])[None, :]
    skip_wide = jnp.repeat(own_slice(skip_gain, shard, heads, 0), HDIM)[None, :]
    gain_own = own_slice(norm_gain, shard, inner, 0)[None, :]
    padding = max(TAIL - heads, 0)
    rate = jnp.pad(-jnp.exp(own_slice(rate_log, shard, heads, 0)), (0, padding))[:, None]
    normed, projected, pre, mixed, states, dt_cols, dt_raw, c_all = mixer_forward(
        shards, bounds, slot_blk, x_all, in_low, taps_all, bias_all, dt_bias[None, :], rate, skip_wide, c_sorted
    )
    conv_bc = projected[:, 2 * inner : 2 * inner + SHARED]
    cot_low, d_out, sums = pack_cotangent(
        shards, slot_blk, c_all.reshape(blocks, BLOCK, width), out_low, mixed, projected, gain_own
    )

    d_cols, d_bc, d_dt, grads, rate_terms, grad_out, no_rows, home_late, out_full = mixer_backward(
        shards, bounds, slot_blk, pre, mixed, projected, d_out, sums, states, dt_cols, cot_low,
        taps_v, rate, skip_wide, gain_own, out_cast[None],
    )
    out_block = out_full.reshape(INNER, -1)
    grad_out = lax.psum_scatter(grad_out, "group", scatter_dimension=1, tiled=True)

    d_dtraw = d_dt[:heads].T * jax.nn.sigmoid(dt_raw[:, :heads])
    grad_dtb = jnp.sum(d_dtraw, axis=0)
    grad_rate = jnp.sum(rate_terms[:heads], axis=1)
    grad_skip = jnp.sum(grads[6].reshape(heads, HDIM), axis=1)
    _, pull_bc = jax.vjp(
        lambda c, t, b: convolve(c, seg_rows, t, b),
        own_slice(conv_bc, shard, shared, 1),
        own_slice(taps[:, INNER:], shard, shared, 1),
        own_slice(conv_bias[INNER:], shard, shared, 0),
    )
    d_conv_bc, grad_taps_bc, grad_bias_bc = pull_bc(d_bc.T)
    rest = 128 - shared - heads
    d_rest = jnp.concatenate([d_conv_bc, d_dtraw, jnp.zeros((total, rest), jnp.float32)], axis=1)
    in_rest = jnp.concatenate(
        [
            own_slice(in_low[2 * inner : 2 * inner + SHARED], shard, shared, 0),
            own_slice(in_low[2 * inner + SHARED :], shard, heads, 0),
            jnp.zeros((rest, width), jnp.bfloat16),
        ]
    )

    mine = [
        grads[:CONV].reshape(-1),
        grad_taps_bc.reshape(-1),
        grads[4],
        grad_bias_bc,
        grad_dtb,
        grad_rate,
        grad_skip,
        grads[5],
    ]
    extents = [piece.shape[0] for piece in mine]
    mine = jnp.concatenate(mine)
    mine = jnp.pad(mine, (0, -mine.shape[0] % 1024)).reshape(-1, 128)
    x_scaled = jnp.dot(sort_mat.astype(jnp.float32), tokens * r_in, precision=lax.Precision.HIGHEST)
    d_rest = d_rest.astype(jnp.bfloat16)
    if direct:
        d_normed, grad_in, grad_marks, small_all, dt_part, gain_all, home, out_full = finish_exchange(
            shards, groups, slot_blk, d_cols, d_rest, normed, in_low, in_rest, no_rows, out_block, mine, x_scaled,
            cols, depth,
        )
    else:
        partial, weight_part, home = project_back(
            slot_blk, d_cols, d_rest, normed, in_low, in_rest, no_rows, shards
        )
        out_full = lax.all_gather(out_block, "group", axis=1, tiled=True)
        d_normed, _, _, small_all, gain_all = tail_exchange(
            shards, groups, partial.reshape(shards, rows, width), weight_part, mine, x_scaled, cols, depth, False
        )

    home = jnp.concatenate([home, home_late], axis=1)
    home = home.reshape(shards, rows, inner).transpose(1, 0, 2).reshape(rows, INNER)
    home = dot32(sort_mat, home, ((0,), (0,))).astype(jnp.bfloat16)
    block_out = tokens + dot32(home, out_full)
    d_normed = jnp.dot(sort_mat.T.astype(jnp.float32), d_normed, precision=lax.Precision.HIGHEST)
    d_scaled = pre_gain[None, :] * d_normed
    inside = jnp.mean(tokens * d_scaled, axis=1, keepdims=True)
    input_grad = cotangent + r_in * (d_scaled - tokens * (r_in * r_in) * inside)
    grad_pre = gain_all.reshape(width)

    mine = small_all.reshape(shards, -1)
    found, offset = [], 0
    for extent in extents:
        found.append(mine[:, offset : offset + extent])
        offset = offset + extent
    if direct:
        dt_part = own_slice(dt_part.reshape(HEADS, width), shard, depth, 1)
        steps = grad_marks[:, :, 0, : piece_rows(shards, groups)].reshape(shards, -1)
        steps = jnp.concatenate(
            [
                steps[:, :inner].reshape(-1),
                steps[:, inner : 2 * inner].reshape(-1),
                steps[:, 2 * inner : 2 * inner + shared].reshape(-1),
                jnp.zeros((HEADS,), jnp.float32),
            ]
        )
        grad_in = grad_in.astype(jnp.float32) * own_slice(steps, group, cols, 0)[:, None]
        last = jnp.concatenate([grad_in[: cols - HEADS], dt_part])
        grad_in = jnp.where(group == groups - 1, last, grad_in)
    else:
        used = 2 * inner + shared + heads
        grad_in = weight_part[:used].reshape(used, shards, groups, part).transpose(2, 1, 0, 3)
        grad_in = lax.psum_scatter(grad_in, "group", scatter_dimension=0)
        grad_in = lax.all_to_all(grad_in, "shard", 0, 0)

        def join(lo, each):
            return grad_in[:, lo : lo + each].reshape(shards * each, part)

        grad_in = jnp.concatenate(
            [
                join(0, inner),
                join(inner, inner),
                join(2 * inner, shared),
                join(2 * inner + shared, heads),
            ]
        )
        grad_in = lax.all_to_all(grad_in.reshape(groups, cols, part), "group", 0, 0)
        grad_in = grad_in.transpose(1, 0, 2).reshape(cols, depth)

    def taps_of(piece):
        return piece.reshape(shards, CONV, -1).transpose(1, 0, 2).reshape(CONV, -1)

    grad_taps = jnp.concatenate([taps_of(found[0]), taps_of(found[1])], axis=1).reshape(-1)
    grad_small = jnp.concatenate([grad_taps] + [piece.reshape(-1) for piece in found[2:]] + [grad_pre])
    in_new = nesterov(in_weight.T, grad_in, in_moment.T, in_average.T, rate_in)
    in_new = tuple(value.T for value in in_new)
    out_new = nesterov(out_weight, grad_out, out_moment, out_average, rate_out)
    small_new = nesterov(small_params, grad_small, small_moment, small_average, rate_small)
    return (block_out, input_grad) + in_new + out_new + small_new


def solution(mesh):
    rows = P(("group", "shard"), None)
    tile = P("shard", "group")
    return jax.shard_map(
        local,
        mesh=mesh,
        in_specs=(
            rows,
            rows,
            P("group", None),
            P(("group", "shard")),
            tile,
            tile,
            P(),
            tile,
            tile,
            P(),
            tile,
            tile,
            P(),
        ),
        out_specs=(rows, rows, tile, tile, tile, tile, tile, tile, P(), P(), P()),
        check_vma=False,
    )
```

```python
import functools

import jax
import jax.numpy as jnp
from jax import lax
from jax.experimental import pallas as pl
from jax.experimental.pallas import tpu as pltpu
from jax.sharding import PartitionSpec as P

D = 2048
HEADS = 64
HDIM = 64
STATE = 128
CONV = 4
BLOCK = 256
INNER = 4096
XBC = 4352
SHARED = 2 * STATE
TAIL = 8
CHUNK = 16
MESH = pl.DeviceIdType.MESH


eps_norm = 1e-05
momentum_decay = 0.9
weight_decay = 0.01
average_decay = 0.99
rate_in = 0.0001
rate_out = 3e-05
rate_small = 0.001


def unpack(packed_small):
    extents = [CONV * XBC, XBC, HEADS, HEADS, HEADS, INNER, D]
    pieces = []
    offset = 0
    for extent in extents:
        pieces.append(packed_small[offset : offset + extent])
        offset = offset + extent
    return pieces


def segment_of(positions, lengths_row):
    bounds = jnp.cumsum(lengths_row)[:-1]
    inside = jnp.sum((positions[:, None] >= bounds[None, :]).astype(jnp.int32), axis=1)
    return jnp.where(positions < 0, -1, inside)


def convolve(conv_rows, seg_rows, conv_taps, conv_bias):
    row_count, width = conv_rows.shape
    extended = jnp.concatenate([jnp.zeros((CONV - 1, width), conv_rows.dtype), conv_rows], axis=0)
    seg_ext = jnp.concatenate([jnp.full((CONV - 1,), -1, jnp.int32), seg_rows], axis=0)
    conv_sum = jnp.zeros_like(conv_rows) + conv_bias[None, :]
    for tap_index in range(CONV):
        same_seq = (seg_ext[tap_index : tap_index + row_count] == seg_rows)[:, None]
        conv_sum = conv_sum + jnp.where(
            same_seq,
            extended[tap_index : tap_index + row_count] * conv_taps[tap_index][None, :],
            0.0,
        )
    return jax.nn.silu(conv_sum)


def split(value):
    high = value.astype(jnp.bfloat16)
    return high, (value - high.astype(jnp.float32)).astype(jnp.bfloat16)


def dots(a, b, contract):
    return lax.dot_general(a, b, (contract, ((), ())), preferred_element_type=jnp.float32)


def dot3(a, b, contract=((1,), (0,))):
    a = a if isinstance(a, tuple) else split(a)
    b = b if isinstance(b, tuple) else split(b)
    return dots(a[0], b[0], contract) + (dots(a[0], b[1], contract) + dots(a[1], b[0], contract))


NT = ((1,), (1,))


def dot_wide(a, wide):
    high, low = split(a)
    lanes = wide.shape[1] // 2
    plain = ((1,), (0,))
    first = dots(high, wide, plain)
    return first[:, :lanes] + (first[:, lanes:] + dots(low, wide[:, :lanes], plain))


def beside(first, second, own):
    moved = pltpu.roll(second.astype(jnp.float32), HDIM, 1).astype(jnp.bfloat16)
    return jnp.where(own, first, moved)


def head_sums(value, marks):
    high = value.astype(jnp.bfloat16)
    rest = value - high.astype(jnp.float32)
    mid = rest.astype(jnp.bfloat16)
    low = (rest - mid.astype(jnp.float32)).astype(jnp.bfloat16)
    return dots(marks, high, NT) + (dots(marks, mid, NT) + dots(marks, low, NT))


def widen(columns, heads):
    rows = columns.shape[0]
    low_half = lax.broadcasted_iota(jnp.int32, (rows, 2 * HDIM), 1) < HDIM
    return jnp.concatenate(
        [
            jnp.where(low_half, columns[:, h : h + 1], columns[:, h + 1 : h + 2])
            for h in range(0, heads, 2)
        ],
        axis=1,
    )


def running_sum(value, reverse=False):
    lane = lax.broadcasted_iota(jnp.int32, value.shape, 1)
    count = value.shape[1]
    step = 1
    while step < count:
        if reverse:
            value = value + jnp.where(lane < count - step, pltpu.roll(value, count - step, 1), 0.0)
        else:
            value = value + jnp.where(lane >= step, pltpu.roll(value, step, 1), 0.0)
        step *= 2
    return value


def sequence_of(positions, bounds):
    inside = jnp.where(positions >= bounds[0], 1, 0) + jnp.where(positions >= bounds[1], 1, 0)
    return jnp.where(positions < 0, -1, inside)


def block_facts(block, bounds, dt_t, rate):
    start = block * BLOCK
    seg_col = sequence_of(start + lax.broadcasted_iota(jnp.int32, (BLOCK, 1), 0), bounds)
    seg_row = sequence_of(start + lax.broadcasted_iota(jnp.int32, (1, BLOCK), 1), bounds)
    before = sequence_of(start - 1 + lax.broadcasted_iota(jnp.int32, (1, 1), 1), bounds)
    last = sequence_of(start + BLOCK - 1 + lax.broadcasted_iota(jnp.int32, (1, 1), 1), bounds)
    run_t = running_sum(dt_t * rate)
    run = run_t.T
    final = run[BLOCK - 1 :, :]
    carried = jnp.where(seg_col == before, jnp.exp(run), 0.0)
    tail = jnp.where(seg_col == last, jnp.exp(final - run), 0.0)
    keep = jnp.where(last == before, jnp.exp(final), 0.0)
    return seg_col, seg_row, run_t, run, carried, tail, keep


def barrier_with(peers):
    barrier = pltpu.get_barrier_semaphore()
    for peer in peers:
        pl.semaphore_signal(barrier, inc=1, device_id=peer, device_id_type=MESH)
    pl.semaphore_wait(barrier, len(peers))


def remote(src, dst, sends, recvs, **where):
    return pltpu.make_async_remote_copy(
        src_ref=src, dst_ref=dst, send_sem=sends, recv_sem=recvs, device_id=where, device_id_type=MESH
    )


def place_of_rows(slots):
    count = slots.shape[1]
    return (lax.broadcasted_iota(jnp.int32, (BLOCK, count), 0) == slots).astype(jnp.bfloat16)


def grid_columns(shards):
    columns = 1
    while 2 * (2 * columns) * (2 * columns) <= shards:
        columns *= 2
    return columns if shards % columns == 0 else 1


def whole(shape):
    return pl.BlockSpec(shape, lambda *_: (0,) * len(shape))


def row_gather(shards, columns, own, gathered, local_sem, sends, recvs):
    shard = lax.axis_index("shard")
    lines = shards // columns
    z, x = shard // columns, shard % columns

    def line_copy(source, way, first=False):
        at = source * columns + x
        peer = jnp.clip(z + 1 - 2 * way, 0, lines - 1) * columns + x
        rows = own if first else gathered.at[:, at]
        return remote(rows, gathered.at[:, at], sends.at[way, source], recvs.at[at], shard=peer)

    def wide_copy(source, hop, first=False):
        at = source * columns + x
        peer = z * columns + (x + hop) % columns
        rows = own if first else gathered.at[:, at]
        return remote(rows, gathered.at[:, at], sends.at[1 + hop, source], recvs.at[at], shard=peer)

    def pass_on(source, ways, first=False):
        for way in ways:
            @pl.when(z < lines - 1 if way == 0 else z > 0)
            def _():
                line_copy(source, way, first).start()

        for hop in range(1, columns):
            wide_copy(source, hop, first).start()

    here = pltpu.make_async_copy(own, gathered.at[:, shard], local_sem)

    def begin():
        pass_on(z, (0, 1), True)
        here.start()

    def hop(step):
        @pl.when(z - step >= 0)
        def _():
            line_copy(z - step, 0).wait_recv()
            pass_on(z - step, (0,))

        @pl.when(z + step < lines)
        def _():
            line_copy(z + step, 1).wait_recv()
            pass_on(z + step, (1,))

    def end():
        here.wait()
        for step in range(1, columns):
            peer = z * columns + (x + step) % columns
            for source in range(lines):
                at = source * columns + (x + step) % columns
                remote(gathered.at[:, at], gathered.at[:, at], sends.at[1 + step, source], recvs.at[at], shard=peer).wait_recv()
        for source in range(lines):
            for step in range(1, columns):
                wide_copy(source, step).wait_send()

            @pl.when((z < lines - 1) & (source <= z))
            def _():
                line_copy(source, 0).wait_send()

            @pl.when((z > 0) & (source >= z))
            def _():
                line_copy(source, 1).wait_send()

    return begin, hop, end


def gather_semaphores(shards, columns):
    dma = pltpu.SemaphoreType.DMA
    return [
        dma,
        dma((1 + columns, shards // columns)),
        dma((shards,)),
    ]


def softplus(value):
    small = jnp.exp(-jnp.abs(value))
    ratio = small / (2.0 + small)
    square = ratio * ratio
    series = jnp.full_like(value, 1.0 / 15.0)
    for power in (13, 11, 9, 7, 5, 3, 1):
        series = series * square + 1.0 / power
    return jnp.maximum(value, 0.0) + 2.0 * ratio * series


def pick_columns(value, marks):
    high = value.astype(jnp.bfloat16)
    rest = value - high.astype(jnp.float32)
    mid = rest.astype(jnp.bfloat16)
    low = (rest - mid.astype(jnp.float32)).astype(jnp.bfloat16)
    plain = ((1,), (0,))
    return dots(high, marks, plain) + (dots(mid, marks, plain) + dots(low, marks, plain))


def forward_kernel(
    heads, shards, columns, bounds, slots, rows_in, weight, taps, bias, dt_bias, rate, skip, cot_own,
    packed, product, pre_out, mixed_out, state_out, dt_out, raw_out, cot_all,
    ext, state, *gather_sems,
):
    block = pl.program_id(0)
    blocks = cot_own.shape[0]
    inner = heads * HDIM
    shard = lax.axis_index("shard")
    begin, hop, end = row_gather(shards, columns, cot_own, cot_all, *gather_sems)
    hops = range(1, shards // columns)

    @pl.when(block == 0)
    def _():
        barrier_with([{"shard": (shard + step) % shards} for step in range(1, shards)])
        begin()
        ext[:TAIL, :] = jnp.zeros((TAIL, ext.shape[1]), jnp.float32)
        state[...] = jnp.zeros_like(state)

    for step in hops:
        if (7 * step + 1) // 2 < blocks:
            pl.when(block == (7 * step + 1) // 2)(functools.partial(hop, step))

    normed = dots(place_of_rows(slots[0]), rows_in[0], ((1,), (0,))).astype(jnp.bfloat16)
    packed[...] = normed
    product[...] = dots(normed, weight[...], NT)
    head = lax.broadcasted_iota(jnp.int32, (HEADS, 128), 0)
    lane = lax.broadcasted_iota(jnp.int32, (HEADS, 128), 1)
    marks = ((head == shard * heads + lane) & (lane < heads)).astype(jnp.bfloat16)
    raw = pick_columns(product[:, 2 * inner + SHARED :] + dt_bias[...], marks)
    raw_out[...] = raw
    dt = softplus(raw)
    dt_out[...] = dt

    bounds = (bounds[0], bounds[1])
    dt_t = dt.T[: rate.shape[0], :]
    seg_col, seg_row, run_t, run, carried, tail, keep = block_facts(block, bounds, dt_t, rate[...])
    ext[TAIL:, :] = product[:, inner : 2 * inner + SHARED]
    place = block * BLOCK + lax.broadcasted_iota(jnp.int32, (BLOCK, 1), 0)
    pre = bias[...] + taps[CONV - 1 : CONV, :] * ext[TAIL:, :]
    for back in range(1, CONV):
        same = sequence_of(place - back, bounds) == seg_col
        moved = ext[TAIL - back : TAIL - back + BLOCK, :]
        pre = pre + jnp.where(same, moved, 0.0) * taps[CONV - 1 - back : CONV - back, :]
    ext[:TAIL, :] = ext[BLOCK:, :]
    pre_out[...] = pre
    conv = pre / (1.0 + jnp.exp(-pre))
    values, b_rows, c_rows = conv[:, :inner], conv[:, inner : inner + STATE], conv[:, inner + STATE :]
    fed = values * widen(dt, heads)
    rows = lax.broadcasted_iota(jnp.int32, (BLOCK, BLOCK), 0)
    cols = lax.broadcasted_iota(jnp.int32, (BLOCK, BLOCK), 1)
    allowed = (seg_col == seg_row) & (rows >= cols)
    b_parts, c_parts = split(b_rows), split(c_rows)
    scores = jnp.where(allowed, dot3(c_parts, b_parts, NT), 0.0)
    old = state[...]
    state_out[0] = old
    output = widen(carried, heads) * dot3(c_parts, old)
    low_half = lax.broadcasted_iota(jnp.int32, (BLOCK, 2 * HDIM), 1) < HDIM
    inside = []
    for h in range(0, heads, 2):
        pair = jnp.concatenate(split(fed[:, h * HDIM : (h + 2) * HDIM]), axis=1)
        found = []
        for k in (h, h + 1):
            mixing = jnp.exp(jnp.minimum(run[:, k : k + 1] - run_t[k : k + 1, :], 0.0)) * scores
            found.append(dot_wide(mixing, pair))
        inside.append(jnp.where(low_half, found[0], found[1]))
    mixed = output + jnp.concatenate(inside, axis=1) + skip[...] * values
    mixed_out[...] = mixed
    state[...] = widen(keep, heads) * old + dot3(b_rows.T, widen(tail, heads) * fed)

    @pl.when(block == blocks - 1)
    def _():
        for step in hops:
            if (7 * step + 1) // 2 >= blocks:
                hop(step)
        end()


def cotangent_kernel(
    shards, slots, rows_in, weight, mixed, gate, gain,
    packed, product, sums_out, own_sums, sums_in, sums_send, sums_recv,
):
    block = pl.program_id(0)
    shard = lax.axis_index("shard")

    @pl.when(block == 0)
    def _():
        barrier_with([{"shard": (shard + step) % shards} for step in range(1, shards)])

    several = rows_in.shape[0]
    for turn in range(several):
        rows = pl.ds(turn * BLOCK, BLOCK)
        packed[rows, :] = dots(place_of_rows(slots[turn]), rows_in[turn], ((1,), (0,))).astype(jnp.bfloat16)
    d_out = dots(packed[...], weight[...], NT)
    product[...] = d_out
    gate_now = gate[...]
    gated = mixed[...] * (gate_now / (1.0 + jnp.exp(-gate_now)))
    squares = jnp.sum(gated * gated, axis=1, keepdims=True)
    products = jnp.sum(gated * gain[...] * d_out, axis=1, keepdims=True)
    lane = lax.broadcasted_iota(jnp.int32, (several * BLOCK, 128), 1)
    both = jnp.where(lane == 0, squares, jnp.where(lane == 1, products, 0.0))
    here = pl.ds(pl.multiple_of(block * several * BLOCK, BLOCK), several * BLOCK)
    own_sums[:, here] = both.T[:8, :]

    def push(step, at):
        return remote(
            own_sums.at[:, at], sums_in.at[step - 1, :, at], sums_send.at[step], sums_recv.at[step],
            shard=(shard + step) % shards,
        )

    for step in range(1, shards):
        push(step, here).start()

    @pl.when(block == pl.num_programs(0) - 1)
    def _():
        everything = pl.ds(0, own_sums.shape[1])
        for step in range(1, shards):
            push(step, everything).wait()
        found = own_sums[...]
        for step in range(1, shards):
            found = found + sums_in[step - 1]
        sums_out[...] = found * (1.0 / INNER)


def backward_kernel(
    heads, blocks, shards, columns, bounds, slots, pre, mixed, gate, d_out, conv_v, sums, state_in, dt_cols, cot,
    taps, rate, skip, gain, marks, out_own,
    d_cols, d_bc, d_dt, grads, grad_rate, grad_out, no_rows, home, out_all,
    ext, carry, bc_rows, bc_wide, bc_sum, bc_in, late_rows, wide_send, wide_recv, bc_send, bc_recv, home_send, home_recv, local_sem, *gather_sems,
):
    step = pl.program_id(0)
    block = blocks - 1 - step
    inner = heads * HDIM
    shard = lax.axis_index("shard")
    shared = SHARED // shards
    lines = shards // columns
    z, x = shard // columns, shard % columns
    begin, hop, end = row_gather(shards, columns, out_own, out_all, *gather_sems)
    hops = range(1, shards // columns)

    @pl.when(step == 0)
    def _():
        barrier_with([{"shard": (shard + turn) % shards} for turn in range(1, shards)])
        begin()
        ext[BLOCK:, :] = jnp.zeros((TAIL, ext.shape[1]), jnp.float32)
        carry[...] = jnp.zeros_like(carry)
        grads[...] = jnp.zeros_like(grads)
        grad_rate[...] = jnp.zeros_like(grad_rate)
        grad_out[...] = jnp.zeros_like(grad_out)

    for turn in hops:
        if 2 * turn < blocks:
            pl.when(step == 2 * turn)(functools.partial(hop, turn))

    bounds = (bounds[0], bounds[1])
    dt = dt_cols[...]
    dt_t = dt.T[: rate.shape[0], :]
    seg_col, seg_row, run_t, run, carried, tail, keep = block_facts(block, bounds, dt_t, rate[...])
    sums_cols = sums[...].T
    r_out = lax.rsqrt(sums_cols[:, 0:1] + 1e-05)
    inside = sums_cols[:, 1:2]
    gate_now = gate[...]
    gate_sig = 1.0 / (1.0 + jnp.exp(-gate_now))
    act = gate_now * gate_sig
    mixed_now = mixed[...]
    gated = mixed_now * act
    d_out_now = d_out[...]
    normed_out = (gated * r_out * gain[...]).astype(jnp.bfloat16)
    to_home = dots(place_of_rows(slots[0]), normed_out, ((0,), (0,)))
    per = BLOCK // shards
    if per % 16 == 0:
        no_rows[0] = to_home.astype(jnp.bfloat16).reshape(shards, per, inner)
    else:
        for turn in range(shards):
            no_rows[0, turn] = to_home[turn * per : (turn + 1) * per].astype(jnp.bfloat16)
    half = home.shape[1]

    def push_home(turn, at):
        peer = (shard + turn) % shards
        return remote(late_rows.at[at, peer], home.at[shard, at], home_send.at[turn], home_recv.at[turn], shard=peer)

    @pl.when(step < blocks - half)
    def _():
        late_rows[block - half] = no_rows[0]
        for turn in range(1, shards):
            push_home(turn, pl.ds(block - half, 1)).start()
    grad_out[...] += dots(normed_out, cot[...], ((0,), (0,)))
    d_gated = r_out * (gain[...] * d_out_now - gated * (r_out * r_out) * inside)
    dy = d_gated * act
    d_cols[:, :inner] = (d_gated * mixed_now * (gate_sig * (1.0 + gate_now * (1.0 - gate_sig)))).astype(jnp.bfloat16)
    grads[5:6, :] += jnp.sum(gated * r_out * d_out_now, axis=0, keepdims=True)
    pre_now = pre[...]
    sig = 1.0 / (1.0 + jnp.exp(-pre_now))
    conv = pre_now * sig
    values, b_rows, c_rows = conv[:, :inner], conv[:, inner : inner + STATE], conv[:, inner + STATE :]
    grads[6:7, :] += jnp.sum(dy * values, axis=0, keepdims=True)
    dt_wide = widen(dt, heads)
    fed = values * dt_wide
    old, after = state_in[0], carry[...]
    b_parts, c_parts, old_parts, after_parts = split(b_rows), split(c_rows), split(old), split(after)
    carried_wide, tail_wide, keep_wide = widen(carried, heads), widen(tail, heads), widen(keep, heads)
    rows = lax.broadcasted_iota(jnp.int32, (BLOCK, BLOCK), 0)
    cols = lax.broadcasted_iota(jnp.int32, (BLOCK, BLOCK), 1)
    allowed = (seg_col == seg_row) & (cols >= rows)
    scores_t = jnp.where(allowed, dot3(b_parts, c_parts, NT), 0.0)
    low_half = lax.broadcasted_iota(jnp.int32, (BLOCK, 2 * HDIM), 1) < HDIM
    d_scores_t = jnp.zeros((BLOCK, BLOCK), jnp.float32)
    d_fed, row_terms, col_terms = [], [], []
    for h in range(0, heads, 2):
        fed_pair = fed[:, h * HDIM : (h + 2) * HDIM]
        fed_high, fed_low = split(fed_pair)
        dy_high, dy_low = split(dy[:, h * HDIM : (h + 2) * HDIM])
        dy_wide = jnp.concatenate([dy_high, dy_low], axis=1)
        found = []
        for k in (h, h + 1):
            own = low_half if k == h else jnp.logical_not(low_half)
            left = jnp.concatenate(
                [beside(fed_high, fed_low, own), jnp.where(own, fed_high, 0.0).astype(jnp.bfloat16)], axis=1
            )
            right = jnp.concatenate([beside(dy_high, dy_high, own), dy_low], axis=1)
            d_mixing = dots(left, right, NT)
            decay = jnp.exp(jnp.minimum(run_t[k : k + 1, :] - run[:, k : k + 1], 0.0))
            mixing = decay * scores_t
            d_scores_t = d_scores_t + decay * d_mixing
            flow = mixing * d_mixing
            row_terms.append(jnp.sum(flow, axis=0, keepdims=True))
            col_terms.append(jnp.sum(flow, axis=1, keepdims=True))
            found.append(dot_wide(mixing, dy_wide))
        d_fed.append(jnp.where(low_half, found[0], found[1]))
    d_scores_t = split(jnp.where(allowed, d_scores_t, 0.0))
    fed_tail = fed * tail_wide
    dy_carried = dy * carried_wide
    d_fed_out = tail_wide * dot3(b_parts, after_parts)
    d_fed = jnp.concatenate(d_fed, axis=1) + d_fed_out
    dy_parts, tail_parts = split(dy_carried), split(fed_tail)
    here = pl.ds(pl.multiple_of(block * BLOCK, BLOCK), BLOCK)
    bc_now = jnp.concatenate(
        [
            (dot3(d_scores_t, c_parts) + dot3(tail_parts, after_parts, NT)).T,
            (dot3(d_scores_t, b_parts, ((0,), (0,))) + dot3(dy_parts, old_parts, NT)).T,
        ],
        axis=0,
    )
    bc_rows[:, :, :, here] = bc_now.reshape(lines, columns, shared, BLOCK)

    def at_step(turn):
        return pl.ds(pl.multiple_of((blocks - 1 - turn) * BLOCK, BLOCK), BLOCK)

    def push_wide(turn, hop):
        to = (x + hop) % columns
        return remote(
            bc_rows.at[:, to, :, at_step(turn)], bc_wide.at[hop - 1, :, :, at_step(turn)],
            wide_send.at[hop - 1, turn], wide_recv.at[hop - 1, turn], shard=z * columns + to,
        )

    def push_line(hop, at):
        to = (z + hop) % lines
        return remote(bc_sum.at[to, :, at], bc_in.at[hop - 1, :, at], bc_send.at[hop], bc_recv.at[hop], shard=to * columns + x)

    def add_wide(turn):
        found = bc_rows[:, x, :, at_step(turn)]
        for hop in range(1, columns):
            push_wide(turn, hop).wait_recv()
            found = found + bc_wide[hop - 1, :, :, at_step(turn)]
        bc_sum[:, :, at_step(turn)] = found
        for hop in range(1, lines):
            push_line(hop, at_step(turn)).start()

    for hop_x in range(1, columns):
        push_wide(step, hop_x).start()

    lag = min(3, blocks - 1)

    @pl.when(step >= lag)
    def _():
        add_wide(step - lag)

    head_count = dt_t.shape[0]
    pad = [jnp.zeros((1, BLOCK), jnp.float32)] * (head_count - heads)
    pad_col = [jnp.zeros((BLOCK, 1), jnp.float32)] * (head_count - heads)
    d_run = jnp.concatenate(row_terms + pad, axis=0) - jnp.concatenate(col_terms + pad_col, axis=1).T
    d_run = d_run + head_sums(dy_carried * dot3(c_parts, old_parts), marks[...])
    leaving = head_sums(fed * d_fed_out, marks[...])
    kept = jnp.sum(old * after, axis=0, keepdims=True) * keep_wide
    kept = jnp.sum(marks[...].astype(jnp.float32) * kept, axis=1, keepdims=True)
    at_end = lax.broadcasted_iota(jnp.int32, (head_count, BLOCK), 1) == BLOCK - 1
    total = jnp.sum(leaving, axis=1, keepdims=True) + kept
    d_run = d_run - leaving + jnp.where(at_end, total, 0.0)
    d_log = running_sum(d_run, reverse=True)
    d_dt[...] = d_log * rate[...] + head_sums(values * d_fed, marks[...])
    grad_rate[...] += d_log * (dt_t * rate[...])
    carry[...] = keep_wide * after + dot3(c_rows.T, dy_parts)
    pre_v, sig_v = pre_now[:, :inner], sig[:, :inner]
    d_values = dt_wide * d_fed + skip[...] * dy
    d_pre = d_values * (sig_v * (1.0 + pre_v * (1.0 - sig_v)))
    ext[:BLOCK, :] = d_pre
    place = block * BLOCK + lax.broadcasted_iota(jnp.int32, (BLOCK, 1), 0)
    conv_in = conv_v[...]
    d_conv = taps[CONV - 1 : CONV, :] * d_pre
    grads[CONV - 1 : CONV, :] += jnp.sum(conv_in * d_pre, axis=0, keepdims=True)
    grads[CONV : CONV + 1, :] += jnp.sum(d_pre, axis=0, keepdims=True)
    for ahead in range(1, CONV):
        same = sequence_of(place + ahead, bounds) == seg_col
        moved = jnp.where(same, ext[ahead : ahead + BLOCK, :], 0.0)
        d_conv = d_conv + taps[CONV - 1 - ahead : CONV - ahead, :] * moved
        grads[CONV - 1 - ahead : CONV - ahead, :] += jnp.sum(conv_in * moved, axis=0, keepdims=True)
    ext[BLOCK:, :] = ext[:TAIL, :]
    d_cols[:, inner:] = d_conv.astype(jnp.bfloat16)

    @pl.when(step == blocks - 1)
    def _():
        everything = pl.ds(0, bc_sum.shape[2])
        for turn in range(blocks - lag, blocks):
            add_wide(turn)
        for turn in hops:
            if 2 * turn >= blocks:
                hop(turn)
        end()
        here = pltpu.make_async_copy(late_rows.at[:, shard], home.at[shard], local_sem)
        here.start()
        for turn in range(1, lines):
            push_line(turn, everything).wait()
        found = bc_sum[z]
        for turn in range(1, lines):
            found = found + bc_in[turn - 1]
        d_bc[...] = found
        for turn in range(1, shards):
            push_home(turn, pl.ds(0, half)).wait()
        here.wait()
        for turn in range(blocks):
            for hop_x in range(1, columns):
                push_wide(turn, hop_x).wait_send()


def mixer_forward(shards, bounds, slots, rows_in, weight, taps, bias, dt_bias, rate, skip, cot_own):
    blocks, _, width = rows_in.shape
    columns = grid_columns(shards)
    total, inner, kept = blocks * BLOCK, INNER // shards, weight.shape[0]
    heads = inner // HDIM
    f32, bf16, any_space = jnp.float32, jnp.bfloat16, pl.BlockSpec(memory_space=pl.ANY)

    def block_of(lanes):
        return pl.BlockSpec((BLOCK, lanes), lambda i: (i, 0))

    return pl.pallas_call(
        functools.partial(forward_kernel, heads, shards, columns),
        grid=(blocks,),
        in_specs=[
            pl.BlockSpec(memory_space=pltpu.SMEM),
            pl.BlockSpec((1, 1, BLOCK), lambda i: (i, 0, 0)),
            pl.BlockSpec((1, BLOCK, width), lambda i: (i, 0, 0)),
            whole(weight.shape),
            whole(taps.shape),
            whole(bias.shape),
            whole(dt_bias.shape),
            whole(rate.shape),
            whole(skip.shape),
            any_space,
        ],
        out_specs=[
            block_of(width),
            block_of(kept),
            block_of(inner + SHARED),
            block_of(inner),
            pl.BlockSpec((1, STATE, inner), lambda i: (i, 0, 0)),
            block_of(128),
            block_of(128),
            any_space,
        ],
        out_shape=[
            jax.ShapeDtypeStruct((total, width), bf16),
            jax.ShapeDtypeStruct((total, kept), f32),
            jax.ShapeDtypeStruct((total, inner + SHARED), f32),
            jax.ShapeDtypeStruct((total, inner), f32),
            jax.ShapeDtypeStruct((blocks, STATE, inner), f32),
            jax.ShapeDtypeStruct((total, 128), f32),
            jax.ShapeDtypeStruct((total, 128), f32),
            jax.ShapeDtypeStruct((cot_own.shape[0], shards) + cot_own.shape[1:], bf16),
        ],
        scratch_shapes=[
            pltpu.VMEM((BLOCK + TAIL, inner + SHARED), f32),
            pltpu.VMEM((STATE, inner), f32),
            *gather_semaphores(shards, columns),
        ],
        compiler_params=pltpu.CompilerParams(
            collective_id=2, has_side_effects=True, vmem_limit_bytes=56 * 1024 * 1024
        ),
        cost_estimate=pl.CostEstimate(flops=0, bytes_accessed=300_000_000, transcendentals=0),
        name="mixer_forward",
    )(bounds, slots, rows_in, weight, taps, bias, dt_bias, rate, skip, cot_own)


def pack_cotangent(shards, slots, rows_in, weight, mixed, projected, gain):
    blocks, _, width = rows_in.shape
    total, inner = mixed.shape
    several = 2

    def block_of(lanes):
        return pl.BlockSpec((several * BLOCK, lanes), lambda i: (i, 0))

    return pl.pallas_call(
        functools.partial(cotangent_kernel, shards),
        grid=(blocks // several,),
        in_specs=[
            pl.BlockSpec((several, 1, BLOCK), lambda i: (i, 0, 0)),
            pl.BlockSpec((several, BLOCK, width), lambda i: (i, 0, 0)),
            whole(weight.shape),
            block_of(inner),
            block_of(inner),
            whole(gain.shape),
        ],
        out_specs=[block_of(width), block_of(inner), whole((8, total))],
        out_shape=[
            jax.ShapeDtypeStruct((total, width), jnp.bfloat16),
            jax.ShapeDtypeStruct((total, inner), jnp.float32),
            jax.ShapeDtypeStruct((8, total), jnp.float32),
        ],
        scratch_shapes=[
            pltpu.VMEM((8, total), jnp.float32),
            pltpu.VMEM((shards - 1, 8, total), jnp.float32),
            pltpu.SemaphoreType.DMA((shards,)),
            pltpu.SemaphoreType.DMA((shards,)),
        ],
        compiler_params=pltpu.CompilerParams(
            collective_id=5, has_side_effects=True, vmem_limit_bytes=48 * 1024 * 1024
        ),
        cost_estimate=pl.CostEstimate(flops=0, bytes_accessed=60_000_000, transcendentals=0),
        name="pack_cotangent",
    )(slots, rows_in, weight, mixed, projected, gain)


def mixer_backward(
    shards, bounds, slots, pre, mixed, projected, d_out, sums, states, dt_cols, cot, taps, rate, skip, gain, out_own
):
    total, inner = d_out.shape
    heads, blocks, padded = inner // HDIM, total // BLOCK, rate.shape[0]
    shared = SHARED // shards
    columns = grid_columns(shards)
    marks = (jnp.arange(padded)[:, None] == jnp.arange(inner)[None, :] // HDIM).astype(jnp.bfloat16)

    def block_of(width, column):
        return pl.BlockSpec((BLOCK, width), lambda i: (blocks - 1 - i, column))

    return pl.pallas_call(
        functools.partial(backward_kernel, heads, blocks, shards, columns),
        grid_spec=pltpu.PrefetchScalarGridSpec(
            num_scalar_prefetch=0,
            grid=(blocks,),
            in_specs=[
                pl.BlockSpec(memory_space=pltpu.SMEM),
                pl.BlockSpec((1, 1, BLOCK), lambda i: (blocks - 1 - i, 0, 0)),
                block_of(inner + SHARED, 0),
                block_of(inner, 0),
                block_of(inner, 0),
                block_of(inner, 0),
                block_of(inner, 1),
                pl.BlockSpec((8, BLOCK), lambda i: (0, blocks - 1 - i)),
                pl.BlockSpec((1, STATE, inner), lambda i: (blocks - 1 - i, 0, 0)),
                block_of(dt_cols.shape[1], 0),
                block_of(cot.shape[1], 0),
                whole(taps.shape),
                whole(rate.shape),
                whole(skip.shape),
                whole(gain.shape),
                whole(marks.shape),
                pl.BlockSpec(memory_space=pl.ANY),
            ],
            out_specs=[
                block_of(2 * inner, 0),
                whole((shared, total)),
                pl.BlockSpec((padded, BLOCK), lambda i: (0, blocks - 1 - i)),
                whole((8, inner)),
                whole((padded, BLOCK)),
                whole((inner, cot.shape[1])),
                pl.BlockSpec((1, shards, BLOCK // shards, inner), lambda i: (blocks - 1 - i, 0, 0, 0)),
                pl.BlockSpec(memory_space=pl.ANY),
                pl.BlockSpec(memory_space=pl.ANY),
            ],
            scratch_shapes=[
                pltpu.VMEM((BLOCK + TAIL, inner), jnp.float32),
                pltpu.VMEM((STATE, inner), jnp.float32),
                pltpu.VMEM((shards // columns, columns, shared, total), jnp.float32),
                pltpu.VMEM((max(columns - 1, 1), shards // columns, shared, total), jnp.float32),
                pltpu.VMEM((shards // columns, shared, total), jnp.float32),
                pltpu.VMEM((shards // columns - 1, shared, total), jnp.float32),
                pltpu.VMEM((blocks // 2, shards, BLOCK // shards, inner), jnp.bfloat16),
                pltpu.SemaphoreType.DMA((max(columns - 1, 1), blocks)),
                pltpu.SemaphoreType.DMA((max(columns - 1, 1), blocks)),
                pltpu.SemaphoreType.DMA((shards,)),
                pltpu.SemaphoreType.DMA((shards,)),
                pltpu.SemaphoreType.DMA((shards,)),
                pltpu.SemaphoreType.DMA((shards,)),
                pltpu.SemaphoreType.DMA,
                *gather_semaphores(shards, columns),
            ],
        ),
        out_shape=[
            jax.ShapeDtypeStruct((total, 2 * inner), jnp.bfloat16),
            jax.ShapeDtypeStruct((shared, total), jnp.float32),
            jax.ShapeDtypeStruct((padded, total), jnp.float32),
            jax.ShapeDtypeStruct((8, inner), jnp.float32),
            jax.ShapeDtypeStruct((padded, BLOCK), jnp.float32),
            jax.ShapeDtypeStruct((inner, cot.shape[1]), jnp.float32),
            jax.ShapeDtypeStruct((blocks, shards, BLOCK // shards, inner), jnp.bfloat16),
            jax.ShapeDtypeStruct((shards, blocks // 2, BLOCK // shards, inner), jnp.bfloat16),
            jax.ShapeDtypeStruct((out_own.shape[0], shards) + out_own.shape[1:], jnp.bfloat16),
        ],
        compiler_params=pltpu.CompilerParams(
            collective_id=3, has_side_effects=True, vmem_limit_bytes=56 * 1024 * 1024
        ),
        cost_estimate=pl.CostEstimate(flops=0, bytes_accessed=200_000_000, transcendentals=0),
        name="mixer_backward",
    )(bounds, slots, pre, mixed, projected, d_out, projected, sums, states, dt_cols, cot, taps, rate, skip, gain, marks, out_own)


def piece_rows(shards, groups):
    chunks = (2 * INNER // shards + SHARED // shards) // CHUNK
    return -(-chunks // groups) * CHUNK


def column_runs(shards, groups):
    inner, width = INNER // shards, (2 * INNER + SHARED + HEADS) // groups
    kept = 2 * inner + SHARED + HEADS
    quarter = kept // groups
    spans = []
    for shard in range(shards):
        spans.append((inner * shard, shard, 0, inner))
        spans.append((INNER + inner * shard, shard, inner, inner))
    spans.append((2 * INNER, None, 2 * inner, SHARED + HEADS))
    runs = []
    for column, shard, row, length in spans:
        while length > 0:
            step = min(length, width - column % width, quarter - row % quarter)
            runs.append((column // width, column % width, shard, row, step))
            column, row, length = column + step, row + step, length - step
    return runs


def front_kernel(
    shards, groups, columns,
    rows_in, gain, cot_in, weight_in, out_in, slot_row, slot_col,
    rows_all, weight_all, out_all, slot_all, cot_own, out_cast, scaled_rows,
    rows_own, weight_own, out_own, slot_own,
    run_send, run_recv, share_send, share_recv, out_send, out_recv, slot_send, slot_recv, local_sem, *gather_sems,
):
    shard, group = lax.axis_index("shard"), lax.axis_index("group")
    lines, rows_y = shards // columns, groups // 2
    y, core = group // 2, group % 2
    mate = y * 2 + 1 - core
    quarter = weight_all.shape[0] // groups
    depth = weight_own.shape[1]
    out_width = out_own.shape[1]
    everyone = []
    for step in range(1, shards * groups):
        other_shard = (shard + step % shards) % shards
        other_group = (group + step // shards) % groups
        everyone.append({"shard": other_shard, "group": other_group})
    barrier_with(everyone)

    count = rows_in.shape[0]
    below = (slot_col[...] < slot_row[...]).astype(jnp.int32).astype(jnp.float32)
    rank = jnp.sum(below, axis=0, keepdims=True).astype(jnp.int32)
    sort = (lax.broadcasted_iota(jnp.int32, (count, count), 0) == rank).astype(jnp.bfloat16)
    value = rows_in[...]
    scale = lax.rsqrt(jnp.sum(value * value, axis=1, keepdims=True) * (1.0 / value.shape[1]) + 1e-05)
    scaled = value * scale
    value = (scaled * gain[...]).astype(jnp.bfloat16)
    rows_own[...] = dots(sort, value, ((1,), (0,))).astype(jnp.bfloat16).reshape(rows_own.shape)
    begin, hop, end = row_gather(shards, columns, rows_own, rows_all, *gather_sems)
    begin()
    slots = slot_row[...]
    high = slots // 256
    both = jnp.where(lax.broadcasted_iota(jnp.int32, (8, count), 0) == 0, high, slots - 256 * high)
    both = dots(both.astype(jnp.float32).astype(jnp.bfloat16), sort, NT)
    slot_own[...] = jnp.broadcast_to(256.0 * both[0:1, :] + both[1:2, :], (8, count)).astype(jnp.int32)
    out_own[...] = out_in[...].astype(jnp.bfloat16)
    weight_own[...] = weight_in[...].astype(jnp.bfloat16)

    def slot_copy(step):
        return remote(slot_own, slot_all.at[shard], slot_send.at[step], slot_recv.at[step], shard=(shard + step) % shards)

    for step in range(1, shards):
        slot_copy(step).start()
    slot_here = pltpu.make_async_copy(slot_own, slot_all.at[shard], local_sem.at[0])
    slot_here.start()

    runs = column_runs(shards, groups)
    lanes = pl.ds(pl.multiple_of(shard * depth, depth), depth)
    jobs = {owner: [] for owner in range(groups)}
    for owner, column, target, row, length in runs:
        for to in range(shards) if target is None else (target,):
            jobs[owner].append((column, to, row, length))

    def run_copy(number, column, to, row, length):
        return remote(
            weight_own.at[pl.ds(column, length)], weight_all.at[pl.ds(row, length), lanes],
            run_send.at[number], run_recv, shard=to, group=row // quarter,
        )

    def each_run(act):
        for owner in range(groups):
            @pl.when(group == owner)
            def _():
                for number, (column, to, row, length) in enumerate(jobs[owner]):
                    if row // quarter == owner:
                        here = shard == to
                        act(number, column, to, row, length, here)
                    else:
                        act(number, column, to, row, length, None)

    def start_run(number, column, to, row, length, here):
        if here is None:
            run_copy(number, column, to, row, length).start()
            return

        @pl.when(here)
        def _():
            pltpu.make_async_copy(weight_own.at[pl.ds(column, length)], weight_all.at[pl.ds(row, length), lanes], run_recv).start()

        @pl.when(jnp.logical_not(here))
        def _():
            run_copy(number, column, to, row, length).start()

    def end_run(number, column, to, row, length, here):
        if here is None:
            run_copy(number, column, to, row, length).wait_send()
            return

        @pl.when(jnp.logical_not(here))
        def _():
            run_copy(number, column, to, row, length).wait_send()

    each_run(start_run)

    def own_part(ref, part):
        if ref is out_all:
            return ref.at[:, pl.ds(pl.multiple_of(part * out_width, out_width), out_width)]
        return ref.at[pl.ds(pl.multiple_of(part * quarter, quarter), quarter)]

    def share(ref, part, sends, recvs, number, peer, first=None):
        source = own_part(ref, part) if first is None else first
        return remote(source, own_part(ref, part), sends.at[number], recvs.at[part], group=peer)

    def share_start(ref, sends, recvs, first=None):
        share(ref, group, sends, recvs, 0, mate, first).start()
        for step in range(1, rows_y):
            share(ref, group, sends, recvs, step, (y + step) % rows_y * 2 + core, first).start()

    def share_pass(ref, sends, recvs):
        for step in range(1, rows_y):
            part = (y + step) % rows_y * 2 + core
            share(ref, part, sends, recvs, step, part).wait_recv()
            share(ref, part, sends, recvs, rows_y - 1 + step, mate).start()

    def share_end(ref, sends, recvs):
        for turn in range(rows_y):
            part = turn * 2 + 1 - core
            share(ref, part, sends, recvs, 0, mate).wait_recv()
        for number in range(2 * rows_y - 1):
            share(ref, group, sends, recvs, number, mate).wait_send()

    out_here = pltpu.make_async_copy(out_own, own_part(out_all, group), local_sem.at[1])
    out_here.start()
    share_start(out_all, out_send, out_recv, out_own)
    out_cast[...] = out_own[...]
    high = scaled.astype(jnp.bfloat16)
    left = scaled - high.astype(jnp.float32)
    mid = left.astype(jnp.bfloat16)
    low = (left - mid.astype(jnp.float32)).astype(jnp.bfloat16)
    plain = ((1,), (0,))
    scaled_rows[...] = dots(sort, high, plain) + (dots(sort, mid, plain) + dots(sort, low, plain))
    cot_own[...] = (
        dots(sort, cot_in[...].astype(jnp.bfloat16), ((1,), (0,))).astype(jnp.bfloat16).reshape(cot_own.shape)
    )

    for step in range(1, lines):
        hop(step)
        if step == 1:
            share_pass(out_all, out_send, out_recv)
            kept = own_part(weight_all, group)
            pltpu.make_async_copy(kept, kept, run_recv).wait()
            share_start(weight_all, share_send, share_recv)
    share_pass(weight_all, share_send, share_recv)

    end()
    out_here.wait()
    share_end(out_all, out_send, out_recv)
    share_end(weight_all, share_send, share_recv)
    each_run(end_run)
    for step in range(1, shards):
        slot_copy(step).wait()
    slot_here.wait()


def front_exchange(shards, groups, rows_in, gain, cot_in, weight_in, out_in, slots):
    columns = grid_columns(shards)
    rows_y = groups // 2
    count, width = rows_in.shape
    blocks, per = shards * count // BLOCK, BLOCK // shards
    kept = 2 * INNER // shards + SHARED + HEADS
    any_space, vmem = pl.BlockSpec(memory_space=pl.ANY), pl.BlockSpec(memory_space=pltpu.VMEM)
    dma, bf16 = pltpu.SemaphoreType.DMA, jnp.bfloat16
    counts = {}
    for owner, _, target, _, _ in column_runs(shards, groups):
        counts[owner] = counts.get(owner, 0) + (shards if target is None else 1)
    return pl.pallas_call(
        functools.partial(front_kernel, shards, groups, columns),
        in_specs=[vmem] * 7,
        out_specs=[any_space] * 4 + [vmem] * 3,
        out_shape=[
            jax.ShapeDtypeStruct((blocks, shards, per, width), bf16),
            jax.ShapeDtypeStruct((kept, width), bf16),
            jax.ShapeDtypeStruct((out_in.shape[0], out_in.shape[1] * groups), bf16),
            jax.ShapeDtypeStruct((shards, 8, count), jnp.int32),
            jax.ShapeDtypeStruct((blocks, per, width), bf16),
            jax.ShapeDtypeStruct(out_in.shape, bf16),
            jax.ShapeDtypeStruct((count, width), jnp.float32),
        ],
        scratch_shapes=[
            pltpu.VMEM((blocks, per, width), bf16),
            pltpu.VMEM(weight_in.shape, bf16),
            pltpu.VMEM(out_in.shape, bf16),
            pltpu.VMEM((8, count), jnp.int32),
            dma((max(counts.values()),)),
            dma,
            dma((2 * rows_y - 1,)),
            dma((groups,)),
            dma((2 * rows_y - 1,)),
            dma((groups,)),
            dma((shards,)),
            dma((shards,)),
            dma((2,)),
            *gather_semaphores(shards, columns),
        ],
        compiler_params=pltpu.CompilerParams(
            collective_id=4, has_side_effects=True, vmem_limit_bytes=48 * 1024 * 1024
        ),
        cost_estimate=pl.CostEstimate(flops=0, bytes_accessed=300_000_000, transcendentals=0),
        name="front_exchange",
    )(rows_in, gain[None, :], cot_in, weight_in, out_in, slots[None, :], slots[:, None])


def unpack_kernel(
    shards, slots, d_cols, d_rest, normed, weight, weight_rest, no_rows,
    partial, grad, home, moved_cols, moved_rest, local_sem, home_send, home_recv,
):
    step = pl.program_id(0)
    shard = lax.axis_index("shard")
    main = d_cols.shape[1]
    per = BLOCK // shards

    def push(turn):
        peer = (shard + turn) % shards
        return remote(no_rows.at[first, peer], home.at[shard], home_send.at[turn], home_recv.at[turn], shard=peer)

    first = pl.ds(0, home.shape[1])
    here = pltpu.make_async_copy(no_rows.at[first, shard], home.at[shard], local_sem)

    @pl.when(step == 0)
    def _():
        barrier_with([{"shard": (shard + turn) % shards} for turn in range(1, shards)])
        for turn in range(1, shards):
            push(turn).start()
        here.start()
        grad[...] = jnp.zeros_like(grad)

    several = d_cols.shape[0] // BLOCK
    for turn in range(several):
        rows = pl.ds(turn * BLOCK, BLOCK)
        place = place_of_rows(slots[turn])
        moved_cols[rows, :] = dots(place, d_cols[rows, :], ((0,), (0,))).astype(jnp.bfloat16)
        moved_rest[rows, :] = dots(place, d_rest[rows, :], ((0,), (0,))).astype(jnp.bfloat16)
    tile = 512
    for lane in range(0, weight.shape[1], tile):
        lanes = pl.ds(lane, tile)
        found = dots(moved_cols[...], weight[:, lanes], ((1,), (0,)))
        found = found + dots(moved_rest[...], weight_rest[:, lanes], ((1,), (0,)))
        for turn in range(several):
            rows = found[turn * BLOCK : (turn + 1) * BLOCK]
            partial[:, turn, :, lanes] = rows.reshape(shards, per, tile)
    grad[:main, :] += dots(d_cols[...], normed[...], ((0,), (0,)))
    grad[main:, :] += dots(d_rest[...], normed[...], ((0,), (0,)))

    @pl.when(step == pl.num_programs(0) - 1)
    def _():
        for turn in range(1, shards):
            push(turn).wait()
        here.wait()


def project_back(slots, d_cols, d_rest, normed, weight, weight_rest, no_rows, shards):
    blocks, width = slots.shape[0], normed.shape[1]
    per, main, rest = BLOCK // shards, d_cols.shape[1], d_rest.shape[1]
    several = 2
    any_space = pl.BlockSpec(memory_space=pl.ANY)

    def block_of(columns):
        return pl.BlockSpec((several * BLOCK, columns), lambda i: (i, 0))

    return pl.pallas_call(
        functools.partial(unpack_kernel, shards),
        grid=(blocks // several,),
        in_specs=[
            pl.BlockSpec((several, 1, BLOCK), lambda i: (i, 0, 0)),
            block_of(main),
            block_of(rest),
            block_of(width),
            pl.BlockSpec((main, width), lambda i: (0, 0)),
            whole(weight_rest.shape),
            any_space,
        ],
        out_specs=[
            pl.BlockSpec((shards, several, per, width), lambda i: (0, i, 0, 0)),
            whole((main + rest, width)),
            any_space,
        ],
        out_shape=[
            jax.ShapeDtypeStruct((shards, blocks, per, width), jnp.float32),
            jax.ShapeDtypeStruct((main + rest, width), jnp.float32),
            jax.ShapeDtypeStruct((shards, blocks // 2) + no_rows.shape[2:], jnp.bfloat16),
        ],
        scratch_shapes=[
            pltpu.VMEM((several * BLOCK, main), jnp.bfloat16),
            pltpu.VMEM((several * BLOCK, rest), jnp.bfloat16),
            pltpu.SemaphoreType.DMA,
            pltpu.SemaphoreType.DMA((shards,)),
            pltpu.SemaphoreType.DMA((shards,)),
        ],
        compiler_params=pltpu.CompilerParams(
            collective_id=6, has_side_effects=True, vmem_limit_bytes=60 * 1024 * 1024
        ),
        cost_estimate=pl.CostEstimate(flops=0, bytes_accessed=90_000_000, transcendentals=0),
        name="project_back",
    )(slots, d_cols, d_rest, normed, weight, weight_rest, no_rows)


def other_place(step, place, count):
    upwards = count - 1 - place
    low = jnp.where(step < upwards, count - 1 - step, step - upwards)
    high = jnp.where(step < place, step, count - 1 - (step - place))
    return jnp.where(2 * place < count, low, high)


def tail_kernel(
    shards, groups, columns, near, direct,
    partial, weight_part, small, scaled_rows,
    rows_out, weight_out, mark_out, small_out, gain_out, core_in, row_in, row_scale_in, small_in, gain_in,
    wide_in, wide_scale, line_in, line_scale,
    held, coded, scales, line_coded, line_scales, got, got_scale, marks, total, other, send_rows, send_scales, row_got, row_scale_got, deal_rows, deal_scales, small_sum, small_got,
    gain_sum, gain_part,
    load_sem, wide_send, wide_recv, line_send, line_recv, core_send, core_recv, row_send, row_recv,
    deal_send, deal_recv, mark_send, mark_recv, small_send, small_recv, gain_send, gain_recv,
):
    shard, group = lax.axis_index("shard"), lax.axis_index("group")
    lines = shards // columns
    rows_y = groups // 2
    z, x = shard // columns, shard % columns
    y, core = group // 2, group % 2
    count = held.shape[0]
    owned, depth = weight_out.shape
    piece, chunk = total.shape[0], CHUNK
    inner, shared = INNER // shards, SHARED // shards

    def load(src, dst):
        copy = pltpu.make_async_copy(src, dst, load_sem)
        copy.start()
        copy.wait()

    shard_peers = [(shard + step) % shards for step in range(1, shards)]
    group_peers = [(group + step) % groups for step in range(1, groups)]
    if direct:
        barrier_with(
            [
                {"shard": (shard + step % shards) % shards, "group": (group + step // shards) % groups}
                for step in range(1, shards * groups)
            ]
        )
    else:
        barrier_with([{"shard": peer} for peer in shard_peers] + [{"group": peer} for peer in group_peers])

    mate = y * 2 + 1 - core

    def core_copy(turn):
        return remote(piece_of(turn * 2 + 1 - core), core_in.at[turn], core_send.at[turn], core_recv.at[turn], group=mate)

    def piece_of(owner):
        return weight_part.at[pl.ds(pl.multiple_of(owner * piece, piece), piece)]

    for turn in range(rows_y if direct else 0):
        core_copy(turn).start()

    def small_copy(step):
        return remote(small, small_in.at[step - 1], small_send.at[step - 1], small_recv.at[step - 1], group=(group + step) % groups)

    for step in range(1, groups):
        small_copy(step).start()

    def code(coded_to, scales_to, values=held, lot=32):
        @pl.loop(0, values.shape[0] // lot, unroll=2)
        def _(turn):
            rows = pl.ds(pl.multiple_of(turn * lot, lot), lot)
            value = values[rows, :]
            most = jnp.maximum(jnp.max(jnp.abs(value), axis=1, keepdims=True), 1e-30)
            coded_to[rows, :] = jnp.round(value * (32767.0 / most)).astype(jnp.int32).astype(jnp.int16)
            marks[rows, :] = jnp.broadcast_to(most * (1.0 / 32767.0), (lot, 128))

        scales_to[...] = marks[: scales_to.shape[1], :].T[:8, :]

    def add(coded_from, scales_from):
        if not near:
            load(coded_from, got)
            load(scales_from, got_scale)
            coded_from, scales_from = got, got_scale
        marks[:count, :] = jnp.broadcast_to(scales_from[0:1, :], (128, count)).T

        @pl.loop(0, count // 32, unroll=2)
        def _(turn):
            rows = pl.ds(pl.multiple_of(turn * 32, 32), 32)
            held[rows, :] += coded_from[rows, :].astype(jnp.float32) * marks[rows, 0:1]

    def place_of(step):
        return other_place(step, z, lines) if step < lines - 1 else z

    def wide_copies(step, hop):
        at = (hop - 1) * lines + step
        peer = z * columns + (x + hop) % columns
        target = place_of(step)
        return (
            remote(coded.at[step], wide_in.at[hop - 1, target], wide_send.at[0, at], wide_recv.at[0, at], shard=peer),
            remote(scales.at[step], wide_scale.at[hop - 1, target], wide_send.at[1, at], wide_recv.at[1, at], shard=peer),
        )

    def send_wide(hop, steps):
        for step in steps:
            if hop > 1:
                for copy in wide_copies(step, hop - 1):
                    copy.wait_send()
            load(partial.at[place_of(step) * columns + (x + hop) % columns], held)
            code(coded.at[step], scales.at[step])
            for copy in wide_copies(step, hop):
                copy.start()

    def row_copies(step):
        peer = (y + step) % rows_y * 2 + core
        return (
            remote(send_rows.at[step - 1], row_in.at[step - 1], row_send.at[0, step - 1], row_recv.at[0, step - 1], group=peer),
            remote(send_scales.at[step - 1], row_scale_in.at[step - 1], row_send.at[1, step - 1], row_recv.at[1, step - 1], group=peer),
        )

    def core_sum(turn):
        load(piece_of(turn * 2 + core), total)
        load(core_in.at[turn], other)

        @pl.loop(0, piece // chunk)
        def _(turn):
            rows = pl.ds(pl.multiple_of(turn * chunk, chunk), chunk)
            total[rows, :] += other[rows, :]

    if columns > 1:
        send_wide(1, range(0, 1))
    if direct:
        for turn in range(rows_y):
            core_copy(turn).wait_recv()
        for step in range(1, rows_y):
            core_sum((y + step) % rows_y)
            code(send_rows.at[step - 1], send_scales.at[step - 1], total, chunk)
            for copy in row_copies(step):
                copy.start()
        core_sum(y)
    if columns > 1:
        send_wide(1, range(1, lines))
    for hop in range(2, columns):
        send_wide(hop, range(lines))

    load(small, small_sum)
    for step in range(1, groups):
        small_copy(step).wait_recv()
        load(small_in.at[step - 1], small_got)
        small_sum[...] += small_got[...]

    def small_deal(step):
        return remote(small_sum, small_out.at[shard], small_send.at[groups + step], small_recv.at[groups + step], shard=(shard + step) % shards)

    for step in range(1, shards):
        small_deal(step).start()
    load(small_sum, small_out.at[shard])

    def line_copies(step):
        target = place_of(step)
        way = jnp.where(target > z, 0, 1)
        peer = jnp.where(target > z, z + 1, z - 1) * columns + x
        return (
            remote(line_coded.at[step], line_in.at[way, target], line_send.at[0, step], line_recv.at[0, way, target], shard=peer),
            remote(line_scales.at[step], line_scale.at[way, target], line_send.at[1, step], line_recv.at[1, way, target], shard=peer),
        )

    def take(way, target):
        source = jnp.where(way == 0, z - 1, z + 1)
        peer = jnp.clip(source, 0, lines - 1) * columns + x
        remote(line_coded.at[0], line_in.at[way, target], line_send.at[0, 0], line_recv.at[0, way, target], shard=peer).wait_recv()
        remote(line_scales.at[0], line_scale.at[way, target], line_send.at[1, 0], line_recv.at[1, way, target], shard=peer).wait_recv()
        add(line_in.at[way, target], line_scale.at[way, target])

    def gather_wide(step):
        target = place_of(step)
        load(partial.at[target * columns + x], held)
        for hop in range(1, columns):
            for copy in wide_copies(step, hop):
                copy.wait_recv()
            add(wide_in.at[hop - 1, target], wide_scale.at[hop - 1, target])

    def deal_copy(turn, step):
        first = group * piece + turn * chunk
        column = jnp.where(
            first < inner,
            inner * shard + first,
            jnp.where(first < 2 * inner, INNER + inner * shard + first - inner, 2 * INNER + shared * shard + first - 2 * inner),
        )
        owner = jnp.minimum(column // owned, groups - 1)
        peer = (shard + step) % shards
        source = deal_rows.at[
            pl.ds(pl.multiple_of(turn * chunk, chunk), chunk), pl.ds(pl.multiple_of(peer * depth, depth), depth)
        ]
        target = weight_out.at[pl.ds(pl.multiple_of(column - owner * owned, chunk), chunk)]
        real = first < 2 * inner + shared
        here = real & (owner == group) if step == 0 else None
        away = real & (owner != group) if step == 0 else real

        def near_copy():
            return pltpu.make_async_copy(source, target, deal_recv)

        def far():
            return remote(source, target, deal_send.at[turn, step], deal_recv, shard=peer, group=owner)

        return here, near_copy, away, far

    def deal():
        for step in range(1, rows_y):
            for copy in row_copies(step):
                copy.wait_recv()
            load(row_in.at[step - 1], row_got)
            load(row_scale_in.at[step - 1], row_scale_got)
            marks[: row_scale_got.shape[1], :] = jnp.broadcast_to(row_scale_got[0:1, :], (128, row_scale_got.shape[1])).T

            @pl.loop(0, piece // chunk)
            def _(turn):
                rows = pl.ds(pl.multiple_of(turn * chunk, chunk), chunk)
                total[rows, :] += row_got[rows, :].astype(jnp.float32) * marks[rows, 0:1]

        code(deal_rows, deal_scales, total, chunk)
        load(deal_scales, mark_out.at[shard, group])
        for step in range(1, groups):
            mark_copy(step).start()

    def deal_some(part, parts):
        chunks = piece // chunk

        @pl.loop(part * chunks // parts, (part + 1) * chunks // parts)
        def _(turn):
            for step in range(shards):
                here, near_copy, away, far = deal_copy(turn, step)
                if here is not None:
                    pl.when(here)(lambda: near_copy().start())
                pl.when(away)(lambda: far().start())

    def mark_copy(step):
        to = (group + step) % groups
        return remote(deal_scales, mark_out.at[shard, group], mark_send.at[step], mark_recv.at[step], group=to)

    def mark_spread(step):
        to, at = (shard + step) % shards, groups + step
        return remote(mark_out.at[shard], mark_out.at[shard], mark_send.at[at], mark_recv.at[at], shard=to)

    def mark_pass():
        for step in range(1, groups):
            mark_copy(step).wait_recv()
        for step in range(1, shards):
            mark_spread(step).start()

    def deal_end():
        for step in range(1, groups):
            mark_copy(step).wait_send()
        for step in range(1, shards):
            mark_spread(step).wait()

        @pl.when(group == groups - 1)
        def _():
            most = weight_out.at[pl.ds(0, owned - HEADS)]
            pltpu.make_async_copy(most, most, deal_recv).wait()

        @pl.when(group < groups - 1)
        def _():
            pltpu.make_async_copy(weight_out, weight_out, deal_recv).wait()

        @pl.loop(0, piece // chunk)
        def _(turn):
            for step in range(shards):
                _, _, away, far = deal_copy(turn, step)
                pl.when(away)(lambda: far().wait_send())

    for step in range(lines - 1):
        if direct and step == min(1, lines - 2):
            deal()
        target = place_of(step)
        way = jnp.where(target > z, 0, 1)
        gather_wide(step)

        @pl.when(jnp.where(target > z, z > 0, z < lines - 1))
        def _():
            take(way, target)

        code(line_coded.at[step], line_scales.at[step])
        for copy in line_copies(step):
            copy.start()
        if direct and step >= min(1, lines - 2):
            deal_some(step - min(1, lines - 2), lines - 1 - min(1, lines - 2))
    if direct:
        mark_pass()
    gather_wide(lines - 1)

    @pl.when(z > 0)
    def _():
        take(0, z)

    @pl.when(z < lines - 1)
    def _():
        take(1, z)

    rows_out[...] = held[...]
    gain_sum[...] = jnp.zeros_like(gain_sum)

    @pl.loop(0, count // 8)
    def _(turn):
        rows = pl.ds(pl.multiple_of(turn * 8, 8), 8)
        gain_sum[...] += held[rows, :] * scaled_rows[rows, :]

    def gain_copy(step):
        return remote(gain_part, gain_in.at[step - 1], gain_send.at[step - 1], gain_recv.at[step - 1], shard=(shard + step) % shards)

    def gain_deal(step):
        at = shards - 1 + step - 1
        return remote(gain_out, gain_in.at[at], gain_send.at[at], gain_recv.at[at], group=(group + step) % groups)

    lanes = gain_out.shape[1]
    products = jnp.sum(gain_sum[...], axis=0, keepdims=True)
    gain_part[...] = jnp.concatenate([products[:, row * lanes : (row + 1) * lanes] for row in range(8)], axis=0)
    for step in range(1, shards):
        gain_copy(step).start()
    gain_out[...] = gain_part[...]
    for step in range(1, shards):
        gain_copy(step).wait_recv()
        gain_out[...] += gain_in[step - 1]
    for step in range(1, groups):
        gain_deal(step).start()
    for step in range(1, groups):
        gain_deal(step).wait_recv()
    for step in range(1, groups):
        gain_deal(step).wait_send()
    for step in range(1, groups):
        gain_out[...] += gain_in[shards - 1 + step - 1]

    for step in range(1, shards):
        gain_copy(step).wait_send()
        small_deal(step).wait()
    for step in range(1, groups):
        small_copy(step).wait_send()
    if direct:
        deal_end()
        for step in range(1, rows_y):
            for copy in row_copies(step):
                copy.wait_send()
        for turn in range(rows_y):
            core_copy(turn).wait_send()
    for step in range(lines):
        for copy in wide_copies(step, columns - 1) if columns > 1 else ():
            copy.wait_send()
    for step in range(lines - 1):
        for copy in line_copies(step):
            copy.wait_send()


def tail_exchange(shards, groups, partial, weight_part, small, scaled_rows, owned, depth, direct):
    columns = grid_columns(shards)
    lines, rows_y = shards // columns, groups // 2
    count, width = scaled_rows.shape
    piece = piece_rows(shards, groups) if direct else CHUNK
    padded = -(-piece // 128) * 128
    small_shape = small.shape
    coded, scale = (count, width), (8, count)
    any_space, vmem = pl.BlockSpec(memory_space=pl.ANY), pl.BlockSpec(memory_space=pltpu.VMEM)
    f32, i16 = jnp.float32, jnp.int16
    slots = max(columns - 1, 1)
    dma = pltpu.SemaphoreType.DMA
    landing = [
        ((slots, lines) + coded, i16),
        ((slots, lines) + scale, f32),
        ((2, lines) + coded, i16),
        ((2, lines) + scale, f32),
    ]
    near = shards * count * width <= 1 << 22
    out = pl.pallas_call(
        functools.partial(tail_kernel, shards, groups, columns, near, direct),
        in_specs=[any_space, any_space, any_space, vmem],
        out_specs=[vmem, any_space, any_space, any_space, vmem] + [any_space] * 4 + [vmem] + ([] if near else [any_space] * 4),
        out_shape=[
            jax.ShapeDtypeStruct((count, width), f32),
            jax.ShapeDtypeStruct((owned, depth), i16),
            jax.ShapeDtypeStruct((shards, groups, 8, padded), f32),
            jax.ShapeDtypeStruct((shards,) + small_shape, f32),
            jax.ShapeDtypeStruct((8, width // 8), f32),
            jax.ShapeDtypeStruct((rows_y, piece, width), f32),
            jax.ShapeDtypeStruct((max(rows_y - 1, 1), piece, width), i16),
            jax.ShapeDtypeStruct((max(rows_y - 1, 1), 8, padded), f32),
            jax.ShapeDtypeStruct((max(groups - 1, 1),) + small_shape, f32),
            jax.ShapeDtypeStruct((shards - 1 + groups - 1, 8, width // 8), f32),
        ]
        + ([] if near else [jax.ShapeDtypeStruct(*each) for each in landing]),
        scratch_shapes=([pltpu.VMEM(*each) for each in landing] if near else [])
        + [
            pltpu.VMEM((count, width), f32),
            pltpu.VMEM((lines,) + coded, i16),
            pltpu.VMEM((lines,) + scale, f32),
            pltpu.VMEM((lines,) + coded, i16),
            pltpu.VMEM((lines,) + scale, f32),
            pltpu.VMEM((16, 128) if near else coded, i16),
            pltpu.VMEM((8, 128) if near else scale, f32),
            pltpu.VMEM((max(count, padded), 128), f32),
            pltpu.VMEM((piece, width), f32),
            pltpu.VMEM((piece, width), f32),
            pltpu.VMEM((max(rows_y - 1, 1), piece, width), i16),
            pltpu.VMEM((max(rows_y - 1, 1), 8, padded), f32),
            pltpu.VMEM((piece, width), i16),
            pltpu.VMEM((8, padded), f32),
            pltpu.VMEM((piece, width), i16),
            pltpu.VMEM((8, padded), f32),
            pltpu.VMEM(small_shape, f32),
            pltpu.VMEM(small_shape, f32),
            pltpu.VMEM((8, width), f32),
            pltpu.VMEM((8, width // 8), f32),
            dma,
            dma((2, slots * lines)),
            dma((2, slots * lines)),
            dma((2, lines)),
            dma((2, 2, lines)),
            dma((rows_y,)),
            dma((rows_y,)),
            dma((2, max(rows_y - 1, 1))),
            dma((2, max(rows_y - 1, 1))),
            dma((piece // CHUNK, shards)),
            dma,
            dma((shards + groups,)),
            dma((shards + groups,)),
            dma((groups + shards,)),
            dma((groups + shards,)),
            dma((shards + groups,)),
            dma((shards + groups,)),
        ],
        compiler_params=pltpu.CompilerParams(
            collective_id=1, has_side_effects=True, vmem_limit_bytes=60 * 1024 * 1024
        ),
        cost_estimate=pl.CostEstimate(flops=0, bytes_accessed=400_000_000, transcendentals=0),
        name="tail_exchange",
    )(partial, weight_part, small, scaled_rows)
    return out[:5]


def finish_kernel(
    shards, groups, columns,
    slots, d_cols, d_rest, normed, weight, weight_rest, no_rows, out_part, small, scaled_rows,
    rows_out, weight_out, mark_out, small_out, dt_out, gain_out, home, out_full, weight_part,
    core_in, row_in, row_scale_in, small_in, dt_in, gain_in,
    wide_in, wide_scale, line_in, line_scale,
    held, coded, scales, line_coded, line_scales, marks, total, other, send_rows, send_scales, row_got, row_scale_got,
    deal_rows, deal_scales, small_sum, small_got, dt_sum, dt_got, gain_sum, gain_part,
    moved, moved_rest, turned, weight_all, lot, tile, made,
    load_sem, fetch_sem, lot_sem, tile_sem, made_sem, out_sem, out_send, out_recv, out_pass_send, home_sem, home_send, home_recv,
    wide_send, wide_recv, line_send, line_recv, core_send, core_recv, row_send, row_recv,
    deal_send, deal_recv, mark_send, mark_recv, small_send, small_recv, dt_send, dt_recv, gain_send, gain_recv,
):
    shard, group = lax.axis_index("shard"), lax.axis_index("group")
    lines = shards // columns
    rows_y = groups // 2
    z, x = shard // columns, shard % columns
    y, core = group // 2, group % 2
    count = held.shape[0]
    parts = count // scales.shape[2]
    span = count // parts
    owned, depth = weight_out.shape
    piece, chunk = total.shape[0], CHUNK
    inner, shared = INNER // shards, SHARED // shards

    def load(src, dst):
        copy = pltpu.make_async_copy(src, dst, load_sem)
        copy.start()
        copy.wait()

    blocks, main, width = slots.shape[0], d_cols.shape[1], held.shape[1]
    per = BLOCK // shards
    fetch_weight = pltpu.make_async_copy(weight.at[pl.ds(0, main)], weight_all, fetch_sem)
    fetch_weight.start()

    lots = lot_sem.shape[0]

    def fetch_lot(turn):
        rows = pl.ds(turn * (lot.shape[0] // lots), lot.shape[0] // lots)
        return pltpu.make_async_copy(d_cols.at[rows], lot.at[rows], lot_sem.at[turn])

    tile_width = tile.shape[2]

    def fetch_tile(turn):
        lanes = pl.ds(turn * tile_width, tile_width)
        return pltpu.make_async_copy(normed.at[:, lanes], tile.at[turn % 2], tile_sem.at[turn % 2])

    for turn in range(lots):
        fetch_lot(turn).start()
    fetch_tile(0).start()
    barrier_with(
        [
            {"shard": (shard + step % shards) % shards, "group": (group + step // shards) % groups}
            for step in range(1, shards * groups)
        ]
    )

    def push_home(step):
        peer = (shard + step) % shards
        rows = no_rows.at[pl.ds(0, home.shape[1]), peer]
        return remote(rows, home.at[shard], home_send.at[step], home_recv.at[step], shard=peer)

    for step in range(1, shards):
        push_home(step).start()
    home_here = pltpu.make_async_copy(no_rows.at[pl.ds(0, home.shape[1]), shard], home.at[shard], home_sem)
    home_here.start()

    mate = y * 2 + 1 - core

    def core_copy(turn):
        return remote(piece_of(turn * 2 + 1 - core), core_in.at[turn], core_send.at[turn], core_recv.at[turn], group=mate)

    def piece_of(owner):
        return weight_part.at[pl.ds(pl.multiple_of(owner * piece, piece), piece)]

    out_lots, out_width = out_sem.shape[0], out_part.shape[1]
    out_rows = out_part.shape[0] // out_lots

    def out_place(part, turn):
        return out_full.at[pl.ds(turn * out_rows, out_rows), pl.ds(pl.multiple_of(part * out_width, out_width), out_width)]

    def out_here(turn):
        return pltpu.make_async_copy(out_part.at[pl.ds(turn * out_rows, out_rows)], out_place(group, turn), out_sem.at[turn])

    def out_copy(step, turn):
        peer = mate if step == 0 else (y + step) % rows_y * 2 + core
        rows = out_part.at[pl.ds(turn * out_rows, out_rows)]
        return remote(rows, out_place(group, turn), out_send.at[step, turn], out_recv.at[group, turn], group=peer)

    def out_pass(step, turn):
        part = (y + step) % rows_y * 2 + core
        return remote(
            out_place(part, turn), out_place(part, turn), out_pass_send.at[step, turn], out_recv.at[part, turn], group=mate
        )

    def out_from(part, turn):
        rows = out_part.at[pl.ds(turn * out_rows, out_rows)]
        return remote(rows, out_place(part, turn), out_send.at[0, turn], out_recv.at[part, turn], group=mate)

    def out_start(turns):
        for turn in turns:
            for step in range(1, rows_y):
                out_copy(step, turn).start()
            out_copy(0, turn).start()

    def out_forward(turns):
        for turn in turns:
            for step in range(1, rows_y):
                out_from((y + step) % rows_y * 2 + core, turn).wait_recv()
                out_pass(step, turn).start()

    def out_end():
        for turn in range(out_lots):
            for step in range(rows_y):
                out_copy(step, turn).wait_send()
                out_from(step * 2 + 1 - core, turn).wait_recv()
            for step in range(1, rows_y):
                out_pass(step, turn).wait_send()
            out_here(turn).wait()

    half = out_lots // 2
    out_start(range(half))
    for turn in range(out_lots):
        out_here(turn).start()

    for turn in range(blocks):
        if turn * lots % blocks == 0:
            fetch_lot(turn * lots // blocks).wait()
        rows = pl.ds(turn * BLOCK, BLOCK)
        place = place_of_rows(slots[turn])
        cols, rest = lot[rows, :], d_rest[rows, :]
        moved[:, turn] = dots(place, cols, ((0,), (0,))).astype(jnp.bfloat16).reshape(shards, per, main)
        moved_rest[:, turn] = dots(place, rest, ((0,), (0,))).astype(jnp.bfloat16).reshape(shards, per, rest.shape[1])
        turned[:main, rows] = cols.T
        turned[main:, rows] = rest.T
    fetch_weight.wait()

    def fetch(owner):
        cols, rest = moved[owner].reshape(count, main), moved_rest[owner].reshape(count, d_rest.shape[1])
        step = min(512, width)
        for lane in range(0, width, step):
            lanes = pl.ds(lane, step)
            found = dots(cols, weight_all[:, lanes], ((1,), (0,)))
            held[:, lanes] = found + dots(rest, weight_rest[:, lanes], ((1,), (0,)))

    def small_copy(step):
        return remote(small, small_in.at[step - 1], small_send.at[step - 1], small_recv.at[step - 1], group=(group + step) % groups)

    for step in range(1, groups):
        small_copy(step).start()

    def piece_of_rows(half):
        return held.at[pl.ds(half * span, span)]

    def code(coded_to, scales_to, values, lot=32):
        @pl.loop(0, values.shape[0] // lot, unroll=2)
        def _(turn):
            rows = pl.ds(pl.multiple_of(turn * lot, lot), lot)
            value = values[rows, :]
            most = jnp.maximum(jnp.max(jnp.abs(value), axis=1, keepdims=True), 1e-30)
            coded_to[rows, :] = jnp.round(value * (32767.0 / most)).astype(jnp.int32).astype(jnp.int16)
            marks[rows, :] = jnp.broadcast_to(most * (1.0 / 32767.0), (lot, 128))

        scales_to[...] = marks[: scales_to.shape[1], :].T[:8, :]

    def add(sums, coded_from, scales_from):
        marks[:span, :] = jnp.broadcast_to(scales_from[0:1, :], (128, span)).T

        @pl.loop(0, span // 32, unroll=2)
        def _(turn):
            rows = pl.ds(pl.multiple_of(turn * 32, 32), 32)
            sums[rows, :] += coded_from[rows, :].astype(jnp.float32) * marks[rows, 0:1]

    def place_of(step):
        return other_place(step, z, lines) if step < lines - 1 else z

    def wide_copies(step, half, hop):
        own = step * parts + half
        at = (hop - 1) * lines * parts + own
        peer = z * columns + (x + hop) % columns
        spot = place_of(step) * parts + half
        return (
            remote(coded.at[own], wide_in.at[hop - 1, spot], wide_send.at[0, at], wide_recv.at[0, at], shard=peer),
            remote(scales.at[own], wide_scale.at[hop - 1, spot], wide_send.at[1, at], wide_recv.at[1, at], shard=peer),
        )

    def send_wide(hop, steps):
        for step in steps:
            fetch(place_of(step) * columns + (x + hop) % columns)
            for half in range(parts):
                if hop > 1:
                    for copy in wide_copies(step, half, hop - 1):
                        copy.wait_send()
                code(coded.at[step * parts + half], scales.at[step * parts + half], piece_of_rows(half))
                for copy in wide_copies(step, half, hop):
                    copy.start()

    def row_copies(step):
        peer = (y + step) % rows_y * 2 + core
        return (
            remote(send_rows.at[step - 1], row_in.at[step - 1], row_send.at[0, step - 1], row_recv.at[0, step - 1], group=peer),
            remote(send_scales.at[step - 1], row_scale_in.at[step - 1], row_send.at[1, step - 1], row_recv.at[1, step - 1], group=peer),
        )

    def core_sum(turn):
        load(piece_of(turn * 2 + core), total)
        load(core_in.at[turn], other)

        @pl.loop(0, piece // chunk)
        def _(turn):
            rows = pl.ds(pl.multiple_of(turn * chunk, chunk), chunk)
            total[rows, :] += other[rows, :]

    early = min(2, lines)
    if columns > 1:
        send_wide(1, range(early))

    def store_made(turn):
        lanes = pl.ds(turn * tile_width, tile_width)
        return pltpu.make_async_copy(made.at[turn % 2], weight_part.at[:, lanes], made_sem.at[turn % 2])

    tiles = width // tile_width
    for turn in range(tiles):
        fetch_tile(turn).wait()
        if turn + 1 < tiles:
            fetch_tile(turn + 1).start()
        if turn >= 2:
            store_made(turn - 2).wait()
        made[turn % 2] = dots(turned[...], tile[turn % 2], ((1,), (0,)))
        store_made(turn).start()
    for turn in range(max(0, tiles - 2), tiles):
        store_made(turn).wait()
    for turn in range(rows_y):
        core_copy(turn).start()

    dt_own = weight_part.at[pl.ds(main + shared, HEADS // shards)]

    def dt_copy(step):
        return remote(dt_own, dt_in.at[step - 1], dt_send.at[step], dt_recv.at[step], group=(group + step) % groups)

    def dt_deal(step):
        at = groups + step
        peer = (shard + step) % shards
        lanes = pl.ds(pl.multiple_of(peer * depth, depth), depth)
        return remote(dt_sum.at[:, lanes], dt_out.at[shard], dt_send.at[at], dt_recv.at[at], shard=peer)

    for step in range(1, groups):
        dt_copy(step).start()
    if columns > 1:
        send_wide(1, range(early, lines))
    for hop in range(2, columns):
        send_wide(hop, range(lines))
    for turn in range(rows_y):
        core_copy(turn).wait_recv()
    for step in range(1, rows_y):
        core_sum((y + step) % rows_y)
        code(send_rows.at[step - 1], send_scales.at[step - 1], total, chunk)
        for copy in row_copies(step):
            copy.start()
    out_start(range(half, out_lots))
    core_sum(y)

    load(small, small_sum)
    for step in range(1, groups):
        small_copy(step).wait_recv()
        load(small_in.at[step - 1], small_got)
        small_sum[...] += small_got[...]

    def small_deal(step):
        return remote(small_sum, small_out.at[shard], small_send.at[groups + step], small_recv.at[groups + step], shard=(shard + step) % shards)

    load(dt_own, dt_sum)
    for step in range(1, groups):
        dt_copy(step).wait_recv()
        load(dt_in.at[step - 1], dt_got)
        dt_sum[...] += dt_got[...]
    for step in range(1, shards):
        small_deal(step).start()
        dt_deal(step).start()
    load(small_sum, small_out.at[shard])
    load(dt_sum.at[:, pl.ds(pl.multiple_of(shard * depth, depth), depth)], dt_out.at[shard])

    def line_copies(step, half):
        target = place_of(step)
        own = step * parts + half
        peer = jnp.where(target > z, z + 1, z - 1) * columns + x
        spot = jnp.where(target == z - 1, lines, target) * parts + half
        return (
            remote(line_coded.at[own], line_in.at[spot], line_send.at[0, own], line_recv.at[0, spot], shard=peer),
            remote(line_scales.at[own], line_scale.at[spot], line_send.at[1, own], line_recv.at[1, spot], shard=peer),
        )

    def take(way, target, half):
        source = jnp.where(way == 0, z - 1, z + 1)
        peer = jnp.clip(source, 0, lines - 1) * columns + x
        spot = jnp.where((way == 1) & (target == z), lines, target) * parts + half
        remote(line_coded.at[0], line_in.at[spot], line_send.at[0, 0], line_recv.at[0, spot], shard=peer).wait_recv()
        remote(line_scales.at[0], line_scale.at[spot], line_send.at[1, 0], line_recv.at[1, spot], shard=peer).wait_recv()
        add(piece_of_rows(half), line_in.at[spot], line_scale.at[spot])

    def gather_wide(step, half):
        spot = place_of(step) * parts + half
        for hop in range(1, columns):
            for copy in wide_copies(step, half, hop):
                copy.wait_recv()
            add(piece_of_rows(half), wide_in.at[hop - 1, spot], wide_scale.at[hop - 1, spot])

    def deal_copy(turn, step):
        first = group * piece + turn * chunk
        column = jnp.where(
            first < inner,
            inner * shard + first,
            jnp.where(first < 2 * inner, INNER + inner * shard + first - inner, 2 * INNER + shared * shard + first - 2 * inner),
        )
        owner = jnp.minimum(column // owned, groups - 1)
        peer = (shard + step) % shards
        source = deal_rows.at[
            pl.ds(pl.multiple_of(turn * chunk, chunk), chunk), pl.ds(pl.multiple_of(peer * depth, depth), depth)
        ]
        target = weight_out.at[pl.ds(pl.multiple_of(column - owner * owned, chunk), chunk)]
        real = first < 2 * inner + shared
        here = real & (owner == group) if step == 0 else None
        away = real & (owner != group) if step == 0 else real

        def near_copy():
            return pltpu.make_async_copy(source, target, deal_recv)

        def far():
            return remote(source, target, deal_send.at[turn, step], deal_recv, shard=peer, group=owner)

        return here, near_copy, away, far

    def deal():
        for step in range(1, rows_y):
            for copy in row_copies(step):
                copy.wait_recv()
            load(row_in.at[step - 1], row_got)
            load(row_scale_in.at[step - 1], row_scale_got)
            marks[: row_scale_got.shape[1], :] = jnp.broadcast_to(row_scale_got[0:1, :], (128, row_scale_got.shape[1])).T

            @pl.loop(0, piece // chunk)
            def _(turn):
                rows = pl.ds(pl.multiple_of(turn * chunk, chunk), chunk)
                total[rows, :] += row_got[rows, :].astype(jnp.float32) * marks[rows, 0:1]

        code(deal_rows, deal_scales, total, chunk)
        load(deal_scales, mark_out.at[shard, group])
        for step in range(1, groups):
            mark_copy(step).start()

    def deal_some(part, parts):
        chunks = piece // chunk

        @pl.loop(part * chunks // parts, (part + 1) * chunks // parts)
        def _(turn):
            for step in range(shards):
                here, near_copy, away, far = deal_copy(turn, step)
                if here is not None:
                    pl.when(here)(lambda: near_copy().start())
                pl.when(away)(lambda: far().start())

    def mark_copy(step):
        to = (group + step) % groups
        return remote(deal_scales, mark_out.at[shard, group], mark_send.at[step], mark_recv.at[step], group=to)

    def mark_spread(step):
        to, at = (shard + step) % shards, groups + step
        return remote(mark_out.at[shard], mark_out.at[shard], mark_send.at[at], mark_recv.at[at], shard=to)

    def mark_pass():
        for step in range(1, groups):
            mark_copy(step).wait_recv()
        for step in range(1, shards):
            mark_spread(step).start()

    def deal_end():
        for step in range(1, groups):
            mark_copy(step).wait_send()
        for step in range(1, shards):
            mark_spread(step).wait()

        @pl.when(group == groups - 1)
        def _():
            most = weight_out.at[pl.ds(0, owned - HEADS)]
            pltpu.make_async_copy(most, most, deal_recv).wait()

        @pl.when(group < groups - 1)
        def _():
            pltpu.make_async_copy(weight_out, weight_out, deal_recv).wait()

        @pl.loop(0, piece // chunk)
        def _(turn):
            for step in range(shards):
                _, _, away, far = deal_copy(turn, step)
                pl.when(away)(lambda: far().wait_send())

    for step in range(lines - 1):
        if step == min(1, lines - 2):
            deal()
            out_forward(range(half))
        target = place_of(step)
        way = jnp.where(target > z, 0, 1)
        fetch(target * columns + x)
        for half in range(parts):
            gather_wide(step, half)

            @pl.when(jnp.where(target > z, z > 0, z < lines - 1))
            def _():
                take(way, target, half)

            code(line_coded.at[step * parts + half], line_scales.at[step * parts + half], piece_of_rows(half))
            for copy in line_copies(step, half):
                copy.start()
        if step >= min(1, lines - 2):
            deal_some(step - min(1, lines - 2), lines - 1 - min(1, lines - 2))
    mark_pass()
    fetch(z * columns + x)
    for half in range(parts):
        gather_wide(lines - 1, half)

        @pl.when(z > 0)
        def _():
            take(0, z, half)

        @pl.when(z < lines - 1)
        def _():
            take(1, z, half)

    rows_out[...] = held[...]
    gain_sum[...] = jnp.zeros_like(gain_sum)

    @pl.loop(0, count // 8)
    def _(turn):
        rows = pl.ds(pl.multiple_of(turn * 8, 8), 8)
        gain_sum[...] += held[rows, :] * scaled_rows[rows, :]

    def gain_copy(step):
        return remote(gain_part, gain_in.at[step - 1], gain_send.at[step - 1], gain_recv.at[step - 1], shard=(shard + step) % shards)

    def gain_deal(step):
        at = shards - 1 + step - 1
        return remote(gain_out, gain_in.at[at], gain_send.at[at], gain_recv.at[at], group=(group + step) % groups)

    lanes = gain_out.shape[1]
    products = jnp.sum(gain_sum[...], axis=0, keepdims=True)
    gain_part[...] = jnp.concatenate([products[:, row * lanes : (row + 1) * lanes] for row in range(8)], axis=0)
    for step in range(1, shards):
        gain_copy(step).start()
    gain_out[...] = gain_part[...]
    out_forward(range(half, out_lots))
    for step in range(1, shards):
        gain_copy(step).wait_recv()
        gain_out[...] += gain_in[step - 1]
    for step in range(1, groups):
        gain_deal(step).start()
    for step in range(1, groups):
        gain_deal(step).wait_recv()
    for step in range(1, groups):
        gain_deal(step).wait_send()
    for step in range(1, groups):
        gain_out[...] += gain_in[shards - 1 + step - 1]

    for step in range(1, shards):
        gain_copy(step).wait_send()
        small_deal(step).wait()
        dt_deal(step).wait()
        push_home(step).wait()
    home_here.wait()
    for step in range(1, groups):
        small_copy(step).wait_send()
        dt_copy(step).wait_send()
    deal_end()
    out_end()
    for step in range(1, rows_y):
        for copy in row_copies(step):
            copy.wait_send()
    for turn in range(rows_y):
        core_copy(turn).wait_send()
    for half in range(parts):
        for step in range(lines):
            for copy in wide_copies(step, half, columns - 1) if columns > 1 else ():
                copy.wait_send()
        for step in range(lines - 1):
            for copy in line_copies(step, half):
                copy.wait_send()


def finish_exchange(
    shards, groups, slots, d_cols, d_rest, normed, weight, weight_rest, no_rows, out_part, small, scaled_rows, owned, depth
):
    columns = grid_columns(shards)
    lines, rows_y = shards // columns, groups // 2
    count, width = scaled_rows.shape
    blocks, main, rest = slots.shape[0], d_cols.shape[1], d_rest.shape[1]
    total, per, heads = blocks * BLOCK, BLOCK // shards, HEADS // shards
    piece = piece_rows(shards, groups)
    padded = -(-piece // 128) * 128
    small_shape = small.shape
    parts = 2
    coded, scale = (count // parts, width), (8, count // parts)
    any_space, vmem = pl.BlockSpec(memory_space=pl.ANY), pl.BlockSpec(memory_space=pltpu.VMEM)
    f32, i16, bf16 = jnp.float32, jnp.int16, jnp.bfloat16
    hops, turns, others = max(columns - 1, 1), max(rows_y - 1, 1), max(groups - 1, 1)
    lots, tile = 4, 256
    dma = pltpu.SemaphoreType.DMA
    out = pl.pallas_call(
        functools.partial(finish_kernel, shards, groups, columns),
        in_specs=[vmem, any_space, vmem, any_space, any_space, vmem, any_space, any_space, any_space, vmem],
        out_specs=[vmem] + [any_space] * 4 + [vmem] + [any_space] * 8 + [vmem],
        out_shape=[
            jax.ShapeDtypeStruct((count, width), f32),
            jax.ShapeDtypeStruct((owned, depth), i16),
            jax.ShapeDtypeStruct((shards, groups, 8, padded), f32),
            jax.ShapeDtypeStruct((shards,) + small_shape, f32),
            jax.ShapeDtypeStruct((shards, heads, depth), f32),
            jax.ShapeDtypeStruct((8, width // 8), f32),
            jax.ShapeDtypeStruct((shards, blocks // 2) + no_rows.shape[2:], bf16),
            jax.ShapeDtypeStruct((out_part.shape[0], out_part.shape[1] * groups), bf16),
            jax.ShapeDtypeStruct((main + rest, width), f32),
            jax.ShapeDtypeStruct((rows_y, piece, width), f32),
            jax.ShapeDtypeStruct((turns, piece, width), i16),
            jax.ShapeDtypeStruct((turns, 8, padded), f32),
            jax.ShapeDtypeStruct((others,) + small_shape, f32),
            jax.ShapeDtypeStruct((others, heads, width), f32),
            jax.ShapeDtypeStruct((shards - 1 + groups - 1, 8, width // 8), f32),
        ],
        scratch_shapes=[
            pltpu.VMEM((hops, lines * parts) + coded, i16),
            pltpu.VMEM((hops, lines * parts) + scale, f32),
            pltpu.VMEM(((lines + 1) * parts,) + coded, i16),
            pltpu.VMEM(((lines + 1) * parts,) + scale, f32),
            pltpu.VMEM((count, width), f32),
            pltpu.VMEM((lines * parts,) + coded, i16),
            pltpu.VMEM((lines * parts,) + scale, f32),
            pltpu.VMEM(((lines - 1) * parts,) + coded, i16),
            pltpu.VMEM(((lines - 1) * parts,) + scale, f32),
            pltpu.VMEM((max(count, padded), 128), f32),
            pltpu.VMEM((piece, width), f32),
            pltpu.VMEM((piece, width), f32),
            pltpu.VMEM((turns, piece, width), i16),
            pltpu.VMEM((turns, 8, padded), f32),
            pltpu.VMEM((piece, width), i16),
            pltpu.VMEM((8, padded), f32),
            pltpu.VMEM((piece, width), i16),
            pltpu.VMEM((8, padded), f32),
            pltpu.VMEM(small_shape, f32),
            pltpu.VMEM(small_shape, f32),
            pltpu.VMEM((heads, width), f32),
            pltpu.VMEM((heads, width), f32),
            pltpu.VMEM((8, width), f32),
            pltpu.VMEM((8, width // 8), f32),
            pltpu.VMEM((shards, blocks, per, main), bf16),
            pltpu.VMEM((shards, blocks, per, rest), bf16),
            pltpu.VMEM((main + rest, total), bf16),
            pltpu.VMEM((main, width), bf16),
            pltpu.VMEM((total, main), bf16),
            pltpu.VMEM((2, total, tile), bf16),
            pltpu.VMEM((2, main + rest, tile), f32),
            dma,
            dma,
            dma((2,)),
            dma((2,)),
            dma((2,)),
            dma((lots,)),
            dma((rows_y, lots)),
            dma((groups, lots)),
            dma((rows_y, lots)),
            dma,
            dma((shards,)),
            dma((shards,)),
            dma((2, hops * lines * parts)),
            dma((2, hops * lines * parts)),
            dma((2, lines * parts)),
            dma((2, (lines + 1) * parts)),
            dma((rows_y,)),
            dma((rows_y,)),
            dma((2, turns)),
            dma((2, turns)),
            dma((piece // CHUNK, shards)),
            dma,
            dma((shards + groups,)),
            dma((shards + groups,)),
            dma((groups + shards,)),
            dma((groups + shards,)),
            dma((groups + shards,)),
            dma((groups + shards,)),
            dma((shards + groups,)),
            dma((shards + groups,)),
        ],
        compiler_params=pltpu.CompilerParams(
            collective_id=7, has_side_effects=True, vmem_limit_bytes=62 * 1024 * 1024
        ),
        cost_estimate=pl.CostEstimate(flops=0, bytes_accessed=450_000_000, transcendentals=0),
        name="finish_exchange",
    )(slots, d_cols, d_rest, normed, weight, weight_rest, no_rows, out_part, small, scaled_rows)
    return out[:8]


def nesterov(weight, gradient, moment, average, step_rate):
    decayed = gradient + weight_decay * weight
    new_moment = momentum_decay * moment + decayed
    new_weight = weight - step_rate * (decayed + momentum_decay * new_moment)
    new_average = average_decay * average + (1.0 - average_decay) * new_weight
    return (new_moment, new_weight, new_average)


def dot32(a, b, contract=((1,), (0,))):
    return lax.dot_general(a, b, (contract, ((), ())), preferred_element_type=jnp.float32)


def own_slice(value, index, width, axis):
    return lax.dynamic_slice_in_dim(value, index * width, width, axis)


def local(
    tokens,
    cotangent,
    lengths,
    deal_slot,
    in_weight,
    out_weight,
    small_params,
    in_moment,
    out_moment,
    small_moment,
    in_average,
    out_average,
    small_average,
):
    shards, groups = lax.axis_size("shard"), lax.axis_size("group")
    shard, group = lax.axis_index("shard"), lax.axis_index("group")
    rows, width = tokens.shape
    per = rows // shards
    total = rows * shards
    blocks = total // BLOCK
    heads = HEADS // shards
    inner = INNER // shards
    shared = SHARED // shards
    conv_flat, conv_bias, dt_bias, rate_log, skip_gain, norm_gain, pre_gain = unpack(small_params)
    taps = conv_flat.reshape(CONV, XBC)

    cols, depth, sends = in_weight.shape[1], in_weight.shape[0], out_weight.shape[1]
    direct = cols % CHUNK == 0 and depth % 128 == 0 and sends % 128 == 0 and per % CHUNK == 0
    direct = direct and (2 * inner + SHARED + HEADS) % (groups * CHUNK) == 0 and shared % CHUNK == 0
    bounds = jnp.cumsum(lengths[0])[:-1].astype(jnp.int32)
    seg_rows = segment_of(jnp.arange(total, dtype=jnp.int32), lengths[0])

    rank = jnp.sum((deal_slot[None, :] < deal_slot[:, None]).astype(jnp.int32), axis=1)
    sort_mat = (rank[None, :] == jnp.arange(rows)[:, None]).astype(jnp.bfloat16)
    r_in = lax.rsqrt(jnp.mean(tokens * tokens, axis=1, keepdims=True) + eps_norm)
    in_turned = in_weight.T

    if direct:
        x_all, in_low, out_low, slot_all, c_sorted, out_cast, x_scaled = front_exchange(
            shards, groups, tokens, pre_gain, cotangent, in_turned, out_weight, deal_slot
        )
        x_all = x_all.reshape(blocks, BLOCK, width)
        slot_all = slot_all[:, 0, :]
    else:
        sorted_slot = jnp.sum(jnp.where(sort_mat > 0, deal_slot[None, :], 0), axis=1)
        x_scaled = jnp.dot(sort_mat.astype(jnp.float32), tokens * r_in, precision=lax.Precision.HIGHEST)
        normed_low = (tokens * r_in * pre_gain[None, :]).astype(jnp.bfloat16)
        x_sorted = dot32(sort_mat, normed_low).astype(jnp.bfloat16).reshape(blocks, per, width)
        c_sorted = dot32(sort_mat, cotangent.astype(jnp.bfloat16)).astype(jnp.bfloat16)
        c_sorted = c_sorted.reshape(blocks, per, width)
        in_turned = in_turned.astype(jnp.bfloat16)
        out_cast = out_weight.astype(jnp.bfloat16)
        x_all = lax.all_gather(x_sorted, "shard").transpose(1, 0, 2, 3).reshape(blocks, BLOCK, width)
        slot_all = lax.all_gather(sorted_slot, "shard")
        part = depth // groups
        pieces = lax.all_to_all(in_turned.reshape(cols, groups, part), "group", 1, 0)
        pieces = pieces.reshape(groups * cols, part)

        def cut(lo, each):
            return pieces[lo : lo + each * shards].reshape(shards, each, part)

        spread = jnp.broadcast_to(pieces[None, 2 * INNER :], (shards, SHARED + HEADS, part))
        got = jnp.concatenate([cut(0, inner), cut(INNER, inner), spread], axis=1)
        got = lax.all_gather(lax.all_to_all(got, "shard", 0, 0), "group")
        in_low = got.transpose(2, 1, 0, 3).reshape(-1, width)
        out_low = lax.all_gather(out_cast, "group", axis=1, tiled=True)
    slot_blk = slot_all.reshape(shards, blocks, per).transpose(1, 0, 2).reshape(blocks, 1, BLOCK)
    slot_blk = slot_blk - jnp.arange(blocks, dtype=jnp.int32)[:, None, None] * BLOCK

    taps_v = own_slice(taps[:, :INNER], shard, inner, 1)
    taps_all = jnp.concatenate([taps_v, taps[:, INNER:]], axis=1)
    bias_all = jnp.concatenate([own_slice(conv_bias[:INNER], shard, inner, 0), conv_bias[INNER:]])[None, :]
    skip_wide = jnp.repeat(own_slice(skip_gain, shard, heads, 0), HDIM)[None, :]
    gain_own = own_slice(norm_gain, shard, inner, 0)[None, :]
    padding = max(TAIL - heads, 0)
    rate = jnp.pad(-jnp.exp(own_slice(rate_log, shard, heads, 0)), (0, padding))[:, None]
    normed, projected, pre, mixed, states, dt_cols, dt_raw, c_all = mixer_forward(
        shards, bounds, slot_blk, x_all, in_low, taps_all, bias_all, dt_bias[None, :], rate, skip_wide, c_sorted
    )
    conv_bc = lax.dynamic_slice_in_dim(projected, 2 * inner + shard * shared, shared, 1)
    cot_low, d_out, sums = pack_cotangent(
        shards, slot_blk, c_all.reshape(blocks, BLOCK, width), out_low, mixed, projected, gain_own
    )

    d_cols, d_bc, d_dt, grads, rate_terms, grad_out, no_rows, home_late, out_full = mixer_backward(
        shards, bounds, slot_blk, pre, mixed, projected, d_out, sums, states, dt_cols, cot_low,
        taps_v, rate, skip_wide, gain_own, out_cast[None],
    )
    out_block = out_full.reshape(INNER, -1)
    grad_out = lax.psum_scatter(grad_out, "group", scatter_dimension=1, tiled=True)

    d_dtraw = d_dt[:heads].T * jax.nn.sigmoid(dt_raw[:, :heads])
    grad_dtb = jnp.sum(d_dtraw, axis=0)
    grad_rate = jnp.sum(rate_terms[:heads], axis=1)
    grad_skip = jnp.sum(grads[6].reshape(heads, HDIM), axis=1)
    _, pull_bc = jax.vjp(
        lambda c, t, b: convolve(c, seg_rows, t, b),
        conv_bc,
        own_slice(taps[:, INNER:], shard, shared, 1),
        own_slice(conv_bias[INNER:], shard, shared, 0),
    )
    d_conv_bc, grad_taps_bc, grad_bias_bc = pull_bc(d_bc.T)
    rest = 128 - shared - heads
    d_rest = jnp.concatenate([d_conv_bc, d_dtraw, jnp.zeros((total, rest), jnp.float32)], axis=1)
    in_rest = jnp.concatenate(
        [
            own_slice(in_low[2 * inner : 2 * inner + SHARED], shard, shared, 0),
            own_slice(in_low[2 * inner + SHARED :], shard, heads, 0),
            jnp.zeros((rest, width), jnp.bfloat16),
        ]
    )

    mine = [
        grads[:CONV].reshape(-1),
        grad_taps_bc.reshape(-1),
        grads[4],
        grad_bias_bc,
        grad_dtb,
        grad_rate,
        grad_skip,
        grads[5],
    ]
    extents = [piece.shape[0] for piece in mine]
    mine = jnp.concatenate(mine)
    mine = jnp.pad(mine, (0, -mine.shape[0] % 1024)).reshape(-1, 128)
    d_rest = d_rest.astype(jnp.bfloat16)
    if direct:
        d_normed, grad_in, grad_marks, small_all, dt_part, gain_all, home, out_full = finish_exchange(
            shards, groups, slot_blk, d_cols, d_rest, normed, in_low, in_rest, no_rows, out_block, mine, x_scaled,
            cols, depth,
        )
    else:
        partial, weight_part, home = project_back(
            slot_blk, d_cols, d_rest, normed, in_low, in_rest, no_rows, shards
        )
        out_full = lax.all_gather(out_block, "group", axis=1, tiled=True)
        d_normed, _, _, small_all, gain_all = tail_exchange(
            shards, groups, partial.reshape(shards, rows, width), weight_part, mine, x_scaled, cols, depth, False
        )

    home = jnp.concatenate([home, home_late], axis=1)
    home = home.reshape(shards, rows, inner).transpose(1, 0, 2).reshape(rows, INNER)
    home = dot32(sort_mat, home, ((0,), (0,))).astype(jnp.bfloat16)
    block_out = tokens + dot32(home, out_full)
    d_normed = jnp.dot(sort_mat.T.astype(jnp.float32), d_normed, precision=lax.Precision.HIGHEST)
    d_scaled = pre_gain[None, :] * d_normed
    inside = jnp.mean(tokens * d_scaled, axis=1, keepdims=True)
    input_grad = cotangent + r_in * (d_scaled - tokens * (r_in * r_in) * inside)
    grad_pre = gain_all.reshape(width)

    mine = small_all.reshape(shards, -1)
    found, offset = [], 0
    for extent in extents:
        found.append(mine[:, offset : offset + extent])
        offset = offset + extent
    if direct:
        dt_part = dt_part.reshape(HEADS, depth)
        steps = grad_marks[:, :, 0, : piece_rows(shards, groups)].reshape(shards, -1)
        steps = jnp.concatenate(
            [
                steps[:, :inner].reshape(-1),
                steps[:, inner : 2 * inner].reshape(-1),
                steps[:, 2 * inner : 2 * inner + shared].reshape(-1),
                jnp.zeros((HEADS,), jnp.float32),
            ]
        )
        grad_in = grad_in.astype(jnp.float32) * own_slice(steps, group, cols, 0)[:, None]
        last = jnp.concatenate([grad_in[: cols - HEADS], dt_part])
        grad_in = jnp.where(group == groups - 1, last, grad_in)
    else:
        used = 2 * inner + shared + heads
        grad_in = weight_part[:used].reshape(used, shards, groups, part).transpose(2, 1, 0, 3)
        grad_in = lax.psum_scatter(grad_in, "group", scatter_dimension=0)
        grad_in = lax.all_to_all(grad_in, "shard", 0, 0)

        def join(lo, each):
            return grad_in[:, lo : lo + each].reshape(shards * each, part)

        grad_in = jnp.concatenate(
            [
                join(0, inner),
                join(inner, inner),
                join(2 * inner, shared),
                join(2 * inner + shared, heads),
            ]
        )
        grad_in = lax.all_to_all(grad_in.reshape(groups, cols, part), "group", 0, 0)
        grad_in = grad_in.transpose(1, 0, 2).reshape(cols, depth)

    def taps_of(piece):
        return piece.reshape(shards, CONV, -1).transpose(1, 0, 2).reshape(CONV, -1)

    grad_taps = jnp.concatenate([taps_of(found[0]), taps_of(found[1])], axis=1).reshape(-1)
    grad_small = jnp.concatenate([grad_taps] + [piece.reshape(-1) for piece in found[2:]] + [grad_pre])
    in_new = nesterov(in_weight.T, grad_in, in_moment.T, in_average.T, rate_in)
    in_new = tuple(value.T for value in in_new)
    out_new = nesterov(out_weight, grad_out, out_moment, out_average, rate_out)
    small_new = nesterov(small_params, grad_small, small_moment, small_average, rate_small)
    return (block_out, input_grad) + in_new + out_new + small_new


def solution(mesh):
    rows = P(("group", "shard"), None)
    tile = P("shard", "group")
    return jax.shard_map(
        local,
        mesh=mesh,
        in_specs=(
            rows,
            rows,
            P("group", None),
            P(("group", "shard")),
            tile,
            tile,
            P(),
            tile,
            tile,
            P(),
            tile,
            tile,
            P(),
        ),
        out_specs=(rows, rows, tile, tile, tile, tile, tile, tile, P(), P(), P()),
        check_vma=False,
    )
```

```python
import functools

import jax
import jax.numpy as jnp
from jax import lax
from jax.experimental import pallas as pl
from jax.experimental.pallas import tpu as pltpu
from jax.sharding import PartitionSpec as P

D = 2048
HEADS = 64
HDIM = 64
STATE = 128
CONV = 4
BLOCK = 256
INNER = 4096
XBC = 4352
SHARED = 2 * STATE
TAIL = 8
CHUNK = 16
MESH = pl.DeviceIdType.MESH


eps_norm = 1e-05
momentum_decay = 0.9
weight_decay = 0.01
average_decay = 0.99
rate_in = 0.0001
rate_out = 3e-05
rate_small = 0.001


def unpack(packed_small):
    extents = [CONV * XBC, XBC, HEADS, HEADS, HEADS, INNER, D]
    pieces = []
    offset = 0
    for extent in extents:
        pieces.append(packed_small[offset : offset + extent])
        offset = offset + extent
    return pieces


def segment_of(positions, lengths_row):
    bounds = jnp.cumsum(lengths_row)[:-1]
    inside = jnp.sum((positions[:, None] >= bounds[None, :]).astype(jnp.int32), axis=1)
    return jnp.where(positions < 0, -1, inside)


def convolve(conv_rows, seg_rows, conv_taps, conv_bias):
    row_count, width = conv_rows.shape
    extended = jnp.concatenate([jnp.zeros((CONV - 1, width), conv_rows.dtype), conv_rows], axis=0)
    seg_ext = jnp.concatenate([jnp.full((CONV - 1,), -1, jnp.int32), seg_rows], axis=0)
    conv_sum = jnp.zeros_like(conv_rows) + conv_bias[None, :]
    for tap_index in range(CONV):
        same_seq = (seg_ext[tap_index : tap_index + row_count] == seg_rows)[:, None]
        conv_sum = conv_sum + jnp.where(
            same_seq,
            extended[tap_index : tap_index + row_count] * conv_taps[tap_index][None, :],
            0.0,
        )
    return jax.nn.silu(conv_sum)


def split(value):
    high = value.astype(jnp.bfloat16)
    return high, (value - high.astype(jnp.float32)).astype(jnp.bfloat16)


def dots(a, b, contract):
    return lax.dot_general(a, b, (contract, ((), ())), preferred_element_type=jnp.float32)


def dot3(a, b, contract=((1,), (0,))):
    a = a if isinstance(a, tuple) else split(a)
    b = b if isinstance(b, tuple) else split(b)
    return dots(a[0], b[0], contract) + (dots(a[0], b[1], contract) + dots(a[1], b[0], contract))


NT = ((1,), (1,))


def dot_wide(a, wide):
    high, low = split(a)
    lanes = wide.shape[1] // 2
    plain = ((1,), (0,))
    first = dots(high, wide, plain)
    return first[:, :lanes] + (first[:, lanes:] + dots(low, wide[:, :lanes], plain))


def beside(first, second, own):
    moved = pltpu.roll(second.astype(jnp.float32), HDIM, 1).astype(jnp.bfloat16)
    return jnp.where(own, first, moved)


def head_sums(value, marks):
    high = value.astype(jnp.bfloat16)
    rest = value - high.astype(jnp.float32)
    mid = rest.astype(jnp.bfloat16)
    low = (rest - mid.astype(jnp.float32)).astype(jnp.bfloat16)
    return dots(marks, high, NT) + (dots(marks, mid, NT) + dots(marks, low, NT))


def widen(columns, heads):
    rows = columns.shape[0]
    low_half = lax.broadcasted_iota(jnp.int32, (rows, 2 * HDIM), 1) < HDIM
    return jnp.concatenate(
        [
            jnp.where(low_half, columns[:, h : h + 1], columns[:, h + 1 : h + 2])
            for h in range(0, heads, 2)
        ],
        axis=1,
    )


def running_sum(value, reverse=False):
    lane = lax.broadcasted_iota(jnp.int32, value.shape, 1)
    count = value.shape[1]
    step = 1
    while step < count:
        if reverse:
            value = value + jnp.where(lane < count - step, pltpu.roll(value, count - step, 1), 0.0)
        else:
            value = value + jnp.where(lane >= step, pltpu.roll(value, step, 1), 0.0)
        step *= 2
    return value


def sequence_of(positions, bounds):
    inside = jnp.where(positions >= bounds[0], 1, 0) + jnp.where(positions >= bounds[1], 1, 0)
    return jnp.where(positions < 0, -1, inside)


def block_facts(block, bounds, dt_t, rate):
    start = block * BLOCK
    seg_col = sequence_of(start + lax.broadcasted_iota(jnp.int32, (BLOCK, 1), 0), bounds)
    seg_row = sequence_of(start + lax.broadcasted_iota(jnp.int32, (1, BLOCK), 1), bounds)
    before = sequence_of(start - 1 + lax.broadcasted_iota(jnp.int32, (1, 1), 1), bounds)
    last = sequence_of(start + BLOCK - 1 + lax.broadcasted_iota(jnp.int32, (1, 1), 1), bounds)
    run_t = running_sum(dt_t * rate)
    run = run_t.T
    final = run[BLOCK - 1 :, :]
    carried = jnp.where(seg_col == before, jnp.exp(run), 0.0)
    tail = jnp.where(seg_col == last, jnp.exp(final - run), 0.0)
    keep = jnp.where(last == before, jnp.exp(final), 0.0)
    return seg_col, seg_row, run_t, run, carried, tail, keep


def barrier_with(peers):
    barrier = pltpu.get_barrier_semaphore()
    for peer in peers:
        pl.semaphore_signal(barrier, inc=1, device_id=peer, device_id_type=MESH)
    pl.semaphore_wait(barrier, len(peers))


def remote(src, dst, sends, recvs, **where):
    return pltpu.make_async_remote_copy(
        src_ref=src, dst_ref=dst, send_sem=sends, recv_sem=recvs, device_id=where, device_id_type=MESH
    )


def place_of_rows(slots):
    count = slots.shape[1]
    return (lax.broadcasted_iota(jnp.int32, (BLOCK, count), 0) == slots).astype(jnp.bfloat16)


def grid_columns(shards):
    columns = 1
    while 2 * (2 * columns) * (2 * columns) <= shards:
        columns *= 2
    return columns if shards % columns == 0 else 1


def whole(shape):
    return pl.BlockSpec(shape, lambda *_: (0,) * len(shape))


def row_gather(shards, columns, own, gathered, local_sem, sends, recvs):
    shard = lax.axis_index("shard")
    lines = shards // columns
    z, x = shard // columns, shard % columns

    def line_copy(source, way, first=False):
        at = source * columns + x
        peer = jnp.clip(z + 1 - 2 * way, 0, lines - 1) * columns + x
        rows = own if first else gathered.at[:, at]
        return remote(rows, gathered.at[:, at], sends.at[way, source], recvs.at[at], shard=peer)

    def wide_copy(source, hop, first=False):
        at = source * columns + x
        peer = z * columns + (x + hop) % columns
        rows = own if first else gathered.at[:, at]
        return remote(rows, gathered.at[:, at], sends.at[1 + hop, source], recvs.at[at], shard=peer)

    def pass_on(source, ways, first=False):
        for way in ways:
            @pl.when(z < lines - 1 if way == 0 else z > 0)
            def _():
                line_copy(source, way, first).start()

        for hop in range(1, columns):
            wide_copy(source, hop, first).start()

    here = pltpu.make_async_copy(own, gathered.at[:, shard], local_sem)

    def begin():
        pass_on(z, (0, 1), True)
        here.start()

    def hop(step):
        @pl.when(z - step >= 0)
        def _():
            line_copy(z - step, 0).wait_recv()
            pass_on(z - step, (0,))

        @pl.when(z + step < lines)
        def _():
            line_copy(z + step, 1).wait_recv()
            pass_on(z + step, (1,))

    def end():
        here.wait()
        for step in range(1, columns):
            peer = z * columns + (x + step) % columns
            for source in range(lines):
                at = source * columns + (x + step) % columns
                remote(gathered.at[:, at], gathered.at[:, at], sends.at[1 + step, source], recvs.at[at], shard=peer).wait_recv()
        for source in range(lines):
            for step in range(1, columns):
                wide_copy(source, step).wait_send()

            @pl.when((z < lines - 1) & (source <= z))
            def _():
                line_copy(source, 0).wait_send()

            @pl.when((z > 0) & (source >= z))
            def _():
                line_copy(source, 1).wait_send()

    return begin, hop, end


def gather_semaphores(shards, columns):
    dma = pltpu.SemaphoreType.DMA
    return [
        dma,
        dma((1 + columns, shards // columns)),
        dma((shards,)),
    ]


def softplus(value):
    small = jnp.exp(-jnp.abs(value))
    ratio = small / (2.0 + small)
    square = ratio * ratio
    series = jnp.full_like(value, 1.0 / 15.0)
    for power in (13, 11, 9, 7, 5, 3, 1):
        series = series * square + 1.0 / power
    return jnp.maximum(value, 0.0) + 2.0 * ratio * series


def pick_columns(value, marks):
    high = value.astype(jnp.bfloat16)
    rest = value - high.astype(jnp.float32)
    mid = rest.astype(jnp.bfloat16)
    low = (rest - mid.astype(jnp.float32)).astype(jnp.bfloat16)
    plain = ((1,), (0,))
    return dots(high, marks, plain) + (dots(mid, marks, plain) + dots(low, marks, plain))


def forward_kernel(
    heads, shards, columns, bounds, slots, rows_in, weight, taps, bias, dt_bias, rate, skip, cot_own,
    packed, product, pre_out, mixed_out, state_out, dt_out, raw_out, cot_all,
    ext, state, *gather_sems,
):
    block = pl.program_id(0)
    blocks = cot_own.shape[0]
    inner = heads * HDIM
    shard = lax.axis_index("shard")
    begin, hop, end = row_gather(shards, columns, cot_own, cot_all, *gather_sems)
    hops = range(1, shards // columns)

    @pl.when(block == 0)
    def _():
        barrier_with([{"shard": (shard + step) % shards} for step in range(1, shards)])
        begin()
        ext[:TAIL, :] = jnp.zeros((TAIL, ext.shape[1]), jnp.float32)
        state[...] = jnp.zeros_like(state)

    for step in hops:
        if (7 * step + 1) // 2 < blocks:
            pl.when(block == (7 * step + 1) // 2)(functools.partial(hop, step))

    normed = dots(place_of_rows(slots[0]), rows_in[0], ((1,), (0,))).astype(jnp.bfloat16)
    packed[...] = normed
    product[...] = dots(normed, weight[...], NT)
    head = lax.broadcasted_iota(jnp.int32, (HEADS, 128), 0)
    lane = lax.broadcasted_iota(jnp.int32, (HEADS, 128), 1)
    marks = ((head == shard * heads + lane) & (lane < heads)).astype(jnp.bfloat16)
    raw = pick_columns(product[:, 2 * inner + SHARED :] + dt_bias[...], marks)
    raw_out[...] = raw
    dt = softplus(raw)
    dt_out[...] = dt

    bounds = (bounds[0], bounds[1])
    dt_t = dt.T[: rate.shape[0], :]
    seg_col, seg_row, run_t, run, carried, tail, keep = block_facts(block, bounds, dt_t, rate[...])
    ext[TAIL:, :] = product[:, inner : 2 * inner + SHARED]
    place = block * BLOCK + lax.broadcasted_iota(jnp.int32, (BLOCK, 1), 0)
    pre = bias[...] + taps[CONV - 1 : CONV, :] * ext[TAIL:, :]
    for back in range(1, CONV):
        same = sequence_of(place - back, bounds) == seg_col
        moved = ext[TAIL - back : TAIL - back + BLOCK, :]
        pre = pre + jnp.where(same, moved, 0.0) * taps[CONV - 1 - back : CONV - back, :]
    ext[:TAIL, :] = ext[BLOCK:, :]
    pre_out[...] = pre
    conv = pre / (1.0 + jnp.exp(-pre))
    values, b_rows, c_rows = conv[:, :inner], conv[:, inner : inner + STATE], conv[:, inner + STATE :]
    fed = values * widen(dt, heads)
    rows = lax.broadcasted_iota(jnp.int32, (BLOCK, BLOCK), 0)
    cols = lax.broadcasted_iota(jnp.int32, (BLOCK, BLOCK), 1)
    allowed = (seg_col == seg_row) & (rows >= cols)
    b_parts, c_parts = split(b_rows), split(c_rows)
    scores = jnp.where(allowed, dot3(c_parts, b_parts, NT), 0.0)
    old = state[...]
    state_out[0] = old
    output = widen(carried, heads) * dot3(c_parts, old)
    low_half = lax.broadcasted_iota(jnp.int32, (BLOCK, 2 * HDIM), 1) < HDIM
    inside = []
    for h in range(0, heads, 2):
        pair = jnp.concatenate(split(fed[:, h * HDIM : (h + 2) * HDIM]), axis=1)
        found = []
        for k in (h, h + 1):
            mixing = jnp.exp(jnp.minimum(run[:, k : k + 1] - run_t[k : k + 1, :], 0.0)) * scores
            found.append(dot_wide(mixing, pair))
        inside.append(jnp.where(low_half, found[0], found[1]))
    mixed = output + jnp.concatenate(inside, axis=1) + skip[...] * values
    mixed_out[...] = mixed
    state[...] = widen(keep, heads) * old + dot3(b_rows.T, widen(tail, heads) * fed)

    @pl.when(block == blocks - 1)
    def _():
        for step in hops:
            if (7 * step + 1) // 2 >= blocks:
                hop(step)
        end()


def cotangent_kernel(
    shards, slots, rows_in, weight, mixed, gate, gain,
    packed, product, sums_out, own_sums, sums_in, sums_send, sums_recv,
):
    block = pl.program_id(0)
    shard = lax.axis_index("shard")

    @pl.when(block == 0)
    def _():
        barrier_with([{"shard": (shard + step) % shards} for step in range(1, shards)])

    several = rows_in.shape[0]
    for turn in range(several):
        rows = pl.ds(turn * BLOCK, BLOCK)
        packed[rows, :] = dots(place_of_rows(slots[turn]), rows_in[turn], ((1,), (0,))).astype(jnp.bfloat16)
    d_out = dots(packed[...], weight[...], NT)
    product[...] = d_out
    gate_now = gate[...]
    gated = mixed[...] * (gate_now / (1.0 + jnp.exp(-gate_now)))
    squares = jnp.sum(gated * gated, axis=1, keepdims=True)
    products = jnp.sum(gated * gain[...] * d_out, axis=1, keepdims=True)
    lane = lax.broadcasted_iota(jnp.int32, (several * BLOCK, 128), 1)
    both = jnp.where(lane == 0, squares, jnp.where(lane == 1, products, 0.0))
    here = pl.ds(pl.multiple_of(block * several * BLOCK, BLOCK), several * BLOCK)
    own_sums[:, here] = both.T[:8, :]

    def push(step, at):
        return remote(
            own_sums.at[:, at], sums_in.at[step - 1, :, at], sums_send.at[step], sums_recv.at[step],
            shard=(shard + step) % shards,
        )

    for step in range(1, shards):
        push(step, here).start()

    @pl.when(block == pl.num_programs(0) - 1)
    def _():
        everything = pl.ds(0, own_sums.shape[1])
        for step in range(1, shards):
            push(step, everything).wait()
        found = own_sums[...]
        for step in range(1, shards):
            found = found + sums_in[step - 1]
        sums_out[...] = found * (1.0 / INNER)


def backward_kernel(
    heads, blocks, shards, columns, bounds, slots, pre, mixed, gate, d_out, conv_v, sums, state_in, dt_cols,
    taps, rate, skip, gain, marks, out_own,
    d_cols, d_bc, d_dt, grads, grad_rate, no_rows, home, out_all,
    ext, carry, bc_rows, bc_wide, bc_sum, bc_in, late_rows, wide_send, wide_recv, bc_send, bc_recv, home_send, home_recv, local_sem, *gather_sems,
):
    step = pl.program_id(0)
    block = blocks - 1 - step
    inner = heads * HDIM
    shard = lax.axis_index("shard")
    shared = SHARED // shards
    lines = shards // columns
    z, x = shard // columns, shard % columns
    begin, hop, end = row_gather(shards, columns, out_own, out_all, *gather_sems)
    hops = range(1, shards // columns)

    @pl.when(step == 0)
    def _():
        barrier_with([{"shard": (shard + turn) % shards} for turn in range(1, shards)])
        begin()
        ext[BLOCK:, :] = jnp.zeros((TAIL, ext.shape[1]), jnp.float32)
        carry[...] = jnp.zeros_like(carry)
        grads[...] = jnp.zeros_like(grads)
        grad_rate[...] = jnp.zeros_like(grad_rate)

    for turn in hops:
        if 2 * turn < blocks:
            pl.when(step == 2 * turn)(functools.partial(hop, turn))

    bounds = (bounds[0], bounds[1])
    dt = dt_cols[...]
    dt_t = dt.T[: rate.shape[0], :]
    seg_col, seg_row, run_t, run, carried, tail, keep = block_facts(block, bounds, dt_t, rate[...])
    sums_cols = sums[...].T
    r_out = lax.rsqrt(sums_cols[:, 0:1] + 1e-05)
    inside = sums_cols[:, 1:2]
    gate_now = gate[...]
    gate_sig = 1.0 / (1.0 + jnp.exp(-gate_now))
    act = gate_now * gate_sig
    mixed_now = mixed[...]
    gated = mixed_now * act
    d_out_now = d_out[...]
    normed_out = (gated * r_out * gain[...]).astype(jnp.bfloat16)
    to_home = dots(place_of_rows(slots[0]), normed_out, ((0,), (0,)))
    per = BLOCK // shards
    if per % 16 == 0:
        no_rows[0] = to_home.astype(jnp.bfloat16).reshape(shards, per, inner)
    else:
        for turn in range(shards):
            no_rows[0, turn] = to_home[turn * per : (turn + 1) * per].astype(jnp.bfloat16)
    half = home.shape[0]
    lanes = pl.ds(pl.multiple_of(shard * inner, inner), inner)

    def push_home(turn, at):
        peer = (shard + turn) % shards
        return remote(late_rows.at[at, peer], home.at[at, :, lanes], home_send.at[turn], home_recv.at[turn], shard=peer)

    @pl.when(step < blocks - half)
    def _():
        late_rows[block - half] = no_rows[0]
        for turn in range(1, shards):
            push_home(turn, pl.ds(block - half, 1)).start()
    d_gated = r_out * (gain[...] * d_out_now - gated * (r_out * r_out) * inside)
    dy = d_gated * act
    d_cols[:, :inner] = (d_gated * mixed_now * (gate_sig * (1.0 + gate_now * (1.0 - gate_sig)))).astype(jnp.bfloat16)
    grads[5:6, :] += jnp.sum(gated * r_out * d_out_now, axis=0, keepdims=True)
    pre_now = pre[...]
    sig = 1.0 / (1.0 + jnp.exp(-pre_now))
    conv = pre_now * sig
    values, b_rows, c_rows = conv[:, :inner], conv[:, inner : inner + STATE], conv[:, inner + STATE :]
    grads[6:7, :] += jnp.sum(dy * values, axis=0, keepdims=True)
    dt_wide = widen(dt, heads)
    fed = values * dt_wide
    old, after = state_in[0], carry[...]
    b_parts, c_parts, old_parts, after_parts = split(b_rows), split(c_rows), split(old), split(after)
    carried_wide, tail_wide, keep_wide = widen(carried, heads), widen(tail, heads), widen(keep, heads)
    rows = lax.broadcasted_iota(jnp.int32, (BLOCK, BLOCK), 0)
    cols = lax.broadcasted_iota(jnp.int32, (BLOCK, BLOCK), 1)
    allowed = (seg_col == seg_row) & (cols >= rows)
    scores_t = jnp.where(allowed, dot3(b_parts, c_parts, NT), 0.0)
    low_half = lax.broadcasted_iota(jnp.int32, (BLOCK, 2 * HDIM), 1) < HDIM
    d_scores_t = jnp.zeros((BLOCK, BLOCK), jnp.float32)
    d_fed, row_terms, col_terms = [], [], []
    for h in range(0, heads, 2):
        fed_pair = fed[:, h * HDIM : (h + 2) * HDIM]
        fed_high, fed_low = split(fed_pair)
        dy_high, dy_low = split(dy[:, h * HDIM : (h + 2) * HDIM])
        dy_wide = jnp.concatenate([dy_high, dy_low], axis=1)
        found = []
        for k in (h, h + 1):
            own = low_half if k == h else jnp.logical_not(low_half)
            left = jnp.concatenate(
                [beside(fed_high, fed_low, own), jnp.where(own, fed_high, 0.0).astype(jnp.bfloat16)], axis=1
            )
            right = jnp.concatenate([beside(dy_high, dy_high, own), dy_low], axis=1)
            d_mixing = dots(left, right, NT)
            decay = jnp.exp(jnp.minimum(run_t[k : k + 1, :] - run[:, k : k + 1], 0.0))
            mixing = decay * scores_t
            d_scores_t = d_scores_t + decay * d_mixing
            flow = mixing * d_mixing
            row_terms.append(jnp.sum(flow, axis=0, keepdims=True))
            col_terms.append(jnp.sum(flow, axis=1, keepdims=True))
            found.append(dot_wide(mixing, dy_wide))
        d_fed.append(jnp.where(low_half, found[0], found[1]))
    d_scores_t = split(jnp.where(allowed, d_scores_t, 0.0))
    fed_tail = fed * tail_wide
    dy_carried = dy * carried_wide
    d_fed_out = tail_wide * dot3(b_parts, after_parts)
    d_fed = jnp.concatenate(d_fed, axis=1) + d_fed_out
    dy_parts, tail_parts = split(dy_carried), split(fed_tail)
    here = pl.ds(pl.multiple_of(block * BLOCK, BLOCK), BLOCK)
    bc_now = jnp.concatenate(
        [
            (dot3(d_scores_t, c_parts) + dot3(tail_parts, after_parts, NT)).T,
            (dot3(d_scores_t, b_parts, ((0,), (0,))) + dot3(dy_parts, old_parts, NT)).T,
        ],
        axis=0,
    )
    bc_rows[:, :, :, here] = bc_now.reshape(lines, columns, shared, BLOCK)

    def at_step(turn):
        return pl.ds(pl.multiple_of((blocks - 1 - turn) * BLOCK, BLOCK), BLOCK)

    def push_wide(turn, hop):
        to = (x + hop) % columns
        return remote(
            bc_rows.at[:, to, :, at_step(turn)], bc_wide.at[hop - 1, :, :, at_step(turn)],
            wide_send.at[hop - 1, turn], wide_recv.at[hop - 1, turn], shard=z * columns + to,
        )

    def push_line(hop, at):
        to = (z + hop) % lines
        return remote(bc_sum.at[to, :, at], bc_in.at[hop - 1, :, at], bc_send.at[hop], bc_recv.at[hop], shard=to * columns + x)

    def add_wide(turn):
        found = bc_rows[:, x, :, at_step(turn)]
        for hop in range(1, columns):
            push_wide(turn, hop).wait_recv()
            found = found + bc_wide[hop - 1, :, :, at_step(turn)]
        bc_sum[:, :, at_step(turn)] = found
        for hop in range(1, lines):
            push_line(hop, at_step(turn)).start()

    for hop_x in range(1, columns):
        push_wide(step, hop_x).start()

    lag = min(3, blocks - 1)

    @pl.when(step >= lag)
    def _():
        add_wide(step - lag)

    head_count = dt_t.shape[0]
    pad = [jnp.zeros((1, BLOCK), jnp.float32)] * (head_count - heads)
    pad_col = [jnp.zeros((BLOCK, 1), jnp.float32)] * (head_count - heads)
    d_run = jnp.concatenate(row_terms + pad, axis=0) - jnp.concatenate(col_terms + pad_col, axis=1).T
    d_run = d_run + head_sums(dy_carried * dot3(c_parts, old_parts), marks[...])
    leaving = head_sums(fed * d_fed_out, marks[...])
    kept = jnp.sum(old * after, axis=0, keepdims=True) * keep_wide
    kept = jnp.sum(marks[...].astype(jnp.float32) * kept, axis=1, keepdims=True)
    at_end = lax.broadcasted_iota(jnp.int32, (head_count, BLOCK), 1) == BLOCK - 1
    total = jnp.sum(leaving, axis=1, keepdims=True) + kept
    d_run = d_run - leaving + jnp.where(at_end, total, 0.0)
    d_log = running_sum(d_run, reverse=True)
    d_dt[...] = d_log * rate[...] + head_sums(values * d_fed, marks[...])
    grad_rate[...] += d_log * (dt_t * rate[...])
    carry[...] = keep_wide * after + dot3(c_rows.T, dy_parts)
    pre_v, sig_v = pre_now[:, :inner], sig[:, :inner]
    d_values = dt_wide * d_fed + skip[...] * dy
    d_pre = d_values * (sig_v * (1.0 + pre_v * (1.0 - sig_v)))
    ext[:BLOCK, :] = d_pre
    place = block * BLOCK + lax.broadcasted_iota(jnp.int32, (BLOCK, 1), 0)
    conv_in = conv_v[...]
    d_conv = taps[CONV - 1 : CONV, :] * d_pre
    grads[CONV - 1 : CONV, :] += jnp.sum(conv_in * d_pre, axis=0, keepdims=True)
    grads[CONV : CONV + 1, :] += jnp.sum(d_pre, axis=0, keepdims=True)
    for ahead in range(1, CONV):
        same = sequence_of(place + ahead, bounds) == seg_col
        moved = jnp.where(same, ext[ahead : ahead + BLOCK, :], 0.0)
        d_conv = d_conv + taps[CONV - 1 - ahead : CONV - ahead, :] * moved
        grads[CONV - 1 - ahead : CONV - ahead, :] += jnp.sum(conv_in * moved, axis=0, keepdims=True)
    ext[BLOCK:, :] = ext[:TAIL, :]
    d_cols[:, inner:] = d_conv.astype(jnp.bfloat16)

    @pl.when(step == blocks - 1)
    def _():
        everything = pl.ds(0, bc_sum.shape[2])
        for turn in range(blocks - lag, blocks):
            add_wide(turn)
        for turn in hops:
            if 2 * turn >= blocks:
                hop(turn)
        end()
        here = pltpu.make_async_copy(late_rows.at[:, shard], home.at[:, :, lanes], local_sem)
        here.start()
        for turn in range(1, lines):
            push_line(turn, everything).wait()
        found = bc_sum[z]
        for turn in range(1, lines):
            found = found + bc_in[turn - 1]
        d_bc[...] = found
        for turn in range(1, shards):
            push_home(turn, pl.ds(0, half)).wait()
        here.wait()
        for turn in range(blocks):
            for hop_x in range(1, columns):
                push_wide(turn, hop_x).wait_send()


def mixer_forward(shards, bounds, slots, rows_in, weight, taps, bias, dt_bias, rate, skip, cot_own):
    blocks, _, width = rows_in.shape
    columns = grid_columns(shards)
    total, inner, kept = blocks * BLOCK, INNER // shards, weight.shape[0]
    heads = inner // HDIM
    f32, bf16, any_space = jnp.float32, jnp.bfloat16, pl.BlockSpec(memory_space=pl.ANY)

    def block_of(lanes):
        return pl.BlockSpec((BLOCK, lanes), lambda i: (i, 0))

    return pl.pallas_call(
        functools.partial(forward_kernel, heads, shards, columns),
        grid=(blocks,),
        in_specs=[
            pl.BlockSpec(memory_space=pltpu.SMEM),
            pl.BlockSpec((1, 1, BLOCK), lambda i: (i, 0, 0)),
            pl.BlockSpec((1, BLOCK, width), lambda i: (i, 0, 0)),
            whole(weight.shape),
            whole(taps.shape),
            whole(bias.shape),
            whole(dt_bias.shape),
            whole(rate.shape),
            whole(skip.shape),
            any_space,
        ],
        out_specs=[
            block_of(width),
            block_of(kept),
            block_of(inner + SHARED),
            block_of(inner),
            pl.BlockSpec((1, STATE, inner), lambda i: (i, 0, 0)),
            block_of(128),
            block_of(128),
            any_space,
        ],
        out_shape=[
            jax.ShapeDtypeStruct((total, width), bf16),
            jax.ShapeDtypeStruct((total, kept), f32),
            jax.ShapeDtypeStruct((total, inner + SHARED), f32),
            jax.ShapeDtypeStruct((total, inner), f32),
            jax.ShapeDtypeStruct((blocks, STATE, inner), f32),
            jax.ShapeDtypeStruct((total, 128), f32),
            jax.ShapeDtypeStruct((total, 128), f32),
            jax.ShapeDtypeStruct((cot_own.shape[0], shards) + cot_own.shape[1:], bf16),
        ],
        scratch_shapes=[
            pltpu.VMEM((BLOCK + TAIL, inner + SHARED), f32),
            pltpu.VMEM((STATE, inner), f32),
            *gather_semaphores(shards, columns),
        ],
        compiler_params=pltpu.CompilerParams(
            collective_id=2, has_side_effects=True, vmem_limit_bytes=56 * 1024 * 1024
        ),
        cost_estimate=pl.CostEstimate(flops=0, bytes_accessed=300_000_000, transcendentals=0),
        name="mixer_forward",
    )(bounds, slots, rows_in, weight, taps, bias, dt_bias, rate, skip, cot_own)


def pack_cotangent(shards, slots, rows_in, weight, mixed, projected, gain):
    blocks, _, width = rows_in.shape
    total, inner = mixed.shape
    several = 2

    def block_of(lanes):
        return pl.BlockSpec((several * BLOCK, lanes), lambda i: (i, 0))

    return pl.pallas_call(
        functools.partial(cotangent_kernel, shards),
        grid=(blocks // several,),
        in_specs=[
            pl.BlockSpec((several, 1, BLOCK), lambda i: (i, 0, 0)),
            pl.BlockSpec((several, BLOCK, width), lambda i: (i, 0, 0)),
            whole(weight.shape),
            block_of(inner),
            block_of(inner),
            whole(gain.shape),
        ],
        out_specs=[block_of(width), block_of(inner), whole((8, total))],
        out_shape=[
            jax.ShapeDtypeStruct((total, width), jnp.bfloat16),
            jax.ShapeDtypeStruct((total, inner), jnp.float32),
            jax.ShapeDtypeStruct((8, total), jnp.float32),
        ],
        scratch_shapes=[
            pltpu.VMEM((8, total), jnp.float32),
            pltpu.VMEM((shards - 1, 8, total), jnp.float32),
            pltpu.SemaphoreType.DMA((shards,)),
            pltpu.SemaphoreType.DMA((shards,)),
        ],
        compiler_params=pltpu.CompilerParams(
            collective_id=5, has_side_effects=True, vmem_limit_bytes=48 * 1024 * 1024
        ),
        cost_estimate=pl.CostEstimate(flops=0, bytes_accessed=60_000_000, transcendentals=0),
        name="pack_cotangent",
    )(slots, rows_in, weight, mixed, projected, gain)


def mixer_backward(
    shards, bounds, slots, pre, mixed, projected, d_out, sums, states, dt_cols, taps, rate, skip, gain, out_own
):
    total, inner = d_out.shape
    heads, blocks, padded = inner // HDIM, total // BLOCK, rate.shape[0]
    shared = SHARED // shards
    columns = grid_columns(shards)
    marks = (jnp.arange(padded)[:, None] == jnp.arange(inner)[None, :] // HDIM).astype(jnp.bfloat16)

    def block_of(width, column):
        return pl.BlockSpec((BLOCK, width), lambda i: (blocks - 1 - i, column))

    return pl.pallas_call(
        functools.partial(backward_kernel, heads, blocks, shards, columns),
        grid_spec=pltpu.PrefetchScalarGridSpec(
            num_scalar_prefetch=0,
            grid=(blocks,),
            in_specs=[
                pl.BlockSpec(memory_space=pltpu.SMEM),
                pl.BlockSpec((1, 1, BLOCK), lambda i: (blocks - 1 - i, 0, 0)),
                block_of(inner + SHARED, 0),
                block_of(inner, 0),
                block_of(inner, 0),
                block_of(inner, 0),
                block_of(inner, 1),
                pl.BlockSpec((8, BLOCK), lambda i: (0, blocks - 1 - i)),
                pl.BlockSpec((1, STATE, inner), lambda i: (blocks - 1 - i, 0, 0)),
                block_of(dt_cols.shape[1], 0),
                whole(taps.shape),
                whole(rate.shape),
                whole(skip.shape),
                whole(gain.shape),
                whole(marks.shape),
                pl.BlockSpec(memory_space=pl.ANY),
            ],
            out_specs=[
                block_of(2 * inner, 0),
                whole((shared, total)),
                pl.BlockSpec((padded, BLOCK), lambda i: (0, blocks - 1 - i)),
                whole((8, inner)),
                whole((padded, BLOCK)),
                pl.BlockSpec((1, shards, BLOCK // shards, inner), lambda i: (blocks - 1 - i, 0, 0, 0)),
                pl.BlockSpec(memory_space=pl.ANY),
                pl.BlockSpec(memory_space=pl.ANY),
            ],
            scratch_shapes=[
                pltpu.VMEM((BLOCK + TAIL, inner), jnp.float32),
                pltpu.VMEM((STATE, inner), jnp.float32),
                pltpu.VMEM((shards // columns, columns, shared, total), jnp.float32),
                pltpu.VMEM((max(columns - 1, 1), shards // columns, shared, total), jnp.float32),
                pltpu.VMEM((shards // columns, shared, total), jnp.float32),
                pltpu.VMEM((shards // columns - 1, shared, total), jnp.float32),
                pltpu.VMEM((blocks // 2, shards, BLOCK // shards, inner), jnp.bfloat16),
                pltpu.SemaphoreType.DMA((max(columns - 1, 1), blocks)),
                pltpu.SemaphoreType.DMA((max(columns - 1, 1), blocks)),
                pltpu.SemaphoreType.DMA((shards,)),
                pltpu.SemaphoreType.DMA((shards,)),
                pltpu.SemaphoreType.DMA((shards,)),
                pltpu.SemaphoreType.DMA((shards,)),
                pltpu.SemaphoreType.DMA,
                *gather_semaphores(shards, columns),
            ],
        ),
        out_shape=[
            jax.ShapeDtypeStruct((total, 2 * inner), jnp.bfloat16),
            jax.ShapeDtypeStruct((shared, total), jnp.float32),
            jax.ShapeDtypeStruct((padded, total), jnp.float32),
            jax.ShapeDtypeStruct((8, inner), jnp.float32),
            jax.ShapeDtypeStruct((padded, BLOCK), jnp.float32),
            jax.ShapeDtypeStruct((blocks, shards, BLOCK // shards, inner), jnp.bfloat16),
            jax.ShapeDtypeStruct((blocks // 2, BLOCK // shards, INNER), jnp.bfloat16),
            jax.ShapeDtypeStruct((out_own.shape[0], shards) + out_own.shape[1:], jnp.bfloat16),
        ],
        compiler_params=pltpu.CompilerParams(
            collective_id=3, has_side_effects=True, vmem_limit_bytes=56 * 1024 * 1024
        ),
        cost_estimate=pl.CostEstimate(flops=0, bytes_accessed=200_000_000, transcendentals=0),
        name="mixer_backward",
    )(bounds, slots, pre, mixed, projected, d_out, projected, sums, states, dt_cols, taps, rate, skip, gain, marks, out_own)


def piece_rows(shards, groups):
    chunks = (2 * INNER // shards + SHARED // shards) // CHUNK
    return -(-chunks // groups) * CHUNK


def column_runs(shards, groups):
    inner, width = INNER // shards, (2 * INNER + SHARED + HEADS) // groups
    kept = 2 * inner + SHARED + HEADS
    quarter = kept // groups
    spans = []
    for shard in range(shards):
        spans.append((inner * shard, shard, 0, inner))
        spans.append((INNER + inner * shard, shard, inner, inner))
    spans.append((2 * INNER, None, 2 * inner, SHARED + HEADS))
    runs = []
    for column, shard, row, length in spans:
        while length > 0:
            step = min(length, width - column % width, quarter - row % quarter)
            runs.append((column // width, column % width, shard, row, step))
            column, row, length = column + step, row + step, length - step
    return runs


def front_kernel(
    shards, groups, columns,
    rows_in, gain, cot_in, weight_in, out_in, slot_row, slot_col,
    rows_all, weight_all, out_all, slot_all, cot_own, out_cast, scaled_rows,
    rows_own, weight_own, out_own, slot_own,
    run_send, run_recv, share_send, share_recv, out_send, out_recv, slot_send, slot_recv, local_sem, *gather_sems,
):
    shard, group = lax.axis_index("shard"), lax.axis_index("group")
    lines, rows_y = shards // columns, groups // 2
    y, core = group // 2, group % 2
    mate = y * 2 + 1 - core
    quarter = weight_all.shape[0] // groups
    depth = weight_own.shape[1]
    out_width = out_own.shape[1]
    everyone = []
    for step in range(1, shards * groups):
        other_shard = (shard + step % shards) % shards
        other_group = (group + step // shards) % groups
        everyone.append({"shard": other_shard, "group": other_group})
    barrier_with(everyone)

    count = rows_in.shape[0]
    below = (slot_col[...] < slot_row[...]).astype(jnp.int32).astype(jnp.float32)
    rank = jnp.sum(below, axis=0, keepdims=True).astype(jnp.int32)
    sort = (lax.broadcasted_iota(jnp.int32, (count, count), 0) == rank).astype(jnp.bfloat16)
    value = rows_in[...]
    scale = lax.rsqrt(jnp.sum(value * value, axis=1, keepdims=True) * (1.0 / value.shape[1]) + 1e-05)
    scaled = value * scale
    value = (scaled * gain[...]).astype(jnp.bfloat16)
    rows_own[...] = dots(sort, value, ((1,), (0,))).astype(jnp.bfloat16).reshape(rows_own.shape)
    begin, hop, end = row_gather(shards, columns, rows_own, rows_all, *gather_sems)
    begin()
    slots = slot_row[...]
    high = slots // 256
    both = jnp.where(lax.broadcasted_iota(jnp.int32, (8, count), 0) == 0, high, slots - 256 * high)
    both = dots(both.astype(jnp.float32).astype(jnp.bfloat16), sort, NT)
    slot_own[...] = jnp.broadcast_to(256.0 * both[0:1, :] + both[1:2, :], (8, count)).astype(jnp.int32)
    out_own[...] = out_in[...].astype(jnp.bfloat16)
    weight_own[...] = weight_in[...].astype(jnp.bfloat16)

    def slot_copy(step):
        return remote(slot_own, slot_all.at[shard], slot_send.at[step], slot_recv.at[step], shard=(shard + step) % shards)

    for step in range(1, shards):
        slot_copy(step).start()
    slot_here = pltpu.make_async_copy(slot_own, slot_all.at[shard], local_sem.at[0])
    slot_here.start()

    runs = column_runs(shards, groups)
    lanes = pl.ds(pl.multiple_of(shard * depth, depth), depth)
    jobs = {owner: [] for owner in range(groups)}
    for owner, column, target, row, length in runs:
        for to in range(shards) if target is None else (target,):
            jobs[owner].append((column, to, row, length))

    def run_copy(number, column, to, row, length):
        return remote(
            weight_own.at[pl.ds(column, length)], weight_all.at[pl.ds(row, length), lanes],
            run_send.at[number], run_recv, shard=to, group=row // quarter,
        )

    def each_run(act):
        for owner in range(groups):
            @pl.when(group == owner)
            def _():
                for number, (column, to, row, length) in enumerate(jobs[owner]):
                    if row // quarter == owner:
                        here = shard == to
                        act(number, column, to, row, length, here)
                    else:
                        act(number, column, to, row, length, None)

    def start_run(number, column, to, row, length, here):
        if here is None:
            run_copy(number, column, to, row, length).start()
            return

        @pl.when(here)
        def _():
            pltpu.make_async_copy(weight_own.at[pl.ds(column, length)], weight_all.at[pl.ds(row, length), lanes], run_recv).start()

        @pl.when(jnp.logical_not(here))
        def _():
            run_copy(number, column, to, row, length).start()

    def end_run(number, column, to, row, length, here):
        if here is None:
            run_copy(number, column, to, row, length).wait_send()
            return

        @pl.when(jnp.logical_not(here))
        def _():
            run_copy(number, column, to, row, length).wait_send()

    each_run(start_run)

    def own_part(ref, part):
        if ref is out_all:
            return ref.at[:, pl.ds(pl.multiple_of(part * out_width, out_width), out_width)]
        return ref.at[pl.ds(pl.multiple_of(part * quarter, quarter), quarter)]

    def share(ref, part, sends, recvs, number, peer, first=None):
        source = own_part(ref, part) if first is None else first
        return remote(source, own_part(ref, part), sends.at[number], recvs.at[part], group=peer)

    def share_start(ref, sends, recvs, first=None):
        share(ref, group, sends, recvs, 0, mate, first).start()
        for step in range(1, rows_y):
            share(ref, group, sends, recvs, step, (y + step) % rows_y * 2 + core, first).start()

    def share_pass(ref, sends, recvs):
        for step in range(1, rows_y):
            part = (y + step) % rows_y * 2 + core
            share(ref, part, sends, recvs, step, part).wait_recv()
            share(ref, part, sends, recvs, rows_y - 1 + step, mate).start()

    def share_end(ref, sends, recvs):
        for turn in range(rows_y):
            part = turn * 2 + 1 - core
            share(ref, part, sends, recvs, 0, mate).wait_recv()
        for number in range(2 * rows_y - 1):
            share(ref, group, sends, recvs, number, mate).wait_send()

    out_here = pltpu.make_async_copy(out_own, own_part(out_all, group), local_sem.at[1])
    out_here.start()
    share_start(out_all, out_send, out_recv, out_own)
    out_cast[...] = out_own[...]
    high = scaled.astype(jnp.bfloat16)
    left = scaled - high.astype(jnp.float32)
    mid = left.astype(jnp.bfloat16)
    low = (left - mid.astype(jnp.float32)).astype(jnp.bfloat16)
    plain = ((1,), (0,))
    scaled_rows[...] = dots(sort, high, plain) + (dots(sort, mid, plain) + dots(sort, low, plain))
    cot_own[...] = (
        dots(sort, cot_in[...].astype(jnp.bfloat16), ((1,), (0,))).astype(jnp.bfloat16).reshape(cot_own.shape)
    )

    for step in range(1, lines):
        hop(step)
        if step == 1:
            share_pass(out_all, out_send, out_recv)
            kept = own_part(weight_all, group)
            pltpu.make_async_copy(kept, kept, run_recv).wait()
            share_start(weight_all, share_send, share_recv)
    share_pass(weight_all, share_send, share_recv)

    end()
    out_here.wait()
    share_end(out_all, out_send, out_recv)
    share_end(weight_all, share_send, share_recv)
    each_run(end_run)
    for step in range(1, shards):
        slot_copy(step).wait()
    slot_here.wait()


def front_exchange(shards, groups, rows_in, gain, cot_in, weight_in, out_in, slots):
    columns = grid_columns(shards)
    rows_y = groups // 2
    count, width = rows_in.shape
    blocks, per = shards * count // BLOCK, BLOCK // shards
    kept = 2 * INNER // shards + SHARED + HEADS
    any_space, vmem = pl.BlockSpec(memory_space=pl.ANY), pl.BlockSpec(memory_space=pltpu.VMEM)
    dma, bf16 = pltpu.SemaphoreType.DMA, jnp.bfloat16
    counts = {}
    for owner, _, target, _, _ in column_runs(shards, groups):
        counts[owner] = counts.get(owner, 0) + (shards if target is None else 1)
    return pl.pallas_call(
        functools.partial(front_kernel, shards, groups, columns),
        in_specs=[vmem] * 7,
        out_specs=[any_space] * 4 + [vmem] * 3,
        out_shape=[
            jax.ShapeDtypeStruct((blocks, shards, per, width), bf16),
            jax.ShapeDtypeStruct((kept, width), bf16),
            jax.ShapeDtypeStruct((out_in.shape[0], out_in.shape[1] * groups), bf16),
            jax.ShapeDtypeStruct((shards, 8, count), jnp.int32),
            jax.ShapeDtypeStruct((blocks, per, width), bf16),
            jax.ShapeDtypeStruct(out_in.shape, bf16),
            jax.ShapeDtypeStruct((count, width), jnp.float32),
        ],
        scratch_shapes=[
            pltpu.VMEM((blocks, per, width), bf16),
            pltpu.VMEM(weight_in.shape, bf16),
            pltpu.VMEM(out_in.shape, bf16),
            pltpu.VMEM((8, count), jnp.int32),
            dma((max(counts.values()),)),
            dma,
            dma((2 * rows_y - 1,)),
            dma((groups,)),
            dma((2 * rows_y - 1,)),
            dma((groups,)),
            dma((shards,)),
            dma((shards,)),
            dma((2,)),
            *gather_semaphores(shards, columns),
        ],
        compiler_params=pltpu.CompilerParams(
            collective_id=4, has_side_effects=True, vmem_limit_bytes=48 * 1024 * 1024
        ),
        cost_estimate=pl.CostEstimate(flops=0, bytes_accessed=300_000_000, transcendentals=0),
        name="front_exchange",
    )(rows_in, gain[None, :], cot_in, weight_in, out_in, slots[None, :], slots[:, None])


def unpack_kernel(
    shards, slots, d_cols, d_rest, normed, weight, weight_rest, no_rows,
    partial, grad, home, moved_cols, moved_rest, local_sem, home_send, home_recv,
):
    step = pl.program_id(0)
    shard = lax.axis_index("shard")
    main = d_cols.shape[1]
    per = BLOCK // shards

    def push(turn):
        peer = (shard + turn) % shards
        return remote(no_rows.at[first, peer], home.at[:, :, lanes], home_send.at[turn], home_recv.at[turn], shard=peer)

    first, inner = pl.ds(0, home.shape[0]), no_rows.shape[3]
    lanes = pl.ds(pl.multiple_of(shard * inner, inner), inner)
    here = pltpu.make_async_copy(no_rows.at[first, shard], home.at[:, :, lanes], local_sem)

    @pl.when(step == 0)
    def _():
        barrier_with([{"shard": (shard + turn) % shards} for turn in range(1, shards)])
        for turn in range(1, shards):
            push(turn).start()
        here.start()
        grad[...] = jnp.zeros_like(grad)

    several = d_cols.shape[0] // BLOCK
    for turn in range(several):
        rows = pl.ds(turn * BLOCK, BLOCK)
        place = place_of_rows(slots[turn])
        moved_cols[rows, :] = dots(place, d_cols[rows, :], ((0,), (0,))).astype(jnp.bfloat16)
        moved_rest[rows, :] = dots(place, d_rest[rows, :], ((0,), (0,))).astype(jnp.bfloat16)
    tile = 512
    for lane in range(0, weight.shape[1], tile):
        lanes = pl.ds(lane, tile)
        found = dots(moved_cols[...], weight[:, lanes], ((1,), (0,)))
        found = found + dots(moved_rest[...], weight_rest[:, lanes], ((1,), (0,)))
        for turn in range(several):
            rows = found[turn * BLOCK : (turn + 1) * BLOCK]
            partial[:, turn, :, lanes] = rows.reshape(shards, per, tile)
    grad[:main, :] += dots(d_cols[...], normed[...], ((0,), (0,)))
    grad[main:, :] += dots(d_rest[...], normed[...], ((0,), (0,)))

    @pl.when(step == pl.num_programs(0) - 1)
    def _():
        for turn in range(1, shards):
            push(turn).wait()
        here.wait()


def project_back(slots, d_cols, d_rest, normed, weight, weight_rest, no_rows, shards):
    blocks, width = slots.shape[0], normed.shape[1]
    per, main, rest = BLOCK // shards, d_cols.shape[1], d_rest.shape[1]
    several = 2
    any_space = pl.BlockSpec(memory_space=pl.ANY)

    def block_of(columns):
        return pl.BlockSpec((several * BLOCK, columns), lambda i: (i, 0))

    return pl.pallas_call(
        functools.partial(unpack_kernel, shards),
        grid=(blocks // several,),
        in_specs=[
            pl.BlockSpec((several, 1, BLOCK), lambda i: (i, 0, 0)),
            block_of(main),
            block_of(rest),
            block_of(width),
            pl.BlockSpec((main, width), lambda i: (0, 0)),
            whole(weight_rest.shape),
            any_space,
        ],
        out_specs=[
            pl.BlockSpec((shards, several, per, width), lambda i: (0, i, 0, 0)),
            whole((main + rest, width)),
            any_space,
        ],
        out_shape=[
            jax.ShapeDtypeStruct((shards, blocks, per, width), jnp.float32),
            jax.ShapeDtypeStruct((main + rest, width), jnp.float32),
            jax.ShapeDtypeStruct((blocks // 2, per, INNER), jnp.bfloat16),
        ],
        scratch_shapes=[
            pltpu.VMEM((several * BLOCK, main), jnp.bfloat16),
            pltpu.VMEM((several * BLOCK, rest), jnp.bfloat16),
            pltpu.SemaphoreType.DMA,
            pltpu.SemaphoreType.DMA((shards,)),
            pltpu.SemaphoreType.DMA((shards,)),
        ],
        compiler_params=pltpu.CompilerParams(
            collective_id=6, has_side_effects=True, vmem_limit_bytes=60 * 1024 * 1024
        ),
        cost_estimate=pl.CostEstimate(flops=0, bytes_accessed=90_000_000, transcendentals=0),
        name="project_back",
    )(slots, d_cols, d_rest, normed, weight, weight_rest, no_rows)


def other_place(step, place, count):
    upwards = count - 1 - place
    low = jnp.where(step < upwards, count - 1 - step, step - upwards)
    high = jnp.where(step < place, step, count - 1 - (step - place))
    return jnp.where(2 * place < count, low, high)


def tail_kernel(
    shards, groups, columns, near, direct,
    partial, weight_part, small, scaled_rows,
    rows_out, weight_out, mark_out, small_out, gain_out, core_in, row_in, row_scale_in, small_in, gain_in,
    wide_in, wide_scale, line_in, line_scale,
    held, coded, scales, line_coded, line_scales, got, got_scale, marks, total, other, send_rows, send_scales, row_got, row_scale_got, deal_rows, deal_scales, small_sum, small_got,
    gain_sum, gain_part,
    load_sem, wide_send, wide_recv, line_send, line_recv, core_send, core_recv, row_send, row_recv,
    deal_send, deal_recv, mark_send, mark_recv, small_send, small_recv, gain_send, gain_recv,
):
    shard, group = lax.axis_index("shard"), lax.axis_index("group")
    lines = shards // columns
    rows_y = groups // 2
    z, x = shard // columns, shard % columns
    y, core = group // 2, group % 2
    count = held.shape[0]
    owned, depth = weight_out.shape
    piece, chunk = total.shape[0], CHUNK
    inner, shared = INNER // shards, SHARED // shards

    def load(src, dst):
        copy = pltpu.make_async_copy(src, dst, load_sem)
        copy.start()
        copy.wait()

    shard_peers = [(shard + step) % shards for step in range(1, shards)]
    group_peers = [(group + step) % groups for step in range(1, groups)]
    if direct:
        barrier_with(
            [
                {"shard": (shard + step % shards) % shards, "group": (group + step // shards) % groups}
                for step in range(1, shards * groups)
            ]
        )
    else:
        barrier_with([{"shard": peer} for peer in shard_peers] + [{"group": peer} for peer in group_peers])

    mate = y * 2 + 1 - core

    def core_copy(turn):
        return remote(piece_of(turn * 2 + 1 - core), core_in.at[turn], core_send.at[turn], core_recv.at[turn], group=mate)

    def piece_of(owner):
        return weight_part.at[pl.ds(pl.multiple_of(owner * piece, piece), piece)]

    for turn in range(rows_y if direct else 0):
        core_copy(turn).start()

    def small_copy(step):
        return remote(small, small_in.at[step - 1], small_send.at[step - 1], small_recv.at[step - 1], group=(group + step) % groups)

    for step in range(1, groups):
        small_copy(step).start()

    def code(coded_to, scales_to, values=held, lot=32):
        @pl.loop(0, values.shape[0] // lot, unroll=2)
        def _(turn):
            rows = pl.ds(pl.multiple_of(turn * lot, lot), lot)
            value = values[rows, :]
            most = jnp.maximum(jnp.max(jnp.abs(value), axis=1, keepdims=True), 1e-30)
            coded_to[rows, :] = jnp.round(value * (32767.0 / most)).astype(jnp.int32).astype(jnp.int16)
            marks[rows, :] = jnp.broadcast_to(most * (1.0 / 32767.0), (lot, 128))

        scales_to[...] = marks[: scales_to.shape[1], :].T[:8, :]

    def add(coded_from, scales_from):
        if not near:
            load(coded_from, got)
            load(scales_from, got_scale)
            coded_from, scales_from = got, got_scale
        marks[:count, :] = jnp.broadcast_to(scales_from[0:1, :], (128, count)).T

        @pl.loop(0, count // 32, unroll=2)
        def _(turn):
            rows = pl.ds(pl.multiple_of(turn * 32, 32), 32)
            held[rows, :] += coded_from[rows, :].astype(jnp.float32) * marks[rows, 0:1]

    def place_of(step):
        return other_place(step, z, lines) if step < lines - 1 else z

    def wide_copies(step, hop):
        at = (hop - 1) * lines + step
        peer = z * columns + (x + hop) % columns
        target = place_of(step)
        return (
            remote(coded.at[step], wide_in.at[hop - 1, target], wide_send.at[0, at], wide_recv.at[0, at], shard=peer),
            remote(scales.at[step], wide_scale.at[hop - 1, target], wide_send.at[1, at], wide_recv.at[1, at], shard=peer),
        )

    def send_wide(hop, steps):
        for step in steps:
            if hop > 1:
                for copy in wide_copies(step, hop - 1):
                    copy.wait_send()
            load(partial.at[place_of(step) * columns + (x + hop) % columns], held)
            code(coded.at[step], scales.at[step])
            for copy in wide_copies(step, hop):
                copy.start()

    def row_copies(step):
        peer = (y + step) % rows_y * 2 + core
        return (
            remote(send_rows.at[step - 1], row_in.at[step - 1], row_send.at[0, step - 1], row_recv.at[0, step - 1], group=peer),
            remote(send_scales.at[step - 1], row_scale_in.at[step - 1], row_send.at[1, step - 1], row_recv.at[1, step - 1], group=peer),
        )

    def core_sum(turn):
        load(piece_of(turn * 2 + core), total)
        load(core_in.at[turn], other)

        @pl.loop(0, piece // chunk)
        def _(turn):
            rows = pl.ds(pl.multiple_of(turn * chunk, chunk), chunk)
            total[rows, :] += other[rows, :]

    if columns > 1:
        send_wide(1, range(0, 1))
    if direct:
        for turn in range(rows_y):
            core_copy(turn).wait_recv()
        for step in range(1, rows_y):
            core_sum((y + step) % rows_y)
            code(send_rows.at[step - 1], send_scales.at[step - 1], total, chunk)
            for copy in row_copies(step):
                copy.start()
        core_sum(y)
    if columns > 1:
        send_wide(1, range(1, lines))
    for hop in range(2, columns):
        send_wide(hop, range(lines))

    load(small, small_sum)
    for step in range(1, groups):
        small_copy(step).wait_recv()
        load(small_in.at[step - 1], small_got)
        small_sum[...] += small_got[...]

    def small_deal(step):
        return remote(small_sum, small_out.at[shard], small_send.at[groups + step], small_recv.at[groups + step], shard=(shard + step) % shards)

    for step in range(1, shards):
        small_deal(step).start()
    load(small_sum, small_out.at[shard])

    def line_copies(step):
        target = place_of(step)
        way = jnp.where(target > z, 0, 1)
        peer = jnp.where(target > z, z + 1, z - 1) * columns + x
        return (
            remote(line_coded.at[step], line_in.at[way, target], line_send.at[0, step], line_recv.at[0, way, target], shard=peer),
            remote(line_scales.at[step], line_scale.at[way, target], line_send.at[1, step], line_recv.at[1, way, target], shard=peer),
        )

    def take(way, target):
        source = jnp.where(way == 0, z - 1, z + 1)
        peer = jnp.clip(source, 0, lines - 1) * columns + x
        remote(line_coded.at[0], line_in.at[way, target], line_send.at[0, 0], line_recv.at[0, way, target], shard=peer).wait_recv()
        remote(line_scales.at[0], line_scale.at[way, target], line_send.at[1, 0], line_recv.at[1, way, target], shard=peer).wait_recv()
        add(line_in.at[way, target], line_scale.at[way, target])

    def gather_wide(step):
        target = place_of(step)
        load(partial.at[target * columns + x], held)
        for hop in range(1, columns):
            for copy in wide_copies(step, hop):
                copy.wait_recv()
            add(wide_in.at[hop - 1, target], wide_scale.at[hop - 1, target])

    def deal_copy(turn, step):
        first = group * piece + turn * chunk
        column = jnp.where(
            first < inner,
            inner * shard + first,
            jnp.where(first < 2 * inner, INNER + inner * shard + first - inner, 2 * INNER + shared * shard + first - 2 * inner),
        )
        owner = jnp.minimum(column // owned, groups - 1)
        peer = (shard + step) % shards
        source = deal_rows.at[
            pl.ds(pl.multiple_of(turn * chunk, chunk), chunk), pl.ds(pl.multiple_of(peer * depth, depth), depth)
        ]
        target = weight_out.at[pl.ds(pl.multiple_of(column - owner * owned, chunk), chunk)]
        real = first < 2 * inner + shared
        here = real & (owner == group) if step == 0 else None
        away = real & (owner != group) if step == 0 else real

        def near_copy():
            return pltpu.make_async_copy(source, target, deal_recv)

        def far():
            return remote(source, target, deal_send.at[turn, step], deal_recv, shard=peer, group=owner)

        return here, near_copy, away, far

    def deal():
        for step in range(1, rows_y):
            for copy in row_copies(step):
                copy.wait_recv()
            load(row_in.at[step - 1], row_got)
            load(row_scale_in.at[step - 1], row_scale_got)
            marks[: row_scale_got.shape[1], :] = jnp.broadcast_to(row_scale_got[0:1, :], (128, row_scale_got.shape[1])).T

            @pl.loop(0, piece // chunk)
            def _(turn):
                rows = pl.ds(pl.multiple_of(turn * chunk, chunk), chunk)
                total[rows, :] += row_got[rows, :].astype(jnp.float32) * marks[rows, 0:1]

        code(deal_rows, deal_scales, total, chunk)
        load(deal_scales, mark_out.at[shard, group])
        for step in range(1, groups):
            mark_copy(step).start()

    def deal_some(part, parts):
        chunks = piece // chunk

        @pl.loop(part * chunks // parts, (part + 1) * chunks // parts)
        def _(turn):
            for step in range(shards):
                here, near_copy, away, far = deal_copy(turn, step)
                if here is not None:
                    pl.when(here)(lambda: near_copy().start())
                pl.when(away)(lambda: far().start())

    def mark_copy(step):
        to = (group + step) % groups
        return remote(deal_scales, mark_out.at[shard, group], mark_send.at[step], mark_recv.at[step], group=to)

    def mark_spread(step):
        to, at = (shard + step) % shards, groups + step
        return remote(mark_out.at[shard], mark_out.at[shard], mark_send.at[at], mark_recv.at[at], shard=to)

    def mark_pass():
        for step in range(1, groups):
            mark_copy(step).wait_recv()
        for step in range(1, shards):
            mark_spread(step).start()

    def deal_end():
        for step in range(1, groups):
            mark_copy(step).wait_send()
        for step in range(1, shards):
            mark_spread(step).wait()

        @pl.when(group == groups - 1)
        def _():
            most = weight_out.at[pl.ds(0, owned - HEADS)]
            pltpu.make_async_copy(most, most, deal_recv).wait()

        @pl.when(group < groups - 1)
        def _():
            pltpu.make_async_copy(weight_out, weight_out, deal_recv).wait()

        @pl.loop(0, piece // chunk)
        def _(turn):
            for step in range(shards):
                _, _, away, far = deal_copy(turn, step)
                pl.when(away)(lambda: far().wait_send())

    for step in range(lines - 1):
        if direct and step == min(1, lines - 2):
            deal()
        target = place_of(step)
        way = jnp.where(target > z, 0, 1)
        gather_wide(step)

        @pl.when(jnp.where(target > z, z > 0, z < lines - 1))
        def _():
            take(way, target)

        code(line_coded.at[step], line_scales.at[step])
        for copy in line_copies(step):
            copy.start()
        if direct and step >= min(1, lines - 2):
            deal_some(step - min(1, lines - 2), lines - 1 - min(1, lines - 2))
    if direct:
        mark_pass()
    gather_wide(lines - 1)

    @pl.when(z > 0)
    def _():
        take(0, z)

    @pl.when(z < lines - 1)
    def _():
        take(1, z)

    rows_out[...] = held[...]
    gain_sum[...] = jnp.zeros_like(gain_sum)

    @pl.loop(0, count // 8)
    def _(turn):
        rows = pl.ds(pl.multiple_of(turn * 8, 8), 8)
        gain_sum[...] += held[rows, :] * scaled_rows[rows, :]

    def gain_copy(step):
        return remote(gain_part, gain_in.at[step - 1], gain_send.at[step - 1], gain_recv.at[step - 1], shard=(shard + step) % shards)

    def gain_deal(step):
        at = shards - 1 + step - 1
        return remote(gain_out, gain_in.at[at], gain_send.at[at], gain_recv.at[at], group=(group + step) % groups)

    lanes = gain_out.shape[1]
    products = jnp.sum(gain_sum[...], axis=0, keepdims=True)
    gain_part[...] = jnp.concatenate([products[:, row * lanes : (row + 1) * lanes] for row in range(8)], axis=0)
    for step in range(1, shards):
        gain_copy(step).start()
    gain_out[...] = gain_part[...]
    for step in range(1, shards):
        gain_copy(step).wait_recv()
        gain_out[...] += gain_in[step - 1]
    for step in range(1, groups):
        gain_deal(step).start()
    for step in range(1, groups):
        gain_deal(step).wait_recv()
    for step in range(1, groups):
        gain_deal(step).wait_send()
    for step in range(1, groups):
        gain_out[...] += gain_in[shards - 1 + step - 1]

    for step in range(1, shards):
        gain_copy(step).wait_send()
        small_deal(step).wait()
    for step in range(1, groups):
        small_copy(step).wait_send()
    if direct:
        deal_end()
        for step in range(1, rows_y):
            for copy in row_copies(step):
                copy.wait_send()
        for turn in range(rows_y):
            core_copy(turn).wait_send()
    for step in range(lines):
        for copy in wide_copies(step, columns - 1) if columns > 1 else ():
            copy.wait_send()
    for step in range(lines - 1):
        for copy in line_copies(step):
            copy.wait_send()


def tail_exchange(shards, groups, partial, weight_part, small, scaled_rows, owned, depth, direct):
    columns = grid_columns(shards)
    lines, rows_y = shards // columns, groups // 2
    count, width = scaled_rows.shape
    piece = piece_rows(shards, groups) if direct else CHUNK
    padded = -(-piece // 128) * 128
    small_shape = small.shape
    coded, scale = (count, width), (8, count)
    any_space, vmem = pl.BlockSpec(memory_space=pl.ANY), pl.BlockSpec(memory_space=pltpu.VMEM)
    f32, i16 = jnp.float32, jnp.int16
    slots = max(columns - 1, 1)
    dma = pltpu.SemaphoreType.DMA
    landing = [
        ((slots, lines) + coded, i16),
        ((slots, lines) + scale, f32),
        ((2, lines) + coded, i16),
        ((2, lines) + scale, f32),
    ]
    near = shards * count * width <= 1 << 22
    out = pl.pallas_call(
        functools.partial(tail_kernel, shards, groups, columns, near, direct),
        in_specs=[any_space, any_space, any_space, vmem],
        out_specs=[vmem, any_space, any_space, any_space, vmem] + [any_space] * 4 + [vmem] + ([] if near else [any_space] * 4),
        out_shape=[
            jax.ShapeDtypeStruct((count, width), f32),
            jax.ShapeDtypeStruct((owned, depth), i16),
            jax.ShapeDtypeStruct((shards, groups, 8, padded), f32),
            jax.ShapeDtypeStruct((shards,) + small_shape, f32),
            jax.ShapeDtypeStruct((8, width // 8), f32),
            jax.ShapeDtypeStruct((rows_y, piece, width), f32),
            jax.ShapeDtypeStruct((max(rows_y - 1, 1), piece, width), i16),
            jax.ShapeDtypeStruct((max(rows_y - 1, 1), 8, padded), f32),
            jax.ShapeDtypeStruct((max(groups - 1, 1),) + small_shape, f32),
            jax.ShapeDtypeStruct((shards - 1 + groups - 1, 8, width // 8), f32),
        ]
        + ([] if near else [jax.ShapeDtypeStruct(*each) for each in landing]),
        scratch_shapes=([pltpu.VMEM(*each) for each in landing] if near else [])
        + [
            pltpu.VMEM((count, width), f32),
            pltpu.VMEM((lines,) + coded, i16),
            pltpu.VMEM((lines,) + scale, f32),
            pltpu.VMEM((lines,) + coded, i16),
            pltpu.VMEM((lines,) + scale, f32),
            pltpu.VMEM((16, 128) if near else coded, i16),
            pltpu.VMEM((8, 128) if near else scale, f32),
            pltpu.VMEM((max(count, padded), 128), f32),
            pltpu.VMEM((piece, width), f32),
            pltpu.VMEM((piece, width), f32),
            pltpu.VMEM((max(rows_y - 1, 1), piece, width), i16),
            pltpu.VMEM((max(rows_y - 1, 1), 8, padded), f32),
            pltpu.VMEM((piece, width), i16),
            pltpu.VMEM((8, padded), f32),
            pltpu.VMEM((piece, width), i16),
            pltpu.VMEM((8, padded), f32),
            pltpu.VMEM(small_shape, f32),
            pltpu.VMEM(small_shape, f32),
            pltpu.VMEM((8, width), f32),
            pltpu.VMEM((8, width // 8), f32),
            dma,
            dma((2, slots * lines)),
            dma((2, slots * lines)),
            dma((2, lines)),
            dma((2, 2, lines)),
            dma((rows_y,)),
            dma((rows_y,)),
            dma((2, max(rows_y - 1, 1))),
            dma((2, max(rows_y - 1, 1))),
            dma((piece // CHUNK, shards)),
            dma,
            dma((shards + groups,)),
            dma((shards + groups,)),
            dma((groups + shards,)),
            dma((groups + shards,)),
            dma((shards + groups,)),
            dma((shards + groups,)),
        ],
        compiler_params=pltpu.CompilerParams(
            collective_id=1, has_side_effects=True, vmem_limit_bytes=60 * 1024 * 1024
        ),
        cost_estimate=pl.CostEstimate(flops=0, bytes_accessed=400_000_000, transcendentals=0),
        name="tail_exchange",
    )(partial, weight_part, small, scaled_rows)
    return out[:5]


def finish_kernel(
    shards, groups, columns,
    slots, d_cols, d_rest, normed, weight, weight_rest, no_rows, out_part, small, scaled_rows,
    rows_out, weight_out, mark_out, small_out, dt_out, gain_out, home, out_full, weight_part,
    core_in, row_in, row_scale_in, small_in, dt_in, gain_in,
    wide_in, wide_scale, line_in, line_scale,
    held, coded, scales, line_coded, line_scales, marks, total, other, send_rows, send_scales, row_got, row_scale_got,
    deal_rows, deal_scales, small_sum, small_got, dt_sum, dt_got, gain_sum, gain_part,
    moved, moved_rest, turned, weight_all, lot, tile, made,
    load_sem, fetch_sem, lot_sem, tile_sem, made_sem, out_sem, out_send, out_recv, out_pass_send, home_sem, home_send, home_recv,
    wide_send, wide_recv, line_send, line_recv, core_send, core_recv, row_send, row_recv,
    deal_send, deal_recv, mark_send, mark_recv, small_send, small_recv, dt_send, dt_recv, gain_send, gain_recv,
):
    shard, group = lax.axis_index("shard"), lax.axis_index("group")
    lines = shards // columns
    rows_y = groups // 2
    z, x = shard // columns, shard % columns
    y, core = group // 2, group % 2
    count = held.shape[0]
    parts = count // scales.shape[2]
    span = count // parts
    owned, depth = weight_out.shape
    piece, chunk = total.shape[0], CHUNK
    inner, shared = INNER // shards, SHARED // shards

    def load(src, dst):
        copy = pltpu.make_async_copy(src, dst, load_sem)
        copy.start()
        copy.wait()

    blocks, main, width = slots.shape[0], d_cols.shape[1], held.shape[1]
    per = BLOCK // shards
    fetch_weight = pltpu.make_async_copy(weight.at[pl.ds(0, main)], weight_all, fetch_sem)
    fetch_weight.start()

    lots = lot_sem.shape[0]

    def fetch_lot(turn):
        rows = pl.ds(turn * (lot.shape[0] // lots), lot.shape[0] // lots)
        return pltpu.make_async_copy(d_cols.at[rows], lot.at[rows], lot_sem.at[turn])

    tile_width = tile.shape[2]

    def fetch_tile(turn):
        lanes = pl.ds(turn * tile_width, tile_width)
        return pltpu.make_async_copy(normed.at[:, lanes], tile.at[turn % 2], tile_sem.at[turn % 2])

    for turn in range(lots):
        fetch_lot(turn).start()
    fetch_tile(0).start()
    barrier_with(
        [
            {"shard": (shard + step % shards) % shards, "group": (group + step // shards) % groups}
            for step in range(1, shards * groups)
        ]
    )

    def push_home(step):
        peer = (shard + step) % shards
        rows = no_rows.at[pl.ds(0, home.shape[0]), peer]
        return remote(rows, home_at, home_send.at[step], home_recv.at[step], shard=peer)

    home_at = home.at[:, :, pl.ds(pl.multiple_of(shard * inner, inner), inner)]

    for step in range(1, shards):
        push_home(step).start()
    home_here = pltpu.make_async_copy(no_rows.at[pl.ds(0, home.shape[0]), shard], home_at, home_sem)
    home_here.start()

    mate = y * 2 + 1 - core

    def core_copy(turn):
        return remote(piece_of(turn * 2 + 1 - core), core_in.at[turn], core_send.at[turn], core_recv.at[turn], group=mate)

    def piece_of(owner):
        return weight_part.at[pl.ds(pl.multiple_of(owner * piece, piece), piece)]

    out_lots, out_width = out_sem.shape[0], out_part.shape[1]
    out_rows = out_part.shape[0] // out_lots

    def out_place(part, turn):
        return out_full.at[pl.ds(turn * out_rows, out_rows), pl.ds(pl.multiple_of(part * out_width, out_width), out_width)]

    def out_here(turn):
        return pltpu.make_async_copy(out_part.at[pl.ds(turn * out_rows, out_rows)], out_place(group, turn), out_sem.at[turn])

    def out_copy(step, turn):
        peer = mate if step == 0 else (y + step) % rows_y * 2 + core
        rows = out_part.at[pl.ds(turn * out_rows, out_rows)]
        return remote(rows, out_place(group, turn), out_send.at[step, turn], out_recv.at[group, turn], group=peer)

    def out_pass(step, turn):
        part = (y + step) % rows_y * 2 + core
        return remote(
            out_place(part, turn), out_place(part, turn), out_pass_send.at[step, turn], out_recv.at[part, turn], group=mate
        )

    def out_from(part, turn):
        rows = out_part.at[pl.ds(turn * out_rows, out_rows)]
        return remote(rows, out_place(part, turn), out_send.at[0, turn], out_recv.at[part, turn], group=mate)

    def out_start(turns):
        for turn in turns:
            for step in range(1, rows_y):
                out_copy(step, turn).start()
            out_copy(0, turn).start()

    def out_forward(turns):
        for turn in turns:
            for step in range(1, rows_y):
                out_from((y + step) % rows_y * 2 + core, turn).wait_recv()
                out_pass(step, turn).start()

    def out_end():
        for turn in range(out_lots):
            for step in range(rows_y):
                out_copy(step, turn).wait_send()
                out_from(step * 2 + 1 - core, turn).wait_recv()
            for step in range(1, rows_y):
                out_pass(step, turn).wait_send()
            out_here(turn).wait()

    half = out_lots // 2
    out_start(range(half))
    for turn in range(out_lots):
        out_here(turn).start()

    for turn in range(blocks):
        if turn * lots % blocks == 0:
            fetch_lot(turn * lots // blocks).wait()
        rows = pl.ds(turn * BLOCK, BLOCK)
        place = place_of_rows(slots[turn])
        cols, rest = lot[rows, :], d_rest[rows, :]
        moved[:, turn] = dots(place, cols, ((0,), (0,))).astype(jnp.bfloat16).reshape(shards, per, main)
        moved_rest[:, turn] = dots(place, rest, ((0,), (0,))).astype(jnp.bfloat16).reshape(shards, per, rest.shape[1])
        turned[:main, rows] = cols.T
        turned[main:, rows] = rest.T
    fetch_weight.wait()

    def fetch(owner):
        cols, rest = moved[owner].reshape(count, main), moved_rest[owner].reshape(count, d_rest.shape[1])
        step = min(512, width)
        for lane in range(0, width, step):
            lanes = pl.ds(lane, step)
            found = dots(cols, weight_all[:, lanes], ((1,), (0,)))
            held[:, lanes] = found + dots(rest, weight_rest[:, lanes], ((1,), (0,)))

    def small_copy(step):
        return remote(small, small_in.at[step - 1], small_send.at[step - 1], small_recv.at[step - 1], group=(group + step) % groups)

    for step in range(1, groups):
        small_copy(step).start()

    def piece_of_rows(half):
        return held.at[pl.ds(half * span, span)]

    def code(coded_to, scales_to, values, lot=32):
        @pl.loop(0, values.shape[0] // lot, unroll=2)
        def _(turn):
            rows = pl.ds(pl.multiple_of(turn * lot, lot), lot)
            value = values[rows, :]
            most = jnp.maximum(jnp.max(jnp.abs(value), axis=1, keepdims=True), 1e-30)
            coded_to[rows, :] = jnp.round(value * (32767.0 / most)).astype(jnp.int32).astype(jnp.int16)
            marks[rows, :] = jnp.broadcast_to(most * (1.0 / 32767.0), (lot, 128))

        scales_to[...] = marks[: scales_to.shape[1], :].T[:8, :]

    def add(sums, coded_from, scales_from):
        marks[:span, :] = jnp.broadcast_to(scales_from[0:1, :], (128, span)).T

        @pl.loop(0, span // 32, unroll=2)
        def _(turn):
            rows = pl.ds(pl.multiple_of(turn * 32, 32), 32)
            sums[rows, :] += coded_from[rows, :].astype(jnp.float32) * marks[rows, 0:1]

    def place_of(step):
        return other_place(step, z, lines) if step < lines - 1 else z

    def wide_copies(step, half, hop):
        own = step * parts + half
        at = (hop - 1) * lines * parts + own
        peer = z * columns + (x + hop) % columns
        spot = place_of(step) * parts + half
        return (
            remote(coded.at[own], wide_in.at[hop - 1, spot], wide_send.at[0, at], wide_recv.at[0, at], shard=peer),
            remote(scales.at[own], wide_scale.at[hop - 1, spot], wide_send.at[1, at], wide_recv.at[1, at], shard=peer),
        )

    def send_wide(hop, steps):
        for step in steps:
            fetch(place_of(step) * columns + (x + hop) % columns)
            for half in range(parts):
                if hop > 1:
                    for copy in wide_copies(step, half, hop - 1):
                        copy.wait_send()
                code(coded.at[step * parts + half], scales.at[step * parts + half], piece_of_rows(half))
                for copy in wide_copies(step, half, hop):
                    copy.start()

    def row_copies(step):
        peer = (y + step) % rows_y * 2 + core
        return (
            remote(send_rows.at[step - 1], row_in.at[step - 1], row_send.at[0, step - 1], row_recv.at[0, step - 1], group=peer),
            remote(send_scales.at[step - 1], row_scale_in.at[step - 1], row_send.at[1, step - 1], row_recv.at[1, step - 1], group=peer),
        )

    def core_sum(turn):
        load(piece_of(turn * 2 + core), total)
        load(core_in.at[turn], other)

        @pl.loop(0, piece // chunk)
        def _(turn):
            rows = pl.ds(pl.multiple_of(turn * chunk, chunk), chunk)
            total[rows, :] += other[rows, :]

    early = min(2, lines)
    if columns > 1:
        send_wide(1, range(early))

    def store_made(turn):
        lanes = pl.ds(turn * tile_width, tile_width)
        return pltpu.make_async_copy(made.at[turn % 2], weight_part.at[:, lanes], made_sem.at[turn % 2])

    tiles = width // tile_width
    for turn in range(tiles):
        fetch_tile(turn).wait()
        if turn + 1 < tiles:
            fetch_tile(turn + 1).start()
        if turn >= 2:
            store_made(turn - 2).wait()
        made[turn % 2] = dots(turned[...], tile[turn % 2], ((1,), (0,)))
        store_made(turn).start()
    for turn in range(max(0, tiles - 2), tiles):
        store_made(turn).wait()
    for turn in range(rows_y):
        core_copy(turn).start()

    dt_own = weight_part.at[pl.ds(main + shared, HEADS // shards)]

    def dt_copy(step):
        return remote(dt_own, dt_in.at[step - 1], dt_send.at[step], dt_recv.at[step], group=(group + step) % groups)

    def dt_deal(step):
        at = groups + step
        peer = (shard + step) % shards
        lanes = pl.ds(pl.multiple_of(peer * depth, depth), depth)
        return remote(dt_sum.at[:, lanes], dt_out.at[shard], dt_send.at[at], dt_recv.at[at], shard=peer)

    for step in range(1, groups):
        dt_copy(step).start()
    if columns > 1:
        send_wide(1, range(early, lines))
    for hop in range(2, columns):
        send_wide(hop, range(lines))
    for turn in range(rows_y):
        core_copy(turn).wait_recv()
    for step in range(1, rows_y):
        core_sum((y + step) % rows_y)
        code(send_rows.at[step - 1], send_scales.at[step - 1], total, chunk)
        for copy in row_copies(step):
            copy.start()
    out_start(range(half, out_lots))
    core_sum(y)

    load(small, small_sum)
    for step in range(1, groups):
        small_copy(step).wait_recv()
        load(small_in.at[step - 1], small_got)
        small_sum[...] += small_got[...]

    def small_deal(step):
        return remote(small_sum, small_out.at[shard], small_send.at[groups + step], small_recv.at[groups + step], shard=(shard + step) % shards)

    load(dt_own, dt_sum)
    for step in range(1, groups):
        dt_copy(step).wait_recv()
        load(dt_in.at[step - 1], dt_got)
        dt_sum[...] += dt_got[...]
    for step in range(1, shards):
        small_deal(step).start()
        dt_deal(step).start()
    load(small_sum, small_out.at[shard])
    load(dt_sum.at[:, pl.ds(pl.multiple_of(shard * depth, depth), depth)], dt_out.at[shard])

    def line_copies(step, half):
        target = place_of(step)
        own = step * parts + half
        peer = jnp.where(target > z, z + 1, z - 1) * columns + x
        spot = jnp.where(target == z - 1, lines, target) * parts + half
        return (
            remote(line_coded.at[own], line_in.at[spot], line_send.at[0, own], line_recv.at[0, spot], shard=peer),
            remote(line_scales.at[own], line_scale.at[spot], line_send.at[1, own], line_recv.at[1, spot], shard=peer),
        )

    def take(way, target, half):
        source = jnp.where(way == 0, z - 1, z + 1)
        peer = jnp.clip(source, 0, lines - 1) * columns + x
        spot = jnp.where((way == 1) & (target == z), lines, target) * parts + half
        remote(line_coded.at[0], line_in.at[spot], line_send.at[0, 0], line_recv.at[0, spot], shard=peer).wait_recv()
        remote(line_scales.at[0], line_scale.at[spot], line_send.at[1, 0], line_recv.at[1, spot], shard=peer).wait_recv()
        add(piece_of_rows(half), line_in.at[spot], line_scale.at[spot])

    def gather_wide(step, half):
        spot = place_of(step) * parts + half
        for hop in range(1, columns):
            for copy in wide_copies(step, half, hop):
                copy.wait_recv()
            add(piece_of_rows(half), wide_in.at[hop - 1, spot], wide_scale.at[hop - 1, spot])

    def deal_copy(turn, step):
        first = group * piece + turn * chunk
        column = jnp.where(
            first < inner,
            inner * shard + first,
            jnp.where(first < 2 * inner, INNER + inner * shard + first - inner, 2 * INNER + shared * shard + first - 2 * inner),
        )
        owner = jnp.minimum(column // owned, groups - 1)
        peer = (shard + step) % shards
        source = deal_rows.at[
            pl.ds(pl.multiple_of(turn * chunk, chunk), chunk), pl.ds(pl.multiple_of(peer * depth, depth), depth)
        ]
        target = weight_out.at[pl.ds(pl.multiple_of(column - owner * owned, chunk), chunk)]
        real = first < 2 * inner + shared
        here = real & (owner == group) if step == 0 else None
        away = real & (owner != group) if step == 0 else real

        def near_copy():
            return pltpu.make_async_copy(source, target, deal_recv)

        def far():
            return remote(source, target, deal_send.at[turn, step], deal_recv, shard=peer, group=owner)

        return here, near_copy, away, far

    def deal():
        for step in range(1, rows_y):
            for copy in row_copies(step):
                copy.wait_recv()
            load(row_in.at[step - 1], row_got)
            load(row_scale_in.at[step - 1], row_scale_got)
            marks[: row_scale_got.shape[1], :] = jnp.broadcast_to(row_scale_got[0:1, :], (128, row_scale_got.shape[1])).T

            @pl.loop(0, piece // chunk)
            def _(turn):
                rows = pl.ds(pl.multiple_of(turn * chunk, chunk), chunk)
                total[rows, :] += row_got[rows, :].astype(jnp.float32) * marks[rows, 0:1]

        code(deal_rows, deal_scales, total, chunk)
        load(deal_scales, mark_out.at[shard, group])
        for step in range(1, groups):
            mark_copy(step).start()

    def deal_some(part, parts):
        chunks = piece // chunk

        @pl.loop(part * chunks // parts, (part + 1) * chunks // parts)
        def _(turn):
            for step in range(shards):
                here, near_copy, away, far = deal_copy(turn, step)
                if here is not None:
                    pl.when(here)(lambda: near_copy().start())
                pl.when(away)(lambda: far().start())

    def mark_copy(step):
        to = (group + step) % groups
        return remote(deal_scales, mark_out.at[shard, group], mark_send.at[step], mark_recv.at[step], group=to)

    def mark_spread(step):
        to, at = (shard + step) % shards, groups + step
        return remote(mark_out.at[shard], mark_out.at[shard], mark_send.at[at], mark_recv.at[at], shard=to)

    def mark_pass():
        for step in range(1, groups):
            mark_copy(step).wait_recv()
        for step in range(1, shards):
            mark_spread(step).start()

    def deal_end():
        for step in range(1, groups):
            mark_copy(step).wait_send()
        for step in range(1, shards):
            mark_spread(step).wait()

        @pl.when(group == groups - 1)
        def _():
            most = weight_out.at[pl.ds(0, owned - HEADS)]
            pltpu.make_async_copy(most, most, deal_recv).wait()

        @pl.when(group < groups - 1)
        def _():
            pltpu.make_async_copy(weight_out, weight_out, deal_recv).wait()

        @pl.loop(0, piece // chunk)
        def _(turn):
            for step in range(shards):
                _, _, away, far = deal_copy(turn, step)
                pl.when(away)(lambda: far().wait_send())

    for step in range(lines - 1):
        if step == min(1, lines - 2):
            deal()
            out_forward(range(half))
        target = place_of(step)
        way = jnp.where(target > z, 0, 1)
        fetch(target * columns + x)
        for half in range(parts):
            gather_wide(step, half)

            @pl.when(jnp.where(target > z, z > 0, z < lines - 1))
            def _():
                take(way, target, half)

            code(line_coded.at[step * parts + half], line_scales.at[step * parts + half], piece_of_rows(half))
            for copy in line_copies(step, half):
                copy.start()
        if step >= min(1, lines - 2):
            deal_some(step - min(1, lines - 2), lines - 1 - min(1, lines - 2))
    mark_pass()
    fetch(z * columns + x)
    for half in range(parts):
        gather_wide(lines - 1, half)

        @pl.when(z > 0)
        def _():
            take(0, z, half)

        @pl.when(z < lines - 1)
        def _():
            take(1, z, half)

    rows_out[...] = held[...]
    gain_sum[...] = jnp.zeros_like(gain_sum)

    @pl.loop(0, count // 8)
    def _(turn):
        rows = pl.ds(pl.multiple_of(turn * 8, 8), 8)
        gain_sum[...] += held[rows, :] * scaled_rows[rows, :]

    def gain_copy(step):
        return remote(gain_part, gain_in.at[step - 1], gain_send.at[step - 1], gain_recv.at[step - 1], shard=(shard + step) % shards)

    def gain_deal(step):
        at = shards - 1 + step - 1
        return remote(gain_out, gain_in.at[at], gain_send.at[at], gain_recv.at[at], group=(group + step) % groups)

    lanes = gain_out.shape[1]
    products = jnp.sum(gain_sum[...], axis=0, keepdims=True)
    gain_part[...] = jnp.concatenate([products[:, row * lanes : (row + 1) * lanes] for row in range(8)], axis=0)
    for step in range(1, shards):
        gain_copy(step).start()
    gain_out[...] = gain_part[...]
    out_forward(range(half, out_lots))
    for step in range(1, shards):
        gain_copy(step).wait_recv()
        gain_out[...] += gain_in[step - 1]
    for step in range(1, groups):
        gain_deal(step).start()
    for step in range(1, groups):
        gain_deal(step).wait_recv()
    for step in range(1, groups):
        gain_deal(step).wait_send()
    for step in range(1, groups):
        gain_out[...] += gain_in[shards - 1 + step - 1]

    for step in range(1, shards):
        gain_copy(step).wait_send()
        small_deal(step).wait()
        dt_deal(step).wait()
        push_home(step).wait()
    home_here.wait()
    for step in range(1, groups):
        small_copy(step).wait_send()
        dt_copy(step).wait_send()
    deal_end()
    out_end()
    for step in range(1, rows_y):
        for copy in row_copies(step):
            copy.wait_send()
    for turn in range(rows_y):
        core_copy(turn).wait_send()
    for half in range(parts):
        for step in range(lines):
            for copy in wide_copies(step, half, columns - 1) if columns > 1 else ():
                copy.wait_send()
        for step in range(lines - 1):
            for copy in line_copies(step, half):
                copy.wait_send()


def finish_exchange(
    shards, groups, slots, d_cols, d_rest, normed, weight, weight_rest, no_rows, out_part, small, scaled_rows, owned, depth
):
    columns = grid_columns(shards)
    lines, rows_y = shards // columns, groups // 2
    count, width = scaled_rows.shape
    blocks, main, rest = slots.shape[0], d_cols.shape[1], d_rest.shape[1]
    total, per, heads = blocks * BLOCK, BLOCK // shards, HEADS // shards
    piece = piece_rows(shards, groups)
    padded = -(-piece // 128) * 128
    small_shape = small.shape
    parts = 2
    coded, scale = (count // parts, width), (8, count // parts)
    any_space, vmem = pl.BlockSpec(memory_space=pl.ANY), pl.BlockSpec(memory_space=pltpu.VMEM)
    f32, i16, bf16 = jnp.float32, jnp.int16, jnp.bfloat16
    hops, turns, others = max(columns - 1, 1), max(rows_y - 1, 1), max(groups - 1, 1)
    lots, tile = 4, 256
    dma = pltpu.SemaphoreType.DMA
    out = pl.pallas_call(
        functools.partial(finish_kernel, shards, groups, columns),
        in_specs=[vmem, any_space, vmem, any_space, any_space, vmem, any_space, any_space, any_space, vmem],
        out_specs=[vmem] + [any_space] * 4 + [vmem] + [any_space] * 8 + [vmem],
        out_shape=[
            jax.ShapeDtypeStruct((count, width), f32),
            jax.ShapeDtypeStruct((owned, depth), i16),
            jax.ShapeDtypeStruct((shards, groups, 8, padded), f32),
            jax.ShapeDtypeStruct((shards,) + small_shape, f32),
            jax.ShapeDtypeStruct((shards, heads, depth), f32),
            jax.ShapeDtypeStruct((8, width // 8), f32),
            jax.ShapeDtypeStruct((blocks // 2, per, INNER), bf16),
            jax.ShapeDtypeStruct((out_part.shape[0], out_part.shape[1] * groups), bf16),
            jax.ShapeDtypeStruct((main + rest, width), f32),
            jax.ShapeDtypeStruct((rows_y, piece, width), f32),
            jax.ShapeDtypeStruct((turns, piece, width), i16),
            jax.ShapeDtypeStruct((turns, 8, padded), f32),
            jax.ShapeDtypeStruct((others,) + small_shape, f32),
            jax.ShapeDtypeStruct((others, heads, width), f32),
            jax.ShapeDtypeStruct((shards - 1 + groups - 1, 8, width // 8), f32),
        ],
        scratch_shapes=[
            pltpu.VMEM((hops, lines * parts) + coded, i16),
            pltpu.VMEM((hops, lines * parts) + scale, f32),
            pltpu.VMEM(((lines + 1) * parts,) + coded, i16),
            pltpu.VMEM(((lines + 1) * parts,) + scale, f32),
            pltpu.VMEM((count, width), f32),
            pltpu.VMEM((lines * parts,) + coded, i16),
            pltpu.VMEM((lines * parts,) + scale, f32),
            pltpu.VMEM(((lines - 1) * parts,) + coded, i16),
            pltpu.VMEM(((lines - 1) * parts,) + scale, f32),
            pltpu.VMEM((max(count, padded), 128), f32),
            pltpu.VMEM((piece, width), f32),
            pltpu.VMEM((piece, width), f32),
            pltpu.VMEM((turns, piece, width), i16),
            pltpu.VMEM((turns, 8, padded), f32),
            pltpu.VMEM((piece, width), i16),
            pltpu.VMEM((8, padded), f32),
            pltpu.VMEM((piece, width), i16),
            pltpu.VMEM((8, padded), f32),
            pltpu.VMEM(small_shape, f32),
            pltpu.VMEM(small_shape, f32),
            pltpu.VMEM((heads, width), f32),
            pltpu.VMEM((heads, width), f32),
            pltpu.VMEM((8, width), f32),
            pltpu.VMEM((8, width // 8), f32),
            pltpu.VMEM((shards, blocks, per, main), bf16),
            pltpu.VMEM((shards, blocks, per, rest), bf16),
            pltpu.VMEM((main + rest, total), bf16),
            pltpu.VMEM((main, width), bf16),
            pltpu.VMEM((total, main), bf16),
            pltpu.VMEM((2, total, tile), bf16),
            pltpu.VMEM((2, main + rest, tile), f32),
            dma,
            dma,
            dma((2,)),
            dma((2,)),
            dma((2,)),
            dma((lots,)),
            dma((rows_y, lots)),
            dma((groups, lots)),
            dma((rows_y, lots)),
            dma,
            dma((shards,)),
            dma((shards,)),
            dma((2, hops * lines * parts)),
            dma((2, hops * lines * parts)),
            dma((2, lines * parts)),
            dma((2, (lines + 1) * parts)),
            dma((rows_y,)),
            dma((rows_y,)),
            dma((2, turns)),
            dma((2, turns)),
            dma((piece // CHUNK, shards)),
            dma,
            dma((shards + groups,)),
            dma((shards + groups,)),
            dma((groups + shards,)),
            dma((groups + shards,)),
            dma((groups + shards,)),
            dma((groups + shards,)),
            dma((shards + groups,)),
            dma((shards + groups,)),
        ],
        compiler_params=pltpu.CompilerParams(
            collective_id=7, has_side_effects=True, vmem_limit_bytes=62 * 1024 * 1024
        ),
        cost_estimate=pl.CostEstimate(flops=0, bytes_accessed=450_000_000, transcendentals=0),
        name="finish_exchange",
    )(slots, d_cols, d_rest, normed, weight, weight_rest, no_rows, out_part, small, scaled_rows)
    return out[:8]


def nesterov(weight, gradient, moment, average, step_rate):
    decayed = gradient + weight_decay * weight
    new_moment = momentum_decay * moment + decayed
    new_weight = weight - step_rate * (decayed + momentum_decay * new_moment)
    new_average = average_decay * average + (1.0 - average_decay) * new_weight
    return (new_moment, new_weight, new_average)


def dot32(a, b, contract=((1,), (0,))):
    return lax.dot_general(a, b, (contract, ((), ())), preferred_element_type=jnp.float32)


def own_slice(value, index, width, axis):
    return lax.dynamic_slice_in_dim(value, index * width, width, axis)


def local(
    tokens,
    cotangent,
    lengths,
    deal_slot,
    in_weight,
    out_weight,
    small_params,
    in_moment,
    out_moment,
    small_moment,
    in_average,
    out_average,
    small_average,
):
    shards, groups = lax.axis_size("shard"), lax.axis_size("group")
    shard, group = lax.axis_index("shard"), lax.axis_index("group")
    rows, width = tokens.shape
    per = rows // shards
    total = rows * shards
    blocks = total // BLOCK
    heads = HEADS // shards
    inner = INNER // shards
    shared = SHARED // shards
    conv_flat, conv_bias, dt_bias, rate_log, skip_gain, norm_gain, pre_gain = unpack(small_params)
    taps = conv_flat.reshape(CONV, XBC)

    cols, depth, sends = in_weight.shape[1], in_weight.shape[0], out_weight.shape[1]
    direct = cols % CHUNK == 0 and depth % 128 == 0 and sends % 128 == 0 and per % CHUNK == 0
    direct = direct and (2 * inner + SHARED + HEADS) % (groups * CHUNK) == 0 and shared % CHUNK == 0
    bounds = jnp.cumsum(lengths[0])[:-1].astype(jnp.int32)
    seg_rows = segment_of(jnp.arange(total, dtype=jnp.int32), lengths[0])

    rank = jnp.sum((deal_slot[None, :] < deal_slot[:, None]).astype(jnp.int32), axis=1)
    sort_mat = (rank[None, :] == jnp.arange(rows)[:, None]).astype(jnp.bfloat16)
    r_in = lax.rsqrt(jnp.mean(tokens * tokens, axis=1, keepdims=True) + eps_norm)
    in_turned = in_weight.T

    if direct:
        x_all, in_low, out_low, slot_all, c_sorted, out_cast, x_scaled = front_exchange(
            shards, groups, tokens, pre_gain, cotangent, in_turned, out_weight, deal_slot
        )
        x_all = x_all.reshape(blocks, BLOCK, width)
        slot_all = slot_all[:, 0, :]
    else:
        sorted_slot = jnp.sum(jnp.where(sort_mat > 0, deal_slot[None, :], 0), axis=1)
        x_scaled = jnp.dot(sort_mat.astype(jnp.float32), tokens * r_in, precision=lax.Precision.HIGHEST)
        normed_low = (tokens * r_in * pre_gain[None, :]).astype(jnp.bfloat16)
        x_sorted = dot32(sort_mat, normed_low).astype(jnp.bfloat16).reshape(blocks, per, width)
        c_sorted = dot32(sort_mat, cotangent.astype(jnp.bfloat16)).astype(jnp.bfloat16)
        c_sorted = c_sorted.reshape(blocks, per, width)
        in_turned = in_turned.astype(jnp.bfloat16)
        out_cast = out_weight.astype(jnp.bfloat16)
        x_all = lax.all_gather(x_sorted, "shard").transpose(1, 0, 2, 3).reshape(blocks, BLOCK, width)
        slot_all = lax.all_gather(sorted_slot, "shard")
        part = depth // groups
        pieces = lax.all_to_all(in_turned.reshape(cols, groups, part), "group", 1, 0)
        pieces = pieces.reshape(groups * cols, part)

        def cut(lo, each):
            return pieces[lo : lo + each * shards].reshape(shards, each, part)

        spread = jnp.broadcast_to(pieces[None, 2 * INNER :], (shards, SHARED + HEADS, part))
        got = jnp.concatenate([cut(0, inner), cut(INNER, inner), spread], axis=1)
        got = lax.all_gather(lax.all_to_all(got, "shard", 0, 0), "group")
        in_low = got.transpose(2, 1, 0, 3).reshape(-1, width)
        out_low = lax.all_gather(out_cast, "group", axis=1, tiled=True)
    slot_blk = slot_all.reshape(shards, blocks, per).transpose(1, 0, 2).reshape(blocks, 1, BLOCK)
    slot_blk = slot_blk - jnp.arange(blocks, dtype=jnp.int32)[:, None, None] * BLOCK

    taps_v = own_slice(taps[:, :INNER], shard, inner, 1)
    taps_all = jnp.concatenate([taps_v, taps[:, INNER:]], axis=1)
    bias_all = jnp.concatenate([own_slice(conv_bias[:INNER], shard, inner, 0), conv_bias[INNER:]])[None, :]
    skip_wide = jnp.repeat(own_slice(skip_gain, shard, heads, 0), HDIM)[None, :]
    gain_own = own_slice(norm_gain, shard, inner, 0)[None, :]
    padding = max(TAIL - heads, 0)
    rate = jnp.pad(-jnp.exp(own_slice(rate_log, shard, heads, 0)), (0, padding))[:, None]
    normed, projected, pre, mixed, states, dt_cols, dt_raw, c_all = mixer_forward(
        shards, bounds, slot_blk, x_all, in_low, taps_all, bias_all, dt_bias[None, :], rate, skip_wide, c_sorted
    )
    conv_bc = lax.dynamic_slice_in_dim(projected, 2 * inner + shard * shared, shared, 1)
    cot_low, d_out, sums = pack_cotangent(
        shards, slot_blk, c_all.reshape(blocks, BLOCK, width), out_low, mixed, projected, gain_own
    )

    r_out = lax.rsqrt(sums[0][:, None] + eps_norm)
    normed_out = (mixed * jax.nn.silu(projected[:, :inner]) * r_out * gain_own).astype(jnp.bfloat16)
    grad_out = dot32(normed_out, cot_low, ((0,), (0,)))
    grad_out, mixed = lax.optimization_barrier((grad_out, mixed))
    grad_out = lax.psum_scatter(grad_out, "group", scatter_dimension=1, tiled=True)
    d_cols, d_bc, d_dt, grads, rate_terms, no_rows, home_late, out_full = mixer_backward(
        shards, bounds, slot_blk, pre, mixed, projected, d_out, sums, states, dt_cols,
        taps_v, rate, skip_wide, gain_own, out_cast[None],
    )
    out_block = out_full.reshape(INNER, -1)

    d_dtraw = d_dt[:heads].T * jax.nn.sigmoid(dt_raw[:, :heads])
    grad_dtb = jnp.sum(d_dtraw, axis=0)
    grad_rate = jnp.sum(rate_terms[:heads], axis=1)
    grad_skip = jnp.sum(grads[6].reshape(heads, HDIM), axis=1)
    _, pull_bc = jax.vjp(
        lambda c, t, b: convolve(c, seg_rows, t, b),
        conv_bc,
        own_slice(taps[:, INNER:], shard, shared, 1),
        own_slice(conv_bias[INNER:], shard, shared, 0),
    )
    d_conv_bc, grad_taps_bc, grad_bias_bc = pull_bc(d_bc.T)
    rest = 128 - shared - heads
    d_rest = jnp.concatenate([d_conv_bc, d_dtraw, jnp.zeros((total, rest), jnp.float32)], axis=1)
    in_rest = jnp.concatenate(
        [
            own_slice(in_low[2 * inner : 2 * inner + SHARED], shard, shared, 0),
            own_slice(in_low[2 * inner + SHARED :], shard, heads, 0),
            jnp.zeros((rest, width), jnp.bfloat16),
        ]
    )

    mine = [
        grads[:CONV].reshape(-1),
        grad_taps_bc.reshape(-1),
        grads[4],
        grad_bias_bc,
        grad_dtb,
        grad_rate,
        grad_skip,
        grads[5],
    ]
    extents = [piece.shape[0] for piece in mine]
    mine = jnp.concatenate(mine)
    mine = jnp.pad(mine, (0, -mine.shape[0] % 1024)).reshape(-1, 128)
    d_rest = d_rest.astype(jnp.bfloat16)
    if direct:
        d_normed, grad_in, grad_marks, small_all, dt_part, gain_all, home, out_full = finish_exchange(
            shards, groups, slot_blk, d_cols, d_rest, normed, in_low, in_rest, no_rows, out_block, mine, x_scaled,
            cols, depth,
        )
    else:
        partial, weight_part, home = project_back(
            slot_blk, d_cols, d_rest, normed, in_low, in_rest, no_rows, shards
        )
        out_full = lax.all_gather(out_block, "group", axis=1, tiled=True)
        d_normed, _, _, small_all, gain_all = tail_exchange(
            shards, groups, partial.reshape(shards, rows, width), weight_part, mine, x_scaled, cols, depth, False
        )

    home = jnp.concatenate([home, home_late], axis=0).reshape(rows, INNER)
    home = dot32(sort_mat, home, ((0,), (0,))).astype(jnp.bfloat16)
    block_out = tokens + dot32(home, out_full)
    d_normed = jnp.dot(sort_mat.T.astype(jnp.float32), d_normed, precision=lax.Precision.HIGHEST)
    d_scaled = pre_gain[None, :] * d_normed
    inside = jnp.mean(tokens * d_scaled, axis=1, keepdims=True)
    input_grad = cotangent + r_in * (d_scaled - tokens * (r_in * r_in) * inside)
    grad_pre = gain_all.reshape(width)

    mine = small_all.reshape(shards, -1)
    found, offset = [], 0
    for extent in extents:
        found.append(mine[:, offset : offset + extent])
        offset = offset + extent
    if direct:
        dt_part = dt_part.reshape(HEADS, depth)
        steps = grad_marks[:, :, 0, : piece_rows(shards, groups)].reshape(shards, -1)
        steps = jnp.concatenate(
            [
                steps[:, :inner].reshape(-1),
                steps[:, inner : 2 * inner].reshape(-1),
                steps[:, 2 * inner : 2 * inner + shared].reshape(-1),
                jnp.zeros((HEADS,), jnp.float32),
            ]
        )
        grad_in = grad_in.astype(jnp.float32) * own_slice(steps, group, cols, 0)[:, None]
        last = jnp.concatenate([grad_in[: cols - HEADS], dt_part])
        grad_in = jnp.where(group == groups - 1, last, grad_in)
    else:
        used = 2 * inner + shared + heads
        grad_in = weight_part[:used].reshape(used, shards, groups, part).transpose(2, 1, 0, 3)
        grad_in = lax.psum_scatter(grad_in, "group", scatter_dimension=0)
        grad_in = lax.all_to_all(grad_in, "shard", 0, 0)

        def join(lo, each):
            return grad_in[:, lo : lo + each].reshape(shards * each, part)

        grad_in = jnp.concatenate(
            [
                join(0, inner),
                join(inner, inner),
                join(2 * inner, shared),
                join(2 * inner + shared, heads),
            ]
        )
        grad_in = lax.all_to_all(grad_in.reshape(groups, cols, part), "group", 0, 0)
        grad_in = grad_in.transpose(1, 0, 2).reshape(cols, depth)

    def taps_of(piece):
        return piece.reshape(shards, CONV, -1).transpose(1, 0, 2).reshape(CONV, -1)

    grad_taps = jnp.concatenate([taps_of(found[0]), taps_of(found[1])], axis=1).reshape(-1)
    grad_small = jnp.concatenate([grad_taps] + [piece.reshape(-1) for piece in found[2:]] + [grad_pre])
    in_new = nesterov(in_weight.T, grad_in, in_moment.T, in_average.T, rate_in)
    in_new = tuple(value.T for value in in_new)
    out_new = nesterov(out_weight, grad_out, out_moment, out_average, rate_out)
    small_new = nesterov(small_params, grad_small, small_moment, small_average, rate_small)
    return (block_out, input_grad) + in_new + out_new + small_new


def solution(mesh):
    rows = P(("group", "shard"), None)
    tile = P("shard", "group")
    return jax.shard_map(
        local,
        mesh=mesh,
        in_specs=(
            rows,
            rows,
            P("group", None),
            P(("group", "shard")),
            tile,
            tile,
            P(),
            tile,
            tile,
            P(),
            tile,
            tile,
            P(),
        ),
        out_specs=(rows, rows, tile, tile, tile, tile, tile, tile, P(), P(), P()),
        check_vma=False,
    )
```

```python
import functools

import jax
import jax.numpy as jnp
from jax import lax
from jax.experimental import pallas as pl
from jax.experimental.pallas import tpu as pltpu
from jax.sharding import PartitionSpec as P

D = 2048
HEADS = 64
HDIM = 64
STATE = 128
CONV = 4
BLOCK = 256
INNER = 4096
XBC = 4352
SHARED = 2 * STATE
TAIL = 8
CHUNK = 16
MESH = pl.DeviceIdType.MESH


eps_norm = 1e-05
momentum_decay = 0.9
weight_decay = 0.01
average_decay = 0.99
rate_in = 0.0001
rate_out = 3e-05
rate_small = 0.001


def unpack(packed_small):
    extents = [CONV * XBC, XBC, HEADS, HEADS, HEADS, INNER, D]
    pieces = []
    offset = 0
    for extent in extents:
        pieces.append(packed_small[offset : offset + extent])
        offset = offset + extent
    return pieces


def segment_of(positions, lengths_row):
    bounds = jnp.cumsum(lengths_row)[:-1]
    inside = jnp.sum((positions[:, None] >= bounds[None, :]).astype(jnp.int32), axis=1)
    return jnp.where(positions < 0, -1, inside)


def convolve(conv_rows, seg_rows, conv_taps, conv_bias):
    row_count, width = conv_rows.shape
    extended = jnp.concatenate([jnp.zeros((CONV - 1, width), conv_rows.dtype), conv_rows], axis=0)
    seg_ext = jnp.concatenate([jnp.full((CONV - 1,), -1, jnp.int32), seg_rows], axis=0)
    conv_sum = jnp.zeros_like(conv_rows) + conv_bias[None, :]
    for tap_index in range(CONV):
        same_seq = (seg_ext[tap_index : tap_index + row_count] == seg_rows)[:, None]
        conv_sum = conv_sum + jnp.where(
            same_seq,
            extended[tap_index : tap_index + row_count] * conv_taps[tap_index][None, :],
            0.0,
        )
    return jax.nn.silu(conv_sum)


def split(value):
    high = value.astype(jnp.bfloat16)
    return high, (value - high.astype(jnp.float32)).astype(jnp.bfloat16)


def dots(a, b, contract):
    return lax.dot_general(a, b, (contract, ((), ())), preferred_element_type=jnp.float32)


def dot3(a, b, contract=((1,), (0,))):
    a = a if isinstance(a, tuple) else split(a)
    b = b if isinstance(b, tuple) else split(b)
    return dots(a[0], b[0], contract) + (dots(a[0], b[1], contract) + dots(a[1], b[0], contract))


NT = ((1,), (1,))


def dot_wide(a, wide):
    high, low = split(a)
    lanes = wide.shape[1] // 2
    plain = ((1,), (0,))
    first = dots(high, wide, plain)
    return first[:, :lanes] + (first[:, lanes:] + dots(low, wide[:, :lanes], plain))


def beside(first, second, own):
    moved = pltpu.roll(second.astype(jnp.float32), HDIM, 1).astype(jnp.bfloat16)
    return jnp.where(own, first, moved)


def head_sums(value, marks):
    high = value.astype(jnp.bfloat16)
    rest = value - high.astype(jnp.float32)
    mid = rest.astype(jnp.bfloat16)
    low = (rest - mid.astype(jnp.float32)).astype(jnp.bfloat16)
    return dots(marks, high, NT) + (dots(marks, mid, NT) + dots(marks, low, NT))


def widen(columns, heads):
    rows = columns.shape[0]
    low_half = lax.broadcasted_iota(jnp.int32, (rows, 2 * HDIM), 1) < HDIM
    return jnp.concatenate(
        [
            jnp.where(low_half, columns[:, h : h + 1], columns[:, h + 1 : h + 2])
            for h in range(0, heads, 2)
        ],
        axis=1,
    )


def running_sum(value, reverse=False):
    lane = lax.broadcasted_iota(jnp.int32, value.shape, 1)
    count = value.shape[1]
    step = 1
    while step < count:
        if reverse:
            value = value + jnp.where(lane < count - step, pltpu.roll(value, count - step, 1), 0.0)
        else:
            value = value + jnp.where(lane >= step, pltpu.roll(value, step, 1), 0.0)
        step *= 2
    return value


def sequence_of(positions, bounds):
    inside = jnp.where(positions >= bounds[0], 1, 0) + jnp.where(positions >= bounds[1], 1, 0)
    return jnp.where(positions < 0, -1, inside)


def block_facts(block, bounds, dt_t, rate):
    start = block * BLOCK
    seg_col = sequence_of(start + lax.broadcasted_iota(jnp.int32, (BLOCK, 1), 0), bounds)
    seg_row = sequence_of(start + lax.broadcasted_iota(jnp.int32, (1, BLOCK), 1), bounds)
    before = sequence_of(start - 1 + lax.broadcasted_iota(jnp.int32, (1, 1), 1), bounds)
    last = sequence_of(start + BLOCK - 1 + lax.broadcasted_iota(jnp.int32, (1, 1), 1), bounds)
    run_t = running_sum(dt_t * rate)
    run = run_t.T
    final = run[BLOCK - 1 :, :]
    carried = jnp.where(seg_col == before, jnp.exp(run), 0.0)
    tail = jnp.where(seg_col == last, jnp.exp(final - run), 0.0)
    keep = jnp.where(last == before, jnp.exp(final), 0.0)
    return seg_col, seg_row, run_t, run, carried, tail, keep


def barrier_with(peers):
    barrier = pltpu.get_barrier_semaphore()
    for peer in peers:
        pl.semaphore_signal(barrier, inc=1, device_id=peer, device_id_type=MESH)
    pl.semaphore_wait(barrier, len(peers))


def remote(src, dst, sends, recvs, **where):
    return pltpu.make_async_remote_copy(
        src_ref=src, dst_ref=dst, send_sem=sends, recv_sem=recvs, device_id=where, device_id_type=MESH
    )


def place_of_rows(slots):
    count = slots.shape[1]
    return (lax.broadcasted_iota(jnp.int32, (BLOCK, count), 0) == slots).astype(jnp.bfloat16)


def grid_columns(shards):
    columns = 1
    while 2 * (2 * columns) * (2 * columns) <= shards:
        columns *= 2
    return columns if shards % columns == 0 else 1


def whole(shape):
    return pl.BlockSpec(shape, lambda *_: (0,) * len(shape))


def row_gather(shards, columns, own, gathered, local_sem, sends, recvs):
    shard = lax.axis_index("shard")
    lines = shards // columns
    z, x = shard // columns, shard % columns

    def line_copy(source, way, first=False):
        at = source * columns + x
        peer = jnp.clip(z + 1 - 2 * way, 0, lines - 1) * columns + x
        rows = own if first else gathered.at[:, at]
        return remote(rows, gathered.at[:, at], sends.at[way, source], recvs.at[at], shard=peer)

    def wide_copy(source, hop, first=False):
        at = source * columns + x
        peer = z * columns + (x + hop) % columns
        rows = own if first else gathered.at[:, at]
        return remote(rows, gathered.at[:, at], sends.at[1 + hop, source], recvs.at[at], shard=peer)

    def pass_on(source, ways, first=False):
        for way in ways:
            @pl.when(z < lines - 1 if way == 0 else z > 0)
            def _():
                line_copy(source, way, first).start()

        for hop in range(1, columns):
            wide_copy(source, hop, first).start()

    here = pltpu.make_async_copy(own, gathered.at[:, shard], local_sem)

    def begin():
        pass_on(z, (0, 1), True)
        here.start()

    def hop(step):
        @pl.when(z - step >= 0)
        def _():
            line_copy(z - step, 0).wait_recv()
            pass_on(z - step, (0,))

        @pl.when(z + step < lines)
        def _():
            line_copy(z + step, 1).wait_recv()
            pass_on(z + step, (1,))

    def end():
        here.wait()
        for step in range(1, columns):
            peer = z * columns + (x + step) % columns
            for source in range(lines):
                at = source * columns + (x + step) % columns
                remote(gathered.at[:, at], gathered.at[:, at], sends.at[1 + step, source], recvs.at[at], shard=peer).wait_recv()
        for source in range(lines):
            for step in range(1, columns):
                wide_copy(source, step).wait_send()

            @pl.when((z < lines - 1) & (source <= z))
            def _():
                line_copy(source, 0).wait_send()

            @pl.when((z > 0) & (source >= z))
            def _():
                line_copy(source, 1).wait_send()

    return begin, hop, end


def gather_semaphores(shards, columns):
    dma = pltpu.SemaphoreType.DMA
    return [
        dma,
        dma((1 + columns, shards // columns)),
        dma((shards,)),
    ]


def softplus(value):
    small = jnp.exp(-jnp.abs(value))
    ratio = small / (2.0 + small)
    square = ratio * ratio
    series = jnp.full_like(value, 1.0 / 15.0)
    for power in (13, 11, 9, 7, 5, 3, 1):
        series = series * square + 1.0 / power
    return jnp.maximum(value, 0.0) + 2.0 * ratio * series


def pick_columns(value, marks):
    high = value.astype(jnp.bfloat16)
    rest = value - high.astype(jnp.float32)
    mid = rest.astype(jnp.bfloat16)
    low = (rest - mid.astype(jnp.float32)).astype(jnp.bfloat16)
    plain = ((1,), (0,))
    return dots(high, marks, plain) + (dots(mid, marks, plain) + dots(low, marks, plain))


def forward_kernel(
    heads, shards, columns, bounds, slots, rows_in, weight, taps, bias, dt_bias, rate, skip, cot_own,
    packed, product, pre_out, mixed_out, state_out, dt_out, raw_out, cot_all,
    ext, state, *gather_sems,
):
    block = pl.program_id(0)
    blocks = cot_own.shape[0]
    inner = heads * HDIM
    shard = lax.axis_index("shard")
    begin, hop, end = row_gather(shards, columns, cot_own, cot_all, *gather_sems)
    hops = range(1, shards // columns)

    @pl.when(block == 0)
    def _():
        barrier_with([{"shard": (shard + step) % shards} for step in range(1, shards)])
        begin()
        ext[:TAIL, :] = jnp.zeros((TAIL, ext.shape[1]), jnp.float32)
        state[...] = jnp.zeros_like(state)

    for step in hops:
        if (7 * step + 1) // 2 < blocks:
            pl.when(block == (7 * step + 1) // 2)(functools.partial(hop, step))

    normed = dots(place_of_rows(slots[0]), rows_in[0], ((1,), (0,))).astype(jnp.bfloat16)
    packed[...] = normed
    product[...] = dots(normed, weight[...], NT)
    head = lax.broadcasted_iota(jnp.int32, (HEADS, 128), 0)
    lane = lax.broadcasted_iota(jnp.int32, (HEADS, 128), 1)
    marks = ((head == shard * heads + lane) & (lane < heads)).astype(jnp.bfloat16)
    raw = pick_columns(product[:, 2 * inner + SHARED :] + dt_bias[...], marks)
    raw_out[...] = raw
    dt = softplus(raw)
    dt_out[...] = dt

    bounds = (bounds[0], bounds[1])
    dt_t = dt.T[: rate.shape[0], :]
    seg_col, seg_row, run_t, run, carried, tail, keep = block_facts(block, bounds, dt_t, rate[...])
    ext[TAIL:, :] = product[:, inner : 2 * inner + SHARED]
    place = block * BLOCK + lax.broadcasted_iota(jnp.int32, (BLOCK, 1), 0)
    pre = bias[...] + taps[CONV - 1 : CONV, :] * ext[TAIL:, :]
    for back in range(1, CONV):
        same = sequence_of(place - back, bounds) == seg_col
        moved = ext[TAIL - back : TAIL - back + BLOCK, :]
        pre = pre + jnp.where(same, moved, 0.0) * taps[CONV - 1 - back : CONV - back, :]
    ext[:TAIL, :] = ext[BLOCK:, :]
    pre_out[...] = pre
    conv = pre / (1.0 + jnp.exp(-pre))
    values, b_rows, c_rows = conv[:, :inner], conv[:, inner : inner + STATE], conv[:, inner + STATE :]
    fed = values * widen(dt, heads)
    rows = lax.broadcasted_iota(jnp.int32, (BLOCK, BLOCK), 0)
    cols = lax.broadcasted_iota(jnp.int32, (BLOCK, BLOCK), 1)
    allowed = (seg_col == seg_row) & (rows >= cols)
    b_parts, c_parts = split(b_rows), split(c_rows)
    scores = jnp.where(allowed, dot3(c_parts, b_parts, NT), 0.0)
    old = state[...]
    state_out[0] = old
    output = widen(carried, heads) * dot3(c_parts, old)
    low_half = lax.broadcasted_iota(jnp.int32, (BLOCK, 2 * HDIM), 1) < HDIM
    inside = []
    for h in range(0, heads, 2):
        pair = jnp.concatenate(split(fed[:, h * HDIM : (h + 2) * HDIM]), axis=1)
        found = []
        for k in (h, h + 1):
            mixing = jnp.exp(jnp.minimum(run[:, k : k + 1] - run_t[k : k + 1, :], 0.0)) * scores
            found.append(dot_wide(mixing, pair))
        inside.append(jnp.where(low_half, found[0], found[1]))
    mixed = output + jnp.concatenate(inside, axis=1) + skip[...] * values
    mixed_out[...] = mixed
    state[...] = widen(keep, heads) * old + dot3(b_rows.T, widen(tail, heads) * fed)

    @pl.when(block == blocks - 1)
    def _():
        for step in hops:
            if (7 * step + 1) // 2 >= blocks:
                hop(step)
        end()


def cotangent_kernel(
    shards, slots, rows_in, weight, mixed, gate, gain,
    packed, product, sums_out, own_sums, sums_in, sums_send, sums_recv,
):
    block = pl.program_id(0)
    shard = lax.axis_index("shard")

    @pl.when(block == 0)
    def _():
        barrier_with([{"shard": (shard + step) % shards} for step in range(1, shards)])

    several = rows_in.shape[0]
    for turn in range(several):
        rows = pl.ds(turn * BLOCK, BLOCK)
        packed[rows, :] = dots(place_of_rows(slots[turn]), rows_in[turn], ((1,), (0,))).astype(jnp.bfloat16)
    d_out = dots(packed[...], weight[...], NT)
    product[...] = d_out
    gate_now = gate[...]
    gated = mixed[...] * (gate_now / (1.0 + jnp.exp(-gate_now)))
    squares = jnp.sum(gated * gated, axis=1, keepdims=True)
    products = jnp.sum(gated * gain[...] * d_out, axis=1, keepdims=True)
    lane = lax.broadcasted_iota(jnp.int32, (several * BLOCK, 128), 1)
    both = jnp.where(lane == 0, squares, jnp.where(lane == 1, products, 0.0))
    here = pl.ds(pl.multiple_of(block * several * BLOCK, BLOCK), several * BLOCK)
    own_sums[:, here] = both.T[:8, :]

    def push(step, at):
        return remote(
            own_sums.at[:, at], sums_in.at[step - 1, :, at], sums_send.at[step], sums_recv.at[step],
            shard=(shard + step) % shards,
        )

    for step in range(1, shards):
        push(step, here).start()

    @pl.when(block == pl.num_programs(0) - 1)
    def _():
        everything = pl.ds(0, own_sums.shape[1])
        for step in range(1, shards):
            push(step, everything).wait()
        found = own_sums[...]
        for step in range(1, shards):
            found = found + sums_in[step - 1]
        sums_out[...] = found * (1.0 / INNER)


def backward_kernel(
    heads, blocks, shards, columns, bounds, slots, pre, mixed, gate, d_out, conv_v, sums, state_in, dt_cols,
    taps, rate, skip, gain, marks, out_own,
    d_cols, d_bc, d_dt, grads, grad_rate, no_rows, out_all,
    ext, carry, bc_rows, bc_wide, bc_sum, bc_in, wide_send, wide_recv, bc_send, bc_recv, *gather_sems,
):
    step = pl.program_id(0)
    block = blocks - 1 - step
    inner = heads * HDIM
    shard = lax.axis_index("shard")
    shared = SHARED // shards
    lines = shards // columns
    z, x = shard // columns, shard % columns
    begin, hop, end = row_gather(shards, columns, out_own, out_all, *gather_sems)
    hops = range(1, shards // columns)

    @pl.when(step == 0)
    def _():
        barrier_with([{"shard": (shard + turn) % shards} for turn in range(1, shards)])
        begin()
        ext[BLOCK:, :] = jnp.zeros((TAIL, ext.shape[1]), jnp.float32)
        carry[...] = jnp.zeros_like(carry)
        grads[...] = jnp.zeros_like(grads)
        grad_rate[...] = jnp.zeros_like(grad_rate)

    for turn in hops:
        if 2 * turn < blocks:
            pl.when(step == 2 * turn)(functools.partial(hop, turn))

    bounds = (bounds[0], bounds[1])
    dt = dt_cols[...]
    dt_t = dt.T[: rate.shape[0], :]
    seg_col, seg_row, run_t, run, carried, tail, keep = block_facts(block, bounds, dt_t, rate[...])
    sums_cols = sums[...].T
    r_out = lax.rsqrt(sums_cols[:, 0:1] + 1e-05)
    inside = sums_cols[:, 1:2]
    gate_now = gate[...]
    gate_sig = 1.0 / (1.0 + jnp.exp(-gate_now))
    act = gate_now * gate_sig
    mixed_now = mixed[...]
    gated = mixed_now * act
    d_out_now = d_out[...]
    normed_out = (gated * r_out * gain[...]).astype(jnp.bfloat16)
    to_home = dots(place_of_rows(slots[0]), normed_out, ((0,), (0,)))
    per = BLOCK // shards
    if per % 16 == 0:
        no_rows[0] = to_home.astype(jnp.bfloat16).reshape(shards, per, inner)
    else:
        for turn in range(shards):
            no_rows[0, turn] = to_home[turn * per : (turn + 1) * per].astype(jnp.bfloat16)
    d_gated = r_out * (gain[...] * d_out_now - gated * (r_out * r_out) * inside)
    dy = d_gated * act
    d_cols[:, :inner] = (d_gated * mixed_now * (gate_sig * (1.0 + gate_now * (1.0 - gate_sig)))).astype(jnp.bfloat16)
    grads[5:6, :] += jnp.sum(gated * r_out * d_out_now, axis=0, keepdims=True)
    pre_now = pre[...]
    sig = 1.0 / (1.0 + jnp.exp(-pre_now))
    conv = pre_now * sig
    values, b_rows, c_rows = conv[:, :inner], conv[:, inner : inner + STATE], conv[:, inner + STATE :]
    grads[6:7, :] += jnp.sum(dy * values, axis=0, keepdims=True)
    dt_wide = widen(dt, heads)
    fed = values * dt_wide
    old, after = state_in[0], carry[...]
    b_parts, c_parts, old_parts, after_parts = split(b_rows), split(c_rows), split(old), split(after)
    carried_wide, tail_wide, keep_wide = widen(carried, heads), widen(tail, heads), widen(keep, heads)
    rows = lax.broadcasted_iota(jnp.int32, (BLOCK, BLOCK), 0)
    cols = lax.broadcasted_iota(jnp.int32, (BLOCK, BLOCK), 1)
    allowed = (seg_col == seg_row) & (cols >= rows)
    scores_t = jnp.where(allowed, dot3(b_parts, c_parts, NT), 0.0)
    low_half = lax.broadcasted_iota(jnp.int32, (BLOCK, 2 * HDIM), 1) < HDIM
    d_scores_t = jnp.zeros((BLOCK, BLOCK), jnp.float32)
    d_fed, row_terms, col_terms = [], [], []
    for h in range(0, heads, 2):
        fed_pair = fed[:, h * HDIM : (h + 2) * HDIM]
        fed_high, fed_low = split(fed_pair)
        dy_high, dy_low = split(dy[:, h * HDIM : (h + 2) * HDIM])
        dy_wide = jnp.concatenate([dy_high, dy_low], axis=1)
        found = []
        for k in (h, h + 1):
            own = low_half if k == h else jnp.logical_not(low_half)
            left = jnp.concatenate(
                [beside(fed_high, fed_low, own), jnp.where(own, fed_high, 0.0).astype(jnp.bfloat16)], axis=1
            )
            right = jnp.concatenate([beside(dy_high, dy_high, own), dy_low], axis=1)
            d_mixing = dots(left, right, NT)
            decay = jnp.exp(jnp.minimum(run_t[k : k + 1, :] - run[:, k : k + 1], 0.0))
            mixing = decay * scores_t
            d_scores_t = d_scores_t + decay * d_mixing
            flow = mixing * d_mixing
            row_terms.append(jnp.sum(flow, axis=0, keepdims=True))
            col_terms.append(jnp.sum(flow, axis=1, keepdims=True))
            found.append(dot_wide(mixing, dy_wide))
        d_fed.append(jnp.where(low_half, found[0], found[1]))
    d_scores_t = split(jnp.where(allowed, d_scores_t, 0.0))
    fed_tail = fed * tail_wide
    dy_carried = dy * carried_wide
    d_fed_out = tail_wide * dot3(b_parts, after_parts)
    d_fed = jnp.concatenate(d_fed, axis=1) + d_fed_out
    dy_parts, tail_parts = split(dy_carried), split(fed_tail)
    here = pl.ds(pl.multiple_of(block * BLOCK, BLOCK), BLOCK)
    bc_now = jnp.concatenate(
        [
            (dot3(d_scores_t, c_parts) + dot3(tail_parts, after_parts, NT)).T,
            (dot3(d_scores_t, b_parts, ((0,), (0,))) + dot3(dy_parts, old_parts, NT)).T,
        ],
        axis=0,
    )
    bc_rows[:, :, :, here] = bc_now.reshape(lines, columns, shared, BLOCK)

    def at_step(turn):
        return pl.ds(pl.multiple_of((blocks - 1 - turn) * BLOCK, BLOCK), BLOCK)

    def push_wide(turn, hop):
        to = (x + hop) % columns
        return remote(
            bc_rows.at[:, to, :, at_step(turn)], bc_wide.at[hop - 1, :, :, at_step(turn)],
            wide_send.at[hop - 1, turn], wide_recv.at[hop - 1, turn], shard=z * columns + to,
        )

    def push_line(hop, at):
        to = (z + hop) % lines
        return remote(bc_sum.at[to, :, at], bc_in.at[hop - 1, :, at], bc_send.at[hop], bc_recv.at[hop], shard=to * columns + x)

    def add_wide(turn):
        found = bc_rows[:, x, :, at_step(turn)]
        for hop in range(1, columns):
            push_wide(turn, hop).wait_recv()
            found = found + bc_wide[hop - 1, :, :, at_step(turn)]
        bc_sum[:, :, at_step(turn)] = found
        for hop in range(1, lines):
            push_line(hop, at_step(turn)).start()

    for hop_x in range(1, columns):
        push_wide(step, hop_x).start()

    lag = min(3, blocks - 1)

    @pl.when(step >= lag)
    def _():
        add_wide(step - lag)

    head_count = dt_t.shape[0]
    pad = [jnp.zeros((1, BLOCK), jnp.float32)] * (head_count - heads)
    pad_col = [jnp.zeros((BLOCK, 1), jnp.float32)] * (head_count - heads)
    d_run = jnp.concatenate(row_terms + pad, axis=0) - jnp.concatenate(col_terms + pad_col, axis=1).T
    d_run = d_run + head_sums(dy_carried * dot3(c_parts, old_parts), marks[...])
    leaving = head_sums(fed * d_fed_out, marks[...])
    kept = jnp.sum(old * after, axis=0, keepdims=True) * keep_wide
    kept = jnp.sum(marks[...].astype(jnp.float32) * kept, axis=1, keepdims=True)
    at_end = lax.broadcasted_iota(jnp.int32, (head_count, BLOCK), 1) == BLOCK - 1
    total = jnp.sum(leaving, axis=1, keepdims=True) + kept
    d_run = d_run - leaving + jnp.where(at_end, total, 0.0)
    d_log = running_sum(d_run, reverse=True)
    d_dt[...] = d_log * rate[...] + head_sums(values * d_fed, marks[...])
    grad_rate[...] += d_log * (dt_t * rate[...])
    carry[...] = keep_wide * after + dot3(c_rows.T, dy_parts)
    pre_v, sig_v = pre_now[:, :inner], sig[:, :inner]
    d_values = dt_wide * d_fed + skip[...] * dy
    d_pre = d_values * (sig_v * (1.0 + pre_v * (1.0 - sig_v)))
    ext[:BLOCK, :] = d_pre
    place = block * BLOCK + lax.broadcasted_iota(jnp.int32, (BLOCK, 1), 0)
    conv_in = conv_v[...]
    d_conv = taps[CONV - 1 : CONV, :] * d_pre
    grads[CONV - 1 : CONV, :] += jnp.sum(conv_in * d_pre, axis=0, keepdims=True)
    grads[CONV : CONV + 1, :] += jnp.sum(d_pre, axis=0, keepdims=True)
    for ahead in range(1, CONV):
        same = sequence_of(place + ahead, bounds) == seg_col
        moved = jnp.where(same, ext[ahead : ahead + BLOCK, :], 0.0)
        d_conv = d_conv + taps[CONV - 1 - ahead : CONV - ahead, :] * moved
        grads[CONV - 1 - ahead : CONV - ahead, :] += jnp.sum(conv_in * moved, axis=0, keepdims=True)
    ext[BLOCK:, :] = ext[:TAIL, :]
    d_cols[:, inner:] = d_conv.astype(jnp.bfloat16)

    @pl.when(step == blocks - 1)
    def _():
        everything = pl.ds(0, bc_sum.shape[2])
        for turn in range(blocks - lag, blocks):
            add_wide(turn)
        for turn in hops:
            if 2 * turn >= blocks:
                hop(turn)
        end()
        for turn in range(1, lines):
            push_line(turn, everything).wait()
        found = bc_sum[z]
        for turn in range(1, lines):
            found = found + bc_in[turn - 1]
        d_bc[...] = found
        for turn in range(blocks):
            for hop_x in range(1, columns):
                push_wide(turn, hop_x).wait_send()


def mixer_forward(shards, bounds, slots, rows_in, weight, taps, bias, dt_bias, rate, skip, cot_own):
    blocks, _, width = rows_in.shape
    columns = grid_columns(shards)
    total, inner, kept = blocks * BLOCK, INNER // shards, weight.shape[0]
    heads = inner // HDIM
    f32, bf16, any_space = jnp.float32, jnp.bfloat16, pl.BlockSpec(memory_space=pl.ANY)

    def block_of(lanes):
        return pl.BlockSpec((BLOCK, lanes), lambda i: (i, 0))

    return pl.pallas_call(
        functools.partial(forward_kernel, heads, shards, columns),
        grid=(blocks,),
        in_specs=[
            pl.BlockSpec(memory_space=pltpu.SMEM),
            pl.BlockSpec((1, 1, BLOCK), lambda i: (i, 0, 0)),
            pl.BlockSpec((1, BLOCK, width), lambda i: (i, 0, 0)),
            whole(weight.shape),
            whole(taps.shape),
            whole(bias.shape),
            whole(dt_bias.shape),
            whole(rate.shape),
            whole(skip.shape),
            any_space,
        ],
        out_specs=[
            block_of(width),
            block_of(kept),
            block_of(inner + SHARED),
            block_of(inner),
            pl.BlockSpec((1, STATE, inner), lambda i: (i, 0, 0)),
            block_of(128),
            block_of(128),
            any_space,
        ],
        out_shape=[
            jax.ShapeDtypeStruct((total, width), bf16),
            jax.ShapeDtypeStruct((total, kept), f32),
            jax.ShapeDtypeStruct((total, inner + SHARED), f32),
            jax.ShapeDtypeStruct((total, inner), f32),
            jax.ShapeDtypeStruct((blocks, STATE, inner), f32),
            jax.ShapeDtypeStruct((total, 128), f32),
            jax.ShapeDtypeStruct((total, 128), f32),
            jax.ShapeDtypeStruct((cot_own.shape[0], shards) + cot_own.shape[1:], bf16),
        ],
        scratch_shapes=[
            pltpu.VMEM((BLOCK + TAIL, inner + SHARED), f32),
            pltpu.VMEM((STATE, inner), f32),
            *gather_semaphores(shards, columns),
        ],
        compiler_params=pltpu.CompilerParams(
            collective_id=2, has_side_effects=True, vmem_limit_bytes=56 * 1024 * 1024
        ),
        cost_estimate=pl.CostEstimate(flops=0, bytes_accessed=300_000_000, transcendentals=0),
        name="mixer_forward",
    )(bounds, slots, rows_in, weight, taps, bias, dt_bias, rate, skip, cot_own)


def pack_cotangent(shards, slots, rows_in, weight, mixed, projected, gain):
    blocks, _, width = rows_in.shape
    total, inner = mixed.shape
    several = 2

    def block_of(lanes):
        return pl.BlockSpec((several * BLOCK, lanes), lambda i: (i, 0))

    return pl.pallas_call(
        functools.partial(cotangent_kernel, shards),
        grid=(blocks // several,),
        in_specs=[
            pl.BlockSpec((several, 1, BLOCK), lambda i: (i, 0, 0)),
            pl.BlockSpec((several, BLOCK, width), lambda i: (i, 0, 0)),
            whole(weight.shape),
            block_of(inner),
            block_of(inner),
            whole(gain.shape),
        ],
        out_specs=[block_of(width), block_of(inner), whole((8, total))],
        out_shape=[
            jax.ShapeDtypeStruct((total, width), jnp.bfloat16),
            jax.ShapeDtypeStruct((total, inner), jnp.float32),
            jax.ShapeDtypeStruct((8, total), jnp.float32),
        ],
        scratch_shapes=[
            pltpu.VMEM((8, total), jnp.float32),
            pltpu.VMEM((shards - 1, 8, total), jnp.float32),
            pltpu.SemaphoreType.DMA((shards,)),
            pltpu.SemaphoreType.DMA((shards,)),
        ],
        compiler_params=pltpu.CompilerParams(
            collective_id=5, has_side_effects=True, vmem_limit_bytes=48 * 1024 * 1024
        ),
        cost_estimate=pl.CostEstimate(flops=0, bytes_accessed=60_000_000, transcendentals=0),
        name="pack_cotangent",
    )(slots, rows_in, weight, mixed, projected, gain)


def mixer_backward(
    shards, bounds, slots, pre, mixed, projected, d_out, sums, states, dt_cols, taps, rate, skip, gain, out_own
):
    total, inner = d_out.shape
    heads, blocks, padded = inner // HDIM, total // BLOCK, rate.shape[0]
    shared = SHARED // shards
    columns = grid_columns(shards)
    marks = (jnp.arange(padded)[:, None] == jnp.arange(inner)[None, :] // HDIM).astype(jnp.bfloat16)

    def block_of(width, column):
        return pl.BlockSpec((BLOCK, width), lambda i: (blocks - 1 - i, column))

    return pl.pallas_call(
        functools.partial(backward_kernel, heads, blocks, shards, columns),
        grid_spec=pltpu.PrefetchScalarGridSpec(
            num_scalar_prefetch=0,
            grid=(blocks,),
            in_specs=[
                pl.BlockSpec(memory_space=pltpu.SMEM),
                pl.BlockSpec((1, 1, BLOCK), lambda i: (blocks - 1 - i, 0, 0)),
                block_of(inner + SHARED, 0),
                block_of(inner, 0),
                block_of(inner, 0),
                block_of(inner, 0),
                block_of(inner, 1),
                pl.BlockSpec((8, BLOCK), lambda i: (0, blocks - 1 - i)),
                pl.BlockSpec((1, STATE, inner), lambda i: (blocks - 1 - i, 0, 0)),
                block_of(dt_cols.shape[1], 0),
                whole(taps.shape),
                whole(rate.shape),
                whole(skip.shape),
                whole(gain.shape),
                whole(marks.shape),
                pl.BlockSpec(memory_space=pl.ANY),
            ],
            out_specs=[
                block_of(2 * inner, 0),
                whole((shared, total)),
                pl.BlockSpec((padded, BLOCK), lambda i: (0, blocks - 1 - i)),
                whole((8, inner)),
                whole((padded, BLOCK)),
                pl.BlockSpec((1, shards, BLOCK // shards, inner), lambda i: (blocks - 1 - i, 0, 0, 0)),
                pl.BlockSpec(memory_space=pl.ANY),
            ],
            scratch_shapes=[
                pltpu.VMEM((BLOCK + TAIL, inner), jnp.float32),
                pltpu.VMEM((STATE, inner), jnp.float32),
                pltpu.VMEM((shards // columns, columns, shared, total), jnp.float32),
                pltpu.VMEM((max(columns - 1, 1), shards // columns, shared, total), jnp.float32),
                pltpu.VMEM((shards // columns, shared, total), jnp.float32),
                pltpu.VMEM((shards // columns - 1, shared, total), jnp.float32),
                pltpu.SemaphoreType.DMA((max(columns - 1, 1), blocks)),
                pltpu.SemaphoreType.DMA((max(columns - 1, 1), blocks)),
                pltpu.SemaphoreType.DMA((shards,)),
                pltpu.SemaphoreType.DMA((shards,)),
                *gather_semaphores(shards, columns),
            ],
        ),
        out_shape=[
            jax.ShapeDtypeStruct((total, 2 * inner), jnp.bfloat16),
            jax.ShapeDtypeStruct((shared, total), jnp.float32),
            jax.ShapeDtypeStruct((padded, total), jnp.float32),
            jax.ShapeDtypeStruct((8, inner), jnp.float32),
            jax.ShapeDtypeStruct((padded, BLOCK), jnp.float32),
            jax.ShapeDtypeStruct((blocks, shards, BLOCK // shards, inner), jnp.bfloat16),
            jax.ShapeDtypeStruct((out_own.shape[0], shards) + out_own.shape[1:], jnp.bfloat16),
        ],
        compiler_params=pltpu.CompilerParams(
            collective_id=3, has_side_effects=True, vmem_limit_bytes=56 * 1024 * 1024
        ),
        cost_estimate=pl.CostEstimate(flops=0, bytes_accessed=200_000_000, transcendentals=0),
        name="mixer_backward",
    )(bounds, slots, pre, mixed, projected, d_out, projected, sums, states, dt_cols, taps, rate, skip, gain, marks, out_own)


def piece_rows(shards, groups):
    chunks = (2 * INNER // shards + SHARED // shards) // CHUNK
    return -(-chunks // groups) * CHUNK


def column_runs(shards, groups):
    inner, width = INNER // shards, (2 * INNER + SHARED + HEADS) // groups
    kept = 2 * inner + SHARED + HEADS
    quarter = kept // groups
    spans = []
    for shard in range(shards):
        spans.append((inner * shard, shard, 0, inner))
        spans.append((INNER + inner * shard, shard, inner, inner))
    spans.append((2 * INNER, None, 2 * inner, SHARED + HEADS))
    runs = []
    for column, shard, row, length in spans:
        while length > 0:
            step = min(length, width - column % width, quarter - row % quarter)
            runs.append((column // width, column % width, shard, row, step))
            column, row, length = column + step, row + step, length - step
    return runs


def front_kernel(
    shards, groups, columns,
    rows_in, gain, cot_in, weight_in, out_in, slot_row, slot_col,
    rows_all, weight_all, out_all, slot_all, cot_own, out_cast, scaled_rows,
    rows_own, weight_own, out_own, slot_own,
    run_send, run_recv, share_send, share_recv, out_send, out_recv, slot_send, slot_recv, local_sem, *gather_sems,
):
    shard, group = lax.axis_index("shard"), lax.axis_index("group")
    lines, rows_y = shards // columns, groups // 2
    y, core = group // 2, group % 2
    mate = y * 2 + 1 - core
    quarter = weight_all.shape[0] // groups
    depth = weight_own.shape[1]
    out_width = out_own.shape[1]
    everyone = []
    for step in range(1, shards * groups):
        other_shard = (shard + step % shards) % shards
        other_group = (group + step // shards) % groups
        everyone.append({"shard": other_shard, "group": other_group})
    barrier_with(everyone)

    count = rows_in.shape[0]
    below = (slot_col[...] < slot_row[...]).astype(jnp.int32).astype(jnp.float32)
    rank = jnp.sum(below, axis=0, keepdims=True).astype(jnp.int32)
    sort = (lax.broadcasted_iota(jnp.int32, (count, count), 0) == rank).astype(jnp.bfloat16)
    value = rows_in[...]
    scale = lax.rsqrt(jnp.sum(value * value, axis=1, keepdims=True) * (1.0 / value.shape[1]) + 1e-05)
    scaled = value * scale
    value = (scaled * gain[...]).astype(jnp.bfloat16)
    rows_own[...] = dots(sort, value, ((1,), (0,))).astype(jnp.bfloat16).reshape(rows_own.shape)
    begin, hop, end = row_gather(shards, columns, rows_own, rows_all, *gather_sems)
    begin()
    slots = slot_row[...]
    high = slots // 256
    both = jnp.where(lax.broadcasted_iota(jnp.int32, (8, count), 0) == 0, high, slots - 256 * high)
    both = dots(both.astype(jnp.float32).astype(jnp.bfloat16), sort, NT)
    slot_own[...] = jnp.broadcast_to(256.0 * both[0:1, :] + both[1:2, :], (8, count)).astype(jnp.int32)
    out_own[...] = out_in[...].astype(jnp.bfloat16)
    weight_own[...] = weight_in[...].astype(jnp.bfloat16)

    def slot_copy(step):
        return remote(slot_own, slot_all.at[shard], slot_send.at[step], slot_recv.at[step], shard=(shard + step) % shards)

    for step in range(1, shards):
        slot_copy(step).start()
    slot_here = pltpu.make_async_copy(slot_own, slot_all.at[shard], local_sem.at[0])
    slot_here.start()

    runs = column_runs(shards, groups)
    lanes = pl.ds(pl.multiple_of(shard * depth, depth), depth)
    jobs = {owner: [] for owner in range(groups)}
    for owner, column, target, row, length in runs:
        for to in range(shards) if target is None else (target,):
            jobs[owner].append((column, to, row, length))

    def run_copy(number, column, to, row, length):
        return remote(
            weight_own.at[pl.ds(column, length)], weight_all.at[pl.ds(row, length), lanes],
            run_send.at[number], run_recv, shard=to, group=row // quarter,
        )

    def each_run(act):
        for owner in range(groups):
            @pl.when(group == owner)
            def _():
                for number, (column, to, row, length) in enumerate(jobs[owner]):
                    if row // quarter == owner:
                        here = shard == to
                        act(number, column, to, row, length, here)
                    else:
                        act(number, column, to, row, length, None)

    def start_run(number, column, to, row, length, here):
        if here is None:
            run_copy(number, column, to, row, length).start()
            return

        @pl.when(here)
        def _():
            pltpu.make_async_copy(weight_own.at[pl.ds(column, length)], weight_all.at[pl.ds(row, length), lanes], run_recv).start()

        @pl.when(jnp.logical_not(here))
        def _():
            run_copy(number, column, to, row, length).start()

    def end_run(number, column, to, row, length, here):
        if here is None:
            run_copy(number, column, to, row, length).wait_send()
            return

        @pl.when(jnp.logical_not(here))
        def _():
            run_copy(number, column, to, row, length).wait_send()

    each_run(start_run)

    def own_part(ref, part):
        if ref is out_all:
            return ref.at[:, pl.ds(pl.multiple_of(part * out_width, out_width), out_width)]
        return ref.at[pl.ds(pl.multiple_of(part * quarter, quarter), quarter)]

    def share(ref, part, sends, recvs, number, peer, first=None):
        source = own_part(ref, part) if first is None else first
        return remote(source, own_part(ref, part), sends.at[number], recvs.at[part], group=peer)

    def share_start(ref, sends, recvs, first=None):
        share(ref, group, sends, recvs, 0, mate, first).start()
        for step in range(1, rows_y):
            share(ref, group, sends, recvs, step, (y + step) % rows_y * 2 + core, first).start()

    def share_pass(ref, sends, recvs):
        for step in range(1, rows_y):
            part = (y + step) % rows_y * 2 + core
            share(ref, part, sends, recvs, step, part).wait_recv()
            share(ref, part, sends, recvs, rows_y - 1 + step, mate).start()

    def share_end(ref, sends, recvs):
        for turn in range(rows_y):
            part = turn * 2 + 1 - core
            share(ref, part, sends, recvs, 0, mate).wait_recv()
        for number in range(2 * rows_y - 1):
            share(ref, group, sends, recvs, number, mate).wait_send()

    out_here = pltpu.make_async_copy(out_own, own_part(out_all, group), local_sem.at[1])
    out_here.start()
    share_start(out_all, out_send, out_recv, out_own)
    out_cast[...] = out_own[...]
    high = scaled.astype(jnp.bfloat16)
    left = scaled - high.astype(jnp.float32)
    mid = left.astype(jnp.bfloat16)
    low = (left - mid.astype(jnp.float32)).astype(jnp.bfloat16)
    plain = ((1,), (0,))
    scaled_rows[...] = dots(sort, high, plain) + (dots(sort, mid, plain) + dots(sort, low, plain))
    cot_own[...] = (
        dots(sort, cot_in[...].astype(jnp.bfloat16), ((1,), (0,))).astype(jnp.bfloat16).reshape(cot_own.shape)
    )

    for step in range(1, lines):
        hop(step)
        if step == 1:
            share_pass(out_all, out_send, out_recv)
            kept = own_part(weight_all, group)
            pltpu.make_async_copy(kept, kept, run_recv).wait()
            share_start(weight_all, share_send, share_recv)
    share_pass(weight_all, share_send, share_recv)

    end()
    out_here.wait()
    share_end(out_all, out_send, out_recv)
    share_end(weight_all, share_send, share_recv)
    each_run(end_run)
    for step in range(1, shards):
        slot_copy(step).wait()
    slot_here.wait()


def front_exchange(shards, groups, rows_in, gain, cot_in, weight_in, out_in, slots):
    columns = grid_columns(shards)
    rows_y = groups // 2
    count, width = rows_in.shape
    blocks, per = shards * count // BLOCK, BLOCK // shards
    kept = 2 * INNER // shards + SHARED + HEADS
    any_space, vmem = pl.BlockSpec(memory_space=pl.ANY), pl.BlockSpec(memory_space=pltpu.VMEM)
    dma, bf16 = pltpu.SemaphoreType.DMA, jnp.bfloat16
    counts = {}
    for owner, _, target, _, _ in column_runs(shards, groups):
        counts[owner] = counts.get(owner, 0) + (shards if target is None else 1)
    return pl.pallas_call(
        functools.partial(front_kernel, shards, groups, columns),
        in_specs=[vmem] * 7,
        out_specs=[any_space] * 4 + [vmem] * 3,
        out_shape=[
            jax.ShapeDtypeStruct((blocks, shards, per, width), bf16),
            jax.ShapeDtypeStruct((kept, width), bf16),
            jax.ShapeDtypeStruct((out_in.shape[0], out_in.shape[1] * groups), bf16),
            jax.ShapeDtypeStruct((shards, 8, count), jnp.int32),
            jax.ShapeDtypeStruct((blocks, per, width), bf16),
            jax.ShapeDtypeStruct(out_in.shape, bf16),
            jax.ShapeDtypeStruct((count, width), jnp.float32),
        ],
        scratch_shapes=[
            pltpu.VMEM((blocks, per, width), bf16),
            pltpu.VMEM(weight_in.shape, bf16),
            pltpu.VMEM(out_in.shape, bf16),
            pltpu.VMEM((8, count), jnp.int32),
            dma((max(counts.values()),)),
            dma,
            dma((2 * rows_y - 1,)),
            dma((groups,)),
            dma((2 * rows_y - 1,)),
            dma((groups,)),
            dma((shards,)),
            dma((shards,)),
            dma((2,)),
            *gather_semaphores(shards, columns),
        ],
        compiler_params=pltpu.CompilerParams(
            collective_id=4, has_side_effects=True, vmem_limit_bytes=48 * 1024 * 1024
        ),
        cost_estimate=pl.CostEstimate(flops=0, bytes_accessed=300_000_000, transcendentals=0),
        name="front_exchange",
    )(rows_in, gain[None, :], cot_in, weight_in, out_in, slots[None, :], slots[:, None])


def unpack_kernel(
    shards, slots, d_cols, d_rest, normed, weight, weight_rest, no_rows,
    partial, grad, home, moved_cols, moved_rest, local_sem, home_send, home_recv,
):
    step = pl.program_id(0)
    shard = lax.axis_index("shard")
    main = d_cols.shape[1]
    per = BLOCK // shards

    def push(turn):
        peer = (shard + turn) % shards
        return remote(no_rows.at[first, peer], home.at[:, :, lanes], home_send.at[turn], home_recv.at[turn], shard=peer)

    first, inner = pl.ds(0, home.shape[0]), no_rows.shape[3]
    lanes = pl.ds(pl.multiple_of(shard * inner, inner), inner)
    here = pltpu.make_async_copy(no_rows.at[first, shard], home.at[:, :, lanes], local_sem)

    @pl.when(step == 0)
    def _():
        barrier_with([{"shard": (shard + turn) % shards} for turn in range(1, shards)])
        for turn in range(1, shards):
            push(turn).start()
        here.start()
        grad[...] = jnp.zeros_like(grad)

    several = d_cols.shape[0] // BLOCK
    for turn in range(several):
        rows = pl.ds(turn * BLOCK, BLOCK)
        place = place_of_rows(slots[turn])
        moved_cols[rows, :] = dots(place, d_cols[rows, :], ((0,), (0,))).astype(jnp.bfloat16)
        moved_rest[rows, :] = dots(place, d_rest[rows, :], ((0,), (0,))).astype(jnp.bfloat16)
    tile = 512
    for lane in range(0, weight.shape[1], tile):
        lanes = pl.ds(lane, tile)
        found = dots(moved_cols[...], weight[:, lanes], ((1,), (0,)))
        found = found + dots(moved_rest[...], weight_rest[:, lanes], ((1,), (0,)))
        for turn in range(several):
            rows = found[turn * BLOCK : (turn + 1) * BLOCK]
            partial[:, turn, :, lanes] = rows.reshape(shards, per, tile)
    grad[:main, :] += dots(d_cols[...], normed[...], ((0,), (0,)))
    grad[main:, :] += dots(d_rest[...], normed[...], ((0,), (0,)))

    @pl.when(step == pl.num_programs(0) - 1)
    def _():
        for turn in range(1, shards):
            push(turn).wait()
        here.wait()


def project_back(slots, d_cols, d_rest, normed, weight, weight_rest, no_rows, shards):
    blocks, width = slots.shape[0], normed.shape[1]
    per, main, rest = BLOCK // shards, d_cols.shape[1], d_rest.shape[1]
    several = 2
    any_space = pl.BlockSpec(memory_space=pl.ANY)

    def block_of(columns):
        return pl.BlockSpec((several * BLOCK, columns), lambda i: (i, 0))

    return pl.pallas_call(
        functools.partial(unpack_kernel, shards),
        grid=(blocks // several,),
        in_specs=[
            pl.BlockSpec((several, 1, BLOCK), lambda i: (i, 0, 0)),
            block_of(main),
            block_of(rest),
            block_of(width),
            pl.BlockSpec((main, width), lambda i: (0, 0)),
            whole(weight_rest.shape),
            any_space,
        ],
        out_specs=[
            pl.BlockSpec((shards, several, per, width), lambda i: (0, i, 0, 0)),
            whole((main + rest, width)),
            any_space,
        ],
        out_shape=[
            jax.ShapeDtypeStruct((shards, blocks, per, width), jnp.float32),
            jax.ShapeDtypeStruct((main + rest, width), jnp.float32),
            jax.ShapeDtypeStruct((blocks, per, INNER), jnp.bfloat16),
        ],
        scratch_shapes=[
            pltpu.VMEM((several * BLOCK, main), jnp.bfloat16),
            pltpu.VMEM((several * BLOCK, rest), jnp.bfloat16),
            pltpu.SemaphoreType.DMA,
            pltpu.SemaphoreType.DMA((shards,)),
            pltpu.SemaphoreType.DMA((shards,)),
        ],
        compiler_params=pltpu.CompilerParams(
            collective_id=6, has_side_effects=True, vmem_limit_bytes=60 * 1024 * 1024
        ),
        cost_estimate=pl.CostEstimate(flops=0, bytes_accessed=90_000_000, transcendentals=0),
        name="project_back",
    )(slots, d_cols, d_rest, normed, weight, weight_rest, no_rows)


def other_place(step, place, count):
    upwards = count - 1 - place
    low = jnp.where(step < upwards, count - 1 - step, step - upwards)
    high = jnp.where(step < place, step, count - 1 - (step - place))
    return jnp.where(2 * place < count, low, high)


def tail_kernel(
    shards, groups, columns, near, direct,
    partial, weight_part, small, scaled_rows,
    rows_out, weight_out, mark_out, small_out, gain_out, core_in, row_in, row_scale_in, small_in, gain_in,
    wide_in, wide_scale, line_in, line_scale,
    held, coded, scales, line_coded, line_scales, got, got_scale, marks, total, other, send_rows, send_scales, row_got, row_scale_got, deal_rows, deal_scales, small_sum, small_got,
    gain_sum, gain_part,
    load_sem, wide_send, wide_recv, line_send, line_recv, core_send, core_recv, row_send, row_recv,
    deal_send, deal_recv, mark_send, mark_recv, small_send, small_recv, gain_send, gain_recv,
):
    shard, group = lax.axis_index("shard"), lax.axis_index("group")
    lines = shards // columns
    rows_y = groups // 2
    z, x = shard // columns, shard % columns
    y, core = group // 2, group % 2
    count = held.shape[0]
    owned, depth = weight_out.shape
    piece, chunk = total.shape[0], CHUNK
    inner, shared = INNER // shards, SHARED // shards

    def load(src, dst):
        copy = pltpu.make_async_copy(src, dst, load_sem)
        copy.start()
        copy.wait()

    shard_peers = [(shard + step) % shards for step in range(1, shards)]
    group_peers = [(group + step) % groups for step in range(1, groups)]
    if direct:
        barrier_with(
            [
                {"shard": (shard + step % shards) % shards, "group": (group + step // shards) % groups}
                for step in range(1, shards * groups)
            ]
        )
    else:
        barrier_with([{"shard": peer} for peer in shard_peers] + [{"group": peer} for peer in group_peers])

    mate = y * 2 + 1 - core

    def core_copy(turn):
        return remote(piece_of(turn * 2 + 1 - core), core_in.at[turn], core_send.at[turn], core_recv.at[turn], group=mate)

    def piece_of(owner):
        return weight_part.at[pl.ds(pl.multiple_of(owner * piece, piece), piece)]

    for turn in range(rows_y if direct else 0):
        core_copy(turn).start()

    def small_copy(step):
        return remote(small, small_in.at[step - 1], small_send.at[step - 1], small_recv.at[step - 1], group=(group + step) % groups)

    for step in range(1, groups):
        small_copy(step).start()

    def code(coded_to, scales_to, values=held, lot=32):
        @pl.loop(0, values.shape[0] // lot, unroll=2)
        def _(turn):
            rows = pl.ds(pl.multiple_of(turn * lot, lot), lot)
            value = values[rows, :]
            most = jnp.maximum(jnp.max(jnp.abs(value), axis=1, keepdims=True), 1e-30)
            coded_to[rows, :] = jnp.round(value * (32767.0 / most)).astype(jnp.int32).astype(jnp.int16)
            marks[rows, :] = jnp.broadcast_to(most * (1.0 / 32767.0), (lot, 128))

        scales_to[...] = marks[: scales_to.shape[1], :].T[:8, :]

    def add(coded_from, scales_from):
        if not near:
            load(coded_from, got)
            load(scales_from, got_scale)
            coded_from, scales_from = got, got_scale
        marks[:count, :] = jnp.broadcast_to(scales_from[0:1, :], (128, count)).T

        @pl.loop(0, count // 32, unroll=2)
        def _(turn):
            rows = pl.ds(pl.multiple_of(turn * 32, 32), 32)
            held[rows, :] += coded_from[rows, :].astype(jnp.float32) * marks[rows, 0:1]

    def place_of(step):
        return other_place(step, z, lines) if step < lines - 1 else z

    def wide_copies(step, hop):
        at = (hop - 1) * lines + step
        peer = z * columns + (x + hop) % columns
        target = place_of(step)
        return (
            remote(coded.at[step], wide_in.at[hop - 1, target], wide_send.at[0, at], wide_recv.at[0, at], shard=peer),
            remote(scales.at[step], wide_scale.at[hop - 1, target], wide_send.at[1, at], wide_recv.at[1, at], shard=peer),
        )

    def send_wide(hop, steps):
        for step in steps:
            if hop > 1:
                for copy in wide_copies(step, hop - 1):
                    copy.wait_send()
            load(partial.at[place_of(step) * columns + (x + hop) % columns], held)
            code(coded.at[step], scales.at[step])
            for copy in wide_copies(step, hop):
                copy.start()

    def row_copies(step):
        peer = (y + step) % rows_y * 2 + core
        return (
            remote(send_rows.at[step - 1], row_in.at[step - 1], row_send.at[0, step - 1], row_recv.at[0, step - 1], group=peer),
            remote(send_scales.at[step - 1], row_scale_in.at[step - 1], row_send.at[1, step - 1], row_recv.at[1, step - 1], group=peer),
        )

    def core_sum(turn):
        load(piece_of(turn * 2 + core), total)
        load(core_in.at[turn], other)

        @pl.loop(0, piece // chunk)
        def _(turn):
            rows = pl.ds(pl.multiple_of(turn * chunk, chunk), chunk)
            total[rows, :] += other[rows, :]

    if columns > 1:
        send_wide(1, range(0, 1))
    if direct:
        for turn in range(rows_y):
            core_copy(turn).wait_recv()
        for step in range(1, rows_y):
            core_sum((y + step) % rows_y)
            code(send_rows.at[step - 1], send_scales.at[step - 1], total, chunk)
            for copy in row_copies(step):
                copy.start()
        core_sum(y)
    if columns > 1:
        send_wide(1, range(1, lines))
    for hop in range(2, columns):
        send_wide(hop, range(lines))

    load(small, small_sum)
    for step in range(1, groups):
        small_copy(step).wait_recv()
        load(small_in.at[step - 1], small_got)
        small_sum[...] += small_got[...]

    def small_deal(step):
        return remote(small_sum, small_out.at[shard], small_send.at[groups + step], small_recv.at[groups + step], shard=(shard + step) % shards)

    for step in range(1, shards):
        small_deal(step).start()
    load(small_sum, small_out.at[shard])

    def line_copies(step):
        target = place_of(step)
        way = jnp.where(target > z, 0, 1)
        peer = jnp.where(target > z, z + 1, z - 1) * columns + x
        return (
            remote(line_coded.at[step], line_in.at[way, target], line_send.at[0, step], line_recv.at[0, way, target], shard=peer),
            remote(line_scales.at[step], line_scale.at[way, target], line_send.at[1, step], line_recv.at[1, way, target], shard=peer),
        )

    def take(way, target):
        source = jnp.where(way == 0, z - 1, z + 1)
        peer = jnp.clip(source, 0, lines - 1) * columns + x
        remote(line_coded.at[0], line_in.at[way, target], line_send.at[0, 0], line_recv.at[0, way, target], shard=peer).wait_recv()
        remote(line_scales.at[0], line_scale.at[way, target], line_send.at[1, 0], line_recv.at[1, way, target], shard=peer).wait_recv()
        add(line_in.at[way, target], line_scale.at[way, target])

    def gather_wide(step):
        target = place_of(step)
        load(partial.at[target * columns + x], held)
        for hop in range(1, columns):
            for copy in wide_copies(step, hop):
                copy.wait_recv()
            add(wide_in.at[hop - 1, target], wide_scale.at[hop - 1, target])

    def deal_copy(turn, step):
        first = group * piece + turn * chunk
        column = jnp.where(
            first < inner,
            inner * shard + first,
            jnp.where(first < 2 * inner, INNER + inner * shard + first - inner, 2 * INNER + shared * shard + first - 2 * inner),
        )
        owner = jnp.minimum(column // owned, groups - 1)
        peer = (shard + step) % shards
        source = deal_rows.at[
            pl.ds(pl.multiple_of(turn * chunk, chunk), chunk), pl.ds(pl.multiple_of(peer * depth, depth), depth)
        ]
        target = weight_out.at[pl.ds(pl.multiple_of(column - owner * owned, chunk), chunk)]
        real = first < 2 * inner + shared
        here = real & (owner == group) if step == 0 else None
        away = real & (owner != group) if step == 0 else real

        def near_copy():
            return pltpu.make_async_copy(source, target, deal_recv)

        def far():
            return remote(source, target, deal_send.at[turn, step], deal_recv, shard=peer, group=owner)

        return here, near_copy, away, far

    def deal():
        for step in range(1, rows_y):
            for copy in row_copies(step):
                copy.wait_recv()
            load(row_in.at[step - 1], row_got)
            load(row_scale_in.at[step - 1], row_scale_got)
            marks[: row_scale_got.shape[1], :] = jnp.broadcast_to(row_scale_got[0:1, :], (128, row_scale_got.shape[1])).T

            @pl.loop(0, piece // chunk)
            def _(turn):
                rows = pl.ds(pl.multiple_of(turn * chunk, chunk), chunk)
                total[rows, :] += row_got[rows, :].astype(jnp.float32) * marks[rows, 0:1]

        code(deal_rows, deal_scales, total, chunk)
        load(deal_scales, mark_out.at[shard, group])
        for step in range(1, groups):
            mark_copy(step).start()

    def deal_some(part, parts):
        chunks = piece // chunk

        @pl.loop(part * chunks // parts, (part + 1) * chunks // parts)
        def _(turn):
            for step in range(shards):
                here, near_copy, away, far = deal_copy(turn, step)
                if here is not None:
                    pl.when(here)(lambda: near_copy().start())
                pl.when(away)(lambda: far().start())

    def mark_copy(step):
        to = (group + step) % groups
        return remote(deal_scales, mark_out.at[shard, group], mark_send.at[step], mark_recv.at[step], group=to)

    def mark_spread(step):
        to, at = (shard + step) % shards, groups + step
        return remote(mark_out.at[shard], mark_out.at[shard], mark_send.at[at], mark_recv.at[at], shard=to)

    def mark_pass():
        for step in range(1, groups):
            mark_copy(step).wait_recv()
        for step in range(1, shards):
            mark_spread(step).start()

    def deal_end():
        for step in range(1, groups):
            mark_copy(step).wait_send()
        for step in range(1, shards):
            mark_spread(step).wait()

        @pl.when(group == groups - 1)
        def _():
            most = weight_out.at[pl.ds(0, owned - HEADS)]
            pltpu.make_async_copy(most, most, deal_recv).wait()

        @pl.when(group < groups - 1)
        def _():
            pltpu.make_async_copy(weight_out, weight_out, deal_recv).wait()

        @pl.loop(0, piece // chunk)
        def _(turn):
            for step in range(shards):
                _, _, away, far = deal_copy(turn, step)
                pl.when(away)(lambda: far().wait_send())

    for step in range(lines - 1):
        if direct and step == min(1, lines - 2):
            deal()
        target = place_of(step)
        way = jnp.where(target > z, 0, 1)
        gather_wide(step)

        @pl.when(jnp.where(target > z, z > 0, z < lines - 1))
        def _():
            take(way, target)

        code(line_coded.at[step], line_scales.at[step])
        for copy in line_copies(step):
            copy.start()
        if direct and step >= min(1, lines - 2):
            deal_some(step - min(1, lines - 2), lines - 1 - min(1, lines - 2))
    if direct:
        mark_pass()
    gather_wide(lines - 1)

    @pl.when(z > 0)
    def _():
        take(0, z)

    @pl.when(z < lines - 1)
    def _():
        take(1, z)

    rows_out[...] = held[...]
    gain_sum[...] = jnp.zeros_like(gain_sum)

    @pl.loop(0, count // 8)
    def _(turn):
        rows = pl.ds(pl.multiple_of(turn * 8, 8), 8)
        gain_sum[...] += held[rows, :] * scaled_rows[rows, :]

    def gain_copy(step):
        return remote(gain_part, gain_in.at[step - 1], gain_send.at[step - 1], gain_recv.at[step - 1], shard=(shard + step) % shards)

    def gain_deal(step):
        at = shards - 1 + step - 1
        return remote(gain_out, gain_in.at[at], gain_send.at[at], gain_recv.at[at], group=(group + step) % groups)

    lanes = gain_out.shape[1]
    products = jnp.sum(gain_sum[...], axis=0, keepdims=True)
    gain_part[...] = jnp.concatenate([products[:, row * lanes : (row + 1) * lanes] for row in range(8)], axis=0)
    for step in range(1, shards):
        gain_copy(step).start()
    gain_out[...] = gain_part[...]
    for step in range(1, shards):
        gain_copy(step).wait_recv()
        gain_out[...] += gain_in[step - 1]
    for step in range(1, groups):
        gain_deal(step).start()
    for step in range(1, groups):
        gain_deal(step).wait_recv()
    for step in range(1, groups):
        gain_deal(step).wait_send()
    for step in range(1, groups):
        gain_out[...] += gain_in[shards - 1 + step - 1]

    for step in range(1, shards):
        gain_copy(step).wait_send()
        small_deal(step).wait()
    for step in range(1, groups):
        small_copy(step).wait_send()
    if direct:
        deal_end()
        for step in range(1, rows_y):
            for copy in row_copies(step):
                copy.wait_send()
        for turn in range(rows_y):
            core_copy(turn).wait_send()
    for step in range(lines):
        for copy in wide_copies(step, columns - 1) if columns > 1 else ():
            copy.wait_send()
    for step in range(lines - 1):
        for copy in line_copies(step):
            copy.wait_send()


def tail_exchange(shards, groups, partial, weight_part, small, scaled_rows, owned, depth, direct):
    columns = grid_columns(shards)
    lines, rows_y = shards // columns, groups // 2
    count, width = scaled_rows.shape
    piece = piece_rows(shards, groups) if direct else CHUNK
    padded = -(-piece // 128) * 128
    small_shape = small.shape
    coded, scale = (count, width), (8, count)
    any_space, vmem = pl.BlockSpec(memory_space=pl.ANY), pl.BlockSpec(memory_space=pltpu.VMEM)
    f32, i16 = jnp.float32, jnp.int16
    slots = max(columns - 1, 1)
    dma = pltpu.SemaphoreType.DMA
    landing = [
        ((slots, lines) + coded, i16),
        ((slots, lines) + scale, f32),
        ((2, lines) + coded, i16),
        ((2, lines) + scale, f32),
    ]
    near = shards * count * width <= 1 << 22
    out = pl.pallas_call(
        functools.partial(tail_kernel, shards, groups, columns, near, direct),
        in_specs=[any_space, any_space, any_space, vmem],
        out_specs=[vmem, any_space, any_space, any_space, vmem] + [any_space] * 4 + [vmem] + ([] if near else [any_space] * 4),
        out_shape=[
            jax.ShapeDtypeStruct((count, width), f32),
            jax.ShapeDtypeStruct((owned, depth), i16),
            jax.ShapeDtypeStruct((shards, groups, 8, padded), f32),
            jax.ShapeDtypeStruct((shards,) + small_shape, f32),
            jax.ShapeDtypeStruct((8, width // 8), f32),
            jax.ShapeDtypeStruct((rows_y, piece, width), f32),
            jax.ShapeDtypeStruct((max(rows_y - 1, 1), piece, width), i16),
            jax.ShapeDtypeStruct((max(rows_y - 1, 1), 8, padded), f32),
            jax.ShapeDtypeStruct((max(groups - 1, 1),) + small_shape, f32),
            jax.ShapeDtypeStruct((shards - 1 + groups - 1, 8, width // 8), f32),
        ]
        + ([] if near else [jax.ShapeDtypeStruct(*each) for each in landing]),
        scratch_shapes=([pltpu.VMEM(*each) for each in landing] if near else [])
        + [
            pltpu.VMEM((count, width), f32),
            pltpu.VMEM((lines,) + coded, i16),
            pltpu.VMEM((lines,) + scale, f32),
            pltpu.VMEM((lines,) + coded, i16),
            pltpu.VMEM((lines,) + scale, f32),
            pltpu.VMEM((16, 128) if near else coded, i16),
            pltpu.VMEM((8, 128) if near else scale, f32),
            pltpu.VMEM((max(count, padded), 128), f32),
            pltpu.VMEM((piece, width), f32),
            pltpu.VMEM((piece, width), f32),
            pltpu.VMEM((max(rows_y - 1, 1), piece, width), i16),
            pltpu.VMEM((max(rows_y - 1, 1), 8, padded), f32),
            pltpu.VMEM((piece, width), i16),
            pltpu.VMEM((8, padded), f32),
            pltpu.VMEM((piece, width), i16),
            pltpu.VMEM((8, padded), f32),
            pltpu.VMEM(small_shape, f32),
            pltpu.VMEM(small_shape, f32),
            pltpu.VMEM((8, width), f32),
            pltpu.VMEM((8, width // 8), f32),
            dma,
            dma((2, slots * lines)),
            dma((2, slots * lines)),
            dma((2, lines)),
            dma((2, 2, lines)),
            dma((rows_y,)),
            dma((rows_y,)),
            dma((2, max(rows_y - 1, 1))),
            dma((2, max(rows_y - 1, 1))),
            dma((piece // CHUNK, shards)),
            dma,
            dma((shards + groups,)),
            dma((shards + groups,)),
            dma((groups + shards,)),
            dma((groups + shards,)),
            dma((shards + groups,)),
            dma((shards + groups,)),
        ],
        compiler_params=pltpu.CompilerParams(
            collective_id=1, has_side_effects=True, vmem_limit_bytes=60 * 1024 * 1024
        ),
        cost_estimate=pl.CostEstimate(flops=0, bytes_accessed=400_000_000, transcendentals=0),
        name="tail_exchange",
    )(partial, weight_part, small, scaled_rows)
    return out[:5]


def finish_kernel(
    shards, groups, columns,
    slots, d_cols, d_rest, normed, weight, weight_rest, no_rows, out_part, small, scaled_rows,
    rows_out, weight_out, mark_out, small_out, dt_out, gain_out, home, out_full, weight_part,
    core_in, row_in, row_scale_in, small_in, dt_in, gain_in,
    wide_in, wide_scale, line_in, line_scale,
    held, coded, scales, line_coded, line_scales, marks, total, other, send_rows, send_scales, row_got, row_scale_got,
    deal_rows, deal_scales, small_sum, small_got, dt_sum, dt_got, gain_sum, gain_part,
    moved, moved_rest, turned, weight_all, lot, tile, made,
    load_sem, fetch_sem, lot_sem, tile_sem, made_sem, out_sem, out_send, out_recv, out_pass_send, home_sem, home_send, home_recv,
    wide_send, wide_recv, line_send, line_recv, core_send, core_recv, row_send, row_recv,
    deal_send, deal_recv, mark_send, mark_recv, small_send, small_recv, dt_send, dt_recv, gain_send, gain_recv,
):
    shard, group = lax.axis_index("shard"), lax.axis_index("group")
    lines = shards // columns
    rows_y = groups // 2
    z, x = shard // columns, shard % columns
    y, core = group // 2, group % 2
    count = held.shape[0]
    parts = count // scales.shape[2]
    span = count // parts
    owned, depth = weight_out.shape
    piece, chunk = total.shape[0], CHUNK
    inner, shared = INNER // shards, SHARED // shards

    def load(src, dst):
        copy = pltpu.make_async_copy(src, dst, load_sem)
        copy.start()
        copy.wait()

    blocks, main, width = slots.shape[0], d_cols.shape[1], held.shape[1]
    per = BLOCK // shards
    fetch_weight = pltpu.make_async_copy(weight.at[pl.ds(0, main)], weight_all, fetch_sem)
    fetch_weight.start()

    lots = lot_sem.shape[0]

    def fetch_lot(turn):
        rows = pl.ds(turn * (lot.shape[0] // lots), lot.shape[0] // lots)
        return pltpu.make_async_copy(d_cols.at[rows], lot.at[rows], lot_sem.at[turn])

    tile_width = tile.shape[2]

    def fetch_tile(turn):
        lanes = pl.ds(turn * tile_width, tile_width)
        return pltpu.make_async_copy(normed.at[:, lanes], tile.at[turn % 2], tile_sem.at[turn % 2])

    for turn in range(lots):
        fetch_lot(turn).start()
    fetch_tile(0).start()
    barrier_with(
        [
            {"shard": (shard + step % shards) % shards, "group": (group + step // shards) % groups}
            for step in range(1, shards * groups)
        ]
    )

    def push_home(step):
        peer = (shard + step) % shards
        rows = no_rows.at[pl.ds(0, home.shape[0]), peer]
        return remote(rows, home_at, home_send.at[step], home_recv.at[step], shard=peer)

    home_at = home.at[:, :, pl.ds(pl.multiple_of(shard * inner, inner), inner)]

    for step in range(1, shards):
        push_home(step).start()
    home_here = pltpu.make_async_copy(no_rows.at[pl.ds(0, home.shape[0]), shard], home_at, home_sem)
    home_here.start()

    mate = y * 2 + 1 - core

    def core_copy(turn):
        return remote(piece_of(turn * 2 + 1 - core), core_in.at[turn], core_send.at[turn], core_recv.at[turn], group=mate)

    def piece_of(owner):
        return weight_part.at[pl.ds(pl.multiple_of(owner * piece, piece), piece)]

    out_lots, out_width = out_sem.shape[0], out_part.shape[1]
    out_rows = out_part.shape[0] // out_lots

    def out_place(part, turn):
        return out_full.at[pl.ds(turn * out_rows, out_rows), pl.ds(pl.multiple_of(part * out_width, out_width), out_width)]

    def out_here(turn):
        return pltpu.make_async_copy(out_part.at[pl.ds(turn * out_rows, out_rows)], out_place(group, turn), out_sem.at[turn])

    def out_copy(step, turn):
        peer = mate if step == 0 else (y + step) % rows_y * 2 + core
        rows = out_part.at[pl.ds(turn * out_rows, out_rows)]
        return remote(rows, out_place(group, turn), out_send.at[step, turn], out_recv.at[group, turn], group=peer)

    def out_pass(step, turn):
        part = (y + step) % rows_y * 2 + core
        return remote(
            out_place(part, turn), out_place(part, turn), out_pass_send.at[step, turn], out_recv.at[part, turn], group=mate
        )

    def out_from(part, turn):
        rows = out_part.at[pl.ds(turn * out_rows, out_rows)]
        return remote(rows, out_place(part, turn), out_send.at[0, turn], out_recv.at[part, turn], group=mate)

    def out_start(turns):
        for turn in turns:
            for step in range(1, rows_y):
                out_copy(step, turn).start()
            out_copy(0, turn).start()

    def out_forward(turns):
        for turn in turns:
            for step in range(1, rows_y):
                out_from((y + step) % rows_y * 2 + core, turn).wait_recv()
                out_pass(step, turn).start()

    def out_end():
        for turn in range(out_lots):
            for step in range(rows_y):
                out_copy(step, turn).wait_send()
                out_from(step * 2 + 1 - core, turn).wait_recv()
            for step in range(1, rows_y):
                out_pass(step, turn).wait_send()
            out_here(turn).wait()

    half = out_lots // 2
    out_start(range(half))
    for turn in range(out_lots):
        out_here(turn).start()

    for turn in range(blocks):
        if turn * lots % blocks == 0:
            fetch_lot(turn * lots // blocks).wait()
        rows = pl.ds(turn * BLOCK, BLOCK)
        place = place_of_rows(slots[turn])
        cols, rest = lot[rows, :], d_rest[rows, :]
        moved[:, turn] = dots(place, cols, ((0,), (0,))).astype(jnp.bfloat16).reshape(shards, per, main)
        moved_rest[:, turn] = dots(place, rest, ((0,), (0,))).astype(jnp.bfloat16).reshape(shards, per, rest.shape[1])
        turned[:main, rows] = cols.T
        turned[main:, rows] = rest.T
    fetch_weight.wait()

    def fetch(owner):
        cols, rest = moved[owner].reshape(count, main), moved_rest[owner].reshape(count, d_rest.shape[1])
        step = min(512, width)
        for lane in range(0, width, step):
            lanes = pl.ds(lane, step)
            found = dots(cols, weight_all[:, lanes], ((1,), (0,)))
            held[:, lanes] = found + dots(rest, weight_rest[:, lanes], ((1,), (0,)))

    def small_copy(step):
        return remote(small, small_in.at[step - 1], small_send.at[step - 1], small_recv.at[step - 1], group=(group + step) % groups)

    for step in range(1, groups):
        small_copy(step).start()

    def piece_of_rows(half):
        return held.at[pl.ds(half * span, span)]

    def code(coded_to, scales_to, values, lot=32):
        @pl.loop(0, values.shape[0] // lot, unroll=2)
        def _(turn):
            rows = pl.ds(pl.multiple_of(turn * lot, lot), lot)
            value = values[rows, :]
            most = jnp.maximum(jnp.max(jnp.abs(value), axis=1, keepdims=True), 1e-30)
            coded_to[rows, :] = jnp.round(value * (32767.0 / most)).astype(jnp.int32).astype(jnp.int16)
            marks[rows, :] = jnp.broadcast_to(most * (1.0 / 32767.0), (lot, 128))

        scales_to[...] = marks[: scales_to.shape[1], :].T[:8, :]

    def add(sums, coded_from, scales_from):
        marks[:span, :] = jnp.broadcast_to(scales_from[0:1, :], (128, span)).T

        @pl.loop(0, span // 32, unroll=2)
        def _(turn):
            rows = pl.ds(pl.multiple_of(turn * 32, 32), 32)
            sums[rows, :] += coded_from[rows, :].astype(jnp.float32) * marks[rows, 0:1]

    def place_of(step):
        return other_place(step, z, lines) if step < lines - 1 else z

    def wide_copies(step, half, hop):
        own = step * parts + half
        at = (hop - 1) * lines * parts + own
        peer = z * columns + (x + hop) % columns
        spot = place_of(step) * parts + half
        return (
            remote(coded.at[own], wide_in.at[hop - 1, spot], wide_send.at[0, at], wide_recv.at[0, at], shard=peer),
            remote(scales.at[own], wide_scale.at[hop - 1, spot], wide_send.at[1, at], wide_recv.at[1, at], shard=peer),
        )

    def send_wide(hop, steps):
        for step in steps:
            fetch(place_of(step) * columns + (x + hop) % columns)
            for half in range(parts):
                if hop > 1:
                    for copy in wide_copies(step, half, hop - 1):
                        copy.wait_send()
                code(coded.at[step * parts + half], scales.at[step * parts + half], piece_of_rows(half))
                for copy in wide_copies(step, half, hop):
                    copy.start()

    def row_copies(step):
        peer = (y + step) % rows_y * 2 + core
        return (
            remote(send_rows.at[step - 1], row_in.at[step - 1], row_send.at[0, step - 1], row_recv.at[0, step - 1], group=peer),
            remote(send_scales.at[step - 1], row_scale_in.at[step - 1], row_send.at[1, step - 1], row_recv.at[1, step - 1], group=peer),
        )

    def core_sum(turn):
        load(piece_of(turn * 2 + core), total)
        load(core_in.at[turn], other)

        @pl.loop(0, piece // chunk)
        def _(turn):
            rows = pl.ds(pl.multiple_of(turn * chunk, chunk), chunk)
            total[rows, :] += other[rows, :]

    early = min(2, lines)
    if columns > 1:
        send_wide(1, range(early))

    def store_made(turn):
        lanes = pl.ds(turn * tile_width, tile_width)
        return pltpu.make_async_copy(made.at[turn % 2], weight_part.at[:, lanes], made_sem.at[turn % 2])

    tiles = width // tile_width
    for turn in range(tiles):
        fetch_tile(turn).wait()
        if turn + 1 < tiles:
            fetch_tile(turn + 1).start()
        if turn >= 2:
            store_made(turn - 2).wait()
        made[turn % 2] = dots(turned[...], tile[turn % 2], ((1,), (0,)))
        store_made(turn).start()
    for turn in range(max(0, tiles - 2), tiles):
        store_made(turn).wait()
    for turn in range(rows_y):
        core_copy(turn).start()

    dt_own = weight_part.at[pl.ds(main + shared, HEADS // shards)]

    def dt_copy(step):
        return remote(dt_own, dt_in.at[step - 1], dt_send.at[step], dt_recv.at[step], group=(group + step) % groups)

    def dt_deal(step):
        at = groups + step
        peer = (shard + step) % shards
        lanes = pl.ds(pl.multiple_of(peer * depth, depth), depth)
        return remote(dt_sum.at[:, lanes], dt_out.at[shard], dt_send.at[at], dt_recv.at[at], shard=peer)

    for step in range(1, groups):
        dt_copy(step).start()
    if columns > 1:
        send_wide(1, range(early, lines))
    for hop in range(2, columns):
        send_wide(hop, range(lines))
    for turn in range(rows_y):
        core_copy(turn).wait_recv()
    for step in range(1, rows_y):
        core_sum((y + step) % rows_y)
        code(send_rows.at[step - 1], send_scales.at[step - 1], total, chunk)
        for copy in row_copies(step):
            copy.start()
    out_start(range(half, out_lots))
    core_sum(y)

    load(small, small_sum)
    for step in range(1, groups):
        small_copy(step).wait_recv()
        load(small_in.at[step - 1], small_got)
        small_sum[...] += small_got[...]

    def small_deal(step):
        return remote(small_sum, small_out.at[shard], small_send.at[groups + step], small_recv.at[groups + step], shard=(shard + step) % shards)

    load(dt_own, dt_sum)
    for step in range(1, groups):
        dt_copy(step).wait_recv()
        load(dt_in.at[step - 1], dt_got)
        dt_sum[...] += dt_got[...]
    for step in range(1, shards):
        small_deal(step).start()
        dt_deal(step).start()
    load(small_sum, small_out.at[shard])
    load(dt_sum.at[:, pl.ds(pl.multiple_of(shard * depth, depth), depth)], dt_out.at[shard])

    def line_copies(step, half):
        target = place_of(step)
        own = step * parts + half
        peer = jnp.where(target > z, z + 1, z - 1) * columns + x
        spot = jnp.where(target == z - 1, lines, target) * parts + half
        return (
            remote(line_coded.at[own], line_in.at[spot], line_send.at[0, own], line_recv.at[0, spot], shard=peer),
            remote(line_scales.at[own], line_scale.at[spot], line_send.at[1, own], line_recv.at[1, spot], shard=peer),
        )

    def take(way, target, half):
        source = jnp.where(way == 0, z - 1, z + 1)
        peer = jnp.clip(source, 0, lines - 1) * columns + x
        spot = jnp.where((way == 1) & (target == z), lines, target) * parts + half
        remote(line_coded.at[0], line_in.at[spot], line_send.at[0, 0], line_recv.at[0, spot], shard=peer).wait_recv()
        remote(line_scales.at[0], line_scale.at[spot], line_send.at[1, 0], line_recv.at[1, spot], shard=peer).wait_recv()
        add(piece_of_rows(half), line_in.at[spot], line_scale.at[spot])

    def gather_wide(step, half):
        spot = place_of(step) * parts + half
        for hop in range(1, columns):
            for copy in wide_copies(step, half, hop):
                copy.wait_recv()
            add(piece_of_rows(half), wide_in.at[hop - 1, spot], wide_scale.at[hop - 1, spot])

    def deal_copy(turn, step):
        first = group * piece + turn * chunk
        column = jnp.where(
            first < inner,
            inner * shard + first,
            jnp.where(first < 2 * inner, INNER + inner * shard + first - inner, 2 * INNER + shared * shard + first - 2 * inner),
        )
        owner = jnp.minimum(column // owned, groups - 1)
        peer = (shard + step) % shards
        source = deal_rows.at[
            pl.ds(pl.multiple_of(turn * chunk, chunk), chunk), pl.ds(pl.multiple_of(peer * depth, depth), depth)
        ]
        target = weight_out.at[pl.ds(pl.multiple_of(column - owner * owned, chunk), chunk)]
        real = first < 2 * inner + shared
        here = real & (owner == group) if step == 0 else None
        away = real & (owner != group) if step == 0 else real

        def near_copy():
            return pltpu.make_async_copy(source, target, deal_recv)

        def far():
            return remote(source, target, deal_send.at[turn, step], deal_recv, shard=peer, group=owner)

        return here, near_copy, away, far

    def deal():
        for step in range(1, rows_y):
            for copy in row_copies(step):
                copy.wait_recv()
            load(row_in.at[step - 1], row_got)
            load(row_scale_in.at[step - 1], row_scale_got)
            marks[: row_scale_got.shape[1], :] = jnp.broadcast_to(row_scale_got[0:1, :], (128, row_scale_got.shape[1])).T

            @pl.loop(0, piece // chunk)
            def _(turn):
                rows = pl.ds(pl.multiple_of(turn * chunk, chunk), chunk)
                total[rows, :] += row_got[rows, :].astype(jnp.float32) * marks[rows, 0:1]

        code(deal_rows, deal_scales, total, chunk)
        load(deal_scales, mark_out.at[shard, group])
        for step in range(1, groups):
            mark_copy(step).start()

    def deal_some(part, parts):
        chunks = piece // chunk

        @pl.loop(part * chunks // parts, (part + 1) * chunks // parts)
        def _(turn):
            for step in range(shards):
                here, near_copy, away, far = deal_copy(turn, step)
                if here is not None:
                    pl.when(here)(lambda: near_copy().start())
                pl.when(away)(lambda: far().start())

    def mark_copy(step):
        to = (group + step) % groups
        return remote(deal_scales, mark_out.at[shard, group], mark_send.at[step], mark_recv.at[step], group=to)

    def mark_spread(step):
        to, at = (shard + step) % shards, groups + step
        return remote(mark_out.at[shard], mark_out.at[shard], mark_send.at[at], mark_recv.at[at], shard=to)

    def mark_pass():
        for step in range(1, groups):
            mark_copy(step).wait_recv()
        for step in range(1, shards):
            mark_spread(step).start()

    def deal_end():
        for step in range(1, groups):
            mark_copy(step).wait_send()
        for step in range(1, shards):
            mark_spread(step).wait()

        @pl.when(group == groups - 1)
        def _():
            most = weight_out.at[pl.ds(0, owned - HEADS)]
            pltpu.make_async_copy(most, most, deal_recv).wait()

        @pl.when(group < groups - 1)
        def _():
            pltpu.make_async_copy(weight_out, weight_out, deal_recv).wait()

        @pl.loop(0, piece // chunk)
        def _(turn):
            for step in range(shards):
                _, _, away, far = deal_copy(turn, step)
                pl.when(away)(lambda: far().wait_send())

    for step in range(lines - 1):
        if step == min(1, lines - 2):
            deal()
            out_forward(range(half))
        target = place_of(step)
        way = jnp.where(target > z, 0, 1)
        fetch(target * columns + x)
        for half in range(parts):
            gather_wide(step, half)

            @pl.when(jnp.where(target > z, z > 0, z < lines - 1))
            def _():
                take(way, target, half)

            code(line_coded.at[step * parts + half], line_scales.at[step * parts + half], piece_of_rows(half))
            for copy in line_copies(step, half):
                copy.start()
        if step >= min(1, lines - 2):
            deal_some(step - min(1, lines - 2), lines - 1 - min(1, lines - 2))
    mark_pass()
    fetch(z * columns + x)
    for half in range(parts):
        gather_wide(lines - 1, half)

        @pl.when(z > 0)
        def _():
            take(0, z, half)

        @pl.when(z < lines - 1)
        def _():
            take(1, z, half)

    rows_out[...] = held[...]
    gain_sum[...] = jnp.zeros_like(gain_sum)

    @pl.loop(0, count // 8)
    def _(turn):
        rows = pl.ds(pl.multiple_of(turn * 8, 8), 8)
        gain_sum[...] += held[rows, :] * scaled_rows[rows, :]

    def gain_copy(step):
        return remote(gain_part, gain_in.at[step - 1], gain_send.at[step - 1], gain_recv.at[step - 1], shard=(shard + step) % shards)

    def gain_deal(step):
        at = shards - 1 + step - 1
        return remote(gain_out, gain_in.at[at], gain_send.at[at], gain_recv.at[at], group=(group + step) % groups)

    lanes = gain_out.shape[1]
    products = jnp.sum(gain_sum[...], axis=0, keepdims=True)
    gain_part[...] = jnp.concatenate([products[:, row * lanes : (row + 1) * lanes] for row in range(8)], axis=0)
    for step in range(1, shards):
        gain_copy(step).start()
    gain_out[...] = gain_part[...]
    out_forward(range(half, out_lots))
    for step in range(1, shards):
        gain_copy(step).wait_recv()
        gain_out[...] += gain_in[step - 1]
    for step in range(1, groups):
        gain_deal(step).start()
    for step in range(1, groups):
        gain_deal(step).wait_recv()
    for step in range(1, groups):
        gain_deal(step).wait_send()
    for step in range(1, groups):
        gain_out[...] += gain_in[shards - 1 + step - 1]

    for step in range(1, shards):
        gain_copy(step).wait_send()
        small_deal(step).wait()
        dt_deal(step).wait()
        push_home(step).wait()
    home_here.wait()
    for step in range(1, groups):
        small_copy(step).wait_send()
        dt_copy(step).wait_send()
    deal_end()
    out_end()
    for step in range(1, rows_y):
        for copy in row_copies(step):
            copy.wait_send()
    for turn in range(rows_y):
        core_copy(turn).wait_send()
    for half in range(parts):
        for step in range(lines):
            for copy in wide_copies(step, half, columns - 1) if columns > 1 else ():
                copy.wait_send()
        for step in range(lines - 1):
            for copy in line_copies(step, half):
                copy.wait_send()


def finish_exchange(
    shards, groups, slots, d_cols, d_rest, normed, weight, weight_rest, no_rows, out_part, small, scaled_rows, owned, depth
):
    columns = grid_columns(shards)
    lines, rows_y = shards // columns, groups // 2
    count, width = scaled_rows.shape
    blocks, main, rest = slots.shape[0], d_cols.shape[1], d_rest.shape[1]
    total, per, heads = blocks * BLOCK, BLOCK // shards, HEADS // shards
    piece = piece_rows(shards, groups)
    padded = -(-piece // 128) * 128
    small_shape = small.shape
    parts = 2
    coded, scale = (count // parts, width), (8, count // parts)
    any_space, vmem = pl.BlockSpec(memory_space=pl.ANY), pl.BlockSpec(memory_space=pltpu.VMEM)
    f32, i16, bf16 = jnp.float32, jnp.int16, jnp.bfloat16
    hops, turns, others = max(columns - 1, 1), max(rows_y - 1, 1), max(groups - 1, 1)
    lots, tile = 4, 256
    dma = pltpu.SemaphoreType.DMA
    out = pl.pallas_call(
        functools.partial(finish_kernel, shards, groups, columns),
        in_specs=[vmem, any_space, vmem, any_space, any_space, vmem, any_space, any_space, any_space, vmem],
        out_specs=[vmem] + [any_space] * 4 + [vmem] + [any_space] * 8 + [vmem],
        out_shape=[
            jax.ShapeDtypeStruct((count, width), f32),
            jax.ShapeDtypeStruct((owned, depth), i16),
            jax.ShapeDtypeStruct((shards, groups, 8, padded), f32),
            jax.ShapeDtypeStruct((shards,) + small_shape, f32),
            jax.ShapeDtypeStruct((shards, heads, depth), f32),
            jax.ShapeDtypeStruct((8, width // 8), f32),
            jax.ShapeDtypeStruct((blocks, per, INNER), bf16),
            jax.ShapeDtypeStruct((out_part.shape[0], out_part.shape[1] * groups), bf16),
            jax.ShapeDtypeStruct((main + rest, width), f32),
            jax.ShapeDtypeStruct((rows_y, piece, width), f32),
            jax.ShapeDtypeStruct((turns, piece, width), i16),
            jax.ShapeDtypeStruct((turns, 8, padded), f32),
            jax.ShapeDtypeStruct((others,) + small_shape, f32),
            jax.ShapeDtypeStruct((others, heads, width), f32),
            jax.ShapeDtypeStruct((shards - 1 + groups - 1, 8, width // 8), f32),
        ],
        scratch_shapes=[
            pltpu.VMEM((hops, lines * parts) + coded, i16),
            pltpu.VMEM((hops, lines * parts) + scale, f32),
            pltpu.VMEM(((lines + 1) * parts,) + coded, i16),
            pltpu.VMEM(((lines + 1) * parts,) + scale, f32),
            pltpu.VMEM((count, width), f32),
            pltpu.VMEM((lines * parts,) + coded, i16),
            pltpu.VMEM((lines * parts,) + scale, f32),
            pltpu.VMEM(((lines - 1) * parts,) + coded, i16),
            pltpu.VMEM(((lines - 1) * parts,) + scale, f32),
            pltpu.VMEM((max(count, padded), 128), f32),
            pltpu.VMEM((piece, width), f32),
            pltpu.VMEM((piece, width), f32),
            pltpu.VMEM((turns, piece, width), i16),
            pltpu.VMEM((turns, 8, padded), f32),
            pltpu.VMEM((piece, width), i16),
            pltpu.VMEM((8, padded), f32),
            pltpu.VMEM((piece, width), i16),
            pltpu.VMEM((8, padded), f32),
            pltpu.VMEM(small_shape, f32),
            pltpu.VMEM(small_shape, f32),
            pltpu.VMEM((heads, width), f32),
            pltpu.VMEM((heads, width), f32),
            pltpu.VMEM((8, width), f32),
            pltpu.VMEM((8, width // 8), f32),
            pltpu.VMEM((shards, blocks, per, main), bf16),
            pltpu.VMEM((shards, blocks, per, rest), bf16),
            pltpu.VMEM((main + rest, total), bf16),
            pltpu.VMEM((main, width), bf16),
            pltpu.VMEM((total, main), bf16),
            pltpu.VMEM((2, total, tile), bf16),
            pltpu.VMEM((2, main + rest, tile), f32),
            dma,
            dma,
            dma((2,)),
            dma((2,)),
            dma((2,)),
            dma((lots,)),
            dma((rows_y, lots)),
            dma((groups, lots)),
            dma((rows_y, lots)),
            dma,
            dma((shards,)),
            dma((shards,)),
            dma((2, hops * lines * parts)),
            dma((2, hops * lines * parts)),
            dma((2, lines * parts)),
            dma((2, (lines + 1) * parts)),
            dma((rows_y,)),
            dma((rows_y,)),
            dma((2, turns)),
            dma((2, turns)),
            dma((piece // CHUNK, shards)),
            dma,
            dma((shards + groups,)),
            dma((shards + groups,)),
            dma((groups + shards,)),
            dma((groups + shards,)),
            dma((groups + shards,)),
            dma((groups + shards,)),
            dma((shards + groups,)),
            dma((shards + groups,)),
        ],
        compiler_params=pltpu.CompilerParams(
            collective_id=7, has_side_effects=True, vmem_limit_bytes=62 * 1024 * 1024
        ),
        cost_estimate=pl.CostEstimate(flops=0, bytes_accessed=450_000_000, transcendentals=0),
        name="finish_exchange",
    )(slots, d_cols, d_rest, normed, weight, weight_rest, no_rows, out_part, small, scaled_rows)
    return out[:8]


def nesterov(weight, gradient, moment, average, step_rate):
    decayed = gradient + weight_decay * weight
    new_moment = momentum_decay * moment + decayed
    new_weight = weight - step_rate * (decayed + momentum_decay * new_moment)
    new_average = average_decay * average + (1.0 - average_decay) * new_weight
    return (new_moment, new_weight, new_average)


def dot32(a, b, contract=((1,), (0,))):
    return lax.dot_general(a, b, (contract, ((), ())), preferred_element_type=jnp.float32)


def own_slice(value, index, width, axis):
    return lax.dynamic_slice_in_dim(value, index * width, width, axis)


def local(
    tokens,
    cotangent,
    lengths,
    deal_slot,
    in_weight,
    out_weight,
    small_params,
    in_moment,
    out_moment,
    small_moment,
    in_average,
    out_average,
    small_average,
):
    shards, groups = lax.axis_size("shard"), lax.axis_size("group")
    shard, group = lax.axis_index("shard"), lax.axis_index("group")
    rows, width = tokens.shape
    per = rows // shards
    total = rows * shards
    blocks = total // BLOCK
    heads = HEADS // shards
    inner = INNER // shards
    shared = SHARED // shards
    conv_flat, conv_bias, dt_bias, rate_log, skip_gain, norm_gain, pre_gain = unpack(small_params)
    taps = conv_flat.reshape(CONV, XBC)

    cols, depth, sends = in_weight.shape[1], in_weight.shape[0], out_weight.shape[1]
    direct = cols % CHUNK == 0 and depth % 128 == 0 and sends % 128 == 0 and per % CHUNK == 0
    direct = direct and (2 * inner + SHARED + HEADS) % (groups * CHUNK) == 0 and shared % CHUNK == 0
    bounds = jnp.cumsum(lengths[0])[:-1].astype(jnp.int32)
    seg_rows = segment_of(jnp.arange(total, dtype=jnp.int32), lengths[0])

    rank = jnp.sum((deal_slot[None, :] < deal_slot[:, None]).astype(jnp.int32), axis=1)
    sort_mat = (rank[None, :] == jnp.arange(rows)[:, None]).astype(jnp.bfloat16)
    r_in = lax.rsqrt(jnp.mean(tokens * tokens, axis=1, keepdims=True) + eps_norm)
    in_turned = in_weight.T

    if direct:
        x_all, in_low, out_low, slot_all, c_sorted, out_cast, x_scaled = front_exchange(
            shards, groups, tokens, pre_gain, cotangent, in_turned, out_weight, deal_slot
        )
        x_all = x_all.reshape(blocks, BLOCK, width)
        slot_all = slot_all[:, 0, :]
    else:
        sorted_slot = jnp.sum(jnp.where(sort_mat > 0, deal_slot[None, :], 0), axis=1)
        x_scaled = jnp.dot(sort_mat.astype(jnp.float32), tokens * r_in, precision=lax.Precision.HIGHEST)
        normed_low = (tokens * r_in * pre_gain[None, :]).astype(jnp.bfloat16)
        x_sorted = dot32(sort_mat, normed_low).astype(jnp.bfloat16).reshape(blocks, per, width)
        c_sorted = dot32(sort_mat, cotangent.astype(jnp.bfloat16)).astype(jnp.bfloat16)
        c_sorted = c_sorted.reshape(blocks, per, width)
        in_turned = in_turned.astype(jnp.bfloat16)
        out_cast = out_weight.astype(jnp.bfloat16)
        x_all = lax.all_gather(x_sorted, "shard").transpose(1, 0, 2, 3).reshape(blocks, BLOCK, width)
        slot_all = lax.all_gather(sorted_slot, "shard")
        part = depth // groups
        pieces = lax.all_to_all(in_turned.reshape(cols, groups, part), "group", 1, 0)
        pieces = pieces.reshape(groups * cols, part)

        def cut(lo, each):
            return pieces[lo : lo + each * shards].reshape(shards, each, part)

        spread = jnp.broadcast_to(pieces[None, 2 * INNER :], (shards, SHARED + HEADS, part))
        got = jnp.concatenate([cut(0, inner), cut(INNER, inner), spread], axis=1)
        got = lax.all_gather(lax.all_to_all(got, "shard", 0, 0), "group")
        in_low = got.transpose(2, 1, 0, 3).reshape(-1, width)
        out_low = lax.all_gather(out_cast, "group", axis=1, tiled=True)
    slot_blk = slot_all.reshape(shards, blocks, per).transpose(1, 0, 2).reshape(blocks, 1, BLOCK)
    slot_blk = slot_blk - jnp.arange(blocks, dtype=jnp.int32)[:, None, None] * BLOCK

    taps_v = own_slice(taps[:, :INNER], shard, inner, 1)
    taps_all = jnp.concatenate([taps_v, taps[:, INNER:]], axis=1)
    bias_all = jnp.concatenate([own_slice(conv_bias[:INNER], shard, inner, 0), conv_bias[INNER:]])[None, :]
    skip_wide = jnp.repeat(own_slice(skip_gain, shard, heads, 0), HDIM)[None, :]
    gain_own = own_slice(norm_gain, shard, inner, 0)[None, :]
    padding = max(TAIL - heads, 0)
    rate = jnp.pad(-jnp.exp(own_slice(rate_log, shard, heads, 0)), (0, padding))[:, None]
    normed, projected, pre, mixed, states, dt_cols, dt_raw, c_all = mixer_forward(
        shards, bounds, slot_blk, x_all, in_low, taps_all, bias_all, dt_bias[None, :], rate, skip_wide, c_sorted
    )
    conv_bc = lax.dynamic_slice_in_dim(projected, 2 * inner + shard * shared, shared, 1)
    cot_low, d_out, sums = pack_cotangent(
        shards, slot_blk, c_all.reshape(blocks, BLOCK, width), out_low, mixed, projected, gain_own
    )

    r_out = lax.rsqrt(sums[0][:, None] + eps_norm)
    normed_out = (mixed * jax.nn.silu(projected[:, :inner]) * r_out * gain_own).astype(jnp.bfloat16)
    grad_out = dot32(normed_out, cot_low, ((0,), (0,)))
    grad_out, mixed = lax.optimization_barrier((grad_out, mixed))
    grad_out = lax.psum_scatter(grad_out, "group", scatter_dimension=1, tiled=True)
    d_cols, d_bc, d_dt, grads, rate_terms, no_rows, out_full = mixer_backward(
        shards, bounds, slot_blk, pre, mixed, projected, d_out, sums, states, dt_cols,
        taps_v, rate, skip_wide, gain_own, out_cast[None],
    )
    out_block = out_full.reshape(INNER, -1)

    d_dtraw = d_dt[:heads].T * jax.nn.sigmoid(dt_raw[:, :heads])
    grad_dtb = jnp.sum(d_dtraw, axis=0)
    grad_rate = jnp.sum(rate_terms[:heads], axis=1)
    grad_skip = jnp.sum(grads[6].reshape(heads, HDIM), axis=1)
    _, pull_bc = jax.vjp(
        lambda c, t, b: convolve(c, seg_rows, t, b),
        conv_bc,
        own_slice(taps[:, INNER:], shard, shared, 1),
        own_slice(conv_bias[INNER:], shard, shared, 0),
    )
    d_conv_bc, grad_taps_bc, grad_bias_bc = pull_bc(d_bc.T)
    rest = 128 - shared - heads
    d_rest = jnp.concatenate([d_conv_bc, d_dtraw, jnp.zeros((total, rest), jnp.float32)], axis=1)
    in_rest = jnp.concatenate(
        [
            own_slice(in_low[2 * inner : 2 * inner + SHARED], shard, shared, 0),
            own_slice(in_low[2 * inner + SHARED :], shard, heads, 0),
            jnp.zeros((rest, width), jnp.bfloat16),
        ]
    )

    mine = [
        grads[:CONV].reshape(-1),
        grad_taps_bc.reshape(-1),
        grads[4],
        grad_bias_bc,
        grad_dtb,
        grad_rate,
        grad_skip,
        grads[5],
    ]
    extents = [piece.shape[0] for piece in mine]
    mine = jnp.concatenate(mine)
    mine = jnp.pad(mine, (0, -mine.shape[0] % 1024)).reshape(-1, 128)
    d_rest = d_rest.astype(jnp.bfloat16)
    if direct:
        d_normed, grad_in, grad_marks, small_all, dt_part, gain_all, home, out_full = finish_exchange(
            shards, groups, slot_blk, d_cols, d_rest, normed, in_low, in_rest, no_rows, out_block, mine, x_scaled,
            cols, depth,
        )
    else:
        partial, weight_part, home = project_back(
            slot_blk, d_cols, d_rest, normed, in_low, in_rest, no_rows, shards
        )
        out_full = lax.all_gather(out_block, "group", axis=1, tiled=True)
        d_normed, _, _, small_all, gain_all = tail_exchange(
            shards, groups, partial.reshape(shards, rows, width), weight_part, mine, x_scaled, cols, depth, False
        )

    home = home.reshape(rows, INNER)
    home = dot32(sort_mat, home, ((0,), (0,))).astype(jnp.bfloat16)
    block_out = tokens + dot32(home, out_full)
    d_normed = jnp.dot(sort_mat.T.astype(jnp.float32), d_normed, precision=lax.Precision.HIGHEST)
    d_scaled = pre_gain[None, :] * d_normed
    inside = jnp.mean(tokens * d_scaled, axis=1, keepdims=True)
    input_grad = cotangent + r_in * (d_scaled - tokens * (r_in * r_in) * inside)
    grad_pre = gain_all.reshape(width)

    mine = small_all.reshape(shards, -1)
    found, offset = [], 0
    for extent in extents:
        found.append(mine[:, offset : offset + extent])
        offset = offset + extent
    if direct:
        dt_part = dt_part.reshape(HEADS, depth)
        steps = grad_marks[:, :, 0, : piece_rows(shards, groups)].reshape(shards, -1)
        steps = jnp.concatenate(
            [
                steps[:, :inner].reshape(-1),
                steps[:, inner : 2 * inner].reshape(-1),
                steps[:, 2 * inner : 2 * inner + shared].reshape(-1),
                jnp.zeros((HEADS,), jnp.float32),
            ]
        )
        grad_in = grad_in.astype(jnp.float32) * own_slice(steps, group, cols, 0)[:, None]
        last = jnp.concatenate([grad_in[: cols - HEADS], dt_part])
        grad_in = jnp.where(group == groups - 1, last, grad_in)
    else:
        used = 2 * inner + shared + heads
        grad_in = weight_part[:used].reshape(used, shards, groups, part).transpose(2, 1, 0, 3)
        grad_in = lax.psum_scatter(grad_in, "group", scatter_dimension=0)
        grad_in = lax.all_to_all(grad_in, "shard", 0, 0)

        def join(lo, each):
            return grad_in[:, lo : lo + each].reshape(shards * each, part)

        grad_in = jnp.concatenate(
            [
                join(0, inner),
                join(inner, inner),
                join(2 * inner, shared),
                join(2 * inner + shared, heads),
            ]
        )
        grad_in = lax.all_to_all(grad_in.reshape(groups, cols, part), "group", 0, 0)
        grad_in = grad_in.transpose(1, 0, 2).reshape(cols, depth)

    def taps_of(piece):
        return piece.reshape(shards, CONV, -1).transpose(1, 0, 2).reshape(CONV, -1)

    grad_taps = jnp.concatenate([taps_of(found[0]), taps_of(found[1])], axis=1).reshape(-1)
    grad_small = jnp.concatenate([grad_taps] + [piece.reshape(-1) for piece in found[2:]] + [grad_pre])
    in_new = nesterov(in_weight.T, grad_in, in_moment.T, in_average.T, rate_in)
    in_new = tuple(value.T for value in in_new)
    out_new = nesterov(out_weight, grad_out, out_moment, out_average, rate_out)
    small_new = nesterov(small_params, grad_small, small_moment, small_average, rate_small)
    return (block_out, input_grad) + in_new + out_new + small_new


def solution(mesh):
    rows = P(("group", "shard"), None)
    tile = P("shard", "group")
    return jax.shard_map(
        local,
        mesh=mesh,
        in_specs=(
            rows,
            rows,
            P("group", None),
            P(("group", "shard")),
            tile,
            tile,
            P(),
            tile,
            tile,
            P(),
            tile,
            tile,
            P(),
        ),
        out_specs=(rows, rows, tile, tile, tile, tile, tile, tile, P(), P(), P()),
        check_vma=False,
    )
```

```python
import functools

import jax
import jax.numpy as jnp
from jax import lax
from jax.experimental import pallas as pl
from jax.experimental.pallas import tpu as pltpu
from jax.sharding import PartitionSpec as P

D = 2048
HEADS = 64
HDIM = 64
STATE = 128
CONV = 4
BLOCK = 256
INNER = 4096
XBC = 4352
SHARED = 2 * STATE
TAIL = 8
CHUNK = 16
MESH = pl.DeviceIdType.MESH


eps_norm = 1e-05
momentum_decay = 0.9
weight_decay = 0.01
average_decay = 0.99
rate_in = 0.0001
rate_out = 3e-05
rate_small = 0.001


def unpack(packed_small):
    extents = [CONV * XBC, XBC, HEADS, HEADS, HEADS, INNER, D]
    pieces = []
    offset = 0
    for extent in extents:
        pieces.append(packed_small[offset : offset + extent])
        offset = offset + extent
    return pieces


def segment_of(positions, lengths_row):
    bounds = jnp.cumsum(lengths_row)[:-1]
    inside = jnp.sum((positions[:, None] >= bounds[None, :]).astype(jnp.int32), axis=1)
    return jnp.where(positions < 0, -1, inside)


def convolve(conv_rows, seg_rows, conv_taps, conv_bias):
    row_count, width = conv_rows.shape
    extended = jnp.concatenate([jnp.zeros((CONV - 1, width), conv_rows.dtype), conv_rows], axis=0)
    seg_ext = jnp.concatenate([jnp.full((CONV - 1,), -1, jnp.int32), seg_rows], axis=0)
    conv_sum = jnp.zeros_like(conv_rows) + conv_bias[None, :]
    for tap_index in range(CONV):
        same_seq = (seg_ext[tap_index : tap_index + row_count] == seg_rows)[:, None]
        conv_sum = conv_sum + jnp.where(
            same_seq,
            extended[tap_index : tap_index + row_count] * conv_taps[tap_index][None, :],
            0.0,
        )
    return jax.nn.silu(conv_sum)


def split(value):
    high = value.astype(jnp.bfloat16)
    return high, (value - high.astype(jnp.float32)).astype(jnp.bfloat16)


def dots(a, b, contract):
    return lax.dot_general(a, b, (contract, ((), ())), preferred_element_type=jnp.float32)


def dot3(a, b, contract=((1,), (0,))):
    a = a if isinstance(a, tuple) else split(a)
    b = b if isinstance(b, tuple) else split(b)
    return dots(a[0], b[0], contract) + (dots(a[0], b[1], contract) + dots(a[1], b[0], contract))


NT = ((1,), (1,))


def dot_wide(a, wide):
    high, low = split(a)
    lanes = wide.shape[1] // 2
    plain = ((1,), (0,))
    first = dots(high, wide, plain)
    return first[:, :lanes] + (first[:, lanes:] + dots(low, wide[:, :lanes], plain))


def beside(first, second, own):
    moved = pltpu.roll(second.astype(jnp.float32), HDIM, 1).astype(jnp.bfloat16)
    return jnp.where(own, first, moved)


def head_sums(value, marks):
    high = value.astype(jnp.bfloat16)
    rest = value - high.astype(jnp.float32)
    mid = rest.astype(jnp.bfloat16)
    low = (rest - mid.astype(jnp.float32)).astype(jnp.bfloat16)
    return dots(marks, high, NT) + (dots(marks, mid, NT) + dots(marks, low, NT))


def widen(columns, heads):
    rows = columns.shape[0]
    low_half = lax.broadcasted_iota(jnp.int32, (rows, 2 * HDIM), 1) < HDIM
    return jnp.concatenate(
        [
            jnp.where(low_half, columns[:, h : h + 1], columns[:, h + 1 : h + 2])
            for h in range(0, heads, 2)
        ],
        axis=1,
    )


def running_sum(value, reverse=False):
    lane = lax.broadcasted_iota(jnp.int32, value.shape, 1)
    count = value.shape[1]
    step = 1
    while step < count:
        if reverse:
            value = value + jnp.where(lane < count - step, pltpu.roll(value, count - step, 1), 0.0)
        else:
            value = value + jnp.where(lane >= step, pltpu.roll(value, step, 1), 0.0)
        step *= 2
    return value


def sequence_of(positions, bounds):
    inside = jnp.where(positions >= bounds[0], 1, 0) + jnp.where(positions >= bounds[1], 1, 0)
    return jnp.where(positions < 0, -1, inside)


def block_facts(block, bounds, dt_t, rate):
    start = block * BLOCK
    seg_col = sequence_of(start + lax.broadcasted_iota(jnp.int32, (BLOCK, 1), 0), bounds)
    seg_row = sequence_of(start + lax.broadcasted_iota(jnp.int32, (1, BLOCK), 1), bounds)
    before = sequence_of(start - 1 + lax.broadcasted_iota(jnp.int32, (1, 1), 1), bounds)
    last = sequence_of(start + BLOCK - 1 + lax.broadcasted_iota(jnp.int32, (1, 1), 1), bounds)
    run_t = running_sum(dt_t * rate)
    run = run_t.T
    final = run[BLOCK - 1 :, :]
    carried = jnp.where(seg_col == before, jnp.exp(run), 0.0)
    tail = jnp.where(seg_col == last, jnp.exp(final - run), 0.0)
    keep = jnp.where(last == before, jnp.exp(final), 0.0)
    return seg_col, seg_row, run_t, run, carried, tail, keep


def barrier_with(peers):
    barrier = pltpu.get_barrier_semaphore()
    for peer in peers:
        pl.semaphore_signal(barrier, inc=1, device_id=peer, device_id_type=MESH)
    pl.semaphore_wait(barrier, len(peers))


def remote(src, dst, sends, recvs, **where):
    return pltpu.make_async_remote_copy(
        src_ref=src, dst_ref=dst, send_sem=sends, recv_sem=recvs, device_id=where, device_id_type=MESH
    )


def place_of_rows(slots):
    count = slots.shape[1]
    return (lax.broadcasted_iota(jnp.int32, (BLOCK, count), 0) == slots).astype(jnp.bfloat16)


def grid_columns(shards):
    columns = 1
    while 2 * (2 * columns) * (2 * columns) <= shards:
        columns *= 2
    return columns if shards % columns == 0 else 1


def whole(shape):
    return pl.BlockSpec(shape, lambda *_: (0,) * len(shape))


def row_gather(shards, columns, own, gathered, local_sem, sends, recvs):
    shard = lax.axis_index("shard")
    lines = shards // columns
    z, x = shard // columns, shard % columns

    def line_copy(source, way, first=False):
        at = source * columns + x
        peer = jnp.clip(z + 1 - 2 * way, 0, lines - 1) * columns + x
        rows = own if first else gathered.at[:, at]
        return remote(rows, gathered.at[:, at], sends.at[way, source], recvs.at[at], shard=peer)

    def wide_copy(source, hop, first=False):
        at = source * columns + x
        peer = z * columns + (x + hop) % columns
        rows = own if first else gathered.at[:, at]
        return remote(rows, gathered.at[:, at], sends.at[1 + hop, source], recvs.at[at], shard=peer)

    def pass_on(source, ways, first=False):
        for way in ways:
            @pl.when(z < lines - 1 if way == 0 else z > 0)
            def _():
                line_copy(source, way, first).start()

        for hop in range(1, columns):
            wide_copy(source, hop, first).start()

    here = pltpu.make_async_copy(own, gathered.at[:, shard], local_sem)

    def begin():
        pass_on(z, (0, 1), True)
        here.start()

    def hop(step):
        @pl.when(z - step >= 0)
        def _():
            line_copy(z - step, 0).wait_recv()
            pass_on(z - step, (0,))

        @pl.when(z + step < lines)
        def _():
            line_copy(z + step, 1).wait_recv()
            pass_on(z + step, (1,))

    def end():
        here.wait()
        for step in range(1, columns):
            peer = z * columns + (x + step) % columns
            for source in range(lines):
                at = source * columns + (x + step) % columns
                remote(gathered.at[:, at], gathered.at[:, at], sends.at[1 + step, source], recvs.at[at], shard=peer).wait_recv()
        for source in range(lines):
            for step in range(1, columns):
                wide_copy(source, step).wait_send()

            @pl.when((z < lines - 1) & (source <= z))
            def _():
                line_copy(source, 0).wait_send()

            @pl.when((z > 0) & (source >= z))
            def _():
                line_copy(source, 1).wait_send()

    return begin, hop, end


def gather_semaphores(shards, columns):
    dma = pltpu.SemaphoreType.DMA
    return [
        dma,
        dma((1 + columns, shards // columns)),
        dma((shards,)),
    ]


def softplus(value):
    small = jnp.exp(-jnp.abs(value))
    ratio = small / (2.0 + small)
    square = ratio * ratio
    series = jnp.full_like(value, 1.0 / 15.0)
    for power in (13, 11, 9, 7, 5, 3, 1):
        series = series * square + 1.0 / power
    return jnp.maximum(value, 0.0) + 2.0 * ratio * series


def pick_columns(value, marks):
    high = value.astype(jnp.bfloat16)
    rest = value - high.astype(jnp.float32)
    mid = rest.astype(jnp.bfloat16)
    low = (rest - mid.astype(jnp.float32)).astype(jnp.bfloat16)
    plain = ((1,), (0,))
    return dots(high, marks, plain) + (dots(mid, marks, plain) + dots(low, marks, plain))


def forward_kernel(
    heads, shards, columns, bounds, slots, rows_in, weight, taps, bias, dt_bias, rate, skip, cot_own,
    packed, product, pre_out, mixed_out, state_out, dt_out, raw_out, cot_all,
    ext, state, *gather_sems,
):
    block = pl.program_id(0)
    blocks = cot_own.shape[0]
    inner = heads * HDIM
    shard = lax.axis_index("shard")
    begin, hop, end = row_gather(shards, columns, cot_own, cot_all, *gather_sems)
    hops = range(1, shards // columns)

    @pl.when(block == 0)
    def _():
        barrier_with([{"shard": (shard + step) % shards} for step in range(1, shards)])
        begin()
        ext[:TAIL, :] = jnp.zeros((TAIL, ext.shape[1]), jnp.float32)
        state[...] = jnp.zeros_like(state)

    for step in hops:
        if (7 * step + 1) // 2 < blocks:
            pl.when(block == (7 * step + 1) // 2)(functools.partial(hop, step))

    normed = dots(place_of_rows(slots[0]), rows_in[0], ((1,), (0,))).astype(jnp.bfloat16)
    packed[...] = normed
    product[...] = dots(normed, weight[...], NT)
    head = lax.broadcasted_iota(jnp.int32, (HEADS, 128), 0)
    lane = lax.broadcasted_iota(jnp.int32, (HEADS, 128), 1)
    marks = ((head == shard * heads + lane) & (lane < heads)).astype(jnp.bfloat16)
    raw = pick_columns(product[:, 2 * inner + SHARED :] + dt_bias[...], marks)
    raw_out[...] = raw
    dt = softplus(raw)
    dt_out[...] = dt

    bounds = (bounds[0], bounds[1])
    dt_t = dt.T[: rate.shape[0], :]
    seg_col, seg_row, run_t, run, carried, tail, keep = block_facts(block, bounds, dt_t, rate[...])
    ext[TAIL:, :] = product[:, inner : 2 * inner + SHARED]
    place = block * BLOCK + lax.broadcasted_iota(jnp.int32, (BLOCK, 1), 0)
    pre = bias[...] + taps[CONV - 1 : CONV, :] * ext[TAIL:, :]
    for back in range(1, CONV):
        same = sequence_of(place - back, bounds) == seg_col
        moved = ext[TAIL - back : TAIL - back + BLOCK, :]
        pre = pre + jnp.where(same, moved, 0.0) * taps[CONV - 1 - back : CONV - back, :]
    ext[:TAIL, :] = ext[BLOCK:, :]
    pre_out[...] = pre
    conv = pre / (1.0 + jnp.exp(-pre))
    values, b_rows, c_rows = conv[:, :inner], conv[:, inner : inner + STATE], conv[:, inner + STATE :]
    fed = values * widen(dt, heads)
    rows = lax.broadcasted_iota(jnp.int32, (BLOCK, BLOCK), 0)
    cols = lax.broadcasted_iota(jnp.int32, (BLOCK, BLOCK), 1)
    allowed = (seg_col == seg_row) & (rows >= cols)
    b_parts, c_parts = split(b_rows), split(c_rows)
    scores = jnp.where(allowed, dot3(c_parts, b_parts, NT), 0.0)
    old = state[...]
    state_out[0] = old
    output = widen(carried, heads) * dot3(c_parts, old)
    low_half = lax.broadcasted_iota(jnp.int32, (BLOCK, 2 * HDIM), 1) < HDIM
    inside = []
    for h in range(0, heads, 2):
        pair = jnp.concatenate(split(fed[:, h * HDIM : (h + 2) * HDIM]), axis=1)
        found = []
        for k in (h, h + 1):
            mixing = jnp.exp(jnp.minimum(run[:, k : k + 1] - run_t[k : k + 1, :], 0.0)) * scores
            found.append(dot_wide(mixing, pair))
        inside.append(jnp.where(low_half, found[0], found[1]))
    mixed = output + jnp.concatenate(inside, axis=1) + skip[...] * values
    mixed_out[...] = mixed
    state[...] = widen(keep, heads) * old + dot3(b_rows.T, widen(tail, heads) * fed)

    @pl.when(block == blocks - 1)
    def _():
        for step in hops:
            if (7 * step + 1) // 2 >= blocks:
                hop(step)
        end()


def cotangent_kernel(
    shards, slots, rows_in, weight, mixed, gate, gain,
    packed, product, sums_out, own_sums, sums_in, sums_send, sums_recv,
):
    block = pl.program_id(0)
    shard = lax.axis_index("shard")

    @pl.when(block == 0)
    def _():
        barrier_with([{"shard": (shard + step) % shards} for step in range(1, shards)])

    several = rows_in.shape[0]
    for turn in range(several):
        rows = pl.ds(turn * BLOCK, BLOCK)
        packed[rows, :] = dots(place_of_rows(slots[turn]), rows_in[turn], ((1,), (0,))).astype(jnp.bfloat16)
    d_out = dots(packed[...], weight[...], NT)
    product[...] = d_out
    gate_now = gate[...]
    gated = mixed[...] * (gate_now / (1.0 + jnp.exp(-gate_now)))
    squares = jnp.sum(gated * gated, axis=1, keepdims=True)
    products = jnp.sum(gated * gain[...] * d_out, axis=1, keepdims=True)
    lane = lax.broadcasted_iota(jnp.int32, (several * BLOCK, 128), 1)
    both = jnp.where(lane == 0, squares, jnp.where(lane == 1, products, 0.0))
    here = pl.ds(pl.multiple_of(block * several * BLOCK, BLOCK), several * BLOCK)
    own_sums[:, here] = both.T[:8, :]

    def push(step, at):
        return remote(
            own_sums.at[:, at], sums_in.at[step - 1, :, at], sums_send.at[step], sums_recv.at[step],
            shard=(shard + step) % shards,
        )

    for step in range(1, shards):
        push(step, here).start()

    @pl.when(block == pl.num_programs(0) - 1)
    def _():
        everything = pl.ds(0, own_sums.shape[1])
        for step in range(1, shards):
            push(step, everything).wait()
        found = own_sums[...]
        for step in range(1, shards):
            found = found + sums_in[step - 1]
        sums_out[...] = found * (1.0 / INNER)


def backward_kernel(
    heads, blocks, shards, columns, bounds, slots, pre, mixed, gate, d_out, conv_v, sums, state_in, dt_cols,
    taps, rate, skip, gain, marks, out_own,
    d_cols, d_bc, d_dt, grads, grad_rate, no_rows, out_all,
    ext, carry, bc_rows, bc_wide, bc_sum, bc_in, wide_send, wide_recv, bc_send, bc_recv, *gather_sems,
):
    step = pl.program_id(0)
    block = blocks - 1 - step
    inner = heads * HDIM
    shard = lax.axis_index("shard")
    shared = SHARED // shards
    lines = shards // columns
    z, x = shard // columns, shard % columns
    begin, hop, end = row_gather(shards, columns, out_own, out_all, *gather_sems)
    hops = range(1, shards // columns)

    @pl.when(step == 0)
    def _():
        barrier_with([{"shard": (shard + turn) % shards} for turn in range(1, shards)])
        begin()
        ext[BLOCK:, :] = jnp.zeros((TAIL, ext.shape[1]), jnp.float32)
        carry[...] = jnp.zeros_like(carry)
        grads[...] = jnp.zeros_like(grads)
        grad_rate[...] = jnp.zeros_like(grad_rate)

    for turn in hops:
        if 2 * turn < blocks:
            pl.when(step == 2 * turn)(functools.partial(hop, turn))

    bounds = (bounds[0], bounds[1])
    dt = dt_cols[...]
    dt_t = dt.T[: rate.shape[0], :]
    seg_col, seg_row, run_t, run, carried, tail, keep = block_facts(block, bounds, dt_t, rate[...])
    sums_cols = sums[...].T
    r_out = lax.rsqrt(sums_cols[:, 0:1] + 1e-05)
    inside = sums_cols[:, 1:2]
    gate_now = gate[...]
    gate_sig = 1.0 / (1.0 + jnp.exp(-gate_now))
    act = gate_now * gate_sig
    mixed_now = mixed[...]
    gated = mixed_now * act
    d_out_now = d_out[...]
    normed_out = (gated * r_out * gain[...]).astype(jnp.bfloat16)
    to_home = dots(place_of_rows(slots[0]), normed_out, ((0,), (0,)))
    per = BLOCK // shards
    if per % 16 == 0:
        no_rows[0] = to_home.astype(jnp.bfloat16).reshape(shards, per, inner)
    else:
        for turn in range(shards):
            no_rows[0, turn] = to_home[turn * per : (turn + 1) * per].astype(jnp.bfloat16)
    d_gated = r_out * (gain[...] * d_out_now - gated * (r_out * r_out) * inside)
    dy = d_gated * act
    d_cols[:, :inner] = (d_gated * mixed_now * (gate_sig * (1.0 + gate_now * (1.0 - gate_sig)))).astype(jnp.bfloat16)
    grads[5:6, :] += jnp.sum(gated * r_out * d_out_now, axis=0, keepdims=True)
    pre_now = pre[...]
    sig = 1.0 / (1.0 + jnp.exp(-pre_now))
    conv = pre_now * sig
    values, b_rows, c_rows = conv[:, :inner], conv[:, inner : inner + STATE], conv[:, inner + STATE :]
    grads[6:7, :] += jnp.sum(dy * values, axis=0, keepdims=True)
    dt_wide = widen(dt, heads)
    fed = values * dt_wide
    old, after = state_in[0], carry[...]
    b_parts, c_parts, old_parts, after_parts = split(b_rows), split(c_rows), split(old), split(after)
    carried_wide, tail_wide, keep_wide = widen(carried, heads), widen(tail, heads), widen(keep, heads)
    rows = lax.broadcasted_iota(jnp.int32, (BLOCK, BLOCK), 0)
    cols = lax.broadcasted_iota(jnp.int32, (BLOCK, BLOCK), 1)
    allowed = (seg_col == seg_row) & (cols >= rows)
    scores_t = jnp.where(allowed, dot3(b_parts, c_parts, NT), 0.0)
    low_half = lax.broadcasted_iota(jnp.int32, (BLOCK, 2 * HDIM), 1) < HDIM
    d_scores_t = jnp.zeros((BLOCK, BLOCK), jnp.float32)
    d_fed, row_terms, col_terms = [], [], []
    for h in range(0, heads, 2):
        fed_pair = fed[:, h * HDIM : (h + 2) * HDIM]
        fed_high, fed_low = split(fed_pair)
        dy_high, dy_low = split(dy[:, h * HDIM : (h + 2) * HDIM])
        dy_wide = jnp.concatenate([dy_high, dy_low], axis=1)
        found = []
        for k in (h, h + 1):
            own = low_half if k == h else jnp.logical_not(low_half)
            left = jnp.concatenate(
                [beside(fed_high, fed_low, own), jnp.where(own, fed_high, 0.0).astype(jnp.bfloat16)], axis=1
            )
            right = jnp.concatenate([beside(dy_high, dy_high, own), dy_low], axis=1)
            d_mixing = dots(left, right, NT)
            decay = jnp.exp(jnp.minimum(run_t[k : k + 1, :] - run[:, k : k + 1], 0.0))
            mixing = decay * scores_t
            d_scores_t = d_scores_t + decay * d_mixing
            flow = mixing * d_mixing
            row_terms.append(jnp.sum(flow, axis=0, keepdims=True))
            col_terms.append(jnp.sum(flow, axis=1, keepdims=True))
            found.append(dot_wide(mixing, dy_wide))
        d_fed.append(jnp.where(low_half, found[0], found[1]))
    d_scores_t = split(jnp.where(allowed, d_scores_t, 0.0))
    fed_tail = fed * tail_wide
    dy_carried = dy * carried_wide
    d_fed_out = tail_wide * dot3(b_parts, after_parts)
    d_fed = jnp.concatenate(d_fed, axis=1) + d_fed_out
    dy_parts, tail_parts = split(dy_carried), split(fed_tail)
    here = pl.ds(pl.multiple_of(block * BLOCK, BLOCK), BLOCK)
    bc_now = jnp.concatenate(
        [
            (dot3(d_scores_t, c_parts) + dot3(tail_parts, after_parts, NT)).T,
            (dot3(d_scores_t, b_parts, ((0,), (0,))) + dot3(dy_parts, old_parts, NT)).T,
        ],
        axis=0,
    )
    bc_rows[:, :, :, here] = bc_now.reshape(lines, columns, shared, BLOCK)

    def at_step(turn):
        return pl.ds(pl.multiple_of((blocks - 1 - turn) * BLOCK, BLOCK), BLOCK)

    def push_wide(turn, hop):
        to = (x + hop) % columns
        return remote(
            bc_rows.at[:, to, :, at_step(turn)], bc_wide.at[hop - 1, :, :, at_step(turn)],
            wide_send.at[hop - 1, turn], wide_recv.at[hop - 1, turn], shard=z * columns + to,
        )

    def push_line(hop, at):
        to = (z + hop) % lines
        return remote(bc_sum.at[to, :, at], bc_in.at[hop - 1, :, at], bc_send.at[hop], bc_recv.at[hop], shard=to * columns + x)

    def add_wide(turn):
        found = bc_rows[:, x, :, at_step(turn)]
        for hop in range(1, columns):
            push_wide(turn, hop).wait_recv()
            found = found + bc_wide[hop - 1, :, :, at_step(turn)]
        bc_sum[:, :, at_step(turn)] = found
        for hop in range(1, lines):
            push_line(hop, at_step(turn)).start()

    for hop_x in range(1, columns):
        push_wide(step, hop_x).start()

    lag = min(3, blocks - 1)

    @pl.when(step >= lag)
    def _():
        add_wide(step - lag)

    head_count = dt_t.shape[0]
    pad = [jnp.zeros((1, BLOCK), jnp.float32)] * (head_count - heads)
    pad_col = [jnp.zeros((BLOCK, 1), jnp.float32)] * (head_count - heads)
    d_run = jnp.concatenate(row_terms + pad, axis=0) - jnp.concatenate(col_terms + pad_col, axis=1).T
    d_run = d_run + head_sums(dy_carried * dot3(c_parts, old_parts), marks[...])
    leaving = head_sums(fed * d_fed_out, marks[...])
    kept = jnp.sum(old * after, axis=0, keepdims=True) * keep_wide
    kept = jnp.sum(marks[...].astype(jnp.float32) * kept, axis=1, keepdims=True)
    at_end = lax.broadcasted_iota(jnp.int32, (head_count, BLOCK), 1) == BLOCK - 1
    total = jnp.sum(leaving, axis=1, keepdims=True) + kept
    d_run = d_run - leaving + jnp.where(at_end, total, 0.0)
    d_log = running_sum(d_run, reverse=True)
    d_dt[...] = d_log * rate[...] + head_sums(values * d_fed, marks[...])
    grad_rate[...] += d_log * (dt_t * rate[...])
    carry[...] = keep_wide * after + dot3(c_rows.T, dy_parts)
    pre_v, sig_v = pre_now[:, :inner], sig[:, :inner]
    d_values = dt_wide * d_fed + skip[...] * dy
    d_pre = d_values * (sig_v * (1.0 + pre_v * (1.0 - sig_v)))
    ext[:BLOCK, :] = d_pre
    place = block * BLOCK + lax.broadcasted_iota(jnp.int32, (BLOCK, 1), 0)
    conv_in = conv_v[...]
    d_conv = taps[CONV - 1 : CONV, :] * d_pre
    grads[CONV - 1 : CONV, :] += jnp.sum(conv_in * d_pre, axis=0, keepdims=True)
    grads[CONV : CONV + 1, :] += jnp.sum(d_pre, axis=0, keepdims=True)
    for ahead in range(1, CONV):
        same = sequence_of(place + ahead, bounds) == seg_col
        moved = jnp.where(same, ext[ahead : ahead + BLOCK, :], 0.0)
        d_conv = d_conv + taps[CONV - 1 - ahead : CONV - ahead, :] * moved
        grads[CONV - 1 - ahead : CONV - ahead, :] += jnp.sum(conv_in * moved, axis=0, keepdims=True)
    ext[BLOCK:, :] = ext[:TAIL, :]
    d_cols[:, inner:] = d_conv.astype(jnp.bfloat16)

    @pl.when(step == blocks - 1)
    def _():
        everything = pl.ds(0, bc_sum.shape[2])
        for turn in range(blocks - lag, blocks):
            add_wide(turn)
        for turn in hops:
            if 2 * turn >= blocks:
                hop(turn)
        end()
        for turn in range(1, lines):
            push_line(turn, everything).wait()
        found = bc_sum[z]
        for turn in range(1, lines):
            found = found + bc_in[turn - 1]
        d_bc[...] = found
        for turn in range(blocks):
            for hop_x in range(1, columns):
                push_wide(turn, hop_x).wait_send()


def mixer_forward(shards, bounds, slots, rows_in, weight, taps, bias, dt_bias, rate, skip, cot_own):
    blocks, _, width = rows_in.shape
    columns = grid_columns(shards)
    total, inner, kept = blocks * BLOCK, INNER // shards, weight.shape[0]
    heads = inner // HDIM
    f32, bf16, any_space = jnp.float32, jnp.bfloat16, pl.BlockSpec(memory_space=pl.ANY)

    def block_of(lanes):
        return pl.BlockSpec((BLOCK, lanes), lambda i: (i, 0))

    return pl.pallas_call(
        functools.partial(forward_kernel, heads, shards, columns),
        grid=(blocks,),
        in_specs=[
            pl.BlockSpec(memory_space=pltpu.SMEM),
            pl.BlockSpec((1, 1, BLOCK), lambda i: (i, 0, 0)),
            pl.BlockSpec((1, BLOCK, width), lambda i: (i, 0, 0)),
            whole(weight.shape),
            whole(taps.shape),
            whole(bias.shape),
            whole(dt_bias.shape),
            whole(rate.shape),
            whole(skip.shape),
            any_space,
        ],
        out_specs=[
            block_of(width),
            block_of(kept),
            block_of(inner + SHARED),
            block_of(inner),
            pl.BlockSpec((1, STATE, inner), lambda i: (i, 0, 0)),
            block_of(128),
            block_of(128),
            any_space,
        ],
        out_shape=[
            jax.ShapeDtypeStruct((total, width), bf16),
            jax.ShapeDtypeStruct((total, kept), f32),
            jax.ShapeDtypeStruct((total, inner + SHARED), f32),
            jax.ShapeDtypeStruct((total, inner), f32),
            jax.ShapeDtypeStruct((blocks, STATE, inner), f32),
            jax.ShapeDtypeStruct((total, 128), f32),
            jax.ShapeDtypeStruct((total, 128), f32),
            jax.ShapeDtypeStruct((cot_own.shape[0], shards) + cot_own.shape[1:], bf16),
        ],
        scratch_shapes=[
            pltpu.VMEM((BLOCK + TAIL, inner + SHARED), f32),
            pltpu.VMEM((STATE, inner), f32),
            *gather_semaphores(shards, columns),
        ],
        compiler_params=pltpu.CompilerParams(
            collective_id=2, has_side_effects=True, vmem_limit_bytes=56 * 1024 * 1024
        ),
        cost_estimate=pl.CostEstimate(flops=0, bytes_accessed=300_000_000, transcendentals=0),
        name="mixer_forward",
    )(bounds, slots, rows_in, weight, taps, bias, dt_bias, rate, skip, cot_own)


def pack_cotangent(shards, slots, rows_in, weight, mixed, projected, gain):
    blocks, _, width = rows_in.shape
    total, inner = mixed.shape
    several = 2

    def block_of(lanes):
        return pl.BlockSpec((several * BLOCK, lanes), lambda i: (i, 0))

    return pl.pallas_call(
        functools.partial(cotangent_kernel, shards),
        grid=(blocks // several,),
        in_specs=[
            pl.BlockSpec((several, 1, BLOCK), lambda i: (i, 0, 0)),
            pl.BlockSpec((several, BLOCK, width), lambda i: (i, 0, 0)),
            whole(weight.shape),
            block_of(inner),
            block_of(inner),
            whole(gain.shape),
        ],
        out_specs=[block_of(width), block_of(inner), whole((8, total))],
        out_shape=[
            jax.ShapeDtypeStruct((total, width), jnp.bfloat16),
            jax.ShapeDtypeStruct((total, inner), jnp.float32),
            jax.ShapeDtypeStruct((8, total), jnp.float32),
        ],
        scratch_shapes=[
            pltpu.VMEM((8, total), jnp.float32),
            pltpu.VMEM((shards - 1, 8, total), jnp.float32),
            pltpu.SemaphoreType.DMA((shards,)),
            pltpu.SemaphoreType.DMA((shards,)),
        ],
        compiler_params=pltpu.CompilerParams(
            collective_id=5, has_side_effects=True, vmem_limit_bytes=48 * 1024 * 1024
        ),
        cost_estimate=pl.CostEstimate(flops=0, bytes_accessed=60_000_000, transcendentals=0),
        name="pack_cotangent",
    )(slots, rows_in, weight, mixed, projected, gain)


def mixer_backward(
    shards, bounds, slots, pre, mixed, projected, d_out, sums, states, dt_cols, taps, rate, skip, gain, out_own
):
    total, inner = d_out.shape
    heads, blocks, padded = inner // HDIM, total // BLOCK, rate.shape[0]
    shared = SHARED // shards
    columns = grid_columns(shards)
    marks = (jnp.arange(padded)[:, None] == jnp.arange(inner)[None, :] // HDIM).astype(jnp.bfloat16)

    def block_of(width, column):
        return pl.BlockSpec((BLOCK, width), lambda i: (blocks - 1 - i, column))

    return pl.pallas_call(
        functools.partial(backward_kernel, heads, blocks, shards, columns),
        grid_spec=pltpu.PrefetchScalarGridSpec(
            num_scalar_prefetch=0,
            grid=(blocks,),
            in_specs=[
                pl.BlockSpec(memory_space=pltpu.SMEM),
                pl.BlockSpec((1, 1, BLOCK), lambda i: (blocks - 1 - i, 0, 0)),
                block_of(inner + SHARED, 0),
                block_of(inner, 0),
                block_of(inner, 0),
                block_of(inner, 0),
                block_of(inner, 1),
                pl.BlockSpec((8, BLOCK), lambda i: (0, blocks - 1 - i)),
                pl.BlockSpec((1, STATE, inner), lambda i: (blocks - 1 - i, 0, 0)),
                block_of(dt_cols.shape[1], 0),
                whole(taps.shape),
                whole(rate.shape),
                whole(skip.shape),
                whole(gain.shape),
                whole(marks.shape),
                pl.BlockSpec(memory_space=pl.ANY),
            ],
            out_specs=[
                block_of(2 * inner, 0),
                whole((shared, total)),
                pl.BlockSpec((padded, BLOCK), lambda i: (0, blocks - 1 - i)),
                whole((8, inner)),
                whole((padded, BLOCK)),
                pl.BlockSpec((1, shards, BLOCK // shards, inner), lambda i: (blocks - 1 - i, 0, 0, 0)),
                pl.BlockSpec(memory_space=pl.ANY),
            ],
            scratch_shapes=[
                pltpu.VMEM((BLOCK + TAIL, inner), jnp.float32),
                pltpu.VMEM((STATE, inner), jnp.float32),
                pltpu.VMEM((shards // columns, columns, shared, total), jnp.float32),
                pltpu.VMEM((max(columns - 1, 1), shards // columns, shared, total), jnp.float32),
                pltpu.VMEM((shards // columns, shared, total), jnp.float32),
                pltpu.VMEM((shards // columns - 1, shared, total), jnp.float32),
                pltpu.SemaphoreType.DMA((max(columns - 1, 1), blocks)),
                pltpu.SemaphoreType.DMA((max(columns - 1, 1), blocks)),
                pltpu.SemaphoreType.DMA((shards,)),
                pltpu.SemaphoreType.DMA((shards,)),
                *gather_semaphores(shards, columns),
            ],
        ),
        out_shape=[
            jax.ShapeDtypeStruct((total, 2 * inner), jnp.bfloat16),
            jax.ShapeDtypeStruct((shared, total), jnp.float32),
            jax.ShapeDtypeStruct((padded, total), jnp.float32),
            jax.ShapeDtypeStruct((8, inner), jnp.float32),
            jax.ShapeDtypeStruct((padded, BLOCK), jnp.float32),
            jax.ShapeDtypeStruct((blocks, shards, BLOCK // shards, inner), jnp.bfloat16),
            jax.ShapeDtypeStruct((out_own.shape[0], shards) + out_own.shape[1:], jnp.bfloat16),
        ],
        compiler_params=pltpu.CompilerParams(
            collective_id=3, has_side_effects=True, vmem_limit_bytes=56 * 1024 * 1024
        ),
        cost_estimate=pl.CostEstimate(flops=0, bytes_accessed=200_000_000, transcendentals=0),
        name="mixer_backward",
    )(bounds, slots, pre, mixed, projected, d_out, projected, sums, states, dt_cols, taps, rate, skip, gain, marks, out_own)


def piece_rows(shards, groups):
    chunks = (2 * INNER // shards + SHARED // shards) // CHUNK
    return -(-chunks // groups) * CHUNK


def column_runs(shards, groups):
    inner, width = INNER // shards, (2 * INNER + SHARED + HEADS) // groups
    kept = 2 * inner + SHARED + HEADS
    quarter = kept // groups
    spans = []
    for shard in range(shards):
        spans.append((inner * shard, shard, 0, inner))
        spans.append((INNER + inner * shard, shard, inner, inner))
    spans.append((2 * INNER, None, 2 * inner, SHARED + HEADS))
    runs = []
    for column, shard, row, length in spans:
        while length > 0:
            step = min(length, width - column % width, quarter - row % quarter)
            runs.append((column // width, column % width, shard, row, step))
            column, row, length = column + step, row + step, length - step
    return runs


def front_kernel(
    shards, groups, columns,
    rows_in, gain, cot_in, weight_in, out_in, slot_row, slot_col,
    rows_all, weight_all, out_all, slot_all, cot_own, out_cast, scaled_rows,
    rows_own, weight_own, out_own, slot_own,
    run_send, run_recv, share_send, share_recv, out_send, out_recv, slot_send, slot_recv, local_sem, *gather_sems,
):
    shard, group = lax.axis_index("shard"), lax.axis_index("group")
    lines, rows_y = shards // columns, groups // 2
    y, core = group // 2, group % 2
    mate = y * 2 + 1 - core
    quarter = weight_all.shape[0] // groups
    depth = weight_own.shape[1]
    out_width = out_own.shape[1]
    everyone = []
    for step in range(1, shards * groups):
        other_shard = (shard + step % shards) % shards
        other_group = (group + step // shards) % groups
        everyone.append({"shard": other_shard, "group": other_group})
    barrier_with(everyone)

    count = rows_in.shape[0]
    below = (slot_col[...] < slot_row[...]).astype(jnp.int32).astype(jnp.float32)
    rank = jnp.sum(below, axis=0, keepdims=True).astype(jnp.int32)
    sort = (lax.broadcasted_iota(jnp.int32, (count, count), 0) == rank).astype(jnp.bfloat16)
    value = rows_in[...]
    scale = lax.rsqrt(jnp.sum(value * value, axis=1, keepdims=True) * (1.0 / value.shape[1]) + 1e-05)
    scaled = value * scale
    value = (scaled * gain[...]).astype(jnp.bfloat16)
    rows_own[...] = dots(sort, value, ((1,), (0,))).astype(jnp.bfloat16).reshape(rows_own.shape)
    begin, hop, end = row_gather(shards, columns, rows_own, rows_all, *gather_sems)
    begin()
    slots = slot_row[...]
    high = slots // 256
    both = jnp.where(lax.broadcasted_iota(jnp.int32, (8, count), 0) == 0, high, slots - 256 * high)
    both = dots(both.astype(jnp.float32).astype(jnp.bfloat16), sort, NT)
    slot_own[...] = jnp.broadcast_to(256.0 * both[0:1, :] + both[1:2, :], (8, count)).astype(jnp.int32)
    out_own[...] = out_in[...].astype(jnp.bfloat16)
    weight_own[...] = weight_in[...].astype(jnp.bfloat16)

    def slot_copy(step):
        return remote(slot_own, slot_all.at[shard], slot_send.at[step], slot_recv.at[step], shard=(shard + step) % shards)

    for step in range(1, shards):
        slot_copy(step).start()
    slot_here = pltpu.make_async_copy(slot_own, slot_all.at[shard], local_sem.at[0])
    slot_here.start()

    runs = column_runs(shards, groups)
    lanes = pl.ds(pl.multiple_of(shard * depth, depth), depth)
    jobs = {owner: [] for owner in range(groups)}
    for owner, column, target, row, length in runs:
        for to in range(shards) if target is None else (target,):
            jobs[owner].append((column, to, row, length))

    def run_copy(number, column, to, row, length):
        return remote(
            weight_own.at[pl.ds(column, length)], weight_all.at[pl.ds(row, length), lanes],
            run_send.at[number], run_recv, shard=to, group=row // quarter,
        )

    def each_run(act):
        for owner in range(groups):
            @pl.when(group == owner)
            def _():
                for number, (column, to, row, length) in enumerate(jobs[owner]):
                    if row // quarter == owner:
                        here = shard == to
                        act(number, column, to, row, length, here)
                    else:
                        act(number, column, to, row, length, None)

    def start_run(number, column, to, row, length, here):
        if here is None:
            run_copy(number, column, to, row, length).start()
            return

        @pl.when(here)
        def _():
            pltpu.make_async_copy(weight_own.at[pl.ds(column, length)], weight_all.at[pl.ds(row, length), lanes], run_recv).start()

        @pl.when(jnp.logical_not(here))
        def _():
            run_copy(number, column, to, row, length).start()

    def end_run(number, column, to, row, length, here):
        if here is None:
            run_copy(number, column, to, row, length).wait_send()
            return

        @pl.when(jnp.logical_not(here))
        def _():
            run_copy(number, column, to, row, length).wait_send()

    each_run(start_run)

    def own_part(ref, part):
        if ref is out_all:
            return ref.at[:, pl.ds(pl.multiple_of(part * out_width, out_width), out_width)]
        return ref.at[pl.ds(pl.multiple_of(part * quarter, quarter), quarter)]

    def share(ref, part, sends, recvs, number, peer, first=None):
        source = own_part(ref, part) if first is None else first
        return remote(source, own_part(ref, part), sends.at[number], recvs.at[part], group=peer)

    def share_start(ref, sends, recvs, first=None):
        share(ref, group, sends, recvs, 0, mate, first).start()
        for step in range(1, rows_y):
            share(ref, group, sends, recvs, step, (y + step) % rows_y * 2 + core, first).start()

    def share_pass(ref, sends, recvs):
        for step in range(1, rows_y):
            part = (y + step) % rows_y * 2 + core
            share(ref, part, sends, recvs, step, part).wait_recv()
            share(ref, part, sends, recvs, rows_y - 1 + step, mate).start()

    def share_end(ref, sends, recvs):
        for turn in range(rows_y):
            part = turn * 2 + 1 - core
            share(ref, part, sends, recvs, 0, mate).wait_recv()
        for number in range(2 * rows_y - 1):
            share(ref, group, sends, recvs, number, mate).wait_send()

    out_here = pltpu.make_async_copy(out_own, own_part(out_all, group), local_sem.at[1])
    out_here.start()
    share_start(out_all, out_send, out_recv, out_own)
    out_cast[...] = out_own[...]
    high = scaled.astype(jnp.bfloat16)
    left = scaled - high.astype(jnp.float32)
    mid = left.astype(jnp.bfloat16)
    low = (left - mid.astype(jnp.float32)).astype(jnp.bfloat16)
    plain = ((1,), (0,))
    scaled_rows[...] = dots(sort, high, plain) + (dots(sort, mid, plain) + dots(sort, low, plain))
    cot_own[...] = (
        dots(sort, cot_in[...].astype(jnp.bfloat16), ((1,), (0,))).astype(jnp.bfloat16).reshape(cot_own.shape)
    )

    for step in range(1, lines):
        hop(step)
        if step == 1:
            share_pass(out_all, out_send, out_recv)
            kept = own_part(weight_all, group)
            pltpu.make_async_copy(kept, kept, run_recv).wait()
            share_start(weight_all, share_send, share_recv)
    share_pass(weight_all, share_send, share_recv)

    end()
    out_here.wait()
    share_end(out_all, out_send, out_recv)
    share_end(weight_all, share_send, share_recv)
    each_run(end_run)
    for step in range(1, shards):
        slot_copy(step).wait()
    slot_here.wait()


def front_exchange(shards, groups, rows_in, gain, cot_in, weight_in, out_in, slots):
    columns = grid_columns(shards)
    rows_y = groups // 2
    count, width = rows_in.shape
    blocks, per = shards * count // BLOCK, BLOCK // shards
    kept = 2 * INNER // shards + SHARED + HEADS
    any_space, vmem = pl.BlockSpec(memory_space=pl.ANY), pl.BlockSpec(memory_space=pltpu.VMEM)
    dma, bf16 = pltpu.SemaphoreType.DMA, jnp.bfloat16
    counts = {}
    for owner, _, target, _, _ in column_runs(shards, groups):
        counts[owner] = counts.get(owner, 0) + (shards if target is None else 1)
    return pl.pallas_call(
        functools.partial(front_kernel, shards, groups, columns),
        in_specs=[vmem] * 7,
        out_specs=[any_space] * 4 + [vmem] * 3,
        out_shape=[
            jax.ShapeDtypeStruct((blocks, shards, per, width), bf16),
            jax.ShapeDtypeStruct((kept, width), bf16),
            jax.ShapeDtypeStruct((out_in.shape[0], out_in.shape[1] * groups), bf16),
            jax.ShapeDtypeStruct((shards, 8, count), jnp.int32),
            jax.ShapeDtypeStruct((blocks, per, width), bf16),
            jax.ShapeDtypeStruct(out_in.shape, bf16),
            jax.ShapeDtypeStruct((count, width), jnp.float32),
        ],
        scratch_shapes=[
            pltpu.VMEM((blocks, per, width), bf16),
            pltpu.VMEM(weight_in.shape, bf16),
            pltpu.VMEM(out_in.shape, bf16),
            pltpu.VMEM((8, count), jnp.int32),
            dma((max(counts.values()),)),
            dma,
            dma((2 * rows_y - 1,)),
            dma((groups,)),
            dma((2 * rows_y - 1,)),
            dma((groups,)),
            dma((shards,)),
            dma((shards,)),
            dma((2,)),
            *gather_semaphores(shards, columns),
        ],
        compiler_params=pltpu.CompilerParams(
            collective_id=4, has_side_effects=True, vmem_limit_bytes=48 * 1024 * 1024
        ),
        cost_estimate=pl.CostEstimate(flops=0, bytes_accessed=300_000_000, transcendentals=0),
        name="front_exchange",
    )(rows_in, gain[None, :], cot_in, weight_in, out_in, slots[None, :], slots[:, None])


def unpack_kernel(
    shards, slots, d_cols, d_rest, normed, weight, weight_rest, no_rows,
    partial, grad, home, moved_cols, moved_rest, local_sem, home_send, home_recv,
):
    step = pl.program_id(0)
    shard = lax.axis_index("shard")
    main = d_cols.shape[1]
    per = BLOCK // shards

    def push(turn):
        peer = (shard + turn) % shards
        return remote(no_rows.at[first, peer], home.at[:, :, lanes], home_send.at[turn], home_recv.at[turn], shard=peer)

    first, inner = pl.ds(0, home.shape[0]), no_rows.shape[3]
    lanes = pl.ds(pl.multiple_of(shard * inner, inner), inner)
    here = pltpu.make_async_copy(no_rows.at[first, shard], home.at[:, :, lanes], local_sem)

    @pl.when(step == 0)
    def _():
        barrier_with([{"shard": (shard + turn) % shards} for turn in range(1, shards)])
        for turn in range(1, shards):
            push(turn).start()
        here.start()
        grad[...] = jnp.zeros_like(grad)

    several = d_cols.shape[0] // BLOCK
    for turn in range(several):
        rows = pl.ds(turn * BLOCK, BLOCK)
        place = place_of_rows(slots[turn])
        moved_cols[rows, :] = dots(place, d_cols[rows, :], ((0,), (0,))).astype(jnp.bfloat16)
        moved_rest[rows, :] = dots(place, d_rest[rows, :], ((0,), (0,))).astype(jnp.bfloat16)
    tile = 512
    for lane in range(0, weight.shape[1], tile):
        lanes = pl.ds(lane, tile)
        found = dots(moved_cols[...], weight[:, lanes], ((1,), (0,)))
        found = found + dots(moved_rest[...], weight_rest[:, lanes], ((1,), (0,)))
        for turn in range(several):
            rows = found[turn * BLOCK : (turn + 1) * BLOCK]
            partial[:, turn, :, lanes] = rows.reshape(shards, per, tile)
    grad[:main, :] += dots(d_cols[...], normed[...], ((0,), (0,)))
    grad[main:, :] += dots(d_rest[...], normed[...], ((0,), (0,)))

    @pl.when(step == pl.num_programs(0) - 1)
    def _():
        for turn in range(1, shards):
            push(turn).wait()
        here.wait()


def project_back(slots, d_cols, d_rest, normed, weight, weight_rest, no_rows, shards):
    blocks, width = slots.shape[0], normed.shape[1]
    per, main, rest = BLOCK // shards, d_cols.shape[1], d_rest.shape[1]
    several = 2
    any_space = pl.BlockSpec(memory_space=pl.ANY)

    def block_of(columns):
        return pl.BlockSpec((several * BLOCK, columns), lambda i: (i, 0))

    return pl.pallas_call(
        functools.partial(unpack_kernel, shards),
        grid=(blocks // several,),
        in_specs=[
            pl.BlockSpec((several, 1, BLOCK), lambda i: (i, 0, 0)),
            block_of(main),
            block_of(rest),
            block_of(width),
            pl.BlockSpec((main, width), lambda i: (0, 0)),
            whole(weight_rest.shape),
            any_space,
        ],
        out_specs=[
            pl.BlockSpec((shards, several, per, width), lambda i: (0, i, 0, 0)),
            whole((main + rest, width)),
            any_space,
        ],
        out_shape=[
            jax.ShapeDtypeStruct((shards, blocks, per, width), jnp.float32),
            jax.ShapeDtypeStruct((main + rest, width), jnp.float32),
            jax.ShapeDtypeStruct((blocks, per, INNER), jnp.bfloat16),
        ],
        scratch_shapes=[
            pltpu.VMEM((several * BLOCK, main), jnp.bfloat16),
            pltpu.VMEM((several * BLOCK, rest), jnp.bfloat16),
            pltpu.SemaphoreType.DMA,
            pltpu.SemaphoreType.DMA((shards,)),
            pltpu.SemaphoreType.DMA((shards,)),
        ],
        compiler_params=pltpu.CompilerParams(
            collective_id=6, has_side_effects=True, vmem_limit_bytes=60 * 1024 * 1024
        ),
        cost_estimate=pl.CostEstimate(flops=0, bytes_accessed=90_000_000, transcendentals=0),
        name="project_back",
    )(slots, d_cols, d_rest, normed, weight, weight_rest, no_rows)


def other_place(step, place, count):
    upwards = count - 1 - place
    low = jnp.where(step < upwards, count - 1 - step, step - upwards)
    high = jnp.where(step < place, step, count - 1 - (step - place))
    return jnp.where(2 * place < count, low, high)


def tail_kernel(
    shards, groups, columns, near, direct,
    partial, weight_part, small, scaled_rows,
    rows_out, weight_out, mark_out, small_out, gain_out, core_in, row_in, row_scale_in, small_in, gain_in,
    wide_in, wide_scale, line_in, line_scale,
    held, coded, scales, line_coded, line_scales, got, got_scale, marks, total, other, send_rows, send_scales, row_got, row_scale_got, deal_rows, deal_scales, small_sum, small_got,
    gain_sum, gain_part,
    load_sem, wide_send, wide_recv, line_send, line_recv, core_send, core_recv, row_send, row_recv,
    deal_send, deal_recv, mark_send, mark_recv, small_send, small_recv, gain_send, gain_recv,
):
    shard, group = lax.axis_index("shard"), lax.axis_index("group")
    lines = shards // columns
    rows_y = groups // 2
    z, x = shard // columns, shard % columns
    y, core = group // 2, group % 2
    count = held.shape[0]
    owned, depth = weight_out.shape
    piece, chunk = total.shape[0], CHUNK
    inner, shared = INNER // shards, SHARED // shards

    def load(src, dst):
        copy = pltpu.make_async_copy(src, dst, load_sem)
        copy.start()
        copy.wait()

    shard_peers = [(shard + step) % shards for step in range(1, shards)]
    group_peers = [(group + step) % groups for step in range(1, groups)]
    if direct:
        barrier_with(
            [
                {"shard": (shard + step % shards) % shards, "group": (group + step // shards) % groups}
                for step in range(1, shards * groups)
            ]
        )
    else:
        barrier_with([{"shard": peer} for peer in shard_peers] + [{"group": peer} for peer in group_peers])

    mate = y * 2 + 1 - core

    def core_copy(turn):
        return remote(piece_of(turn * 2 + 1 - core), core_in.at[turn], core_send.at[turn], core_recv.at[turn], group=mate)

    def piece_of(owner):
        return weight_part.at[pl.ds(pl.multiple_of(owner * piece, piece), piece)]

    for turn in range(rows_y if direct else 0):
        core_copy(turn).start()

    def small_copy(step):
        return remote(small, small_in.at[step - 1], small_send.at[step - 1], small_recv.at[step - 1], group=(group + step) % groups)

    for step in range(1, groups):
        small_copy(step).start()

    def code(coded_to, scales_to, values=held, lot=32):
        @pl.loop(0, values.shape[0] // lot, unroll=2)
        def _(turn):
            rows = pl.ds(pl.multiple_of(turn * lot, lot), lot)
            value = values[rows, :]
            most = jnp.maximum(jnp.max(jnp.abs(value), axis=1, keepdims=True), 1e-30)
            coded_to[rows, :] = jnp.round(value * (32767.0 / most)).astype(jnp.int32).astype(jnp.int16)
            marks[rows, :] = jnp.broadcast_to(most * (1.0 / 32767.0), (lot, 128))

        scales_to[...] = marks[: scales_to.shape[1], :].T[:8, :]

    def add(coded_from, scales_from):
        if not near:
            load(coded_from, got)
            load(scales_from, got_scale)
            coded_from, scales_from = got, got_scale
        marks[:count, :] = jnp.broadcast_to(scales_from[0:1, :], (128, count)).T

        @pl.loop(0, count // 32, unroll=2)
        def _(turn):
            rows = pl.ds(pl.multiple_of(turn * 32, 32), 32)
            held[rows, :] += coded_from[rows, :].astype(jnp.float32) * marks[rows, 0:1]

    def place_of(step):
        return other_place(step, z, lines) if step < lines - 1 else z

    def wide_copies(step, hop):
        at = (hop - 1) * lines + step
        peer = z * columns + (x + hop) % columns
        target = place_of(step)
        return (
            remote(coded.at[step], wide_in.at[hop - 1, target], wide_send.at[0, at], wide_recv.at[0, at], shard=peer),
            remote(scales.at[step], wide_scale.at[hop - 1, target], wide_send.at[1, at], wide_recv.at[1, at], shard=peer),
        )

    def send_wide(hop, steps):
        for step in steps:
            if hop > 1:
                for copy in wide_copies(step, hop - 1):
                    copy.wait_send()
            load(partial.at[place_of(step) * columns + (x + hop) % columns], held)
            code(coded.at[step], scales.at[step])
            for copy in wide_copies(step, hop):
                copy.start()

    def row_copies(step):
        peer = (y + step) % rows_y * 2 + core
        return (
            remote(send_rows.at[step - 1], row_in.at[step - 1], row_send.at[0, step - 1], row_recv.at[0, step - 1], group=peer),
            remote(send_scales.at[step - 1], row_scale_in.at[step - 1], row_send.at[1, step - 1], row_recv.at[1, step - 1], group=peer),
        )

    def core_sum(turn):
        load(piece_of(turn * 2 + core), total)
        load(core_in.at[turn], other)

        @pl.loop(0, piece // chunk)
        def _(turn):
            rows = pl.ds(pl.multiple_of(turn * chunk, chunk), chunk)
            total[rows, :] += other[rows, :]

    if columns > 1:
        send_wide(1, range(0, 1))
    if direct:
        for turn in range(rows_y):
            core_copy(turn).wait_recv()
        for step in range(1, rows_y):
            core_sum((y + step) % rows_y)
            code(send_rows.at[step - 1], send_scales.at[step - 1], total, chunk)
            for copy in row_copies(step):
                copy.start()
        core_sum(y)
    if columns > 1:
        send_wide(1, range(1, lines))
    for hop in range(2, columns):
        send_wide(hop, range(lines))

    load(small, small_sum)
    for step in range(1, groups):
        small_copy(step).wait_recv()
        load(small_in.at[step - 1], small_got)
        small_sum[...] += small_got[...]

    def small_deal(step):
        return remote(small_sum, small_out.at[shard], small_send.at[groups + step], small_recv.at[groups + step], shard=(shard + step) % shards)

    for step in range(1, shards):
        small_deal(step).start()
    load(small_sum, small_out.at[shard])

    def line_copies(step):
        target = place_of(step)
        way = jnp.where(target > z, 0, 1)
        peer = jnp.where(target > z, z + 1, z - 1) * columns + x
        return (
            remote(line_coded.at[step], line_in.at[way, target], line_send.at[0, step], line_recv.at[0, way, target], shard=peer),
            remote(line_scales.at[step], line_scale.at[way, target], line_send.at[1, step], line_recv.at[1, way, target], shard=peer),
        )

    def take(way, target):
        source = jnp.where(way == 0, z - 1, z + 1)
        peer = jnp.clip(source, 0, lines - 1) * columns + x
        remote(line_coded.at[0], line_in.at[way, target], line_send.at[0, 0], line_recv.at[0, way, target], shard=peer).wait_recv()
        remote(line_scales.at[0], line_scale.at[way, target], line_send.at[1, 0], line_recv.at[1, way, target], shard=peer).wait_recv()
        add(line_in.at[way, target], line_scale.at[way, target])

    def gather_wide(step):
        target = place_of(step)
        load(partial.at[target * columns + x], held)
        for hop in range(1, columns):
            for copy in wide_copies(step, hop):
                copy.wait_recv()
            add(wide_in.at[hop - 1, target], wide_scale.at[hop - 1, target])

    def deal_copy(turn, step):
        first = group * piece + turn * chunk
        column = jnp.where(
            first < inner,
            inner * shard + first,
            jnp.where(first < 2 * inner, INNER + inner * shard + first - inner, 2 * INNER + shared * shard + first - 2 * inner),
        )
        owner = jnp.minimum(column // owned, groups - 1)
        peer = (shard + step) % shards
        source = deal_rows.at[
            pl.ds(pl.multiple_of(turn * chunk, chunk), chunk), pl.ds(pl.multiple_of(peer * depth, depth), depth)
        ]
        target = weight_out.at[pl.ds(pl.multiple_of(column - owner * owned, chunk), chunk)]
        real = first < 2 * inner + shared
        here = real & (owner == group) if step == 0 else None
        away = real & (owner != group) if step == 0 else real

        def near_copy():
            return pltpu.make_async_copy(source, target, deal_recv)

        def far():
            return remote(source, target, deal_send.at[turn, step], deal_recv, shard=peer, group=owner)

        return here, near_copy, away, far

    def deal():
        for step in range(1, rows_y):
            for copy in row_copies(step):
                copy.wait_recv()
            load(row_in.at[step - 1], row_got)
            load(row_scale_in.at[step - 1], row_scale_got)
            marks[: row_scale_got.shape[1], :] = jnp.broadcast_to(row_scale_got[0:1, :], (128, row_scale_got.shape[1])).T

            @pl.loop(0, piece // chunk)
            def _(turn):
                rows = pl.ds(pl.multiple_of(turn * chunk, chunk), chunk)
                total[rows, :] += row_got[rows, :].astype(jnp.float32) * marks[rows, 0:1]

        code(deal_rows, deal_scales, total, chunk)
        load(deal_scales, mark_out.at[shard, group])
        for step in range(1, groups):
            mark_copy(step).start()

    def deal_some(part, parts):
        chunks = piece // chunk

        @pl.loop(part * chunks // parts, (part + 1) * chunks // parts)
        def _(turn):
            for step in range(shards):
                here, near_copy, away, far = deal_copy(turn, step)
                if here is not None:
                    pl.when(here)(lambda: near_copy().start())
                pl.when(away)(lambda: far().start())

    def mark_copy(step):
        to = (group + step) % groups
        return remote(deal_scales, mark_out.at[shard, group], mark_send.at[step], mark_recv.at[step], group=to)

    def mark_spread(step):
        to, at = (shard + step) % shards, groups + step
        return remote(mark_out.at[shard], mark_out.at[shard], mark_send.at[at], mark_recv.at[at], shard=to)

    def mark_pass():
        for step in range(1, groups):
            mark_copy(step).wait_recv()
        for step in range(1, shards):
            mark_spread(step).start()

    def deal_end():
        for step in range(1, groups):
            mark_copy(step).wait_send()
        for step in range(1, shards):
            mark_spread(step).wait()

        @pl.when(group == groups - 1)
        def _():
            most = weight_out.at[pl.ds(0, owned - HEADS)]
            pltpu.make_async_copy(most, most, deal_recv).wait()

        @pl.when(group < groups - 1)
        def _():
            pltpu.make_async_copy(weight_out, weight_out, deal_recv).wait()

        @pl.loop(0, piece // chunk)
        def _(turn):
            for step in range(shards):
                _, _, away, far = deal_copy(turn, step)
                pl.when(away)(lambda: far().wait_send())

    for step in range(lines - 1):
        if direct and step == min(1, lines - 2):
            deal()
        target = place_of(step)
        way = jnp.where(target > z, 0, 1)
        gather_wide(step)

        @pl.when(jnp.where(target > z, z > 0, z < lines - 1))
        def _():
            take(way, target)

        code(line_coded.at[step], line_scales.at[step])
        for copy in line_copies(step):
            copy.start()
        if direct and step >= min(1, lines - 2):
            deal_some(step - min(1, lines - 2), lines - 1 - min(1, lines - 2))
    if direct:
        mark_pass()
    gather_wide(lines - 1)

    @pl.when(z > 0)
    def _():
        take(0, z)

    @pl.when(z < lines - 1)
    def _():
        take(1, z)

    rows_out[...] = held[...]
    gain_sum[...] = jnp.zeros_like(gain_sum)

    @pl.loop(0, count // 8)
    def _(turn):
        rows = pl.ds(pl.multiple_of(turn * 8, 8), 8)
        gain_sum[...] += held[rows, :] * scaled_rows[rows, :]

    def gain_copy(step):
        return remote(gain_part, gain_in.at[step - 1], gain_send.at[step - 1], gain_recv.at[step - 1], shard=(shard + step) % shards)

    def gain_deal(step):
        at = shards - 1 + step - 1
        return remote(gain_out, gain_in.at[at], gain_send.at[at], gain_recv.at[at], group=(group + step) % groups)

    lanes = gain_out.shape[1]
    products = jnp.sum(gain_sum[...], axis=0, keepdims=True)
    gain_part[...] = jnp.concatenate([products[:, row * lanes : (row + 1) * lanes] for row in range(8)], axis=0)
    for step in range(1, shards):
        gain_copy(step).start()
    gain_out[...] = gain_part[...]
    for step in range(1, shards):
        gain_copy(step).wait_recv()
        gain_out[...] += gain_in[step - 1]
    for step in range(1, groups):
        gain_deal(step).start()
    for step in range(1, groups):
        gain_deal(step).wait_recv()
    for step in range(1, groups):
        gain_deal(step).wait_send()
    for step in range(1, groups):
        gain_out[...] += gain_in[shards - 1 + step - 1]

    for step in range(1, shards):
        gain_copy(step).wait_send()
        small_deal(step).wait()
    for step in range(1, groups):
        small_copy(step).wait_send()
    if direct:
        deal_end()
        for step in range(1, rows_y):
            for copy in row_copies(step):
                copy.wait_send()
        for turn in range(rows_y):
            core_copy(turn).wait_send()
    for step in range(lines):
        for copy in wide_copies(step, columns - 1) if columns > 1 else ():
            copy.wait_send()
    for step in range(lines - 1):
        for copy in line_copies(step):
            copy.wait_send()


def tail_exchange(shards, groups, partial, weight_part, small, scaled_rows, owned, depth, direct):
    columns = grid_columns(shards)
    lines, rows_y = shards // columns, groups // 2
    count, width = scaled_rows.shape
    piece = piece_rows(shards, groups) if direct else CHUNK
    padded = -(-piece // 128) * 128
    small_shape = small.shape
    coded, scale = (count, width), (8, count)
    any_space, vmem = pl.BlockSpec(memory_space=pl.ANY), pl.BlockSpec(memory_space=pltpu.VMEM)
    f32, i16 = jnp.float32, jnp.int16
    slots = max(columns - 1, 1)
    dma = pltpu.SemaphoreType.DMA
    landing = [
        ((slots, lines) + coded, i16),
        ((slots, lines) + scale, f32),
        ((2, lines) + coded, i16),
        ((2, lines) + scale, f32),
    ]
    near = shards * count * width <= 1 << 22
    out = pl.pallas_call(
        functools.partial(tail_kernel, shards, groups, columns, near, direct),
        in_specs=[any_space, any_space, any_space, vmem],
        out_specs=[vmem, any_space, any_space, any_space, vmem] + [any_space] * 4 + [vmem] + ([] if near else [any_space] * 4),
        out_shape=[
            jax.ShapeDtypeStruct((count, width), f32),
            jax.ShapeDtypeStruct((owned, depth), i16),
            jax.ShapeDtypeStruct((shards, groups, 8, padded), f32),
            jax.ShapeDtypeStruct((shards,) + small_shape, f32),
            jax.ShapeDtypeStruct((8, width // 8), f32),
            jax.ShapeDtypeStruct((rows_y, piece, width), f32),
            jax.ShapeDtypeStruct((max(rows_y - 1, 1), piece, width), i16),
            jax.ShapeDtypeStruct((max(rows_y - 1, 1), 8, padded), f32),
            jax.ShapeDtypeStruct((max(groups - 1, 1),) + small_shape, f32),
            jax.ShapeDtypeStruct((shards - 1 + groups - 1, 8, width // 8), f32),
        ]
        + ([] if near else [jax.ShapeDtypeStruct(*each) for each in landing]),
        scratch_shapes=([pltpu.VMEM(*each) for each in landing] if near else [])
        + [
            pltpu.VMEM((count, width), f32),
            pltpu.VMEM((lines,) + coded, i16),
            pltpu.VMEM((lines,) + scale, f32),
            pltpu.VMEM((lines,) + coded, i16),
            pltpu.VMEM((lines,) + scale, f32),
            pltpu.VMEM((16, 128) if near else coded, i16),
            pltpu.VMEM((8, 128) if near else scale, f32),
            pltpu.VMEM((max(count, padded), 128), f32),
            pltpu.VMEM((piece, width), f32),
            pltpu.VMEM((piece, width), f32),
            pltpu.VMEM((max(rows_y - 1, 1), piece, width), i16),
            pltpu.VMEM((max(rows_y - 1, 1), 8, padded), f32),
            pltpu.VMEM((piece, width), i16),
            pltpu.VMEM((8, padded), f32),
            pltpu.VMEM((piece, width), i16),
            pltpu.VMEM((8, padded), f32),
            pltpu.VMEM(small_shape, f32),
            pltpu.VMEM(small_shape, f32),
            pltpu.VMEM((8, width), f32),
            pltpu.VMEM((8, width // 8), f32),
            dma,
            dma((2, slots * lines)),
            dma((2, slots * lines)),
            dma((2, lines)),
            dma((2, 2, lines)),
            dma((rows_y,)),
            dma((rows_y,)),
            dma((2, max(rows_y - 1, 1))),
            dma((2, max(rows_y - 1, 1))),
            dma((piece // CHUNK, shards)),
            dma,
            dma((shards + groups,)),
            dma((shards + groups,)),
            dma((groups + shards,)),
            dma((groups + shards,)),
            dma((shards + groups,)),
            dma((shards + groups,)),
        ],
        compiler_params=pltpu.CompilerParams(
            collective_id=1, has_side_effects=True, vmem_limit_bytes=60 * 1024 * 1024
        ),
        cost_estimate=pl.CostEstimate(flops=0, bytes_accessed=400_000_000, transcendentals=0),
        name="tail_exchange",
    )(partial, weight_part, small, scaled_rows)
    return out[:5]


def finish_kernel(
    shards, groups, columns,
    slots, d_cols, d_rest, normed, weight, weight_rest, no_rows, out_part, small, scaled_rows,
    rows_out, weight_out, mark_out, small_out, dt_out, gain_out, home, out_full, weight_part,
    core_in, row_in, row_scale_in, small_in, dt_in, gain_in,
    wide_in, wide_scale, line_in, line_scale,
    held, coded, scales, line_coded, line_scales, marks, total, other, send_rows, send_scales, row_got, row_scale_got,
    deal_rows, deal_scales, small_sum, small_got, dt_sum, dt_got, gain_sum, gain_part,
    moved, moved_rest, turned, weight_all, lot, tile, made,
    load_sem, fetch_sem, lot_sem, tile_sem, made_sem, out_sem, out_send, out_recv, out_pass_send, home_sem, home_send, home_recv,
    wide_send, wide_recv, line_send, line_recv, core_send, core_recv, row_send, row_recv,
    deal_send, deal_recv, mark_send, mark_recv, small_send, small_recv, dt_send, dt_recv, gain_send, gain_recv,
):
    shard, group = lax.axis_index("shard"), lax.axis_index("group")
    lines = shards // columns
    rows_y = groups // 2
    z, x = shard // columns, shard % columns
    y, core = group // 2, group % 2
    count = held.shape[0]
    parts = count // scales.shape[2]
    span = count // parts
    owned, depth = weight_out.shape
    piece, chunk = total.shape[0], CHUNK
    inner, shared = INNER // shards, SHARED // shards

    def load(src, dst):
        copy = pltpu.make_async_copy(src, dst, load_sem)
        copy.start()
        copy.wait()

    blocks, main, width = slots.shape[0], d_cols.shape[1], held.shape[1]
    per = BLOCK // shards
    fetch_weight = pltpu.make_async_copy(weight.at[pl.ds(0, main)], weight_all, fetch_sem)
    fetch_weight.start()

    lots = lot_sem.shape[0]

    def fetch_lot(turn):
        rows = pl.ds(turn * (lot.shape[0] // lots), lot.shape[0] // lots)
        return pltpu.make_async_copy(d_cols.at[rows], lot.at[rows], lot_sem.at[turn])

    tile_width = tile.shape[2]

    def fetch_tile(turn):
        lanes = pl.ds(turn * tile_width, tile_width)
        return pltpu.make_async_copy(normed.at[:, lanes], tile.at[turn % 2], tile_sem.at[turn % 2])

    for turn in range(lots):
        fetch_lot(turn).start()
    fetch_tile(0).start()
    barrier_with(
        [
            {"shard": (shard + step % shards) % shards, "group": (group + step // shards) % groups}
            for step in range(1, shards * groups)
        ]
    )

    def push_home(step):
        peer = (shard + step) % shards
        rows = no_rows.at[pl.ds(0, home.shape[0]), peer]
        return remote(rows, home_at, home_send.at[step], home_recv.at[step], shard=peer)

    home_at = home.at[:, :, pl.ds(pl.multiple_of(shard * inner, inner), inner)]

    for step in range(1, shards):
        push_home(step).start()
    home_here = pltpu.make_async_copy(no_rows.at[pl.ds(0, home.shape[0]), shard], home_at, home_sem)
    home_here.start()

    mate = y * 2 + 1 - core

    def core_copy(turn):
        return remote(piece_of(turn * 2 + 1 - core), core_in.at[turn], core_send.at[turn], core_recv.at[turn], group=mate)

    def piece_of(owner):
        return weight_part.at[pl.ds(pl.multiple_of(owner * piece, piece), piece)]

    out_lots, out_width = out_sem.shape[0], out_part.shape[1]
    out_rows = out_part.shape[0] // out_lots

    def out_place(part, turn):
        return out_full.at[pl.ds(turn * out_rows, out_rows), pl.ds(pl.multiple_of(part * out_width, out_width), out_width)]

    def out_here(turn):
        return pltpu.make_async_copy(out_part.at[pl.ds(turn * out_rows, out_rows)], out_place(group, turn), out_sem.at[turn])

    def out_copy(step, turn):
        peer = mate if step == 0 else (y + step) % rows_y * 2 + core
        rows = out_part.at[pl.ds(turn * out_rows, out_rows)]
        return remote(rows, out_place(group, turn), out_send.at[step, turn], out_recv.at[group, turn], group=peer)

    def out_pass(step, turn):
        part = (y + step) % rows_y * 2 + core
        return remote(
            out_place(part, turn), out_place(part, turn), out_pass_send.at[step, turn], out_recv.at[part, turn], group=mate
        )

    def out_from(part, turn):
        rows = out_part.at[pl.ds(turn * out_rows, out_rows)]
        return remote(rows, out_place(part, turn), out_send.at[0, turn], out_recv.at[part, turn], group=mate)

    def out_start(turns):
        for turn in turns:
            for step in range(1, rows_y):
                out_copy(step, turn).start()
            out_copy(0, turn).start()

    def out_forward(turns):
        for turn in turns:
            for step in range(1, rows_y):
                out_from((y + step) % rows_y * 2 + core, turn).wait_recv()
                out_pass(step, turn).start()

    def out_end():
        for turn in range(out_lots):
            for step in range(rows_y):
                out_copy(step, turn).wait_send()
                out_from(step * 2 + 1 - core, turn).wait_recv()
            for step in range(1, rows_y):
                out_pass(step, turn).wait_send()
            out_here(turn).wait()

    half = 3
    out_start(range(half))
    for turn in range(out_lots):
        out_here(turn).start()

    for turn in range(blocks):
        if turn * lots % blocks == 0:
            fetch_lot(turn * lots // blocks).wait()
        rows = pl.ds(turn * BLOCK, BLOCK)
        place = place_of_rows(slots[turn])
        cols, rest = lot[rows, :], d_rest[rows, :]
        moved[:, turn] = dots(place, cols, ((0,), (0,))).astype(jnp.bfloat16).reshape(shards, per, main)
        moved_rest[:, turn] = dots(place, rest, ((0,), (0,))).astype(jnp.bfloat16).reshape(shards, per, rest.shape[1])
        turned[:main, rows] = cols.T
        turned[main:, rows] = rest.T
    fetch_weight.wait()

    def fetch(owner):
        cols, rest = moved[owner].reshape(count, main), moved_rest[owner].reshape(count, d_rest.shape[1])
        step = min(512, width)
        for lane in range(0, width, step):
            lanes = pl.ds(lane, step)
            found = dots(cols, weight_all[:, lanes], ((1,), (0,)))
            held[:, lanes] = found + dots(rest, weight_rest[:, lanes], ((1,), (0,)))

    def small_copy(step):
        return remote(small, small_in.at[step - 1], small_send.at[step - 1], small_recv.at[step - 1], group=(group + step) % groups)

    for step in range(1, groups):
        small_copy(step).start()

    def piece_of_rows(half):
        return held.at[pl.ds(half * span, span)]

    def code(coded_to, scales_to, values, lot=32):
        @pl.loop(0, values.shape[0] // lot, unroll=2)
        def _(turn):
            rows = pl.ds(pl.multiple_of(turn * lot, lot), lot)
            value = values[rows, :]
            most = jnp.maximum(jnp.max(jnp.abs(value), axis=1, keepdims=True), 1e-30)
            coded_to[rows, :] = jnp.round(value * (32767.0 / most)).astype(jnp.int32).astype(jnp.int16)
            marks[rows, :] = jnp.broadcast_to(most * (1.0 / 32767.0), (lot, 128))

        scales_to[...] = marks[: scales_to.shape[1], :].T[:8, :]

    def add(sums, coded_from, scales_from):
        marks[:span, :] = jnp.broadcast_to(scales_from[0:1, :], (128, span)).T

        @pl.loop(0, span // 32, unroll=2)
        def _(turn):
            rows = pl.ds(pl.multiple_of(turn * 32, 32), 32)
            sums[rows, :] += coded_from[rows, :].astype(jnp.float32) * marks[rows, 0:1]

    def place_of(step):
        return other_place(step, z, lines) if step < lines - 1 else z

    def wide_copies(step, half, hop):
        own = step * parts + half
        at = (hop - 1) * lines * parts + own
        peer = z * columns + (x + hop) % columns
        spot = place_of(step) * parts + half
        return (
            remote(coded.at[own], wide_in.at[hop - 1, spot], wide_send.at[0, at], wide_recv.at[0, at], shard=peer),
            remote(scales.at[own], wide_scale.at[hop - 1, spot], wide_send.at[1, at], wide_recv.at[1, at], shard=peer),
        )

    def send_wide(hop, steps):
        for step in steps:
            fetch(place_of(step) * columns + (x + hop) % columns)
            for half in range(parts):
                if hop > 1:
                    for copy in wide_copies(step, half, hop - 1):
                        copy.wait_send()
                code(coded.at[step * parts + half], scales.at[step * parts + half], piece_of_rows(half))
                for copy in wide_copies(step, half, hop):
                    copy.start()

    def row_copies(step):
        peer = (y + step) % rows_y * 2 + core
        return (
            remote(send_rows.at[step - 1], row_in.at[step - 1], row_send.at[0, step - 1], row_recv.at[0, step - 1], group=peer),
            remote(send_scales.at[step - 1], row_scale_in.at[step - 1], row_send.at[1, step - 1], row_recv.at[1, step - 1], group=peer),
        )

    def core_sum(turn):
        load(piece_of(turn * 2 + core), total)
        load(core_in.at[turn], other)

        @pl.loop(0, piece // chunk)
        def _(turn):
            rows = pl.ds(pl.multiple_of(turn * chunk, chunk), chunk)
            total[rows, :] += other[rows, :]

    early = min(2, lines)
    if columns > 1:
        send_wide(1, range(early))

    def store_made(turn):
        lanes = pl.ds(turn * tile_width, tile_width)
        return pltpu.make_async_copy(made.at[turn % 2], weight_part.at[:, lanes], made_sem.at[turn % 2])

    tiles = width // tile_width
    for turn in range(tiles):
        fetch_tile(turn).wait()
        if turn + 1 < tiles:
            fetch_tile(turn + 1).start()
        if turn >= 2:
            store_made(turn - 2).wait()
        made[turn % 2] = dots(turned[...], tile[turn % 2], ((1,), (0,)))
        store_made(turn).start()
    for turn in range(max(0, tiles - 2), tiles):
        store_made(turn).wait()
    for turn in range(rows_y):
        core_copy(turn).start()

    dt_own = weight_part.at[pl.ds(main + shared, HEADS // shards)]

    def dt_copy(step):
        return remote(dt_own, dt_in.at[step - 1], dt_send.at[step], dt_recv.at[step], group=(group + step) % groups)

    def dt_deal(step):
        at = groups + step
        peer = (shard + step) % shards
        lanes = pl.ds(pl.multiple_of(peer * depth, depth), depth)
        return remote(dt_sum.at[:, lanes], dt_out.at[shard], dt_send.at[at], dt_recv.at[at], shard=peer)

    for step in range(1, groups):
        dt_copy(step).start()
    if columns > 1:
        send_wide(1, range(early, lines))
    for hop in range(2, columns):
        send_wide(hop, range(lines))
    for turn in range(rows_y):
        core_copy(turn).wait_recv()
    for step in range(1, rows_y):
        core_sum((y + step) % rows_y)
        code(send_rows.at[step - 1], send_scales.at[step - 1], total, chunk)
        for copy in row_copies(step):
            copy.start()
    out_start(range(half, out_lots))
    core_sum(y)

    load(small, small_sum)
    for step in range(1, groups):
        small_copy(step).wait_recv()
        load(small_in.at[step - 1], small_got)
        small_sum[...] += small_got[...]

    def small_deal(step):
        return remote(small_sum, small_out.at[shard], small_send.at[groups + step], small_recv.at[groups + step], shard=(shard + step) % shards)

    load(dt_own, dt_sum)
    for step in range(1, groups):
        dt_copy(step).wait_recv()
        load(dt_in.at[step - 1], dt_got)
        dt_sum[...] += dt_got[...]
    for step in range(1, shards):
        small_deal(step).start()
        dt_deal(step).start()
    load(small_sum, small_out.at[shard])
    load(dt_sum.at[:, pl.ds(pl.multiple_of(shard * depth, depth), depth)], dt_out.at[shard])

    def line_copies(step, half):
        target = place_of(step)
        own = step * parts + half
        peer = jnp.where(target > z, z + 1, z - 1) * columns + x
        spot = jnp.where(target == z - 1, lines, target) * parts + half
        return (
            remote(line_coded.at[own], line_in.at[spot], line_send.at[0, own], line_recv.at[0, spot], shard=peer),
            remote(line_scales.at[own], line_scale.at[spot], line_send.at[1, own], line_recv.at[1, spot], shard=peer),
        )

    def take(way, target, half):
        source = jnp.where(way == 0, z - 1, z + 1)
        peer = jnp.clip(source, 0, lines - 1) * columns + x
        spot = jnp.where((way == 1) & (target == z), lines, target) * parts + half
        remote(line_coded.at[0], line_in.at[spot], line_send.at[0, 0], line_recv.at[0, spot], shard=peer).wait_recv()
        remote(line_scales.at[0], line_scale.at[spot], line_send.at[1, 0], line_recv.at[1, spot], shard=peer).wait_recv()
        add(piece_of_rows(half), line_in.at[spot], line_scale.at[spot])

    def gather_wide(step, half):
        spot = place_of(step) * parts + half
        for hop in range(1, columns):
            for copy in wide_copies(step, half, hop):
                copy.wait_recv()
            add(piece_of_rows(half), wide_in.at[hop - 1, spot], wide_scale.at[hop - 1, spot])

    def deal_copy(turn, step):
        first = group * piece + turn * chunk
        column = jnp.where(
            first < inner,
            inner * shard + first,
            jnp.where(first < 2 * inner, INNER + inner * shard + first - inner, 2 * INNER + shared * shard + first - 2 * inner),
        )
        owner = jnp.minimum(column // owned, groups - 1)
        peer = (shard + step) % shards
        source = deal_rows.at[
            pl.ds(pl.multiple_of(turn * chunk, chunk), chunk), pl.ds(pl.multiple_of(peer * depth, depth), depth)
        ]
        target = weight_out.at[pl.ds(pl.multiple_of(column - owner * owned, chunk), chunk)]
        real = first < 2 * inner + shared
        here = real & (owner == group) if step == 0 else None
        away = real & (owner != group) if step == 0 else real

        def near_copy():
            return pltpu.make_async_copy(source, target, deal_recv)

        def far():
            return remote(source, target, deal_send.at[turn, step], deal_recv, shard=peer, group=owner)

        return here, near_copy, away, far

    def deal():
        for step in range(1, rows_y):
            for copy in row_copies(step):
                copy.wait_recv()
            load(row_in.at[step - 1], row_got)
            load(row_scale_in.at[step - 1], row_scale_got)
            marks[: row_scale_got.shape[1], :] = jnp.broadcast_to(row_scale_got[0:1, :], (128, row_scale_got.shape[1])).T

            @pl.loop(0, piece // chunk)
            def _(turn):
                rows = pl.ds(pl.multiple_of(turn * chunk, chunk), chunk)
                total[rows, :] += row_got[rows, :].astype(jnp.float32) * marks[rows, 0:1]

        code(deal_rows, deal_scales, total, chunk)
        load(deal_scales, mark_out.at[shard, group])
        for step in range(1, groups):
            mark_copy(step).start()

    def deal_some(part, parts):
        chunks = piece // chunk

        @pl.loop(part * chunks // parts, (part + 1) * chunks // parts)
        def _(turn):
            for step in range(shards):
                here, near_copy, away, far = deal_copy(turn, step)
                if here is not None:
                    pl.when(here)(lambda: near_copy().start())
                pl.when(away)(lambda: far().start())

    def mark_copy(step):
        to = (group + step) % groups
        return remote(deal_scales, mark_out.at[shard, group], mark_send.at[step], mark_recv.at[step], group=to)

    def mark_spread(step):
        to, at = (shard + step) % shards, groups + step
        return remote(mark_out.at[shard], mark_out.at[shard], mark_send.at[at], mark_recv.at[at], shard=to)

    def mark_pass():
        for step in range(1, groups):
            mark_copy(step).wait_recv()
        for step in range(1, shards):
            mark_spread(step).start()

    def deal_end():
        for step in range(1, groups):
            mark_copy(step).wait_send()
        for step in range(1, shards):
            mark_spread(step).wait()

        @pl.when(group == groups - 1)
        def _():
            most = weight_out.at[pl.ds(0, owned - HEADS)]
            pltpu.make_async_copy(most, most, deal_recv).wait()

        @pl.when(group < groups - 1)
        def _():
            pltpu.make_async_copy(weight_out, weight_out, deal_recv).wait()

        @pl.loop(0, piece // chunk)
        def _(turn):
            for step in range(shards):
                _, _, away, far = deal_copy(turn, step)
                pl.when(away)(lambda: far().wait_send())

    for step in range(lines - 1):
        if step == min(1, lines - 2):
            deal()
        target = place_of(step)
        way = jnp.where(target > z, 0, 1)
        fetch(target * columns + x)
        for half in range(parts):
            gather_wide(step, half)

            @pl.when(jnp.where(target > z, z > 0, z < lines - 1))
            def _():
                take(way, target, half)

            code(line_coded.at[step * parts + half], line_scales.at[step * parts + half], piece_of_rows(half))
            for copy in line_copies(step, half):
                copy.start()
        if step >= min(1, lines - 2):
            deal_some(step - min(1, lines - 2), lines - 1 - min(1, lines - 2))
    out_forward(range(half))
    fetch(z * columns + x)
    for half in range(parts):
        gather_wide(lines - 1, half)

        @pl.when(z > 0)
        def _():
            take(0, z, half)

        @pl.when(z < lines - 1)
        def _():
            take(1, z, half)

    rows_out[...] = held[...]
    gain_sum[...] = jnp.zeros_like(gain_sum)

    @pl.loop(0, count // 8)
    def _(turn):
        rows = pl.ds(pl.multiple_of(turn * 8, 8), 8)
        gain_sum[...] += held[rows, :] * scaled_rows[rows, :]

    def gain_copy(step):
        return remote(gain_part, gain_in.at[step - 1], gain_send.at[step - 1], gain_recv.at[step - 1], shard=(shard + step) % shards)

    def gain_deal(step):
        at = shards - 1 + step - 1
        return remote(gain_out, gain_in.at[at], gain_send.at[at], gain_recv.at[at], group=(group + step) % groups)

    lanes = gain_out.shape[1]
    products = jnp.sum(gain_sum[...], axis=0, keepdims=True)
    gain_part[...] = jnp.concatenate([products[:, row * lanes : (row + 1) * lanes] for row in range(8)], axis=0)
    for step in range(1, shards):
        gain_copy(step).start()
    gain_out[...] = gain_part[...]
    mark_pass()
    out_forward(range(half, out_lots))
    for step in range(1, shards):
        gain_copy(step).wait_recv()
        gain_out[...] += gain_in[step - 1]
    for step in range(1, groups):
        gain_deal(step).start()
    for step in range(1, groups):
        gain_deal(step).wait_recv()
    for step in range(1, groups):
        gain_deal(step).wait_send()
    for step in range(1, groups):
        gain_out[...] += gain_in[shards - 1 + step - 1]

    for step in range(1, shards):
        gain_copy(step).wait_send()
        small_deal(step).wait()
        dt_deal(step).wait()
        push_home(step).wait()
    home_here.wait()
    for step in range(1, groups):
        small_copy(step).wait_send()
        dt_copy(step).wait_send()
    deal_end()
    out_end()
    for step in range(1, rows_y):
        for copy in row_copies(step):
            copy.wait_send()
    for turn in range(rows_y):
        core_copy(turn).wait_send()
    for half in range(parts):
        for step in range(lines):
            for copy in wide_copies(step, half, columns - 1) if columns > 1 else ():
                copy.wait_send()
        for step in range(lines - 1):
            for copy in line_copies(step, half):
                copy.wait_send()


def finish_exchange(
    shards, groups, slots, d_cols, d_rest, normed, weight, weight_rest, no_rows, out_part, small, scaled_rows, owned, depth
):
    columns = grid_columns(shards)
    lines, rows_y = shards // columns, groups // 2
    count, width = scaled_rows.shape
    blocks, main, rest = slots.shape[0], d_cols.shape[1], d_rest.shape[1]
    total, per, heads = blocks * BLOCK, BLOCK // shards, HEADS // shards
    piece = piece_rows(shards, groups)
    padded = -(-piece // 128) * 128
    small_shape = small.shape
    parts = 2
    coded, scale = (count // parts, width), (8, count // parts)
    any_space, vmem = pl.BlockSpec(memory_space=pl.ANY), pl.BlockSpec(memory_space=pltpu.VMEM)
    f32, i16, bf16 = jnp.float32, jnp.int16, jnp.bfloat16
    hops, turns, others = max(columns - 1, 1), max(rows_y - 1, 1), max(groups - 1, 1)
    lots, tile = 8, 256
    dma = pltpu.SemaphoreType.DMA
    out = pl.pallas_call(
        functools.partial(finish_kernel, shards, groups, columns),
        in_specs=[vmem, any_space, vmem, any_space, any_space, vmem, any_space, any_space, any_space, vmem],
        out_specs=[vmem] + [any_space] * 4 + [vmem] + [any_space] * 8 + [vmem],
        out_shape=[
            jax.ShapeDtypeStruct((count, width), f32),
            jax.ShapeDtypeStruct((owned, depth), i16),
            jax.ShapeDtypeStruct((shards, groups, 8, padded), f32),
            jax.ShapeDtypeStruct((shards,) + small_shape, f32),
            jax.ShapeDtypeStruct((shards, heads, depth), f32),
            jax.ShapeDtypeStruct((8, width // 8), f32),
            jax.ShapeDtypeStruct((blocks, per, INNER), bf16),
            jax.ShapeDtypeStruct((out_part.shape[0], out_part.shape[1] * groups), bf16),
            jax.ShapeDtypeStruct((main + rest, width), f32),
            jax.ShapeDtypeStruct((rows_y, piece, width), f32),
            jax.ShapeDtypeStruct((turns, piece, width), i16),
            jax.ShapeDtypeStruct((turns, 8, padded), f32),
            jax.ShapeDtypeStruct((others,) + small_shape, f32),
            jax.ShapeDtypeStruct((others, heads, width), f32),
            jax.ShapeDtypeStruct((shards - 1 + groups - 1, 8, width // 8), f32),
        ],
        scratch_shapes=[
            pltpu.VMEM((hops, lines * parts) + coded, i16),
            pltpu.VMEM((hops, lines * parts) + scale, f32),
            pltpu.VMEM(((lines + 1) * parts,) + coded, i16),
            pltpu.VMEM(((lines + 1) * parts,) + scale, f32),
            pltpu.VMEM((count, width), f32),
            pltpu.VMEM((lines * parts,) + coded, i16),
            pltpu.VMEM((lines * parts,) + scale, f32),
            pltpu.VMEM(((lines - 1) * parts,) + coded, i16),
            pltpu.VMEM(((lines - 1) * parts,) + scale, f32),
            pltpu.VMEM((max(count, padded), 128), f32),
            pltpu.VMEM((piece, width), f32),
            pltpu.VMEM((piece, width), f32),
            pltpu.VMEM((turns, piece, width), i16),
            pltpu.VMEM((turns, 8, padded), f32),
            pltpu.VMEM((piece, width), i16),
            pltpu.VMEM((8, padded), f32),
            pltpu.VMEM((piece, width), i16),
            pltpu.VMEM((8, padded), f32),
            pltpu.VMEM(small_shape, f32),
            pltpu.VMEM(small_shape, f32),
            pltpu.VMEM((heads, width), f32),
            pltpu.VMEM((heads, width), f32),
            pltpu.VMEM((8, width), f32),
            pltpu.VMEM((8, width // 8), f32),
            pltpu.VMEM((shards, blocks, per, main), bf16),
            pltpu.VMEM((shards, blocks, per, rest), bf16),
            pltpu.VMEM((main + rest, total), bf16),
            pltpu.VMEM((main, width), bf16),
            pltpu.VMEM((total, main), bf16),
            pltpu.VMEM((2, total, tile), bf16),
            pltpu.VMEM((2, main + rest, tile), f32),
            dma,
            dma,
            dma((2,)),
            dma((2,)),
            dma((2,)),
            dma((lots,)),
            dma((rows_y, lots)),
            dma((groups, lots)),
            dma((rows_y, lots)),
            dma,
            dma((shards,)),
            dma((shards,)),
            dma((2, hops * lines * parts)),
            dma((2, hops * lines * parts)),
            dma((2, lines * parts)),
            dma((2, (lines + 1) * parts)),
            dma((rows_y,)),
            dma((rows_y,)),
            dma((2, turns)),
            dma((2, turns)),
            dma((piece // CHUNK, shards)),
            dma,
            dma((shards + groups,)),
            dma((shards + groups,)),
            dma((groups + shards,)),
            dma((groups + shards,)),
            dma((groups + shards,)),
            dma((groups + shards,)),
            dma((shards + groups,)),
            dma((shards + groups,)),
        ],
        compiler_params=pltpu.CompilerParams(
            collective_id=7, has_side_effects=True, vmem_limit_bytes=62 * 1024 * 1024
        ),
        cost_estimate=pl.CostEstimate(flops=0, bytes_accessed=450_000_000, transcendentals=0),
        name="finish_exchange",
    )(slots, d_cols, d_rest, normed, weight, weight_rest, no_rows, out_part, small, scaled_rows)
    return out[:8]


def nesterov(weight, gradient, moment, average, step_rate):
    decayed = gradient + weight_decay * weight
    new_moment = momentum_decay * moment + decayed
    new_weight = weight - step_rate * (decayed + momentum_decay * new_moment)
    new_average = average_decay * average + (1.0 - average_decay) * new_weight
    return (new_moment, new_weight, new_average)


def dot32(a, b, contract=((1,), (0,))):
    return lax.dot_general(a, b, (contract, ((), ())), preferred_element_type=jnp.float32)


def own_slice(value, index, width, axis):
    return lax.dynamic_slice_in_dim(value, index * width, width, axis)


def local(
    tokens,
    cotangent,
    lengths,
    deal_slot,
    in_weight,
    out_weight,
    small_params,
    in_moment,
    out_moment,
    small_moment,
    in_average,
    out_average,
    small_average,
):
    shards, groups = lax.axis_size("shard"), lax.axis_size("group")
    shard, group = lax.axis_index("shard"), lax.axis_index("group")
    rows, width = tokens.shape
    per = rows // shards
    total = rows * shards
    blocks = total // BLOCK
    heads = HEADS // shards
    inner = INNER // shards
    shared = SHARED // shards
    conv_flat, conv_bias, dt_bias, rate_log, skip_gain, norm_gain, pre_gain = unpack(small_params)
    taps = conv_flat.reshape(CONV, XBC)

    cols, depth, sends = in_weight.shape[1], in_weight.shape[0], out_weight.shape[1]
    direct = cols % CHUNK == 0 and depth % 128 == 0 and sends % 128 == 0 and per % CHUNK == 0
    direct = direct and (2 * inner + SHARED + HEADS) % (groups * CHUNK) == 0 and shared % CHUNK == 0
    bounds = jnp.cumsum(lengths[0])[:-1].astype(jnp.int32)
    seg_rows = segment_of(jnp.arange(total, dtype=jnp.int32), lengths[0])

    rank = jnp.sum((deal_slot[None, :] < deal_slot[:, None]).astype(jnp.int32), axis=1)
    sort_mat = (rank[None, :] == jnp.arange(rows)[:, None]).astype(jnp.bfloat16)
    r_in = lax.rsqrt(jnp.mean(tokens * tokens, axis=1, keepdims=True) + eps_norm)
    in_turned = in_weight.T

    if direct:
        x_all, in_low, out_low, slot_all, c_sorted, out_cast, x_scaled = front_exchange(
            shards, groups, tokens, pre_gain, cotangent, in_turned, out_weight, deal_slot
        )
        x_all = x_all.reshape(blocks, BLOCK, width)
        slot_all = slot_all[:, 0, :]
    else:
        sorted_slot = jnp.sum(jnp.where(sort_mat > 0, deal_slot[None, :], 0), axis=1)
        x_scaled = jnp.dot(sort_mat.astype(jnp.float32), tokens * r_in, precision=lax.Precision.HIGHEST)
        normed_low = (tokens * r_in * pre_gain[None, :]).astype(jnp.bfloat16)
        x_sorted = dot32(sort_mat, normed_low).astype(jnp.bfloat16).reshape(blocks, per, width)
        c_sorted = dot32(sort_mat, cotangent.astype(jnp.bfloat16)).astype(jnp.bfloat16)
        c_sorted = c_sorted.reshape(blocks, per, width)
        in_turned = in_turned.astype(jnp.bfloat16)
        out_cast = out_weight.astype(jnp.bfloat16)
        x_all = lax.all_gather(x_sorted, "shard").transpose(1, 0, 2, 3).reshape(blocks, BLOCK, width)
        slot_all = lax.all_gather(sorted_slot, "shard")
        part = depth // groups
        pieces = lax.all_to_all(in_turned.reshape(cols, groups, part), "group", 1, 0)
        pieces = pieces.reshape(groups * cols, part)

        def cut(lo, each):
            return pieces[lo : lo + each * shards].reshape(shards, each, part)

        spread = jnp.broadcast_to(pieces[None, 2 * INNER :], (shards, SHARED + HEADS, part))
        got = jnp.concatenate([cut(0, inner), cut(INNER, inner), spread], axis=1)
        got = lax.all_gather(lax.all_to_all(got, "shard", 0, 0), "group")
        in_low = got.transpose(2, 1, 0, 3).reshape(-1, width)
        out_low = lax.all_gather(out_cast, "group", axis=1, tiled=True)
    slot_blk = slot_all.reshape(shards, blocks, per).transpose(1, 0, 2).reshape(blocks, 1, BLOCK)
    slot_blk = slot_blk - jnp.arange(blocks, dtype=jnp.int32)[:, None, None] * BLOCK

    taps_v = own_slice(taps[:, :INNER], shard, inner, 1)
    taps_all = jnp.concatenate([taps_v, taps[:, INNER:]], axis=1)
    bias_all = jnp.concatenate([own_slice(conv_bias[:INNER], shard, inner, 0), conv_bias[INNER:]])[None, :]
    skip_wide = jnp.repeat(own_slice(skip_gain, shard, heads, 0), HDIM)[None, :]
    gain_own = own_slice(norm_gain, shard, inner, 0)[None, :]
    padding = max(TAIL - heads, 0)
    rate = jnp.pad(-jnp.exp(own_slice(rate_log, shard, heads, 0)), (0, padding))[:, None]
    normed, projected, pre, mixed, states, dt_cols, dt_raw, c_all = mixer_forward(
        shards, bounds, slot_blk, x_all, in_low, taps_all, bias_all, dt_bias[None, :], rate, skip_wide, c_sorted
    )
    conv_bc = lax.dynamic_slice_in_dim(projected, 2 * inner + shard * shared, shared, 1)
    cot_low, d_out, sums = pack_cotangent(
        shards, slot_blk, c_all.reshape(blocks, BLOCK, width), out_low, mixed, projected, gain_own
    )

    r_out = lax.rsqrt(sums[0][:, None] + eps_norm)
    normed_out = (mixed * jax.nn.silu(projected[:, :inner]) * r_out * gain_own).astype(jnp.bfloat16)
    grad_out = dot32(normed_out, cot_low, ((0,), (0,)))
    grad_out, mixed = lax.optimization_barrier((grad_out, mixed))
    grad_out = lax.psum_scatter(grad_out, "group", scatter_dimension=1, tiled=True)
    d_cols, d_bc, d_dt, grads, rate_terms, no_rows, out_full = mixer_backward(
        shards, bounds, slot_blk, pre, mixed, projected, d_out, sums, states, dt_cols,
        taps_v, rate, skip_wide, gain_own, out_cast[None],
    )
    out_block = out_full.reshape(INNER, -1)

    d_dtraw = d_dt[:heads].T * jax.nn.sigmoid(dt_raw[:, :heads])
    grad_dtb = jnp.sum(d_dtraw, axis=0)
    grad_rate = jnp.sum(rate_terms[:heads], axis=1)
    grad_skip = jnp.sum(grads[6].reshape(heads, HDIM), axis=1)
    _, pull_bc = jax.vjp(
        lambda c, t, b: convolve(c, seg_rows, t, b),
        conv_bc,
        own_slice(taps[:, INNER:], shard, shared, 1),
        own_slice(conv_bias[INNER:], shard, shared, 0),
    )
    d_conv_bc, grad_taps_bc, grad_bias_bc = pull_bc(d_bc.T)
    rest = 128 - shared - heads
    d_rest = jnp.concatenate([d_conv_bc, d_dtraw, jnp.zeros((total, rest), jnp.float32)], axis=1)
    in_rest = jnp.concatenate(
        [
            own_slice(in_low[2 * inner : 2 * inner + SHARED], shard, shared, 0),
            own_slice(in_low[2 * inner + SHARED :], shard, heads, 0),
            jnp.zeros((rest, width), jnp.bfloat16),
        ]
    )

    mine = [
        grads[:CONV].reshape(-1),
        grad_taps_bc.reshape(-1),
        grads[4],
        grad_bias_bc,
        grad_dtb,
        grad_rate,
        grad_skip,
        grads[5],
    ]
    extents = [piece.shape[0] for piece in mine]
    mine = jnp.concatenate(mine)
    mine = jnp.pad(mine, (0, -mine.shape[0] % 1024)).reshape(-1, 128)
    d_rest = d_rest.astype(jnp.bfloat16)
    if direct:
        d_normed, grad_in, grad_marks, small_all, dt_part, gain_all, home, out_full = finish_exchange(
            shards, groups, slot_blk, d_cols, d_rest, normed, in_low, in_rest, no_rows, out_block, mine, x_scaled,
            cols, depth,
        )
    else:
        partial, weight_part, home = project_back(
            slot_blk, d_cols, d_rest, normed, in_low, in_rest, no_rows, shards
        )
        out_full = lax.all_gather(out_block, "group", axis=1, tiled=True)
        d_normed, _, _, small_all, gain_all = tail_exchange(
            shards, groups, partial.reshape(shards, rows, width), weight_part, mine, x_scaled, cols, depth, False
        )

    home = home.reshape(rows, INNER)
    home = dot32(sort_mat, home, ((0,), (0,))).astype(jnp.bfloat16)
    block_out = tokens + dot32(home, out_full)
    d_normed = jnp.dot(sort_mat.T.astype(jnp.float32), d_normed, precision=lax.Precision.HIGHEST)
    d_scaled = pre_gain[None, :] * d_normed
    inside = jnp.mean(tokens * d_scaled, axis=1, keepdims=True)
    input_grad = cotangent + r_in * (d_scaled - tokens * (r_in * r_in) * inside)
    grad_pre = gain_all.reshape(width)

    mine = small_all.reshape(shards, -1)
    found, offset = [], 0
    for extent in extents:
        found.append(mine[:, offset : offset + extent])
        offset = offset + extent
    if direct:
        dt_part = dt_part.reshape(HEADS, depth)
        steps = grad_marks[:, :, 0, : piece_rows(shards, groups)].reshape(shards, -1)
        steps = jnp.concatenate(
            [
                steps[:, :inner].reshape(-1),
                steps[:, inner : 2 * inner].reshape(-1),
                steps[:, 2 * inner : 2 * inner + shared].reshape(-1),
                jnp.zeros((HEADS,), jnp.float32),
            ]
        )
        grad_in = grad_in.astype(jnp.float32) * own_slice(steps, group, cols, 0)[:, None]
        last = jnp.concatenate([grad_in[: cols - HEADS], dt_part])
        grad_in = jnp.where(group == groups - 1, last, grad_in)
    else:
        used = 2 * inner + shared + heads
        grad_in = weight_part[:used].reshape(used, shards, groups, part).transpose(2, 1, 0, 3)
        grad_in = lax.psum_scatter(grad_in, "group", scatter_dimension=0)
        grad_in = lax.all_to_all(grad_in, "shard", 0, 0)

        def join(lo, each):
            return grad_in[:, lo : lo + each].reshape(shards * each, part)

        grad_in = jnp.concatenate(
            [
                join(0, inner),
                join(inner, inner),
                join(2 * inner, shared),
                join(2 * inner + shared, heads),
            ]
        )
        grad_in = lax.all_to_all(grad_in.reshape(groups, cols, part), "group", 0, 0)
        grad_in = grad_in.transpose(1, 0, 2).reshape(cols, depth)

    def taps_of(piece):
        return piece.reshape(shards, CONV, -1).transpose(1, 0, 2).reshape(CONV, -1)

    grad_taps = jnp.concatenate([taps_of(found[0]), taps_of(found[1])], axis=1).reshape(-1)
    grad_small = jnp.concatenate([grad_taps] + [piece.reshape(-1) for piece in found[2:]] + [grad_pre])
    in_new = nesterov(in_weight.T, grad_in, in_moment.T, in_average.T, rate_in)
    in_new = tuple(value.T for value in in_new)
    out_new = nesterov(out_weight, grad_out, out_moment, out_average, rate_out)
    small_new = nesterov(small_params, grad_small, small_moment, small_average, rate_small)
    return (block_out, input_grad) + in_new + out_new + small_new


def solution(mesh):
    rows = P(("group", "shard"), None)
    tile = P("shard", "group")
    return jax.shard_map(
        local,
        mesh=mesh,
        in_specs=(
            rows,
            rows,
            P("group", None),
            P(("group", "shard")),
            tile,
            tile,
            P(),
            tile,
            tile,
            P(),
            tile,
            tile,
            P(),
        ),
        out_specs=(rows, rows, tile, tile, tile, tile, tile, tile, P(), P(), P()),
        check_vma=False,
    )
```
